32 devices in a mesh: dp: 8 (over z, core), tensor: 4 (over y, x).
Axes of the slice: x: 2, y: 2, z: 4, core: 2. Of those that a mesh axis runs over, the one named last changes fastest.
Arguments:
- hidden_in: bfloat16 [8192, 2048], P(('dp', 'tensor')), may hold values from -6 to 6
- gain_attn: bfloat16 [2048], P('dp'), may hold values from 0.099609375 to 1.8984375
- w_query: bfloat16 [2048, 2048], P('dp', 'tensor'), may hold values from -0.125 to 0.125
- w_key: bfloat16 [2048, 512], P('dp', 'tensor'), may hold values from -0.125 to 0.125
- w_value: bfloat16 [2048, 512], P('dp', 'tensor'), may hold values from -0.125 to 0.125
- w_out: bfloat16 [2048, 2048], P('tensor', 'dp'), may hold values from -0.5 to 0.5
- gain_mlp: bfloat16 [2048], P('dp'), may hold values from 0.099609375 to 1.8984375
- w_gate: bfloat16 [2048, 8192], P('dp', 'tensor'), may hold values from -0.125 to 0.125
- w_up: bfloat16 [2048, 8192], P('dp', 'tensor'), may hold values from -0.125 to 0.125
- w_down: bfloat16 [8192, 2048], P('tensor', 'dp'), may hold values from -0.09375 to 0.09375
- positions: int32 [8192], P('dp'), may hold values from 0 to 3069, as said below
- cotangent: bfloat16 [8192, 2048], P(('dp', 'tensor')), may hold values from -6 to 6
Outputs:
- out: bfloat16 [8192, 2048], P(('dp', 'tensor'))
- grad_in: float32 [8192, 2048], P(('dp', 'tensor'))
- grad_gain_attn: float32 [2048], P(('dp', 'tensor'))
- grad_query: float32 [2048, 2048], P('dp', 'tensor')
- grad_key: float32 [2048, 512], P('dp', 'tensor')
- grad_value: float32 [2048, 512], P('dp', 'tensor')
- grad_out_proj: float32 [2048, 2048], P('tensor', 'dp')
- grad_gain_mlp: float32 [2048], P(('dp', 'tensor'))
- grad_gate: float32 [2048, 8192], P('dp', 'tensor')
- grad_up: float32 [2048, 8192], P('dp', 'tensor')
- grad_down: float32 [8192, 2048], P('tensor', 'dp')
The draws below stay inside these ranges and needn't reach their ends.
Inputs may be any that keep to these rules, and one draw needn't show every extreme that they name: Within each sequence the first position is 0 and positions rise by 1 to 3 from one token to the next; in one sequence they rise by 3 at every token.
All inputs are finite; a program needn't handle non-finite values.
Results may differ from the reference program's by a relative error of at most 0.02.
Values may be sent and summed in bfloat16 or wider, within the bound.
No kernel may reach another device: no remote copies, remote signals or barrier semaphores. Data moves between devices by JAX's collectives and lax.ppermute only.
A program may use at most 256 MiB of HBM per device.

```python
import math
import jax
import jax.numpy as jnp
from jax import lax

D = 2048
HEADS = 32
KV_HEADS = 8
HEAD_DIM = 64
FF = 8192
SEQ_LEN = 1024
SEQS = 8
TOKENS = 8192
QD = 2048
KVD = 512


def draw_positions(key, part):
    key = jax.random.fold_in(key, 17)
    strides = jax.random.randint(key, (SEQS, SEQ_LEN), 1, 4)
    chosen = jax.random.randint(jax.random.fold_in(key, 5), (), 0, SEQS)
    strides = jnp.where(jnp.arange(SEQS)[:, None] == chosen, 3, strides)
    places = jnp.cumsum(strides, axis=1) - strides[:, :1]
    return places.reshape(SEQS * SEQ_LEN).astype(jnp.int32)


def block_scale(stream_key, extent, pieces, smallest, largest):
    factor_of = 1.0
    for dim, blocks in pieces:
        steps = jax.random.uniform(jax.random.fold_in(jax.random.fold_in(stream_key, 6), dim), (blocks,), jnp.float32, smallest / len(pieces), largest / len(pieces))
        factor_of = factor_of * jnp.repeat(jnp.exp(steps), extent[dim] // blocks).reshape((-1,) + (1,) * (len(extent) - 1 - dim))
    return factor_of


def centred(stream_key, dims, width, most, cuts=(), dtype=jnp.bfloat16):
    factor_of = block_scale(stream_key, dims, cuts, -0.22, 0.18) if cuts else 1.0
    drawn = jax.random.normal(stream_key, dims, jnp.float32) * width * factor_of
    return jnp.minimum(jnp.maximum(drawn, -most), most).astype(dtype)


def setup_inputs(seed: int = 0) -> dict:
    key_of = jax.random.split(jax.random.key(seed), 13)
    hidden_in = centred(key_of[0], (TOKENS, D), 1.0, 6.0, ((0, 32),))
    gain_attn = jnp.clip(1.0 + 0.18 * jax.random.normal(key_of[1], (D,), jnp.float32), 0.099609375, 1.8984375).astype(jnp.bfloat16)
    w_query = centred(key_of[2], (D, QD), D ** -0.5, 0.125, ((0, 8), (1, 4)))
    w_key = centred(key_of[3], (D, KVD), D ** -0.5, 0.125, ((0, 8), (1, 4)))
    w_value = centred(key_of[4], (D, KVD), D ** -0.5, 0.125, ((0, 8), (1, 4)))
    w_out = centred(key_of[5], (QD, D), (QD // 16) ** -0.5, 0.5, ((0, 4), (1, 8)))
    gain_mlp = jnp.clip(1.0 + 0.18 * jax.random.normal(key_of[6], (D,), jnp.float32), 0.099609375, 1.8984375).astype(jnp.bfloat16)
    w_gate = centred(key_of[7], (D, FF), D ** -0.5, 0.125, ((0, 8), (1, 4)))
    w_up = centred(key_of[8], (D, FF), D ** -0.5, 0.125, ((0, 8), (1, 4)))
    w_down = centred(key_of[9], (FF, D), (FF // 2) ** -0.5, 0.09375, ((0, 4), (1, 8)))
    positions = draw_positions(jax.random.fold_in(key_of[12], 71), 0)
    cotangent = centred(key_of[11], (TOKENS, D), 1.0, 6.0, ((0, 32),))
    return {"hidden_in": hidden_in, "gain_attn": gain_attn, "w_query": w_query, "w_key": w_key, "w_value": w_value, "w_out": w_out, "gain_mlp": gain_mlp, "w_gate": w_gate, "w_up": w_up, "w_down": w_down, "positions": positions, "cotangent": cotangent}


EPS = 1e-05
ROPE_BASE = 500000.0
HIGHEST = lax.Precision.HIGHEST

@jax.custom_vjp
def low(v):
    return lax.optimization_barrier(v.astype(jnp.bfloat16)).astype(jnp.float32)

@jax.custom_vjp
def low_back(v):
    return v

def low_keep(v):
    return (low(v), None)

def low_pass(kept, grad):
    return (grad,)

def back_keep(v):
    return (v, None)

def back_low(kept, grad):
    return (low(grad),)
low.defvjp(low_keep, low_pass)
low_back.defvjp(back_keep, back_low)

def matmul(left, right):
    return jnp.dot(left, right, precision=HIGHEST, preferred_element_type=jnp.float32)

def rms_norm(values, gain):
    scale = lax.rsqrt(lax.optimization_barrier(jnp.mean(values * values, axis=-1, keepdims=True)) + EPS)
    return values * scale * gain

def rotary(values, cosine, sine):
    half = values.shape[-1] // 2
    first = values[..., :half]
    second = values[..., half:]
    return jnp.concatenate([first * cosine - second * sine, second * cosine + first * sine], axis=-1)

def tables(position):
    freqs = ROPE_BASE ** (-jnp.arange(0, HEAD_DIM, 2).astype(jnp.float32) / HEAD_DIM)
    angles = position.astype(jnp.float32)[:, None] * freqs[None, :]
    return (jnp.cos(angles)[:, None, :], jnp.sin(angles)[:, None, :])

def layer(inputs, weights, cosine, sine):
    gain_attn, w_query, w_key, w_value, w_out, gain_mlp, w_gate, w_up, w_down = weights
    group = HEADS // KV_HEADS
    scale = 1.0 / math.sqrt(HEAD_DIM)
    normed_one = low(rms_norm(inputs, gain_attn))
    query = rotary(low_back(matmul(normed_one, w_query)).reshape(SEQ_LEN, HEADS, HEAD_DIM), cosine, sine)
    keys = rotary(low_back(matmul(normed_one, w_key)).reshape(SEQ_LEN, KV_HEADS, HEAD_DIM), cosine, sine)
    values = low(low_back(matmul(normed_one, w_value))).reshape(SEQ_LEN, KV_HEADS, HEAD_DIM)
    query = low(query).reshape(SEQ_LEN, KV_HEADS, group, HEAD_DIM)
    keys = low(keys)
    scores = low_back(jnp.einsum('qkgd,jkd->kgqj', query, keys, precision=HIGHEST) * scale)
    places = jnp.arange(SEQ_LEN)
    causal = places[:, None] >= places[None, :]
    probs = low(jax.nn.softmax(jnp.where(causal, scores, -1000000000.0), axis=-1))
    attended = jnp.einsum('kgqj,jkd->qkgd', probs, values, precision=HIGHEST).reshape(SEQ_LEN, HEADS * HEAD_DIM)
    attended = low(low_back(attended))
    middle = inputs + low_back(matmul(attended, w_out))
    normed_two = low(rms_norm(middle, gain_mlp))
    gate = low_back(matmul(normed_two, w_gate))
    up_proj = low_back(matmul(normed_two, w_up))
    hidden = low(jax.nn.silu(gate) * up_proj)
    return middle + low_back(matmul(hidden, w_down))

def reference(hidden_in, gain_attn, w_query, w_key, w_value, w_out, gain_mlp, w_gate, w_up, w_down, positions, cotangent):
    params = (gain_attn.astype(jnp.float32), w_query.astype(jnp.float32), w_key.astype(jnp.float32), w_value.astype(jnp.float32), w_out.astype(jnp.float32), gain_mlp.astype(jnp.float32), w_gate.astype(jnp.float32), w_up.astype(jnp.float32), w_down.astype(jnp.float32))
    inputs = hidden_in.astype(jnp.float32).reshape(SEQS, SEQ_LEN, D)
    seeds = cotangent.astype(jnp.float32).reshape(SEQS, SEQ_LEN, D)
    places = positions.reshape(SEQS, SEQ_LEN)

    def one_sequence(totals, item):
        rows_in, rows_grad, rows_pos = item
        cosine, sine = tables(rows_pos)

        def forward(rows, weights):
            return layer(rows, weights, cosine, sine)
        output, pull = jax.vjp(forward, rows_in, params)
        grad_rows, grad_weights = pull(rows_grad)
        totals = jax.tree.map(lambda left, right: left + right, totals, grad_weights)
        return (totals, (output, grad_rows))
    init = jax.tree.map(lambda weight: jnp.zeros(weight.shape, jnp.float32), params)
    totals, (outputs, grads) = lax.scan(one_sequence, init, (inputs, seeds, places))
    return (outputs.reshape(TOKENS, D).astype(jnp.bfloat16), grads.reshape(TOKENS, D), totals[0], totals[1], totals[2], totals[3], totals[4], totals[5], totals[6], totals[7], totals[8])
```

```python
import math

import jax
import jax.numpy as jnp
from jax import lax
from jax.sharding import PartitionSpec as P

HEAD_DIM = 64
SEQ_LEN = 1024


EPS = 1e-05
ROPE_BASE = 500000.0


def rms_scale(values):
    return lax.rsqrt(jnp.mean(values * values, axis=-1, keepdims=True) + EPS)


def norm_back(grad, values, scale, gain):
    inner = grad * gain
    cubed = scale * scale * scale
    result = scale * inner - values * cubed * jnp.mean(inner * values, axis=-1, keepdims=True)
    return (result, jnp.sum(grad * values * scale, axis=0))


def rotary(values, cosine, sine):
    half = values.shape[-1] // 2
    first = values[..., :half]
    second = values[..., half:]
    return jnp.concatenate(
        [first * cosine - second * sine, second * cosine + first * sine], axis=-1
    )


def unrotary(grad, cosine, sine):
    half = grad.shape[-1] // 2
    first = grad[..., :half]
    second = grad[..., half:]
    return jnp.concatenate(
        [first * cosine + second * sine, second * cosine - first * sine], axis=-1
    )


def score_block(query, keys):
    scale = 1.0 / math.sqrt(query.shape[-1])
    raw = jnp.einsum("qkgd,jkd->kgqj", query, keys, preferred_element_type=jnp.float32) * scale
    return raw


def attend(block, causal):
    query, keys, values = block
    raw = score_block(query, keys)
    masked = jnp.where(causal, raw, -1000000000.0)
    row_max = jnp.max(masked, axis=-1, keepdims=True)
    exponent_terms = jnp.exp(masked - row_max)
    row_total = jnp.sum(exponent_terms, axis=-1, keepdims=True)
    probs = (exponent_terms / row_total).astype(jnp.bfloat16)
    attended = jnp.einsum("kgqj,jkd->qkgd", probs, values, preferred_element_type=jnp.float32)
    log_total = (row_max + jnp.log(row_total))[..., 0]
    return (attended.reshape(query.shape[0], -1).astype(jnp.bfloat16), log_total)


def attend_back(block, causal):
    query, keys, values, out_grad, log_total = block
    raw = score_block(query, keys)
    scale = 1.0 / math.sqrt(query.shape[-1])
    probs = jnp.where(causal, jnp.exp(raw - log_total[..., None]), 0.0)
    prob_grad = jnp.einsum("qkgd,jkd->kgqj", out_grad, values, preferred_element_type=jnp.float32)
    inner = jnp.sum(probs * prob_grad, axis=-1, keepdims=True)
    score_grad = (probs * (prob_grad - inner)).astype(jnp.bfloat16)
    query_grad = (
        jnp.einsum("kgqj,jkd->qkgd", score_grad, keys, preferred_element_type=jnp.float32) * scale
    )
    key_grad = (
        jnp.einsum("kgqj,qkgd->jkd", score_grad, query, preferred_element_type=jnp.float32) * scale
    )
    value_grad = jnp.einsum(
        "kgqj,qkgd->jkd", probs.astype(jnp.bfloat16), out_grad, preferred_element_type=jnp.float32
    )
    return (query_grad, key_grad, value_grad)


def swap(values, step):
    size = lax.axis_size("tensor")
    return lax.ppermute(values, "tensor", [(i, i ^ step) for i in range(size)])


def spread(values):
    return [values] + [swap(values, step) for step in range(1, lax.axis_size("tensor"))]


def collect(partial):
    size = lax.axis_size("tensor")
    blocks = partial.reshape((size, partial.shape[0] // size) + partial.shape[1:])
    total = blocks[0].astype(jnp.float32)
    for step in range(1, size):
        total = total + swap(blocks[step].astype(jnp.bfloat16), step).astype(jnp.float32)
    return total


def mm(left, right):
    return jnp.dot(left, right, preferred_element_type=jnp.float32)


def mm_nt(left, right):
    return lax.dot_general(left, right, (((1,), (1,)), ((), ())), preferred_element_type=jnp.float32)


def mm_tn(left, right):
    return lax.dot_general(left, right, (((0,), (0,)), ((), ())), preferred_element_type=jnp.float32)


def per_device(
    hidden_in,
    gain_attn,
    w_query,
    w_key,
    w_value,
    w_out,
    gain_mlp,
    w_gate,
    w_up,
    w_down,
    positions,
    cotangent,
):
    size = lax.axis_size("tensor")
    me = lax.axis_index("tensor")
    rows = hidden_in.shape[0]
    total_rows = rows * size
    q_width, kv_width = w_query.shape[1], w_key.shape[1]
    qkv_width = q_width + 2 * kv_width
    features = hidden_in.shape[1]

    gains = jnp.stack([gain_attn, gain_mlp], axis=1)
    gains = jnp.pad(gains, ((0, 0), (0, 126)))
    attn_shard = jnp.concatenate([w_query, w_key, w_value, w_out.T, gains], axis=1)
    attn_full = lax.all_gather(attn_shard, "dp", axis=0, tiled=True)
    qkv_full = attn_full[:, :qkv_width]
    out_t = attn_full[:, qkv_width : qkv_width + q_width]
    gain_one = attn_full[:, qkv_width + q_width].astype(jnp.float32)
    gain_two = attn_full[:, qkv_width + q_width + 1].astype(jnp.float32)
    w_gate, w_up, w_down, attn_full = lax.optimization_barrier((w_gate, w_up, w_down, attn_full))
    gate_full = lax.all_gather(w_gate, "dp", axis=0, tiled=True)
    up_full = lax.all_gather(w_up, "dp", axis=0, tiled=True)
    down_full = lax.all_gather(w_down, "dp", axis=1, tiled=True)

    tokens_in = jnp.concatenate(spread(hidden_in), axis=0)
    cot_full = jnp.concatenate(spread(cotangent), axis=0)
    ranks = [me ^ step for step in range(size)]
    places = jnp.concatenate([r * rows + jnp.arange(rows) for r in ranks])
    own_pos = jnp.concatenate(
        [lax.dynamic_slice_in_dim(positions, r * rows, rows) for r in ranks]
    )
    causal = places[:, None] >= places[None, :]

    residual = hidden_in.astype(jnp.float32)
    scale_one = rms_scale(residual)
    tokens32 = tokens_in.astype(jnp.float32)
    tokens_one = (tokens32 * rms_scale(tokens32) * gain_one).astype(jnp.bfloat16)

    freqs = ROPE_BASE ** (-jnp.arange(0, HEAD_DIM, 2).astype(jnp.float32) / HEAD_DIM)
    angles = own_pos.astype(jnp.float32)[:, None] * freqs[None, :]
    cosine = jnp.cos(angles)[:, None, :]
    sine = jnp.sin(angles)[:, None, :]
    query_heads = q_width // HEAD_DIM
    key_heads = kv_width // HEAD_DIM
    group = query_heads // key_heads
    lin = mm(tokens_one, qkv_full)
    query = rotary(
        lin[:, :q_width].reshape(total_rows, query_heads, HEAD_DIM), cosine, sine
    ).astype(jnp.bfloat16)
    keys = rotary(
        lin[:, q_width : q_width + kv_width].reshape(total_rows, key_heads, HEAD_DIM), cosine, sine
    ).astype(jnp.bfloat16)
    values = lin[:, q_width + kv_width :].astype(jnp.bfloat16)
    query_seq = query.reshape(total_rows, key_heads, group, HEAD_DIM)
    key_seq = keys
    value_seq = values.reshape(total_rows, key_heads, HEAD_DIM)
    attended, log_total = attend((query_seq, key_seq, value_seq), causal)
    middle = residual + collect(mm_nt(attended, out_t))

    scale_two = rms_scale(middle)
    normed_two = (middle * scale_two * gain_two).astype(jnp.bfloat16)
    tokens_two = jnp.concatenate(spread(normed_two), axis=0)
    gate = mm(tokens_two, gate_full)
    up_proj = mm(tokens_two, up_full)
    hidden = (jax.nn.silu(gate) * up_proj).astype(jnp.bfloat16)
    hidden_grad = mm_nt(cot_full, down_full)
    sigma = jax.nn.sigmoid(gate)
    gate_grad = (hidden_grad * up_proj * sigma * (1.0 + gate * (1.0 - sigma))).astype(jnp.bfloat16)
    up_grad = (hidden_grad * gate * sigma).astype(jnp.bfloat16)
    normed_two_grad = collect(mm_nt(gate_grad, gate_full) + mm_nt(up_grad, up_full))
    grad_gate = lax.psum_scatter(
        mm_tn(tokens_two, gate_grad).astype(jnp.bfloat16), "dp", scatter_dimension=0, tiled=True
    ).astype(jnp.float32)
    grad_up = lax.psum_scatter(
        mm_tn(tokens_two, up_grad).astype(jnp.bfloat16), "dp", scatter_dimension=0, tiled=True
    ).astype(jnp.float32)
    grad_down = lax.psum_scatter(
        mm_tn(hidden, cot_full).astype(jnp.bfloat16), "dp", scatter_dimension=1, tiled=True
    ).astype(jnp.float32)
    out = (middle + collect(mm(hidden, down_full))).astype(jnp.bfloat16)

    middle_norm_grad, gain_two_part = norm_back(normed_two_grad, middle, scale_two, gain_two)
    middle_grad = cotangent.astype(jnp.float32) + middle_norm_grad
    branch_grad = jnp.concatenate(spread(middle_grad.astype(jnp.bfloat16)), axis=0)
    attended_grad = mm(branch_grad, out_t).astype(jnp.bfloat16)
    grad_out_t = mm_tn(branch_grad, attended).astype(jnp.bfloat16)
    query_grad, key_grad, value_grad = attend_back(
        (query_seq, key_seq, value_seq, attended_grad.reshape(query_seq.shape), log_total), causal
    )
    query_grad = unrotary(query_grad.reshape(total_rows, query_heads, HEAD_DIM), cosine, sine)
    key_grad = unrotary(key_grad, cosine, sine)
    qkv_grad = jnp.concatenate(
        [
            query_grad.reshape(total_rows, q_width),
            key_grad.reshape(total_rows, kv_width),
            value_grad.reshape(total_rows, kv_width),
        ],
        axis=1,
    ).astype(jnp.bfloat16)
    grad_qkv = mm_tn(tokens_one, qkv_grad)
    gain_one_part = (
        jnp.sum(grad_qkv * qkv_full.astype(jnp.float32), axis=1) / gain_one
    )
    gain_parts = jnp.pad(jnp.stack([gain_one_part, gain_two_part], axis=1), ((0, 0), (0, 126)))
    attn_grads = jnp.concatenate(
        [grad_qkv.astype(jnp.bfloat16), grad_out_t, gain_parts.astype(jnp.bfloat16)], axis=1
    )
    attn_grads = lax.psum_scatter(attn_grads, "dp", scatter_dimension=0, tiled=True)
    attn_grads = attn_grads.astype(jnp.float32)
    normed_one_grad = collect(mm_nt(qkv_grad, qkv_full))
    input_norm_grad, _ = norm_back(normed_one_grad, residual, scale_one, gain_one)
    grad_in = middle_grad + input_norm_grad

    gain_sums = attn_grads[:, qkv_width + q_width : qkv_width + q_width + 2]
    gain_blocks = gain_sums.reshape(size, -1, 2)
    gain_own = lax.dynamic_index_in_dim(gain_blocks, me, 0, keepdims=False)
    for step in range(1, size):
        other = lax.dynamic_index_in_dim(gain_blocks, me ^ step, 0, keepdims=False)
        gain_own = gain_own + swap(other, step)
    return (
        out,
        grad_in,
        gain_own[:, 0],
        attn_grads[:, :q_width],
        attn_grads[:, q_width : q_width + kv_width],
        attn_grads[:, q_width + kv_width : qkv_width],
        attn_grads[:, qkv_width : qkv_width + q_width].T,
        gain_own[:, 1],
        grad_gate,
        grad_up,
        grad_down,
    )


def solution(mesh):
    return jax.shard_map(
        per_device,
        mesh=mesh,
        in_specs=(
            P(("dp", "tensor"), None),
            P("dp"),
            P("dp", "tensor"),
            P("dp", "tensor"),
            P("dp", "tensor"),
            P("tensor", "dp"),
            P("dp"),
            P("dp", "tensor"),
            P("dp", "tensor"),
            P("tensor", "dp"),
            P("dp"),
            P(("dp", "tensor"), None),
        ),
        out_specs=(
            P(("dp", "tensor"), None),
            P(("dp", "tensor"), None),
            P(("dp", "tensor")),
            P("dp", "tensor"),
            P("dp", "tensor"),
            P("dp", "tensor"),
            P("tensor", "dp"),
            P(("dp", "tensor")),
            P("dp", "tensor"),
            P("dp", "tensor"),
            P("tensor", "dp"),
        ),
        check_vma=False,
    )
```

```python
import functools
import math

import jax
import jax.numpy as jnp
from jax import lax
from jax.experimental import pallas as pl
from jax.experimental.pallas import tpu as pltpu
from jax.sharding import PartitionSpec as P

HEAD_DIM = 64
PAIR = 2 * HEAD_DIM
SEQ_LEN = 1024


EPS = 1e-05
ROPE_BASE = 500000.0
SCALE = 1.0 / math.sqrt(HEAD_DIM)
PARAMS = pltpu.CompilerParams(vmem_limit_bytes=58 * 2**20)
ONCE = pl.Buffered(1)

barrier = lax.optimization_barrier


def rms_scale(values):
    return lax.rsqrt(jnp.mean(values * values, axis=-1, keepdims=True) + EPS)


def norm_back(grad, values, scale, gain):
    inner = grad * gain
    cubed = scale * scale * scale
    result = scale * inner - values * cubed * jnp.mean(inner * values, axis=-1, keepdims=True)
    return (result, jnp.sum(grad * values * scale, axis=0))


def mm(left, right):
    return jnp.dot(left, right, preferred_element_type=jnp.float32)


def mm_nt(left, right):
    return lax.dot_general(left, right, (((1,), (1,)), ((), ())), preferred_element_type=jnp.float32)


def mm_tn(left, right):
    return lax.dot_general(left, right, (((0,), (0,)), ((), ())), preferred_element_type=jnp.float32)


def lane_index(rows):
    return lax.broadcasted_iota(jnp.int32, (rows, PAIR), 1)


def turn(pair, cosine, sine):
    lower = lane_index(pair.shape[0]) % HEAD_DIM < HEAD_DIM // 2
    other = jnp.where(
        lower, pltpu.roll(pair, PAIR - HEAD_DIM // 2, 1), pltpu.roll(pair, HEAD_DIM // 2, 1)
    )
    return pair * cosine + other * sine


def project_kernel(place_ref, *refs, size, q_width, kv_width):
    x_refs = refs[:size]
    gain_ref, w_ref, cos_ref, sin_ref, n_ref, q_ref, k_ref, v_ref = refs[size:]
    rows = q_ref.shape[0]

    def one(x_ref):
        x = x_ref[...].astype(jnp.float32)
        normed = (x * rms_scale(x) * gain_ref[...]).astype(jnp.bfloat16)
        n_ref[...] = normed
        cosine, sine = cos_ref[...], sin_ref[...]
        lin = mm(normed, w_ref[...])
        for low in range(0, q_width, PAIR):
            query = turn(lin[:, low : low + PAIR], cosine, sine).astype(jnp.bfloat16)
            q_ref[:, low : low + PAIR] = query * jnp.bfloat16(SCALE)
        first = lane_index(rows) < HEAD_DIM
        for ref, start, rotate in ((k_ref, q_width, True), (v_ref, q_width + kv_width, False)):
            for head in range(kv_width // HEAD_DIM):
                low = start + head * HEAD_DIM
                block = lin[:, low // PAIR * PAIR : low // PAIR * PAIR + PAIR]
                if rotate:
                    block = turn(block, cosine, sine)
                moved = pltpu.roll(block, HEAD_DIM, 1)
                if low % PAIR:
                    block, moved = moved, block
                ref[head, 0] = jnp.where(first, block, 0.0).astype(jnp.bfloat16)
                ref[head, 1] = jnp.where(first, 0.0, moved).astype(jnp.bfloat16)

    for step in range(size):
        pl.when(pl.program_id(0) == step)(functools.partial(one, x_refs[step]))


def project(me, blocks, gain, weights, cosine, sine, q_width, kv_width):
    size = len(blocks)
    rows, features = blocks[0].shape
    total = rows * size
    key_heads = kv_width // HEAD_DIM
    width = q_width + 2 * kv_width
    fixed = lambda p, m: (0, 0)
    placed = lambda p, m: (jnp.bitwise_xor(p, m[0]), 0)
    padded = pl.BlockSpec(
        (key_heads, 2, rows, PAIR), lambda p, m: (0, 0, jnp.bitwise_xor(p, m[0]), 0)
    )
    spec = pltpu.PrefetchScalarGridSpec(
        num_scalar_prefetch=1,
        grid=(size,),
        in_specs=[pl.BlockSpec((rows, features), fixed, pipeline_mode=ONCE)] * size
        + [
            pl.BlockSpec((1, features), fixed),
            pl.BlockSpec((features, width), fixed, pipeline_mode=ONCE),
            pl.BlockSpec((rows, PAIR), placed),
            pl.BlockSpec((rows, PAIR), placed),
        ],
        out_specs=[
            pl.BlockSpec((rows, features), lambda p, m: (p, 0)),
            pl.BlockSpec((rows, q_width), lambda p, m: (p, 0)),
            padded,
            padded,
        ],
    )
    padded_shape = jax.ShapeDtypeStruct((key_heads, 2, total, PAIR), jnp.bfloat16)
    return pl.pallas_call(
        functools.partial(project_kernel, size=size, q_width=q_width, kv_width=kv_width),
        grid_spec=spec,
        out_shape=[
            jax.ShapeDtypeStruct((total, features), jnp.bfloat16),
            jax.ShapeDtypeStruct((total, q_width), jnp.bfloat16),
            padded_shape,
            padded_shape,
        ],
        compiler_params=PARAMS,
        cost_estimate=pl.CostEstimate(
            flops=2 * total * features * width,
            bytes_accessed=4 * total * features + 2 * features * width,
            transcendentals=0,
        ),
    )(me, *blocks, gain, weights, cosine, sine)


def attend_kernel(me_ref, q_ref, k_ref, v_ref, o_ref, l_ref, vt_ref, *, size, heads, group):
    rows = q_ref.shape[0]
    mine = jnp.bitwise_xor(me_ref[0], pl.program_id(0))
    key_place = lax.broadcasted_iota(jnp.int32, (rows, rows), 0)
    query_place = lax.broadcasted_iota(jnp.int32, (rows, rows), 1)

    @pl.when(pl.program_id(0) == 0)
    def _():
        for head in range(heads // group):
            for side in range(2):
                vt_ref[head, side] = v_ref[head, side].T

    def one(span):
        keys = span * rows
        for pair in range(heads // 2):
            head = 2 * pair // group
            lanes = slice(pair * PAIR, (pair + 1) * PAIR)
            query = q_ref[:, lanes]
            acc = None
            inverse = []
            for side in range(2):
                diag = mm_nt(k_ref[head, side, keys : keys + rows, :], query)
                diag = jnp.where(key_place <= query_place, diag, -1e9)
                top = jnp.max(diag, axis=0, keepdims=True)
                if span:
                    body = mm_nt(k_ref[head, side, :keys, :], query)
                    top = jnp.maximum(top, jnp.max(body, axis=0, keepdims=True))
                diag = jnp.exp(diag - top)
                total = jnp.sum(diag, axis=0, keepdims=True)
                part = mm(vt_ref[head, side, :, keys : keys + rows], diag.astype(jnp.bfloat16))
                if span:
                    body = jnp.exp(body - top)
                    total = total + jnp.sum(body, axis=0, keepdims=True)
                    part = part + mm(vt_ref[head, side, :, :keys], body.astype(jnp.bfloat16))
                acc = part if acc is None else acc + part
                inverse.append(jnp.broadcast_to(1.0 / total, (HEAD_DIM, rows)))
                l_ref[2 * pair + side : 2 * pair + side + 1, :] = top + jnp.log(total)
            acc = acc * jnp.concatenate(inverse, axis=0)
            o_ref[:, lanes] = acc.T.astype(jnp.bfloat16)

    for span in range(size):
        pl.when(mine == span)(functools.partial(one, span))


def attend(me, query, key_pad, value_pad, size, group):
    total, width = query.shape
    rows, heads = total // size, width // HEAD_DIM
    whole = pl.BlockSpec(key_pad.shape, lambda p, m: (0, 0, 0, 0), pipeline_mode=ONCE)
    spec = pltpu.PrefetchScalarGridSpec(
        num_scalar_prefetch=1,
        grid=(size,),
        in_specs=[pl.BlockSpec((rows, width), lambda p, m: (p, 0)), whole, whole],
        out_specs=[
            pl.BlockSpec((rows, width), lambda p, m: (p, 0)),
            pl.BlockSpec((heads, rows), lambda p, m: (0, p)),
        ],
        scratch_shapes=[pltpu.VMEM((heads // group, 2, PAIR, total), jnp.bfloat16)],
    )
    return pl.pallas_call(
        functools.partial(attend_kernel, size=size, heads=heads, group=group),
        grid_spec=spec,
        out_shape=[
            jax.ShapeDtypeStruct((total, width), jnp.bfloat16),
            jax.ShapeDtypeStruct((heads, total), jnp.float32),
        ],
        compiler_params=PARAMS,
        cost_estimate=pl.CostEstimate(
            flops=8 * heads * total * total * HEAD_DIM,
            bytes_accessed=8 * total * width,
            transcendentals=heads * total * total,
        ),
    )(me, query, key_pad, value_pad)


def attend_back_kernel(
    me_ref,
    q_ref,
    do_ref,
    l_ref,
    k_ref,
    v_ref,
    cos_ref,
    sin_ref,
    out_ref,
    dk_ref,
    dv_ref,
    kt_ref,
    *,
    size,
    heads,
    group,
):
    rows = q_ref.shape[0]
    key_heads = heads // group
    step = pl.program_id(0)
    me = me_ref[0]
    mine = jnp.bitwise_xor(me, step)
    key_place = lax.broadcasted_iota(jnp.int32, (rows, rows), 0)
    query_place = lax.broadcasted_iota(jnp.int32, (rows, rows), 1)

    def rows_of(block):
        return pl.ds(pl.multiple_of(block * rows, rows), rows)

    @pl.when(step == 0)
    def _():
        dk_ref[...] = jnp.zeros_like(dk_ref)
        dv_ref[...] = jnp.zeros_like(dv_ref)
        for head in range(key_heads):
            for side in range(2):
                kt_ref[head, side] = k_ref[head, side].T

    def one(span):
        keys = span * rows
        parts = [(keys, keys + rows, True)] + ([(0, keys, False)] if span else [])
        cosine, sine = cos_ref[keys : keys + rows, :], sin_ref[keys : keys + rows, :]
        for pair in range(heads // 2):
            head = 2 * pair // group
            lanes = slice(pair * PAIR, (pair + 1) * PAIR)
            query, grad = q_ref[:, lanes], do_ref[:, lanes]
            acc = None
            for side in range(2):
                log_total = l_ref[2 * pair + side : 2 * pair + side + 1, :]
                inner = None
                kept = []
                for low, high, diagonal in parts:
                    probs = mm_nt(k_ref[head, side, low:high, :], query)
                    probs = jnp.exp(probs - log_total)
                    if diagonal:
                        probs = jnp.where(key_place <= query_place, probs, 0.0)
                    prob_grad = mm_nt(v_ref[head, side, low:high, :], grad)
                    dv_ref[head, side, low:high, :] += mm(probs.astype(jnp.bfloat16), grad)
                    term = jnp.sum(probs * prob_grad, axis=0, keepdims=True)
                    inner = term if inner is None else inner + term
                    kept.append((low, high, probs, prob_grad))
                for low, high, probs, prob_grad in kept:
                    score_grad = (probs * (prob_grad - inner)).astype(jnp.bfloat16)
                    dk_ref[head, side, low:high, :] += mm(score_grad, query)
                    part = mm(kt_ref[head, side, :, low:high], score_grad)
                    acc = part if acc is None else acc + part
            turned = turn(acc.T * SCALE, cosine, -sine)
            out_ref[rows_of(step), lanes] = turned.astype(jnp.bfloat16)

    for span in range(size):
        pl.when(mine == span)(functools.partial(one, span))

    @pl.when(step == size - 1)
    def _():
        first = lane_index(rows) < HEAD_DIM
        wanted = [(dk_ref, head, True) for head in range(key_heads)]
        wanted += [(dv_ref, head, False) for head in range(key_heads)]
        for span in range(size):
            place = slice(span * rows, (span + 1) * rows)
            cosine, sine = cos_ref[place, :], sin_ref[place, :]
            for block in range(len(wanted) // 2):
                halves, rotate = [], []
                for half in range(2):
                    ref, head, is_key = wanted[2 * block + half]
                    low, high = ref[head, 0, place, :], ref[head, 1, place, :]
                    if half:
                        halves.append(pltpu.roll(low, HEAD_DIM, 1) + high)
                    else:
                        halves.append(low + pltpu.roll(high, HEAD_DIM, 1))
                    rotate.append(is_key)
                value = jnp.where(first, halves[0], halves[1])
                if rotate[0] and rotate[1]:
                    value = turn(value, cosine, -sine)
                elif rotate[0]:
                    value = jnp.where(first, turn(value, cosine, -sine), value)
                start = heads * HEAD_DIM + block * PAIR
                target = rows_of(jnp.bitwise_xor(me, span))
                out_ref[target, start : start + PAIR] = value.astype(jnp.bfloat16)


def attend_back(me, query, grad, log_total, key_pad, value_pad, cosine, sine, size, group):
    total, width = query.shape
    rows, heads = total // size, width // HEAD_DIM
    key_heads = heads // group
    out_width = width + 2 * key_heads * HEAD_DIM
    whole = pl.BlockSpec(key_pad.shape, lambda p, m: (0, 0, 0, 0), pipeline_mode=ONCE)
    table = pl.BlockSpec((total, PAIR), lambda p, m: (0, 0), pipeline_mode=ONCE)
    spec = pltpu.PrefetchScalarGridSpec(
        num_scalar_prefetch=1,
        grid=(size,),
        in_specs=[
            pl.BlockSpec((rows, width), lambda p, m: (p, 0)),
            pl.BlockSpec((rows, width), lambda p, m: (p, 0)),
            pl.BlockSpec((heads, rows), lambda p, m: (0, p)),
            whole,
            whole,
            table,
            table,
        ],
        out_specs=pl.BlockSpec((total, out_width), lambda p, m: (0, 0)),
        scratch_shapes=[
            pltpu.VMEM(key_pad.shape, jnp.float32),
            pltpu.VMEM(key_pad.shape, jnp.float32),
            pltpu.VMEM((key_heads, 2, PAIR, total), jnp.bfloat16),
        ],
    )
    return pl.pallas_call(
        functools.partial(attend_back_kernel, size=size, heads=heads, group=group),
        grid_spec=spec,
        out_shape=jax.ShapeDtypeStruct((total, out_width), jnp.bfloat16),
        compiler_params=PARAMS,
        cost_estimate=pl.CostEstimate(
            flops=20 * heads * total * total * HEAD_DIM,
            bytes_accessed=16 * total * width,
            transcendentals=heads * total * total,
        ),
    )(me, query, grad, log_total, key_pad, value_pad, cosine, sine)


def mlp_kernel(*refs, adds):
    n_ref, e_ref, gate_ref, up_ref, down_ref = refs[:5]
    h_ref, dg_ref, du_ref, dn_ref, y_ref = refs[-5:]
    gate = mm(n_ref[...], gate_ref[...])
    up = mm(n_ref[...], up_ref[...])
    grad = mm_nt(e_ref[...], down_ref[...])
    sigma = jax.nn.sigmoid(gate)
    silu = gate * sigma
    hidden = (silu * up).astype(jnp.bfloat16)
    gate_grad = (grad * up * sigma * (1.0 + gate * (1.0 - sigma))).astype(jnp.bfloat16)
    up_grad = (grad * silu).astype(jnp.bfloat16)
    h_ref[...] = hidden
    dg_ref[...] = gate_grad
    du_ref[...] = up_grad
    dn = mm_nt(gate_grad, gate_ref[...]) + mm_nt(up_grad, up_ref[...])
    y = mm(hidden, down_ref[...])
    if adds:
        dn = dn + refs[5][...]
        y = y + refs[6][...]
    dn_ref[...] = dn.astype(dn_ref.dtype)
    y_ref[...] = y.astype(y_ref.dtype)


def mlp(tokens, cot, gate_up, down, size, earlier):
    total, features = tokens.shape
    rows, units = total // size, down.shape[0]
    fixed = lambda p: (0, 0)
    moving = lambda p: (p, 0)
    wide = pl.BlockSpec((rows, features), moving)
    narrow = pl.BlockSpec((rows, units), moving)
    sums = jax.ShapeDtypeStruct((total, features), jnp.bfloat16 if earlier else jnp.float32)
    thin = jax.ShapeDtypeStruct((total, units), jnp.bfloat16)
    return pl.pallas_call(
        functools.partial(mlp_kernel, adds=bool(earlier)),
        grid=(size,),
        in_specs=[
            wide,
            wide,
            pl.BlockSpec((features, units), fixed, pipeline_mode=ONCE),
            pl.BlockSpec((features, units), lambda p: (0, 1), pipeline_mode=ONCE),
            pl.BlockSpec((units, features), fixed, pipeline_mode=ONCE),
        ]
        + [wide] * len(earlier),
        out_specs=[narrow, narrow, narrow, wide, wide],
        out_shape=[thin, thin, thin, sums, sums],
        compiler_params=PARAMS,
        cost_estimate=pl.CostEstimate(
            flops=12 * total * features * units,
            bytes_accessed=6 * features * units + 20 * total * features,
            transcendentals=total * units,
        ),
    )(tokens, cot, gate_up, gate_up, down, *earlier)


def grad_kernel(order_ref, n_ref, e_ref, dg_ref, du_ref, h_ref, theirs_ref, mine_ref):
    units = dg_ref.shape[1]
    count = pl.num_programs(0)

    def one(ref):
        ref[0, :, :units] = mm_tn(n_ref[...], dg_ref[...]).astype(jnp.bfloat16)
        ref[0, :, units : 2 * units] = mm_tn(n_ref[...], du_ref[...]).astype(jnp.bfloat16)
        ref[0, :, 2 * units :] = mm_tn(e_ref[...], h_ref[...]).astype(jnp.bfloat16)

    pl.when(pl.program_id(0) < count // 2)(lambda: one(theirs_ref))
    pl.when(pl.program_id(0) >= count // 2)(lambda: one(mine_ref))


def split_specs(count, depth, width):
    half = count // 2
    shape = jax.ShapeDtypeStruct((half, depth, width), jnp.bfloat16)
    theirs = pl.BlockSpec((1, depth, width), lambda b, o: (jnp.minimum(b, half - 1), 0, 0))
    mine = pl.BlockSpec((1, depth, width), lambda b, o: (jnp.maximum(b - half, 0), 0, 0))
    return [theirs, mine], [shape, shape]


def mlp_grads(order, tokens, cot, gate_grad, up_grad, hidden):
    total, features = tokens.shape
    units = hidden.shape[1]
    count = order.shape[0]
    depth = features // count
    column = pl.BlockSpec((total, depth), lambda b, o: (0, o[b]))
    fixed = pl.BlockSpec((total, units), lambda b, o: (0, 0), pipeline_mode=ONCE)
    out_specs, out_shape = split_specs(count, depth, 3 * units)
    return pl.pallas_call(
        grad_kernel,
        grid_spec=pltpu.PrefetchScalarGridSpec(
            num_scalar_prefetch=1,
            grid=(count,),
            in_specs=[column, column, fixed, fixed, fixed],
            out_specs=out_specs,
        ),
        out_shape=out_shape,
        compiler_params=PARAMS,
        cost_estimate=pl.CostEstimate(
            flops=6 * total * features * units,
            bytes_accessed=4 * total * features + 6 * features * units + 6 * total * units,
            transcendentals=0,
        ),
    )(order, tokens, cot, gate_grad, up_grad, hidden)


def attn_grad_kernel(
    order_ref, n_ref, e_ref, d_ref, o_ref, w_ref, g1_ref, g2_ref, theirs_ref, mine_ref
):
    width, out_width = d_ref.shape[1], o_ref.shape[1]
    count = pl.num_programs(0)

    def one(ref):
        grad = mm_tn(n_ref[...], d_ref[...])
        ref[0, :, :width] = grad.astype(jnp.bfloat16)
        out = mm_tn(e_ref[...], o_ref[...])
        ref[0, :, width : width + out_width] = out.astype(jnp.bfloat16)
        first = jnp.sum(grad * w_ref[...].astype(jnp.float32), axis=1, keepdims=True) / g1_ref[...]
        lane = lane_index(grad.shape[0])
        both = jnp.where(lane == 0, first, jnp.where(lane == 1, g2_ref[...], 0.0))
        ref[0, :, width + out_width :] = both.astype(jnp.bfloat16)

    pl.when(pl.program_id(0) < count // 2)(lambda: one(theirs_ref))
    pl.when(pl.program_id(0) >= count // 2)(lambda: one(mine_ref))


def attn_grads(order, tokens, branch, qkv_grad, attended, weights, gain_one, gain_two_part):
    total, features = tokens.shape
    width, out_width = qkv_grad.shape[1], attended.shape[1]
    count = order.shape[0]
    depth = features // count
    column = pl.BlockSpec((total, depth), lambda b, o: (0, o[b]))
    fixed = lambda b, o: (0, 0)
    row = lambda b, o: (o[b], 0)
    out_specs, out_shape = split_specs(count, depth, width + out_width + PAIR)
    return pl.pallas_call(
        attn_grad_kernel,
        grid_spec=pltpu.PrefetchScalarGridSpec(
            num_scalar_prefetch=1,
            grid=(count,),
            in_specs=[
                column,
                column,
                pl.BlockSpec((total, width), fixed, pipeline_mode=ONCE),
                pl.BlockSpec((total, out_width), fixed, pipeline_mode=ONCE),
                pl.BlockSpec((depth, width), row),
                pl.BlockSpec((depth, 1), row),
                pl.BlockSpec((depth, 1), row),
            ],
            out_specs=out_specs,
        ),
        out_shape=out_shape,
        compiler_params=PARAMS,
        cost_estimate=pl.CostEstimate(
            flops=2 * total * features * (width + out_width),
            bytes_accessed=4 * total * features + 4 * features * (width + out_width),
            transcendentals=0,
        ),
    )(order, tokens, branch, qkv_grad, attended, weights, gain_one, gain_two_part)


def swap(values, step):
    size = lax.axis_size("tensor")
    return lax.ppermute(values, "tensor", [(i, i ^ step) for i in range(size)])


def spread(values):
    return [values] + [swap(values, step) for step in range(1, lax.axis_size("tensor"))]


def send_blocks(partial):
    size = lax.axis_size("tensor")
    blocks = partial.reshape((size, partial.shape[0] // size) + partial.shape[1:])
    return [blocks[0]] + [swap(blocks[step].astype(jnp.bfloat16), step) for step in range(1, size)]


def add_up(blocks):
    total = blocks[0].astype(jnp.float32)
    for block in blocks[1:]:
        total = total + block.astype(jnp.float32)
    return total


def cross(values):
    count = lax.axis_size("dp")
    return lax.ppermute(values, "dp", [(i, i ^ 1) for i in range(count)])


def hop(values, reach, up):
    chips = lax.axis_size("dp") // 2
    pairs = []
    for chip in range(chips):
        target = chip + 1 if up else chip - 1
        far = chip + reach if up else chip - reach
        if 0 <= far < chips:
            pairs += [(2 * chip + core, 2 * target + core) for core in range(2)]
    return lax.ppermute(values, "dp", pairs)


class ChipSum:
    def __init__(self, theirs, mine):
        self.mine, self.crossed = mine, cross(theirs)
        self.chips = mine.shape[0]
        self.left = self.chips - 1
        self.down = self.up = None

    def state(self):
        return [v for v in (self.crossed, self.mine, self.down, self.up) if v is not None]

    def set(self, state):
        state = list(state)
        self.crossed, self.mine = state[:2]
        if self.down is not None:
            self.down, self.up = state[2:]

    def block(self, index):
        total = self.mine[index].astype(jnp.float32) + self.crossed[index].astype(jnp.float32)
        return total

    def advance(self):
        reach = self.left
        down, up = self.block(reach), self.block(self.chips - reach)
        if self.down is not None:
            down = down + self.down.astype(jnp.float32)
            up = up + self.up.astype(jnp.float32)
        self.down = hop(down.astype(jnp.bfloat16), reach, False)
        self.up = hop(up.astype(jnp.bfloat16), reach, True)
        self.left -= 1

    def result(self):
        return self.block(0) + self.down.astype(jnp.float32) + self.up.astype(jnp.float32)


def tables(positions):
    freqs = ROPE_BASE ** (-jnp.arange(0, HEAD_DIM, 2).astype(jnp.float32) / HEAD_DIM)
    angles = positions.astype(jnp.float32)[:, None] * freqs[None, :]
    cosine, sine = jnp.cos(angles), jnp.sin(angles)
    return (
        jnp.concatenate([cosine] * 4, axis=1),
        jnp.concatenate([-sine, sine, -sine, sine], axis=1),
    )


def gather(values, dim):
    return lax.all_gather(values, "dp", axis=dim, tiled=True)


def per_device(
    hidden_in,
    gain_attn,
    w_query,
    w_key,
    w_value,
    w_out,
    gain_mlp,
    w_gate,
    w_up,
    w_down,
    positions,
    cotangent,
):
    size = lax.axis_size("tensor")
    chips = lax.axis_size("dp") // 2
    me = lax.axis_index("tensor")
    me_array = jnp.full((1,), me, jnp.int32)
    spot = lax.axis_index("dp")
    chip, core = spot // 2, spot % 2
    line = (chip - jnp.arange(chips)) % chips
    order = jnp.concatenate([2 * line + (1 - core), 2 * line + core]).astype(jnp.int32)
    q_width, kv_width = w_query.shape[1], w_key.shape[1]
    qkv_width = q_width + 2 * kv_width
    group = q_width // kv_width
    units = w_down.shape[0] // 2

    gains = gather(jnp.stack([gain_attn, gain_mlp]), 1)
    gain_one = gains[0].astype(jnp.float32)
    gain_two = gains[1].astype(jnp.float32)
    attn_full = gather(jnp.concatenate([w_query, w_key, w_value, w_out.T], axis=1), 0)
    blocks_in = spread(hidden_in)
    cosine, sine = tables(positions)
    w_gate, w_up, w_down, attn_full, blocks_in, cosine, sine = barrier(
        (w_gate, w_up, w_down, attn_full, blocks_in, cosine, sine)
    )
    gate_up, down = [], []
    for part in range(2):
        cut = slice(part * units, (part + 1) * units)
        gate_up.append(gather(jnp.concatenate([w_gate[:, cut], w_up[:, cut]], axis=1), 0))
        down.append(gather(w_down[cut], 1))
    out_t = attn_full[:, qkv_width:]

    residual = hidden_in.astype(jnp.float32)
    scale_one = rms_scale(residual)
    tokens_one, query, key_pad, value_pad = project(
        me_array, blocks_in, gain_one[None, :], attn_full, cosine, sine, q_width, kv_width
    )
    attended, log_total = attend(me_array, query, key_pad, value_pad, size, group)
    arrived = send_blocks(mm_nt(attended, out_t))
    middle = residual + add_up(arrived)

    scale_two = rms_scale(middle)
    normed_two = (middle * scale_two * gain_two).astype(jnp.bfloat16)
    tokens_two = spread(normed_two)
    cotangent, tokens_two = barrier((cotangent, tokens_two))
    tokens_two = jnp.concatenate(tokens_two, axis=0)
    cot_full = jnp.concatenate(spread(cotangent), axis=0)

    hidden, gate_grad, up_grad, dn_part, y_part = mlp(
        tokens_two, cot_full, gate_up[0], down[0], size, ()
    )
    first = ChipSum(*mlp_grads(order, tokens_two, cot_full, gate_grad, up_grad, hidden))
    hidden, gate_grad, up_grad, dn_part, y_part = mlp(
        tokens_two, cot_full, gate_up[1], down[1], size, (dn_part, y_part)
    )
    state, dn_part = barrier((first.state(), dn_part))
    first.set(state)
    first.advance()
    arrived = send_blocks(dn_part)
    second = ChipSum(*mlp_grads(order, tokens_two, cot_full, gate_grad, up_grad, hidden))
    state, other, arrived, y_part = barrier((first.state(), second.state(), arrived, y_part))
    first.set(state)
    second.set(other)
    first.advance()
    normed_two_grad = add_up(arrived)
    middle_norm_grad, gain_two_part = norm_back(normed_two_grad, middle, scale_two, gain_two)
    middle_grad = cotangent.astype(jnp.float32) + middle_norm_grad
    branch_blocks = spread(middle_grad.astype(jnp.bfloat16))
    state, branch_blocks, y_part = barrier((first.state(), branch_blocks, y_part))
    first.set(state)
    first.advance()
    branch_grad = jnp.concatenate(branch_blocks, axis=0)
    down_arrived = send_blocks(y_part)

    attended_grad = mm(branch_grad, out_t).astype(jnp.bfloat16)
    state, other, attended_grad = barrier((first.state(), second.state(), attended_grad))
    first.set(state)
    second.set(other)
    second.advance()
    qkv_grad = attend_back(
        me_array,
        query,
        attended_grad,
        log_total,
        key_pad,
        value_pad,
        cosine,
        sine,
        size,
        group,
    )
    state, qkv_grad, down_arrived = barrier((second.state(), qkv_grad, down_arrived))
    second.set(state)
    second.advance()
    out = (middle + add_up(down_arrived)).astype(jnp.bfloat16)
    third = ChipSum(
        *attn_grads(
            order,
            tokens_one,
            branch_grad,
            qkv_grad,
            attended,
            attn_full,
            gain_one[:, None],
            gain_two_part[:, None],
        )
    )
    normed_part = mm_nt(qkv_grad, attn_full[:, :qkv_width])
    state, other, normed_part = barrier((second.state(), third.state(), normed_part))
    second.set(state)
    third.set(other)
    second.advance()
    arrived = send_blocks(normed_part)
    for _ in range(chips - 1):
        third.advance()
    while second.left:
        second.advance()
    while first.left:
        first.advance()
    normed_one_grad = add_up(arrived)
    input_norm_grad, _ = norm_back(normed_one_grad, residual, scale_one, gain_one)
    grad_in = middle_grad + input_norm_grad

    halves = [first.result(), second.result()]
    grad_gate = jnp.concatenate([h[:, :units] for h in halves], axis=1)
    grad_up = jnp.concatenate([h[:, units : 2 * units] for h in halves], axis=1)
    grad_down = jnp.concatenate([h[:, 2 * units :].T for h in halves], axis=0)
    attn_sums = third.result()
    gain_sums = attn_sums[:, qkv_width + q_width : qkv_width + q_width + 2]
    gain_blocks = gain_sums.reshape(size, -1, 2)
    gain_own = lax.dynamic_index_in_dim(gain_blocks, me, 0, keepdims=False)
    for step in range(1, size):
        other = lax.dynamic_index_in_dim(gain_blocks, me ^ step, 0, keepdims=False)
        gain_own = gain_own + swap(other, step)
    return (
        out,
        grad_in,
        gain_own[:, 0],
        attn_sums[:, :q_width],
        attn_sums[:, q_width : q_width + kv_width],
        attn_sums[:, q_width + kv_width : qkv_width],
        attn_sums[:, qkv_width : qkv_width + q_width].T,
        gain_own[:, 1],
        grad_gate,
        grad_up,
        grad_down,
    )


def solution(mesh):
    return jax.shard_map(
        per_device,
        mesh=mesh,
        in_specs=(
            P(("dp", "tensor"), None),
            P("dp"),
            P("dp", "tensor"),
            P("dp", "tensor"),
            P("dp", "tensor"),
            P("tensor", "dp"),
            P("dp"),
            P("dp", "tensor"),
            P("dp", "tensor"),
            P("tensor", "dp"),
            P("dp"),
            P(("dp", "tensor"), None),
        ),
        out_specs=(
            P(("dp", "tensor"), None),
            P(("dp", "tensor"), None),
            P(("dp", "tensor")),
            P("dp", "tensor"),
            P("dp", "tensor"),
            P("dp", "tensor"),
            P("tensor", "dp"),
            P(("dp", "tensor")),
            P("dp", "tensor"),
            P("dp", "tensor"),
            P("tensor", "dp"),
        ),
        check_vma=False,
    )
```

```python
import functools
import math

import jax
import jax.numpy as jnp
from jax import lax
from jax.experimental import pallas as pl
from jax.experimental.pallas import tpu as pltpu
from jax.sharding import PartitionSpec as P

HEAD_DIM = 64
PAIR = 2 * HEAD_DIM
SEQ_LEN = 1024


EPS = 1e-05
ROPE_BASE = 500000.0
SCALE = 1.0 / math.sqrt(HEAD_DIM)
PARAMS = pltpu.CompilerParams(vmem_limit_bytes=58 * 2**20)
ONCE = pl.Buffered(1)

barrier = lax.optimization_barrier


def rms_scale(values):
    return lax.rsqrt(jnp.mean(values * values, axis=-1, keepdims=True) + EPS)


def norm_back(grad, values, scale, gain):
    inner = grad * gain
    cubed = scale * scale * scale
    result = scale * inner - values * cubed * jnp.mean(inner * values, axis=-1, keepdims=True)
    return (result, jnp.sum(grad * values * scale, axis=0))


def mm(left, right):
    return jnp.dot(left, right, preferred_element_type=jnp.float32)


def mm_nt(left, right):
    return lax.dot_general(left, right, (((1,), (1,)), ((), ())), preferred_element_type=jnp.float32)


def mm_tn(left, right):
    return lax.dot_general(left, right, (((0,), (0,)), ((), ())), preferred_element_type=jnp.float32)


def lane_index(rows):
    return lax.broadcasted_iota(jnp.int32, (rows, PAIR), 1)


def turn(pair, cosine, sine):
    lower = lane_index(pair.shape[0]) % HEAD_DIM < HEAD_DIM // 2
    other = jnp.where(
        lower, pltpu.roll(pair, PAIR - HEAD_DIM // 2, 1), pltpu.roll(pair, HEAD_DIM // 2, 1)
    )
    return pair * cosine + other * sine


def project_kernel(place_ref, *refs, size, q_width, kv_width):
    x_refs = refs[:size]
    gain_ref, wo_ref, wx_ref, cos_ref, sin_ref, n_ref, q_ref, k_ref, v_ref = refs[size:]
    rows = q_ref.shape[0]
    half = wo_ref.shape[0]

    def one(x_ref):
        x = x_ref[...].astype(jnp.float32)
        normed = (x * rms_scale(x) * gain_ref[...]).astype(jnp.bfloat16)
        n_ref[...] = normed
        cosine, sine = cos_ref[...], sin_ref[...]
        lin = mm(normed[:, :half], wo_ref[...]) + mm(normed[:, half:], wx_ref[...])
        for low in range(0, q_width, PAIR):
            query = turn(lin[:, low : low + PAIR], cosine, sine).astype(jnp.bfloat16)
            q_ref[:, low : low + PAIR] = query * jnp.bfloat16(SCALE)
        first = lane_index(rows) < HEAD_DIM
        for ref, start, rotate in ((k_ref, q_width, True), (v_ref, q_width + kv_width, False)):
            for head in range(kv_width // HEAD_DIM):
                low = start + head * HEAD_DIM
                block = lin[:, low // PAIR * PAIR : low // PAIR * PAIR + PAIR]
                if rotate:
                    block = turn(block, cosine, sine)
                moved = pltpu.roll(block, HEAD_DIM, 1)
                if low % PAIR:
                    block, moved = moved, block
                ref[head, 0] = jnp.where(first, block, 0.0).astype(jnp.bfloat16)
                ref[head, 1] = jnp.where(first, 0.0, moved).astype(jnp.bfloat16)

    for step in range(size):
        pl.when(pl.program_id(0) == step)(functools.partial(one, x_refs[step]))


def project(me, blocks, gain, own, other, cosine, sine, q_width, kv_width):
    size = len(blocks)
    rows, features = blocks[0].shape
    total = rows * size
    key_heads = kv_width // HEAD_DIM
    width = q_width + 2 * kv_width
    fixed = lambda p, m: (0, 0)
    placed = lambda p, m: (jnp.bitwise_xor(p, m[0]), 0)
    padded = pl.BlockSpec(
        (key_heads, 2, rows, PAIR), lambda p, m: (0, 0, jnp.bitwise_xor(p, m[0]), 0)
    )
    spec = pltpu.PrefetchScalarGridSpec(
        num_scalar_prefetch=1,
        grid=(size,),
        in_specs=[pl.BlockSpec((rows, features), fixed, pipeline_mode=ONCE)] * size
        + [
            pl.BlockSpec((1, features), fixed),
            pl.BlockSpec((features // 2, width), fixed, pipeline_mode=ONCE),
            pl.BlockSpec((features // 2, width), fixed, pipeline_mode=ONCE),
            pl.BlockSpec((rows, PAIR), placed),
            pl.BlockSpec((rows, PAIR), placed),
        ],
        out_specs=[
            pl.BlockSpec((rows, features), lambda p, m: (p, 0)),
            pl.BlockSpec((rows, q_width), lambda p, m: (p, 0)),
            padded,
            padded,
        ],
    )
    padded_shape = jax.ShapeDtypeStruct((key_heads, 2, total, PAIR), jnp.bfloat16)
    return pl.pallas_call(
        functools.partial(project_kernel, size=size, q_width=q_width, kv_width=kv_width),
        grid_spec=spec,
        out_shape=[
            jax.ShapeDtypeStruct((total, features), jnp.bfloat16),
            jax.ShapeDtypeStruct((total, q_width), jnp.bfloat16),
            padded_shape,
            padded_shape,
        ],
        compiler_params=PARAMS,
        cost_estimate=pl.CostEstimate(
            flops=2 * total * features * width,
            bytes_accessed=4 * total * features + 2 * features * width,
            transcendentals=0,
        ),
    )(me, *blocks, gain, own, other, cosine, sine)


def attend_kernel(
    me_ref, q_ref, k_ref, v_ref, wo_ref, wx_ref, o_ref, l_ref, *refs, size, heads, group
):
    part_refs, vt_ref = refs[:size], refs[size]
    rows = q_ref.shape[0]
    half = wo_ref.shape[0]
    mine = jnp.bitwise_xor(me_ref[0], pl.program_id(0))
    key_place = lax.broadcasted_iota(jnp.int32, (rows, rows), 0)
    query_place = lax.broadcasted_iota(jnp.int32, (rows, rows), 1)

    @pl.when(pl.program_id(0) == 0)
    def _():
        for head in range(heads // group):
            for side in range(2):
                vt_ref[head, side] = v_ref[head, side].T

    def one(span):
        keys = span * rows
        for pair in range(heads // 2):
            head = 2 * pair // group
            lanes = slice(pair * PAIR, (pair + 1) * PAIR)
            query = q_ref[:, lanes]
            acc = None
            inverse = []
            for side in range(2):
                diag = mm_nt(k_ref[head, side, keys : keys + rows, :], query)
                diag = jnp.where(key_place <= query_place, diag, -1e9)
                top = jnp.max(diag, axis=0, keepdims=True)
                if span:
                    body = mm_nt(k_ref[head, side, :keys, :], query)
                    top = jnp.maximum(top, jnp.max(body, axis=0, keepdims=True))
                diag = jnp.exp(diag - top)
                total = jnp.sum(diag, axis=0, keepdims=True)
                part = mm(vt_ref[head, side, :, keys : keys + rows], diag.astype(jnp.bfloat16))
                if span:
                    body = jnp.exp(body - top)
                    total = total + jnp.sum(body, axis=0, keepdims=True)
                    part = part + mm(vt_ref[head, side, :, :keys], body.astype(jnp.bfloat16))
                acc = part if acc is None else acc + part
                inverse.append(jnp.broadcast_to(1.0 / total, (HEAD_DIM, rows)))
                l_ref[2 * pair + side : 2 * pair + side + 1, :] = top + jnp.log(total)
            acc = acc * jnp.concatenate(inverse, axis=0)
            o_ref[:, lanes] = acc.T.astype(jnp.bfloat16)

    for span in range(size):
        pl.when(mine == span)(functools.partial(one, span))

    def project_out(ref):
        ref[:, :half] = mm_nt(o_ref[...], wo_ref[...]).astype(jnp.bfloat16)
        ref[:, half:] = mm_nt(o_ref[...], wx_ref[...]).astype(jnp.bfloat16)

    for step in range(size):
        pl.when(pl.program_id(0) == step)(functools.partial(project_out, part_refs[step]))


def attend(me, query, key_pad, value_pad, own, other, size, group):
    total, width = query.shape
    features = 2 * own.shape[0]
    rows, heads = total // size, width // HEAD_DIM
    whole = pl.BlockSpec(key_pad.shape, lambda p, m: (0, 0, 0, 0), pipeline_mode=ONCE)
    spec = pltpu.PrefetchScalarGridSpec(
        num_scalar_prefetch=1,
        grid=(size,),
        in_specs=[pl.BlockSpec((rows, width), lambda p, m: (p, 0)), whole, whole]
        + [pl.BlockSpec(own.shape, lambda p, m: (0, 0), pipeline_mode=ONCE)] * 2,
        out_specs=[
            pl.BlockSpec((rows, width), lambda p, m: (p, 0)),
            pl.BlockSpec((heads, rows), lambda p, m: (0, p)),
        ]
        + [pl.BlockSpec((rows, features), lambda p, m: (0, 0))] * size,
        scratch_shapes=[pltpu.VMEM((heads // group, 2, PAIR, total), jnp.bfloat16)],
    )
    return pl.pallas_call(
        functools.partial(attend_kernel, size=size, heads=heads, group=group),
        grid_spec=spec,
        out_shape=[
            jax.ShapeDtypeStruct((total, width), jnp.bfloat16),
            jax.ShapeDtypeStruct((heads, total), jnp.float32),
        ]
        + [jax.ShapeDtypeStruct((rows, features), jnp.bfloat16)] * size,
        compiler_params=PARAMS,
        cost_estimate=pl.CostEstimate(
            flops=8 * heads * total * total * HEAD_DIM,
            bytes_accessed=8 * total * width,
            transcendentals=heads * total * total,
        ),
    )(me, query, key_pad, value_pad, own, other)


def attend_back_kernel(
    me_ref, q_ref, l_ref, k_ref, v_ref, cos_ref, sin_ref, wo_ref, wx_ref, *refs, size, heads, group
):
    e_refs = refs[:size]
    out_ref, dk_ref, dv_ref, kt_ref, do_ref = refs[size:]
    half = wo_ref.shape[0]
    rows = q_ref.shape[0]
    key_heads = heads // group
    step = pl.program_id(0)
    me = me_ref[0]
    mine = jnp.bitwise_xor(me, step)
    key_place = lax.broadcasted_iota(jnp.int32, (rows, rows), 0)
    query_place = lax.broadcasted_iota(jnp.int32, (rows, rows), 1)

    def rows_of(block):
        return pl.ds(pl.multiple_of(block * rows, rows), rows)

    @pl.when(step == 0)
    def _():
        dk_ref[...] = jnp.zeros_like(dk_ref)
        dv_ref[...] = jnp.zeros_like(dv_ref)
        for head in range(key_heads):
            for side in range(2):
                kt_ref[head, side] = k_ref[head, side].T

    def attended_grad(ref):
        grad = mm(ref[:, :half], wo_ref[...]) + mm(ref[:, half:], wx_ref[...])
        do_ref[...] = grad.astype(jnp.bfloat16)

    for block in range(size):
        pl.when(step == block)(functools.partial(attended_grad, e_refs[block]))

    def one(span):
        keys = span * rows
        parts = [(keys, keys + rows, True)] + ([(0, keys, False)] if span else [])
        cosine, sine = cos_ref[keys : keys + rows, :], sin_ref[keys : keys + rows, :]
        for pair in range(heads // 2):
            head = 2 * pair // group
            lanes = slice(pair * PAIR, (pair + 1) * PAIR)
            query, grad = q_ref[:, lanes], do_ref[:, lanes]
            acc = None
            for side in range(2):
                log_total = l_ref[2 * pair + side : 2 * pair + side + 1, :]
                inner = None
                kept = []
                for low, high, diagonal in parts:
                    probs = mm_nt(k_ref[head, side, low:high, :], query)
                    probs = jnp.exp(probs - log_total)
                    if diagonal:
                        probs = jnp.where(key_place <= query_place, probs, 0.0)
                    prob_grad = mm_nt(v_ref[head, side, low:high, :], grad)
                    dv_ref[head, side, low:high, :] += mm(probs.astype(jnp.bfloat16), grad)
                    term = jnp.sum(probs * prob_grad, axis=0, keepdims=True)
                    inner = term if inner is None else inner + term
                    kept.append((low, high, probs, prob_grad))
                for low, high, probs, prob_grad in kept:
                    score_grad = (probs * (prob_grad - inner)).astype(jnp.bfloat16)
                    dk_ref[head, side, low:high, :] += mm(score_grad, query)
                    part = mm(kt_ref[head, side, :, low:high], score_grad)
                    acc = part if acc is None else acc + part
            turned = turn(acc.T * SCALE, cosine, -sine)
            out_ref[rows_of(step), lanes] = turned.astype(jnp.bfloat16)

    for span in range(size):
        pl.when(mine == span)(functools.partial(one, span))

    @pl.when(step == size - 1)
    def _():
        first = lane_index(rows) < HEAD_DIM
        wanted = [(dk_ref, head, True) for head in range(key_heads)]
        wanted += [(dv_ref, head, False) for head in range(key_heads)]
        for span in range(size):
            place = slice(span * rows, (span + 1) * rows)
            cosine, sine = cos_ref[place, :], sin_ref[place, :]
            for block in range(len(wanted) // 2):
                halves, rotate = [], []
                for half in range(2):
                    ref, head, is_key = wanted[2 * block + half]
                    low, high = ref[head, 0, place, :], ref[head, 1, place, :]
                    if half:
                        halves.append(pltpu.roll(low, HEAD_DIM, 1) + high)
                    else:
                        halves.append(low + pltpu.roll(high, HEAD_DIM, 1))
                    rotate.append(is_key)
                value = jnp.where(first, halves[0], halves[1])
                if rotate[0] and rotate[1]:
                    value = turn(value, cosine, -sine)
                elif rotate[0]:
                    value = jnp.where(first, turn(value, cosine, -sine), value)
                start = heads * HEAD_DIM + block * PAIR
                target = rows_of(jnp.bitwise_xor(me, span))
                out_ref[target, start : start + PAIR] = value.astype(jnp.bfloat16)


def attend_back(
    me, query, log_total, key_pad, value_pad, cosine, sine, own, other, branch_blocks, group
):
    total, width = query.shape
    size = len(branch_blocks)
    rows, heads = total // size, width // HEAD_DIM
    key_heads = heads // group
    out_width = width + 2 * key_heads * HEAD_DIM
    whole = pl.BlockSpec(key_pad.shape, lambda p, m: (0, 0, 0, 0), pipeline_mode=ONCE)
    table = pl.BlockSpec((total, PAIR), lambda p, m: (0, 0), pipeline_mode=ONCE)
    spec = pltpu.PrefetchScalarGridSpec(
        num_scalar_prefetch=1,
        grid=(size,),
        in_specs=[
            pl.BlockSpec((rows, width), lambda p, m: (p, 0)),
            pl.BlockSpec((heads, rows), lambda p, m: (0, p)),
            whole,
            whole,
            table,
            table,
        ]
        + [pl.BlockSpec(own.shape, lambda p, m: (0, 0), pipeline_mode=ONCE)] * 2
        + [pl.BlockSpec(branch_blocks[0].shape, lambda p, m: (0, 0), pipeline_mode=ONCE)] * size,
        out_specs=pl.BlockSpec((total, out_width), lambda p, m: (0, 0)),
        scratch_shapes=[
            pltpu.VMEM(key_pad.shape, jnp.float32),
            pltpu.VMEM(key_pad.shape, jnp.float32),
            pltpu.VMEM((key_heads, 2, PAIR, total), jnp.bfloat16),
            pltpu.VMEM((rows, width), jnp.bfloat16),
        ],
    )
    return pl.pallas_call(
        functools.partial(attend_back_kernel, size=size, heads=heads, group=group),
        grid_spec=spec,
        out_shape=jax.ShapeDtypeStruct((total, out_width), jnp.bfloat16),
        compiler_params=PARAMS,
        cost_estimate=pl.CostEstimate(
            flops=20 * heads * total * total * HEAD_DIM,
            bytes_accessed=16 * total * width,
            transcendentals=heads * total * total,
        ),
    )(me, query, log_total, key_pad, value_pad, cosine, sine, own, other, *branch_blocks)


def mlp_kernel(*refs, size, adds):
    n_refs, e_refs = refs[:size], refs[size : 2 * size]
    gate_o, up_o, down_o, gate_x, up_x, down_x = refs[2 * size : 2 * size + 6]
    h_ref, dg_ref, du_ref, dn_ref, y_ref, n_ref, e_ref = refs[-7:]
    half = gate_o.shape[0]

    def fetch(step):
        n_ref[...] = n_refs[step][...]
        e_ref[...] = e_refs[step][...]

    for step in range(size):
        pl.when(pl.program_id(0) == step)(functools.partial(fetch, step))
    gate = mm(n_ref[:, :half], gate_o[...]) + mm(n_ref[:, half:], gate_x[...])
    up = mm(n_ref[:, :half], up_o[...]) + mm(n_ref[:, half:], up_x[...])
    grad = mm(e_ref[:, :half], down_o[...]) + mm(e_ref[:, half:], down_x[...])
    sigma = jax.nn.sigmoid(gate)
    silu = gate * sigma
    hidden = (silu * up).astype(jnp.bfloat16)
    gate_grad = (grad * up * sigma * (1.0 + gate * (1.0 - sigma))).astype(jnp.bfloat16)
    up_grad = (grad * silu).astype(jnp.bfloat16)
    h_ref[...] = hidden
    dg_ref[...] = gate_grad
    du_ref[...] = up_grad
    for part, gate_w, up_w, down_w in ((0, gate_o, up_o, down_o), (1, gate_x, up_x, down_x)):
        lanes = slice(part * half, (part + 1) * half)
        dn = mm_nt(gate_grad, gate_w[...]) + mm_nt(up_grad, up_w[...])
        y = mm_nt(hidden, down_w[...])
        if adds:
            dn = dn + refs[2 * size + 6][:, lanes].astype(jnp.float32)
            y = y + refs[2 * size + 7][:, lanes].astype(jnp.float32)
        dn_ref[:, lanes] = dn.astype(dn_ref.dtype)
        y_ref[:, lanes] = y.astype(y_ref.dtype)


def mlp(tokens, cot, own, other, earlier):
    size = len(tokens)
    rows, features = tokens[0].shape
    half, units = own.shape[0], own.shape[1] // 3
    total = rows * size
    fixed = lambda p: (0, 0)
    moving = lambda p: (p, 0)
    wide = pl.BlockSpec((rows, features), moving)
    narrow = pl.BlockSpec((rows, units), moving)
    sums = jax.ShapeDtypeStruct((total, features), jnp.bfloat16)
    thin = jax.ShapeDtypeStruct((total, units), jnp.bfloat16)
    block = pl.BlockSpec((rows, features), fixed, pipeline_mode=ONCE)
    thirds = [
        pl.BlockSpec((half, units), lambda p, t=t: (0, t), pipeline_mode=ONCE) for t in range(3)
    ]
    return pl.pallas_call(
        functools.partial(mlp_kernel, size=size, adds=bool(earlier)),
        grid=(size,),
        in_specs=[block] * (2 * size)
        + thirds * 2
        + [wide] * len(earlier),
        out_specs=[narrow, narrow, narrow, wide, wide],
        out_shape=[thin, thin, thin, sums, sums],
        scratch_shapes=[pltpu.VMEM((rows, features), jnp.bfloat16)] * 2,
        compiler_params=PARAMS,
        cost_estimate=pl.CostEstimate(
            flops=12 * total * features * units,
            bytes_accessed=6 * features * units + 20 * total * features,
            transcendentals=total * units,
        ),
    )(*tokens, *cot, own, own, own, other, other, other, *earlier)


def column_grad(blocks, values, lanes=slice(None)):
    rows = blocks[0].shape[0]
    total = None
    for index, block in enumerate(blocks):
        part = mm_tn(block[...], values[index * rows : (index + 1) * rows, lanes])
        total = part if total is None else total + part
    return total


def grad_kernel(order_ref, *refs, size):
    n_refs, e_refs = refs[:size], refs[size : 2 * size]
    dg_ref, du_ref, h_ref, theirs_ref, mine_ref = refs[2 * size :]
    units = dg_ref.shape[1]
    count = pl.num_programs(0)

    def one(ref):
        ref[0, :, :units] = column_grad(n_refs, dg_ref).astype(jnp.bfloat16)
        ref[0, :, units : 2 * units] = column_grad(n_refs, du_ref).astype(jnp.bfloat16)
        ref[0, :, 2 * units :] = column_grad(e_refs, h_ref).astype(jnp.bfloat16)

    pl.when(pl.program_id(0) < count // 2)(lambda: one(theirs_ref))
    pl.when(pl.program_id(0) >= count // 2)(lambda: one(mine_ref))


def split_specs(count, depth, width):
    half = count // 2
    shape = jax.ShapeDtypeStruct((half, depth, width), jnp.bfloat16)
    theirs = pl.BlockSpec((1, depth, width), lambda b, o: (jnp.minimum(b, half - 1), 0, 0))
    mine = pl.BlockSpec((1, depth, width), lambda b, o: (jnp.maximum(b - half, 0), 0, 0))
    return [theirs, mine], [shape, shape]


def mlp_grads(order, tokens, cot, gate_grad, up_grad, hidden):
    size = len(tokens)
    rows, features = tokens[0].shape
    total, units = hidden.shape
    count = order.shape[0]
    depth = features // count
    column = pl.BlockSpec((rows, depth), lambda b, o: (0, o[b]))
    fixed = pl.BlockSpec((total, units), lambda b, o: (0, 0), pipeline_mode=ONCE)
    out_specs, out_shape = split_specs(count, depth, 3 * units)
    return pl.pallas_call(
        functools.partial(grad_kernel, size=size),
        grid_spec=pltpu.PrefetchScalarGridSpec(
            num_scalar_prefetch=1,
            grid=(count,),
            in_specs=[column] * (2 * size) + [fixed, fixed, fixed],
            out_specs=out_specs,
        ),
        out_shape=out_shape,
        compiler_params=PARAMS,
        cost_estimate=pl.CostEstimate(
            flops=6 * total * features * units,
            bytes_accessed=4 * total * features + 6 * features * units + 6 * total * units,
            transcendentals=0,
        ),
    )(order, *tokens, *cot, gate_grad, up_grad, hidden)


def attn_grad_kernel(order_ref, n_ref, *refs, size):
    e_refs = refs[:size]
    d_ref, o_ref, wo_ref, wx_ref, g1_ref, g2_ref, theirs_ref, mine_ref = refs[size:]
    width, out_width = d_ref.shape[1], o_ref.shape[1]
    count = pl.num_programs(0)

    def one(ref, w_ref):
        grad = mm_tn(n_ref[...], d_ref[...])
        ref[0, :, :width] = grad.astype(jnp.bfloat16)
        ref[0, :, width : width + out_width] = column_grad(e_refs, o_ref).astype(jnp.bfloat16)
        first = jnp.sum(grad * w_ref[...].astype(jnp.float32), axis=1, keepdims=True) / g1_ref[...]
        lane = lane_index(grad.shape[0])
        both = jnp.where(lane == 0, first, jnp.where(lane == 1, g2_ref[...], 0.0))
        ref[0, :, width + out_width :] = both.astype(jnp.bfloat16)

    pl.when(pl.program_id(0) < count // 2)(lambda: one(theirs_ref, wx_ref))
    pl.when(pl.program_id(0) >= count // 2)(lambda: one(mine_ref, wo_ref))


def attn_grads(order, tokens, branch, qkv_grad, attended, own, other, gain_one, gain_two_part):
    size = len(branch)
    total, features = tokens.shape
    rows = total // size
    width, out_width = qkv_grad.shape[1], attended.shape[1]
    count = order.shape[0]
    half = count // 2
    depth = features // count
    fixed = lambda b, o: (0, 0)
    row = lambda b, o: (o[b], 0)
    out_specs, out_shape = split_specs(count, depth, width + out_width + PAIR)
    return pl.pallas_call(
        functools.partial(attn_grad_kernel, size=size),
        grid_spec=pltpu.PrefetchScalarGridSpec(
            num_scalar_prefetch=1,
            grid=(count,),
            in_specs=[pl.BlockSpec((total, depth), lambda b, o: (0, o[b]))]
            + [pl.BlockSpec((rows, depth), lambda b, o: (0, o[b]))] * size
            + [
                pl.BlockSpec((total, width), fixed, pipeline_mode=ONCE),
                pl.BlockSpec((total, out_width), fixed, pipeline_mode=ONCE),
                pl.BlockSpec((depth, width), lambda b, o: (jnp.where(b < half, 0, o[b]), 0)),
                pl.BlockSpec((depth, width), lambda b, o: (jnp.where(b < half, o[b] - half, 0), 0)),
                pl.BlockSpec((depth, 1), row),
                pl.BlockSpec((depth, 1), row),
            ],
            out_specs=out_specs,
        ),
        out_shape=out_shape,
        compiler_params=PARAMS,
        cost_estimate=pl.CostEstimate(
            flops=2 * total * features * (width + out_width),
            bytes_accessed=4 * total * features + 4 * features * (width + out_width),
            transcendentals=0,
        ),
    )(order, tokens, *branch, qkv_grad, attended, own, other, gain_one, gain_two_part)


def swap(values, step):
    size = lax.axis_size("tensor")
    return lax.ppermute(values, "tensor", [(i, i ^ step) for i in range(size)])


def spread(values):
    return [values] + [swap(values, step) for step in range(1, lax.axis_size("tensor"))]


def send_blocks(blocks):
    return [blocks[0]] + [swap(block, step + 1) for step, block in enumerate(blocks[1:])]


def send_rows(partial):
    size = lax.axis_size("tensor")
    return send_blocks(list(partial.reshape((size, -1) + partial.shape[1:])))


def add_up(blocks):
    total = blocks[0].astype(jnp.float32)
    for block in blocks[1:]:
        total = total + block.astype(jnp.float32)
    return total


def cross(values):
    count = lax.axis_size("dp")
    return lax.ppermute(values, "dp", [(i, i ^ 1) for i in range(count)])


def hop(values, reach, up):
    chips = lax.axis_size("dp") // 2
    pairs = []
    for chip in range(chips):
        target = chip + 1 if up else chip - 1
        far = chip + reach if up else chip - reach
        if 0 <= far < chips:
            pairs += [(2 * chip + core, 2 * target + core) for core in range(2)]
    return lax.ppermute(values, "dp", pairs)


class ChipSum:
    def __init__(self, theirs, mine):
        self.mine, self.crossed = mine, cross(theirs)
        self.chips = mine.shape[0]
        self.left = self.chips - 1
        self.down = self.up = None

    def state(self):
        return [v for v in (self.crossed, self.mine, self.down, self.up) if v is not None]

    def set(self, state):
        state = list(state)
        self.crossed, self.mine = state[:2]
        if self.down is not None:
            self.down, self.up = state[2:]

    def block(self, index):
        total = self.mine[index].astype(jnp.float32) + self.crossed[index].astype(jnp.float32)
        return total

    def advance(self):
        reach = self.left
        down, up = self.block(reach), self.block(self.chips - reach)
        if self.down is not None:
            down = down + self.down.astype(jnp.float32)
            up = up + self.up.astype(jnp.float32)
        self.down = hop(down.astype(jnp.bfloat16), reach, False)
        self.up = hop(up.astype(jnp.bfloat16), reach, True)
        self.left -= 1

    def result(self):
        return self.block(0) + self.down.astype(jnp.float32) + self.up.astype(jnp.float32)


def tables(positions):
    freqs = ROPE_BASE ** (-jnp.arange(0, HEAD_DIM, 2).astype(jnp.float32) / HEAD_DIM)
    angles = positions.astype(jnp.float32)[:, None] * freqs[None, :]
    cosine, sine = jnp.cos(angles), jnp.sin(angles)
    return (
        jnp.concatenate([cosine] * 4, axis=1),
        jnp.concatenate([-sine, sine, -sine, sine], axis=1),
    )


def gather(values, dim):
    count = lax.axis_size("dp")
    groups = [list(range(core, count, 2)) for core in range(2)]
    return lax.all_gather(values, "dp", axis=dim, tiled=True, axis_index_groups=groups)


def feature_blocks(values):
    width = values.shape[-1] // lax.axis_size("dp")
    return [values[..., low : low + width] for low in range(0, values.shape[-1], width)]


def by_core(values, core):
    blocks = feature_blocks(values)
    pairs = list(zip(blocks[0::2], blocks[1::2]))
    own = [jnp.where(core == 0, even, odd) for even, odd in pairs]
    other = [jnp.where(core == 0, odd, even) for even, odd in pairs]
    return jnp.concatenate(own + other, axis=-1)


def by_device(values, core):
    blocks = feature_blocks(values)
    chips = len(blocks) // 2
    placed = []
    for own, other in zip(blocks[:chips], blocks[chips:]):
        placed += [jnp.where(core == 0, own, other), jnp.where(core == 0, other, own)]
    return jnp.concatenate(placed, axis=-1)


def per_device(
    hidden_in,
    gain_attn,
    w_query,
    w_key,
    w_value,
    w_out,
    gain_mlp,
    w_gate,
    w_up,
    w_down,
    positions,
    cotangent,
):
    size = lax.axis_size("tensor")
    chips = lax.axis_size("dp") // 2
    me = lax.axis_index("tensor")
    me_array = jnp.full((1,), me, jnp.int32)
    spot = lax.axis_index("dp")
    chip, core = spot // 2, spot % 2
    line = (chip - jnp.arange(chips)) % chips
    order = jnp.concatenate([line + chips, line]).astype(jnp.int32)
    q_width, kv_width = w_query.shape[1], w_key.shape[1]
    qkv_width = q_width + 2 * kv_width
    group = q_width // kv_width
    units = w_down.shape[0] // 2

    gains = lax.all_gather(jnp.stack([gain_attn, gain_mlp]), "dp", axis=1, tiled=True)
    gains = by_core(gains, core).astype(jnp.float32)
    qkv_own = gather(jnp.concatenate([w_query, w_key, w_value], axis=1), 0)
    out_own = gather(w_out.T, 0)
    residual = by_core(hidden_in, core)
    blocks_in = spread(residual)
    residual = residual.astype(jnp.float32)
    cosine, sine = tables(positions)
    cotangent = by_core(cotangent, core)
    down_t = w_down.T
    shares = []
    for part in range(2):
        cut = slice(part * units, (part + 1) * units)
        shares.append(jnp.concatenate([w_gate[:, cut], w_up[:, cut], down_t[:, cut]], axis=1))
    shares, qkv_own, out_own, blocks_in, cosine, sine, gains, cotangent = barrier(
        (shares, qkv_own, out_own, blocks_in, cosine, sine, gains, cotangent)
    )
    cot_blocks = spread(cotangent)
    gain_one, gain_two = gains[0], gains[1]
    mlp_own = [gather(share, 0) for share in shares]
    qkv = (qkv_own, cross(qkv_own))
    out_t = (out_own, cross(out_own))

    scale_one = rms_scale(residual)
    tokens_one, query, key_pad, value_pad = project(
        me_array, blocks_in, gain_one[None, :], *qkv, cosine, sine, q_width, kv_width
    )
    attended, log_total, *parts = attend(
        me_array, query, key_pad, value_pad, *out_t, size, group
    )
    parts, cot_blocks = barrier((parts, cot_blocks))
    arrived = send_blocks(parts)
    middle = residual + add_up(arrived)

    scale_two = rms_scale(middle)
    normed_two = (middle * scale_two * gain_two).astype(jnp.bfloat16)
    tokens_two = spread(normed_two)

    weights = (mlp_own[0], cross(mlp_own[0]))
    tokens_two, weights = barrier((tokens_two, weights))
    hidden, gate_grad, up_grad, dn_part, y_part = mlp(tokens_two, cot_blocks, *weights, ())
    first = ChipSum(*mlp_grads(order, tokens_two, cot_blocks, gate_grad, up_grad, hidden))
    weights = (mlp_own[1], cross(mlp_own[1]))
    state, weights = barrier((first.state(), weights))
    first.set(state)
    first.advance()
    hidden, gate_grad, up_grad, dn_part, y_part = mlp(
        tokens_two, cot_blocks, *weights, (dn_part, y_part)
    )
    state, dn_part, hidden = barrier((first.state(), dn_part, hidden))
    first.set(state)
    first.advance()
    arrived = send_rows(dn_part)
    grads = mlp_grads(order, tokens_two, cot_blocks, gate_grad, up_grad, hidden)
    state, grads, arrived, y_part = barrier((first.state(), grads, arrived, y_part))
    first.set(state)
    second = ChipSum(*grads)
    first.advance()
    second.advance()
    normed_two_grad = add_up(arrived)
    middle_norm_grad, gain_two_part = norm_back(normed_two_grad, middle, scale_two, gain_two)
    middle_grad = cotangent.astype(jnp.float32) + middle_norm_grad
    branch_blocks = spread(middle_grad.astype(jnp.bfloat16))
    branch_blocks, y_part, state, other = barrier(
        (branch_blocks, y_part, first.state(), second.state())
    )
    first.set(state)
    second.set(other)
    second.advance()
    down_arrived = send_rows(y_part)
    qkv_grad = attend_back(
        me_array,
        query,
        log_total,
        key_pad,
        value_pad,
        cosine,
        sine,
        *out_t,
        branch_blocks,
        group,
    )
    state, qkv_grad, down_arrived = barrier((second.state(), qkv_grad, down_arrived))
    second.set(state)
    second.advance()
    out = (middle + add_up(down_arrived)).astype(jnp.bfloat16)
    normed_part = jnp.concatenate([mm_nt(qkv_grad, w) for w in qkv], axis=1).astype(jnp.bfloat16)
    arrived = send_rows(normed_part)
    grads = attn_grads(
        order,
        tokens_one,
        branch_blocks,
        qkv_grad,
        attended,
        *qkv,
        gain_one[:, None],
        gain_two_part[:, None],
    )
    grads, out = barrier((grads, out))
    third = ChipSum(*grads)
    third.advance()
    other, arrived = barrier((third.state(), arrived))
    third.set(other)
    while third.left:
        third.advance()
    while second.left:
        second.advance()
    while first.left:
        first.advance()
    normed_one_grad = add_up(arrived)
    input_norm_grad, _ = norm_back(normed_one_grad, residual, scale_one, gain_one)
    grad_in = middle_grad + input_norm_grad

    halves = [first.result(), second.result()]
    grad_gate = jnp.concatenate([h[:, :units] for h in halves], axis=1)
    grad_up = jnp.concatenate([h[:, units : 2 * units] for h in halves], axis=1)
    grad_down = jnp.concatenate([h[:, 2 * units :].T for h in halves], axis=0)
    attn_sums = third.result()
    gain_sums = attn_sums[:, qkv_width + q_width : qkv_width + q_width + 2]
    gain_blocks = gain_sums.reshape(size, -1, 2)
    gain_own = lax.dynamic_index_in_dim(gain_blocks, me, 0, keepdims=False)
    for step in range(1, size):
        other = lax.dynamic_index_in_dim(gain_blocks, me ^ step, 0, keepdims=False)
        gain_own = gain_own + swap(other, step)
    return (
        by_device(out, core),
        by_device(grad_in, core),
        gain_own[:, 0],
        attn_sums[:, :q_width],
        attn_sums[:, q_width : q_width + kv_width],
        attn_sums[:, q_width + kv_width : qkv_width],
        attn_sums[:, qkv_width : qkv_width + q_width].T,
        gain_own[:, 1],
        grad_gate,
        grad_up,
        grad_down,
    )


def solution(mesh):
    return jax.shard_map(
        per_device,
        mesh=mesh,
        in_specs=(
            P(("dp", "tensor"), None),
            P("dp"),
            P("dp", "tensor"),
            P("dp", "tensor"),
            P("dp", "tensor"),
            P("tensor", "dp"),
            P("dp"),
            P("dp", "tensor"),
            P("dp", "tensor"),
            P("tensor", "dp"),
            P("dp"),
            P(("dp", "tensor"), None),
        ),
        out_specs=(
            P(("dp", "tensor"), None),
            P(("dp", "tensor"), None),
            P(("dp", "tensor")),
            P("dp", "tensor"),
            P("dp", "tensor"),
            P("dp", "tensor"),
            P("tensor", "dp"),
            P(("dp", "tensor")),
            P("dp", "tensor"),
            P("dp", "tensor"),
            P("tensor", "dp"),
        ),
        check_vma=False,
    )
```

```python
import functools
import math

import jax
import jax.numpy as jnp
from jax import lax
from jax.experimental import pallas as pl
from jax.experimental.pallas import tpu as pltpu
from jax.sharding import PartitionSpec as P

HEAD_DIM = 64
PAIR = 2 * HEAD_DIM
SEQ_LEN = 1024


EPS = 1e-05
ROPE_BASE = 500000.0
SCALE = 1.0 / math.sqrt(HEAD_DIM)
PARAMS = pltpu.CompilerParams(vmem_limit_bytes=58 * 2**20)
ONCE = pl.Buffered(1)

barrier = lax.optimization_barrier


def hint(flops):
    return pl.CostEstimate(flops=flops, bytes_accessed=0, transcendentals=0)


def rms_scale(values):
    return lax.rsqrt(jnp.mean(values * values, axis=-1, keepdims=True) + EPS)


def norm_back(grad, values, scale, gain):
    inner = grad * gain
    cubed = scale * scale * scale
    result = scale * inner - values * cubed * jnp.mean(inner * values, axis=-1, keepdims=True)
    return (result, jnp.sum(grad * values * scale, axis=0))


def mm(left, right):
    return jnp.dot(left, right, preferred_element_type=jnp.float32)


def mm_nt(left, right):
    return lax.dot_general(left, right, (((1,), (1,)), ((), ())), preferred_element_type=jnp.float32)


def mm_tn(left, right):
    return lax.dot_general(left, right, (((0,), (0,)), ((), ())), preferred_element_type=jnp.float32)


def lane_index(rows):
    return lax.broadcasted_iota(jnp.int32, (rows, PAIR), 1)


def turn(pair, cosine, sine):
    lower = lane_index(pair.shape[0]) % HEAD_DIM < HEAD_DIM // 2
    other = jnp.where(
        lower, pltpu.roll(pair, PAIR - HEAD_DIM // 2, 1), pltpu.roll(pair, HEAD_DIM // 2, 1)
    )
    return pair * cosine + other * sine


def project_kernel(place_ref, *refs, size, q_width, kv_width):
    x_refs = refs[:size]
    gain_ref, wo_ref, wx_ref, cos_ref, sin_ref, n_ref, q_ref, k_ref, v_ref = refs[size:]
    rows = q_ref.shape[0]
    half = wo_ref.shape[0]

    def one(x_ref):
        x = x_ref[...].astype(jnp.float32)
        normed = (x * rms_scale(x) * gain_ref[...]).astype(jnp.bfloat16)
        n_ref[...] = normed
        cosine, sine = cos_ref[...], sin_ref[...]
        lin = mm(normed[:, :half], wo_ref[...]) + mm(normed[:, half:], wx_ref[...])
        for low in range(0, q_width, PAIR):
            query = turn(lin[:, low : low + PAIR], cosine, sine).astype(jnp.bfloat16)
            q_ref[:, low : low + PAIR] = query * jnp.bfloat16(SCALE)
        first = lane_index(rows) < HEAD_DIM
        for ref, start, rotate in ((k_ref, q_width, True), (v_ref, q_width + kv_width, False)):
            for head in range(kv_width // HEAD_DIM):
                low = start + head * HEAD_DIM
                block = lin[:, low // PAIR * PAIR : low // PAIR * PAIR + PAIR]
                if rotate:
                    block = turn(block, cosine, sine)
                moved = pltpu.roll(block, HEAD_DIM, 1)
                if low % PAIR:
                    block, moved = moved, block
                ref[head, 0] = jnp.where(first, block, 0.0).astype(jnp.bfloat16)
                ref[head, 1] = jnp.where(first, 0.0, moved).astype(jnp.bfloat16)

    for step in range(size):
        pl.when(pl.program_id(0) == step)(functools.partial(one, x_refs[step]))


def project(me, blocks, gain, own, other, cosine, sine, q_width, kv_width):
    size = len(blocks)
    rows, features = blocks[0].shape
    total = rows * size
    key_heads = kv_width // HEAD_DIM
    width = q_width + 2 * kv_width
    fixed = lambda p, m: (0, 0)
    placed = lambda p, m: (jnp.bitwise_xor(p, m[0]), 0)
    padded = pl.BlockSpec(
        (key_heads, 2, rows, PAIR), lambda p, m: (0, 0, jnp.bitwise_xor(p, m[0]), 0)
    )
    spec = pltpu.PrefetchScalarGridSpec(
        num_scalar_prefetch=1,
        grid=(size,),
        in_specs=[pl.BlockSpec((rows, features), fixed, pipeline_mode=ONCE)] * size
        + [
            pl.BlockSpec((1, features), fixed),
            pl.BlockSpec((features // 2, width), fixed, pipeline_mode=ONCE),
            pl.BlockSpec((features // 2, width), fixed, pipeline_mode=ONCE),
            pl.BlockSpec((rows, PAIR), placed),
            pl.BlockSpec((rows, PAIR), placed),
        ],
        out_specs=[
            pl.BlockSpec((rows, features), lambda p, m: (p, 0)),
            pl.BlockSpec((rows, q_width), lambda p, m: (p, 0)),
            padded,
            padded,
        ],
    )
    padded_shape = jax.ShapeDtypeStruct((key_heads, 2, total, PAIR), jnp.bfloat16)
    return pl.pallas_call(
        functools.partial(project_kernel, size=size, q_width=q_width, kv_width=kv_width),
        grid_spec=spec,
        out_shape=[
            jax.ShapeDtypeStruct((total, features), jnp.bfloat16),
            jax.ShapeDtypeStruct((total, q_width), jnp.bfloat16),
            padded_shape,
            padded_shape,
        ],
        compiler_params=PARAMS,
        cost_estimate=hint(2 * total * features * width),
    )(me, *blocks, gain, own, other, cosine, sine)


def attend_kernel(
    me_ref, q_ref, k_ref, v_ref, wo_ref, wx_ref, o_ref, l_ref, *refs, size, heads, group
):
    part_refs, vt_ref = refs[:size], refs[size]
    rows = q_ref.shape[0]
    half = wo_ref.shape[0]
    mine = jnp.bitwise_xor(me_ref[0], pl.program_id(0))
    key_place = lax.broadcasted_iota(jnp.int32, (rows, rows), 0)
    query_place = lax.broadcasted_iota(jnp.int32, (rows, rows), 1)

    @pl.when(pl.program_id(0) == 0)
    def _():
        for head in range(heads // group):
            for side in range(2):
                vt_ref[head, side] = v_ref[head, side].T

    def one(span):
        keys = span * rows
        for pair in range(heads // 2):
            head = 2 * pair // group
            lanes = slice(pair * PAIR, (pair + 1) * PAIR)
            query = q_ref[:, lanes]
            acc = None
            inverse = []
            for side in range(2):
                diag = mm_nt(k_ref[head, side, keys : keys + rows, :], query)
                diag = jnp.where(key_place <= query_place, diag, -1e9)
                top = jnp.max(diag, axis=0, keepdims=True)
                if span:
                    body = mm_nt(k_ref[head, side, :keys, :], query)
                    top = jnp.maximum(top, jnp.max(body, axis=0, keepdims=True))
                diag = jnp.exp(diag - top)
                total = jnp.sum(diag, axis=0, keepdims=True)
                part = mm(vt_ref[head, side, :, keys : keys + rows], diag.astype(jnp.bfloat16))
                if span:
                    body = jnp.exp(body - top)
                    total = total + jnp.sum(body, axis=0, keepdims=True)
                    part = part + mm(vt_ref[head, side, :, :keys], body.astype(jnp.bfloat16))
                acc = part if acc is None else acc + part
                inverse.append(jnp.broadcast_to(1.0 / total, (HEAD_DIM, rows)))
                l_ref[2 * pair + side : 2 * pair + side + 1, :] = top + jnp.log(total)
            acc = acc * jnp.concatenate(inverse, axis=0)
            o_ref[:, lanes] = acc.T.astype(jnp.bfloat16)

    for span in range(size):
        pl.when(mine == span)(functools.partial(one, span))

    def project_out(ref):
        ref[:, :half] = mm_nt(o_ref[...], wo_ref[...]).astype(jnp.bfloat16)
        ref[:, half:] = mm_nt(o_ref[...], wx_ref[...]).astype(jnp.bfloat16)

    for step in range(size):
        pl.when(pl.program_id(0) == step)(functools.partial(project_out, part_refs[step]))


def attend(me, query, key_pad, value_pad, own, other, size, group):
    total, width = query.shape
    features = 2 * own.shape[0]
    rows, heads = total // size, width // HEAD_DIM
    whole = pl.BlockSpec(key_pad.shape, lambda p, m: (0, 0, 0, 0), pipeline_mode=ONCE)
    spec = pltpu.PrefetchScalarGridSpec(
        num_scalar_prefetch=1,
        grid=(size,),
        in_specs=[pl.BlockSpec((rows, width), lambda p, m: (p, 0)), whole, whole]
        + [pl.BlockSpec(own.shape, lambda p, m: (0, 0), pipeline_mode=ONCE)] * 2,
        out_specs=[
            pl.BlockSpec((rows, width), lambda p, m: (p, 0)),
            pl.BlockSpec((heads, rows), lambda p, m: (0, p)),
        ]
        + [pl.BlockSpec((rows, features), lambda p, m: (0, 0))] * size,
        scratch_shapes=[pltpu.VMEM((heads // group, 2, PAIR, total), jnp.bfloat16)],
    )
    return pl.pallas_call(
        functools.partial(attend_kernel, size=size, heads=heads, group=group),
        grid_spec=spec,
        out_shape=[
            jax.ShapeDtypeStruct((total, width), jnp.bfloat16),
            jax.ShapeDtypeStruct((heads, total), jnp.float32),
        ]
        + [jax.ShapeDtypeStruct((rows, features), jnp.bfloat16)] * size,
        compiler_params=PARAMS,
        cost_estimate=hint(8 * heads * total * total * HEAD_DIM),
    )(me, query, key_pad, value_pad, own, other)


def attend_back_kernel(
    me_ref, q_ref, l_ref, k_ref, v_ref, cos_ref, sin_ref, wo_ref, wx_ref, *refs, size, heads, group
):
    e_refs = refs[:size]
    out_ref, dk_ref, dv_ref, kt_ref, do_ref = refs[size:]
    half = wo_ref.shape[0]
    rows = q_ref.shape[0]
    key_heads = heads // group
    step = pl.program_id(0)
    me = me_ref[0]
    mine = jnp.bitwise_xor(me, step)
    key_place = lax.broadcasted_iota(jnp.int32, (rows, rows), 0)
    query_place = lax.broadcasted_iota(jnp.int32, (rows, rows), 1)

    def rows_of(block):
        return pl.ds(pl.multiple_of(block * rows, rows), rows)

    @pl.when(step == 0)
    def _():
        dk_ref[...] = jnp.zeros_like(dk_ref)
        dv_ref[...] = jnp.zeros_like(dv_ref)
        for head in range(key_heads):
            for side in range(2):
                kt_ref[head, side] = k_ref[head, side].T

    def attended_grad(ref):
        grad = mm(ref[:, :half], wo_ref[...]) + mm(ref[:, half:], wx_ref[...])
        do_ref[...] = grad.astype(jnp.bfloat16)

    for block in range(size):
        pl.when(step == block)(functools.partial(attended_grad, e_refs[block]))

    def one(span):
        keys = span * rows
        parts = [(keys, keys + rows, True)] + ([(0, keys, False)] if span else [])
        cosine, sine = cos_ref[keys : keys + rows, :], sin_ref[keys : keys + rows, :]
        for pair in range(heads // 2):
            head = 2 * pair // group
            lanes = slice(pair * PAIR, (pair + 1) * PAIR)
            query, grad = q_ref[:, lanes], do_ref[:, lanes]
            acc = None
            for side in range(2):
                log_total = l_ref[2 * pair + side : 2 * pair + side + 1, :]
                inner = None
                kept = []
                for low, high, diagonal in parts:
                    probs = mm_nt(k_ref[head, side, low:high, :], query)
                    probs = jnp.exp(probs - log_total)
                    if diagonal:
                        probs = jnp.where(key_place <= query_place, probs, 0.0)
                    prob_grad = mm_nt(v_ref[head, side, low:high, :], grad)
                    dv_ref[head, side, low:high, :] += mm(probs.astype(jnp.bfloat16), grad)
                    term = jnp.sum(probs * prob_grad, axis=0, keepdims=True)
                    inner = term if inner is None else inner + term
                    kept.append((low, high, probs, prob_grad))
                for low, high, probs, prob_grad in kept:
                    score_grad = (probs * (prob_grad - inner)).astype(jnp.bfloat16)
                    dk_ref[head, side, low:high, :] += mm(score_grad, query)
                    part = mm(kt_ref[head, side, :, low:high], score_grad)
                    acc = part if acc is None else acc + part
            turned = turn(acc.T * SCALE, cosine, -sine)
            out_ref[rows_of(step), lanes] = turned.astype(jnp.bfloat16)

    for span in range(size):
        pl.when(mine == span)(functools.partial(one, span))

    @pl.when(step == size - 1)
    def _():
        first = lane_index(rows) < HEAD_DIM
        wanted = [(dk_ref, head, True) for head in range(key_heads)]
        wanted += [(dv_ref, head, False) for head in range(key_heads)]
        for span in range(size):
            place = slice(span * rows, (span + 1) * rows)
            cosine, sine = cos_ref[place, :], sin_ref[place, :]
            for block in range(len(wanted) // 2):
                halves, rotate = [], []
                for half in range(2):
                    ref, head, is_key = wanted[2 * block + half]
                    low, high = ref[head, 0, place, :], ref[head, 1, place, :]
                    if half:
                        halves.append(pltpu.roll(low, HEAD_DIM, 1) + high)
                    else:
                        halves.append(low + pltpu.roll(high, HEAD_DIM, 1))
                    rotate.append(is_key)
                value = jnp.where(first, halves[0], halves[1])
                if rotate[0] and rotate[1]:
                    value = turn(value, cosine, -sine)
                elif rotate[0]:
                    value = jnp.where(first, turn(value, cosine, -sine), value)
                start = heads * HEAD_DIM + block * PAIR
                target = rows_of(jnp.bitwise_xor(me, span))
                out_ref[target, start : start + PAIR] = value.astype(jnp.bfloat16)


def attend_back(
    me, query, log_total, key_pad, value_pad, cosine, sine, own, other, branch_blocks, group
):
    total, width = query.shape
    size = len(branch_blocks)
    rows, heads = total // size, width // HEAD_DIM
    key_heads = heads // group
    out_width = width + 2 * key_heads * HEAD_DIM
    whole = pl.BlockSpec(key_pad.shape, lambda p, m: (0, 0, 0, 0), pipeline_mode=ONCE)
    table = pl.BlockSpec((total, PAIR), lambda p, m: (0, 0), pipeline_mode=ONCE)
    spec = pltpu.PrefetchScalarGridSpec(
        num_scalar_prefetch=1,
        grid=(size,),
        in_specs=[
            pl.BlockSpec((rows, width), lambda p, m: (p, 0)),
            pl.BlockSpec((heads, rows), lambda p, m: (0, p)),
            whole,
            whole,
            table,
            table,
        ]
        + [pl.BlockSpec(own.shape, lambda p, m: (0, 0), pipeline_mode=ONCE)] * 2
        + [pl.BlockSpec(branch_blocks[0].shape, lambda p, m: (0, 0), pipeline_mode=ONCE)] * size,
        out_specs=pl.BlockSpec((total, out_width), lambda p, m: (0, 0)),
        scratch_shapes=[
            pltpu.VMEM(key_pad.shape, jnp.float32),
            pltpu.VMEM(key_pad.shape, jnp.float32),
            pltpu.VMEM((key_heads, 2, PAIR, total), jnp.bfloat16),
            pltpu.VMEM((rows, width), jnp.bfloat16),
        ],
    )
    return pl.pallas_call(
        functools.partial(attend_back_kernel, size=size, heads=heads, group=group),
        grid_spec=spec,
        out_shape=jax.ShapeDtypeStruct((total, out_width), jnp.bfloat16),
        compiler_params=PARAMS,
        cost_estimate=hint(20 * heads * total * total * HEAD_DIM),
    )(me, query, log_total, key_pad, value_pad, cosine, sine, own, other, *branch_blocks)


def mlp_kernel(*refs, size, adds):
    n_refs, e_refs = refs[:size], refs[size : 2 * size]
    gate_o, up_o, down_o, gate_x, up_x, down_x = refs[2 * size : 2 * size + 6]
    dg_ref, du_ref, h_ref, dn_ref, y_ref, n_ref, e_ref = refs[-7:]
    half = gate_o.shape[0]

    def fetch(step):
        n_ref[...] = n_refs[step][...]
        e_ref[...] = e_refs[step][...]

    for step in range(size):
        pl.when(pl.program_id(0) == step)(functools.partial(fetch, step))
    gate = mm(n_ref[:, :half], gate_o[...]) + mm(n_ref[:, half:], gate_x[...])
    up = mm(n_ref[:, :half], up_o[...]) + mm(n_ref[:, half:], up_x[...])
    grad = mm(e_ref[:, :half], down_o[...]) + mm(e_ref[:, half:], down_x[...])
    sigma = jax.nn.sigmoid(gate)
    silu = gate * sigma
    hidden = (silu * up).astype(jnp.bfloat16)
    gate_grad = (grad * up * sigma * (1.0 + gate * (1.0 - sigma))).astype(jnp.bfloat16)
    up_grad = (grad * silu).astype(jnp.bfloat16)
    dg_ref[...] = gate_grad
    du_ref[...] = up_grad
    h_ref[...] = hidden
    for part, gate_w, up_w, down_w in ((0, gate_o, up_o, down_o), (1, gate_x, up_x, down_x)):
        lanes = slice(part * half, (part + 1) * half)
        dn = mm_nt(gate_grad, gate_w[...]) + mm_nt(up_grad, up_w[...])
        y = mm_nt(hidden, down_w[...])
        if adds:
            dn = dn + refs[2 * size + 6][:, lanes].astype(jnp.float32)
            y = y + refs[2 * size + 7][:, lanes].astype(jnp.float32)
        dn_ref[:, lanes] = dn.astype(dn_ref.dtype)
        y_ref[:, lanes] = y.astype(y_ref.dtype)


def mlp(tokens, cot, own, other, earlier):
    size = len(tokens)
    rows, features = tokens[0].shape
    half, units = own.shape[0], own.shape[1] // 3
    total = rows * size
    fixed = lambda p: (0, 0)
    moving = lambda p: (p, 0)
    wide = pl.BlockSpec((rows, features), moving)
    sums = jax.ShapeDtypeStruct((total, features), jnp.bfloat16)
    block = pl.BlockSpec((rows, features), fixed, pipeline_mode=ONCE)
    thirds = [
        pl.BlockSpec((half, units), lambda p, t=t: (0, t), pipeline_mode=ONCE) for t in range(3)
    ]
    return pl.pallas_call(
        functools.partial(mlp_kernel, size=size, adds=bool(earlier)),
        grid=(size,),
        in_specs=[block] * (2 * size)
        + thirds * 2
        + [wide] * len(earlier),
        out_specs=[pl.BlockSpec((rows, units), moving)] * 3 + [wide, wide],
        out_shape=[jax.ShapeDtypeStruct((total, units), jnp.bfloat16)] * 3 + [sums, sums],
        scratch_shapes=[pltpu.VMEM((rows, features), jnp.bfloat16)] * 2,
        compiler_params=PARAMS,
        cost_estimate=hint(12 * total * features * units),
    )(*tokens, *cot, own, own, own, other, other, other, *earlier)


def column_grad(blocks, other, mine, theirs):
    rows = blocks[0].shape[0]
    total = mm_tn(other[...], theirs[...])
    for index, block in enumerate(blocks):
        total = total + mm_tn(block[...], mine[index * rows : (index + 1) * rows, :])
    return total


def grad_kernel(*refs, size):
    n_refs, e_refs = refs[:size], refs[size : 2 * size]
    n_other, e_other = refs[2 * size : 2 * size + 2]
    acts, out_ref = refs[2 * size + 2 : -1], refs[-1]
    units = acts[0].shape[1]
    for third in range(3):
        blocks, other = (e_refs, e_other) if third == 2 else (n_refs, n_other)
        grad = column_grad(blocks, other, acts[third], acts[third + 3])
        out_ref[0, :, third * units : (third + 1) * units] = grad.astype(jnp.bfloat16)


def mlp_grads(chips, tokens, cot, tokens_other, cot_other, mine, theirs):
    size = len(tokens)
    rows, features = tokens[0].shape
    total, units = mine[0].shape
    depth = features // (2 * chips)
    column = pl.BlockSpec((rows, depth), lambda b: (0, b))
    long = pl.BlockSpec((total, depth), lambda b: (0, b))
    fixed = pl.BlockSpec((total, units), lambda b: (0, 0), pipeline_mode=ONCE)
    return pl.pallas_call(
        functools.partial(grad_kernel, size=size),
        grid=(chips,),
        in_specs=[column] * (2 * size) + [long, long] + [fixed] * 6,
        out_specs=pl.BlockSpec((1, depth, 3 * units), lambda b: (b, 0, 0)),
        out_shape=jax.ShapeDtypeStruct((chips, depth, 3 * units), jnp.bfloat16),
        compiler_params=PARAMS,
        cost_estimate=hint(6 * total * features * units),
    )(*tokens, *cot, tokens_other, cot_other, *mine, *theirs)


def attn_grad_kernel(*refs, size):
    e_refs = refs[2 : 2 + size]
    n_ref, n_other = refs[:2]
    e_other, d_ref, d_other, o_ref, o_other, w_ref, g1_ref, g2_ref = refs[2 + size : -2]
    out_ref, gain_ref = refs[-2:]
    width, out_width = d_ref.shape[1], o_ref.shape[1]
    grad = column_grad([n_ref], n_other, d_ref, d_other)
    out_ref[0, :, :width] = grad.astype(jnp.bfloat16)
    out_grad = column_grad(e_refs, e_other, o_ref, o_other)
    out_ref[0, :, width : width + out_width] = out_grad.astype(jnp.bfloat16)
    first = jnp.sum(grad * w_ref[...].astype(jnp.float32), axis=1, keepdims=True) / g1_ref[...]
    lane = lane_index(grad.shape[0])
    gain_ref[0] = jnp.where(lane == 0, first, g2_ref[...])


def attn_grads(chips, tokens, branch, mine, theirs, weights, gain_one, gain_two_part):
    size = len(branch)
    qkv_grad, attended = mine
    tokens_other, branch_other, qkv_other, attended_other = theirs
    total, features = tokens.shape
    rows = total // size
    width, out_width = qkv_grad.shape[1], attended.shape[1]
    depth = features // (2 * chips)
    column = lambda b: (0, b)
    row = lambda b: (b, 0)
    long = pl.BlockSpec((total, depth), column)
    fixed = lambda array: pl.BlockSpec(array.shape, lambda b: (0, 0), pipeline_mode=ONCE)
    place = lambda b: (b, 0, 0)
    return pl.pallas_call(
        functools.partial(attn_grad_kernel, size=size),
        grid=(chips,),
        in_specs=[long, long]
        + [pl.BlockSpec((rows, depth), column)] * size
        + [long]
        + [fixed(qkv_grad)] * 2
        + [fixed(attended)] * 2
        + [
            pl.BlockSpec((depth, width), row),
            pl.BlockSpec((depth, 1), row),
            pl.BlockSpec((depth, 1), row),
        ],
        out_specs=[
            pl.BlockSpec((1, depth, width + out_width), place),
            pl.BlockSpec((1, depth, PAIR), place),
        ],
        out_shape=[
            jax.ShapeDtypeStruct((chips, depth, width + out_width), jnp.bfloat16),
            jax.ShapeDtypeStruct((chips, depth, PAIR), jnp.float32),
        ],
        compiler_params=PARAMS,
        cost_estimate=hint(2 * total * features * (width + out_width)),
    )(
        tokens,
        tokens_other,
        *branch,
        branch_other,
        qkv_grad,
        qkv_other,
        attended,
        attended_other,
        weights,
        gain_one,
        gain_two_part,
    )


def swap(values, step):
    size = lax.axis_size("tensor")
    return lax.ppermute(values, "tensor", [(i, i ^ step) for i in range(size)])


def spread(values):
    return [values] + [swap(values, step) for step in range(1, lax.axis_size("tensor"))]


def send_blocks(blocks):
    return [blocks[0]] + [swap(block, step + 1) for step, block in enumerate(blocks[1:])]


def send_rows(partial):
    size = lax.axis_size("tensor")
    return send_blocks(list(partial.reshape((size, -1) + partial.shape[1:])))


def add_up(blocks):
    total = blocks[0].astype(jnp.float32)
    for block in blocks[1:]:
        total = total + block.astype(jnp.float32)
    return total


def cross(values):
    count = lax.axis_size("dp")
    return lax.ppermute(values, "dp", [(i, i ^ 1) for i in range(count)])


def tables(positions):
    freqs = ROPE_BASE ** (-jnp.arange(0, HEAD_DIM, 2).astype(jnp.float32) / HEAD_DIM)
    angles = positions.astype(jnp.float32)[:, None] * freqs[None, :]
    cosine, sine = jnp.cos(angles), jnp.sin(angles)
    return (
        jnp.concatenate([cosine] * 4, axis=1),
        jnp.concatenate([-sine, sine, -sine, sine], axis=1),
    )


def chip_lines():
    count = lax.axis_size("dp")
    return [list(range(core, count, 2)) for core in range(2)]


def gather(values):
    return lax.all_gather(values, "dp", axis=0, tiled=True, axis_index_groups=chip_lines())


def scatter(values):
    total = lax.psum_scatter(
        values, "dp", scatter_dimension=0, tiled=True, axis_index_groups=chip_lines()
    )
    return total[0]


def small_sums(parts):
    count = lax.axis_size("dp")
    chips = count // 2
    chip = lax.axis_index("dp") // 2
    own = lax.dynamic_index_in_dim(parts, chip, 0, keepdims=False)
    for step in range(1, chips):
        sent = lax.dynamic_index_in_dim(parts, (chip + step) % chips, 0, keepdims=False)
        pairs = [(i, (i + 2 * step) % count) for i in range(count)]
        own = own + lax.ppermute(sent, "dp", pairs)
    size = lax.axis_size("tensor")
    me = lax.axis_index("tensor")
    blocks = own.reshape((size, -1) + own.shape[1:])
    own = lax.dynamic_index_in_dim(blocks, me, 0, keepdims=False)
    for step in range(1, size):
        sent = lax.dynamic_index_in_dim(blocks, me ^ step, 0, keepdims=False)
        own = own + swap(sent, step)
    return own


def other_half(blocks):
    half = blocks[0].shape[1] // 2
    return cross(jnp.concatenate([block[:, half:] for block in blocks], axis=0))


def feature_blocks(values):
    width = values.shape[-1] // lax.axis_size("dp")
    return [values[..., low : low + width] for low in range(0, values.shape[-1], width)]


def by_core(values, core):
    blocks = feature_blocks(values)
    pairs = list(zip(blocks[0::2], blocks[1::2]))
    own = [jnp.where(core == 0, even, odd) for even, odd in pairs]
    other = [jnp.where(core == 0, odd, even) for even, odd in pairs]
    return jnp.concatenate(own + other, axis=-1)


def by_device(values, core):
    blocks = feature_blocks(values)
    chips = len(blocks) // 2
    placed = []
    for own, other in zip(blocks[:chips], blocks[chips:]):
        placed += [jnp.where(core == 0, own, other), jnp.where(core == 0, other, own)]
    return jnp.concatenate(placed, axis=-1)


def per_device(
    hidden_in,
    gain_attn,
    w_query,
    w_key,
    w_value,
    w_out,
    gain_mlp,
    w_gate,
    w_up,
    w_down,
    positions,
    cotangent,
):
    size = lax.axis_size("tensor")
    chips = lax.axis_size("dp") // 2
    me = lax.axis_index("tensor")
    me_array = jnp.full((1,), me, jnp.int32)
    core = lax.axis_index("dp") % 2
    q_width, kv_width = w_query.shape[1], w_key.shape[1]
    qkv_width = q_width + 2 * kv_width
    group = q_width // kv_width
    units = w_down.shape[0] // 2
    half = hidden_in.shape[1] // 2

    attn_own = gather(jnp.concatenate([w_query, w_key, w_value, w_out.T], axis=1))
    residual = by_core(hidden_in, core)
    blocks_in = spread(residual)
    residual = residual.astype(jnp.float32)
    gains = lax.all_gather(jnp.stack([gain_attn, gain_mlp]), "dp", axis=1, tiled=True)
    gains = by_core(gains, core).astype(jnp.float32)
    cosine, sine = tables(positions)
    cotangent = by_core(cotangent, core)
    down_t = w_down.T
    shares = []
    for part in range(2):
        cut = slice(part * units, (part + 1) * units)
        shares.append(jnp.concatenate([w_gate[:, cut], w_up[:, cut], down_t[:, cut]], axis=1))
    shares, attn_own, blocks_in, cosine, sine, gains, cotangent = barrier(
        (shares, attn_own, blocks_in, cosine, sine, gains, cotangent)
    )
    mlp_own = [gather(share) for share in shares]
    cot_blocks = spread(cotangent)
    gain_one, gain_two = gains[0], gains[1]
    qkv_own, out_own = attn_own[:, :qkv_width], attn_own[:, qkv_width:]
    qkv = (qkv_own, cross(qkv_own))
    out_t = (out_own, cross(out_own))

    scale_one = rms_scale(residual)
    tokens_one, query, key_pad, value_pad = project(
        me_array, blocks_in, gain_one[None, :], *qkv, cosine, sine, q_width, kv_width
    )
    attended, log_total, *parts = attend(
        me_array, query, key_pad, value_pad, *out_t, size, group
    )
    parts, cot_blocks, tokens_one, attended = barrier((parts, cot_blocks, tokens_one, attended))
    arrived = send_blocks(parts)
    middle = residual + add_up(arrived)

    scale_two = rms_scale(middle)
    normed_two = (middle * scale_two * gain_two).astype(jnp.bfloat16)
    tokens_two = spread(normed_two)
    first, own_share = barrier((tokens_two[: size - 1], mlp_own[0]))
    tokens_two = first + tokens_two[size - 1 :]
    weights = (own_share, cross(own_share))
    tokens_two, weights = barrier((tokens_two, weights))
    cot_other = other_half(cot_blocks)
    early = (cross(tokens_one[:, half:]), cross(attended))
    cot_other, early, tokens_two = barrier((cot_other, early, tokens_two))
    tokens_other = other_half(tokens_two)
    *acts, dn_part, y_part = mlp(tokens_two, cot_blocks, *weights, ())
    acts, tokens_other, cot_other = barrier((acts, tokens_other, cot_other))
    acts_other = [cross(act) for act in acts]
    grads_one = mlp_grads(
        chips, tokens_two, cot_blocks, tokens_other, cot_other, acts, acts_other
    )
    grads_one, own_share = barrier((grads_one, mlp_own[1]))
    sums_one = scatter(grads_one)
    weights = (own_share, cross(own_share))
    *acts, dn_part, y_part = mlp(tokens_two, cot_blocks, *weights, (dn_part, y_part))
    acts, dn_part = barrier((acts, dn_part))
    arrived = send_rows(dn_part)
    acts_other = [cross(act) for act in acts]
    grads_two = mlp_grads(
        chips, tokens_two, cot_blocks, tokens_other, cot_other, acts, acts_other
    )
    grads_two, arrived, y_part = barrier((grads_two, arrived, y_part))
    sums_two = scatter(grads_two)
    normed_two_grad = add_up(arrived)
    middle_norm_grad, gain_two_part = norm_back(normed_two_grad, middle, scale_two, gain_two)
    middle_grad = cotangent.astype(jnp.float32) + middle_norm_grad
    branch_blocks = spread(middle_grad.astype(jnp.bfloat16))
    gain_two_other = cross(gain_two_part[half:])
    branch_blocks, gain_two_other, y_part, sums_one = barrier(
        (branch_blocks, gain_two_other, y_part, sums_one)
    )
    tokens_other, attended_other = early
    down_arrived = send_rows(y_part)
    branch_other = other_half(branch_blocks)
    qkv_grad = attend_back(
        me_array,
        query,
        log_total,
        key_pad,
        value_pad,
        cosine,
        sine,
        *out_t,
        branch_blocks,
        group,
    )
    qkv_grad, branch_other, down_arrived = barrier((qkv_grad, branch_other, down_arrived))
    out = (middle + add_up(down_arrived)).astype(jnp.bfloat16)
    qkv_other = cross(qkv_grad)
    normed_part = jnp.concatenate([mm_nt(qkv_grad, w) for w in qkv], axis=1).astype(jnp.bfloat16)
    arrived = send_rows(normed_part)
    grads = attn_grads(
        chips,
        tokens_one,
        branch_blocks,
        (qkv_grad, attended),
        (tokens_other, branch_other, qkv_other, attended_other),
        qkv[0],
        gain_one[:half, None],
        (gain_two_part[:half] + gain_two_other)[:, None],
    )
    attn_sums = scatter(grads[0])
    grads, arrived, out = barrier((grads, arrived, out))
    gain_sums = small_sums(grads[1][:, :, :2])
    normed_one_grad = add_up(arrived)
    input_norm_grad, _ = norm_back(normed_one_grad, residual, scale_one, gain_one)
    grad_in = by_device(middle_grad + input_norm_grad, core)

    sums_two, grad_in, gain_sums = barrier((sums_two, grad_in, gain_sums))
    shares = [share.astype(jnp.float32) for share in (sums_one, sums_two)]
    grad_gate = jnp.concatenate([h[:, :units] for h in shares], axis=1)
    grad_up = jnp.concatenate([h[:, units : 2 * units] for h in shares], axis=1)
    grad_down = jnp.concatenate([h[:, 2 * units :].T for h in shares], axis=0)
    grad_gate, grad_up, grad_down, attn_sums = barrier((grad_gate, grad_up, grad_down, attn_sums))
    attn_sums = attn_sums.astype(jnp.float32)
    return (
        by_device(out, core),
        grad_in,
        gain_sums[:, 0],
        attn_sums[:, :q_width],
        attn_sums[:, q_width : q_width + kv_width],
        attn_sums[:, q_width + kv_width : qkv_width],
        attn_sums[:, qkv_width : qkv_width + q_width].T,
        gain_sums[:, 1],
        grad_gate,
        grad_up,
        grad_down,
    )


def solution(mesh):
    return jax.shard_map(
        per_device,
        mesh=mesh,
        in_specs=(
            P(("dp", "tensor"), None),
            P("dp"),
            P("dp", "tensor"),
            P("dp", "tensor"),
            P("dp", "tensor"),
            P("tensor", "dp"),
            P("dp"),
            P("dp", "tensor"),
            P("dp", "tensor"),
            P("tensor", "dp"),
            P("dp"),
            P(("dp", "tensor"), None),
        ),
        out_specs=(
            P(("dp", "tensor"), None),
            P(("dp", "tensor"), None),
            P(("dp", "tensor")),
            P("dp", "tensor"),
            P("dp", "tensor"),
            P("dp", "tensor"),
            P("tensor", "dp"),
            P(("dp", "tensor")),
            P("dp", "tensor"),
            P("dp", "tensor"),
            P("tensor", "dp"),
        ),
        check_vma=False,
    )
```

```python
import functools
import math

import jax
import jax.numpy as jnp
from jax import lax
from jax.experimental import pallas as pl
from jax.experimental.pallas import tpu as pltpu
from jax.sharding import PartitionSpec as P

HEAD_DIM = 64
PAIR = 2 * HEAD_DIM
SEQ_LEN = 1024


EPS = 1e-05
ROPE_BASE = 500000.0
SCALE = 1.0 / math.sqrt(HEAD_DIM)
PARAMS = pltpu.CompilerParams(vmem_limit_bytes=58 * 2**20)
ONCE = pl.Buffered(1)

barrier = lax.optimization_barrier


def hint(flops):
    return pl.CostEstimate(flops=flops, bytes_accessed=0, transcendentals=0)


def rms_scale(values):
    return lax.rsqrt(jnp.mean(values * values, axis=-1, keepdims=True) + EPS)


def norm_back(grad, values, scale, gain):
    inner = grad * gain
    cubed = scale * scale * scale
    result = scale * inner - values * cubed * jnp.mean(inner * values, axis=-1, keepdims=True)
    return (result, jnp.sum(grad * values * scale, axis=0))


def mm(left, right):
    return jnp.dot(left, right, preferred_element_type=jnp.float32)


def mm_nt(left, right):
    return lax.dot_general(left, right, (((1,), (1,)), ((), ())), preferred_element_type=jnp.float32)


def mm_tn(left, right):
    return lax.dot_general(left, right, (((0,), (0,)), ((), ())), preferred_element_type=jnp.float32)


def lane_index(rows):
    return lax.broadcasted_iota(jnp.int32, (rows, PAIR), 1)


def turn(pair, cosine, sine):
    lower = lane_index(pair.shape[0]) % HEAD_DIM < HEAD_DIM // 2
    other = jnp.where(
        lower, pltpu.roll(pair, PAIR - HEAD_DIM // 2, 1), pltpu.roll(pair, HEAD_DIM // 2, 1)
    )
    return pair * cosine + other * sine


def project_kernel(place_ref, *refs, size, q_width, kv_width):
    x_refs = refs[:size]
    gain_ref, wo_ref, wx_ref, cos_ref, sin_ref, n_ref, q_ref, k_ref, v_ref = refs[size:]
    rows = q_ref.shape[0]
    half = wo_ref.shape[0]

    def one(x_ref):
        x = x_ref[...].astype(jnp.float32)
        normed = (x * rms_scale(x) * gain_ref[...]).astype(jnp.bfloat16)
        n_ref[...] = normed
        cosine, sine = cos_ref[...], sin_ref[...]
        lin = mm(normed[:, :half], wo_ref[...]) + mm(normed[:, half:], wx_ref[...])
        for low in range(0, q_width, PAIR):
            query = turn(lin[:, low : low + PAIR], cosine, sine).astype(jnp.bfloat16)
            q_ref[:, low : low + PAIR] = query * jnp.bfloat16(SCALE)
        first = lane_index(rows) < HEAD_DIM
        for ref, start, rotate in ((k_ref, q_width, True), (v_ref, q_width + kv_width, False)):
            for head in range(kv_width // HEAD_DIM):
                low = start + head * HEAD_DIM
                block = lin[:, low // PAIR * PAIR : low // PAIR * PAIR + PAIR]
                if rotate:
                    block = turn(block, cosine, sine)
                moved = pltpu.roll(block, HEAD_DIM, 1)
                if low % PAIR:
                    block, moved = moved, block
                ref[head, 0] = jnp.where(first, block, 0.0).astype(jnp.bfloat16)
                ref[head, 1] = jnp.where(first, 0.0, moved).astype(jnp.bfloat16)

    for step in range(size):
        pl.when(pl.program_id(0) == step)(functools.partial(one, x_refs[step]))


def project(me, blocks, gain, own, other, cosine, sine, q_width, kv_width):
    size = len(blocks)
    rows, features = blocks[0].shape
    total = rows * size
    key_heads = kv_width // HEAD_DIM
    width = q_width + 2 * kv_width
    fixed = lambda p, m: (0, 0)
    placed = lambda p, m: (jnp.bitwise_xor(p, m[0]), 0)
    padded = pl.BlockSpec(
        (key_heads, 2, rows, PAIR), lambda p, m: (0, 0, jnp.bitwise_xor(p, m[0]), 0)
    )
    spec = pltpu.PrefetchScalarGridSpec(
        num_scalar_prefetch=1,
        grid=(size,),
        in_specs=[pl.BlockSpec((rows, features), fixed, pipeline_mode=ONCE)] * size
        + [
            pl.BlockSpec((1, features), fixed),
            pl.BlockSpec((features // 2, width), fixed, pipeline_mode=ONCE),
            pl.BlockSpec((features // 2, width), fixed, pipeline_mode=ONCE),
            pl.BlockSpec((rows, PAIR), placed),
            pl.BlockSpec((rows, PAIR), placed),
        ],
        out_specs=[
            pl.BlockSpec((rows, features), lambda p, m: (p, 0)),
            pl.BlockSpec((rows, q_width), lambda p, m: (p, 0)),
            padded,
            padded,
        ],
    )
    padded_shape = jax.ShapeDtypeStruct((key_heads, 2, total, PAIR), jnp.bfloat16)
    return pl.pallas_call(
        functools.partial(project_kernel, size=size, q_width=q_width, kv_width=kv_width),
        grid_spec=spec,
        out_shape=[
            jax.ShapeDtypeStruct((total, features), jnp.bfloat16),
            jax.ShapeDtypeStruct((total, q_width), jnp.bfloat16),
            padded_shape,
            padded_shape,
        ],
        compiler_params=PARAMS,
        cost_estimate=hint(2 * total * features * width),
    )(me, *blocks, gain, own, other, cosine, sine)


def attend_kernel(
    me_ref, q_ref, k_ref, v_ref, wo_ref, wx_ref, o_ref, l_ref, *refs, size, heads, group
):
    part_refs, vt_ref = refs[:size], refs[size]
    rows = q_ref.shape[0]
    half = wo_ref.shape[0]
    mine = jnp.bitwise_xor(me_ref[0], pl.program_id(0))
    key_place = lax.broadcasted_iota(jnp.int32, (rows, rows), 0)
    query_place = lax.broadcasted_iota(jnp.int32, (rows, rows), 1)

    @pl.when(pl.program_id(0) == 0)
    def _():
        for head in range(heads // group):
            for side in range(2):
                vt_ref[head, side] = v_ref[head, side].T

    def one(span):
        keys = span * rows
        for pair in range(heads // 2):
            head = 2 * pair // group
            lanes = slice(pair * PAIR, (pair + 1) * PAIR)
            query = q_ref[:, lanes]
            acc = None
            inverse = []
            for side in range(2):
                diag = mm_nt(k_ref[head, side, keys : keys + rows, :], query)
                diag = jnp.where(key_place <= query_place, diag, -1e9)
                top = jnp.max(diag, axis=0, keepdims=True)
                if span:
                    body = mm_nt(k_ref[head, side, :keys, :], query)
                    top = jnp.maximum(top, jnp.max(body, axis=0, keepdims=True))
                diag = jnp.exp(diag - top)
                total = jnp.sum(diag, axis=0, keepdims=True)
                part = mm(vt_ref[head, side, :, keys : keys + rows], diag.astype(jnp.bfloat16))
                if span:
                    body = jnp.exp(body - top)
                    total = total + jnp.sum(body, axis=0, keepdims=True)
                    part = part + mm(vt_ref[head, side, :, :keys], body.astype(jnp.bfloat16))
                acc = part if acc is None else acc + part
                inverse.append(jnp.broadcast_to(1.0 / total, (HEAD_DIM, rows)))
                l_ref[2 * pair + side : 2 * pair + side + 1, :] = top + jnp.log(total)
            acc = acc * jnp.concatenate(inverse, axis=0)
            o_ref[:, lanes] = acc.T.astype(jnp.bfloat16)

    for span in range(size):
        pl.when(mine == span)(functools.partial(one, span))

    def project_out(ref):
        ref[:, :half] = mm_nt(o_ref[...], wo_ref[...]).astype(jnp.bfloat16)
        ref[:, half:] = mm_nt(o_ref[...], wx_ref[...]).astype(jnp.bfloat16)

    for step in range(size):
        pl.when(pl.program_id(0) == step)(functools.partial(project_out, part_refs[step]))


def attend(me, query, key_pad, value_pad, own, other, size, group):
    total, width = query.shape
    features = 2 * own.shape[0]
    rows, heads = total // size, width // HEAD_DIM
    whole = pl.BlockSpec(key_pad.shape, lambda p, m: (0, 0, 0, 0), pipeline_mode=ONCE)
    spec = pltpu.PrefetchScalarGridSpec(
        num_scalar_prefetch=1,
        grid=(size,),
        in_specs=[pl.BlockSpec((rows, width), lambda p, m: (p, 0)), whole, whole]
        + [pl.BlockSpec(own.shape, lambda p, m: (0, 0), pipeline_mode=ONCE)] * 2,
        out_specs=[
            pl.BlockSpec((rows, width), lambda p, m: (p, 0)),
            pl.BlockSpec((heads, rows), lambda p, m: (0, p)),
        ]
        + [pl.BlockSpec((rows, features), lambda p, m: (0, 0))] * size,
        scratch_shapes=[pltpu.VMEM((heads // group, 2, PAIR, total), jnp.bfloat16)],
    )
    return pl.pallas_call(
        functools.partial(attend_kernel, size=size, heads=heads, group=group),
        grid_spec=spec,
        out_shape=[
            jax.ShapeDtypeStruct((total, width), jnp.bfloat16),
            jax.ShapeDtypeStruct((heads, total), jnp.float32),
        ]
        + [jax.ShapeDtypeStruct((rows, features), jnp.bfloat16)] * size,
        compiler_params=PARAMS,
        cost_estimate=hint(8 * heads * total * total * HEAD_DIM),
    )(me, query, key_pad, value_pad, own, other)


def attend_back_kernel(
    me_ref, q_ref, l_ref, k_ref, v_ref, cos_ref, sin_ref, *refs, size, heads, group
):
    do_refs = refs[:size]
    out_ref, dk_ref, dv_ref, kt_ref, do_ref = refs[size:]
    rows = q_ref.shape[0]
    key_heads = heads // group
    step = pl.program_id(0)
    me = me_ref[0]
    mine = jnp.bitwise_xor(me, step)
    key_place = lax.broadcasted_iota(jnp.int32, (rows, rows), 0)
    query_place = lax.broadcasted_iota(jnp.int32, (rows, rows), 1)

    def rows_of(block):
        return pl.ds(pl.multiple_of(block * rows, rows), rows)

    @pl.when(step == 0)
    def _():
        dk_ref[...] = jnp.zeros_like(dk_ref)
        dv_ref[...] = jnp.zeros_like(dv_ref)
        for head in range(key_heads):
            for side in range(2):
                kt_ref[head, side] = k_ref[head, side].T

    def fetch(ref):
        do_ref[...] = ref[...]

    for block in range(size):
        pl.when(step == block)(functools.partial(fetch, do_refs[block]))

    def one(span):
        keys = span * rows
        parts = [(keys, keys + rows, True)] + ([(0, keys, False)] if span else [])
        cosine, sine = cos_ref[keys : keys + rows, :], sin_ref[keys : keys + rows, :]
        for pair in range(heads // 2):
            head = 2 * pair // group
            lanes = slice(pair * PAIR, (pair + 1) * PAIR)
            query, grad = q_ref[:, lanes], do_ref[:, lanes]
            acc = None
            for side in range(2):
                log_total = l_ref[2 * pair + side : 2 * pair + side + 1, :]
                inner = None
                kept = []
                for low, high, diagonal in parts:
                    probs = mm_nt(k_ref[head, side, low:high, :], query)
                    probs = jnp.exp(probs - log_total)
                    if diagonal:
                        probs = jnp.where(key_place <= query_place, probs, 0.0)
                    prob_grad = mm_nt(v_ref[head, side, low:high, :], grad)
                    dv_ref[head, side, low:high, :] += mm(probs.astype(jnp.bfloat16), grad)
                    term = jnp.sum(probs * prob_grad, axis=0, keepdims=True)
                    inner = term if inner is None else inner + term
                    kept.append((low, high, probs, prob_grad))
                for low, high, probs, prob_grad in kept:
                    score_grad = (probs * (prob_grad - inner)).astype(jnp.bfloat16)
                    dk_ref[head, side, low:high, :] += mm(score_grad, query)
                    part = mm(kt_ref[head, side, :, low:high], score_grad)
                    acc = part if acc is None else acc + part
            turned = turn(acc.T * SCALE, cosine, -sine)
            out_ref[rows_of(step), lanes] = turned.astype(jnp.bfloat16)

    for span in range(size):
        pl.when(mine == span)(functools.partial(one, span))

    @pl.when(step == size - 1)
    def _():
        first = lane_index(rows) < HEAD_DIM
        wanted = [(dk_ref, head, True) for head in range(key_heads)]
        wanted += [(dv_ref, head, False) for head in range(key_heads)]
        for span in range(size):
            place = slice(span * rows, (span + 1) * rows)
            cosine, sine = cos_ref[place, :], sin_ref[place, :]
            for block in range(len(wanted) // 2):
                halves, rotate = [], []
                for half in range(2):
                    ref, head, is_key = wanted[2 * block + half]
                    low, high = ref[head, 0, place, :], ref[head, 1, place, :]
                    if half:
                        halves.append(pltpu.roll(low, HEAD_DIM, 1) + high)
                    else:
                        halves.append(low + pltpu.roll(high, HEAD_DIM, 1))
                    rotate.append(is_key)
                value = jnp.where(first, halves[0], halves[1])
                if rotate[0] and rotate[1]:
                    value = turn(value, cosine, -sine)
                elif rotate[0]:
                    value = jnp.where(first, turn(value, cosine, -sine), value)
                start = heads * HEAD_DIM + block * PAIR
                target = rows_of(jnp.bitwise_xor(me, span))
                out_ref[target, start : start + PAIR] = value.astype(jnp.bfloat16)


def attend_back(
    me, query, log_total, key_pad, value_pad, cosine, sine, attended_grad, group
):
    total, width = query.shape
    size = len(attended_grad)
    rows, heads = total // size, width // HEAD_DIM
    key_heads = heads // group
    out_width = width + 2 * key_heads * HEAD_DIM
    whole = pl.BlockSpec(key_pad.shape, lambda p, m: (0, 0, 0, 0), pipeline_mode=ONCE)
    table = pl.BlockSpec((total, PAIR), lambda p, m: (0, 0), pipeline_mode=ONCE)
    spec = pltpu.PrefetchScalarGridSpec(
        num_scalar_prefetch=1,
        grid=(size,),
        in_specs=[
            pl.BlockSpec((rows, width), lambda p, m: (p, 0)),
            pl.BlockSpec((heads, rows), lambda p, m: (0, p)),
            whole,
            whole,
            table,
            table,
        ]
        + [pl.BlockSpec((rows, width), lambda p, m: (0, 0), pipeline_mode=ONCE)] * size,
        out_specs=pl.BlockSpec((total, out_width), lambda p, m: (0, 0)),
        scratch_shapes=[
            pltpu.VMEM(key_pad.shape, jnp.float32),
            pltpu.VMEM(key_pad.shape, jnp.float32),
            pltpu.VMEM((key_heads, 2, PAIR, total), jnp.bfloat16),
            pltpu.VMEM((rows, width), jnp.bfloat16),
        ],
    )
    return pl.pallas_call(
        functools.partial(attend_back_kernel, size=size, heads=heads, group=group),
        grid_spec=spec,
        out_shape=jax.ShapeDtypeStruct((total, out_width), jnp.bfloat16),
        compiler_params=PARAMS,
        cost_estimate=hint(20 * heads * total * total * HEAD_DIM),
    )(me, query, log_total, key_pad, value_pad, cosine, sine, *attended_grad)


def mlp_kernel(*refs, size, adds):
    n_refs, e_refs = refs[:size], refs[size : 2 * size]
    gate_o, up_o, down_o, gate_x, up_x, down_x = refs[2 * size : 2 * size + 6]
    dg_ref, du_ref, h_ref, dn_ref, y_ref, n_ref, e_ref = refs[-7:]
    half = gate_o.shape[0]

    def fetch(step):
        n_ref[...] = n_refs[step][...]
        e_ref[...] = e_refs[step][...]

    for step in range(size):
        pl.when(pl.program_id(0) == step)(functools.partial(fetch, step))
    gate = mm(n_ref[:, :half], gate_o[...]) + mm(n_ref[:, half:], gate_x[...])
    up = mm(n_ref[:, :half], up_o[...]) + mm(n_ref[:, half:], up_x[...])
    grad = mm(e_ref[:, :half], down_o[...]) + mm(e_ref[:, half:], down_x[...])
    sigma = jax.nn.sigmoid(gate)
    silu = gate * sigma
    hidden = (silu * up).astype(jnp.bfloat16)
    gate_grad = (grad * up * sigma * (1.0 + gate * (1.0 - sigma))).astype(jnp.bfloat16)
    up_grad = (grad * silu).astype(jnp.bfloat16)
    dg_ref[...] = gate_grad
    du_ref[...] = up_grad
    h_ref[...] = hidden
    for part, gate_w, up_w, down_w in ((0, gate_o, up_o, down_o), (1, gate_x, up_x, down_x)):
        lanes = slice(part * half, (part + 1) * half)
        dn = mm_nt(gate_grad, gate_w[...]) + mm_nt(up_grad, up_w[...])
        y = mm_nt(hidden, down_w[...])
        if adds:
            dn = dn + refs[2 * size + 6][:, lanes].astype(jnp.float32)
            y = y + refs[2 * size + 7][:, lanes].astype(jnp.float32)
        dn_ref[:, lanes] = dn.astype(dn_ref.dtype)
        y_ref[:, lanes] = y.astype(y_ref.dtype)


def mlp(tokens, cot, own, other, earlier):
    size = len(tokens)
    rows, features = tokens[0].shape
    half, units = own.shape[0], own.shape[1] // 3
    total = rows * size
    fixed = lambda p: (0, 0)
    moving = lambda p: (p, 0)
    wide = pl.BlockSpec((rows, features), moving)
    sums = jax.ShapeDtypeStruct((total, features), jnp.bfloat16)
    block = pl.BlockSpec((rows, features), fixed, pipeline_mode=ONCE)
    thirds = [
        pl.BlockSpec((half, units), lambda p, t=t: (0, t), pipeline_mode=ONCE) for t in range(3)
    ]
    return pl.pallas_call(
        functools.partial(mlp_kernel, size=size, adds=bool(earlier)),
        grid=(size,),
        in_specs=[block] * (2 * size)
        + thirds * 2
        + [wide] * len(earlier),
        out_specs=[pl.BlockSpec((rows, units), moving)] * 3 + [wide, wide],
        out_shape=[jax.ShapeDtypeStruct((total, units), jnp.bfloat16)] * 3 + [sums, sums],
        scratch_shapes=[pltpu.VMEM((rows, features), jnp.bfloat16)] * 2,
        compiler_params=PARAMS,
        cost_estimate=hint(12 * total * features * units),
    )(*tokens, *cot, own, own, own, other, other, other, *earlier)


def middle_back_kernel(*refs, size):
    n_refs, refs = refs[:size], refs[size:]
    x_ref, e_ref, gain_ref, refs = refs[0], refs[1], refs[2], refs[3:]
    own_refs, other_refs, refs = refs[:size], refs[size : 2 * size], refs[2 * size :]
    grad_ref, branch_ref, part_ref, do_refs = refs[0], refs[1], refs[2], refs[3:]
    half = own_refs[0].shape[0]
    grad = n_refs[0][...].astype(jnp.float32)
    for ref in n_refs[1:]:
        grad = grad + ref[...].astype(jnp.float32)
    values = x_ref[...]
    scale = rms_scale(values)
    result, part = norm_back(grad, values, scale, gain_ref[...])

    @pl.when(pl.program_id(0) == 0)
    def _():
        part_ref[...] = jnp.zeros_like(part_ref)

    part_ref[...] += part[None, :]
    result = result + e_ref[...].astype(jnp.float32)
    grad_ref[...] = result
    branch = result.astype(jnp.bfloat16)
    branch_ref[...] = branch
    for own, other, do_ref in zip(own_refs, other_refs, do_refs):
        do = mm(branch[:, :half], own[...]) + mm(branch[:, half:], other[...])
        do_ref[...] = do.astype(jnp.bfloat16)


def middle_back(arrived, middle, cot, gain, own, other):
    size = len(arrived)
    rows, features = middle.shape
    width = own[0].shape[1]
    steps = 2
    wide = pl.BlockSpec((rows // steps, features), lambda i: (i, 0))
    narrow = pl.BlockSpec((rows // steps, width), lambda i: (i, 0))
    row = pl.BlockSpec((1, features), lambda i: (0, 0))
    weight = pl.BlockSpec((features // 2, width), lambda i: (0, 0), pipeline_mode=ONCE)
    grad, branch, part, *do = pl.pallas_call(
        functools.partial(middle_back_kernel, size=size),
        grid=(steps,),
        in_specs=[wide] * size + [wide, wide, row] + [weight] * (2 * size),
        out_specs=[wide, wide, row] + [narrow] * size,
        out_shape=[
            jax.ShapeDtypeStruct((rows, features), jnp.float32),
            jax.ShapeDtypeStruct((rows, features), jnp.bfloat16),
            jax.ShapeDtypeStruct((1, features), jnp.float32),
        ]
        + [jax.ShapeDtypeStruct((rows, width), jnp.bfloat16)] * size,
        compiler_params=PARAMS,
        cost_estimate=hint(2 * rows * features * width * size),
    )(*arrived, middle, cot, gain, *own, *other)
    return grad, branch, part[0], do


def column_grad(blocks, other, mine, theirs):
    rows = blocks[0].shape[0]
    total = mm_tn(other[...], theirs[...])
    for index, block in enumerate(blocks):
        total = total + mm_tn(block[...], mine[index * rows : (index + 1) * rows, :])
    return total


def grad_kernel(*refs, size):
    n_refs, e_refs = refs[:size], refs[size : 2 * size]
    n_other, e_other = refs[2 * size : 2 * size + 2]
    acts, out_ref = refs[2 * size + 2 : -1], refs[-1]
    units = acts[0].shape[1]
    for third in range(3):
        blocks, other = (e_refs, e_other) if third == 2 else (n_refs, n_other)
        grad = column_grad(blocks, other, acts[third], acts[third + 3])
        out_ref[0, :, third * units : (third + 1) * units] = grad.astype(jnp.bfloat16)


def mlp_grads(chips, tokens, cot, tokens_other, cot_other, mine, theirs):
    size = len(tokens)
    rows, features = tokens[0].shape
    total, units = mine[0].shape
    depth = features // (2 * chips)
    column = pl.BlockSpec((rows, depth), lambda b: (0, b))
    long = pl.BlockSpec((total, depth), lambda b: (0, b))
    fixed = pl.BlockSpec((total, units), lambda b: (0, 0), pipeline_mode=ONCE)
    return pl.pallas_call(
        functools.partial(grad_kernel, size=size),
        grid=(chips,),
        in_specs=[column] * (2 * size) + [long, long] + [fixed] * 6,
        out_specs=pl.BlockSpec((1, depth, 3 * units), lambda b: (b, 0, 0)),
        out_shape=jax.ShapeDtypeStruct((chips, depth, 3 * units), jnp.bfloat16),
        compiler_params=PARAMS,
        cost_estimate=hint(6 * total * features * units),
    )(*tokens, *cot, tokens_other, cot_other, *mine, *theirs)


def attn_grad_kernel(*refs, size):
    e_refs = refs[2 : 2 + size]
    n_ref, n_other = refs[:2]
    e_other, d_ref, d_other, o_ref, o_other, w_ref, g1_ref, g2_ref = refs[2 + size : -2]
    out_ref, gain_ref = refs[-2:]
    width, out_width = d_ref.shape[1], o_ref.shape[1]
    grad = column_grad([n_ref], n_other, d_ref, d_other)
    out_ref[0, :, :width] = grad.astype(jnp.bfloat16)
    out_grad = column_grad(e_refs, e_other, o_ref, o_other)
    out_ref[0, :, width : width + out_width] = out_grad.astype(jnp.bfloat16)
    first = jnp.sum(grad * w_ref[...].astype(jnp.float32), axis=1, keepdims=True) / g1_ref[...]
    lane = lane_index(grad.shape[0])
    gain_ref[0] = jnp.where(lane == 0, first, g2_ref[...])


def attn_grads(chips, tokens, branch, mine, theirs, weights, gain_one, gain_two_part):
    size = len(branch)
    qkv_grad, attended = mine
    tokens_other, branch_other, qkv_other, attended_other = theirs
    total, features = tokens.shape
    rows = total // size
    width, out_width = qkv_grad.shape[1], attended.shape[1]
    depth = features // (2 * chips)
    column = lambda b: (0, b)
    row = lambda b: (b, 0)
    long = pl.BlockSpec((total, depth), column)
    fixed = lambda array: pl.BlockSpec(array.shape, lambda b: (0, 0), pipeline_mode=ONCE)
    place = lambda b: (b, 0, 0)
    return pl.pallas_call(
        functools.partial(attn_grad_kernel, size=size),
        grid=(chips,),
        in_specs=[long, long]
        + [pl.BlockSpec((rows, depth), column)] * size
        + [long]
        + [fixed(qkv_grad)] * 2
        + [fixed(attended)] * 2
        + [
            pl.BlockSpec((depth, width), row),
            pl.BlockSpec((depth, 1), row),
            pl.BlockSpec((depth, 1), row),
        ],
        out_specs=[
            pl.BlockSpec((1, depth, width + out_width), place),
            pl.BlockSpec((1, depth, PAIR), place),
        ],
        out_shape=[
            jax.ShapeDtypeStruct((chips, depth, width + out_width), jnp.bfloat16),
            jax.ShapeDtypeStruct((chips, depth, PAIR), jnp.float32),
        ],
        compiler_params=PARAMS,
        cost_estimate=hint(2 * total * features * (width + out_width)),
    )(
        tokens,
        tokens_other,
        *branch,
        branch_other,
        qkv_grad,
        qkv_other,
        attended,
        attended_other,
        weights,
        gain_one,
        gain_two_part,
    )


def swap(values, step):
    size = lax.axis_size("tensor")
    return lax.ppermute(values, "tensor", [(i, i ^ step) for i in range(size)])


def spread(values):
    return [values] + [swap(values, step) for step in range(1, lax.axis_size("tensor"))]


def send_blocks(blocks):
    return [blocks[0]] + [swap(block, step + 1) for step, block in enumerate(blocks[1:])]


def send_rows(partial):
    size = lax.axis_size("tensor")
    return send_blocks(list(partial.reshape((size, -1) + partial.shape[1:])))


def add_up(blocks):
    total = blocks[0].astype(jnp.float32)
    for block in blocks[1:]:
        total = total + block.astype(jnp.float32)
    return total


def cross(values):
    count = lax.axis_size("dp")
    return lax.ppermute(values, "dp", [(i, i ^ 1) for i in range(count)])


def tables(positions):
    freqs = ROPE_BASE ** (-jnp.arange(0, HEAD_DIM, 2).astype(jnp.float32) / HEAD_DIM)
    angles = positions.astype(jnp.float32)[:, None] * freqs[None, :]
    cosine, sine = jnp.cos(angles), jnp.sin(angles)
    return (
        jnp.concatenate([cosine] * 4, axis=1),
        jnp.concatenate([-sine, sine, -sine, sine], axis=1),
    )


def chip_lines():
    count = lax.axis_size("dp")
    return [list(range(core, count, 2)) for core in range(2)]


def gather(values):
    return lax.all_gather(values, "dp", axis=0, tiled=True, axis_index_groups=chip_lines())


def scatter(values):
    total = lax.psum_scatter(
        values, "dp", scatter_dimension=0, tiled=True, axis_index_groups=chip_lines()
    )
    return total[0]


def small_sums(parts):
    count = lax.axis_size("dp")
    chips = count // 2
    chip = lax.axis_index("dp") // 2
    own = lax.dynamic_index_in_dim(parts, chip, 0, keepdims=False)
    for step in range(1, chips):
        sent = lax.dynamic_index_in_dim(parts, (chip + step) % chips, 0, keepdims=False)
        pairs = [(i, (i + 2 * step) % count) for i in range(count)]
        own = own + lax.ppermute(sent, "dp", pairs)
    size = lax.axis_size("tensor")
    me = lax.axis_index("tensor")
    blocks = own.reshape((size, -1) + own.shape[1:])
    own = lax.dynamic_index_in_dim(blocks, me, 0, keepdims=False)
    for step in range(1, size):
        sent = lax.dynamic_index_in_dim(blocks, me ^ step, 0, keepdims=False)
        own = own + swap(sent, step)
    return own


def other_half(blocks):
    half = blocks[0].shape[1] // 2
    return cross(jnp.concatenate([block[:, half:] for block in blocks], axis=0))


def feature_blocks(values):
    width = values.shape[-1] // lax.axis_size("dp")
    return [values[..., low : low + width] for low in range(0, values.shape[-1], width)]


def by_core(values, core):
    blocks = feature_blocks(values)
    pairs = list(zip(blocks[0::2], blocks[1::2]))
    own = [jnp.where(core == 0, even, odd) for even, odd in pairs]
    other = [jnp.where(core == 0, odd, even) for even, odd in pairs]
    return jnp.concatenate(own + other, axis=-1)


def by_device(values, core):
    blocks = feature_blocks(values)
    chips = len(blocks) // 2
    placed = []
    for own, other in zip(blocks[:chips], blocks[chips:]):
        placed += [jnp.where(core == 0, own, other), jnp.where(core == 0, other, own)]
    return jnp.concatenate(placed, axis=-1)


def per_device(
    hidden_in,
    gain_attn,
    w_query,
    w_key,
    w_value,
    w_out,
    gain_mlp,
    w_gate,
    w_up,
    w_down,
    positions,
    cotangent,
):
    size = lax.axis_size("tensor")
    chips = lax.axis_size("dp") // 2
    me = lax.axis_index("tensor")
    me_array = jnp.full((1,), me, jnp.int32)
    core = lax.axis_index("dp") % 2
    q_width, kv_width = w_query.shape[1], w_key.shape[1]
    qkv_width = q_width + 2 * kv_width
    group = q_width // kv_width
    units = w_down.shape[0] // 2
    half = hidden_in.shape[1] // 2

    attn_shard = jnp.concatenate([w_query, w_key, w_value, w_out.T], axis=1)
    attn_shard, hidden_in, gain_attn = barrier((attn_shard, hidden_in, gain_attn))
    attn_own = gather(attn_shard)
    residual = by_core(hidden_in, core)
    blocks_in = spread(residual)
    residual = residual.astype(jnp.float32)
    gains = lax.all_gather(jnp.stack([gain_attn, gain_mlp]), "dp", axis=1, tiled=True)
    gains = by_core(gains, core).astype(jnp.float32)
    cosine, sine = tables(positions)
    cotangent = by_core(cotangent, core)
    down_t = w_down.T
    shares = []
    for part in range(2):
        cut = slice(part * units, (part + 1) * units)
        shares.append(jnp.concatenate([w_gate[:, cut], w_up[:, cut], down_t[:, cut]], axis=1))
    shares, attn_own, blocks_in, cosine, sine, gains, cotangent = barrier(
        (shares, attn_own, blocks_in, cosine, sine, gains, cotangent)
    )
    mlp_own = [gather(share) for share in shares]
    cot_blocks = spread(cotangent)
    gain_one, gain_two = gains[0], gains[1]
    qkv_own, out_own = attn_own[:, :qkv_width], attn_own[:, qkv_width:]
    qkv = (qkv_own, cross(qkv_own))
    out_t = (out_own, cross(out_own))

    scale_one = rms_scale(residual)
    tokens_one, query, key_pad, value_pad = project(
        me_array, blocks_in, gain_one[None, :], *qkv, cosine, sine, q_width, kv_width
    )
    attended, log_total, *parts = attend(
        me_array, query, key_pad, value_pad, *out_t, size, group
    )
    parts, cot_blocks, tokens_one, attended = barrier((parts, cot_blocks, tokens_one, attended))
    arrived = send_blocks(parts)
    cot_other = other_half(cot_blocks)
    early = (cross(tokens_one[:, half:]), cross(attended))
    arrived, cot_other, early = barrier((arrived, cot_other, early))
    middle = residual + add_up(arrived)

    scale_two = rms_scale(middle)
    normed_two = (middle * scale_two * gain_two).astype(jnp.bfloat16)
    tokens_two = spread(normed_two)
    first, own_share = barrier((tokens_two[: size - 1], mlp_own[0]))
    tokens_two = first + tokens_two[size - 1 :]
    weights = (own_share, cross(own_share))
    tokens_two, weights, out_own = barrier((tokens_two, weights, out_t[0]))
    tokens_other = other_half(tokens_two)
    *acts, dn_part, y_part = mlp(tokens_two, cot_blocks, *weights, ())
    out_blocks = spread(out_own)
    acts, tokens_other = barrier((acts, tokens_other))
    acts_other = [cross(act) for act in acts]
    grads_one = mlp_grads(
        chips, tokens_two, cot_blocks, tokens_other, cot_other, acts, acts_other
    )
    grads_one, own_share, out_blocks = barrier((grads_one, mlp_own[1], out_blocks))
    sums_one = scatter(grads_one)
    weights = (own_share, cross(own_share))
    *acts, dn_part, y_part = mlp(tokens_two, cot_blocks, *weights, (dn_part, y_part))
    out_other = [out_t[1]] + [cross(block) for block in out_blocks[1:]]
    acts, dn_part, out_other = barrier((acts, dn_part, out_other))
    arrived = send_rows(dn_part)
    acts_other = [cross(act) for act in acts]
    grads_two = mlp_grads(
        chips, tokens_two, cot_blocks, tokens_other, cot_other, acts, acts_other
    )
    grads_two, arrived = barrier((grads_two, arrived))
    sums_two = scatter(grads_two)
    middle_grad, branch, gain_two_part, do_blocks = middle_back(
        arrived, middle, cotangent, gain_two[None, :], out_blocks, out_other
    )
    do_blocks = send_blocks(do_blocks)
    gain_two_other = cross(gain_two_part[half:])
    do_blocks, branch, gain_two_other, y_part = barrier(
        (do_blocks, branch, gain_two_other, y_part)
    )
    branch_blocks = spread(branch)
    qkv_grad = attend_back(
        me_array, query, log_total, key_pad, value_pad, cosine, sine, do_blocks, group
    )
    branch_blocks, qkv_grad, y_part, sums_one = barrier(
        (branch_blocks, qkv_grad, y_part, sums_one)
    )
    down_arrived = send_rows(y_part)
    branch_other = other_half(branch_blocks)
    qkv_other = cross(qkv_grad)
    tokens_other, attended_other = early
    grads = attn_grads(
        chips,
        tokens_one,
        branch_blocks,
        (qkv_grad, attended),
        (tokens_other, branch_other, qkv_other, attended_other),
        qkv[0],
        gain_one[:half, None],
        (gain_two_part[:half] + gain_two_other)[:, None],
    )
    attn_sums = scatter(grads[0])
    grads, qkv_grad = barrier((grads, qkv_grad))
    normed_part = jnp.concatenate([mm_nt(qkv_grad, w) for w in qkv], axis=1).astype(jnp.bfloat16)
    normed_part, down_arrived, sums_two = barrier((normed_part, down_arrived, sums_two))
    arrived = send_rows(normed_part)
    gain_sums = small_sums(grads[1][:, :, :2])
    out = by_device((middle + add_up(down_arrived)).astype(jnp.bfloat16), core)
    shares = [share.astype(jnp.float32) for share in (sums_one, sums_two)]
    grad_gate = jnp.concatenate([h[:, :units] for h in shares], axis=1)
    grad_up = jnp.concatenate([h[:, units : 2 * units] for h in shares], axis=1)
    grad_down = jnp.concatenate([h[:, 2 * units :].T for h in shares], axis=0)
    arrived, gain_sums, out, attn_sums, grad_gate, grad_up, grad_down = barrier(
        (arrived, gain_sums, out, attn_sums, grad_gate, grad_up, grad_down)
    )
    attn_sums = attn_sums.astype(jnp.float32)
    normed_one_grad = add_up(arrived)
    input_norm_grad, _ = norm_back(normed_one_grad, residual, scale_one, gain_one)
    grad_in = by_device(middle_grad + input_norm_grad, core)

    return (
        out,
        grad_in,
        gain_sums[:, 0],
        attn_sums[:, :q_width],
        attn_sums[:, q_width : q_width + kv_width],
        attn_sums[:, q_width + kv_width : qkv_width],
        attn_sums[:, qkv_width : qkv_width + q_width].T,
        gain_sums[:, 1],
        grad_gate,
        grad_up,
        grad_down,
    )


def solution(mesh):
    return jax.shard_map(
        per_device,
        mesh=mesh,
        in_specs=(
            P(("dp", "tensor"), None),
            P("dp"),
            P("dp", "tensor"),
            P("dp", "tensor"),
            P("dp", "tensor"),
            P("tensor", "dp"),
            P("dp"),
            P("dp", "tensor"),
            P("dp", "tensor"),
            P("tensor", "dp"),
            P("dp"),
            P(("dp", "tensor"), None),
        ),
        out_specs=(
            P(("dp", "tensor"), None),
            P(("dp", "tensor"), None),
            P(("dp", "tensor")),
            P("dp", "tensor"),
            P("dp", "tensor"),
            P("dp", "tensor"),
            P("tensor", "dp"),
            P(("dp", "tensor")),
            P("dp", "tensor"),
            P("dp", "tensor"),
            P("tensor", "dp"),
        ),
        check_vma=False,
    )
```

```python
import functools
import math

import jax
import jax.numpy as jnp
from jax import lax
from jax.experimental import pallas as pl
from jax.experimental.pallas import tpu as pltpu
from jax.sharding import PartitionSpec as P

HEAD_DIM = 64
PAIR = 2 * HEAD_DIM
SEQ_LEN = 1024


EPS = 1e-05
ROPE_BASE = 500000.0
SCALE = 1.0 / math.sqrt(HEAD_DIM)
PARAMS = pltpu.CompilerParams(vmem_limit_bytes=58 * 2**20)
ONCE = pl.Buffered(1)

barrier = lax.optimization_barrier


def hint(flops):
    return pl.CostEstimate(flops=flops, bytes_accessed=0, transcendentals=0)


def rms_scale(values):
    return lax.rsqrt(jnp.mean(values * values, axis=-1, keepdims=True) + EPS)


def norm_back(grad, values, scale, gain):
    inner = grad * gain
    cubed = scale * scale * scale
    result = scale * inner - values * cubed * jnp.mean(inner * values, axis=-1, keepdims=True)
    return (result, jnp.sum(grad * values * scale, axis=0))


def mm(left, right):
    return jnp.dot(left, right, preferred_element_type=jnp.float32)


def mm_nt(left, right):
    return lax.dot_general(left, right, (((1,), (1,)), ((), ())), preferred_element_type=jnp.float32)


def mm_tn(left, right):
    return lax.dot_general(left, right, (((0,), (0,)), ((), ())), preferred_element_type=jnp.float32)


def lane_index(rows):
    return lax.broadcasted_iota(jnp.int32, (rows, PAIR), 1)


def turn(pair, cosine, sine):
    lower = lane_index(pair.shape[0]) % HEAD_DIM < HEAD_DIM // 2
    other = jnp.where(
        lower, pltpu.roll(pair, PAIR - HEAD_DIM // 2, 1), pltpu.roll(pair, HEAD_DIM // 2, 1)
    )
    return pair * cosine + other * sine


def project_kernel(place_ref, *refs, size, q_width, kv_width):
    x_refs = refs[:size]
    gain_ref, wo_ref, wx_ref, cos_ref, sin_ref, n_ref, q_ref, k_ref, v_ref = refs[size:]
    rows = q_ref.shape[0]
    half = wo_ref.shape[0]

    def one(x_ref):
        x = x_ref[...].astype(jnp.float32)
        normed = (x * rms_scale(x) * gain_ref[...]).astype(jnp.bfloat16)
        n_ref[...] = normed
        cosine, sine = cos_ref[...], sin_ref[...]
        lin = mm(normed[:, :half], wo_ref[...]) + mm(normed[:, half:], wx_ref[...])
        for low in range(0, q_width, PAIR):
            query = turn(lin[:, low : low + PAIR], cosine, sine).astype(jnp.bfloat16)
            q_ref[:, low : low + PAIR] = query * jnp.bfloat16(SCALE)
        first = lane_index(rows) < HEAD_DIM
        for ref, start, rotate in ((k_ref, q_width, True), (v_ref, q_width + kv_width, False)):
            for head in range(kv_width // HEAD_DIM):
                low = start + head * HEAD_DIM
                block = lin[:, low // PAIR * PAIR : low // PAIR * PAIR + PAIR]
                if rotate:
                    block = turn(block, cosine, sine)
                moved = pltpu.roll(block, HEAD_DIM, 1)
                if low % PAIR:
                    block, moved = moved, block
                ref[head, 0] = jnp.where(first, block, 0.0).astype(jnp.bfloat16)
                ref[head, 1] = jnp.where(first, 0.0, moved).astype(jnp.bfloat16)

    for step in range(size):
        pl.when(pl.program_id(0) == step)(functools.partial(one, x_refs[step]))


def project(me, blocks, gain, own, other, cosine, sine, q_width, kv_width):
    size = len(blocks)
    rows, features = blocks[0].shape
    total = rows * size
    key_heads = kv_width // HEAD_DIM
    width = q_width + 2 * kv_width
    fixed = lambda p, m: (0, 0)
    placed = lambda p, m: (jnp.bitwise_xor(p, m[0]), 0)
    padded = pl.BlockSpec(
        (key_heads, 2, rows, PAIR), lambda p, m: (0, 0, jnp.bitwise_xor(p, m[0]), 0)
    )
    spec = pltpu.PrefetchScalarGridSpec(
        num_scalar_prefetch=1,
        grid=(size,),
        in_specs=[pl.BlockSpec((rows, features), fixed, pipeline_mode=ONCE)] * size
        + [
            pl.BlockSpec((1, features), fixed),
            pl.BlockSpec((features // 2, width), fixed, pipeline_mode=ONCE),
            pl.BlockSpec((features // 2, width), fixed, pipeline_mode=ONCE),
            pl.BlockSpec((rows, PAIR), placed),
            pl.BlockSpec((rows, PAIR), placed),
        ],
        out_specs=[
            pl.BlockSpec((rows, features), lambda p, m: (p, 0)),
            pl.BlockSpec((rows, q_width), lambda p, m: (p, 0)),
            padded,
            padded,
        ],
    )
    padded_shape = jax.ShapeDtypeStruct((key_heads, 2, total, PAIR), jnp.bfloat16)
    return pl.pallas_call(
        functools.partial(project_kernel, size=size, q_width=q_width, kv_width=kv_width),
        grid_spec=spec,
        out_shape=[
            jax.ShapeDtypeStruct((total, features), jnp.bfloat16),
            jax.ShapeDtypeStruct((total, q_width), jnp.bfloat16),
            padded_shape,
            padded_shape,
        ],
        compiler_params=PARAMS,
        cost_estimate=hint(2 * total * features * width),
    )(me, *blocks, gain, own, other, cosine, sine)


def attend_kernel(
    me_ref, q_ref, k_ref, v_ref, wo_ref, wx_ref, o_ref, l_ref, *refs, size, heads, group
):
    part_refs, vt_ref = refs[:size], refs[size]
    rows = q_ref.shape[0]
    half = wo_ref.shape[0]
    mine = jnp.bitwise_xor(me_ref[0], pl.program_id(0))
    key_place = lax.broadcasted_iota(jnp.int32, (rows, rows), 0)
    query_place = lax.broadcasted_iota(jnp.int32, (rows, rows), 1)

    @pl.when(pl.program_id(0) == 0)
    def _():
        for head in range(heads // group):
            for side in range(2):
                vt_ref[head, side] = v_ref[head, side].T

    def one(span):
        keys = span * rows
        for pair in range(heads // 2):
            head = 2 * pair // group
            lanes = slice(pair * PAIR, (pair + 1) * PAIR)
            query = q_ref[:, lanes]
            acc = None
            inverse = []
            for side in range(2):
                diag = mm_nt(k_ref[head, side, keys : keys + rows, :], query)
                diag = jnp.where(key_place <= query_place, diag, -1e9)
                top = jnp.max(diag, axis=0, keepdims=True)
                if span:
                    body = mm_nt(k_ref[head, side, :keys, :], query)
                    top = jnp.maximum(top, jnp.max(body, axis=0, keepdims=True))
                diag = jnp.exp(diag - top)
                total = jnp.sum(diag, axis=0, keepdims=True)
                part = mm(vt_ref[head, side, :, keys : keys + rows], diag.astype(jnp.bfloat16))
                if span:
                    body = jnp.exp(body - top)
                    total = total + jnp.sum(body, axis=0, keepdims=True)
                    part = part + mm(vt_ref[head, side, :, :keys], body.astype(jnp.bfloat16))
                acc = part if acc is None else acc + part
                inverse.append(jnp.broadcast_to(1.0 / total, (HEAD_DIM, rows)))
                l_ref[2 * pair + side : 2 * pair + side + 1, :] = top + jnp.log(total)
            acc = acc * jnp.concatenate(inverse, axis=0)
            o_ref[:, lanes] = acc.T.astype(jnp.bfloat16)

    for span in range(size):
        pl.when(mine == span)(functools.partial(one, span))

    def project_out(ref):
        ref[:, :half] = mm_nt(o_ref[...], wo_ref[...]).astype(jnp.bfloat16)
        ref[:, half:] = mm_nt(o_ref[...], wx_ref[...]).astype(jnp.bfloat16)

    for step in range(size):
        pl.when(pl.program_id(0) == step)(functools.partial(project_out, part_refs[step]))


def attend(me, query, key_pad, value_pad, own, other, size, group):
    total, width = query.shape
    features = 2 * own.shape[0]
    rows, heads = total // size, width // HEAD_DIM
    whole = pl.BlockSpec(key_pad.shape, lambda p, m: (0, 0, 0, 0), pipeline_mode=ONCE)
    spec = pltpu.PrefetchScalarGridSpec(
        num_scalar_prefetch=1,
        grid=(size,),
        in_specs=[pl.BlockSpec((rows, width), lambda p, m: (p, 0)), whole, whole]
        + [pl.BlockSpec(own.shape, lambda p, m: (0, 0), pipeline_mode=ONCE)] * 2,
        out_specs=[
            pl.BlockSpec((rows, width), lambda p, m: (p, 0)),
            pl.BlockSpec((heads, rows), lambda p, m: (0, p)),
        ]
        + [pl.BlockSpec((rows, features), lambda p, m: (0, 0))] * size,
        scratch_shapes=[pltpu.VMEM((heads // group, 2, PAIR, total), jnp.bfloat16)],
    )
    return pl.pallas_call(
        functools.partial(attend_kernel, size=size, heads=heads, group=group),
        grid_spec=spec,
        out_shape=[
            jax.ShapeDtypeStruct((total, width), jnp.bfloat16),
            jax.ShapeDtypeStruct((heads, total), jnp.float32),
        ]
        + [jax.ShapeDtypeStruct((rows, features), jnp.bfloat16)] * size,
        compiler_params=PARAMS,
        cost_estimate=hint(8 * heads * total * total * HEAD_DIM),
    )(me, query, key_pad, value_pad, own, other)


def attend_back_kernel(
    me_ref, q_ref, l_ref, k_ref, v_ref, cos_ref, sin_ref, *refs, size, heads, group
):
    do_refs = refs[:size]
    out_ref, dk_ref, dv_ref, kt_ref, do_ref = refs[size:]
    rows = q_ref.shape[0]
    key_heads = heads // group
    step = pl.program_id(0)
    me = me_ref[0]
    mine = jnp.bitwise_xor(me, step)
    key_place = lax.broadcasted_iota(jnp.int32, (rows, rows), 0)
    query_place = lax.broadcasted_iota(jnp.int32, (rows, rows), 1)

    def rows_of(block):
        return pl.ds(pl.multiple_of(block * rows, rows), rows)

    @pl.when(step == 0)
    def _():
        dk_ref[...] = jnp.zeros_like(dk_ref)
        dv_ref[...] = jnp.zeros_like(dv_ref)
        for head in range(key_heads):
            for side in range(2):
                kt_ref[head, side] = k_ref[head, side].T

    def fetch(ref):
        do_ref[...] = ref[...]

    for block in range(size):
        pl.when(step == block)(functools.partial(fetch, do_refs[block]))

    def one(span):
        keys = span * rows
        parts = [(keys, keys + rows, True)] + ([(0, keys, False)] if span else [])
        cosine, sine = cos_ref[keys : keys + rows, :], sin_ref[keys : keys + rows, :]
        for pair in range(heads // 2):
            head = 2 * pair // group
            lanes = slice(pair * PAIR, (pair + 1) * PAIR)
            query, grad = q_ref[:, lanes], do_ref[:, lanes]
            acc = None
            for side in range(2):
                log_total = l_ref[2 * pair + side : 2 * pair + side + 1, :]
                inner = None
                kept = []
                for low, high, diagonal in parts:
                    probs = mm_nt(k_ref[head, side, low:high, :], query)
                    probs = jnp.exp(probs - log_total)
                    if diagonal:
                        probs = jnp.where(key_place <= query_place, probs, 0.0)
                    prob_grad = mm_nt(v_ref[head, side, low:high, :], grad)
                    dv_ref[head, side, low:high, :] += mm(probs.astype(jnp.bfloat16), grad)
                    term = jnp.sum(probs * prob_grad, axis=0, keepdims=True)
                    inner = term if inner is None else inner + term
                    kept.append((low, high, probs, prob_grad))
                for low, high, probs, prob_grad in kept:
                    score_grad = (probs * (prob_grad - inner)).astype(jnp.bfloat16)
                    dk_ref[head, side, low:high, :] += mm(score_grad, query)
                    part = mm(kt_ref[head, side, :, low:high], score_grad)
                    acc = part if acc is None else acc + part
            turned = turn(acc.T * SCALE, cosine, -sine)
            out_ref[rows_of(step), lanes] = turned.astype(jnp.bfloat16)

    for span in range(size):
        pl.when(mine == span)(functools.partial(one, span))

    @pl.when(step == size - 1)
    def _():
        first = lane_index(rows) < HEAD_DIM
        wanted = [(dk_ref, head, True) for head in range(key_heads)]
        wanted += [(dv_ref, head, False) for head in range(key_heads)]
        for span in range(size):
            place = slice(span * rows, (span + 1) * rows)
            cosine, sine = cos_ref[place, :], sin_ref[place, :]
            for block in range(len(wanted) // 2):
                halves, rotate = [], []
                for half in range(2):
                    ref, head, is_key = wanted[2 * block + half]
                    low, high = ref[head, 0, place, :], ref[head, 1, place, :]
                    if half:
                        halves.append(pltpu.roll(low, HEAD_DIM, 1) + high)
                    else:
                        halves.append(low + pltpu.roll(high, HEAD_DIM, 1))
                    rotate.append(is_key)
                value = jnp.where(first, halves[0], halves[1])
                if rotate[0] and rotate[1]:
                    value = turn(value, cosine, -sine)
                elif rotate[0]:
                    value = jnp.where(first, turn(value, cosine, -sine), value)
                start = heads * HEAD_DIM + block * PAIR
                target = rows_of(jnp.bitwise_xor(me, span))
                out_ref[target, start : start + PAIR] = value.astype(jnp.bfloat16)


def attend_back(
    me, query, log_total, key_pad, value_pad, cosine, sine, attended_grad, group
):
    total, width = query.shape
    size = len(attended_grad)
    rows, heads = total // size, width // HEAD_DIM
    key_heads = heads // group
    out_width = width + 2 * key_heads * HEAD_DIM
    whole = pl.BlockSpec(key_pad.shape, lambda p, m: (0, 0, 0, 0), pipeline_mode=ONCE)
    table = pl.BlockSpec((total, PAIR), lambda p, m: (0, 0), pipeline_mode=ONCE)
    spec = pltpu.PrefetchScalarGridSpec(
        num_scalar_prefetch=1,
        grid=(size,),
        in_specs=[
            pl.BlockSpec((rows, width), lambda p, m: (p, 0)),
            pl.BlockSpec((heads, rows), lambda p, m: (0, p)),
            whole,
            whole,
            table,
            table,
        ]
        + [pl.BlockSpec((rows, width), lambda p, m: (0, 0), pipeline_mode=ONCE)] * size,
        out_specs=pl.BlockSpec((total, out_width), lambda p, m: (0, 0)),
        scratch_shapes=[
            pltpu.VMEM(key_pad.shape, jnp.float32),
            pltpu.VMEM(key_pad.shape, jnp.float32),
            pltpu.VMEM((key_heads, 2, PAIR, total), jnp.bfloat16),
            pltpu.VMEM((rows, width), jnp.bfloat16),
        ],
    )
    return pl.pallas_call(
        functools.partial(attend_back_kernel, size=size, heads=heads, group=group),
        grid_spec=spec,
        out_shape=jax.ShapeDtypeStruct((total, out_width), jnp.bfloat16),
        compiler_params=PARAMS,
        cost_estimate=hint(20 * heads * total * total * HEAD_DIM),
    )(me, query, log_total, key_pad, value_pad, cosine, sine, *attended_grad)


def mlp_kernel(*refs, size, adds):
    n_refs, e_refs = refs[:size], refs[size : 2 * size]
    gate_o, up_o, down_o, gate_x, up_x, down_x = refs[2 * size : 2 * size + 6]
    dg_ref, du_ref, h_ref, dn_ref, y_ref, n_ref, e_ref = refs[-7:]
    half = gate_o.shape[0]

    def fetch(step):
        n_ref[...] = n_refs[step][...]
        e_ref[...] = e_refs[step][...]

    for step in range(size):
        pl.when(pl.program_id(0) == step)(functools.partial(fetch, step))
    gate = mm(n_ref[:, :half], gate_o[...]) + mm(n_ref[:, half:], gate_x[...])
    up = mm(n_ref[:, :half], up_o[...]) + mm(n_ref[:, half:], up_x[...])
    grad = mm(e_ref[:, :half], down_o[...]) + mm(e_ref[:, half:], down_x[...])
    sigma = jax.nn.sigmoid(gate)
    silu = gate * sigma
    hidden = (silu * up).astype(jnp.bfloat16)
    gate_grad = (grad * up * sigma * (1.0 + gate * (1.0 - sigma))).astype(jnp.bfloat16)
    up_grad = (grad * silu).astype(jnp.bfloat16)
    dg_ref[...] = gate_grad
    du_ref[...] = up_grad
    h_ref[...] = hidden
    for part, gate_w, up_w, down_w in ((0, gate_o, up_o, down_o), (1, gate_x, up_x, down_x)):
        lanes = slice(part * half, (part + 1) * half)
        dn = mm_nt(gate_grad, gate_w[...]) + mm_nt(up_grad, up_w[...])
        y = mm_nt(hidden, down_w[...])
        if adds:
            dn = dn + refs[2 * size + 6][:, lanes].astype(jnp.float32)
            y = y + refs[2 * size + 7][:, lanes].astype(jnp.float32)
        dn_ref[:, lanes] = dn.astype(dn_ref.dtype)
        y_ref[:, lanes] = y.astype(y_ref.dtype)


def mlp(tokens, cot, own, other, earlier):
    size = len(tokens)
    rows, features = tokens[0].shape
    half, units = own.shape[0], own.shape[1] // 3
    total = rows * size
    fixed = lambda p: (0, 0)
    moving = lambda p: (p, 0)
    wide = pl.BlockSpec((rows, features), moving)
    sums = jax.ShapeDtypeStruct((total, features), jnp.bfloat16)
    block = pl.BlockSpec((rows, features), fixed, pipeline_mode=ONCE)
    thirds = [
        pl.BlockSpec((half, units), lambda p, t=t: (0, t), pipeline_mode=ONCE) for t in range(3)
    ]
    return pl.pallas_call(
        functools.partial(mlp_kernel, size=size, adds=bool(earlier)),
        grid=(size,),
        in_specs=[block] * (2 * size)
        + thirds * 2
        + [wide] * len(earlier),
        out_specs=[pl.BlockSpec((rows, units), moving)] * 3 + [wide, wide],
        out_shape=[jax.ShapeDtypeStruct((total, units), jnp.bfloat16)] * 3 + [sums, sums],
        scratch_shapes=[pltpu.VMEM((rows, features), jnp.bfloat16)] * 2,
        compiler_params=PARAMS,
        cost_estimate=hint(12 * total * features * units),
    )(*tokens, *cot, own, own, own, other, other, other, *earlier)


def middle_back_kernel(*refs, size):
    n_refs, refs = refs[:size], refs[size:]
    x_ref, e_ref, gain_ref, refs = refs[0], refs[1], refs[2], refs[3:]
    own_refs, other_refs, refs = refs[:size], refs[size : 2 * size], refs[2 * size :]
    grad_ref, branch_ref, part_ref, do_refs = refs[0], refs[1], refs[2], refs[3:]
    half = own_refs[0].shape[0]
    grad = n_refs[0][...].astype(jnp.float32)
    for ref in n_refs[1:]:
        grad = grad + ref[...].astype(jnp.float32)
    values = x_ref[...]
    scale = rms_scale(values)
    result, part = norm_back(grad, values, scale, gain_ref[...])

    @pl.when(pl.program_id(0) == 0)
    def _():
        part_ref[...] = jnp.zeros_like(part_ref)

    part_ref[...] += part[None, :]
    result = result + e_ref[...].astype(jnp.float32)
    grad_ref[...] = result
    branch = result.astype(jnp.bfloat16)
    branch_ref[...] = branch
    for own, other, do_ref in zip(own_refs, other_refs, do_refs):
        do = mm(branch[:, :half], own[...]) + mm(branch[:, half:], other[...])
        do_ref[...] = do.astype(jnp.bfloat16)


def middle_back(arrived, middle, cot, gain, own, other):
    size = len(arrived)
    rows, features = middle.shape
    width = own[0].shape[1]
    steps = 2
    wide = pl.BlockSpec((rows // steps, features), lambda i: (i, 0))
    narrow = pl.BlockSpec((rows // steps, width), lambda i: (i, 0))
    row = pl.BlockSpec((1, features), lambda i: (0, 0))
    weight = pl.BlockSpec((features // 2, width), lambda i: (0, 0), pipeline_mode=ONCE)
    grad, branch, part, *do = pl.pallas_call(
        functools.partial(middle_back_kernel, size=size),
        grid=(steps,),
        in_specs=[wide] * size + [wide, wide, row] + [weight] * (2 * size),
        out_specs=[wide, wide, row] + [narrow] * size,
        out_shape=[
            jax.ShapeDtypeStruct((rows, features), jnp.float32),
            jax.ShapeDtypeStruct((rows, features), jnp.bfloat16),
            jax.ShapeDtypeStruct((1, features), jnp.float32),
        ]
        + [jax.ShapeDtypeStruct((rows, width), jnp.bfloat16)] * size,
        compiler_params=PARAMS,
        cost_estimate=hint(2 * rows * features * width * size),
    )(*arrived, middle, cot, gain, *own, *other)
    return grad, branch, part[0], do


def column_grad(blocks, other, mine, theirs):
    rows = blocks[0].shape[0]
    total = mm_tn(other[...], theirs[...])
    for index, block in enumerate(blocks):
        total = total + mm_tn(block[...], mine[index * rows : (index + 1) * rows, :])
    return total


def grad_kernel(*refs, size):
    n_refs, e_refs = refs[:size], refs[size : 2 * size]
    n_other, e_other = refs[2 * size : 2 * size + 2]
    acts, out_ref = refs[2 * size + 2 : -1], refs[-1]
    units = acts[0].shape[1]
    for third in range(3):
        blocks, other = (e_refs, e_other) if third == 2 else (n_refs, n_other)
        grad = column_grad(blocks, other, acts[third], acts[third + 3])
        out_ref[0, :, third * units : (third + 1) * units] = grad.astype(jnp.bfloat16)


def mlp_grads(chips, tokens, cot, tokens_other, cot_other, mine, theirs):
    size = len(tokens)
    rows, features = tokens[0].shape
    total, units = mine[0].shape
    depth = features // (2 * chips)
    column = pl.BlockSpec((rows, depth), lambda b: (0, b))
    long = pl.BlockSpec((total, depth), lambda b: (0, b))
    fixed = pl.BlockSpec((total, units), lambda b: (0, 0), pipeline_mode=ONCE)
    return pl.pallas_call(
        functools.partial(grad_kernel, size=size),
        grid=(chips,),
        in_specs=[column] * (2 * size) + [long, long] + [fixed] * 6,
        out_specs=pl.BlockSpec((1, depth, 3 * units), lambda b: (b, 0, 0)),
        out_shape=jax.ShapeDtypeStruct((chips, depth, 3 * units), jnp.bfloat16),
        compiler_params=PARAMS,
        cost_estimate=hint(6 * total * features * units),
    )(*tokens, *cot, tokens_other, cot_other, *mine, *theirs)


def attn_grad_kernel(*refs, size):
    e_refs = refs[2 : 2 + size]
    n_ref, n_other = refs[:2]
    e_other, d_ref, d_other, o_ref, o_other, w_ref, g1_ref, g2_ref = refs[2 + size : -2]
    out_ref, gain_ref = refs[-2:]
    width, out_width = d_ref.shape[1], o_ref.shape[1]
    grad = column_grad([n_ref], n_other, d_ref, d_other)
    out_ref[0, :, :width] = grad.astype(jnp.bfloat16)
    out_grad = column_grad(e_refs, e_other, o_ref, o_other)
    out_ref[0, :, width : width + out_width] = out_grad.astype(jnp.bfloat16)
    first = jnp.sum(grad * w_ref[...].astype(jnp.float32), axis=1, keepdims=True) / g1_ref[...]
    lane = lane_index(grad.shape[0])
    gain_ref[0] = jnp.where(lane == 0, first, g2_ref[...])


def attn_grads(chips, tokens, branch, mine, theirs, weights, gain_one, gain_two_part):
    size = len(branch)
    qkv_grad, attended = mine
    tokens_other, branch_other, qkv_other, attended_other = theirs
    total, features = tokens.shape
    rows = total // size
    width, out_width = qkv_grad.shape[1], attended.shape[1]
    depth = features // (2 * chips)
    column = lambda b: (0, b)
    row = lambda b: (b, 0)
    long = pl.BlockSpec((total, depth), column)
    fixed = lambda array: pl.BlockSpec(array.shape, lambda b: (0, 0), pipeline_mode=ONCE)
    place = lambda b: (b, 0, 0)
    return pl.pallas_call(
        functools.partial(attn_grad_kernel, size=size),
        grid=(chips,),
        in_specs=[long, long]
        + [pl.BlockSpec((rows, depth), column)] * size
        + [long]
        + [fixed(qkv_grad)] * 2
        + [fixed(attended)] * 2
        + [
            pl.BlockSpec((depth, width), row),
            pl.BlockSpec((depth, 1), row),
            pl.BlockSpec((depth, 1), row),
        ],
        out_specs=[
            pl.BlockSpec((1, depth, width + out_width), place),
            pl.BlockSpec((1, depth, PAIR), place),
        ],
        out_shape=[
            jax.ShapeDtypeStruct((chips, depth, width + out_width), jnp.bfloat16),
            jax.ShapeDtypeStruct((chips, depth, PAIR), jnp.float32),
        ],
        compiler_params=PARAMS,
        cost_estimate=hint(2 * total * features * (width + out_width)),
    )(
        tokens,
        tokens_other,
        *branch,
        branch_other,
        qkv_grad,
        qkv_other,
        attended,
        attended_other,
        weights,
        gain_one,
        gain_two_part,
    )


def swap(values, step):
    size = lax.axis_size("tensor")
    return lax.ppermute(values, "tensor", [(i, i ^ step) for i in range(size)])


def spread(values):
    return [values] + [swap(values, step) for step in range(1, lax.axis_size("tensor"))]


def send_blocks(blocks):
    return [blocks[0]] + [swap(block, step + 1) for step, block in enumerate(blocks[1:])]


def send_rows(partial):
    size = lax.axis_size("tensor")
    return send_blocks(list(partial.reshape((size, -1) + partial.shape[1:])))


def add_up(blocks):
    total = blocks[0].astype(jnp.float32)
    for block in blocks[1:]:
        total = total + block.astype(jnp.float32)
    return total


def cross(values):
    count = lax.axis_size("dp")
    return lax.ppermute(values, "dp", [(i, i ^ 1) for i in range(count)])


def tables(positions):
    freqs = ROPE_BASE ** (-jnp.arange(0, HEAD_DIM, 2).astype(jnp.float32) / HEAD_DIM)
    angles = positions.astype(jnp.float32)[:, None] * freqs[None, :]
    cosine, sine = jnp.cos(angles), jnp.sin(angles)
    return (
        jnp.concatenate([cosine] * 4, axis=1),
        jnp.concatenate([-sine, sine, -sine, sine], axis=1),
    )


def chip_lines():
    count = lax.axis_size("dp")
    return [list(range(core, count, 2)) for core in range(2)]


def gather(values):
    return lax.all_gather(values, "dp", axis=0, tiled=True, axis_index_groups=chip_lines())


def scatter(values):
    total = lax.psum_scatter(
        values, "dp", scatter_dimension=0, tiled=True, axis_index_groups=chip_lines()
    )
    return total[0]


def small_sums(parts):
    count = lax.axis_size("dp")
    chips = count // 2
    chip = lax.axis_index("dp") // 2
    own = lax.dynamic_index_in_dim(parts, chip, 0, keepdims=False)
    for step in range(1, chips):
        sent = lax.dynamic_index_in_dim(parts, (chip + step) % chips, 0, keepdims=False)
        pairs = [(i, (i + 2 * step) % count) for i in range(count)]
        own = own + lax.ppermute(sent, "dp", pairs)
    size = lax.axis_size("tensor")
    me = lax.axis_index("tensor")
    blocks = own.reshape((size, -1) + own.shape[1:])
    own = lax.dynamic_index_in_dim(blocks, me, 0, keepdims=False)
    for step in range(1, size):
        sent = lax.dynamic_index_in_dim(blocks, me ^ step, 0, keepdims=False)
        own = own + swap(sent, step)
    return own


def other_half(blocks):
    half = blocks[0].shape[1] // 2
    return cross(jnp.concatenate([block[:, half:] for block in blocks], axis=0))


def feature_blocks(values):
    width = values.shape[-1] // lax.axis_size("dp")
    return [values[..., low : low + width] for low in range(0, values.shape[-1], width)]


def by_core(values, core):
    blocks = feature_blocks(values)
    pairs = list(zip(blocks[0::2], blocks[1::2]))
    own = [jnp.where(core == 0, even, odd) for even, odd in pairs]
    other = [jnp.where(core == 0, odd, even) for even, odd in pairs]
    return jnp.concatenate(own + other, axis=-1)


def by_device(values, core):
    blocks = feature_blocks(values)
    chips = len(blocks) // 2
    placed = []
    for own, other in zip(blocks[:chips], blocks[chips:]):
        placed += [jnp.where(core == 0, own, other), jnp.where(core == 0, other, own)]
    return jnp.concatenate(placed, axis=-1)


def per_device(
    hidden_in,
    gain_attn,
    w_query,
    w_key,
    w_value,
    w_out,
    gain_mlp,
    w_gate,
    w_up,
    w_down,
    positions,
    cotangent,
):
    size = lax.axis_size("tensor")
    chips = lax.axis_size("dp") // 2
    me = lax.axis_index("tensor")
    me_array = jnp.full((1,), me, jnp.int32)
    core = lax.axis_index("dp") % 2
    q_width, kv_width = w_query.shape[1], w_key.shape[1]
    qkv_width = q_width + 2 * kv_width
    group = q_width // kv_width
    units = w_down.shape[0] // 2
    half = hidden_in.shape[1] // 2

    attn_shard = jnp.concatenate([w_query, w_key, w_value, w_out.T], axis=1)
    attn_shard, hidden_in, gain_attn = barrier((attn_shard, hidden_in, gain_attn))
    attn_own = gather(attn_shard)
    residual = by_core(hidden_in, core)
    blocks_in = spread(residual)
    residual = residual.astype(jnp.float32)
    gains = lax.all_gather(jnp.stack([gain_attn, gain_mlp]), "dp", axis=1, tiled=True)
    gains = by_core(gains, core).astype(jnp.float32)
    cosine, sine = tables(positions)
    cotangent = by_core(cotangent, core)
    down_t = w_down.T
    shares = []
    for part in range(2):
        cut = slice(part * units, (part + 1) * units)
        shares.append(jnp.concatenate([w_gate[:, cut], w_up[:, cut], down_t[:, cut]], axis=1))
    shares, attn_own, blocks_in, cosine, sine, gains, cotangent = barrier(
        (shares, attn_own, blocks_in, cosine, sine, gains, cotangent)
    )
    mlp_own = [gather(share) for share in shares]
    cot_blocks = spread(cotangent)
    gain_one, gain_two = gains[0], gains[1]
    qkv_own, out_own = attn_own[:, :qkv_width], attn_own[:, qkv_width:]
    qkv = (qkv_own, cross(qkv_own))
    out_t = (out_own, cross(out_own))

    scale_one = rms_scale(residual)
    tokens_one, query, key_pad, value_pad = project(
        me_array, blocks_in, gain_one[None, :], *qkv, cosine, sine, q_width, kv_width
    )
    attended, log_total, *parts = attend(
        me_array, query, key_pad, value_pad, *out_t, size, group
    )
    parts, cot_blocks, tokens_one, attended = barrier((parts, cot_blocks, tokens_one, attended))
    arrived = send_blocks(parts)
    cot_other = other_half(cot_blocks)
    early = (cross(tokens_one[:, half:]), cross(attended))
    arrived, cot_other, early = barrier((arrived, cot_other, early))
    middle = residual + add_up(arrived)

    scale_two = rms_scale(middle)
    normed_two = (middle * scale_two * gain_two).astype(jnp.bfloat16)
    normed_two, own_share = barrier((normed_two, mlp_own[0]))
    tokens_two = spread(normed_two)
    weights = (own_share, cross(own_share))
    tokens_two, weights, out_own = barrier((tokens_two, weights, out_t[0]))
    tokens_other = other_half(tokens_two)
    *acts, dn_part, y_part = mlp(tokens_two, cot_blocks, *weights, ())
    out_blocks = spread(out_own)
    acts, tokens_other = barrier((acts, tokens_other))
    acts_other = [cross(act) for act in acts]
    grads_one = mlp_grads(
        chips, tokens_two, cot_blocks, tokens_other, cot_other, acts, acts_other
    )
    grads_one, own_share, out_blocks = barrier((grads_one, mlp_own[1], out_blocks))
    sums_one = scatter(grads_one)
    weights = (own_share, cross(own_share))
    *acts, dn_part, y_part = mlp(tokens_two, cot_blocks, *weights, (dn_part, y_part))
    out_other = [out_t[1]] + [cross(block) for block in out_blocks[1:]]
    acts, dn_part, out_other = barrier((acts, dn_part, out_other))
    arrived = send_rows(dn_part)
    acts_other = [cross(act) for act in acts]
    grads_two = mlp_grads(
        chips, tokens_two, cot_blocks, tokens_other, cot_other, acts, acts_other
    )
    grads_two, arrived = barrier((grads_two, arrived))
    sums_two = scatter(grads_two)
    middle_grad, branch, gain_two_part, do_blocks = middle_back(
        arrived, middle, cotangent, gain_two[None, :], out_blocks, out_other
    )
    do_blocks = send_blocks(do_blocks)
    gain_two_other = cross(gain_two_part[half:])
    do_blocks, branch, gain_two_other, y_part = barrier(
        (do_blocks, branch, gain_two_other, y_part)
    )
    branch_blocks = spread(branch)
    qkv_grad = attend_back(
        me_array, query, log_total, key_pad, value_pad, cosine, sine, do_blocks, group
    )
    qkv_grad, sums_one = barrier((qkv_grad, sums_one))
    qkv_other = cross(qkv_grad)
    normed_part = jnp.concatenate([mm_nt(qkv_grad, w) for w in qkv], axis=1).astype(jnp.bfloat16)
    branch_blocks, normed_part, y_part = barrier((branch_blocks, normed_part, y_part))
    arrived = send_rows(normed_part)
    branch_other = other_half(branch_blocks)
    tokens_other, attended_other = early
    grads = attn_grads(
        chips,
        tokens_one,
        branch_blocks,
        (qkv_grad, attended),
        (tokens_other, branch_other, qkv_other, attended_other),
        qkv[0],
        gain_one[:half, None],
        (gain_two_part[:half] + gain_two_other)[:, None],
    )
    attn_sums = scatter(grads[0])
    gain_parts = grads[1][:, :, :2]
    arrived, gain_parts, y_part, sums_two = barrier((arrived, gain_parts, y_part, sums_two))
    down_arrived = send_rows(y_part)
    gain_sums = small_sums(gain_parts)
    normed_one_grad = add_up(arrived)
    input_norm_grad, _ = norm_back(normed_one_grad, residual, scale_one, gain_one)
    grad_in = by_device(middle_grad + input_norm_grad, core)
    shares = [share.astype(jnp.float32) for share in (sums_one, sums_two)]
    grad_gate = jnp.concatenate([h[:, :units] for h in shares], axis=1)
    grad_up = jnp.concatenate([h[:, units : 2 * units] for h in shares], axis=1)
    grad_down = jnp.concatenate([h[:, 2 * units :].T for h in shares], axis=0)
    down_arrived, grad_in, gain_sums, attn_sums, grad_gate, grad_up, grad_down = barrier(
        (down_arrived, grad_in, gain_sums, attn_sums, grad_gate, grad_up, grad_down)
    )
    out = by_device((middle + add_up(down_arrived)).astype(jnp.bfloat16), core)
    attn_sums = attn_sums.astype(jnp.float32)
    return (
        out,
        grad_in,
        gain_sums[:, 0],
        attn_sums[:, :q_width],
        attn_sums[:, q_width : q_width + kv_width],
        attn_sums[:, q_width + kv_width : qkv_width],
        attn_sums[:, qkv_width : qkv_width + q_width].T,
        gain_sums[:, 1],
        grad_gate,
        grad_up,
        grad_down,
    )


def solution(mesh):
    return jax.shard_map(
        per_device,
        mesh=mesh,
        in_specs=(
            P(("dp", "tensor"), None),
            P("dp"),
            P("dp", "tensor"),
            P("dp", "tensor"),
            P("dp", "tensor"),
            P("tensor", "dp"),
            P("dp"),
            P("dp", "tensor"),
            P("dp", "tensor"),
            P("tensor", "dp"),
            P("dp"),
            P(("dp", "tensor"), None),
        ),
        out_specs=(
            P(("dp", "tensor"), None),
            P(("dp", "tensor"), None),
            P(("dp", "tensor")),
            P("dp", "tensor"),
            P("dp", "tensor"),
            P("dp", "tensor"),
            P("tensor", "dp"),
            P(("dp", "tensor")),
            P("dp", "tensor"),
            P("dp", "tensor"),
            P("tensor", "dp"),
        ),
        check_vma=False,
    )
```

```python
import functools
import math

import jax
import jax.numpy as jnp
from jax import lax
from jax.experimental import pallas as pl
from jax.experimental.pallas import tpu as pltpu
from jax.sharding import PartitionSpec as P

HEAD_DIM = 64
PAIR = 2 * HEAD_DIM
SEQ_LEN = 1024


EPS = 1e-05
ROPE_BASE = 500000.0
SCALE = 1.0 / math.sqrt(HEAD_DIM)
PARAMS = pltpu.CompilerParams(vmem_limit_bytes=58 * 2**20)
ONCE = pl.Buffered(1)

barrier = lax.optimization_barrier


def hint(flops):
    return pl.CostEstimate(flops=flops, bytes_accessed=0, transcendentals=0)


def rms_scale(values):
    return lax.rsqrt(jnp.mean(values * values, axis=-1, keepdims=True) + EPS)


def norm_back(grad, values, scale, gain):
    inner = grad * gain
    cubed = scale * scale * scale
    result = scale * inner - values * cubed * jnp.mean(inner * values, axis=-1, keepdims=True)
    return (result, jnp.sum(grad * values * scale, axis=0))


def mm(left, right):
    return jnp.dot(left, right, preferred_element_type=jnp.float32)


def mm_nt(left, right):
    return lax.dot_general(left, right, (((1,), (1,)), ((), ())), preferred_element_type=jnp.float32)


def mm_tn(left, right):
    return lax.dot_general(left, right, (((0,), (0,)), ((), ())), preferred_element_type=jnp.float32)


def lane_index(rows):
    return lax.broadcasted_iota(jnp.int32, (rows, PAIR), 1)


def turn(pair, cosine, sine):
    lower = lane_index(pair.shape[0]) % HEAD_DIM < HEAD_DIM // 2
    other = jnp.where(
        lower, pltpu.roll(pair, PAIR - HEAD_DIM // 2, 1), pltpu.roll(pair, HEAD_DIM // 2, 1)
    )
    return pair * cosine + other * sine


def project_kernel(place_ref, *refs, size, q_width, kv_width):
    x_refs = refs[:size]
    gain_ref, wo_ref, wx_ref, cos_ref, sin_ref, n_ref, q_ref, k_ref, v_ref = refs[size:]
    rows = q_ref.shape[0]
    half = wo_ref.shape[0]

    def one(x_ref):
        x = x_ref[...].astype(jnp.float32)
        normed = (x * rms_scale(x) * gain_ref[...]).astype(jnp.bfloat16)
        n_ref[...] = normed
        cosine, sine = cos_ref[...], sin_ref[...]
        lin = mm(normed[:, :half], wo_ref[...]) + mm(normed[:, half:], wx_ref[...])
        for low in range(0, q_width, PAIR):
            query = turn(lin[:, low : low + PAIR], cosine, sine).astype(jnp.bfloat16)
            q_ref[:, low : low + PAIR] = query * jnp.bfloat16(SCALE)
        first = lane_index(rows) < HEAD_DIM
        for ref, start, rotate in ((k_ref, q_width, True), (v_ref, q_width + kv_width, False)):
            for head in range(kv_width // HEAD_DIM):
                low = start + head * HEAD_DIM
                block = lin[:, low // PAIR * PAIR : low // PAIR * PAIR + PAIR]
                if rotate:
                    block = turn(block, cosine, sine)
                moved = pltpu.roll(block, HEAD_DIM, 1)
                if low % PAIR:
                    block, moved = moved, block
                ref[head, 0] = jnp.where(first, block, 0.0).astype(jnp.bfloat16)
                ref[head, 1] = jnp.where(first, 0.0, moved).astype(jnp.bfloat16)

    for step in range(size):
        pl.when(pl.program_id(0) == step)(functools.partial(one, x_refs[step]))


def project(me, blocks, gain, own, other, cosine, sine, q_width, kv_width):
    size = len(blocks)
    rows, features = blocks[0].shape
    total = rows * size
    key_heads = kv_width // HEAD_DIM
    width = q_width + 2 * kv_width
    fixed = lambda p, m: (0, 0)
    placed = lambda p, m: (jnp.bitwise_xor(p, m[0]), 0)
    padded = pl.BlockSpec(
        (key_heads, 2, rows, PAIR), lambda p, m: (0, 0, jnp.bitwise_xor(p, m[0]), 0)
    )
    spec = pltpu.PrefetchScalarGridSpec(
        num_scalar_prefetch=1,
        grid=(size,),
        in_specs=[pl.BlockSpec((rows, features), fixed, pipeline_mode=ONCE)] * size
        + [
            pl.BlockSpec((1, features), fixed),
            pl.BlockSpec((features // 2, width), fixed, pipeline_mode=ONCE),
            pl.BlockSpec((features // 2, width), fixed, pipeline_mode=ONCE),
            pl.BlockSpec((rows, PAIR), placed),
            pl.BlockSpec((rows, PAIR), placed),
        ],
        out_specs=[
            pl.BlockSpec((rows, features), lambda p, m: (p, 0)),
            pl.BlockSpec((rows, q_width), lambda p, m: (p, 0)),
            padded,
            padded,
        ],
    )
    padded_shape = jax.ShapeDtypeStruct((key_heads, 2, total, PAIR), jnp.bfloat16)
    return pl.pallas_call(
        functools.partial(project_kernel, size=size, q_width=q_width, kv_width=kv_width),
        grid_spec=spec,
        out_shape=[
            jax.ShapeDtypeStruct((total, features), jnp.bfloat16),
            jax.ShapeDtypeStruct((total, q_width), jnp.bfloat16),
            padded_shape,
            padded_shape,
        ],
        compiler_params=PARAMS,
        cost_estimate=hint(2 * total * features * width // 16),
    )(me, *blocks, gain, own, other, cosine, sine)


def attend_kernel(
    me_ref, q_ref, k_ref, v_ref, wo_ref, wx_ref, o_ref, l_ref, *refs, size, heads, group
):
    part_refs, vt_ref = refs[:size], refs[size]
    rows = q_ref.shape[0]
    half = wo_ref.shape[0]
    mine = jnp.bitwise_xor(me_ref[0], pl.program_id(0))
    key_place = lax.broadcasted_iota(jnp.int32, (rows, rows), 0)
    query_place = lax.broadcasted_iota(jnp.int32, (rows, rows), 1)

    @pl.when(pl.program_id(0) == 0)
    def _():
        for head in range(heads // group):
            for side in range(2):
                vt_ref[head, side] = v_ref[head, side].T

    def one(span):
        keys = span * rows
        for pair in range(heads // 2):
            head = 2 * pair // group
            lanes = slice(pair * PAIR, (pair + 1) * PAIR)
            query = q_ref[:, lanes]
            acc = None
            inverse = []
            for side in range(2):
                diag = mm_nt(k_ref[head, side, keys : keys + rows, :], query)
                diag = jnp.where(key_place <= query_place, diag, -1e9)
                top = jnp.max(diag, axis=0, keepdims=True)
                if span:
                    body = mm_nt(k_ref[head, side, :keys, :], query)
                    top = jnp.maximum(top, jnp.max(body, axis=0, keepdims=True))
                diag = jnp.exp(diag - top)
                total = jnp.sum(diag, axis=0, keepdims=True)
                part = mm(vt_ref[head, side, :, keys : keys + rows], diag.astype(jnp.bfloat16))
                if span:
                    body = jnp.exp(body - top)
                    total = total + jnp.sum(body, axis=0, keepdims=True)
                    part = part + mm(vt_ref[head, side, :, :keys], body.astype(jnp.bfloat16))
                acc = part if acc is None else acc + part
                inverse.append(jnp.broadcast_to(1.0 / total, (HEAD_DIM, rows)))
                l_ref[2 * pair + side : 2 * pair + side + 1, :] = top + jnp.log(total)
            acc = acc * jnp.concatenate(inverse, axis=0)
            o_ref[:, lanes] = acc.T.astype(jnp.bfloat16)

    for span in range(size):
        pl.when(mine == span)(functools.partial(one, span))

    def project_out(ref):
        ref[:, :half] = mm_nt(o_ref[...], wo_ref[...]).astype(jnp.bfloat16)
        ref[:, half:] = mm_nt(o_ref[...], wx_ref[...]).astype(jnp.bfloat16)

    for step in range(size):
        pl.when(pl.program_id(0) == step)(functools.partial(project_out, part_refs[step]))


def attend(me, query, key_pad, value_pad, own, other, size, group):
    total, width = query.shape
    features = 2 * own.shape[0]
    rows, heads = total // size, width // HEAD_DIM
    whole = pl.BlockSpec(key_pad.shape, lambda p, m: (0, 0, 0, 0), pipeline_mode=ONCE)
    spec = pltpu.PrefetchScalarGridSpec(
        num_scalar_prefetch=1,
        grid=(size,),
        in_specs=[pl.BlockSpec((rows, width), lambda p, m: (p, 0)), whole, whole]
        + [pl.BlockSpec(own.shape, lambda p, m: (0, 0), pipeline_mode=ONCE)] * 2,
        out_specs=[
            pl.BlockSpec((rows, width), lambda p, m: (p, 0)),
            pl.BlockSpec((heads, rows), lambda p, m: (0, p)),
        ]
        + [pl.BlockSpec((rows, features), lambda p, m: (0, 0))] * size,
        scratch_shapes=[pltpu.VMEM((heads // group, 2, PAIR, total), jnp.bfloat16)],
    )
    return pl.pallas_call(
        functools.partial(attend_kernel, size=size, heads=heads, group=group),
        grid_spec=spec,
        out_shape=[
            jax.ShapeDtypeStruct((total, width), jnp.bfloat16),
            jax.ShapeDtypeStruct((heads, total), jnp.float32),
        ]
        + [jax.ShapeDtypeStruct((rows, features), jnp.bfloat16)] * size,
        compiler_params=PARAMS,
        cost_estimate=hint(8 * heads * total * total * HEAD_DIM // 16),
    )(me, query, key_pad, value_pad, own, other)


def attend_back_kernel(
    me_ref, q_ref, l_ref, k_ref, v_ref, cos_ref, sin_ref, *refs, size, heads, group
):
    do_refs = refs[:size]
    out_ref, dk_ref, dv_ref, kt_ref, do_ref = refs[size:]
    rows = q_ref.shape[0]
    key_heads = heads // group
    step = pl.program_id(0)
    me = me_ref[0]
    mine = jnp.bitwise_xor(me, step)
    key_place = lax.broadcasted_iota(jnp.int32, (rows, rows), 0)
    query_place = lax.broadcasted_iota(jnp.int32, (rows, rows), 1)

    def rows_of(block):
        return pl.ds(pl.multiple_of(block * rows, rows), rows)

    @pl.when(step == 0)
    def _():
        dk_ref[...] = jnp.zeros_like(dk_ref)
        dv_ref[...] = jnp.zeros_like(dv_ref)
        for head in range(key_heads):
            for side in range(2):
                kt_ref[head, side] = k_ref[head, side].T

    def fetch(ref):
        do_ref[...] = ref[...]

    for block in range(size):
        pl.when(step == block)(functools.partial(fetch, do_refs[block]))

    def one(span):
        keys = span * rows
        parts = [(keys, keys + rows, True)] + ([(0, keys, False)] if span else [])
        cosine, sine = cos_ref[keys : keys + rows, :], sin_ref[keys : keys + rows, :]
        for pair in range(heads // 2):
            head = 2 * pair // group
            lanes = slice(pair * PAIR, (pair + 1) * PAIR)
            query, grad = q_ref[:, lanes], do_ref[:, lanes]
            acc = None
            for side in range(2):
                log_total = l_ref[2 * pair + side : 2 * pair + side + 1, :]
                inner = None
                kept = []
                for low, high, diagonal in parts:
                    probs = mm_nt(k_ref[head, side, low:high, :], query)
                    probs = jnp.exp(probs - log_total)
                    if diagonal:
                        probs = jnp.where(key_place <= query_place, probs, 0.0)
                    prob_grad = mm_nt(v_ref[head, side, low:high, :], grad)
                    dv_ref[head, side, low:high, :] += mm(probs.astype(jnp.bfloat16), grad)
                    term = jnp.sum(probs * prob_grad, axis=0, keepdims=True)
                    inner = term if inner is None else inner + term
                    kept.append((low, high, probs, prob_grad))
                for low, high, probs, prob_grad in kept:
                    score_grad = (probs * (prob_grad - inner)).astype(jnp.bfloat16)
                    dk_ref[head, side, low:high, :] += mm(score_grad, query)
                    part = mm(kt_ref[head, side, :, low:high], score_grad)
                    acc = part if acc is None else acc + part
            turned = turn(acc.T * SCALE, cosine, -sine)
            out_ref[rows_of(step), lanes] = turned.astype(jnp.bfloat16)

    for span in range(size):
        pl.when(mine == span)(functools.partial(one, span))

    @pl.when(step == size - 1)
    def _():
        first = lane_index(rows) < HEAD_DIM
        wanted = [(dk_ref, head, True) for head in range(key_heads)]
        wanted += [(dv_ref, head, False) for head in range(key_heads)]
        for span in range(size):
            place = slice(span * rows, (span + 1) * rows)
            cosine, sine = cos_ref[place, :], sin_ref[place, :]
            for block in range(len(wanted) // 2):
                halves, rotate = [], []
                for half in range(2):
                    ref, head, is_key = wanted[2 * block + half]
                    low, high = ref[head, 0, place, :], ref[head, 1, place, :]
                    if half:
                        halves.append(pltpu.roll(low, HEAD_DIM, 1) + high)
                    else:
                        halves.append(low + pltpu.roll(high, HEAD_DIM, 1))
                    rotate.append(is_key)
                value = jnp.where(first, halves[0], halves[1])
                if rotate[0] and rotate[1]:
                    value = turn(value, cosine, -sine)
                elif rotate[0]:
                    value = jnp.where(first, turn(value, cosine, -sine), value)
                start = heads * HEAD_DIM + block * PAIR
                target = rows_of(jnp.bitwise_xor(me, span))
                out_ref[target, start : start + PAIR] = value.astype(jnp.bfloat16)


def attend_back(
    me, query, log_total, key_pad, value_pad, cosine, sine, attended_grad, group
):
    total, width = query.shape
    size = len(attended_grad)
    rows, heads = total // size, width // HEAD_DIM
    key_heads = heads // group
    out_width = width + 2 * key_heads * HEAD_DIM
    whole = pl.BlockSpec(key_pad.shape, lambda p, m: (0, 0, 0, 0), pipeline_mode=ONCE)
    table = pl.BlockSpec((total, PAIR), lambda p, m: (0, 0), pipeline_mode=ONCE)
    spec = pltpu.PrefetchScalarGridSpec(
        num_scalar_prefetch=1,
        grid=(size,),
        in_specs=[
            pl.BlockSpec((rows, width), lambda p, m: (p, 0)),
            pl.BlockSpec((heads, rows), lambda p, m: (0, p)),
            whole,
            whole,
            table,
            table,
        ]
        + [pl.BlockSpec((rows, width), lambda p, m: (0, 0), pipeline_mode=ONCE)] * size,
        out_specs=pl.BlockSpec((total, out_width), lambda p, m: (0, 0)),
        scratch_shapes=[
            pltpu.VMEM(key_pad.shape, jnp.float32),
            pltpu.VMEM(key_pad.shape, jnp.float32),
            pltpu.VMEM((key_heads, 2, PAIR, total), jnp.bfloat16),
            pltpu.VMEM((rows, width), jnp.bfloat16),
        ],
    )
    return pl.pallas_call(
        functools.partial(attend_back_kernel, size=size, heads=heads, group=group),
        grid_spec=spec,
        out_shape=jax.ShapeDtypeStruct((total, out_width), jnp.bfloat16),
        compiler_params=PARAMS,
        cost_estimate=hint(20 * heads * total * total * HEAD_DIM),
    )(me, query, log_total, key_pad, value_pad, cosine, sine, *attended_grad)


def mlp_kernel(*refs, size, adds):
    n_refs, e_refs = refs[:size], refs[size : 2 * size]
    gate_o, up_o, down_o, gate_x, up_x, down_x = refs[2 * size : 2 * size + 6]
    dg_ref, du_ref, h_ref, dn_ref, y_ref, n_ref, e_ref = refs[-7:]
    half = gate_o.shape[0]

    def fetch(step):
        n_ref[...] = n_refs[step][...]
        e_ref[...] = e_refs[step][...]

    for step in range(size):
        pl.when(pl.program_id(0) == step)(functools.partial(fetch, step))
    gate = mm(n_ref[:, :half], gate_o[...]) + mm(n_ref[:, half:], gate_x[...])
    up = mm(n_ref[:, :half], up_o[...]) + mm(n_ref[:, half:], up_x[...])
    grad = mm(e_ref[:, :half], down_o[...]) + mm(e_ref[:, half:], down_x[...])
    sigma = jax.nn.sigmoid(gate)
    silu = gate * sigma
    hidden = (silu * up).astype(jnp.bfloat16)
    gate_grad = (grad * up * sigma * (1.0 + gate * (1.0 - sigma))).astype(jnp.bfloat16)
    up_grad = (grad * silu).astype(jnp.bfloat16)
    dg_ref[...] = gate_grad
    du_ref[...] = up_grad
    h_ref[...] = hidden
    for part, gate_w, up_w, down_w in ((0, gate_o, up_o, down_o), (1, gate_x, up_x, down_x)):
        lanes = slice(part * half, (part + 1) * half)
        dn = mm_nt(gate_grad, gate_w[...]) + mm_nt(up_grad, up_w[...])
        y = mm_nt(hidden, down_w[...])
        if adds:
            dn = dn + refs[2 * size + 6][:, lanes].astype(jnp.float32)
            y = y + refs[2 * size + 7][:, lanes].astype(jnp.float32)
        dn_ref[:, lanes] = dn.astype(dn_ref.dtype)
        y_ref[:, lanes] = y.astype(y_ref.dtype)


def mlp(tokens, cot, own, other, earlier):
    size = len(tokens)
    rows, features = tokens[0].shape
    half, units = own.shape[0], own.shape[1] // 3
    total = rows * size
    fixed = lambda p: (0, 0)
    moving = lambda p: (p, 0)
    wide = pl.BlockSpec((rows, features), moving)
    sums = jax.ShapeDtypeStruct((total, features), jnp.bfloat16)
    block = pl.BlockSpec((rows, features), fixed, pipeline_mode=ONCE)
    thirds = [
        pl.BlockSpec((half, units), lambda p, t=t: (0, t), pipeline_mode=ONCE) for t in range(3)
    ]
    return pl.pallas_call(
        functools.partial(mlp_kernel, size=size, adds=bool(earlier)),
        grid=(size,),
        in_specs=[block] * (2 * size)
        + thirds * 2
        + [wide] * len(earlier),
        out_specs=[pl.BlockSpec((rows, units), moving)] * 3 + [wide, wide],
        out_shape=[jax.ShapeDtypeStruct((total, units), jnp.bfloat16)] * 3 + [sums, sums],
        scratch_shapes=[pltpu.VMEM((rows, features), jnp.bfloat16)] * 2,
        compiler_params=PARAMS,
        cost_estimate=hint(12 * total * features * units),
    )(*tokens, *cot, own, own, own, other, other, other, *earlier)


def middle_back_kernel(*refs, size):
    n_refs, refs = refs[:size], refs[size:]
    x_ref, e_ref, gain_ref, refs = refs[0], refs[1], refs[2], refs[3:]
    own_refs, other_refs, refs = refs[:size], refs[size : 2 * size], refs[2 * size :]
    grad_ref, branch_ref, part_ref, do_refs = refs[0], refs[1], refs[2], refs[3:]
    half = own_refs[0].shape[0]
    grad = n_refs[0][...].astype(jnp.float32)
    for ref in n_refs[1:]:
        grad = grad + ref[...].astype(jnp.float32)
    values = x_ref[...]
    scale = rms_scale(values)
    result, part = norm_back(grad, values, scale, gain_ref[...])

    @pl.when(pl.program_id(0) == 0)
    def _():
        part_ref[...] = jnp.zeros_like(part_ref)

    part_ref[...] += part[None, :]
    result = result + e_ref[...].astype(jnp.float32)
    grad_ref[...] = result
    branch = result.astype(jnp.bfloat16)
    branch_ref[...] = branch
    for own, other, do_ref in zip(own_refs, other_refs, do_refs):
        do = mm(branch[:, :half], own[...]) + mm(branch[:, half:], other[...])
        do_ref[...] = do.astype(jnp.bfloat16)


def middle_back(arrived, middle, cot, gain, own, other):
    size = len(arrived)
    rows, features = middle.shape
    width = own[0].shape[1]
    steps = 2
    wide = pl.BlockSpec((rows // steps, features), lambda i: (i, 0))
    narrow = pl.BlockSpec((rows // steps, width), lambda i: (i, 0))
    row = pl.BlockSpec((1, features), lambda i: (0, 0))
    weight = pl.BlockSpec((features // 2, width), lambda i: (0, 0), pipeline_mode=ONCE)
    grad, branch, part, *do = pl.pallas_call(
        functools.partial(middle_back_kernel, size=size),
        grid=(steps,),
        in_specs=[wide] * size + [wide, wide, row] + [weight] * (2 * size),
        out_specs=[wide, wide, row] + [narrow] * size,
        out_shape=[
            jax.ShapeDtypeStruct((rows, features), jnp.float32),
            jax.ShapeDtypeStruct((rows, features), jnp.bfloat16),
            jax.ShapeDtypeStruct((1, features), jnp.float32),
        ]
        + [jax.ShapeDtypeStruct((rows, width), jnp.bfloat16)] * size,
        compiler_params=PARAMS,
        cost_estimate=hint(2 * rows * features * width * size),
    )(*arrived, middle, cot, gain, *own, *other)
    return grad, branch, part[0], do


def column_grad(blocks, other, mine, theirs):
    rows = blocks[0].shape[0]
    total = mm_tn(other[...], theirs[...])
    for index, block in enumerate(blocks):
        total = total + mm_tn(block[...], mine[index * rows : (index + 1) * rows, :])
    return total


def grad_kernel(*refs, size):
    n_refs, e_refs = refs[:size], refs[size : 2 * size]
    n_other, e_other = refs[2 * size : 2 * size + 2]
    acts, out_ref = refs[2 * size + 2 : -1], refs[-1]
    units = acts[0].shape[1]
    for third in range(3):
        blocks, other = (e_refs, e_other) if third == 2 else (n_refs, n_other)
        grad = column_grad(blocks, other, acts[third], acts[third + 3])
        out_ref[0, :, third * units : (third + 1) * units] = grad.astype(jnp.bfloat16)


def mlp_grads(chips, tokens, cot, tokens_other, cot_other, mine, theirs):
    size = len(tokens)
    rows, features = tokens[0].shape
    total, units = mine[0].shape
    depth = features // (2 * chips)
    column = pl.BlockSpec((rows, depth), lambda b: (0, b))
    long = pl.BlockSpec((total, depth), lambda b: (0, b))
    fixed = pl.BlockSpec((total, units), lambda b: (0, 0), pipeline_mode=ONCE)
    return pl.pallas_call(
        functools.partial(grad_kernel, size=size),
        grid=(chips,),
        in_specs=[column] * (2 * size) + [long, long] + [fixed] * 6,
        out_specs=pl.BlockSpec((1, depth, 3 * units), lambda b: (b, 0, 0)),
        out_shape=jax.ShapeDtypeStruct((chips, depth, 3 * units), jnp.bfloat16),
        compiler_params=PARAMS,
        cost_estimate=hint(6 * total * features * units),
    )(*tokens, *cot, tokens_other, cot_other, *mine, *theirs)


def qkv_grad_kernel(n_ref, n_other, d_ref, d_other, w_ref, g1_ref, g2_ref, out_ref, gain_ref):
    grad = column_grad([n_ref], n_other, d_ref, d_other)
    out_ref[0] = grad.astype(jnp.bfloat16)
    first = jnp.sum(grad * w_ref[...].astype(jnp.float32), axis=1, keepdims=True) / g1_ref[...]
    gain_ref[0] = jnp.where(lane_index(grad.shape[0]) == 0, first, g2_ref[...])


def qkv_grads(chips, tokens, tokens_other, mine, theirs, weights, gain_one, gain_two_part):
    total, features = tokens.shape
    width = mine.shape[1]
    depth = features // (2 * chips)
    column = pl.BlockSpec((total, depth), lambda b: (0, b))
    fixed = pl.BlockSpec((total, width), lambda b: (0, 0), pipeline_mode=ONCE)
    row = lambda b: (b, 0)
    place = lambda b: (b, 0, 0)
    return pl.pallas_call(
        qkv_grad_kernel,
        grid=(chips,),
        in_specs=[
            column,
            column,
            fixed,
            fixed,
            pl.BlockSpec((depth, width), row),
            pl.BlockSpec((depth, 1), row),
            pl.BlockSpec((depth, 1), row),
        ],
        out_specs=[pl.BlockSpec((1, depth, width), place), pl.BlockSpec((1, depth, PAIR), place)],
        out_shape=[
            jax.ShapeDtypeStruct((chips, depth, width), jnp.bfloat16),
            jax.ShapeDtypeStruct((chips, depth, PAIR), jnp.float32),
        ],
        compiler_params=PARAMS,
        cost_estimate=hint(2 * total * features * width),
    )(tokens, tokens_other, mine, theirs, weights, gain_one, gain_two_part)


def out_grad_kernel(*refs, size):
    branch, (other, mine, theirs, gain_ref, out_ref) = refs[:size], refs[size:]
    width = mine.shape[1]
    out_ref[0, :, :width] = column_grad(branch, other, mine, theirs).astype(jnp.bfloat16)
    gains = gain_ref[0]
    coarse = gains.astype(jnp.bfloat16)
    rest = (gains - coarse.astype(jnp.float32)).astype(jnp.bfloat16)
    out_ref[0, :, width : width + PAIR] = coarse
    out_ref[0, :, width + PAIR :] = rest


def out_grads(chips, branch, branch_other, mine, theirs, gains):
    size = len(branch)
    rows, features = branch[0].shape
    total, width = mine.shape
    depth = features // (2 * chips)
    fixed = pl.BlockSpec((total, width), lambda b: (0, 0), pipeline_mode=ONCE)
    place = lambda b: (b, 0, 0)
    return pl.pallas_call(
        functools.partial(out_grad_kernel, size=size),
        grid=(chips,),
        in_specs=[pl.BlockSpec((rows, depth), lambda b: (0, b))] * size
        + [pl.BlockSpec((total, depth), lambda b: (0, b)), fixed, fixed]
        + [pl.BlockSpec((1, depth, PAIR), place)],
        out_specs=pl.BlockSpec((1, depth, width + 2 * PAIR), place),
        out_shape=jax.ShapeDtypeStruct((chips, depth, width + 2 * PAIR), jnp.bfloat16),
        compiler_params=PARAMS,
        cost_estimate=hint(2 * total * features * width),
    )(*branch, branch_other, mine, theirs, gains)


def swap(values, step):
    size = lax.axis_size("tensor")
    return lax.ppermute(values, "tensor", [(i, i ^ step) for i in range(size)])


def spread(values):
    return [values] + [swap(values, step) for step in range(1, lax.axis_size("tensor"))]


def send_blocks(blocks):
    return [blocks[0]] + [swap(block, step + 1) for step, block in enumerate(blocks[1:])]


def send_rows(partial):
    size = lax.axis_size("tensor")
    return send_blocks(list(partial.reshape((size, -1) + partial.shape[1:])))


def add_up(blocks):
    total = blocks[0].astype(jnp.float32)
    for block in blocks[1:]:
        total = total + block.astype(jnp.float32)
    return total


def cross(values):
    count = lax.axis_size("dp")
    return lax.ppermute(values, "dp", [(i, i ^ 1) for i in range(count)])


def tables(positions):
    freqs = ROPE_BASE ** (-jnp.arange(0, HEAD_DIM, 2).astype(jnp.float32) / HEAD_DIM)
    angles = positions.astype(jnp.float32)[:, None] * freqs[None, :]
    cosine, sine = jnp.cos(angles), jnp.sin(angles)
    return (
        jnp.concatenate([cosine] * 4, axis=1),
        jnp.concatenate([-sine, sine, -sine, sine], axis=1),
    )


def chip_lines():
    count = lax.axis_size("dp")
    return [list(range(core, count, 2)) for core in range(2)]


def gather(values):
    return lax.all_gather(values, "dp", axis=0, tiled=True, axis_index_groups=chip_lines())


def scatter(values):
    total = lax.psum_scatter(
        values, "dp", scatter_dimension=0, tiled=True, axis_index_groups=chip_lines()
    )
    return total[0]


def along(values, step):
    count = lax.axis_size("dp")
    return lax.ppermute(values, "dp", [(i, (i + 2 * step) % count) for i in range(count)])


def line_order(blocks):
    chips = len(blocks)
    chip = lax.axis_index("dp") // 2
    placed = jnp.zeros((chips,) + blocks[0].shape, blocks[0].dtype)
    for step, block in enumerate(blocks):
        placed = lax.dynamic_update_index_in_dim(placed, block, (chip - step) % chips, 0)
    return placed.reshape((-1,) + blocks[0].shape[1:])


def line_parts(parts):
    chips = lax.axis_size("dp") // 2
    chip = lax.axis_index("dp") // 2
    blocks = [lax.dynamic_index_in_dim(parts, chip, 0, keepdims=False)]
    for step in range(1, chips):
        sent = lax.dynamic_index_in_dim(parts, (chip + step) % chips, 0, keepdims=False)
        blocks.append(along(sent, step))
    return blocks


def own_part(values):
    size = lax.axis_size("tensor")
    me = lax.axis_index("tensor")
    blocks = values.reshape((size, -1) + values.shape[1:])
    own = lax.dynamic_index_in_dim(blocks, me, 0, keepdims=False)
    for step in range(1, size):
        sent = lax.dynamic_index_in_dim(blocks, me ^ step, 0, keepdims=False)
        own = own + swap(sent, step)
    return own


def other_half(blocks):
    half = blocks[0].shape[1] // 2
    return cross(jnp.concatenate([block[:, half:] for block in blocks], axis=0))


def feature_blocks(values):
    width = values.shape[-1] // lax.axis_size("dp")
    return [values[..., low : low + width] for low in range(0, values.shape[-1], width)]


def by_core(values, core):
    blocks = feature_blocks(values)
    pairs = list(zip(blocks[0::2], blocks[1::2]))
    own = [jnp.where(core == 0, even, odd) for even, odd in pairs]
    other = [jnp.where(core == 0, odd, even) for even, odd in pairs]
    return jnp.concatenate(own + other, axis=-1)


def by_device(values, core):
    blocks = feature_blocks(values)
    chips = len(blocks) // 2
    placed = []
    for own, other in zip(blocks[:chips], blocks[chips:]):
        placed += [jnp.where(core == 0, own, other), jnp.where(core == 0, other, own)]
    return jnp.concatenate(placed, axis=-1)


def per_device(
    hidden_in,
    gain_attn,
    w_query,
    w_key,
    w_value,
    w_out,
    gain_mlp,
    w_gate,
    w_up,
    w_down,
    positions,
    cotangent,
):
    size = lax.axis_size("tensor")
    chips = lax.axis_size("dp") // 2
    me = lax.axis_index("tensor")
    me_array = jnp.full((1,), me, jnp.int32)
    core = lax.axis_index("dp") % 2
    q_width, kv_width = w_query.shape[1], w_key.shape[1]
    group = q_width // kv_width
    units = w_down.shape[0] // 2
    half = hidden_in.shape[1] // 2

    qkv_shard = jnp.concatenate([w_query, w_key, w_value], axis=1)
    out_shard = w_out.T
    qkv_shard, out_shard, hidden_in, gain_attn = barrier(
        (qkv_shard, out_shard, hidden_in, gain_attn)
    )
    qkv_own = gather(qkv_shard)
    residual = by_core(hidden_in, core)
    early_in = [swap(residual, step) for step in range(1, 3)]
    early_out = [along(out_shard, step) for step in range(1, 3)]
    early_in, early_out, residual, out_shard = barrier(
        (early_in, early_out, residual, out_shard)
    )
    blocks_in = [residual] + early_in + [swap(residual, step) for step in range(3, size)]
    out_parts = [out_shard] + early_out + [along(out_shard, step) for step in range(3, chips)]
    residual = residual.astype(jnp.float32)
    gains = lax.all_gather(jnp.stack([gain_attn, gain_mlp]), "dp", axis=1, tiled=True)
    gains = by_core(gains, core).astype(jnp.float32)
    cosine, sine = tables(positions)
    cotangent = by_core(cotangent, core)
    down_t = w_down.T
    shares = []
    for part in range(2):
        cut = slice(part * units, (part + 1) * units)
        shares.append(jnp.concatenate([w_gate[:, cut], w_up[:, cut], down_t[:, cut]], axis=1))
    shares, qkv_own, cosine, sine, gains, early_in, early_out = barrier(
        (shares, qkv_own, cosine, sine, gains, blocks_in[1:3], out_parts[1:3])
    )
    blocks_in[1:3], out_parts[1:3] = early_in, early_out
    blocks_in, cotangent = barrier((blocks_in, cotangent))
    out_own = line_order(out_parts)
    mlp_own = [gather(share) for share in shares]
    cot_blocks = spread(cotangent)
    gain_one, gain_two = gains[0], gains[1]
    qkv = (qkv_own, cross(qkv_own))
    out_t = (out_own, cross(out_own))

    scale_one = rms_scale(residual)
    tokens_one, query, key_pad, value_pad = project(
        me_array, blocks_in, gain_one[None, :], *qkv, cosine, sine, q_width, kv_width
    )
    attended, log_total, *parts = attend(
        me_array, query, key_pad, value_pad, *out_t, size, group
    )
    parts, cot_blocks, tokens_one, attended = barrier((parts, cot_blocks, tokens_one, attended))
    arrived = send_blocks(parts)
    cot_other = other_half(cot_blocks)
    early = (cross(tokens_one[:, half:]), cross(attended))
    arrived, cot_other, early = barrier((arrived, cot_other, early))
    middle = residual + add_up(arrived)

    scale_two = rms_scale(middle)
    normed_two = (middle * scale_two * gain_two).astype(jnp.bfloat16)
    normed_two, own_share = barrier((normed_two, mlp_own[0]))
    tokens_two = spread(normed_two)
    weights = (own_share, cross(own_share))
    tokens_two, weights, out_own = barrier((tokens_two, weights, out_t[0]))
    tokens_other = other_half(tokens_two)
    *acts, dn_part, y_part = mlp(tokens_two, cot_blocks, *weights, ())
    out_blocks = spread(out_own)
    acts, tokens_other = barrier((acts, tokens_other))
    acts_other = [cross(act) for act in acts]
    grads_one = mlp_grads(
        chips, tokens_two, cot_blocks, tokens_other, cot_other, acts, acts_other
    )
    grads_one, own_share = barrier((grads_one, mlp_own[1]))
    sums_one = scatter(grads_one)
    weights = (own_share, cross(own_share))
    *acts, dn_part, y_part = mlp(tokens_two, cot_blocks, *weights, (dn_part, y_part))
    acts, dn_part, out_blocks = barrier((acts, dn_part, out_blocks))
    arrived = send_rows(dn_part)
    out_other = [out_t[1]] + [cross(block) for block in out_blocks[1:]]
    acts_other = [cross(act) for act in acts]
    grads_two = mlp_grads(
        chips, tokens_two, cot_blocks, tokens_other, cot_other, acts, acts_other
    )
    grads_two, arrived, out_other, y_part = barrier((grads_two, arrived, out_other, y_part))
    y_blocks = list(y_part.reshape((size, -1) + y_part.shape[1:]))
    y_early = [swap(y_blocks[step], step) for step in range(1, 3)]
    sums_two = scatter(grads_two)
    middle_grad, branch, gain_two_part, do_blocks = middle_back(
        arrived, middle, cotangent, gain_two[None, :], out_blocks, out_other
    )
    do_blocks = send_blocks(do_blocks)
    gain_two_other = cross(gain_two_part[half:])
    do_blocks, branch, gain_two_other, y_blocks, y_early = barrier(
        (do_blocks, branch, gain_two_other, y_blocks, y_early)
    )
    branch_blocks = spread(branch)
    qkv_grad = attend_back(
        me_array, query, log_total, key_pad, value_pad, cosine, sine, do_blocks, group
    )
    qkv_grad, sums_one = barrier((qkv_grad, sums_one))
    qkv_other = cross(qkv_grad)
    normed_part = jnp.concatenate([mm_nt(qkv_grad, w) for w in qkv], axis=1).astype(jnp.bfloat16)
    branch_blocks, normed_part = barrier((branch_blocks, normed_part))
    arrived = send_rows(normed_part)
    branch_other = other_half(branch_blocks)
    tokens_other, attended_other = early
    grads, gain_parts = qkv_grads(
        chips,
        tokens_one,
        tokens_other,
        qkv_grad,
        qkv_other,
        qkv[0],
        gain_one[:half, None],
        (gain_two_part[:half] + gain_two_other)[:, None],
    )
    attn_sums = scatter(grads)
    out_parts = line_parts(
        out_grads(chips, branch_blocks, branch_other, attended, attended_other, gain_parts)
    )
    arrived, out_parts, y_blocks, sums_two = barrier((arrived, out_parts, y_blocks, sums_two))
    y_late = [swap(y_blocks[step], step) for step in range(3, size)]
    out_sum = add_up(out_parts)
    gain_sums = own_part(
        out_sum[:, q_width : q_width + 2] + out_sum[:, q_width + PAIR : q_width + PAIR + 2]
    )
    grad_out = out_sum[:, :q_width].T
    normed_one_grad = add_up(arrived)
    input_norm_grad, _ = norm_back(normed_one_grad, residual, scale_one, gain_one)
    grad_in = by_device(middle_grad + input_norm_grad, core)
    shares = [share.astype(jnp.float32) for share in (sums_one, sums_two)]
    grad_gate = jnp.concatenate([h[:, :units] for h in shares], axis=1)
    grad_up = jnp.concatenate([h[:, units : 2 * units] for h in shares], axis=1)
    grad_down = jnp.concatenate([h[:, 2 * units :].T for h in shares], axis=0)
    y_late, grad_in, grad_out, gain_sums, attn_sums, grad_gate, grad_up, grad_down = barrier(
        (y_late, grad_in, grad_out, gain_sums, attn_sums, grad_gate, grad_up, grad_down)
    )
    out = middle + add_up([y_blocks[0]] + y_early + y_late)
    out = by_device(out.astype(jnp.bfloat16), core)
    attn_sums = attn_sums.astype(jnp.float32)
    return (
        out,
        grad_in,
        gain_sums[:, 0],
        attn_sums[:, :q_width],
        attn_sums[:, q_width : q_width + kv_width],
        attn_sums[:, q_width + kv_width :],
        grad_out,
        gain_sums[:, 1],
        grad_gate,
        grad_up,
        grad_down,
    )


def solution(mesh):
    return jax.shard_map(
        per_device,
        mesh=mesh,
        in_specs=(
            P(("dp", "tensor"), None),
            P("dp"),
            P("dp", "tensor"),
            P("dp", "tensor"),
            P("dp", "tensor"),
            P("tensor", "dp"),
            P("dp"),
            P("dp", "tensor"),
            P("dp", "tensor"),
            P("tensor", "dp"),
            P("dp"),
            P(("dp", "tensor"), None),
        ),
        out_specs=(
            P(("dp", "tensor"), None),
            P(("dp", "tensor"), None),
            P(("dp", "tensor")),
            P("dp", "tensor"),
            P("dp", "tensor"),
            P("dp", "tensor"),
            P("tensor", "dp"),
            P(("dp", "tensor")),
            P("dp", "tensor"),
            P("dp", "tensor"),
            P("tensor", "dp"),
        ),
        check_vma=False,
    )
```

```python
import functools
import math

import jax
import jax.numpy as jnp
from jax import lax
from jax.experimental import pallas as pl
from jax.experimental.pallas import tpu as pltpu
from jax.sharding import PartitionSpec as P

HEAD_DIM = 64
PAIR = 2 * HEAD_DIM
SEQ_LEN = 1024


EPS = 1e-05
ROPE_BASE = 500000.0
SCALE = 1.0 / math.sqrt(HEAD_DIM)
PARAMS = pltpu.CompilerParams(vmem_limit_bytes=58 * 2**20)
ONCE = pl.Buffered(1)

barrier = lax.optimization_barrier


def hint(flops):
    return pl.CostEstimate(flops=flops, bytes_accessed=0, transcendentals=0)


def rms_scale(values):
    return lax.rsqrt(jnp.mean(values * values, axis=-1, keepdims=True) + EPS)


def norm_back(grad, values, scale, gain):
    inner = grad * gain
    cubed = scale * scale * scale
    result = scale * inner - values * cubed * jnp.mean(inner * values, axis=-1, keepdims=True)
    return (result, jnp.sum(grad * values * scale, axis=0))


def mm(left, right):
    return jnp.dot(left, right, preferred_element_type=jnp.float32)


def mm_nt(left, right):
    return lax.dot_general(left, right, (((1,), (1,)), ((), ())), preferred_element_type=jnp.float32)


def mm_tn(left, right):
    return lax.dot_general(left, right, (((0,), (0,)), ((), ())), preferred_element_type=jnp.float32)


def lane_index(rows):
    return lax.broadcasted_iota(jnp.int32, (rows, PAIR), 1)


def turn(pair, cosine, sine):
    lower = lane_index(pair.shape[0]) % HEAD_DIM < HEAD_DIM // 2
    other = jnp.where(
        lower, pltpu.roll(pair, PAIR - HEAD_DIM // 2, 1), pltpu.roll(pair, HEAD_DIM // 2, 1)
    )
    return pair * cosine + other * sine


def project_kernel(place_ref, *refs, size, q_width, kv_width):
    x_refs = refs[:size]
    gain_ref, wo_ref, wx_ref, cos_ref, sin_ref, n_ref, q_ref, k_ref, v_ref = refs[size:]
    rows = q_ref.shape[0]
    half = wo_ref.shape[0]

    def one(x_ref):
        x = x_ref[...].astype(jnp.float32)
        normed = (x * rms_scale(x) * gain_ref[...]).astype(jnp.bfloat16)
        n_ref[...] = normed
        cosine, sine = cos_ref[...], sin_ref[...]
        lin = mm(normed[:, :half], wo_ref[...]) + mm(normed[:, half:], wx_ref[...])
        for low in range(0, q_width, PAIR):
            query = turn(lin[:, low : low + PAIR], cosine, sine).astype(jnp.bfloat16)
            q_ref[:, low : low + PAIR] = query * jnp.bfloat16(SCALE)
        first = lane_index(rows) < HEAD_DIM
        for ref, start, rotate in ((k_ref, q_width, True), (v_ref, q_width + kv_width, False)):
            for head in range(kv_width // HEAD_DIM):
                low = start + head * HEAD_DIM
                block = lin[:, low // PAIR * PAIR : low // PAIR * PAIR + PAIR]
                if rotate:
                    block = turn(block, cosine, sine)
                moved = pltpu.roll(block, HEAD_DIM, 1)
                if low % PAIR:
                    block, moved = moved, block
                ref[head, 0] = jnp.where(first, block, 0.0).astype(jnp.bfloat16)
                ref[head, 1] = jnp.where(first, 0.0, moved).astype(jnp.bfloat16)

    for step in range(size):
        pl.when(pl.program_id(0) == step)(functools.partial(one, x_refs[step]))


def project(me, blocks, gain, own, other, cosine, sine, q_width, kv_width):
    size = len(blocks)
    rows, features = blocks[0].shape
    total = rows * size
    key_heads = kv_width // HEAD_DIM
    width = q_width + 2 * kv_width
    fixed = lambda p, m: (0, 0)
    placed = lambda p, m: (jnp.bitwise_xor(p, m[0]), 0)
    padded = pl.BlockSpec(
        (key_heads, 2, rows, PAIR), lambda p, m: (0, 0, jnp.bitwise_xor(p, m[0]), 0)
    )
    spec = pltpu.PrefetchScalarGridSpec(
        num_scalar_prefetch=1,
        grid=(size,),
        in_specs=[pl.BlockSpec((rows, features), fixed, pipeline_mode=ONCE)] * size
        + [
            pl.BlockSpec((1, features), fixed),
            pl.BlockSpec((features // 2, width), fixed, pipeline_mode=ONCE),
            pl.BlockSpec((features // 2, width), fixed, pipeline_mode=ONCE),
            pl.BlockSpec((rows, PAIR), placed),
            pl.BlockSpec((rows, PAIR), placed),
        ],
        out_specs=[
            pl.BlockSpec((rows, features), lambda p, m: (p, 0)),
            pl.BlockSpec((rows, q_width), lambda p, m: (p, 0)),
            padded,
            padded,
        ],
    )
    padded_shape = jax.ShapeDtypeStruct((key_heads, 2, total, PAIR), jnp.bfloat16)
    return pl.pallas_call(
        functools.partial(project_kernel, size=size, q_width=q_width, kv_width=kv_width),
        grid_spec=spec,
        out_shape=[
            jax.ShapeDtypeStruct((total, features), jnp.bfloat16),
            jax.ShapeDtypeStruct((total, q_width), jnp.bfloat16),
            padded_shape,
            padded_shape,
        ],
        compiler_params=PARAMS,
        cost_estimate=hint(2 * total * features * width // 16),
    )(me, *blocks, gain, own, other, cosine, sine)


def attend_kernel(
    me_ref, q_ref, k_ref, v_ref, wo_ref, wx_ref, o_ref, l_ref, *refs, size, heads, group
):
    part_refs, vt_ref = refs[:size], refs[size]
    rows = q_ref.shape[0]
    half = wo_ref.shape[0]
    mine = jnp.bitwise_xor(me_ref[0], pl.program_id(0))
    key_place = lax.broadcasted_iota(jnp.int32, (rows, rows), 0)
    query_place = lax.broadcasted_iota(jnp.int32, (rows, rows), 1)

    @pl.when(pl.program_id(0) == 0)
    def _():
        for head in range(heads // group):
            for side in range(2):
                vt_ref[head, side] = v_ref[head, side].T

    def one(span):
        keys = span * rows
        for pair in range(heads // 2):
            head = 2 * pair // group
            lanes = slice(pair * PAIR, (pair + 1) * PAIR)
            query = q_ref[:, lanes]
            acc = None
            inverse = []
            for side in range(2):
                diag = mm_nt(k_ref[head, side, keys : keys + rows, :], query)
                diag = jnp.where(key_place <= query_place, diag, -1e9)
                top = jnp.max(diag, axis=0, keepdims=True)
                if span:
                    body = mm_nt(k_ref[head, side, :keys, :], query)
                    top = jnp.maximum(top, jnp.max(body, axis=0, keepdims=True))
                diag = jnp.exp(diag - top)
                total = jnp.sum(diag, axis=0, keepdims=True)
                part = mm(vt_ref[head, side, :, keys : keys + rows], diag.astype(jnp.bfloat16))
                if span:
                    body = jnp.exp(body - top)
                    total = total + jnp.sum(body, axis=0, keepdims=True)
                    part = part + mm(vt_ref[head, side, :, :keys], body.astype(jnp.bfloat16))
                acc = part if acc is None else acc + part
                inverse.append(jnp.broadcast_to(1.0 / total, (HEAD_DIM, rows)))
                l_ref[2 * pair + side : 2 * pair + side + 1, :] = top + jnp.log(total)
            acc = acc * jnp.concatenate(inverse, axis=0)
            o_ref[:, lanes] = acc.T.astype(jnp.bfloat16)

    for span in range(size):
        pl.when(mine == span)(functools.partial(one, span))

    def project_out(ref):
        ref[:, :half] = mm_nt(o_ref[...], wo_ref[...]).astype(jnp.bfloat16)
        ref[:, half:] = mm_nt(o_ref[...], wx_ref[...]).astype(jnp.bfloat16)

    for step in range(size):
        pl.when(pl.program_id(0) == step)(functools.partial(project_out, part_refs[step]))


def attend(me, query, key_pad, value_pad, own, other, size, group):
    total, width = query.shape
    features = 2 * own.shape[0]
    rows, heads = total // size, width // HEAD_DIM
    whole = pl.BlockSpec(key_pad.shape, lambda p, m: (0, 0, 0, 0), pipeline_mode=ONCE)
    spec = pltpu.PrefetchScalarGridSpec(
        num_scalar_prefetch=1,
        grid=(size,),
        in_specs=[pl.BlockSpec((rows, width), lambda p, m: (p, 0)), whole, whole]
        + [pl.BlockSpec(own.shape, lambda p, m: (0, 0), pipeline_mode=ONCE)] * 2,
        out_specs=[
            pl.BlockSpec((rows, width), lambda p, m: (p, 0)),
            pl.BlockSpec((heads, rows), lambda p, m: (0, p)),
        ]
        + [pl.BlockSpec((rows, features), lambda p, m: (0, 0))] * size,
        scratch_shapes=[pltpu.VMEM((heads // group, 2, PAIR, total), jnp.bfloat16)],
    )
    return pl.pallas_call(
        functools.partial(attend_kernel, size=size, heads=heads, group=group),
        grid_spec=spec,
        out_shape=[
            jax.ShapeDtypeStruct((total, width), jnp.bfloat16),
            jax.ShapeDtypeStruct((heads, total), jnp.float32),
        ]
        + [jax.ShapeDtypeStruct((rows, features), jnp.bfloat16)] * size,
        compiler_params=PARAMS,
        cost_estimate=hint(8 * heads * total * total * HEAD_DIM // 16),
    )(me, query, key_pad, value_pad, own, other)


def attend_back_kernel(
    me_ref, q_ref, l_ref, k_ref, v_ref, cos_ref, sin_ref, *refs, size, heads, group
):
    do_refs = refs[:size]
    out_ref, dk_ref, dv_ref, kt_ref, do_ref = refs[size:]
    rows = q_ref.shape[0]
    key_heads = heads // group
    step = pl.program_id(0)
    me = me_ref[0]
    mine = jnp.bitwise_xor(me, step)
    key_place = lax.broadcasted_iota(jnp.int32, (rows, rows), 0)
    query_place = lax.broadcasted_iota(jnp.int32, (rows, rows), 1)

    def rows_of(block):
        return pl.ds(pl.multiple_of(block * rows, rows), rows)

    @pl.when(step == 0)
    def _():
        dk_ref[...] = jnp.zeros_like(dk_ref)
        dv_ref[...] = jnp.zeros_like(dv_ref)
        for head in range(key_heads):
            for side in range(2):
                kt_ref[head, side] = k_ref[head, side].T

    def fetch(ref):
        do_ref[...] = ref[...]

    for block in range(size):
        pl.when(step == block)(functools.partial(fetch, do_refs[block]))

    def one(span):
        keys = span * rows
        parts = [(keys, keys + rows, True)] + ([(0, keys, False)] if span else [])
        cosine, sine = cos_ref[keys : keys + rows, :], sin_ref[keys : keys + rows, :]
        for pair in range(heads // 2):
            head = 2 * pair // group
            lanes = slice(pair * PAIR, (pair + 1) * PAIR)
            query, grad = q_ref[:, lanes], do_ref[:, lanes]
            acc = None
            for side in range(2):
                log_total = l_ref[2 * pair + side : 2 * pair + side + 1, :]
                inner = None
                kept = []
                for low, high, diagonal in parts:
                    probs = mm_nt(k_ref[head, side, low:high, :], query)
                    probs = jnp.exp(probs - log_total)
                    if diagonal:
                        probs = jnp.where(key_place <= query_place, probs, 0.0)
                    prob_grad = mm_nt(v_ref[head, side, low:high, :], grad)
                    dv_ref[head, side, low:high, :] += mm(probs.astype(jnp.bfloat16), grad)
                    term = jnp.sum(probs * prob_grad, axis=0, keepdims=True)
                    inner = term if inner is None else inner + term
                    kept.append((low, high, probs, prob_grad))
                for low, high, probs, prob_grad in kept:
                    score_grad = (probs * (prob_grad - inner)).astype(jnp.bfloat16)
                    dk_ref[head, side, low:high, :] += mm(score_grad, query)
                    part = mm(kt_ref[head, side, :, low:high], score_grad)
                    acc = part if acc is None else acc + part
            turned = turn(acc.T * SCALE, cosine, -sine)
            out_ref[rows_of(step), lanes] = turned.astype(jnp.bfloat16)

    for span in range(size):
        pl.when(mine == span)(functools.partial(one, span))

    @pl.when(step == size - 1)
    def _():
        first = lane_index(rows) < HEAD_DIM
        wanted = [(dk_ref, head, True) for head in range(key_heads)]
        wanted += [(dv_ref, head, False) for head in range(key_heads)]
        for span in range(size):
            place = slice(span * rows, (span + 1) * rows)
            cosine, sine = cos_ref[place, :], sin_ref[place, :]
            for block in range(len(wanted) // 2):
                halves, rotate = [], []
                for half in range(2):
                    ref, head, is_key = wanted[2 * block + half]
                    low, high = ref[head, 0, place, :], ref[head, 1, place, :]
                    if half:
                        halves.append(pltpu.roll(low, HEAD_DIM, 1) + high)
                    else:
                        halves.append(low + pltpu.roll(high, HEAD_DIM, 1))
                    rotate.append(is_key)
                value = jnp.where(first, halves[0], halves[1])
                if rotate[0] and rotate[1]:
                    value = turn(value, cosine, -sine)
                elif rotate[0]:
                    value = jnp.where(first, turn(value, cosine, -sine), value)
                start = heads * HEAD_DIM + block * PAIR
                target = rows_of(jnp.bitwise_xor(me, span))
                out_ref[target, start : start + PAIR] = value.astype(jnp.bfloat16)


def attend_back(
    me, query, log_total, key_pad, value_pad, cosine, sine, attended_grad, group
):
    total, width = query.shape
    size = len(attended_grad)
    rows, heads = total // size, width // HEAD_DIM
    key_heads = heads // group
    out_width = width + 2 * key_heads * HEAD_DIM
    whole = pl.BlockSpec(key_pad.shape, lambda p, m: (0, 0, 0, 0), pipeline_mode=ONCE)
    table = pl.BlockSpec((total, PAIR), lambda p, m: (0, 0), pipeline_mode=ONCE)
    spec = pltpu.PrefetchScalarGridSpec(
        num_scalar_prefetch=1,
        grid=(size,),
        in_specs=[
            pl.BlockSpec((rows, width), lambda p, m: (p, 0)),
            pl.BlockSpec((heads, rows), lambda p, m: (0, p)),
            whole,
            whole,
            table,
            table,
        ]
        + [pl.BlockSpec((rows, width), lambda p, m: (0, 0), pipeline_mode=ONCE)] * size,
        out_specs=pl.BlockSpec((total, out_width), lambda p, m: (0, 0)),
        scratch_shapes=[
            pltpu.VMEM(key_pad.shape, jnp.float32),
            pltpu.VMEM(key_pad.shape, jnp.float32),
            pltpu.VMEM((key_heads, 2, PAIR, total), jnp.bfloat16),
            pltpu.VMEM((rows, width), jnp.bfloat16),
        ],
    )
    return pl.pallas_call(
        functools.partial(attend_back_kernel, size=size, heads=heads, group=group),
        grid_spec=spec,
        out_shape=jax.ShapeDtypeStruct((total, out_width), jnp.bfloat16),
        compiler_params=PARAMS,
        cost_estimate=hint(20 * heads * total * total * HEAD_DIM),
    )(me, query, log_total, key_pad, value_pad, cosine, sine, *attended_grad)


def mlp_kernel(*refs, size, adds):
    n_refs, e_refs = refs[:size], refs[size : 2 * size]
    gate_o, up_o, down_o, gate_x, up_x, down_x = refs[2 * size : 2 * size + 6]
    y_ref, n_ref, e_ref = refs[-3:]
    dn_refs = refs[-3 - size if adds else -4 : -3]
    dg_ref, du_ref, h_ref = refs[-6 - size if adds else -7 :][:3]
    half = gate_o.shape[0]

    def fetch(step):
        n_ref[...] = n_refs[step][...]
        e_ref[...] = e_refs[step][...]

    for step in range(size):
        pl.when(pl.program_id(0) == step)(functools.partial(fetch, step))
    gate = mm(n_ref[:, :half], gate_o[...]) + mm(n_ref[:, half:], gate_x[...])
    up = mm(n_ref[:, :half], up_o[...]) + mm(n_ref[:, half:], up_x[...])
    grad = mm(e_ref[:, :half], down_o[...]) + mm(e_ref[:, half:], down_x[...])
    sigma = jax.nn.sigmoid(gate)
    silu = gate * sigma
    hidden = (silu * up).astype(jnp.bfloat16)
    gate_grad = (grad * up * sigma * (1.0 + gate * (1.0 - sigma))).astype(jnp.bfloat16)
    up_grad = (grad * silu).astype(jnp.bfloat16)
    dg_ref[...] = gate_grad
    du_ref[...] = up_grad
    h_ref[...] = hidden
    for part, gate_w, up_w, down_w in ((0, gate_o, up_o, down_o), (1, gate_x, up_x, down_x)):
        lanes = slice(part * half, (part + 1) * half)
        dn = mm_nt(gate_grad, gate_w[...]) + mm_nt(up_grad, up_w[...])
        y = mm_nt(hidden, down_w[...])
        if adds:
            dn = dn + refs[2 * size + 6][:, lanes].astype(jnp.float32)
            y = y + refs[2 * size + 7][:, lanes].astype(jnp.float32)
        y_ref[:, lanes] = y.astype(jnp.bfloat16)
        dn = dn.astype(jnp.bfloat16)

        def store(ref):
            ref[:, lanes] = dn

        if adds:
            for step in range(size):
                pl.when(pl.program_id(0) == step)(functools.partial(store, dn_refs[step]))
        else:
            store(dn_refs[0])


def mlp(tokens, cot, own, other, earlier):
    size = len(tokens)
    rows, features = tokens[0].shape
    half, units = own.shape[0], own.shape[1] // 3
    total = rows * size
    fixed = lambda p: (0, 0)
    moving = lambda p: (p, 0)
    wide = pl.BlockSpec((rows, features), moving)
    sums = jax.ShapeDtypeStruct((total, features), jnp.bfloat16)
    dn_specs, dn_shapes = [wide], [sums]
    if earlier:
        dn_specs = [pl.BlockSpec((rows, features), fixed)] * size
        dn_shapes = [jax.ShapeDtypeStruct((rows, features), jnp.bfloat16)] * size
    block = pl.BlockSpec((rows, features), fixed, pipeline_mode=ONCE)
    thirds = [
        pl.BlockSpec((half, units), lambda p, t=t: (0, t), pipeline_mode=ONCE) for t in range(3)
    ]
    return pl.pallas_call(
        functools.partial(mlp_kernel, size=size, adds=bool(earlier)),
        grid=(size,),
        in_specs=[block] * (2 * size)
        + thirds * 2
        + [wide] * len(earlier),
        out_specs=[pl.BlockSpec((rows, units), moving)] * 3 + dn_specs + [wide],
        out_shape=[jax.ShapeDtypeStruct((total, units), jnp.bfloat16)] * 3 + dn_shapes + [sums],
        scratch_shapes=[pltpu.VMEM((rows, features), jnp.bfloat16)] * 2,
        compiler_params=PARAMS,
        cost_estimate=hint(12 * total * features * units),
    )(*tokens, *cot, own, own, own, other, other, other, *earlier)


def add_refs(refs):
    total = refs[0][...].astype(jnp.float32)
    for ref in refs[1:]:
        total = total + ref[...].astype(jnp.float32)
    return total


def store_by_device(out_ref, values, core, chips):
    width = values.shape[1] // (2 * chips)
    for chip in range(chips):
        own = values[:, chip * width : (chip + 1) * width]
        other = values[:, (chips + chip) * width : (chips + chip + 1) * width]
        low = 2 * chip * width
        out_ref[:, low : low + width] = jnp.where(core == 0, own, other)
        out_ref[:, low + width : low + 2 * width] = jnp.where(core == 0, other, own)


def middle_kernel(*refs):
    x_ref, gain_ref, middle_ref, normed_ref = refs[-4:]
    values = x_ref[...].astype(jnp.float32) + add_refs(refs[:-4])
    middle_ref[...] = values
    normed_ref[...] = (values * rms_scale(values) * gain_ref[...]).astype(jnp.bfloat16)


def input_back_kernel(core_ref, *refs, chips):
    x_ref, before_ref, gain_ref, out_ref = refs[-4:]
    values = x_ref[...].astype(jnp.float32)
    inner = add_refs(refs[:-4]) * gain_ref[...]
    scale = rms_scale(values)
    mean = jnp.mean(inner * values, axis=-1, keepdims=True)
    result = before_ref[...] + scale * inner - values * (scale * scale * scale) * mean
    store_by_device(out_ref, result, core_ref[0], chips)


def output_kernel(core_ref, *refs, chips):
    middle_ref, out_ref = refs[-2:]
    values = middle_ref[...] + add_refs(refs[:-2])
    store_by_device(out_ref, values.astype(jnp.bfloat16), core_ref[0], chips)


def row_call(body, dtypes, arrays, core=None):
    rows, features = arrays[0].shape
    steps = 2
    wide = pl.BlockSpec((rows // steps, features), lambda i, *_: (i, 0))
    row = pl.BlockSpec((1, features), lambda i, *_: (0, 0))
    scalars = [] if core is None else [jnp.full((1,), core, jnp.int32)]
    return pl.pallas_call(
        body,
        grid_spec=pltpu.PrefetchScalarGridSpec(
            num_scalar_prefetch=len(scalars),
            grid=(steps,),
            in_specs=[row if array.shape[0] == 1 else wide for array in arrays],
            out_specs=[wide] * len(dtypes),
        ),
        out_shape=[jax.ShapeDtypeStruct((rows, features), dtype) for dtype in dtypes],
        compiler_params=PARAMS,
        cost_estimate=hint(0),
    )(*scalars, *arrays)


def middle_back_kernel(*refs, size):
    n_refs, refs = refs[:size], refs[size:]
    x_ref, e_ref, gain_ref, refs = refs[0], refs[1], refs[2], refs[3:]
    own_refs, other_refs, refs = refs[:size], refs[size : 2 * size], refs[2 * size :]
    grad_ref, branch_ref, part_ref, do_refs = refs[0], refs[1], refs[2], refs[3:]
    half = own_refs[0].shape[0]
    grad = add_refs(n_refs)
    values = x_ref[...]
    scale = rms_scale(values)
    result, part = norm_back(grad, values, scale, gain_ref[...])

    @pl.when(pl.program_id(0) == 0)
    def _():
        part_ref[...] = jnp.zeros_like(part_ref)

    part_ref[...] += part[None, :]
    result = result + e_ref[...].astype(jnp.float32)
    grad_ref[...] = result
    branch = result.astype(jnp.bfloat16)
    branch_ref[...] = branch
    for own, other, do_ref in zip(own_refs, other_refs, do_refs):
        do = mm(branch[:, :half], own[...]) + mm(branch[:, half:], other[...])
        do_ref[...] = do.astype(jnp.bfloat16)


def middle_back(arrived, middle, cot, gain, own, other):
    size = len(arrived)
    rows, features = middle.shape
    width = own[0].shape[1]
    steps = 2
    wide = pl.BlockSpec((rows // steps, features), lambda i: (i, 0))
    narrow = pl.BlockSpec((rows // steps, width), lambda i: (i, 0))
    row = pl.BlockSpec((1, features), lambda i: (0, 0))
    weight = pl.BlockSpec((features // 2, width), lambda i: (0, 0), pipeline_mode=ONCE)
    grad, branch, part, *do = pl.pallas_call(
        functools.partial(middle_back_kernel, size=size),
        grid=(steps,),
        in_specs=[wide] * size + [wide, wide, row] + [weight] * (2 * size),
        out_specs=[wide, wide, row] + [narrow] * size,
        out_shape=[
            jax.ShapeDtypeStruct((rows, features), jnp.float32),
            jax.ShapeDtypeStruct((rows, features), jnp.bfloat16),
            jax.ShapeDtypeStruct((1, features), jnp.float32),
        ]
        + [jax.ShapeDtypeStruct((rows, width), jnp.bfloat16)] * size,
        compiler_params=PARAMS,
        cost_estimate=hint(2 * rows * features * width * size),
    )(*arrived, middle, cot, gain, *own, *other)
    return grad, branch, part[0], do


def column_grad(blocks, other, mine, theirs):
    rows = blocks[0].shape[0]
    total = mm_tn(other[...], theirs[...])
    for index, block in enumerate(blocks):
        total = total + mm_tn(block[...], mine[index * rows : (index + 1) * rows, :])
    return total


def grad_kernel(*refs, size):
    n_refs, e_refs = refs[:size], refs[size : 2 * size]
    n_other, e_other = refs[2 * size : 2 * size + 2]
    acts, out_ref = refs[2 * size + 2 : -1], refs[-1]
    units = acts[0].shape[1]
    for third in range(3):
        blocks, other = (e_refs, e_other) if third == 2 else (n_refs, n_other)
        grad = column_grad(blocks, other, acts[third], acts[third + 3])
        out_ref[0, :, third * units : (third + 1) * units] = grad.astype(jnp.bfloat16)


def mlp_grads(chips, tokens, cot, tokens_other, cot_other, mine, theirs):
    size = len(tokens)
    rows, features = tokens[0].shape
    total, units = mine[0].shape
    depth = features // (2 * chips)
    column = pl.BlockSpec((rows, depth), lambda b: (0, b))
    long = pl.BlockSpec((total, depth), lambda b: (0, b))
    fixed = pl.BlockSpec((total, units), lambda b: (0, 0), pipeline_mode=ONCE)
    return pl.pallas_call(
        functools.partial(grad_kernel, size=size),
        grid=(chips,),
        in_specs=[column] * (2 * size) + [long, long] + [fixed] * 6,
        out_specs=pl.BlockSpec((1, depth, 3 * units), lambda b: (b, 0, 0)),
        out_shape=jax.ShapeDtypeStruct((chips, depth, 3 * units), jnp.bfloat16),
        compiler_params=PARAMS,
        cost_estimate=hint(6 * total * features * units),
    )(*tokens, *cot, tokens_other, cot_other, *mine, *theirs)


def attn_grad_kernel(*refs, size):
    e_refs = refs[2 : 2 + size]
    n_ref, n_other = refs[:2]
    e_other, d_ref, d_other, o_ref, o_other, w_ref, g1_ref, g2_ref = refs[2 + size : -2]
    out_ref, gain_ref = refs[-2:]
    width, out_width = d_ref.shape[1], o_ref.shape[1]
    grad = column_grad([n_ref], n_other, d_ref, d_other)
    out_ref[0, :, :width] = grad.astype(jnp.bfloat16)
    out_grad = column_grad(e_refs, e_other, o_ref, o_other)
    out_ref[0, :, width : width + out_width] = out_grad.astype(jnp.bfloat16)
    first = jnp.sum(grad * w_ref[...].astype(jnp.float32), axis=1, keepdims=True) / g1_ref[...]
    lane = lane_index(grad.shape[0])
    gain_ref[0] = jnp.where(lane == 0, first, g2_ref[...])


def attn_grads(chips, tokens, branch, mine, theirs, weights, gain_one, gain_two_part):
    size = len(branch)
    qkv_grad, attended = mine
    tokens_other, branch_other, qkv_other, attended_other = theirs
    total, features = tokens.shape
    rows = total // size
    width, out_width = qkv_grad.shape[1], attended.shape[1]
    depth = features // (2 * chips)
    column = lambda b: (0, b)
    row = lambda b: (b, 0)
    long = pl.BlockSpec((total, depth), column)
    fixed = lambda array: pl.BlockSpec(array.shape, lambda b: (0, 0), pipeline_mode=ONCE)
    place = lambda b: (b, 0, 0)
    return pl.pallas_call(
        functools.partial(attn_grad_kernel, size=size),
        grid=(chips,),
        in_specs=[long, long]
        + [pl.BlockSpec((rows, depth), column)] * size
        + [long]
        + [fixed(qkv_grad)] * 2
        + [fixed(attended)] * 2
        + [
            pl.BlockSpec((depth, width), row),
            pl.BlockSpec((depth, 1), row),
            pl.BlockSpec((depth, 1), row),
        ],
        out_specs=[
            pl.BlockSpec((1, depth, width + out_width), place),
            pl.BlockSpec((1, depth, PAIR), place),
        ],
        out_shape=[
            jax.ShapeDtypeStruct((chips, depth, width + out_width), jnp.bfloat16),
            jax.ShapeDtypeStruct((chips, depth, PAIR), jnp.float32),
        ],
        compiler_params=PARAMS,
        cost_estimate=hint(2 * total * features * (width + out_width)),
    )(
        tokens,
        tokens_other,
        *branch,
        branch_other,
        qkv_grad,
        qkv_other,
        attended,
        attended_other,
        weights,
        gain_one,
        gain_two_part,
    )


def swap(values, step):
    size = lax.axis_size("tensor")
    return lax.ppermute(values, "tensor", [(i, i ^ step) for i in range(size)])


def spread(values):
    return [values] + [swap(values, step) for step in range(1, lax.axis_size("tensor"))]


def send_blocks(blocks):
    return [blocks[0]] + [swap(block, step + 1) for step, block in enumerate(blocks[1:])]


def send_rows(partial):
    size = lax.axis_size("tensor")
    return send_blocks(list(partial.reshape((size, -1) + partial.shape[1:])))


def add_up(blocks):
    total = blocks[0].astype(jnp.float32)
    for block in blocks[1:]:
        total = total + block.astype(jnp.float32)
    return total


def cross(values):
    count = lax.axis_size("dp")
    return lax.ppermute(values, "dp", [(i, i ^ 1) for i in range(count)])


def tables(positions):
    freqs = ROPE_BASE ** (-jnp.arange(0, HEAD_DIM, 2).astype(jnp.float32) / HEAD_DIM)
    angles = positions.astype(jnp.float32)[:, None] * freqs[None, :]
    cosine, sine = jnp.cos(angles), jnp.sin(angles)
    return (
        jnp.concatenate([cosine] * 4, axis=1),
        jnp.concatenate([-sine, sine, -sine, sine], axis=1),
    )


def chip_lines():
    count = lax.axis_size("dp")
    return [list(range(core, count, 2)) for core in range(2)]


def gather(values):
    return lax.all_gather(values, "dp", axis=0, tiled=True, axis_index_groups=chip_lines())


def scatter(values):
    total = lax.psum_scatter(
        values, "dp", scatter_dimension=0, tiled=True, axis_index_groups=chip_lines()
    )
    return total[0]


def along(values, step):
    count = lax.axis_size("dp")
    return lax.ppermute(values, "dp", [(i, (i + 2 * step) % count) for i in range(count)])


def line_order(blocks):
    chips = len(blocks)
    chip = lax.axis_index("dp") // 2
    placed = jnp.zeros((chips,) + blocks[0].shape, blocks[0].dtype)
    for step, block in enumerate(blocks):
        placed = lax.dynamic_update_index_in_dim(placed, block, (chip - step) % chips, 0)
    return placed.reshape((-1,) + blocks[0].shape[1:])


def line_parts(parts):
    chips = lax.axis_size("dp") // 2
    chip = lax.axis_index("dp") // 2
    blocks = [lax.dynamic_index_in_dim(parts, chip, 0, keepdims=False)]
    for step in range(1, chips):
        sent = lax.dynamic_index_in_dim(parts, (chip + step) % chips, 0, keepdims=False)
        blocks.append(along(sent, step))
    return blocks


def own_part(values):
    size = lax.axis_size("tensor")
    me = lax.axis_index("tensor")
    blocks = values.reshape((size, -1) + values.shape[1:])
    own = lax.dynamic_index_in_dim(blocks, me, 0, keepdims=False)
    for step in range(1, size):
        sent = lax.dynamic_index_in_dim(blocks, me ^ step, 0, keepdims=False)
        own = own + swap(sent, step)
    return own


def stack_kernel(*refs):
    rows = refs[0].shape[0]
    for index, ref in enumerate(refs[:-1]):
        refs[-1][index * rows : (index + 1) * rows, :] = ref[...]


def other_half(blocks):
    size = len(blocks)
    rows, features = blocks[0].shape
    shape = (size * rows, features // 2)
    halves = pl.pallas_call(
        stack_kernel,
        grid=(1,),
        in_specs=[pl.BlockSpec((rows, features // 2), lambda i: (0, 1))] * size,
        out_specs=pl.BlockSpec(shape, lambda i: (0, 0)),
        out_shape=jax.ShapeDtypeStruct(shape, blocks[0].dtype),
        compiler_params=PARAMS,
        cost_estimate=hint(0),
    )(*blocks)
    return cross(halves)


def feature_blocks(values):
    width = values.shape[-1] // lax.axis_size("dp")
    return [values[..., low : low + width] for low in range(0, values.shape[-1], width)]


def by_core(values, core):
    blocks = feature_blocks(values)
    pairs = list(zip(blocks[0::2], blocks[1::2]))
    own = [jnp.where(core == 0, even, odd) for even, odd in pairs]
    other = [jnp.where(core == 0, odd, even) for even, odd in pairs]
    return jnp.concatenate(own + other, axis=-1)


def per_device(
    hidden_in,
    gain_attn,
    w_query,
    w_key,
    w_value,
    w_out,
    gain_mlp,
    w_gate,
    w_up,
    w_down,
    positions,
    cotangent,
):
    size = lax.axis_size("tensor")
    chips = lax.axis_size("dp") // 2
    me = lax.axis_index("tensor")
    me_array = jnp.full((1,), me, jnp.int32)
    core = lax.axis_index("dp") % 2
    q_width, kv_width = w_query.shape[1], w_key.shape[1]
    qkv_width = q_width + 2 * kv_width
    group = q_width // kv_width
    units = w_down.shape[0] // 2
    half = hidden_in.shape[1] // 2

    qkv_shard = jnp.concatenate([w_query, w_key, w_value], axis=1)
    out_shard = w_out.T
    qkv_shard, out_shard, hidden_in, gain_attn = barrier(
        (qkv_shard, out_shard, hidden_in, gain_attn)
    )
    qkv_own = gather(qkv_shard)
    residual = by_core(hidden_in, core)
    blocks_in = spread(residual)
    early_out = along(out_shard, 1)
    gains = lax.all_gather(jnp.stack([gain_attn, gain_mlp]), "dp", axis=1, tiled=True)
    gains = by_core(gains, core).astype(jnp.float32)
    cosine, sine = tables(positions)
    cotangent = by_core(cotangent, core)
    down_t = w_down.T
    shares = []
    for part in range(2):
        cut = slice(part * units, (part + 1) * units)
        shares.append(jnp.concatenate([w_gate[:, cut], w_up[:, cut], down_t[:, cut]], axis=1))
    shares, qkv_own, cosine, sine, gains = barrier((shares, qkv_own, cosine, sine, gains))
    blocks_in, cotangent, early_out, out_shard = barrier(
        (blocks_in, cotangent, early_out, out_shard)
    )
    out_parts = [out_shard, early_out] + [along(out_shard, step) for step in range(2, chips)]
    mlp_own = [gather(share) for share in shares]
    early_cot = [swap(cotangent, step) for step in range(1, 3)]
    gain_one, gain_two = gains[0], gains[1]
    qkv = (qkv_own, cross(qkv_own))

    tokens_one, query, key_pad, value_pad = project(
        me_array, blocks_in, gain_one[None, :], *qkv, cosine, sine, q_width, kv_width
    )
    query, out_parts, early_cot, cotangent = barrier((query, out_parts, early_cot, cotangent))
    cot_blocks = [cotangent] + early_cot + [swap(cotangent, step) for step in range(3, size)]
    out_own = line_order(out_parts)
    out_t = (out_own, cross(out_own))
    attended, log_total, *parts = attend(
        me_array, query, key_pad, value_pad, *out_t, size, group
    )
    parts, cot_blocks, tokens_one, attended = barrier((parts, cot_blocks, tokens_one, attended))
    arrived = send_blocks(parts)
    cot_other = other_half(cot_blocks)
    early = (cross(tokens_one[:, half:]), cross(attended))
    arrived, cot_other, early = barrier((arrived, cot_other, early))
    middle, normed_two = row_call(
        middle_kernel, [jnp.float32, jnp.bfloat16], [*arrived, residual, gain_two[None, :]]
    )
    normed_two, own_share = barrier((normed_two, mlp_own[0]))
    tokens_two = spread(normed_two)
    weights = (own_share, cross(own_share))
    tokens_two, weights, out_own = barrier((tokens_two, weights, out_t[0]))
    tokens_other = other_half(tokens_two)
    *acts, dn_part, y_part = mlp(tokens_two, cot_blocks, *weights, ())
    out_blocks = spread(out_own)
    acts, tokens_other = barrier((acts, tokens_other))
    acts_other = [cross(act) for act in acts]
    grads_one = mlp_grads(
        chips, tokens_two, cot_blocks, tokens_other, cot_other, acts, acts_other
    )
    grads_one, own_share = barrier((grads_one, mlp_own[1]))
    sums_one = scatter(grads_one)
    weights = (own_share, cross(own_share))
    *acts, y_part = mlp(tokens_two, cot_blocks, *weights, (dn_part, y_part))
    acts, dn_part = acts[:3], acts[3:]
    acts, dn_part, out_blocks = barrier((acts, dn_part, out_blocks))
    arrived = send_blocks(dn_part)
    out_other = [out_t[1]] + [cross(block) for block in out_blocks[1:]]
    acts_other = [cross(act) for act in acts]
    grads_two = mlp_grads(
        chips, tokens_two, cot_blocks, tokens_other, cot_other, acts, acts_other
    )
    grads_two, arrived, out_other, y_part = barrier((grads_two, arrived, out_other, y_part))
    y_blocks = list(y_part.reshape((size, -1) + y_part.shape[1:]))
    y_early = [swap(y_blocks[step], step) for step in range(1, 3)]
    sums_two = scatter(grads_two)
    middle_grad, branch, gain_two_part, do_blocks = middle_back(
        arrived, middle, cotangent, gain_two[None, :], out_blocks, out_other
    )
    do_blocks = send_blocks(do_blocks)
    gain_two_other = cross(gain_two_part[half:])
    do_blocks, branch, gain_two_other, y_blocks, y_early = barrier(
        (do_blocks, branch, gain_two_other, y_blocks, y_early)
    )
    branch_blocks = spread(branch)
    qkv_grad = attend_back(
        me_array, query, log_total, key_pad, value_pad, cosine, sine, do_blocks, group
    )
    qkv_grad, sums_one = barrier((qkv_grad, sums_one))
    qkv_other = cross(qkv_grad)
    normed_part = jnp.concatenate([mm_nt(qkv_grad, w) for w in qkv], axis=1).astype(jnp.bfloat16)
    branch_blocks, normed_part = barrier((branch_blocks, normed_part))
    arrived = send_rows(normed_part)
    branch_other = other_half(branch_blocks)
    tokens_other, attended_other = early
    grads, gain_parts = attn_grads(
        chips,
        tokens_one,
        branch_blocks,
        (qkv_grad, attended),
        (tokens_other, branch_other, qkv_other, attended_other),
        qkv[0],
        gain_one[:half, None],
        (gain_two_part[:half] + gain_two_other)[:, None],
    )
    attn_sums = scatter(grads)
    gain_sums = add_up(line_parts(gain_parts[:, :, :2]))
    arrived, gain_sums, y_blocks, sums_two = barrier((arrived, gain_sums, y_blocks, sums_two))
    y_late = [swap(y_blocks[step], step) for step in range(3, size)]
    gain_sums = own_part(gain_sums)
    (grad_in,) = row_call(
        functools.partial(input_back_kernel, chips=chips),
        [jnp.float32],
        [*arrived, residual, middle_grad, gain_one[None, :]],
        core,
    )
    shares = [share.astype(jnp.float32) for share in (sums_one, sums_two)]
    grad_gate = jnp.concatenate([h[:, :units] for h in shares], axis=1)
    grad_up = jnp.concatenate([h[:, units : 2 * units] for h in shares], axis=1)
    grad_down = jnp.concatenate([h[:, 2 * units :].T for h in shares], axis=0)
    y_late, grad_in, gain_sums, grad_gate, grad_up, grad_down = barrier(
        (y_late, grad_in, gain_sums, grad_gate, grad_up, grad_down)
    )
    (out,) = row_call(
        functools.partial(output_kernel, chips=chips),
        [jnp.bfloat16],
        [y_blocks[0], *y_early, *y_late, middle],
        core,
    )
    out, attn_sums = barrier((out, attn_sums))
    attn_sums = attn_sums.astype(jnp.float32)
    return (
        out,
        grad_in,
        gain_sums[:, 0],
        attn_sums[:, :q_width],
        attn_sums[:, q_width : q_width + kv_width],
        attn_sums[:, q_width + kv_width : qkv_width],
        attn_sums[:, qkv_width:].T,
        gain_sums[:, 1],
        grad_gate,
        grad_up,
        grad_down,
    )


def solution(mesh):
    return jax.shard_map(
        per_device,
        mesh=mesh,
        in_specs=(
            P(("dp", "tensor"), None),
            P("dp"),
            P("dp", "tensor"),
            P("dp", "tensor"),
            P("dp", "tensor"),
            P("tensor", "dp"),
            P("dp"),
            P("dp", "tensor"),
            P("dp", "tensor"),
            P("tensor", "dp"),
            P("dp"),
            P(("dp", "tensor"), None),
        ),
        out_specs=(
            P(("dp", "tensor"), None),
            P(("dp", "tensor"), None),
            P(("dp", "tensor")),
            P("dp", "tensor"),
            P("dp", "tensor"),
            P("dp", "tensor"),
            P("tensor", "dp"),
            P(("dp", "tensor")),
            P("dp", "tensor"),
            P("dp", "tensor"),
            P("tensor", "dp"),
        ),
        check_vma=False,
    )
```

```python
import functools
import math

import jax
import jax.numpy as jnp
from jax import lax
from jax.experimental import pallas as pl
from jax.experimental.pallas import tpu as pltpu
from jax.sharding import PartitionSpec as P

HEAD_DIM = 64
PAIR = 2 * HEAD_DIM
SEQ_LEN = 1024


EPS = 1e-05
ROPE_BASE = 500000.0
SCALE = 1.0 / math.sqrt(HEAD_DIM)
PARAMS = pltpu.CompilerParams(vmem_limit_bytes=58 * 2**20)
ONCE = pl.Buffered(1)

barrier = lax.optimization_barrier


def hint(flops):
    return pl.CostEstimate(flops=flops, bytes_accessed=0, transcendentals=0)


def rms_scale(values):
    return lax.rsqrt(jnp.mean(values * values, axis=-1, keepdims=True) + EPS)


def norm_back(grad, values, scale, gain):
    inner = grad * gain
    cubed = scale * scale * scale
    result = scale * inner - values * cubed * jnp.mean(inner * values, axis=-1, keepdims=True)
    return (result, jnp.sum(grad * values * scale, axis=0))


def mm(left, right):
    return jnp.dot(left, right, preferred_element_type=jnp.float32)


def mm_nt(left, right):
    return lax.dot_general(left, right, (((1,), (1,)), ((), ())), preferred_element_type=jnp.float32)


def mm_tn(left, right):
    return lax.dot_general(left, right, (((0,), (0,)), ((), ())), preferred_element_type=jnp.float32)


def lane_index(rows):
    return lax.broadcasted_iota(jnp.int32, (rows, PAIR), 1)


def turn(pair, cosine, sine):
    lower = lane_index(pair.shape[0]) % HEAD_DIM < HEAD_DIM // 2
    other = jnp.where(
        lower, pltpu.roll(pair, PAIR - HEAD_DIM // 2, 1), pltpu.roll(pair, HEAD_DIM // 2, 1)
    )
    return pair * cosine + other * sine


def project_kernel(place_ref, *refs, size, q_width, kv_width):
    x_refs = refs[:size]
    gain_ref, wo_ref, wx_ref, cos_ref, sin_ref, n_ref, q_ref, k_ref, v_ref = refs[size:]
    rows = q_ref.shape[0]
    half = wo_ref.shape[0]

    def one(x_ref):
        x = x_ref[...].astype(jnp.float32)
        normed = (x * rms_scale(x) * gain_ref[...]).astype(jnp.bfloat16)
        n_ref[...] = normed
        cosine, sine = cos_ref[...], sin_ref[...]
        lin = mm(normed[:, :half], wo_ref[...]) + mm(normed[:, half:], wx_ref[...])
        for low in range(0, q_width, PAIR):
            query = turn(lin[:, low : low + PAIR], cosine, sine).astype(jnp.bfloat16)
            q_ref[:, low : low + PAIR] = query * jnp.bfloat16(SCALE)
        first = lane_index(rows) < HEAD_DIM
        for ref, start, rotate in ((k_ref, q_width, True), (v_ref, q_width + kv_width, False)):
            for head in range(kv_width // HEAD_DIM):
                low = start + head * HEAD_DIM
                block = lin[:, low // PAIR * PAIR : low // PAIR * PAIR + PAIR]
                if rotate:
                    block = turn(block, cosine, sine)
                moved = pltpu.roll(block, HEAD_DIM, 1)
                if low % PAIR:
                    block, moved = moved, block
                ref[head, 0] = jnp.where(first, block, 0.0).astype(jnp.bfloat16)
                ref[head, 1] = jnp.where(first, 0.0, moved).astype(jnp.bfloat16)

    for step in range(size):
        pl.when(pl.program_id(0) == step)(functools.partial(one, x_refs[step]))


def project(me, blocks, gain, own, other, cosine, sine, q_width, kv_width):
    size = len(blocks)
    rows, features = blocks[0].shape
    total = rows * size
    key_heads = kv_width // HEAD_DIM
    width = q_width + 2 * kv_width
    fixed = lambda p, m: (0, 0)
    placed = lambda p, m: (jnp.bitwise_xor(p, m[0]), 0)
    padded = pl.BlockSpec(
        (key_heads, 2, rows, PAIR), lambda p, m: (0, 0, jnp.bitwise_xor(p, m[0]), 0)
    )
    spec = pltpu.PrefetchScalarGridSpec(
        num_scalar_prefetch=1,
        grid=(size,),
        in_specs=[pl.BlockSpec((rows, features), fixed, pipeline_mode=ONCE)] * size
        + [
            pl.BlockSpec((1, features), fixed),
            pl.BlockSpec((features // 2, width), fixed, pipeline_mode=ONCE),
            pl.BlockSpec((features // 2, width), fixed, pipeline_mode=ONCE),
            pl.BlockSpec((rows, PAIR), placed),
            pl.BlockSpec((rows, PAIR), placed),
        ],
        out_specs=[
            pl.BlockSpec((rows, features), lambda p, m: (p, 0)),
            pl.BlockSpec((rows, q_width), lambda p, m: (p, 0)),
            padded,
            padded,
        ],
    )
    padded_shape = jax.ShapeDtypeStruct((key_heads, 2, total, PAIR), jnp.bfloat16)
    return pl.pallas_call(
        functools.partial(project_kernel, size=size, q_width=q_width, kv_width=kv_width),
        grid_spec=spec,
        out_shape=[
            jax.ShapeDtypeStruct((total, features), jnp.bfloat16),
            jax.ShapeDtypeStruct((total, q_width), jnp.bfloat16),
            padded_shape,
            padded_shape,
        ],
        compiler_params=PARAMS,
        cost_estimate=hint(2 * total * features * width // 16),
    )(me, *blocks, gain, own, other, cosine, sine)


def attend_kernel(
    me_ref, q_ref, k_ref, v_ref, wo_ref, wx_ref, o_ref, l_ref, *refs, size, heads, group
):
    part_refs, vt_ref = refs[:size], refs[size]
    rows = q_ref.shape[0]
    half = wo_ref.shape[0]
    mine = jnp.bitwise_xor(me_ref[0], pl.program_id(0))
    key_place = lax.broadcasted_iota(jnp.int32, (rows, rows), 0)
    query_place = lax.broadcasted_iota(jnp.int32, (rows, rows), 1)

    @pl.when(pl.program_id(0) == 0)
    def _():
        for head in range(heads // group):
            for side in range(2):
                vt_ref[head, side] = v_ref[head, side].T

    def one(span):
        keys = span * rows
        for pair in range(heads // 2):
            head = 2 * pair // group
            lanes = slice(pair * PAIR, (pair + 1) * PAIR)
            query = q_ref[:, lanes]
            acc = None
            inverse = []
            for side in range(2):
                diag = mm_nt(k_ref[head, side, keys : keys + rows, :], query)
                diag = jnp.where(key_place <= query_place, diag, -1e9)
                top = jnp.max(diag, axis=0, keepdims=True)
                if span:
                    body = mm_nt(k_ref[head, side, :keys, :], query)
                    top = jnp.maximum(top, jnp.max(body, axis=0, keepdims=True))
                diag = jnp.exp(diag - top)
                total = jnp.sum(diag, axis=0, keepdims=True)
                part = mm(vt_ref[head, side, :, keys : keys + rows], diag.astype(jnp.bfloat16))
                if span:
                    body = jnp.exp(body - top)
                    total = total + jnp.sum(body, axis=0, keepdims=True)
                    part = part + mm(vt_ref[head, side, :, :keys], body.astype(jnp.bfloat16))
                acc = part if acc is None else acc + part
                inverse.append(jnp.broadcast_to(1.0 / total, (HEAD_DIM, rows)))
                l_ref[2 * pair + side : 2 * pair + side + 1, :] = top + jnp.log(total)
            acc = acc * jnp.concatenate(inverse, axis=0)
            o_ref[:, lanes] = acc.T.astype(jnp.bfloat16)

    for span in range(size):
        pl.when(mine == span)(functools.partial(one, span))

    def project_out(ref):
        ref[:, :half] = mm_nt(o_ref[...], wo_ref[...]).astype(jnp.bfloat16)
        ref[:, half:] = mm_nt(o_ref[...], wx_ref[...]).astype(jnp.bfloat16)

    for step in range(size):
        pl.when(pl.program_id(0) == step)(functools.partial(project_out, part_refs[step]))


def attend(me, query, key_pad, value_pad, own, other, size, group):
    total, width = query.shape
    features = 2 * own.shape[0]
    rows, heads = total // size, width // HEAD_DIM
    whole = pl.BlockSpec(key_pad.shape, lambda p, m: (0, 0, 0, 0), pipeline_mode=ONCE)
    spec = pltpu.PrefetchScalarGridSpec(
        num_scalar_prefetch=1,
        grid=(size,),
        in_specs=[pl.BlockSpec((rows, width), lambda p, m: (p, 0)), whole, whole]
        + [pl.BlockSpec(own.shape, lambda p, m: (0, 0), pipeline_mode=ONCE)] * 2,
        out_specs=[
            pl.BlockSpec((rows, width), lambda p, m: (p, 0)),
            pl.BlockSpec((heads, rows), lambda p, m: (0, p)),
        ]
        + [pl.BlockSpec((rows, features), lambda p, m: (0, 0))] * size,
        scratch_shapes=[pltpu.VMEM((heads // group, 2, PAIR, total), jnp.bfloat16)],
    )
    return pl.pallas_call(
        functools.partial(attend_kernel, size=size, heads=heads, group=group),
        grid_spec=spec,
        out_shape=[
            jax.ShapeDtypeStruct((total, width), jnp.bfloat16),
            jax.ShapeDtypeStruct((heads, total), jnp.float32),
        ]
        + [jax.ShapeDtypeStruct((rows, features), jnp.bfloat16)] * size,
        compiler_params=PARAMS,
        cost_estimate=hint(8 * heads * total * total * HEAD_DIM // 16),
    )(me, query, key_pad, value_pad, own, other)


def attend_back_kernel(
    me_ref, q_ref, l_ref, k_ref, v_ref, cos_ref, sin_ref, *refs, size, heads, group
):
    do_refs = refs[:size]
    out_ref, dk_ref, dv_ref, kt_ref, do_ref = refs[size:]
    rows = q_ref.shape[0]
    key_heads = heads // group
    step = pl.program_id(0)
    me = me_ref[0]
    mine = jnp.bitwise_xor(me, step)
    key_place = lax.broadcasted_iota(jnp.int32, (rows, rows), 0)
    query_place = lax.broadcasted_iota(jnp.int32, (rows, rows), 1)

    def rows_of(block):
        return pl.ds(pl.multiple_of(block * rows, rows), rows)

    @pl.when(step == 0)
    def _():
        dk_ref[...] = jnp.zeros_like(dk_ref)
        dv_ref[...] = jnp.zeros_like(dv_ref)
        for head in range(key_heads):
            for side in range(2):
                kt_ref[head, side] = k_ref[head, side].T

    def fetch(ref):
        do_ref[...] = ref[...]

    for block in range(size):
        pl.when(step == block)(functools.partial(fetch, do_refs[block]))

    def one(span):
        keys = span * rows
        parts = [(keys, keys + rows, True)] + ([(0, keys, False)] if span else [])
        cosine, sine = cos_ref[keys : keys + rows, :], sin_ref[keys : keys + rows, :]
        for pair in range(heads // 2):
            head = 2 * pair // group
            lanes = slice(pair * PAIR, (pair + 1) * PAIR)
            query, grad = q_ref[:, lanes], do_ref[:, lanes]
            acc = None
            for side in range(2):
                log_total = l_ref[2 * pair + side : 2 * pair + side + 1, :]
                inner = None
                kept = []
                for low, high, diagonal in parts:
                    probs = mm_nt(k_ref[head, side, low:high, :], query)
                    probs = jnp.exp(probs - log_total)
                    if diagonal:
                        probs = jnp.where(key_place <= query_place, probs, 0.0)
                    prob_grad = mm_nt(v_ref[head, side, low:high, :], grad)
                    dv_ref[head, side, low:high, :] += mm(probs.astype(jnp.bfloat16), grad)
                    term = jnp.sum(probs * prob_grad, axis=0, keepdims=True)
                    inner = term if inner is None else inner + term
                    kept.append((low, high, probs, prob_grad))
                for low, high, probs, prob_grad in kept:
                    score_grad = (probs * (prob_grad - inner)).astype(jnp.bfloat16)
                    dk_ref[head, side, low:high, :] += mm(score_grad, query)
                    part = mm(kt_ref[head, side, :, low:high], score_grad)
                    acc = part if acc is None else acc + part
            turned = turn(acc.T * SCALE, cosine, -sine)
            out_ref[rows_of(step), lanes] = turned.astype(jnp.bfloat16)

    for span in range(size):
        pl.when(mine == span)(functools.partial(one, span))

    @pl.when(step == size - 1)
    def _():
        first = lane_index(rows) < HEAD_DIM
        wanted = [(dk_ref, head, True) for head in range(key_heads)]
        wanted += [(dv_ref, head, False) for head in range(key_heads)]
        for span in range(size):
            place = slice(span * rows, (span + 1) * rows)
            cosine, sine = cos_ref[place, :], sin_ref[place, :]
            for block in range(len(wanted) // 2):
                halves, rotate = [], []
                for half in range(2):
                    ref, head, is_key = wanted[2 * block + half]
                    low, high = ref[head, 0, place, :], ref[head, 1, place, :]
                    if half:
                        halves.append(pltpu.roll(low, HEAD_DIM, 1) + high)
                    else:
                        halves.append(low + pltpu.roll(high, HEAD_DIM, 1))
                    rotate.append(is_key)
                value = jnp.where(first, halves[0], halves[1])
                if rotate[0] and rotate[1]:
                    value = turn(value, cosine, -sine)
                elif rotate[0]:
                    value = jnp.where(first, turn(value, cosine, -sine), value)
                start = heads * HEAD_DIM + block * PAIR
                target = rows_of(jnp.bitwise_xor(me, span))
                out_ref[target, start : start + PAIR] = value.astype(jnp.bfloat16)


def attend_back(
    me, query, log_total, key_pad, value_pad, cosine, sine, attended_grad, group
):
    total, width = query.shape
    size = len(attended_grad)
    rows, heads = total // size, width // HEAD_DIM
    key_heads = heads // group
    out_width = width + 2 * key_heads * HEAD_DIM
    whole = pl.BlockSpec(key_pad.shape, lambda p, m: (0, 0, 0, 0), pipeline_mode=ONCE)
    table = pl.BlockSpec((total, PAIR), lambda p, m: (0, 0), pipeline_mode=ONCE)
    spec = pltpu.PrefetchScalarGridSpec(
        num_scalar_prefetch=1,
        grid=(size,),
        in_specs=[
            pl.BlockSpec((rows, width), lambda p, m: (p, 0)),
            pl.BlockSpec((heads, rows), lambda p, m: (0, p)),
            whole,
            whole,
            table,
            table,
        ]
        + [pl.BlockSpec((rows, width), lambda p, m: (0, 0), pipeline_mode=ONCE)] * size,
        out_specs=pl.BlockSpec((total, out_width), lambda p, m: (0, 0)),
        scratch_shapes=[
            pltpu.VMEM(key_pad.shape, jnp.float32),
            pltpu.VMEM(key_pad.shape, jnp.float32),
            pltpu.VMEM((key_heads, 2, PAIR, total), jnp.bfloat16),
            pltpu.VMEM((rows, width), jnp.bfloat16),
        ],
    )
    return pl.pallas_call(
        functools.partial(attend_back_kernel, size=size, heads=heads, group=group),
        grid_spec=spec,
        out_shape=jax.ShapeDtypeStruct((total, out_width), jnp.bfloat16),
        compiler_params=PARAMS,
        cost_estimate=hint(20 * heads * total * total * HEAD_DIM),
    )(me, query, log_total, key_pad, value_pad, cosine, sine, *attended_grad)


def mlp_kernel(*refs, size, adds):
    n_refs, e_refs = refs[:size], refs[size : 2 * size]
    gate_o, up_o, down_o, gate_x, up_x, down_x = refs[2 * size : 2 * size + 6]
    y_ref, n_ref, e_ref = refs[-3:]
    dn_refs = refs[-3 - size if adds else -4 : -3]
    dg_ref, du_ref, h_ref = refs[-6 - size if adds else -7 :][:3]
    half = gate_o.shape[0]

    def fetch(step):
        n_ref[...] = n_refs[step][...]
        e_ref[...] = e_refs[step][...]

    for step in range(size):
        pl.when(pl.program_id(0) == step)(functools.partial(fetch, step))
    gate = mm(n_ref[:, :half], gate_o[...]) + mm(n_ref[:, half:], gate_x[...])
    up = mm(n_ref[:, :half], up_o[...]) + mm(n_ref[:, half:], up_x[...])
    grad = mm(e_ref[:, :half], down_o[...]) + mm(e_ref[:, half:], down_x[...])
    sigma = jax.nn.sigmoid(gate)
    silu = gate * sigma
    hidden = (silu * up).astype(jnp.bfloat16)
    gate_grad = (grad * up * sigma * (1.0 + gate * (1.0 - sigma))).astype(jnp.bfloat16)
    up_grad = (grad * silu).astype(jnp.bfloat16)
    dg_ref[...] = gate_grad
    du_ref[...] = up_grad
    h_ref[...] = hidden
    for part, gate_w, up_w, down_w in ((0, gate_o, up_o, down_o), (1, gate_x, up_x, down_x)):
        lanes = slice(part * half, (part + 1) * half)
        dn = mm_nt(gate_grad, gate_w[...]) + mm_nt(up_grad, up_w[...])
        y = mm_nt(hidden, down_w[...])
        if adds:
            dn = dn + refs[2 * size + 6][:, lanes].astype(jnp.float32)
            y = y + refs[2 * size + 7][:, lanes].astype(jnp.float32)
        y_ref[:, lanes] = y.astype(jnp.bfloat16)
        dn = dn.astype(jnp.bfloat16)

        def store(ref):
            ref[:, lanes] = dn

        if adds:
            for step in range(size):
                pl.when(pl.program_id(0) == step)(functools.partial(store, dn_refs[step]))
        else:
            store(dn_refs[0])


def mlp(tokens, cot, own, other, earlier):
    size = len(tokens)
    rows, features = tokens[0].shape
    half, units = own.shape[0], own.shape[1] // 3
    total = rows * size
    fixed = lambda p: (0, 0)
    moving = lambda p: (p, 0)
    wide = pl.BlockSpec((rows, features), moving)
    sums = jax.ShapeDtypeStruct((total, features), jnp.bfloat16)
    dn_specs, dn_shapes = [wide], [sums]
    if earlier:
        dn_specs = [pl.BlockSpec((rows, features), fixed)] * size
        dn_shapes = [jax.ShapeDtypeStruct((rows, features), jnp.bfloat16)] * size
    block = pl.BlockSpec((rows, features), fixed, pipeline_mode=ONCE)
    thirds = [
        pl.BlockSpec((half, units), lambda p, t=t: (0, t), pipeline_mode=ONCE) for t in range(3)
    ]
    return pl.pallas_call(
        functools.partial(mlp_kernel, size=size, adds=bool(earlier)),
        grid=(size,),
        in_specs=[block] * (2 * size)
        + thirds * 2
        + [wide] * len(earlier),
        out_specs=[pl.BlockSpec((rows, units), moving)] * 3 + dn_specs + [wide],
        out_shape=[jax.ShapeDtypeStruct((total, units), jnp.bfloat16)] * 3 + dn_shapes + [sums],
        scratch_shapes=[pltpu.VMEM((rows, features), jnp.bfloat16)] * 2,
        compiler_params=PARAMS,
        cost_estimate=hint(12 * total * features * units),
    )(*tokens, *cot, own, own, own, other, other, other, *earlier)


def add_refs(refs):
    total = refs[0][...].astype(jnp.float32)
    for ref in refs[1:]:
        total = total + ref[...].astype(jnp.float32)
    return total


def store_by_device(out_ref, values, core, chips):
    width = values.shape[1] // (2 * chips)
    for chip in range(chips):
        own = values[:, chip * width : (chip + 1) * width]
        other = values[:, (chips + chip) * width : (chips + chip + 1) * width]
        low = 2 * chip * width
        out_ref[:, low : low + width] = jnp.where(core == 0, own, other)
        out_ref[:, low + width : low + 2 * width] = jnp.where(core == 0, other, own)


def middle_kernel(*refs):
    x_ref, gain_ref, middle_ref, normed_ref = refs[-4:]
    values = x_ref[...].astype(jnp.float32) + add_refs(refs[:-4])
    middle_ref[...] = values
    normed_ref[...] = (values * rms_scale(values) * gain_ref[...]).astype(jnp.bfloat16)


def input_back_kernel(core_ref, *refs, chips):
    x_ref, before_ref, gain_ref, out_ref = refs[-4:]
    values = x_ref[...].astype(jnp.float32)
    inner = add_refs(refs[:-4]) * gain_ref[...]
    scale = rms_scale(values)
    mean = jnp.mean(inner * values, axis=-1, keepdims=True)
    result = before_ref[...] + scale * inner - values * (scale * scale * scale) * mean
    store_by_device(out_ref, result, core_ref[0], chips)


def output_kernel(core_ref, *refs, chips):
    middle_ref, out_ref = refs[-2:]
    values = middle_ref[...] + add_refs(refs[:-2])
    store_by_device(out_ref, values.astype(jnp.bfloat16), core_ref[0], chips)


def row_call(body, dtypes, arrays, core=None):
    rows, features = arrays[0].shape
    steps = 2
    wide = pl.BlockSpec((rows // steps, features), lambda i, *_: (i, 0))
    row = pl.BlockSpec((1, features), lambda i, *_: (0, 0))
    scalars = [] if core is None else [jnp.full((1,), core, jnp.int32)]
    return pl.pallas_call(
        body,
        grid_spec=pltpu.PrefetchScalarGridSpec(
            num_scalar_prefetch=len(scalars),
            grid=(steps,),
            in_specs=[row if array.shape[0] == 1 else wide for array in arrays],
            out_specs=[wide] * len(dtypes),
        ),
        out_shape=[jax.ShapeDtypeStruct((rows, features), dtype) for dtype in dtypes],
        compiler_params=PARAMS,
        cost_estimate=hint(0),
    )(*scalars, *arrays)


def middle_back_kernel(*refs, size):
    n_refs, refs = refs[:size], refs[size:]
    x_ref, e_ref, gain_ref, refs = refs[0], refs[1], refs[2], refs[3:]
    own_refs, other_refs, refs = refs[:size], refs[size : 2 * size], refs[2 * size :]
    grad_ref, branch_ref, part_ref, do_refs = refs[0], refs[1], refs[2], refs[3:]
    half = own_refs[0].shape[0]
    grad = add_refs(n_refs)
    values = x_ref[...]
    scale = rms_scale(values)
    result, part = norm_back(grad, values, scale, gain_ref[...])

    @pl.when(pl.program_id(0) == 0)
    def _():
        part_ref[...] = jnp.zeros_like(part_ref)

    part_ref[...] += part[None, :]
    result = result + e_ref[...].astype(jnp.float32)
    grad_ref[...] = result
    branch = result.astype(jnp.bfloat16)
    branch_ref[...] = branch
    for own, other, do_ref in zip(own_refs, other_refs, do_refs):
        do = mm(branch[:, :half], own[...]) + mm(branch[:, half:], other[...])
        do_ref[...] = do.astype(jnp.bfloat16)


def middle_back(arrived, middle, cot, gain, own, other):
    size = len(arrived)
    rows, features = middle.shape
    width = own[0].shape[1]
    steps = 2
    wide = pl.BlockSpec((rows // steps, features), lambda i: (i, 0))
    narrow = pl.BlockSpec((rows // steps, width), lambda i: (i, 0))
    row = pl.BlockSpec((1, features), lambda i: (0, 0))
    weight = pl.BlockSpec((features // 2, width), lambda i: (0, 0), pipeline_mode=ONCE)
    grad, branch, part, *do = pl.pallas_call(
        functools.partial(middle_back_kernel, size=size),
        grid=(steps,),
        in_specs=[wide] * size + [wide, wide, row] + [weight] * (2 * size),
        out_specs=[wide, wide, row] + [narrow] * size,
        out_shape=[
            jax.ShapeDtypeStruct((rows, features), jnp.float32),
            jax.ShapeDtypeStruct((rows, features), jnp.bfloat16),
            jax.ShapeDtypeStruct((1, features), jnp.float32),
        ]
        + [jax.ShapeDtypeStruct((rows, width), jnp.bfloat16)] * size,
        compiler_params=PARAMS,
        cost_estimate=hint(2 * rows * features * width * size),
    )(*arrived, middle, cot, gain, *own, *other)
    return grad, branch, part[0], do


def column_grad(blocks, other, mine, theirs):
    rows = blocks[0].shape[0]
    total = mm_tn(other[...], theirs[...])
    for index, block in enumerate(blocks):
        total = total + mm_tn(block[...], mine[index * rows : (index + 1) * rows, :])
    return total


def grad_kernel(*refs, size):
    n_refs, e_refs = refs[:size], refs[size : 2 * size]
    n_other, e_other = refs[2 * size : 2 * size + 2]
    acts, out_ref = refs[2 * size + 2 : -1], refs[-1]
    units = acts[0].shape[1]
    for third in range(3):
        blocks, other = (e_refs, e_other) if third == 2 else (n_refs, n_other)
        grad = column_grad(blocks, other, acts[third], acts[third + 3])
        out_ref[0, :, third * units : (third + 1) * units] = grad.astype(jnp.bfloat16)


def mlp_grads(chips, tokens, cot, tokens_other, cot_other, mine, theirs):
    size = len(tokens)
    rows, features = tokens[0].shape
    total, units = mine[0].shape
    depth = features // (2 * chips)
    column = pl.BlockSpec((rows, depth), lambda b: (0, b))
    long = pl.BlockSpec((total, depth), lambda b: (0, b))
    fixed = pl.BlockSpec((total, units), lambda b: (0, 0), pipeline_mode=ONCE)
    return pl.pallas_call(
        functools.partial(grad_kernel, size=size),
        grid=(chips,),
        in_specs=[column] * (2 * size) + [long, long] + [fixed] * 6,
        out_specs=pl.BlockSpec((1, depth, 3 * units), lambda b: (b, 0, 0)),
        out_shape=jax.ShapeDtypeStruct((chips, depth, 3 * units), jnp.bfloat16),
        compiler_params=PARAMS,
        cost_estimate=hint(6 * total * features * units),
    )(*tokens, *cot, tokens_other, cot_other, *mine, *theirs)


def attn_grad_kernel(*refs, size):
    e_refs = refs[2 : 2 + size]
    n_ref, n_other = refs[:2]
    e_other, d_ref, d_other, o_ref, o_other, w_ref, g1_ref, g2_ref = refs[2 + size : -2]
    out_ref, gain_ref = refs[-2:]
    width, out_width = d_ref.shape[1], o_ref.shape[1]
    grad = column_grad([n_ref], n_other, d_ref, d_other)
    out_ref[0, :, :width] = grad.astype(jnp.bfloat16)
    out_grad = column_grad(e_refs, e_other, o_ref, o_other)
    out_ref[0, :, width : width + out_width] = out_grad.astype(jnp.bfloat16)
    first = jnp.sum(grad * w_ref[...].astype(jnp.float32), axis=1, keepdims=True) / g1_ref[...]
    lane = lane_index(grad.shape[0])
    gain_ref[0] = jnp.where(lane == 0, first, g2_ref[...])


def attn_grads(chips, tokens, branch, mine, theirs, weights, gain_one, gain_two_part):
    size = len(branch)
    qkv_grad, attended = mine
    tokens_other, branch_other, qkv_other, attended_other = theirs
    total, features = tokens.shape
    rows = total // size
    width, out_width = qkv_grad.shape[1], attended.shape[1]
    depth = features // (2 * chips)
    column = lambda b: (0, b)
    row = lambda b: (b, 0)
    long = pl.BlockSpec((total, depth), column)
    fixed = lambda array: pl.BlockSpec(array.shape, lambda b: (0, 0), pipeline_mode=ONCE)
    place = lambda b: (b, 0, 0)
    return pl.pallas_call(
        functools.partial(attn_grad_kernel, size=size),
        grid=(chips,),
        in_specs=[long, long]
        + [pl.BlockSpec((rows, depth), column)] * size
        + [long]
        + [fixed(qkv_grad)] * 2
        + [fixed(attended)] * 2
        + [
            pl.BlockSpec((depth, width), row),
            pl.BlockSpec((depth, 1), row),
            pl.BlockSpec((depth, 1), row),
        ],
        out_specs=[
            pl.BlockSpec((1, depth, width + out_width), place),
            pl.BlockSpec((1, depth, PAIR), place),
        ],
        out_shape=[
            jax.ShapeDtypeStruct((chips, depth, width + out_width), jnp.bfloat16),
            jax.ShapeDtypeStruct((chips, depth, PAIR), jnp.float32),
        ],
        compiler_params=PARAMS,
        cost_estimate=hint(2 * total * features * (width + out_width)),
    )(
        tokens,
        tokens_other,
        *branch,
        branch_other,
        qkv_grad,
        qkv_other,
        attended,
        attended_other,
        weights,
        gain_one,
        gain_two_part,
    )


def input_grad_kernel(d_ref, wo_ref, wx_ref, *out_refs):
    half = wo_ref.shape[0]

    def one(ref):
        ref[:, :half] = mm_nt(d_ref[...], wo_ref[...]).astype(jnp.bfloat16)
        ref[:, half:] = mm_nt(d_ref[...], wx_ref[...]).astype(jnp.bfloat16)

    for step, ref in enumerate(out_refs):
        pl.when(pl.program_id(0) == step)(functools.partial(one, ref))


def input_grad(qkv_grad, own, other, size):
    total, width = qkv_grad.shape
    features = 2 * own.shape[0]
    rows = total // size
    fixed = lambda i: (0, 0)
    weight = pl.BlockSpec(own.shape, fixed, pipeline_mode=ONCE)
    return pl.pallas_call(
        input_grad_kernel,
        grid=(size,),
        in_specs=[pl.BlockSpec((rows, width), lambda i: (i, 0)), weight, weight],
        out_specs=[pl.BlockSpec((rows, features), fixed)] * size,
        out_shape=[jax.ShapeDtypeStruct((rows, features), jnp.bfloat16)] * size,
        compiler_params=PARAMS,
        cost_estimate=hint(2 * total * features * width),
    )(qkv_grad, own, other)


def swap(values, step):
    size = lax.axis_size("tensor")
    return lax.ppermute(values, "tensor", [(i, i ^ step) for i in range(size)])


def spread(values):
    return [values] + [swap(values, step) for step in range(1, lax.axis_size("tensor"))]


def send_blocks(blocks):
    return [blocks[0]] + [swap(block, step + 1) for step, block in enumerate(blocks[1:])]


def add_up(blocks):
    total = blocks[0].astype(jnp.float32)
    for block in blocks[1:]:
        total = total + block.astype(jnp.float32)
    return total


def cross(values):
    count = lax.axis_size("dp")
    return lax.ppermute(values, "dp", [(i, i ^ 1) for i in range(count)])


def tables(positions):
    freqs = ROPE_BASE ** (-jnp.arange(0, HEAD_DIM, 2).astype(jnp.float32) / HEAD_DIM)
    angles = positions.astype(jnp.float32)[:, None] * freqs[None, :]
    cosine, sine = jnp.cos(angles), jnp.sin(angles)
    return (
        jnp.concatenate([cosine] * 4, axis=1),
        jnp.concatenate([-sine, sine, -sine, sine], axis=1),
    )


def chip_lines():
    count = lax.axis_size("dp")
    return [list(range(core, count, 2)) for core in range(2)]


def gather(values):
    return lax.all_gather(values, "dp", axis=0, tiled=True, axis_index_groups=chip_lines())


def scatter(values):
    total = lax.psum_scatter(
        values, "dp", scatter_dimension=0, tiled=True, axis_index_groups=chip_lines()
    )
    return total[0]


def along(values, step):
    count = lax.axis_size("dp")
    return lax.ppermute(values, "dp", [(i, (i + 2 * step) % count) for i in range(count)])


def line_parts(parts):
    chips = lax.axis_size("dp") // 2
    chip = lax.axis_index("dp") // 2
    blocks = [lax.dynamic_index_in_dim(parts, chip, 0, keepdims=False)]
    for step in range(1, chips):
        sent = lax.dynamic_index_in_dim(parts, (chip + step) % chips, 0, keepdims=False)
        blocks.append(along(sent, step))
    return blocks


def own_part(values):
    size = lax.axis_size("tensor")
    me = lax.axis_index("tensor")
    blocks = values.reshape((size, -1) + values.shape[1:])
    own = lax.dynamic_index_in_dim(blocks, me, 0, keepdims=False)
    for step in range(1, size):
        sent = lax.dynamic_index_in_dim(blocks, me ^ step, 0, keepdims=False)
        own = own + swap(sent, step)
    return own


def stack_kernel(*refs):
    rows = refs[0].shape[0]
    for index, ref in enumerate(refs[:-1]):
        refs[-1][index * rows : (index + 1) * rows, :] = ref[...]


def other_half(blocks):
    size = len(blocks)
    rows, features = blocks[0].shape
    shape = (size * rows, features // 2)
    halves = pl.pallas_call(
        stack_kernel,
        grid=(1,),
        in_specs=[pl.BlockSpec((rows, features // 2), lambda i: (0, 1))] * size,
        out_specs=pl.BlockSpec(shape, lambda i: (0, 0)),
        out_shape=jax.ShapeDtypeStruct(shape, blocks[0].dtype),
        compiler_params=PARAMS,
        cost_estimate=hint(0),
    )(*blocks)
    return cross(halves)


def feature_blocks(values):
    width = values.shape[-1] // lax.axis_size("dp")
    return [values[..., low : low + width] for low in range(0, values.shape[-1], width)]


def by_core(values, core):
    blocks = feature_blocks(values)
    pairs = list(zip(blocks[0::2], blocks[1::2]))
    own = [jnp.where(core == 0, even, odd) for even, odd in pairs]
    other = [jnp.where(core == 0, odd, even) for even, odd in pairs]
    return jnp.concatenate(own + other, axis=-1)


def per_device(
    hidden_in,
    gain_attn,
    w_query,
    w_key,
    w_value,
    w_out,
    gain_mlp,
    w_gate,
    w_up,
    w_down,
    positions,
    cotangent,
):
    size = lax.axis_size("tensor")
    chips = lax.axis_size("dp") // 2
    me = lax.axis_index("tensor")
    me_array = jnp.full((1,), me, jnp.int32)
    core = lax.axis_index("dp") % 2
    q_width, kv_width = w_query.shape[1], w_key.shape[1]
    qkv_width = q_width + 2 * kv_width
    group = q_width // kv_width
    units = w_down.shape[0] // 2
    half = hidden_in.shape[1] // 2

    attn_shard = jnp.concatenate([w_query, w_key, w_value, w_out.T], axis=1)
    attn_shard, hidden_in, gain_attn = barrier((attn_shard, hidden_in, gain_attn))
    attn_own = gather(attn_shard)
    residual = by_core(hidden_in, core)
    blocks_in = spread(residual)
    gains = lax.all_gather(jnp.stack([gain_attn, gain_mlp]), "dp", axis=1, tiled=True)
    gains = by_core(gains, core).astype(jnp.float32)
    cosine, sine = tables(positions)
    cotangent = by_core(cotangent, core)
    down_t = w_down.T
    shares = []
    for part in range(2):
        cut = slice(part * units, (part + 1) * units)
        shares.append(jnp.concatenate([w_gate[:, cut], w_up[:, cut], down_t[:, cut]], axis=1))
    shares, attn_own, blocks_in, cosine, sine, gains, cotangent = barrier(
        (shares, attn_own, blocks_in, cosine, sine, gains, cotangent)
    )
    mlp_own = [gather(share) for share in shares]
    cot_blocks = spread(cotangent)
    gain_one, gain_two = gains[0], gains[1]
    qkv_own, out_own = attn_own[:, :qkv_width], attn_own[:, qkv_width:]
    qkv = (qkv_own, cross(qkv_own))
    out_t = (out_own, cross(out_own))

    tokens_one, query, key_pad, value_pad = project(
        me_array, blocks_in, gain_one[None, :], *qkv, cosine, sine, q_width, kv_width
    )
    attended, log_total, *parts = attend(
        me_array, query, key_pad, value_pad, *out_t, size, group
    )
    parts, cot_blocks, tokens_one, attended = barrier((parts, cot_blocks, tokens_one, attended))
    arrived = send_blocks(parts)
    cot_other = other_half(cot_blocks)
    early = (cross(tokens_one[:, half:]), cross(attended))
    arrived, cot_other, early = barrier((arrived, cot_other, early))
    middle, normed_two = row_call(
        middle_kernel, [jnp.float32, jnp.bfloat16], [*arrived, residual, gain_two[None, :]]
    )
    normed_two, own_share = barrier((normed_two, mlp_own[0]))
    tokens_two = spread(normed_two)
    weights = (own_share, cross(own_share))
    tokens_two, weights, out_own = barrier((tokens_two, weights, out_t[0]))
    tokens_other = other_half(tokens_two)
    *acts, dn_part, y_part = mlp(tokens_two, cot_blocks, *weights, ())
    out_blocks = spread(out_own)
    acts, tokens_other = barrier((acts, tokens_other))
    acts_other = [cross(act) for act in acts]
    grads_one = mlp_grads(
        chips, tokens_two, cot_blocks, tokens_other, cot_other, acts, acts_other
    )
    grads_one, own_share = barrier((grads_one, mlp_own[1]))
    sums_one = scatter(grads_one)
    weights = (own_share, cross(own_share))
    *acts, y_part = mlp(tokens_two, cot_blocks, *weights, (dn_part, y_part))
    acts, dn_part = acts[:3], acts[3:]
    acts, dn_part, out_blocks = barrier((acts, dn_part, out_blocks))
    arrived = send_blocks(dn_part)
    out_other = [out_t[1]] + [cross(block) for block in out_blocks[1:]]
    acts_other = [cross(act) for act in acts]
    grads_two = mlp_grads(
        chips, tokens_two, cot_blocks, tokens_other, cot_other, acts, acts_other
    )
    grads_two, arrived, out_other, y_part = barrier((grads_two, arrived, out_other, y_part))
    y_blocks = list(y_part.reshape((size, -1) + y_part.shape[1:]))
    y_early = [swap(y_blocks[step], step) for step in range(1, 3)]
    sums_two = scatter(grads_two)
    middle_grad, branch, gain_two_part, do_blocks = middle_back(
        arrived, middle, cotangent, gain_two[None, :], out_blocks, out_other
    )
    do_blocks = send_blocks(do_blocks)
    gain_two_other = cross(gain_two_part[half:])
    do_blocks, branch, gain_two_other, y_blocks, y_early = barrier(
        (do_blocks, branch, gain_two_other, y_blocks, y_early)
    )
    branch_blocks = spread(branch)
    qkv_grad = attend_back(
        me_array, query, log_total, key_pad, value_pad, cosine, sine, do_blocks, group
    )
    qkv_grad, sums_one = barrier((qkv_grad, sums_one))
    qkv_other = cross(qkv_grad)
    normed_part = input_grad(qkv_grad, *qkv, size)
    branch_blocks, normed_part = barrier((branch_blocks, normed_part))
    arrived = send_blocks(normed_part)
    branch_other = other_half(branch_blocks)
    tokens_other, attended_other = early
    grads, gain_parts = attn_grads(
        chips,
        tokens_one,
        branch_blocks,
        (qkv_grad, attended),
        (tokens_other, branch_other, qkv_other, attended_other),
        qkv[0],
        gain_one[:half, None],
        (gain_two_part[:half] + gain_two_other)[:, None],
    )
    grads, early = barrier((grads, arrived[1:3]))
    arrived[1:3] = early
    attn_sums = scatter(grads)
    gain_sums = add_up(line_parts(gain_parts[:, :, :2]))
    arrived, gain_sums, y_blocks, sums_two = barrier((arrived, gain_sums, y_blocks, sums_two))
    y_late = [swap(y_blocks[step], step) for step in range(3, size)]
    gain_sums = own_part(gain_sums)
    (grad_in,) = row_call(
        functools.partial(input_back_kernel, chips=chips),
        [jnp.float32],
        [*arrived, residual, middle_grad, gain_one[None, :]],
        core,
    )
    shares = [share.astype(jnp.float32) for share in (sums_one, sums_two)]
    grad_gate = jnp.concatenate([h[:, :units] for h in shares], axis=1)
    grad_up = jnp.concatenate([h[:, units : 2 * units] for h in shares], axis=1)
    grad_down = jnp.concatenate([h[:, 2 * units :].T for h in shares], axis=0)
    y_late, grad_in, gain_sums, grad_gate, grad_up, grad_down = barrier(
        (y_late, grad_in, gain_sums, grad_gate, grad_up, grad_down)
    )
    (out,) = row_call(
        functools.partial(output_kernel, chips=chips),
        [jnp.bfloat16],
        [y_blocks[0], *y_early, *y_late, middle],
        core,
    )
    out, attn_sums = barrier((out, attn_sums))
    attn_sums = attn_sums.astype(jnp.float32)
    return (
        out,
        grad_in,
        gain_sums[:, 0],
        attn_sums[:, :q_width],
        attn_sums[:, q_width : q_width + kv_width],
        attn_sums[:, q_width + kv_width : qkv_width],
        attn_sums[:, qkv_width:].T,
        gain_sums[:, 1],
        grad_gate,
        grad_up,
        grad_down,
    )


def solution(mesh):
    return jax.shard_map(
        per_device,
        mesh=mesh,
        in_specs=(
            P(("dp", "tensor"), None),
            P("dp"),
            P("dp", "tensor"),
            P("dp", "tensor"),
            P("dp", "tensor"),
            P("tensor", "dp"),
            P("dp"),
            P("dp", "tensor"),
            P("dp", "tensor"),
            P("tensor", "dp"),
            P("dp"),
            P(("dp", "tensor"), None),
        ),
        out_specs=(
            P(("dp", "tensor"), None),
            P(("dp", "tensor"), None),
            P(("dp", "tensor")),
            P("dp", "tensor"),
            P("dp", "tensor"),
            P("dp", "tensor"),
            P("tensor", "dp"),
            P(("dp", "tensor")),
            P("dp", "tensor"),
            P("dp", "tensor"),
            P("tensor", "dp"),
        ),
        check_vma=False,
    )
```

```python
import functools
import math

import jax
import jax.numpy as jnp
from jax import lax
from jax.experimental import pallas as pl
from jax.experimental.pallas import tpu as pltpu
from jax.sharding import PartitionSpec as P

HEAD_DIM = 64
PAIR = 2 * HEAD_DIM
SEQ_LEN = 1024


EPS = 1e-05
ROPE_BASE = 500000.0
SCALE = 1.0 / math.sqrt(HEAD_DIM)
PARAMS = pltpu.CompilerParams(vmem_limit_bytes=58 * 2**20)
ONCE = pl.Buffered(1)

barrier = lax.optimization_barrier


def hint(flops):
    return pl.CostEstimate(flops=flops, bytes_accessed=0, transcendentals=0)


def rms_scale(values):
    return lax.rsqrt(jnp.mean(values * values, axis=-1, keepdims=True) + EPS)


def norm_back(grad, values, scale, gain):
    inner = grad * gain
    cubed = scale * scale * scale
    result = scale * inner - values * cubed * jnp.mean(inner * values, axis=-1, keepdims=True)
    return (result, jnp.sum(grad * values * scale, axis=0))


def mm(left, right):
    return jnp.dot(left, right, preferred_element_type=jnp.float32)


def mm_nt(left, right):
    return lax.dot_general(left, right, (((1,), (1,)), ((), ())), preferred_element_type=jnp.float32)


def mm_tn(left, right):
    return lax.dot_general(left, right, (((0,), (0,)), ((), ())), preferred_element_type=jnp.float32)


def lane_index(rows):
    return lax.broadcasted_iota(jnp.int32, (rows, PAIR), 1)


def turn(pair, cosine, sine):
    lower = lane_index(pair.shape[0]) % HEAD_DIM < HEAD_DIM // 2
    other = jnp.where(
        lower, pltpu.roll(pair, PAIR - HEAD_DIM // 2, 1), pltpu.roll(pair, HEAD_DIM // 2, 1)
    )
    return pair * cosine + other * sine


def project_kernel(place_ref, *refs, size, q_width, kv_width):
    x_refs = refs[:size]
    go_ref, gx_ref, qo_ref, qx_ref, kvo_ref, kvx_ref, cos_ref, sin_ref = refs[size:-5]
    n_ref, q_ref, k_ref, v_ref, gain_ref = refs[-5:]
    rows = q_ref.shape[0]
    half = qo_ref.shape[0]

    @pl.when(pl.program_id(0) == 0)
    def _():
        gain_ref[:, :half] = go_ref[...].astype(jnp.float32).T[:1, :]
        gain_ref[:, half:] = gx_ref[...].astype(jnp.float32).T[:1, :]

    def one(x_ref):
        x = x_ref[...].astype(jnp.float32)
        normed = (x * rms_scale(x) * gain_ref[...]).astype(jnp.bfloat16)
        n_ref[...] = normed
        cosine, sine = cos_ref[...], sin_ref[...]
        own, other = normed[:, :half], normed[:, half:]
        lin = mm(own, qo_ref[...]) + mm(other, qx_ref[...])
        for low in range(0, q_width, PAIR):
            query = turn(lin[:, low : low + PAIR], cosine, sine).astype(jnp.bfloat16)
            q_ref[:, low : low + PAIR] = query * jnp.bfloat16(SCALE)
        lin = mm(own, kvo_ref[...]) + mm(other, kvx_ref[...])
        first = lane_index(rows) < HEAD_DIM
        for ref, start, rotate in ((k_ref, 0, True), (v_ref, kv_width, False)):
            for head in range(kv_width // HEAD_DIM):
                low = start + head * HEAD_DIM
                block = lin[:, low // PAIR * PAIR : low // PAIR * PAIR + PAIR]
                if rotate:
                    block = turn(block, cosine, sine)
                moved = pltpu.roll(block, HEAD_DIM, 1)
                if low % PAIR:
                    block, moved = moved, block
                ref[head, 0] = jnp.where(first, block, 0.0).astype(jnp.bfloat16)
                ref[head, 1] = jnp.where(first, 0.0, moved).astype(jnp.bfloat16)

    for step in range(size):
        pl.when(pl.program_id(0) == step)(functools.partial(one, x_refs[step]))


class Columns:
    def __init__(self, q_width, kv_width):
        self.q_width, self.kv_width = q_width, kv_width
        self.kv_start, self.gain_start = 2 * q_width, 2 * q_width + 2 * kv_width

    def spec(self, part, rows, place=lambda *_: 0):
        width, start = {
            "q": (self.q_width, 0),
            "out": (self.q_width, self.q_width),
            "kv": (2 * self.kv_width, self.kv_start),
            "gain": (PAIR, self.gain_start),
        }[part]
        index = start // width
        mode = {"pipeline_mode": ONCE} if place() == 0 else {}
        return pl.BlockSpec((rows, width), lambda *grid: (place(*grid), index), **mode)


def project(me, blocks, own, other, cosine, sine, columns):
    size = len(blocks)
    rows, features = blocks[0].shape
    total = rows * size
    q_width, kv_width = columns.q_width, columns.kv_width
    key_heads = kv_width // HEAD_DIM
    width = q_width + 2 * kv_width
    half = features // 2
    fixed = lambda p, m: (0, 0)
    placed = lambda p, m: (jnp.bitwise_xor(p, m[0]), 0)
    padded = pl.BlockSpec(
        (key_heads, 2, rows, PAIR), lambda p, m: (0, 0, jnp.bitwise_xor(p, m[0]), 0)
    )
    spec = pltpu.PrefetchScalarGridSpec(
        num_scalar_prefetch=1,
        grid=(size,),
        in_specs=[pl.BlockSpec((rows, features), fixed, pipeline_mode=ONCE)] * size
        + [
            columns.spec("gain", half),
            columns.spec("gain", half),
            columns.spec("q", half),
            columns.spec("q", half),
            columns.spec("kv", half),
            columns.spec("kv", half),
            pl.BlockSpec((rows, PAIR), placed),
            pl.BlockSpec((rows, PAIR), placed),
        ],
        out_specs=[
            pl.BlockSpec((rows, features), lambda p, m: (p, 0)),
            pl.BlockSpec((rows, q_width), lambda p, m: (p, 0)),
            padded,
            padded,
        ],
        scratch_shapes=[pltpu.VMEM((1, features), jnp.float32)],
    )
    padded_shape = jax.ShapeDtypeStruct((key_heads, 2, total, PAIR), jnp.bfloat16)
    return pl.pallas_call(
        functools.partial(project_kernel, size=size, q_width=q_width, kv_width=kv_width),
        grid_spec=spec,
        out_shape=[
            jax.ShapeDtypeStruct((total, features), jnp.bfloat16),
            jax.ShapeDtypeStruct((total, q_width), jnp.bfloat16),
            padded_shape,
            padded_shape,
        ],
        compiler_params=PARAMS,
        cost_estimate=hint(2 * total * features * width // 16),
    )(me, *blocks, own, other, own, other, own, other, cosine, sine)


def attend_kernel(
    me_ref, q_ref, k_ref, v_ref, wo_ref, wx_ref, o_ref, l_ref, *refs, size, heads, group
):
    part_refs, vt_ref = refs[:size], refs[size]
    rows = q_ref.shape[0]
    half = wo_ref.shape[0]
    mine = jnp.bitwise_xor(me_ref[0], pl.program_id(0))
    key_place = lax.broadcasted_iota(jnp.int32, (rows, rows), 0)
    query_place = lax.broadcasted_iota(jnp.int32, (rows, rows), 1)

    @pl.when(pl.program_id(0) == 0)
    def _():
        for head in range(heads // group):
            for side in range(2):
                vt_ref[head, side] = v_ref[head, side].T

    def one(span):
        keys = span * rows
        for pair in range(heads // 2):
            head = 2 * pair // group
            lanes = slice(pair * PAIR, (pair + 1) * PAIR)
            query = q_ref[:, lanes]
            acc = None
            inverse = []
            for side in range(2):
                diag = mm_nt(k_ref[head, side, keys : keys + rows, :], query)
                diag = jnp.where(key_place <= query_place, diag, -1e9)
                top = jnp.max(diag, axis=0, keepdims=True)
                if span:
                    body = mm_nt(k_ref[head, side, :keys, :], query)
                    top = jnp.maximum(top, jnp.max(body, axis=0, keepdims=True))
                diag = jnp.exp(diag - top)
                total = jnp.sum(diag, axis=0, keepdims=True)
                part = mm(vt_ref[head, side, :, keys : keys + rows], diag.astype(jnp.bfloat16))
                if span:
                    body = jnp.exp(body - top)
                    total = total + jnp.sum(body, axis=0, keepdims=True)
                    part = part + mm(vt_ref[head, side, :, :keys], body.astype(jnp.bfloat16))
                acc = part if acc is None else acc + part
                inverse.append(jnp.broadcast_to(1.0 / total, (HEAD_DIM, rows)))
                l_ref[2 * pair + side : 2 * pair + side + 1, :] = top + jnp.log(total)
            acc = acc * jnp.concatenate(inverse, axis=0)
            o_ref[:, lanes] = acc.T.astype(jnp.bfloat16)

    for span in range(size):
        pl.when(mine == span)(functools.partial(one, span))

    def project_out(ref):
        ref[:, :half] = mm_nt(o_ref[...], wo_ref[...]).astype(jnp.bfloat16)
        ref[:, half:] = mm_nt(o_ref[...], wx_ref[...]).astype(jnp.bfloat16)

    for step in range(size):
        pl.when(pl.program_id(0) == step)(functools.partial(project_out, part_refs[step]))


def attend(me, query, key_pad, value_pad, own, other, columns, size, group):
    total, width = query.shape
    features = 2 * own.shape[0]
    rows, heads = total // size, width // HEAD_DIM
    whole = pl.BlockSpec(key_pad.shape, lambda p, m: (0, 0, 0, 0), pipeline_mode=ONCE)
    spec = pltpu.PrefetchScalarGridSpec(
        num_scalar_prefetch=1,
        grid=(size,),
        in_specs=[pl.BlockSpec((rows, width), lambda p, m: (p, 0)), whole, whole]
        + [columns.spec("out", features // 2)] * 2,
        out_specs=[
            pl.BlockSpec((rows, width), lambda p, m: (p, 0)),
            pl.BlockSpec((heads, rows), lambda p, m: (0, p)),
        ]
        + [pl.BlockSpec((rows, features), lambda p, m: (0, 0))] * size,
        scratch_shapes=[pltpu.VMEM((heads // group, 2, PAIR, total), jnp.bfloat16)],
    )
    return pl.pallas_call(
        functools.partial(attend_kernel, size=size, heads=heads, group=group),
        grid_spec=spec,
        out_shape=[
            jax.ShapeDtypeStruct((total, width), jnp.bfloat16),
            jax.ShapeDtypeStruct((heads, total), jnp.float32),
        ]
        + [jax.ShapeDtypeStruct((rows, features), jnp.bfloat16)] * size,
        compiler_params=PARAMS,
        cost_estimate=hint(8 * heads * total * total * HEAD_DIM // 16),
    )(me, query, key_pad, value_pad, own, other)


def attend_back_kernel(
    me_ref, q_ref, l_ref, k_ref, v_ref, cos_ref, sin_ref, *refs, size, heads, group
):
    do_refs = refs[:size]
    out_ref, dk_ref, dv_ref, kt_ref, do_ref = refs[size:]
    rows = q_ref.shape[0]
    key_heads = heads // group
    step = pl.program_id(0)
    me = me_ref[0]
    mine = jnp.bitwise_xor(me, step)
    key_place = lax.broadcasted_iota(jnp.int32, (rows, rows), 0)
    query_place = lax.broadcasted_iota(jnp.int32, (rows, rows), 1)

    def rows_of(block):
        return pl.ds(pl.multiple_of(block * rows, rows), rows)

    @pl.when(step == 0)
    def _():
        dk_ref[...] = jnp.zeros_like(dk_ref)
        dv_ref[...] = jnp.zeros_like(dv_ref)
        for head in range(key_heads):
            for side in range(2):
                kt_ref[head, side] = k_ref[head, side].T

    def fetch(ref):
        do_ref[...] = ref[...]

    for block in range(size):
        pl.when(step == block)(functools.partial(fetch, do_refs[block]))

    def one(span):
        keys = span * rows
        parts = [(keys, keys + rows, True)] + ([(0, keys, False)] if span else [])
        cosine, sine = cos_ref[keys : keys + rows, :], sin_ref[keys : keys + rows, :]
        for pair in range(heads // 2):
            head = 2 * pair // group
            lanes = slice(pair * PAIR, (pair + 1) * PAIR)
            query, grad = q_ref[:, lanes], do_ref[:, lanes]
            acc = None
            for side in range(2):
                log_total = l_ref[2 * pair + side : 2 * pair + side + 1, :]
                inner = None
                kept = []
                for low, high, diagonal in parts:
                    probs = mm_nt(k_ref[head, side, low:high, :], query)
                    probs = jnp.exp(probs - log_total)
                    if diagonal:
                        probs = jnp.where(key_place <= query_place, probs, 0.0)
                    prob_grad = mm_nt(v_ref[head, side, low:high, :], grad)
                    dv_ref[head, side, low:high, :] += mm(probs.astype(jnp.bfloat16), grad)
                    term = jnp.sum(probs * prob_grad, axis=0, keepdims=True)
                    inner = term if inner is None else inner + term
                    kept.append((low, high, probs, prob_grad))
                for low, high, probs, prob_grad in kept:
                    score_grad = (probs * (prob_grad - inner)).astype(jnp.bfloat16)
                    dk_ref[head, side, low:high, :] += mm(score_grad, query)
                    part = mm(kt_ref[head, side, :, low:high], score_grad)
                    acc = part if acc is None else acc + part
            turned = turn(acc.T * SCALE, cosine, -sine)
            out_ref[rows_of(step), lanes] = turned.astype(jnp.bfloat16)

    for span in range(size):
        pl.when(mine == span)(functools.partial(one, span))

    @pl.when(step == size - 1)
    def _():
        first = lane_index(rows) < HEAD_DIM
        wanted = [(dk_ref, head, True) for head in range(key_heads)]
        wanted += [(dv_ref, head, False) for head in range(key_heads)]
        for span in range(size):
            place = slice(span * rows, (span + 1) * rows)
            cosine, sine = cos_ref[place, :], sin_ref[place, :]
            for block in range(len(wanted) // 2):
                halves, rotate = [], []
                for half in range(2):
                    ref, head, is_key = wanted[2 * block + half]
                    low, high = ref[head, 0, place, :], ref[head, 1, place, :]
                    if half:
                        halves.append(pltpu.roll(low, HEAD_DIM, 1) + high)
                    else:
                        halves.append(low + pltpu.roll(high, HEAD_DIM, 1))
                    rotate.append(is_key)
                value = jnp.where(first, halves[0], halves[1])
                if rotate[0] and rotate[1]:
                    value = turn(value, cosine, -sine)
                elif rotate[0]:
                    value = jnp.where(first, turn(value, cosine, -sine), value)
                start = heads * HEAD_DIM + block * PAIR
                target = rows_of(jnp.bitwise_xor(me, span))
                out_ref[target, start : start + PAIR] = value.astype(jnp.bfloat16)


def attend_back(
    me, query, log_total, key_pad, value_pad, cosine, sine, attended_grad, group
):
    total, width = query.shape
    size = len(attended_grad)
    rows, heads = total // size, width // HEAD_DIM
    key_heads = heads // group
    out_width = width + 2 * key_heads * HEAD_DIM
    whole = pl.BlockSpec(key_pad.shape, lambda p, m: (0, 0, 0, 0), pipeline_mode=ONCE)
    table = pl.BlockSpec((total, PAIR), lambda p, m: (0, 0), pipeline_mode=ONCE)
    spec = pltpu.PrefetchScalarGridSpec(
        num_scalar_prefetch=1,
        grid=(size,),
        in_specs=[
            pl.BlockSpec((rows, width), lambda p, m: (p, 0)),
            pl.BlockSpec((heads, rows), lambda p, m: (0, p)),
            whole,
            whole,
            table,
            table,
        ]
        + [pl.BlockSpec((rows, width), lambda p, m: (0, 0), pipeline_mode=ONCE)] * size,
        out_specs=pl.BlockSpec((total, out_width), lambda p, m: (0, 0)),
        scratch_shapes=[
            pltpu.VMEM(key_pad.shape, jnp.float32),
            pltpu.VMEM(key_pad.shape, jnp.float32),
            pltpu.VMEM((key_heads, 2, PAIR, total), jnp.bfloat16),
            pltpu.VMEM((rows, width), jnp.bfloat16),
        ],
    )
    return pl.pallas_call(
        functools.partial(attend_back_kernel, size=size, heads=heads, group=group),
        grid_spec=spec,
        out_shape=jax.ShapeDtypeStruct((total, out_width), jnp.bfloat16),
        compiler_params=PARAMS,
        cost_estimate=hint(20 * heads * total * total * HEAD_DIM),
    )(me, query, log_total, key_pad, value_pad, cosine, sine, *attended_grad)


def mlp_kernel(*refs, size, adds):
    n_refs, e_refs = refs[:size], refs[size : 2 * size]
    gate_o, up_o, down_o, gate_x, up_x, down_x = refs[2 * size : 2 * size + 6]
    y_ref, n_ref, e_ref = refs[-3:]
    dn_refs = refs[-3 - size if adds else -4 : -3]
    dg_ref, du_ref, h_ref = refs[-6 - size if adds else -7 :][:3]
    half = gate_o.shape[0]

    def fetch(step):
        n_ref[...] = n_refs[step][...]
        e_ref[...] = e_refs[step][...]

    for step in range(size):
        pl.when(pl.program_id(0) == step)(functools.partial(fetch, step))
    gate = mm(n_ref[:, :half], gate_o[...]) + mm(n_ref[:, half:], gate_x[...])
    up = mm(n_ref[:, :half], up_o[...]) + mm(n_ref[:, half:], up_x[...])
    grad = mm(e_ref[:, :half], down_o[...]) + mm(e_ref[:, half:], down_x[...])
    sigma = jax.nn.sigmoid(gate)
    silu = gate * sigma
    hidden = (silu * up).astype(jnp.bfloat16)
    gate_grad = (grad * up * sigma * (1.0 + gate * (1.0 - sigma))).astype(jnp.bfloat16)
    up_grad = (grad * silu).astype(jnp.bfloat16)
    dg_ref[...] = gate_grad
    du_ref[...] = up_grad
    h_ref[...] = hidden
    for part, gate_w, up_w, down_w in ((0, gate_o, up_o, down_o), (1, gate_x, up_x, down_x)):
        lanes = slice(part * half, (part + 1) * half)
        dn = mm_nt(gate_grad, gate_w[...]) + mm_nt(up_grad, up_w[...])
        y = mm_nt(hidden, down_w[...])
        if adds:
            dn = dn + refs[2 * size + 6][:, lanes].astype(jnp.float32)
            y = y + refs[2 * size + 7][:, lanes].astype(jnp.float32)
        y_ref[:, lanes] = y.astype(jnp.bfloat16)
        dn = dn.astype(jnp.bfloat16)

        def store(ref):
            ref[:, lanes] = dn

        if adds:
            for step in range(size):
                pl.when(pl.program_id(0) == step)(functools.partial(store, dn_refs[step]))
        else:
            store(dn_refs[0])


def mlp(tokens, cot, own, other, earlier):
    size = len(tokens)
    rows, features = tokens[0].shape
    half, units = own.shape[0], own.shape[1] // 3
    total = rows * size
    fixed = lambda p: (0, 0)
    moving = lambda p: (p, 0)
    wide = pl.BlockSpec((rows, features), moving)
    sums = jax.ShapeDtypeStruct((total, features), jnp.bfloat16)
    dn_specs, dn_shapes = [wide], [sums]
    if earlier:
        dn_specs = [pl.BlockSpec((rows, features), fixed)] * size
        dn_shapes = [jax.ShapeDtypeStruct((rows, features), jnp.bfloat16)] * size
    block = pl.BlockSpec((rows, features), fixed, pipeline_mode=ONCE)
    thirds = [
        pl.BlockSpec((half, units), lambda p, t=t: (0, t), pipeline_mode=ONCE) for t in range(3)
    ]
    return pl.pallas_call(
        functools.partial(mlp_kernel, size=size, adds=bool(earlier)),
        grid=(size,),
        in_specs=[block] * (2 * size)
        + thirds * 2
        + [wide] * len(earlier),
        out_specs=[pl.BlockSpec((rows, units), moving)] * 3 + dn_specs + [wide],
        out_shape=[jax.ShapeDtypeStruct((total, units), jnp.bfloat16)] * 3 + dn_shapes + [sums],
        scratch_shapes=[pltpu.VMEM((rows, features), jnp.bfloat16)] * 2,
        compiler_params=PARAMS,
        cost_estimate=hint(12 * total * features * units),
    )(*tokens, *cot, own, own, own, other, other, other, *earlier)


def add_refs(refs):
    total = refs[0][...].astype(jnp.float32)
    for ref in refs[1:]:
        total = total + ref[...].astype(jnp.float32)
    return total


def store_by_device(out_ref, values, core, chips):
    width = values.shape[1] // (2 * chips)
    for chip in range(chips):
        own = values[:, chip * width : (chip + 1) * width]
        other = values[:, (chips + chip) * width : (chips + chip + 1) * width]
        low = 2 * chip * width
        out_ref[:, low : low + width] = jnp.where(core == 0, own, other)
        out_ref[:, low + width : low + 2 * width] = jnp.where(core == 0, other, own)


def middle_kernel(*refs):
    x_ref, gain_ref, middle_ref, normed_ref = refs[-4:]
    values = x_ref[...].astype(jnp.float32) + add_refs(refs[:-4])
    middle_ref[...] = values
    normed_ref[...] = (values * rms_scale(values) * gain_ref[...]).astype(jnp.bfloat16)


def input_back_kernel(core_ref, *refs, chips):
    x_ref, before_ref, gain_ref, out_ref = refs[-4:]
    values = x_ref[...].astype(jnp.float32)
    inner = add_refs(refs[:-4]) * gain_ref[...]
    scale = rms_scale(values)
    mean = jnp.mean(inner * values, axis=-1, keepdims=True)
    result = before_ref[...] + scale * inner - values * (scale * scale * scale) * mean
    store_by_device(out_ref, result, core_ref[0], chips)


def output_kernel(core_ref, *refs, chips):
    middle_ref, out_ref = refs[-2:]
    values = middle_ref[...] + add_refs(refs[:-2])
    store_by_device(out_ref, values.astype(jnp.bfloat16), core_ref[0], chips)


def row_call(body, dtypes, arrays, core=None):
    rows, features = arrays[0].shape
    steps = 2
    wide = pl.BlockSpec((rows // steps, features), lambda i, *_: (i, 0))
    row = pl.BlockSpec((1, features), lambda i, *_: (0, 0))
    scalars = [] if core is None else [jnp.full((1,), core, jnp.int32)]
    return pl.pallas_call(
        body,
        grid_spec=pltpu.PrefetchScalarGridSpec(
            num_scalar_prefetch=len(scalars),
            grid=(steps,),
            in_specs=[row if array.shape[0] == 1 else wide for array in arrays],
            out_specs=[wide] * len(dtypes),
        ),
        out_shape=[jax.ShapeDtypeStruct((rows, features), dtype) for dtype in dtypes],
        compiler_params=PARAMS,
        cost_estimate=hint(0),
    )(*scalars, *arrays)


def middle_back_kernel(*refs, size):
    n_refs, refs = refs[:size], refs[size:]
    x_ref, e_ref, gain_ref, refs = refs[0], refs[1], refs[2], refs[3:]
    own_refs, other_refs, refs = refs[:size], refs[size : 2 * size], refs[2 * size :]
    grad_ref, branch_ref, part_ref, do_refs = refs[0], refs[1], refs[2], refs[3:]
    half = own_refs[0].shape[0]
    grad = add_refs(n_refs)
    values = x_ref[...]
    scale = rms_scale(values)
    result, part = norm_back(grad, values, scale, gain_ref[...])

    @pl.when(pl.program_id(0) == 0)
    def _():
        part_ref[...] = jnp.zeros_like(part_ref)

    part_ref[...] += part[None, :]
    result = result + e_ref[...].astype(jnp.float32)
    grad_ref[...] = result
    branch = result.astype(jnp.bfloat16)
    branch_ref[...] = branch
    for own, other, do_ref in zip(own_refs, other_refs, do_refs):
        do = mm(branch[:, :half], own[...]) + mm(branch[:, half:], other[...])
        do_ref[...] = do.astype(jnp.bfloat16)


def middle_back(arrived, middle, cot, gain, own, other):
    size = len(arrived)
    rows, features = middle.shape
    width = own[0].shape[1]
    steps = 2
    wide = pl.BlockSpec((rows // steps, features), lambda i: (i, 0))
    narrow = pl.BlockSpec((rows // steps, width), lambda i: (i, 0))
    row = pl.BlockSpec((1, features), lambda i: (0, 0))
    weight = pl.BlockSpec((features // 2, width), lambda i: (0, 0), pipeline_mode=ONCE)
    grad, branch, part, *do = pl.pallas_call(
        functools.partial(middle_back_kernel, size=size),
        grid=(steps,),
        in_specs=[wide] * size + [wide, wide, row] + [weight] * (2 * size),
        out_specs=[wide, wide, row] + [narrow] * size,
        out_shape=[
            jax.ShapeDtypeStruct((rows, features), jnp.float32),
            jax.ShapeDtypeStruct((rows, features), jnp.bfloat16),
            jax.ShapeDtypeStruct((1, features), jnp.float32),
        ]
        + [jax.ShapeDtypeStruct((rows, width), jnp.bfloat16)] * size,
        compiler_params=PARAMS,
        cost_estimate=hint(2 * rows * features * width * size),
    )(*arrived, middle, cot, gain, *own, *other)
    return grad, branch, part[0], do


def column_grad(blocks, other, mine, theirs):
    rows = blocks[0].shape[0]
    total = mm_tn(other[...], theirs[...])
    for index, block in enumerate(blocks):
        total = total + mm_tn(block[...], mine[index * rows : (index + 1) * rows, :])
    return total


def grad_kernel(*refs, size):
    n_refs, e_refs = refs[:size], refs[size : 2 * size]
    n_other, e_other = refs[2 * size : 2 * size + 2]
    acts, out_ref = refs[2 * size + 2 : -1], refs[-1]
    units = acts[0].shape[1]
    for third in range(3):
        blocks, other = (e_refs, e_other) if third == 2 else (n_refs, n_other)
        grad = column_grad(blocks, other, acts[third], acts[third + 3])
        out_ref[0, :, third * units : (third + 1) * units] = grad.astype(jnp.bfloat16)


def mlp_grads(chips, tokens, cot, tokens_other, cot_other, mine, theirs):
    size = len(tokens)
    rows, features = tokens[0].shape
    total, units = mine[0].shape
    depth = features // (2 * chips)
    column = pl.BlockSpec((rows, depth), lambda b: (0, b))
    long = pl.BlockSpec((total, depth), lambda b: (0, b))
    fixed = pl.BlockSpec((total, units), lambda b: (0, 0), pipeline_mode=ONCE)
    return pl.pallas_call(
        functools.partial(grad_kernel, size=size),
        grid=(chips,),
        in_specs=[column] * (2 * size) + [long, long] + [fixed] * 6,
        out_specs=pl.BlockSpec((1, depth, 3 * units), lambda b: (b, 0, 0)),
        out_shape=jax.ShapeDtypeStruct((chips, depth, 3 * units), jnp.bfloat16),
        compiler_params=PARAMS,
        cost_estimate=hint(6 * total * features * units),
    )(*tokens, *cot, tokens_other, cot_other, *mine, *theirs)


def attn_grad_kernel(*refs, size):
    e_refs = refs[2 : 2 + size]
    n_ref, n_other = refs[:2]
    e_other, d_ref, d_other, o_ref, o_other, q_ref, kv_ref, g1_ref, g2_ref = refs[2 + size : -2]
    out_ref, gain_ref = refs[-2:]
    width, out_width = d_ref.shape[1], o_ref.shape[1]
    grad = column_grad([n_ref], n_other, d_ref, d_other)
    out_ref[0, :, :width] = grad.astype(jnp.bfloat16)
    out_grad = column_grad(e_refs, e_other, o_ref, o_other)
    out_ref[0, :, width : width + out_width] = out_grad.astype(jnp.bfloat16)
    cut = q_ref.shape[1]
    first = jnp.sum(grad[:, :cut] * q_ref[...].astype(jnp.float32), axis=1, keepdims=True)
    first += jnp.sum(grad[:, cut:] * kv_ref[...].astype(jnp.float32), axis=1, keepdims=True)
    first = first / g1_ref[:, :1].astype(jnp.float32)
    lane = lane_index(grad.shape[0])
    gain_ref[0] = jnp.where(lane == 0, first, g2_ref[...])


def attn_grads(chips, tokens, branch, mine, theirs, weights, columns, gain_two_part):
    size = len(branch)
    qkv_grad, attended = mine
    tokens_other, branch_other, qkv_other, attended_other = theirs
    total, features = tokens.shape
    rows = total // size
    width, out_width = qkv_grad.shape[1], attended.shape[1]
    depth = features // (2 * chips)
    column = lambda b: (0, b)
    row = lambda b: (b, 0)
    long = pl.BlockSpec((total, depth), column)
    fixed = lambda array: pl.BlockSpec(array.shape, lambda b: (0, 0), pipeline_mode=ONCE)
    place = lambda b: (b, 0, 0)
    return pl.pallas_call(
        functools.partial(attn_grad_kernel, size=size),
        grid=(chips,),
        in_specs=[long, long]
        + [pl.BlockSpec((rows, depth), column)] * size
        + [long]
        + [fixed(qkv_grad)] * 2
        + [fixed(attended)] * 2
        + [
            columns.spec("q", depth, lambda b=None: b),
            columns.spec("kv", depth, lambda b=None: b),
            columns.spec("gain", depth, lambda b=None: b),
            pl.BlockSpec((depth, 1), row),
        ],
        out_specs=[
            pl.BlockSpec((1, depth, width + out_width), place),
            pl.BlockSpec((1, depth, PAIR), place),
        ],
        out_shape=[
            jax.ShapeDtypeStruct((chips, depth, width + out_width), jnp.bfloat16),
            jax.ShapeDtypeStruct((chips, depth, PAIR), jnp.float32),
        ],
        compiler_params=PARAMS,
        cost_estimate=hint(2 * total * features * (width + out_width)),
    )(
        tokens,
        tokens_other,
        *branch,
        branch_other,
        qkv_grad,
        qkv_other,
        attended,
        attended_other,
        weights,
        weights,
        weights,
        gain_two_part,
    )


def input_grad_kernel(d_ref, qo_ref, qx_ref, kvo_ref, kvx_ref, *out_refs):
    half, cut = qo_ref.shape

    def one(ref):
        query, rest = d_ref[:, :cut], d_ref[:, cut:]
        own = mm_nt(query, qo_ref[...]) + mm_nt(rest, kvo_ref[...])
        other = mm_nt(query, qx_ref[...]) + mm_nt(rest, kvx_ref[...])
        ref[:, :half] = own.astype(jnp.bfloat16)
        ref[:, half:] = other.astype(jnp.bfloat16)

    for step, ref in enumerate(out_refs):
        pl.when(pl.program_id(0) == step)(functools.partial(one, ref))


def input_grad(qkv_grad, own, other, columns, size):
    total, width = qkv_grad.shape
    features = 2 * own.shape[0]
    rows = total // size
    fixed = lambda i: (0, 0)
    weights = [columns.spec(part, own.shape[0]) for part in ("q", "q", "kv", "kv")]
    return pl.pallas_call(
        input_grad_kernel,
        grid=(size,),
        in_specs=[pl.BlockSpec((rows, width), lambda i: (i, 0))] + weights,
        out_specs=[pl.BlockSpec((rows, features), fixed)] * size,
        out_shape=[jax.ShapeDtypeStruct((rows, features), jnp.bfloat16)] * size,
        compiler_params=PARAMS,
        cost_estimate=hint(2 * total * features * width),
    )(qkv_grad, own, other, own, other)


def swap(values, step):
    size = lax.axis_size("tensor")
    return lax.ppermute(values, "tensor", [(i, i ^ step) for i in range(size)])


def spread(values):
    return [values] + [swap(values, step) for step in range(1, lax.axis_size("tensor"))]


def send_blocks(blocks):
    return [blocks[0]] + [swap(block, step + 1) for step, block in enumerate(blocks[1:])]


def add_up(blocks):
    total = blocks[0].astype(jnp.float32)
    for block in blocks[1:]:
        total = total + block.astype(jnp.float32)
    return total


def cross(values):
    count = lax.axis_size("dp")
    return lax.ppermute(values, "dp", [(i, i ^ 1) for i in range(count)])


def tables(positions):
    freqs = ROPE_BASE ** (-jnp.arange(0, HEAD_DIM, 2).astype(jnp.float32) / HEAD_DIM)
    angles = positions.astype(jnp.float32)[:, None] * freqs[None, :]
    cosine, sine = jnp.cos(angles), jnp.sin(angles)
    return (
        jnp.concatenate([cosine] * 4, axis=1),
        jnp.concatenate([-sine, sine, -sine, sine], axis=1),
    )


def chip_lines():
    count = lax.axis_size("dp")
    return [list(range(core, count, 2)) for core in range(2)]


def gather(values):
    return lax.all_gather(values, "dp", axis=0, tiled=True, axis_index_groups=chip_lines())


def scatter(values):
    total = lax.psum_scatter(
        values, "dp", scatter_dimension=0, tiled=True, axis_index_groups=chip_lines()
    )
    return total[0]


def along(values, step):
    count = lax.axis_size("dp")
    return lax.ppermute(values, "dp", [(i, (i + 2 * step) % count) for i in range(count)])


def line_order(blocks):
    chips = len(blocks)
    chip = lax.axis_index("dp") // 2
    placed = jnp.zeros((chips,) + blocks[0].shape, blocks[0].dtype)
    for step, block in enumerate(blocks):
        placed = lax.dynamic_update_index_in_dim(placed, block, (chip - step) % chips, 0)
    return placed.reshape((-1,) + blocks[0].shape[1:])


def line_parts(parts):
    chips = lax.axis_size("dp") // 2
    chip = lax.axis_index("dp") // 2
    blocks = [lax.dynamic_index_in_dim(parts, chip, 0, keepdims=False)]
    for step in range(1, chips):
        sent = lax.dynamic_index_in_dim(parts, (chip + step) % chips, 0, keepdims=False)
        blocks.append(along(sent, step))
    return blocks


def own_part(values):
    size = lax.axis_size("tensor")
    me = lax.axis_index("tensor")
    blocks = values.reshape((size, -1) + values.shape[1:])
    own = lax.dynamic_index_in_dim(blocks, me, 0, keepdims=False)
    for step in range(1, size):
        sent = lax.dynamic_index_in_dim(blocks, me ^ step, 0, keepdims=False)
        own = own + swap(sent, step)
    return own


def stack_kernel(*refs):
    rows = refs[0].shape[0]
    for index, ref in enumerate(refs[:-1]):
        refs[-1][index * rows : (index + 1) * rows, :] = ref[...]


def other_half(blocks):
    size = len(blocks)
    rows, features = blocks[0].shape
    shape = (size * rows, features // 2)
    halves = pl.pallas_call(
        stack_kernel,
        grid=(1,),
        in_specs=[pl.BlockSpec((rows, features // 2), lambda i: (0, 1))] * size,
        out_specs=pl.BlockSpec(shape, lambda i: (0, 0)),
        out_shape=jax.ShapeDtypeStruct(shape, blocks[0].dtype),
        compiler_params=PARAMS,
        cost_estimate=hint(0),
    )(*blocks)
    return cross(halves)


def feature_blocks(values):
    width = values.shape[-1] // lax.axis_size("dp")
    return [values[..., low : low + width] for low in range(0, values.shape[-1], width)]


def by_core(values, core):
    blocks = feature_blocks(values)
    pairs = list(zip(blocks[0::2], blocks[1::2]))
    own = [jnp.where(core == 0, even, odd) for even, odd in pairs]
    other = [jnp.where(core == 0, odd, even) for even, odd in pairs]
    return jnp.concatenate(own + other, axis=-1)


def per_device(
    hidden_in,
    gain_attn,
    w_query,
    w_key,
    w_value,
    w_out,
    gain_mlp,
    w_gate,
    w_up,
    w_down,
    positions,
    cotangent,
):
    size = lax.axis_size("tensor")
    chips = lax.axis_size("dp") // 2
    me = lax.axis_index("tensor")
    me_array = jnp.full((1,), me, jnp.int32)
    core = lax.axis_index("dp") % 2
    q_width, kv_width = w_query.shape[1], w_key.shape[1]
    qkv_width = q_width + 2 * kv_width
    group = q_width // kv_width
    units = w_down.shape[0] // 2
    half = hidden_in.shape[1] // 2

    columns = Columns(q_width, kv_width)
    gain_shard = jnp.pad(jnp.stack([gain_attn, gain_mlp], axis=1), ((0, 0), (0, PAIR - 2)))
    attn_shard = jnp.concatenate([w_query, w_out.T, w_key, w_value, gain_shard], axis=1)
    attn_shard, hidden_in = barrier((attn_shard, hidden_in))
    residual = by_core(hidden_in, core)
    early_in = [swap(residual, step) for step in range(1, 3)]
    ring = [attn_shard]
    for _ in range(2):
        ring.append(along(ring[-1], 1))
    early_in, ring, residual = barrier((early_in, ring, residual))
    blocks_in = [residual] + early_in + [swap(residual, step) for step in range(3, size)]
    while len(ring) < chips:
        ring.append(along(ring[-1], 1))
    cosine, sine = tables(positions)
    cotangent = by_core(cotangent, core)
    down_t = w_down.T
    shares = []
    for part in range(2):
        cut = slice(part * units, (part + 1) * units)
        shares.append(jnp.concatenate([w_gate[:, cut], w_up[:, cut], down_t[:, cut]], axis=1))
    shares, ring, blocks_in, cosine, sine, cotangent = barrier(
        (shares, ring, blocks_in, cosine, sine, cotangent)
    )
    attn_own = line_order(ring)
    mlp_own = [gather(share) for share in shares]
    cot_blocks = spread(cotangent)
    attn = (attn_own, cross(attn_own))

    tokens_one, query, key_pad, value_pad = project(
        me_array, blocks_in, *attn, cosine, sine, columns
    )
    attended, log_total, *parts = attend(
        me_array, query, key_pad, value_pad, *attn, columns, size, group
    )
    parts, cot_blocks, tokens_one, attended = barrier((parts, cot_blocks, tokens_one, attended))
    arrived = send_blocks(parts)
    cot_other = other_half(cot_blocks)
    early = (cross(tokens_one[:, half:]), cross(attended))
    arrived, cot_other, early = barrier((arrived, cot_other, early))
    gain_one, gain_two = [
        jnp.concatenate([w[:, columns.gain_start + index] for w in attn]).astype(jnp.float32)
        for index in range(2)
    ]
    out_t = [w[:, q_width : 2 * q_width] for w in attn]
    middle, normed_two = row_call(
        middle_kernel, [jnp.float32, jnp.bfloat16], [*arrived, residual, gain_two[None, :]]
    )
    normed_two, own_share = barrier((normed_two, mlp_own[0]))
    tokens_two = spread(normed_two)
    weights = (own_share, cross(own_share))
    tokens_two, weights, out_own = barrier((tokens_two, weights, out_t[0]))
    tokens_other = other_half(tokens_two)
    *acts, dn_part, y_part = mlp(tokens_two, cot_blocks, *weights, ())
    out_blocks = spread(out_own)
    acts, tokens_other = barrier((acts, tokens_other))
    acts_other = [cross(act) for act in acts]
    grads_one = mlp_grads(
        chips, tokens_two, cot_blocks, tokens_other, cot_other, acts, acts_other
    )
    grads_one, own_share = barrier((grads_one, mlp_own[1]))
    sums_one = scatter(grads_one)
    weights = (own_share, cross(own_share))
    *acts, y_part = mlp(tokens_two, cot_blocks, *weights, (dn_part, y_part))
    acts, dn_part = acts[:3], acts[3:]
    acts, dn_part, out_blocks = barrier((acts, dn_part, out_blocks))
    arrived = send_blocks(dn_part)
    out_other = [out_t[1]] + [cross(block) for block in out_blocks[1:]]
    acts_other = [cross(act) for act in acts]
    grads_two = mlp_grads(
        chips, tokens_two, cot_blocks, tokens_other, cot_other, acts, acts_other
    )
    grads_two, arrived, out_other, y_part = barrier((grads_two, arrived, out_other, y_part))
    y_blocks = list(y_part.reshape((size, -1) + y_part.shape[1:]))
    y_early = [swap(y_blocks[step], step) for step in range(1, 3)]
    sums_two = scatter(grads_two)
    middle_grad, branch, gain_two_part, do_blocks = middle_back(
        arrived, middle, cotangent, gain_two[None, :], out_blocks, out_other
    )
    do_blocks = send_blocks(do_blocks)
    gain_two_other = cross(gain_two_part[half:])
    do_blocks, branch, gain_two_other, y_blocks, y_early = barrier(
        (do_blocks, branch, gain_two_other, y_blocks, y_early)
    )
    branch_blocks = spread(branch)
    qkv_grad = attend_back(
        me_array, query, log_total, key_pad, value_pad, cosine, sine, do_blocks, group
    )
    qkv_grad, sums_one = barrier((qkv_grad, sums_one))
    qkv_other = cross(qkv_grad)
    normed_part = input_grad(qkv_grad, *attn, columns, size)
    branch_blocks, normed_part = barrier((branch_blocks, normed_part))
    arrived = send_blocks(normed_part)
    branch_other = other_half(branch_blocks)
    tokens_other, attended_other = early
    grads, gain_parts = attn_grads(
        chips,
        tokens_one,
        branch_blocks,
        (qkv_grad, attended),
        (tokens_other, branch_other, qkv_other, attended_other),
        attn_own,
        columns,
        (gain_two_part[:half] + gain_two_other)[:, None],
    )
    grads, early = barrier((grads, arrived[1:3]))
    arrived[1:3] = early
    attn_sums = scatter(grads)
    gain_sums = add_up(line_parts(gain_parts[:, :, :2]))
    arrived, gain_sums, y_blocks, sums_two = barrier((arrived, gain_sums, y_blocks, sums_two))
    y_late = [swap(y_blocks[step], step) for step in range(3, size)]
    gain_sums = own_part(gain_sums)
    (grad_in,) = row_call(
        functools.partial(input_back_kernel, chips=chips),
        [jnp.float32],
        [*arrived, residual, middle_grad, gain_one[None, :]],
        core,
    )
    shares = [share.astype(jnp.float32) for share in (sums_one, sums_two)]
    grad_gate = jnp.concatenate([h[:, :units] for h in shares], axis=1)
    grad_up = jnp.concatenate([h[:, units : 2 * units] for h in shares], axis=1)
    grad_down = jnp.concatenate([h[:, 2 * units :].T for h in shares], axis=0)
    y_late, grad_in, gain_sums, grad_gate, grad_up, grad_down = barrier(
        (y_late, grad_in, gain_sums, grad_gate, grad_up, grad_down)
    )
    (out,) = row_call(
        functools.partial(output_kernel, chips=chips),
        [jnp.bfloat16],
        [y_blocks[0], *y_early, *y_late, middle],
        core,
    )
    out, attn_sums = barrier((out, attn_sums))
    attn_sums = attn_sums.astype(jnp.float32)
    return (
        out,
        grad_in,
        gain_sums[:, 0],
        attn_sums[:, :q_width],
        attn_sums[:, q_width : q_width + kv_width],
        attn_sums[:, q_width + kv_width : qkv_width],
        attn_sums[:, qkv_width:].T,
        gain_sums[:, 1],
        grad_gate,
        grad_up,
        grad_down,
    )


def solution(mesh):
    return jax.shard_map(
        per_device,
        mesh=mesh,
        in_specs=(
            P(("dp", "tensor"), None),
            P("dp"),
            P("dp", "tensor"),
            P("dp", "tensor"),
            P("dp", "tensor"),
            P("tensor", "dp"),
            P("dp"),
            P("dp", "tensor"),
            P("dp", "tensor"),
            P("tensor", "dp"),
            P("dp"),
            P(("dp", "tensor"), None),
        ),
        out_specs=(
            P(("dp", "tensor"), None),
            P(("dp", "tensor"), None),
            P(("dp", "tensor")),
            P("dp", "tensor"),
            P("dp", "tensor"),
            P("dp", "tensor"),
            P("tensor", "dp"),
            P(("dp", "tensor")),
            P("dp", "tensor"),
            P("dp", "tensor"),
            P("tensor", "dp"),
        ),
        check_vma=False,
    )
```

```python
import functools
import math

import jax
import jax.numpy as jnp
from jax import lax
from jax.experimental import pallas as pl
from jax.experimental.pallas import tpu as pltpu
from jax.sharding import PartitionSpec as P

HEAD_DIM = 64
PAIR = 2 * HEAD_DIM
SEQ_LEN = 1024


EPS = 1e-05
ROPE_BASE = 500000.0
SCALE = 1.0 / math.sqrt(HEAD_DIM)
PARAMS = pltpu.CompilerParams(vmem_limit_bytes=58 * 2**20)
ONCE = pl.Buffered(1)

barrier = lax.optimization_barrier


def hint(flops):
    return pl.CostEstimate(flops=flops, bytes_accessed=0, transcendentals=0)


def rms_scale(values):
    return lax.rsqrt(jnp.mean(values * values, axis=-1, keepdims=True) + EPS)


def norm_back(grad, values, scale, gain):
    inner = grad * gain
    cubed = scale * scale * scale
    result = scale * inner - values * cubed * jnp.mean(inner * values, axis=-1, keepdims=True)
    return (result, jnp.sum(grad * values * scale, axis=0))


def mm(left, right):
    return jnp.dot(left, right, preferred_element_type=jnp.float32)


def mm_nt(left, right):
    return lax.dot_general(left, right, (((1,), (1,)), ((), ())), preferred_element_type=jnp.float32)


def mm_tn(left, right):
    return lax.dot_general(left, right, (((0,), (0,)), ((), ())), preferred_element_type=jnp.float32)


def lane_index(rows):
    return lax.broadcasted_iota(jnp.int32, (rows, PAIR), 1)


def turn(pair, cosine, sine):
    lower = lane_index(pair.shape[0]) % HEAD_DIM < HEAD_DIM // 2
    other = jnp.where(
        lower, pltpu.roll(pair, PAIR - HEAD_DIM // 2, 1), pltpu.roll(pair, HEAD_DIM // 2, 1)
    )
    return pair * cosine + other * sine


def project_kernel(place_ref, *refs, size, q_width, kv_width):
    x_refs = refs[:size]
    gain_ref, qo_ref, qx_ref, kvo_ref, kvx_ref, cos_ref, sin_ref = refs[size:-4]
    n_ref, q_ref, k_ref, v_ref = refs[-4:]
    rows = q_ref.shape[0]
    half = qo_ref.shape[0]

    def one(x_ref):
        x = x_ref[...].astype(jnp.float32)
        normed = (x * rms_scale(x) * gain_ref[...]).astype(jnp.bfloat16)
        n_ref[...] = normed
        cosine, sine = cos_ref[...], sin_ref[...]
        own, other = normed[:, :half], normed[:, half:]
        lin = mm(own, qo_ref[...]) + mm(other, qx_ref[...])
        for low in range(0, q_width, PAIR):
            query = turn(lin[:, low : low + PAIR], cosine, sine).astype(jnp.bfloat16)
            q_ref[:, low : low + PAIR] = query * jnp.bfloat16(SCALE)
        lin = mm(own, kvo_ref[...]) + mm(other, kvx_ref[...])
        first = lane_index(rows) < HEAD_DIM
        for ref, start, rotate in ((k_ref, 0, True), (v_ref, kv_width, False)):
            for head in range(kv_width // HEAD_DIM):
                low = start + head * HEAD_DIM
                block = lin[:, low // PAIR * PAIR : low // PAIR * PAIR + PAIR]
                if rotate:
                    block = turn(block, cosine, sine)
                moved = pltpu.roll(block, HEAD_DIM, 1)
                if low % PAIR:
                    block, moved = moved, block
                ref[head, 0] = jnp.where(first, block, 0.0).astype(jnp.bfloat16)
                ref[head, 1] = jnp.where(first, 0.0, moved).astype(jnp.bfloat16)

    for step in range(size):
        pl.when(pl.program_id(0) == step)(functools.partial(one, x_refs[step]))


class Columns:
    def __init__(self, q_width, kv_width):
        self.q_width, self.kv_width = q_width, kv_width

    def spec(self, part, rows, place=lambda *_: 0):
        width, start = {
            "q": (self.q_width, 0),
            "out": (self.q_width, self.q_width),
            "kv": (2 * self.kv_width, 2 * self.q_width),
        }[part]
        index = start // width
        mode = {"pipeline_mode": ONCE} if place() == 0 else {}
        return pl.BlockSpec((rows, width), lambda *grid: (place(*grid), index), **mode)


def project(me, blocks, gain, own, other, cosine, sine, columns):
    size = len(blocks)
    rows, features = blocks[0].shape
    total = rows * size
    q_width, kv_width = columns.q_width, columns.kv_width
    key_heads = kv_width // HEAD_DIM
    width = q_width + 2 * kv_width
    half = features // 2
    fixed = lambda p, m: (0, 0)
    placed = lambda p, m: (jnp.bitwise_xor(p, m[0]), 0)
    padded = pl.BlockSpec(
        (key_heads, 2, rows, PAIR), lambda p, m: (0, 0, jnp.bitwise_xor(p, m[0]), 0)
    )
    spec = pltpu.PrefetchScalarGridSpec(
        num_scalar_prefetch=1,
        grid=(size,),
        in_specs=[pl.BlockSpec((rows, features), fixed, pipeline_mode=ONCE)] * size
        + [
            pl.BlockSpec((1, features), fixed),
            columns.spec("q", half),
            columns.spec("q", half),
            columns.spec("kv", half),
            columns.spec("kv", half),
            pl.BlockSpec((rows, PAIR), placed),
            pl.BlockSpec((rows, PAIR), placed),
        ],
        out_specs=[
            pl.BlockSpec((rows, features), lambda p, m: (p, 0)),
            pl.BlockSpec((rows, q_width), lambda p, m: (p, 0)),
            padded,
            padded,
        ],
    )
    padded_shape = jax.ShapeDtypeStruct((key_heads, 2, total, PAIR), jnp.bfloat16)
    return pl.pallas_call(
        functools.partial(project_kernel, size=size, q_width=q_width, kv_width=kv_width),
        grid_spec=spec,
        out_shape=[
            jax.ShapeDtypeStruct((total, features), jnp.bfloat16),
            jax.ShapeDtypeStruct((total, q_width), jnp.bfloat16),
            padded_shape,
            padded_shape,
        ],
        compiler_params=PARAMS,
        cost_estimate=hint(2 * total * features * width // 16),
    )(me, *blocks, gain, own, other, own, other, cosine, sine)


def attend_kernel(
    me_ref, q_ref, k_ref, v_ref, wo_ref, wx_ref, o_ref, l_ref, *refs, size, heads, group
):
    part_refs, vt_ref = refs[:size], refs[size]
    rows = q_ref.shape[0]
    half = wo_ref.shape[0]
    mine = jnp.bitwise_xor(me_ref[0], pl.program_id(0))
    key_place = lax.broadcasted_iota(jnp.int32, (rows, rows), 0)
    query_place = lax.broadcasted_iota(jnp.int32, (rows, rows), 1)

    @pl.when(pl.program_id(0) == 0)
    def _():
        for head in range(heads // group):
            for side in range(2):
                vt_ref[head, side] = v_ref[head, side].T

    def one(span):
        keys = span * rows
        for pair in range(heads // 2):
            head = 2 * pair // group
            lanes = slice(pair * PAIR, (pair + 1) * PAIR)
            query = q_ref[:, lanes]
            acc = None
            inverse = []
            for side in range(2):
                diag = mm_nt(k_ref[head, side, keys : keys + rows, :], query)
                diag = jnp.where(key_place <= query_place, diag, -1e9)
                top = jnp.max(diag, axis=0, keepdims=True)
                if span:
                    body = mm_nt(k_ref[head, side, :keys, :], query)
                    top = jnp.maximum(top, jnp.max(body, axis=0, keepdims=True))
                diag = jnp.exp(diag - top)
                total = jnp.sum(diag, axis=0, keepdims=True)
                part = mm(vt_ref[head, side, :, keys : keys + rows], diag.astype(jnp.bfloat16))
                if span:
                    body = jnp.exp(body - top)
                    total = total + jnp.sum(body, axis=0, keepdims=True)
                    part = part + mm(vt_ref[head, side, :, :keys], body.astype(jnp.bfloat16))
                acc = part if acc is None else acc + part
                inverse.append(jnp.broadcast_to(1.0 / total, (HEAD_DIM, rows)))
                l_ref[2 * pair + side : 2 * pair + side + 1, :] = top + jnp.log(total)
            acc = acc * jnp.concatenate(inverse, axis=0)
            o_ref[:, lanes] = acc.T.astype(jnp.bfloat16)

    for span in range(size):
        pl.when(mine == span)(functools.partial(one, span))

    def project_out(ref):
        ref[:, :half] = mm_nt(o_ref[...], wo_ref[...]).astype(jnp.bfloat16)
        ref[:, half:] = mm_nt(o_ref[...], wx_ref[...]).astype(jnp.bfloat16)

    for step in range(size):
        pl.when(pl.program_id(0) == step)(functools.partial(project_out, part_refs[step]))


def attend(me, query, key_pad, value_pad, own, other, columns, size, group):
    total, width = query.shape
    features = 2 * own.shape[0]
    rows, heads = total // size, width // HEAD_DIM
    whole = pl.BlockSpec(key_pad.shape, lambda p, m: (0, 0, 0, 0), pipeline_mode=ONCE)
    spec = pltpu.PrefetchScalarGridSpec(
        num_scalar_prefetch=1,
        grid=(size,),
        in_specs=[pl.BlockSpec((rows, width), lambda p, m: (p, 0)), whole, whole]
        + [columns.spec("out", features // 2)] * 2,
        out_specs=[
            pl.BlockSpec((rows, width), lambda p, m: (p, 0)),
            pl.BlockSpec((heads, rows), lambda p, m: (0, p)),
        ]
        + [pl.BlockSpec((rows, features), lambda p, m: (0, 0))] * size,
        scratch_shapes=[pltpu.VMEM((heads // group, 2, PAIR, total), jnp.bfloat16)],
    )
    return pl.pallas_call(
        functools.partial(attend_kernel, size=size, heads=heads, group=group),
        grid_spec=spec,
        out_shape=[
            jax.ShapeDtypeStruct((total, width), jnp.bfloat16),
            jax.ShapeDtypeStruct((heads, total), jnp.float32),
        ]
        + [jax.ShapeDtypeStruct((rows, features), jnp.bfloat16)] * size,
        compiler_params=PARAMS,
        cost_estimate=hint(8 * heads * total * total * HEAD_DIM // 16),
    )(me, query, key_pad, value_pad, own, other)


def attend_back_kernel(
    me_ref, q_ref, l_ref, k_ref, v_ref, cos_ref, sin_ref, *refs, size, heads, group
):
    do_refs = refs[:size]
    out_ref, dk_ref, dv_ref, kt_ref, do_ref = refs[size:]
    rows = q_ref.shape[0]
    key_heads = heads // group
    step = pl.program_id(0)
    me = me_ref[0]
    mine = jnp.bitwise_xor(me, step)
    key_place = lax.broadcasted_iota(jnp.int32, (rows, rows), 0)
    query_place = lax.broadcasted_iota(jnp.int32, (rows, rows), 1)

    def rows_of(block):
        return pl.ds(pl.multiple_of(block * rows, rows), rows)

    @pl.when(step == 0)
    def _():
        dk_ref[...] = jnp.zeros_like(dk_ref)
        dv_ref[...] = jnp.zeros_like(dv_ref)
        for head in range(key_heads):
            for side in range(2):
                kt_ref[head, side] = k_ref[head, side].T

    def fetch(ref):
        do_ref[...] = ref[...]

    for block in range(size):
        pl.when(step == block)(functools.partial(fetch, do_refs[block]))

    def one(span):
        keys = span * rows
        parts = [(keys, keys + rows, True)] + ([(0, keys, False)] if span else [])
        cosine, sine = cos_ref[keys : keys + rows, :], sin_ref[keys : keys + rows, :]
        for pair in range(heads // 2):
            head = 2 * pair // group
            lanes = slice(pair * PAIR, (pair + 1) * PAIR)
            query, grad = q_ref[:, lanes], do_ref[:, lanes]
            acc = None
            for side in range(2):
                log_total = l_ref[2 * pair + side : 2 * pair + side + 1, :]
                inner = None
                kept = []
                for low, high, diagonal in parts:
                    probs = mm_nt(k_ref[head, side, low:high, :], query)
                    probs = jnp.exp(probs - log_total)
                    if diagonal:
                        probs = jnp.where(key_place <= query_place, probs, 0.0)
                    prob_grad = mm_nt(v_ref[head, side, low:high, :], grad)
                    dv_ref[head, side, low:high, :] += mm(probs.astype(jnp.bfloat16), grad)
                    term = jnp.sum(probs * prob_grad, axis=0, keepdims=True)
                    inner = term if inner is None else inner + term
                    kept.append((low, high, probs, prob_grad))
                for low, high, probs, prob_grad in kept:
                    score_grad = (probs * (prob_grad - inner)).astype(jnp.bfloat16)
                    dk_ref[head, side, low:high, :] += mm(score_grad, query)
                    part = mm(kt_ref[head, side, :, low:high], score_grad)
                    acc = part if acc is None else acc + part
            turned = turn(acc.T * SCALE, cosine, -sine)
            out_ref[rows_of(step), lanes] = turned.astype(jnp.bfloat16)

    for span in range(size):
        pl.when(mine == span)(functools.partial(one, span))

    @pl.when(step == size - 1)
    def _():
        first = lane_index(rows) < HEAD_DIM
        wanted = [(dk_ref, head, True) for head in range(key_heads)]
        wanted += [(dv_ref, head, False) for head in range(key_heads)]
        for span in range(size):
            place = slice(span * rows, (span + 1) * rows)
            cosine, sine = cos_ref[place, :], sin_ref[place, :]
            for block in range(len(wanted) // 2):
                halves, rotate = [], []
                for half in range(2):
                    ref, head, is_key = wanted[2 * block + half]
                    low, high = ref[head, 0, place, :], ref[head, 1, place, :]
                    if half:
                        halves.append(pltpu.roll(low, HEAD_DIM, 1) + high)
                    else:
                        halves.append(low + pltpu.roll(high, HEAD_DIM, 1))
                    rotate.append(is_key)
                value = jnp.where(first, halves[0], halves[1])
                if rotate[0] and rotate[1]:
                    value = turn(value, cosine, -sine)
                elif rotate[0]:
                    value = jnp.where(first, turn(value, cosine, -sine), value)
                start = heads * HEAD_DIM + block * PAIR
                target = rows_of(jnp.bitwise_xor(me, span))
                out_ref[target, start : start + PAIR] = value.astype(jnp.bfloat16)


def attend_back(
    me, query, log_total, key_pad, value_pad, cosine, sine, attended_grad, group
):
    total, width = query.shape
    size = len(attended_grad)
    rows, heads = total // size, width // HEAD_DIM
    key_heads = heads // group
    out_width = width + 2 * key_heads * HEAD_DIM
    whole = pl.BlockSpec(key_pad.shape, lambda p, m: (0, 0, 0, 0), pipeline_mode=ONCE)
    table = pl.BlockSpec((total, PAIR), lambda p, m: (0, 0), pipeline_mode=ONCE)
    spec = pltpu.PrefetchScalarGridSpec(
        num_scalar_prefetch=1,
        grid=(size,),
        in_specs=[
            pl.BlockSpec((rows, width), lambda p, m: (p, 0)),
            pl.BlockSpec((heads, rows), lambda p, m: (0, p)),
            whole,
            whole,
            table,
            table,
        ]
        + [pl.BlockSpec((rows, width), lambda p, m: (0, 0), pipeline_mode=ONCE)] * size,
        out_specs=pl.BlockSpec((total, out_width), lambda p, m: (0, 0)),
        scratch_shapes=[
            pltpu.VMEM(key_pad.shape, jnp.float32),
            pltpu.VMEM(key_pad.shape, jnp.float32),
            pltpu.VMEM((key_heads, 2, PAIR, total), jnp.bfloat16),
            pltpu.VMEM((rows, width), jnp.bfloat16),
        ],
    )
    return pl.pallas_call(
        functools.partial(attend_back_kernel, size=size, heads=heads, group=group),
        grid_spec=spec,
        out_shape=jax.ShapeDtypeStruct((total, out_width), jnp.bfloat16),
        compiler_params=PARAMS,
        cost_estimate=hint(20 * heads * total * total * HEAD_DIM),
    )(me, query, log_total, key_pad, value_pad, cosine, sine, *attended_grad)


def mlp_kernel(*refs, size, adds):
    n_refs, e_refs = refs[:size], refs[size : 2 * size]
    gate_o, up_o, down_o, gate_x, up_x, down_x = refs[2 * size : 2 * size + 6]
    y_ref, n_ref, e_ref = refs[-3:]
    dn_refs = refs[-3 - size if adds else -4 : -3]
    dg_ref, du_ref, h_ref = refs[-6 - size if adds else -7 :][:3]
    half = gate_o.shape[0]

    def fetch(step):
        n_ref[...] = n_refs[step][...]
        e_ref[...] = e_refs[step][...]

    for step in range(size):
        pl.when(pl.program_id(0) == step)(functools.partial(fetch, step))
    gate = mm(n_ref[:, :half], gate_o[...]) + mm(n_ref[:, half:], gate_x[...])
    up = mm(n_ref[:, :half], up_o[...]) + mm(n_ref[:, half:], up_x[...])
    grad = mm(e_ref[:, :half], down_o[...]) + mm(e_ref[:, half:], down_x[...])
    sigma = jax.nn.sigmoid(gate)
    silu = gate * sigma
    hidden = (silu * up).astype(jnp.bfloat16)
    gate_grad = (grad * up * sigma * (1.0 + gate * (1.0 - sigma))).astype(jnp.bfloat16)
    up_grad = (grad * silu).astype(jnp.bfloat16)
    dg_ref[...] = gate_grad
    du_ref[...] = up_grad
    h_ref[...] = hidden
    for part, gate_w, up_w, down_w in ((0, gate_o, up_o, down_o), (1, gate_x, up_x, down_x)):
        lanes = slice(part * half, (part + 1) * half)
        dn = mm_nt(gate_grad, gate_w[...]) + mm_nt(up_grad, up_w[...])
        y = mm_nt(hidden, down_w[...])
        if adds:
            dn = dn + refs[2 * size + 6][:, lanes].astype(jnp.float32)
            y = y + refs[2 * size + 7][:, lanes].astype(jnp.float32)
        y_ref[:, lanes] = y.astype(jnp.bfloat16)
        dn = dn.astype(jnp.bfloat16)

        def store(ref):
            ref[:, lanes] = dn

        if adds:
            for step in range(size):
                pl.when(pl.program_id(0) == step)(functools.partial(store, dn_refs[step]))
        else:
            store(dn_refs[0])


def mlp(tokens, cot, own, other, earlier):
    size = len(tokens)
    rows, features = tokens[0].shape
    half, units = own.shape[0], own.shape[1] // 3
    total = rows * size
    fixed = lambda p: (0, 0)
    moving = lambda p: (p, 0)
    wide = pl.BlockSpec((rows, features), moving)
    sums = jax.ShapeDtypeStruct((total, features), jnp.bfloat16)
    dn_specs, dn_shapes = [wide], [sums]
    if earlier:
        dn_specs = [pl.BlockSpec((rows, features), fixed)] * size
        dn_shapes = [jax.ShapeDtypeStruct((rows, features), jnp.bfloat16)] * size
    block = pl.BlockSpec((rows, features), fixed, pipeline_mode=ONCE)
    thirds = [
        pl.BlockSpec((half, units), lambda p, t=t: (0, t), pipeline_mode=ONCE) for t in range(3)
    ]
    return pl.pallas_call(
        functools.partial(mlp_kernel, size=size, adds=bool(earlier)),
        grid=(size,),
        in_specs=[block] * (2 * size)
        + thirds * 2
        + [wide] * len(earlier),
        out_specs=[pl.BlockSpec((rows, units), moving)] * 3 + dn_specs + [wide],
        out_shape=[jax.ShapeDtypeStruct((total, units), jnp.bfloat16)] * 3 + dn_shapes + [sums],
        scratch_shapes=[pltpu.VMEM((rows, features), jnp.bfloat16)] * 2,
        compiler_params=PARAMS,
        cost_estimate=hint(12 * total * features * units),
    )(*tokens, *cot, own, own, own, other, other, other, *earlier)


def add_refs(refs):
    total = refs[0][...].astype(jnp.float32)
    for ref in refs[1:]:
        total = total + ref[...].astype(jnp.float32)
    return total


def store_by_device(out_ref, values, core, chips):
    width = values.shape[1] // (2 * chips)
    for chip in range(chips):
        own = values[:, chip * width : (chip + 1) * width]
        other = values[:, (chips + chip) * width : (chips + chip + 1) * width]
        low = 2 * chip * width
        out_ref[:, low : low + width] = jnp.where(core == 0, own, other)
        out_ref[:, low + width : low + 2 * width] = jnp.where(core == 0, other, own)


def middle_kernel(*refs):
    x_ref, gain_ref, middle_ref, normed_ref = refs[-4:]
    values = x_ref[...].astype(jnp.float32) + add_refs(refs[:-4])
    middle_ref[...] = values
    normed_ref[...] = (values * rms_scale(values) * gain_ref[...]).astype(jnp.bfloat16)


def input_back_kernel(core_ref, *refs, chips):
    x_ref, before_ref, gain_ref, out_ref = refs[-4:]
    values = x_ref[...].astype(jnp.float32)
    inner = add_refs(refs[:-4]) * gain_ref[...]
    scale = rms_scale(values)
    mean = jnp.mean(inner * values, axis=-1, keepdims=True)
    result = before_ref[...] + scale * inner - values * (scale * scale * scale) * mean
    store_by_device(out_ref, result, core_ref[0], chips)


def output_kernel(core_ref, *refs, chips):
    middle_ref, out_ref = refs[-2:]
    values = middle_ref[...] + add_refs(refs[:-2])
    store_by_device(out_ref, values.astype(jnp.bfloat16), core_ref[0], chips)


def row_call(body, dtypes, arrays, core=None):
    rows, features = arrays[0].shape
    steps = 2
    wide = pl.BlockSpec((rows // steps, features), lambda i, *_: (i, 0))
    row = pl.BlockSpec((1, features), lambda i, *_: (0, 0))
    scalars = [] if core is None else [jnp.full((1,), core, jnp.int32)]
    return pl.pallas_call(
        body,
        grid_spec=pltpu.PrefetchScalarGridSpec(
            num_scalar_prefetch=len(scalars),
            grid=(steps,),
            in_specs=[row if array.shape[0] == 1 else wide for array in arrays],
            out_specs=[wide] * len(dtypes),
        ),
        out_shape=[jax.ShapeDtypeStruct((rows, features), dtype) for dtype in dtypes],
        compiler_params=PARAMS,
        cost_estimate=hint(0),
    )(*scalars, *arrays)


def unpack_kernel(sum_ref, q_ref, k_ref, v_ref, out_ref):
    q_width, kv_width = q_ref.shape[1], k_ref.shape[1]
    values = sum_ref[...].astype(jnp.float32)
    q_ref[...] = values[:, :q_width]
    kv = values[:, q_width : q_width + 2 * kv_width]
    k_ref[...] = kv[:, :kv_width]
    v_ref[...] = kv[:, kv_width:]
    out_ref[...] = values[:, q_width + 2 * kv_width :].T


def unpack(sums, q_width, kv_width):
    rows = sums.shape[0]
    widths = [(rows, q_width), (rows, kv_width), (rows, kv_width), (q_width, rows)]
    return pl.pallas_call(
        unpack_kernel,
        out_shape=[jax.ShapeDtypeStruct(shape, jnp.float32) for shape in widths],
        compiler_params=PARAMS,
        cost_estimate=hint(0),
    )(sums)


def middle_back_kernel(*refs, parts, size):
    n_refs, refs = refs[:parts], refs[parts:]
    x_ref, e_ref, gain_ref, refs = refs[0], refs[1], refs[2], refs[3:]
    own_refs, other_refs, refs = refs[:size], refs[size : 2 * size], refs[2 * size :]
    grad_ref, branch_ref, part_ref, do_refs = refs[0], refs[1], refs[2], refs[3:]
    half = own_refs[0].shape[0]
    grad = add_refs(n_refs)
    values = x_ref[...]
    scale = rms_scale(values)
    result, part = norm_back(grad, values, scale, gain_ref[...])

    @pl.when(pl.program_id(0) == 0)
    def _():
        part_ref[...] = jnp.zeros_like(part_ref)

    part_ref[...] += part[None, :]
    result = result + e_ref[...].astype(jnp.float32)
    grad_ref[...] = result
    branch = result.astype(jnp.bfloat16)
    branch_ref[...] = branch
    for own, other, do_ref in zip(own_refs, other_refs, do_refs):
        do = mm(branch[:, :half], own[...]) + mm(branch[:, half:], other[...])
        do_ref[...] = do.astype(jnp.bfloat16)


def middle_back(arrived, middle, cot, gain, own, other):
    parts, size = len(arrived), len(own)
    rows, features = middle.shape
    width = own[0].shape[1]
    steps = 2
    wide = pl.BlockSpec((rows // steps, features), lambda i: (i, 0))
    narrow = pl.BlockSpec((rows // steps, width), lambda i: (i, 0))
    row = pl.BlockSpec((1, features), lambda i: (0, 0))
    weight = pl.BlockSpec((features // 2, width), lambda i: (0, 0), pipeline_mode=ONCE)
    grad, branch, part, *do = pl.pallas_call(
        functools.partial(middle_back_kernel, parts=parts, size=size),
        grid=(steps,),
        in_specs=[wide] * parts + [wide, wide, row] + [weight] * (2 * size),
        out_specs=[wide, wide, row] + [narrow] * size,
        out_shape=[
            jax.ShapeDtypeStruct((rows, features), jnp.float32),
            jax.ShapeDtypeStruct((rows, features), jnp.bfloat16),
            jax.ShapeDtypeStruct((1, features), jnp.float32),
        ]
        + [jax.ShapeDtypeStruct((rows, width), jnp.bfloat16)] * size,
        compiler_params=PARAMS,
        cost_estimate=hint(2 * rows * features * width * size),
    )(*arrived, middle, cot, gain, *own, *other)
    return grad, branch, part[0], do


def column_grad(blocks, other, mine, theirs):
    rows = blocks[0].shape[0]
    total = mm_tn(other[...], theirs[...])
    for index, block in enumerate(blocks):
        total = total + mm_tn(block[...], mine[index * rows : (index + 1) * rows, :])
    return total


def grad_kernel(*refs, size):
    n_refs, e_refs = refs[:size], refs[size : 2 * size]
    n_other, e_other = refs[2 * size : 2 * size + 2]
    acts, out_ref = refs[2 * size + 2 : -1], refs[-1]
    units = acts[0].shape[1]
    for third in range(3):
        blocks, other = (e_refs, e_other) if third == 2 else (n_refs, n_other)
        grad = column_grad(blocks, other, acts[third], acts[third + 3])
        out_ref[0, :, third * units : (third + 1) * units] = grad.astype(jnp.bfloat16)


def mlp_grads(chips, tokens, cot, tokens_other, cot_other, mine, theirs):
    size = len(tokens)
    rows, features = tokens[0].shape
    total, units = mine[0].shape
    depth = features // (2 * chips)
    column = pl.BlockSpec((rows, depth), lambda b: (0, b))
    long = pl.BlockSpec((total, depth), lambda b: (0, b))
    fixed = pl.BlockSpec((total, units), lambda b: (0, 0), pipeline_mode=ONCE)
    return pl.pallas_call(
        functools.partial(grad_kernel, size=size),
        grid=(chips,),
        in_specs=[column] * (2 * size) + [long, long] + [fixed] * 6,
        out_specs=pl.BlockSpec((1, depth, 3 * units), lambda b: (b, 0, 0)),
        out_shape=jax.ShapeDtypeStruct((chips, depth, 3 * units), jnp.bfloat16),
        compiler_params=PARAMS,
        cost_estimate=hint(6 * total * features * units),
    )(*tokens, *cot, tokens_other, cot_other, *mine, *theirs)


def attn_grad_kernel(*refs, size):
    e_refs = refs[2 : 2 + size]
    n_ref, n_other = refs[:2]
    e_other, d_ref, d_other, o_ref, o_other, q_ref, kv_ref, g1_ref, g2_ref = refs[2 + size : -2]
    out_ref, gain_ref = refs[-2:]
    width, out_width = d_ref.shape[1], o_ref.shape[1]
    grad = column_grad([n_ref], n_other, d_ref, d_other)
    out_ref[0, :, :width] = grad.astype(jnp.bfloat16)
    out_grad = column_grad(e_refs, e_other, o_ref, o_other)
    out_ref[0, :, width : width + out_width] = out_grad.astype(jnp.bfloat16)
    cut = q_ref.shape[1]
    first = jnp.sum(grad[:, :cut] * q_ref[...].astype(jnp.float32), axis=1, keepdims=True)
    first += jnp.sum(grad[:, cut:] * kv_ref[...].astype(jnp.float32), axis=1, keepdims=True)
    first = first / g1_ref[...]
    lane = lane_index(grad.shape[0])
    gain_ref[0] = jnp.where(lane == 0, first, g2_ref[...])


def attn_grads(
    chips, tokens, branch, mine, theirs, weights, columns, gain_one, gain_two_part
):
    size = len(branch)
    qkv_grad, attended = mine
    tokens_other, branch_other, qkv_other, attended_other = theirs
    total, features = tokens.shape
    rows = total // size
    width, out_width = qkv_grad.shape[1], attended.shape[1]
    depth = features // (2 * chips)
    column = lambda b: (0, b)
    row = lambda b: (b, 0)
    long = pl.BlockSpec((total, depth), column)
    fixed = lambda array: pl.BlockSpec(array.shape, lambda b: (0, 0), pipeline_mode=ONCE)
    place = lambda b: (b, 0, 0)
    return pl.pallas_call(
        functools.partial(attn_grad_kernel, size=size),
        grid=(chips,),
        in_specs=[long, long]
        + [pl.BlockSpec((rows, depth), column)] * size
        + [long]
        + [fixed(qkv_grad)] * 2
        + [fixed(attended)] * 2
        + [
            columns.spec("q", depth, lambda b=None: b),
            columns.spec("kv", depth, lambda b=None: b),
            pl.BlockSpec((depth, 1), row),
            pl.BlockSpec((depth, 1), row),
        ],
        out_specs=[
            pl.BlockSpec((1, depth, width + out_width), place),
            pl.BlockSpec((1, depth, PAIR), place),
        ],
        out_shape=[
            jax.ShapeDtypeStruct((chips, depth, width + out_width), jnp.bfloat16),
            jax.ShapeDtypeStruct((chips, depth, PAIR), jnp.float32),
        ],
        compiler_params=PARAMS,
        cost_estimate=hint(2 * total * features * (width + out_width)),
    )(
        tokens,
        tokens_other,
        *branch,
        branch_other,
        qkv_grad,
        qkv_other,
        attended,
        attended_other,
        weights,
        weights,
        gain_one,
        gain_two_part,
    )


def input_grad_kernel(d_ref, qo_ref, qx_ref, kvo_ref, kvx_ref, *out_refs):
    half, cut = qo_ref.shape

    def one(ref):
        query, rest = d_ref[:, :cut], d_ref[:, cut:]
        own = mm_nt(query, qo_ref[...]) + mm_nt(rest, kvo_ref[...])
        other = mm_nt(query, qx_ref[...]) + mm_nt(rest, kvx_ref[...])
        ref[:, :half] = own.astype(jnp.bfloat16)
        ref[:, half:] = other.astype(jnp.bfloat16)

    for step, ref in enumerate(out_refs):
        pl.when(pl.program_id(0) == step)(functools.partial(one, ref))


def input_grad(qkv_grad, own, other, columns, size):
    total, width = qkv_grad.shape
    features = 2 * own.shape[0]
    rows = total // size
    fixed = lambda i: (0, 0)
    weights = [columns.spec(part, own.shape[0]) for part in ("q", "q", "kv", "kv")]
    return pl.pallas_call(
        input_grad_kernel,
        grid=(size,),
        in_specs=[pl.BlockSpec((rows, width), lambda i: (i, 0))] + weights,
        out_specs=[pl.BlockSpec((rows, features), fixed)] * size,
        out_shape=[jax.ShapeDtypeStruct((rows, features), jnp.bfloat16)] * size,
        compiler_params=PARAMS,
        cost_estimate=hint(2 * total * features * width),
    )(qkv_grad, own, other, own, other)


def swap(values, step):
    size = lax.axis_size("tensor")
    return lax.ppermute(values, "tensor", [(i, i ^ step) for i in range(size)])


def spread(values):
    return [values] + [swap(values, step) for step in range(1, lax.axis_size("tensor"))]


def send_blocks(blocks):
    return [blocks[0]] + [swap(block, step + 1) for step, block in enumerate(blocks[1:])]


def merge_kernel(x_ref, y_ref, top_ref, bottom_ref, x_out, y_out):
    half = top_ref.shape[0]
    x_out[:half] = x_ref[:half]
    x_out[half:] = add_refs([x_ref.at[half:], bottom_ref]).astype(jnp.bfloat16)
    y_out[:half] = add_refs([y_ref.at[:half], top_ref]).astype(jnp.bfloat16)
    y_out[half:] = y_ref[half:]


def send_sum(blocks, held=()):
    if len(blocks) != 4:
        return send_blocks(blocks), held
    own, near_x, near_y, far = blocks
    half = far.shape[0] // 2
    top, bottom = swap(far[:half], 1), swap(far[half:], 2)
    near_x, near_y = pl.pallas_call(
        merge_kernel,
        out_shape=[jax.ShapeDtypeStruct(near_x.shape, near_x.dtype)] * 2,
        compiler_params=PARAMS,
        cost_estimate=hint(0),
    )(near_x, near_y, top, bottom)
    near_x, near_y, held = barrier((near_x, near_y, held))
    return [own, swap(near_x, 1), swap(near_y, 2)], held


def add_up(blocks):
    total = blocks[0].astype(jnp.float32)
    for block in blocks[1:]:
        total = total + block.astype(jnp.float32)
    return total


def cross(values):
    count = lax.axis_size("dp")
    return lax.ppermute(values, "dp", [(i, i ^ 1) for i in range(count)])


def tables(positions):
    freqs = ROPE_BASE ** (-jnp.arange(0, HEAD_DIM, 2).astype(jnp.float32) / HEAD_DIM)
    angles = positions.astype(jnp.float32)[:, None] * freqs[None, :]
    cosine, sine = jnp.cos(angles), jnp.sin(angles)
    return (
        jnp.concatenate([cosine] * 4, axis=1),
        jnp.concatenate([-sine, sine, -sine, sine], axis=1),
    )


def chip_lines():
    count = lax.axis_size("dp")
    return [list(range(core, count, 2)) for core in range(2)]


def gather(values):
    return lax.all_gather(values, "dp", axis=0, tiled=True, axis_index_groups=chip_lines())


def scatter(values):
    total = lax.psum_scatter(
        values, "dp", scatter_dimension=0, tiled=True, axis_index_groups=chip_lines()
    )
    return total[0]


def along(values, step):
    count = lax.axis_size("dp")
    return lax.ppermute(values, "dp", [(i, (i + 2 * step) % count) for i in range(count)])


def line_parts(parts):
    chips = lax.axis_size("dp") // 2
    chip = lax.axis_index("dp") // 2
    blocks = [lax.dynamic_index_in_dim(parts, chip, 0, keepdims=False)]
    for step in range(1, chips):
        sent = lax.dynamic_index_in_dim(parts, (chip + step) % chips, 0, keepdims=False)
        blocks.append(along(sent, step))
    return blocks


def own_part(values):
    size = lax.axis_size("tensor")
    me = lax.axis_index("tensor")
    blocks = values.reshape((size, -1) + values.shape[1:])
    own = lax.dynamic_index_in_dim(blocks, me, 0, keepdims=False)
    for step in range(1, size):
        sent = lax.dynamic_index_in_dim(blocks, me ^ step, 0, keepdims=False)
        own = own + swap(sent, step)
    return own


def stack_kernel(*refs):
    rows = refs[0].shape[0]
    for index, ref in enumerate(refs[:-1]):
        refs[-1][index * rows : (index + 1) * rows, :] = ref[...]


def other_half(blocks):
    size = len(blocks)
    rows, features = blocks[0].shape
    shape = (size * rows, features // 2)
    halves = pl.pallas_call(
        stack_kernel,
        grid=(1,),
        in_specs=[pl.BlockSpec((rows, features // 2), lambda i: (0, 1))] * size,
        out_specs=pl.BlockSpec(shape, lambda i: (0, 0)),
        out_shape=jax.ShapeDtypeStruct(shape, blocks[0].dtype),
        compiler_params=PARAMS,
        cost_estimate=hint(0),
    )(*blocks)
    return cross(halves)


def feature_blocks(values):
    width = values.shape[-1] // lax.axis_size("dp")
    return [values[..., low : low + width] for low in range(0, values.shape[-1], width)]


def by_core(values, core):
    blocks = feature_blocks(values)
    pairs = list(zip(blocks[0::2], blocks[1::2]))
    own = [jnp.where(core == 0, even, odd) for even, odd in pairs]
    other = [jnp.where(core == 0, odd, even) for even, odd in pairs]
    return jnp.concatenate(own + other, axis=-1)


def per_device(
    hidden_in,
    gain_attn,
    w_query,
    w_key,
    w_value,
    w_out,
    gain_mlp,
    w_gate,
    w_up,
    w_down,
    positions,
    cotangent,
):
    size = lax.axis_size("tensor")
    chips = lax.axis_size("dp") // 2
    me = lax.axis_index("tensor")
    me_array = jnp.full((1,), me, jnp.int32)
    core = lax.axis_index("dp") % 2
    q_width, kv_width = w_query.shape[1], w_key.shape[1]
    group = q_width // kv_width
    units = w_down.shape[0] // 2
    half = hidden_in.shape[1] // 2

    columns = Columns(q_width, kv_width)
    attn_shard = jnp.concatenate([w_query, w_out.T, w_key, w_value], axis=1)
    attn_shard, hidden_in, gain_attn = barrier((attn_shard, hidden_in, gain_attn))
    attn_own = gather(attn_shard)
    residual = by_core(hidden_in, core)
    blocks_in = spread(residual)
    gains = lax.all_gather(jnp.stack([gain_attn, gain_mlp]), "dp", axis=1, tiled=True)
    gains = by_core(gains, core).astype(jnp.float32)
    cosine, sine = tables(positions)
    cotangent = by_core(cotangent, core)
    down_t = w_down.T
    shares = []
    for part in range(2):
        cut = slice(part * units, (part + 1) * units)
        shares.append(jnp.concatenate([w_gate[:, cut], w_up[:, cut], down_t[:, cut]], axis=1))
    shares, attn_own, blocks_in, cosine, sine, gains, cotangent = barrier(
        (shares, attn_own, blocks_in, cosine, sine, gains, cotangent)
    )
    mlp_own = [gather(share) for share in shares]
    cot_blocks = spread(cotangent)
    gain_one, gain_two = gains[0], gains[1]
    attn = (attn_own, cross(attn_own))

    tokens_one, query, key_pad, value_pad = project(
        me_array, blocks_in, gain_one[None, :], *attn, cosine, sine, columns
    )
    attended, log_total, *parts = attend(
        me_array, query, key_pad, value_pad, *attn, columns, size, group
    )
    parts, cot_blocks, tokens_one, attended = barrier((parts, cot_blocks, tokens_one, attended))
    arrived, _ = send_sum(parts)
    cot_other = other_half(cot_blocks)
    early = (cross(tokens_one[:, half:]), cross(attended))
    arrived, cot_other, early = barrier((arrived, cot_other, early))
    out_t = [w[:, q_width : 2 * q_width] for w in attn]
    middle, normed_two = row_call(
        middle_kernel, [jnp.float32, jnp.bfloat16], [*arrived, residual, gain_two[None, :]]
    )
    normed_two, own_share = barrier((normed_two, mlp_own[0]))
    tokens_two = spread(normed_two)
    weights = (own_share, cross(own_share))
    tokens_two, weights, out_own = barrier((tokens_two, weights, out_t[0]))
    tokens_other = other_half(tokens_two)
    *acts, dn_part, y_part = mlp(tokens_two, cot_blocks, *weights, ())
    out_blocks = spread(out_own)
    acts, tokens_other = barrier((acts, tokens_other))
    acts_other = [cross(act) for act in acts]
    grads_one = mlp_grads(
        chips, tokens_two, cot_blocks, tokens_other, cot_other, acts, acts_other
    )
    grads_one, own_share = barrier((grads_one, mlp_own[1]))
    sums_one = scatter(grads_one)
    weights = (own_share, cross(own_share))
    *acts, y_part = mlp(tokens_two, cot_blocks, *weights, (dn_part, y_part))
    acts, dn_part = acts[:3], acts[3:]
    acts, dn_part, out_blocks = barrier((acts, dn_part, out_blocks))
    acts_other = [cross(act) for act in acts]
    arrived, acts = send_sum(dn_part, acts)
    out_other = [out_t[1]] + [cross(block) for block in out_blocks[1:]]
    grads_two = mlp_grads(
        chips, tokens_two, cot_blocks, tokens_other, cot_other, acts, acts_other
    )
    grads_two, arrived, out_other, y_part = barrier((grads_two, arrived, out_other, y_part))
    y_blocks = list(y_part.reshape((size, -1) + y_part.shape[1:]))
    y_early = [swap(y_blocks[step], step) for step in range(1, 3)]
    sums_two = scatter(grads_two)
    middle_grad, branch, gain_two_part, do_blocks = middle_back(
        arrived, middle, cotangent, gain_two[None, :], out_blocks, out_other
    )
    do_blocks = send_blocks(do_blocks)
    gain_two_other = cross(gain_two_part[half:])
    do_blocks, branch, gain_two_other, y_blocks, y_early = barrier(
        (do_blocks, branch, gain_two_other, y_blocks, y_early)
    )
    branch_blocks = spread(branch)
    qkv_grad = attend_back(
        me_array, query, log_total, key_pad, value_pad, cosine, sine, do_blocks, group
    )
    qkv_grad, sums_one = barrier((qkv_grad, sums_one))
    qkv_other = cross(qkv_grad)
    normed_part = input_grad(qkv_grad, *attn, columns, size)
    branch_blocks, normed_part = barrier((branch_blocks, normed_part))
    branch_other = other_half(branch_blocks)
    arrived, qkv_grad = send_sum(normed_part, qkv_grad)
    tokens_other, attended_other = early
    grads, gain_parts = attn_grads(
        chips,
        tokens_one,
        branch_blocks,
        (qkv_grad, attended),
        (tokens_other, branch_other, qkv_other, attended_other),
        attn_own,
        columns,
        gain_one[:half, None],
        (gain_two_part[:half] + gain_two_other)[:, None],
    )
    grads, early = barrier((grads, arrived[1:3]))
    arrived[1:3] = early
    attn_sums = scatter(grads)
    gain_sums = add_up(line_parts(gain_parts[:, :, :2]))
    arrived, gain_sums, y_blocks, sums_two = barrier((arrived, gain_sums, y_blocks, sums_two))
    y_late = [swap(y_blocks[step], step) for step in range(3, size)]
    gain_sums = own_part(gain_sums)
    (grad_in,) = row_call(
        functools.partial(input_back_kernel, chips=chips),
        [jnp.float32],
        [*arrived, residual, middle_grad, gain_one[None, :]],
        core,
    )
    shares = [share.astype(jnp.float32) for share in (sums_one, sums_two)]
    grad_gate = jnp.concatenate([h[:, :units] for h in shares], axis=1)
    grad_up = jnp.concatenate([h[:, units : 2 * units] for h in shares], axis=1)
    grad_down = jnp.concatenate([h[:, 2 * units :].T for h in shares], axis=0)
    y_late, grad_in, gain_sums, grad_gate, grad_up, grad_down = barrier(
        (y_late, grad_in, gain_sums, grad_gate, grad_up, grad_down)
    )
    (out,) = row_call(
        functools.partial(output_kernel, chips=chips),
        [jnp.bfloat16],
        [y_blocks[0], *y_early, *y_late, middle],
        core,
    )
    out, attn_sums = barrier((out, attn_sums))
    grad_query, grad_key, grad_value, grad_out = unpack(attn_sums, q_width, kv_width)
    return (
        out,
        grad_in,
        gain_sums[:, 0],
        grad_query,
        grad_key,
        grad_value,
        grad_out,
        gain_sums[:, 1],
        grad_gate,
        grad_up,
        grad_down,
    )


def solution(mesh):
    return jax.shard_map(
        per_device,
        mesh=mesh,
        in_specs=(
            P(("dp", "tensor"), None),
            P("dp"),
            P("dp", "tensor"),
            P("dp", "tensor"),
            P("dp", "tensor"),
            P("tensor", "dp"),
            P("dp"),
            P("dp", "tensor"),
            P("dp", "tensor"),
            P("tensor", "dp"),
            P("dp"),
            P(("dp", "tensor"), None),
        ),
        out_specs=(
            P(("dp", "tensor"), None),
            P(("dp", "tensor"), None),
            P(("dp", "tensor")),
            P("dp", "tensor"),
            P("dp", "tensor"),
            P("dp", "tensor"),
            P("tensor", "dp"),
            P(("dp", "tensor")),
            P("dp", "tensor"),
            P("dp", "tensor"),
            P("tensor", "dp"),
        ),
        check_vma=False,
    )
```

```python
import functools
import math

import jax
import jax.numpy as jnp
from jax import lax
from jax.experimental import pallas as pl
from jax.experimental.pallas import tpu as pltpu
from jax.sharding import PartitionSpec as P

HEAD_DIM = 64
PAIR = 2 * HEAD_DIM
SEQ_LEN = 1024


EPS = 1e-05
ROPE_BASE = 500000.0
SCALE = 1.0 / math.sqrt(HEAD_DIM)
PARAMS = pltpu.CompilerParams(vmem_limit_bytes=58 * 2**20)
ONCE = pl.Buffered(1)

barrier = lax.optimization_barrier


def hint(flops):
    return pl.CostEstimate(flops=flops, bytes_accessed=0, transcendentals=0)


def rms_scale(values):
    return lax.rsqrt(jnp.mean(values * values, axis=-1, keepdims=True) + EPS)


def norm_back(grad, values, scale, gain):
    inner = grad * gain
    cubed = scale * scale * scale
    result = scale * inner - values * cubed * jnp.mean(inner * values, axis=-1, keepdims=True)
    return (result, jnp.sum(grad * values * scale, axis=0))


def mm(left, right):
    return jnp.dot(left, right, preferred_element_type=jnp.float32)


def mm_nt(left, right):
    return lax.dot_general(left, right, (((1,), (1,)), ((), ())), preferred_element_type=jnp.float32)


def mm_tn(left, right):
    return lax.dot_general(left, right, (((0,), (0,)), ((), ())), preferred_element_type=jnp.float32)


def lane_index(rows):
    return lax.broadcasted_iota(jnp.int32, (rows, PAIR), 1)


def turn(pair, cosine, sine):
    lower = lane_index(pair.shape[0]) % HEAD_DIM < HEAD_DIM // 2
    other = jnp.where(
        lower, pltpu.roll(pair, PAIR - HEAD_DIM // 2, 1), pltpu.roll(pair, HEAD_DIM // 2, 1)
    )
    return pair * cosine + other * sine


def project_kernel(place_ref, *refs, size, q_width, kv_width):
    x_refs = refs[:size]
    gain_ref, qo_ref, qx_ref, kvo_ref, kvx_ref, cos_ref, sin_ref = refs[size:-4]
    n_ref, q_ref, k_ref, v_ref = refs[-4:]
    rows = q_ref.shape[0]
    half = qo_ref.shape[0]

    def one(x_ref):
        x = x_ref[...].astype(jnp.float32)
        normed = (x * rms_scale(x) * gain_ref[...]).astype(jnp.bfloat16)
        n_ref[...] = normed
        cosine, sine = cos_ref[...], sin_ref[...]
        own, other = normed[:, :half], normed[:, half:]
        lin = mm(own, qo_ref[...]) + mm(other, qx_ref[...])
        for low in range(0, q_width, PAIR):
            query = turn(lin[:, low : low + PAIR], cosine, sine).astype(jnp.bfloat16)
            q_ref[:, low : low + PAIR] = query * jnp.bfloat16(SCALE)
        lin = mm(own, kvo_ref[...]) + mm(other, kvx_ref[...])
        first = lane_index(rows) < HEAD_DIM
        for ref, start, rotate in ((k_ref, 0, True), (v_ref, kv_width, False)):
            for head in range(kv_width // HEAD_DIM):
                low = start + head * HEAD_DIM
                block = lin[:, low // PAIR * PAIR : low // PAIR * PAIR + PAIR]
                if rotate:
                    block = turn(block, cosine, sine)
                moved = pltpu.roll(block, HEAD_DIM, 1)
                if low % PAIR:
                    block, moved = moved, block
                ref[head, 0] = jnp.where(first, block, 0.0).astype(jnp.bfloat16)
                ref[head, 1] = jnp.where(first, 0.0, moved).astype(jnp.bfloat16)

    for step in range(size):
        pl.when(pl.program_id(0) == step)(functools.partial(one, x_refs[step]))


class Columns:
    def __init__(self, q_width, kv_width):
        self.q_width, self.kv_width = q_width, kv_width

    def spec(self, part, rows, place=lambda *_: 0):
        width, start = {
            "q": (self.q_width, 0),
            "out": (self.q_width, self.q_width),
            "kv": (2 * self.kv_width, 2 * self.q_width),
        }[part]
        index = start // width
        mode = {"pipeline_mode": ONCE} if place() == 0 else {}
        return pl.BlockSpec((rows, width), lambda *grid: (place(*grid), index), **mode)


def project(me, blocks, gain, own, other, cosine, sine, columns):
    size = len(blocks)
    rows, features = blocks[0].shape
    total = rows * size
    q_width, kv_width = columns.q_width, columns.kv_width
    key_heads = kv_width // HEAD_DIM
    width = q_width + 2 * kv_width
    half = features // 2
    fixed = lambda p, m: (0, 0)
    placed = lambda p, m: (jnp.bitwise_xor(p, m[0]), 0)
    padded = pl.BlockSpec(
        (key_heads, 2, rows, PAIR), lambda p, m: (0, 0, jnp.bitwise_xor(p, m[0]), 0)
    )
    spec = pltpu.PrefetchScalarGridSpec(
        num_scalar_prefetch=1,
        grid=(size,),
        in_specs=[pl.BlockSpec((rows, features), fixed, pipeline_mode=ONCE)] * size
        + [
            pl.BlockSpec((1, features), fixed),
            columns.spec("q", half),
            columns.spec("q", half),
            columns.spec("kv", half),
            columns.spec("kv", half),
            pl.BlockSpec((rows, PAIR), placed),
            pl.BlockSpec((rows, PAIR), placed),
        ],
        out_specs=[
            pl.BlockSpec((rows, features), lambda p, m: (p, 0)),
            pl.BlockSpec((rows, q_width), lambda p, m: (p, 0)),
            padded,
            padded,
        ],
    )
    padded_shape = jax.ShapeDtypeStruct((key_heads, 2, total, PAIR), jnp.bfloat16)
    return pl.pallas_call(
        functools.partial(project_kernel, size=size, q_width=q_width, kv_width=kv_width),
        grid_spec=spec,
        out_shape=[
            jax.ShapeDtypeStruct((total, features), jnp.bfloat16),
            jax.ShapeDtypeStruct((total, q_width), jnp.bfloat16),
            padded_shape,
            padded_shape,
        ],
        compiler_params=PARAMS,
        cost_estimate=hint(2 * total * features * width // 16),
    )(me, *blocks, gain, own, other, own, other, cosine, sine)


def attend_kernel(
    me_ref, q_ref, k_ref, v_ref, wo_ref, wx_ref, o_ref, l_ref, *refs, size, heads, group
):
    part_refs, vt_ref = refs[:size], refs[size]
    rows = q_ref.shape[0]
    half = wo_ref.shape[0]
    mine = jnp.bitwise_xor(me_ref[0], pl.program_id(0))
    key_place = lax.broadcasted_iota(jnp.int32, (rows, rows), 0)
    query_place = lax.broadcasted_iota(jnp.int32, (rows, rows), 1)

    @pl.when(pl.program_id(0) == 0)
    def _():
        for head in range(heads // group):
            for side in range(2):
                vt_ref[head, side] = v_ref[head, side].T

    def one(span):
        keys = span * rows
        for pair in range(heads // 2):
            head = 2 * pair // group
            lanes = slice(pair * PAIR, (pair + 1) * PAIR)
            query = q_ref[:, lanes]
            acc = None
            inverse = []
            for side in range(2):
                diag = mm_nt(k_ref[head, side, keys : keys + rows, :], query)
                diag = jnp.where(key_place <= query_place, diag, -1e9)
                top = jnp.max(diag, axis=0, keepdims=True)
                if span:
                    body = mm_nt(k_ref[head, side, :keys, :], query)
                    top = jnp.maximum(top, jnp.max(body, axis=0, keepdims=True))
                diag = jnp.exp(diag - top)
                total = jnp.sum(diag, axis=0, keepdims=True)
                part = mm(vt_ref[head, side, :, keys : keys + rows], diag.astype(jnp.bfloat16))
                if span:
                    body = jnp.exp(body - top)
                    total = total + jnp.sum(body, axis=0, keepdims=True)
                    part = part + mm(vt_ref[head, side, :, :keys], body.astype(jnp.bfloat16))
                acc = part if acc is None else acc + part
                inverse.append(jnp.broadcast_to(1.0 / total, (HEAD_DIM, rows)))
                l_ref[2 * pair + side : 2 * pair + side + 1, :] = top + jnp.log(total)
            acc = acc * jnp.concatenate(inverse, axis=0)
            o_ref[:, lanes] = acc.T.astype(jnp.bfloat16)

    for span in range(size):
        pl.when(mine == span)(functools.partial(one, span))

    def project_out(ref):
        ref[:, :half] = mm_nt(o_ref[...], wo_ref[...]).astype(jnp.bfloat16)
        ref[:, half:] = mm_nt(o_ref[...], wx_ref[...]).astype(jnp.bfloat16)

    for step in range(size):
        pl.when(pl.program_id(0) == step)(functools.partial(project_out, part_refs[step]))


def attend(me, query, key_pad, value_pad, own, other, columns, size, group):
    total, width = query.shape
    features = 2 * own.shape[0]
    rows, heads = total // size, width // HEAD_DIM
    whole = pl.BlockSpec(key_pad.shape, lambda p, m: (0, 0, 0, 0), pipeline_mode=ONCE)
    spec = pltpu.PrefetchScalarGridSpec(
        num_scalar_prefetch=1,
        grid=(size,),
        in_specs=[pl.BlockSpec((rows, width), lambda p, m: (p, 0)), whole, whole]
        + [columns.spec("out", features // 2)] * 2,
        out_specs=[
            pl.BlockSpec((rows, width), lambda p, m: (p, 0)),
            pl.BlockSpec((heads, rows), lambda p, m: (0, p)),
        ]
        + [pl.BlockSpec((rows, features), lambda p, m: (0, 0))] * size,
        scratch_shapes=[pltpu.VMEM((heads // group, 2, PAIR, total), jnp.bfloat16)],
    )
    return pl.pallas_call(
        functools.partial(attend_kernel, size=size, heads=heads, group=group),
        grid_spec=spec,
        out_shape=[
            jax.ShapeDtypeStruct((total, width), jnp.bfloat16),
            jax.ShapeDtypeStruct((heads, total), jnp.float32),
        ]
        + [jax.ShapeDtypeStruct((rows, features), jnp.bfloat16)] * size,
        compiler_params=PARAMS,
        cost_estimate=hint(8 * heads * total * total * HEAD_DIM // 16),
    )(me, query, key_pad, value_pad, own, other)


def attend_back_kernel(
    me_ref, q_ref, l_ref, k_ref, v_ref, cos_ref, sin_ref, *refs, size, heads, group
):
    do_refs = refs[:size]
    out_ref, dk_ref, dv_ref, kt_ref, do_ref = refs[size:]
    rows = q_ref.shape[0]
    key_heads = heads // group
    step = pl.program_id(0)
    me = me_ref[0]
    mine = jnp.bitwise_xor(me, step)
    key_place = lax.broadcasted_iota(jnp.int32, (rows, rows), 0)
    query_place = lax.broadcasted_iota(jnp.int32, (rows, rows), 1)

    def rows_of(block):
        return pl.ds(pl.multiple_of(block * rows, rows), rows)

    @pl.when(step == 0)
    def _():
        dk_ref[...] = jnp.zeros_like(dk_ref)
        dv_ref[...] = jnp.zeros_like(dv_ref)
        for head in range(key_heads):
            for side in range(2):
                kt_ref[head, side] = k_ref[head, side].T

    def fetch(ref):
        do_ref[...] = ref[...]

    for block in range(size):
        pl.when(step == block)(functools.partial(fetch, do_refs[block]))

    def one(span):
        keys = span * rows
        parts = [(keys, keys + rows, True)] + ([(0, keys, False)] if span else [])
        cosine, sine = cos_ref[keys : keys + rows, :], sin_ref[keys : keys + rows, :]
        for pair in range(heads // 2):
            head = 2 * pair // group
            lanes = slice(pair * PAIR, (pair + 1) * PAIR)
            query, grad = q_ref[:, lanes], do_ref[:, lanes]
            acc = None
            for side in range(2):
                log_total = l_ref[2 * pair + side : 2 * pair + side + 1, :]
                inner = None
                kept = []
                for low, high, diagonal in parts:
                    probs = mm_nt(k_ref[head, side, low:high, :], query)
                    probs = jnp.exp(probs - log_total)
                    if diagonal:
                        probs = jnp.where(key_place <= query_place, probs, 0.0)
                    prob_grad = mm_nt(v_ref[head, side, low:high, :], grad)
                    dv_ref[head, side, low:high, :] += mm(probs.astype(jnp.bfloat16), grad)
                    term = jnp.sum(probs * prob_grad, axis=0, keepdims=True)
                    inner = term if inner is None else inner + term
                    kept.append((low, high, probs, prob_grad))
                for low, high, probs, prob_grad in kept:
                    score_grad = (probs * (prob_grad - inner)).astype(jnp.bfloat16)
                    dk_ref[head, side, low:high, :] += mm(score_grad, query)
                    part = mm(kt_ref[head, side, :, low:high], score_grad)
                    acc = part if acc is None else acc + part
            turned = turn(acc.T * SCALE, cosine, -sine)
            out_ref[rows_of(step), lanes] = turned.astype(jnp.bfloat16)

    for span in range(size):
        pl.when(mine == span)(functools.partial(one, span))

    @pl.when(step == size - 1)
    def _():
        first = lane_index(rows) < HEAD_DIM
        wanted = [(dk_ref, head, True) for head in range(key_heads)]
        wanted += [(dv_ref, head, False) for head in range(key_heads)]
        for span in range(size):
            place = slice(span * rows, (span + 1) * rows)
            cosine, sine = cos_ref[place, :], sin_ref[place, :]
            for block in range(len(wanted) // 2):
                halves, rotate = [], []
                for half in range(2):
                    ref, head, is_key = wanted[2 * block + half]
                    low, high = ref[head, 0, place, :], ref[head, 1, place, :]
                    if half:
                        halves.append(pltpu.roll(low, HEAD_DIM, 1) + high)
                    else:
                        halves.append(low + pltpu.roll(high, HEAD_DIM, 1))
                    rotate.append(is_key)
                value = jnp.where(first, halves[0], halves[1])
                if rotate[0] and rotate[1]:
                    value = turn(value, cosine, -sine)
                elif rotate[0]:
                    value = jnp.where(first, turn(value, cosine, -sine), value)
                start = heads * HEAD_DIM + block * PAIR
                target = rows_of(jnp.bitwise_xor(me, span))
                out_ref[target, start : start + PAIR] = value.astype(jnp.bfloat16)


def attend_back(
    me, query, log_total, key_pad, value_pad, cosine, sine, attended_grad, group
):
    total, width = query.shape
    size = len(attended_grad)
    rows, heads = total // size, width // HEAD_DIM
    key_heads = heads // group
    out_width = width + 2 * key_heads * HEAD_DIM
    whole = pl.BlockSpec(key_pad.shape, lambda p, m: (0, 0, 0, 0), pipeline_mode=ONCE)
    table = pl.BlockSpec((total, PAIR), lambda p, m: (0, 0), pipeline_mode=ONCE)
    spec = pltpu.PrefetchScalarGridSpec(
        num_scalar_prefetch=1,
        grid=(size,),
        in_specs=[
            pl.BlockSpec((rows, width), lambda p, m: (p, 0)),
            pl.BlockSpec((heads, rows), lambda p, m: (0, p)),
            whole,
            whole,
            table,
            table,
        ]
        + [pl.BlockSpec((rows, width), lambda p, m: (0, 0), pipeline_mode=ONCE)] * size,
        out_specs=pl.BlockSpec((total, out_width), lambda p, m: (0, 0)),
        scratch_shapes=[
            pltpu.VMEM(key_pad.shape, jnp.float32),
            pltpu.VMEM(key_pad.shape, jnp.float32),
            pltpu.VMEM((key_heads, 2, PAIR, total), jnp.bfloat16),
            pltpu.VMEM((rows, width), jnp.bfloat16),
        ],
    )
    return pl.pallas_call(
        functools.partial(attend_back_kernel, size=size, heads=heads, group=group),
        grid_spec=spec,
        out_shape=jax.ShapeDtypeStruct((total, out_width), jnp.bfloat16),
        compiler_params=PARAMS,
        cost_estimate=hint(20 * heads * total * total * HEAD_DIM),
    )(me, query, log_total, key_pad, value_pad, cosine, sine, *attended_grad)


def grouped(arrays, counts):
    arrays = iter(arrays)
    return [[next(arrays) for _ in range(count)] for count in counts]


def mlp_kernel(*refs, n_counts, e_counts, adds):
    size = len(n_counts)
    pieces = sum(n_counts) + sum(e_counts)
    n_refs = grouped(refs, n_counts)
    e_refs = grouped(refs[sum(n_counts) :], e_counts)
    gate_o, up_o, down_o, gate_x, up_x, down_x = refs[pieces : pieces + 6]
    y_ref, n_ref, e_ref = refs[-3:]
    dn_refs = refs[-3 - size if adds else -4 : -3]
    dg_ref, du_ref, h_ref = refs[-6 - size if adds else -7 :][:3]
    half = gate_o.shape[0]

    def fetch(step):
        for target, sources in ((n_ref, n_refs[step]), (e_ref, e_refs[step])):
            low = 0
            for source in sources:
                high = low + source.shape[0]
                target[low:high] = source[...]
                low = high

    for step in range(size):
        pl.when(pl.program_id(0) == step)(functools.partial(fetch, step))
    gate = mm(n_ref[:, :half], gate_o[...]) + mm(n_ref[:, half:], gate_x[...])
    up = mm(n_ref[:, :half], up_o[...]) + mm(n_ref[:, half:], up_x[...])
    grad = mm(e_ref[:, :half], down_o[...]) + mm(e_ref[:, half:], down_x[...])
    sigma = jax.nn.sigmoid(gate)
    silu = gate * sigma
    hidden = (silu * up).astype(jnp.bfloat16)
    gate_grad = (grad * up * sigma * (1.0 + gate * (1.0 - sigma))).astype(jnp.bfloat16)
    up_grad = (grad * silu).astype(jnp.bfloat16)
    dg_ref[...] = gate_grad
    du_ref[...] = up_grad
    h_ref[...] = hidden
    for part, gate_w, up_w, down_w in ((0, gate_o, up_o, down_o), (1, gate_x, up_x, down_x)):
        lanes = slice(part * half, (part + 1) * half)
        dn = mm_nt(gate_grad, gate_w[...]) + mm_nt(up_grad, up_w[...])
        y = mm_nt(hidden, down_w[...])
        if adds:
            dn = dn + refs[pieces + 6][:, lanes].astype(jnp.float32)
            y = y + refs[pieces + 7][:, lanes].astype(jnp.float32)
        y_ref[:, lanes] = y.astype(jnp.bfloat16)
        dn = dn.astype(jnp.bfloat16)

        def store(ref):
            ref[:, lanes] = dn

        if adds:
            for step in range(size):
                pl.when(pl.program_id(0) == step)(functools.partial(store, dn_refs[step]))
        else:
            store(dn_refs[0])


def mlp(tokens, cot, own, other, earlier):
    size = len(tokens)
    rows, features = tokens[0][0].shape
    half, units = own.shape[0], own.shape[1] // 3
    total = rows * size
    fixed = lambda p: (0, 0)
    moving = lambda p: (p, 0)
    wide = pl.BlockSpec((rows, features), moving)
    sums = jax.ShapeDtypeStruct((total, features), jnp.bfloat16)
    dn_specs, dn_shapes = [wide], [sums]
    if earlier:
        dn_specs = [pl.BlockSpec((rows, features), fixed)] * size
        dn_shapes = [jax.ShapeDtypeStruct((rows, features), jnp.bfloat16)] * size
    pieces = sum(tokens, []) + sum(cot, [])
    thirds = [
        pl.BlockSpec((half, units), lambda p, t=t: (0, t), pipeline_mode=ONCE) for t in range(3)
    ]
    return pl.pallas_call(
        functools.partial(
            mlp_kernel,
            n_counts=[len(group) for group in tokens],
            e_counts=[len(group) for group in cot],
            adds=bool(earlier),
        ),
        grid=(size,),
        in_specs=[pl.BlockSpec(piece.shape, fixed, pipeline_mode=ONCE) for piece in pieces]
        + thirds * 2
        + [wide] * len(earlier),
        out_specs=[pl.BlockSpec((rows, units), moving)] * 3 + dn_specs + [wide],
        out_shape=[jax.ShapeDtypeStruct((total, units), jnp.bfloat16)] * 3 + dn_shapes + [sums],
        scratch_shapes=[pltpu.VMEM((rows, features), jnp.bfloat16)] * 2,
        compiler_params=PARAMS,
        cost_estimate=hint(12 * total * features * units),
    )(*pieces, own, own, own, other, other, other, *earlier)


def add_refs(refs):
    total = refs[0][...].astype(jnp.float32)
    for ref in refs[1:]:
        total = total + ref[...].astype(jnp.float32)
    return total


def store_by_device(out_ref, values, core, chips):
    width = values.shape[1] // (2 * chips)
    for chip in range(chips):
        own = values[:, chip * width : (chip + 1) * width]
        other = values[:, (chips + chip) * width : (chips + chip + 1) * width]
        low = 2 * chip * width
        out_ref[:, low : low + width] = jnp.where(core == 0, own, other)
        out_ref[:, low + width : low + 2 * width] = jnp.where(core == 0, other, own)


def middle_kernel(*refs):
    x_ref, gain_ref, middle_ref, normed_ref = refs[-4:]
    values = x_ref[...].astype(jnp.float32) + add_refs(refs[:-4])
    middle_ref[...] = values
    normed_ref[...] = (values * rms_scale(values) * gain_ref[...]).astype(jnp.bfloat16)


def input_back_kernel(core_ref, *refs, chips):
    x_ref, before_ref, gain_ref, out_ref = refs[-4:]
    values = x_ref[...].astype(jnp.float32)
    inner = add_refs(refs[:-4]) * gain_ref[...]
    scale = rms_scale(values)
    mean = jnp.mean(inner * values, axis=-1, keepdims=True)
    result = before_ref[...] + scale * inner - values * (scale * scale * scale) * mean
    store_by_device(out_ref, result, core_ref[0], chips)


def output_kernel(core_ref, *refs, chips):
    middle_ref, out_ref = refs[-2:]
    values = middle_ref[...] + add_refs(refs[:-2])
    store_by_device(out_ref, values.astype(jnp.bfloat16), core_ref[0], chips)


def row_call(body, dtypes, arrays, core=None):
    rows, features = arrays[0].shape
    steps = 2
    wide = pl.BlockSpec((rows // steps, features), lambda i, *_: (i, 0))
    row = pl.BlockSpec((1, features), lambda i, *_: (0, 0))
    scalars = [] if core is None else [jnp.full((1,), core, jnp.int32)]
    return pl.pallas_call(
        body,
        grid_spec=pltpu.PrefetchScalarGridSpec(
            num_scalar_prefetch=len(scalars),
            grid=(steps,),
            in_specs=[row if array.shape[0] == 1 else wide for array in arrays],
            out_specs=[wide] * len(dtypes),
        ),
        out_shape=[jax.ShapeDtypeStruct((rows, features), dtype) for dtype in dtypes],
        compiler_params=PARAMS,
        cost_estimate=hint(0),
    )(*scalars, *arrays)


def unpack_kernel(sum_ref, q_ref, k_ref, v_ref, out_ref):
    q_width, kv_width = q_ref.shape[1], k_ref.shape[1]
    values = sum_ref[...].astype(jnp.float32)
    q_ref[...] = values[:, :q_width]
    kv = values[:, q_width : q_width + 2 * kv_width]
    k_ref[...] = kv[:, :kv_width]
    v_ref[...] = kv[:, kv_width:]
    out_ref[...] = values[:, q_width + 2 * kv_width :].T


def unpack(sums, q_width, kv_width):
    rows = sums.shape[0]
    widths = [(rows, q_width), (rows, kv_width), (rows, kv_width), (q_width, rows)]
    return pl.pallas_call(
        unpack_kernel,
        out_shape=[jax.ShapeDtypeStruct(shape, jnp.float32) for shape in widths],
        compiler_params=PARAMS,
        cost_estimate=hint(0),
    )(sums)


def middle_back_kernel(*refs, parts, size):
    n_refs, refs = refs[:parts], refs[parts:]
    x_ref, e_ref, gain_ref, refs = refs[0], refs[1], refs[2], refs[3:]
    own_refs, other_refs, refs = refs[:size], refs[size : 2 * size], refs[2 * size :]
    grad_ref, branch_ref, part_ref, do_refs = refs[0], refs[1], refs[2], refs[3:]
    half = own_refs[0].shape[0]
    grad = add_refs(n_refs)
    values = x_ref[...]
    scale = rms_scale(values)
    result, part = norm_back(grad, values, scale, gain_ref[...])

    @pl.when(pl.program_id(0) == 0)
    def _():
        part_ref[...] = jnp.zeros_like(part_ref)

    part_ref[...] += part[None, :]
    result = result + e_ref[...].astype(jnp.float32)
    grad_ref[...] = result
    branch = result.astype(jnp.bfloat16)
    branch_ref[...] = branch
    for own, other, do_ref in zip(own_refs, other_refs, do_refs):
        do = mm(branch[:, :half], own[...]) + mm(branch[:, half:], other[...])
        do_ref[...] = do.astype(jnp.bfloat16)


def middle_back(arrived, middle, cot, gain, own, other):
    parts, size = len(arrived), len(own)
    rows, features = middle.shape
    width = own[0].shape[1]
    steps = 2
    wide = pl.BlockSpec((rows // steps, features), lambda i: (i, 0))
    narrow = pl.BlockSpec((rows // steps, width), lambda i: (i, 0))
    row = pl.BlockSpec((1, features), lambda i: (0, 0))
    weight = pl.BlockSpec((features // 2, width), lambda i: (0, 0), pipeline_mode=ONCE)
    grad, branch, part, *do = pl.pallas_call(
        functools.partial(middle_back_kernel, parts=parts, size=size),
        grid=(steps,),
        in_specs=[wide] * parts + [wide, wide, row] + [weight] * (2 * size),
        out_specs=[wide, wide, row] + [narrow] * size,
        out_shape=[
            jax.ShapeDtypeStruct((rows, features), jnp.float32),
            jax.ShapeDtypeStruct((rows, features), jnp.bfloat16),
            jax.ShapeDtypeStruct((1, features), jnp.float32),
        ]
        + [jax.ShapeDtypeStruct((rows, width), jnp.bfloat16)] * size,
        compiler_params=PARAMS,
        cost_estimate=hint(2 * rows * features * width * size),
    )(*arrived, middle, cot, gain, *own, *other)
    return grad, branch, part[0], do


def column_grad(blocks, other, mine, theirs):
    total = mm_tn(other[...], theirs[...])
    low = 0
    for block in blocks:
        high = low + block.shape[0]
        total = total + mm_tn(block[...], mine[low:high, :])
        low = high
    return total


def grad_kernel(*refs, n_count, e_count):
    n_refs, refs = refs[:n_count], refs[n_count:]
    e_refs, refs = refs[:e_count], refs[e_count:]
    n_other, e_other = refs[:2]
    acts, out_ref = refs[2:-1], refs[-1]
    units = acts[0].shape[1]
    for third in range(3):
        blocks, other = (e_refs, e_other) if third == 2 else (n_refs, n_other)
        grad = column_grad(blocks, other, acts[third], acts[third + 3])
        out_ref[0, :, third * units : (third + 1) * units] = grad.astype(jnp.bfloat16)


def mlp_grads(chips, tokens, cot, tokens_other, cot_other, mine, theirs):
    tokens, cot = sum(tokens, []), sum(cot, [])
    features = tokens[0].shape[1]
    total, units = mine[0].shape
    depth = features // (2 * chips)
    long = pl.BlockSpec((total, depth), lambda b: (0, b))
    fixed = pl.BlockSpec((total, units), lambda b: (0, 0), pipeline_mode=ONCE)
    return pl.pallas_call(
        functools.partial(grad_kernel, n_count=len(tokens), e_count=len(cot)),
        grid=(chips,),
        in_specs=[pl.BlockSpec((p.shape[0], depth), lambda b: (0, b)) for p in tokens + cot]
        + [long, long]
        + [fixed] * 6,
        out_specs=pl.BlockSpec((1, depth, 3 * units), lambda b: (b, 0, 0)),
        out_shape=jax.ShapeDtypeStruct((chips, depth, 3 * units), jnp.bfloat16),
        compiler_params=PARAMS,
        cost_estimate=hint(6 * total * features * units),
    )(*tokens, *cot, tokens_other, cot_other, *mine, *theirs)


def attn_grad_kernel(*refs, size):
    e_refs = refs[2 : 2 + size]
    n_ref, n_other = refs[:2]
    e_other, d_ref, d_other, o_ref, o_other, q_ref, kv_ref, g1_ref, g2_ref = refs[2 + size : -2]
    out_ref, gain_ref = refs[-2:]
    width, out_width = d_ref.shape[1], o_ref.shape[1]
    grad = column_grad([n_ref], n_other, d_ref, d_other)
    out_ref[0, :, :width] = grad.astype(jnp.bfloat16)
    out_grad = column_grad(e_refs, e_other, o_ref, o_other)
    out_ref[0, :, width : width + out_width] = out_grad.astype(jnp.bfloat16)
    cut = q_ref.shape[1]
    first = jnp.sum(grad[:, :cut] * q_ref[...].astype(jnp.float32), axis=1, keepdims=True)
    first += jnp.sum(grad[:, cut:] * kv_ref[...].astype(jnp.float32), axis=1, keepdims=True)
    first = first / g1_ref[...]
    lane = lane_index(grad.shape[0])
    gain_ref[0] = jnp.where(lane == 0, first, g2_ref[...])


def attn_grads(
    chips, tokens, branch, mine, theirs, weights, columns, gain_one, gain_two_part
):
    size = len(branch)
    qkv_grad, attended = mine
    tokens_other, branch_other, qkv_other, attended_other = theirs
    total, features = tokens.shape
    rows = total // size
    width, out_width = qkv_grad.shape[1], attended.shape[1]
    depth = features // (2 * chips)
    column = lambda b: (0, b)
    row = lambda b: (b, 0)
    long = pl.BlockSpec((total, depth), column)
    fixed = lambda array: pl.BlockSpec(array.shape, lambda b: (0, 0), pipeline_mode=ONCE)
    place = lambda b: (b, 0, 0)
    return pl.pallas_call(
        functools.partial(attn_grad_kernel, size=size),
        grid=(chips,),
        in_specs=[long, long]
        + [pl.BlockSpec((rows, depth), column)] * size
        + [long]
        + [fixed(qkv_grad)] * 2
        + [fixed(attended)] * 2
        + [
            columns.spec("q", depth, lambda b=None: b),
            columns.spec("kv", depth, lambda b=None: b),
            pl.BlockSpec((depth, 1), row),
            pl.BlockSpec((depth, 1), row),
        ],
        out_specs=[
            pl.BlockSpec((1, depth, width + out_width), place),
            pl.BlockSpec((1, depth, PAIR), place),
        ],
        out_shape=[
            jax.ShapeDtypeStruct((chips, depth, width + out_width), jnp.bfloat16),
            jax.ShapeDtypeStruct((chips, depth, PAIR), jnp.float32),
        ],
        compiler_params=PARAMS,
        cost_estimate=hint(2 * total * features * (width + out_width)),
    )(
        tokens,
        tokens_other,
        *branch,
        branch_other,
        qkv_grad,
        qkv_other,
        attended,
        attended_other,
        weights,
        weights,
        gain_one,
        gain_two_part,
    )


def input_grad_kernel(d_ref, qo_ref, qx_ref, kvo_ref, kvx_ref, *out_refs):
    half, cut = qo_ref.shape

    def one(ref):
        query, rest = d_ref[:, :cut], d_ref[:, cut:]
        own = mm_nt(query, qo_ref[...]) + mm_nt(rest, kvo_ref[...])
        other = mm_nt(query, qx_ref[...]) + mm_nt(rest, kvx_ref[...])
        ref[:, :half] = own.astype(jnp.bfloat16)
        ref[:, half:] = other.astype(jnp.bfloat16)

    for step, ref in enumerate(out_refs):
        pl.when(pl.program_id(0) == step)(functools.partial(one, ref))


def input_grad(qkv_grad, own, other, columns, size):
    total, width = qkv_grad.shape
    features = 2 * own.shape[0]
    rows = total // size
    fixed = lambda i: (0, 0)
    weights = [columns.spec(part, own.shape[0]) for part in ("q", "q", "kv", "kv")]
    return pl.pallas_call(
        input_grad_kernel,
        grid=(size,),
        in_specs=[pl.BlockSpec((rows, width), lambda i: (i, 0))] + weights,
        out_specs=[pl.BlockSpec((rows, features), fixed)] * size,
        out_shape=[jax.ShapeDtypeStruct((rows, features), jnp.bfloat16)] * size,
        compiler_params=PARAMS,
        cost_estimate=hint(2 * total * features * width),
    )(qkv_grad, own, other, own, other)


def swap(values, step):
    size = lax.axis_size("tensor")
    return lax.ppermute(values, "tensor", [(i, i ^ step) for i in range(size)])


def spread(values):
    return [values] + [swap(values, step) for step in range(1, lax.axis_size("tensor"))]


def send_blocks(blocks):
    return [blocks[0]] + [swap(block, step + 1) for step, block in enumerate(blocks[1:])]


def spread_around(values, held):
    if lax.axis_size("tensor") != 4:
        blocks = spread(values)
        first, held = barrier((blocks[1], held))
        return [[blocks[0]], [first]] + [[block] for block in blocks[2:]], held
    half = values.shape[0] // 2
    top, bottom = values[:half], values[half:]
    x_bottom, y_top = swap(bottom, 1), swap(top, 2)
    x_bottom, y_top, top, bottom, held = barrier((x_bottom, y_top, top, bottom, held))
    far = [swap(y_top, 1), swap(x_bottom, 2)]
    x_top, y_bottom = swap(top, 1), swap(bottom, 2)
    return [[values], [x_top, x_bottom], [y_top, y_bottom], far], held


def merge_kernel(x_ref, y_ref, top_ref, bottom_ref, x_out, y_out):
    half = top_ref.shape[0]
    x_out[:half] = x_ref[:half]
    x_out[half:] = add_refs([x_ref.at[half:], bottom_ref]).astype(jnp.bfloat16)
    y_out[:half] = add_refs([y_ref.at[:half], top_ref]).astype(jnp.bfloat16)
    y_out[half:] = y_ref[half:]


def send_sum(blocks, held=()):
    if len(blocks) != 4:
        return send_blocks(blocks), held
    own, near_x, near_y, far = blocks
    half = far.shape[0] // 2
    top, bottom = swap(far[:half], 1), swap(far[half:], 2)
    near_x, near_y = pl.pallas_call(
        merge_kernel,
        out_shape=[jax.ShapeDtypeStruct(near_x.shape, near_x.dtype)] * 2,
        compiler_params=PARAMS,
        cost_estimate=hint(0),
    )(near_x, near_y, top, bottom)
    near_x, near_y, held = barrier((near_x, near_y, held))
    return [own, swap(near_x, 1), swap(near_y, 2)], held


def add_up(blocks):
    total = blocks[0].astype(jnp.float32)
    for block in blocks[1:]:
        total = total + block.astype(jnp.float32)
    return total


def cross(values):
    count = lax.axis_size("dp")
    return lax.ppermute(values, "dp", [(i, i ^ 1) for i in range(count)])


def tables(positions):
    freqs = ROPE_BASE ** (-jnp.arange(0, HEAD_DIM, 2).astype(jnp.float32) / HEAD_DIM)
    angles = positions.astype(jnp.float32)[:, None] * freqs[None, :]
    cosine, sine = jnp.cos(angles), jnp.sin(angles)
    return (
        jnp.concatenate([cosine] * 4, axis=1),
        jnp.concatenate([-sine, sine, -sine, sine], axis=1),
    )


def chip_lines():
    count = lax.axis_size("dp")
    return [list(range(core, count, 2)) for core in range(2)]


def gather(values):
    return lax.all_gather(values, "dp", axis=0, tiled=True, axis_index_groups=chip_lines())


def scatter(values):
    total = lax.psum_scatter(
        values, "dp", scatter_dimension=0, tiled=True, axis_index_groups=chip_lines()
    )
    return total[0]


def along(values, step):
    count = lax.axis_size("dp")
    return lax.ppermute(values, "dp", [(i, (i + 2 * step) % count) for i in range(count)])


def line_parts(parts):
    chips = lax.axis_size("dp") // 2
    chip = lax.axis_index("dp") // 2
    blocks = [lax.dynamic_index_in_dim(parts, chip, 0, keepdims=False)]
    for step in range(1, chips):
        sent = lax.dynamic_index_in_dim(parts, (chip + step) % chips, 0, keepdims=False)
        blocks.append(along(sent, step))
    return blocks


def own_part(values):
    size = lax.axis_size("tensor")
    me = lax.axis_index("tensor")
    blocks = values.reshape((size, -1) + values.shape[1:])
    own = lax.dynamic_index_in_dim(blocks, me, 0, keepdims=False)
    for step in range(1, size):
        sent = lax.dynamic_index_in_dim(blocks, me ^ step, 0, keepdims=False)
        own = own + swap(sent, step)
    return own


def stack_kernel(*refs):
    low = 0
    for ref in refs[:-1]:
        high = low + ref.shape[0]
        refs[-1][low:high, :] = ref[...]
        low = high


def other_half(blocks):
    features = blocks[0].shape[1]
    shape = (sum(block.shape[0] for block in blocks), features // 2)
    halves = pl.pallas_call(
        stack_kernel,
        grid=(1,),
        in_specs=[pl.BlockSpec((b.shape[0], features // 2), lambda i: (0, 1)) for b in blocks],
        out_specs=pl.BlockSpec(shape, lambda i: (0, 0)),
        out_shape=jax.ShapeDtypeStruct(shape, blocks[0].dtype),
        compiler_params=PARAMS,
        cost_estimate=hint(0),
    )(*blocks)
    return cross(halves)


def feature_blocks(values):
    width = values.shape[-1] // lax.axis_size("dp")
    return [values[..., low : low + width] for low in range(0, values.shape[-1], width)]


def by_core(values, core):
    blocks = feature_blocks(values)
    pairs = list(zip(blocks[0::2], blocks[1::2]))
    own = [jnp.where(core == 0, even, odd) for even, odd in pairs]
    other = [jnp.where(core == 0, odd, even) for even, odd in pairs]
    return jnp.concatenate(own + other, axis=-1)


def per_device(
    hidden_in,
    gain_attn,
    w_query,
    w_key,
    w_value,
    w_out,
    gain_mlp,
    w_gate,
    w_up,
    w_down,
    positions,
    cotangent,
):
    size = lax.axis_size("tensor")
    chips = lax.axis_size("dp") // 2
    me = lax.axis_index("tensor")
    me_array = jnp.full((1,), me, jnp.int32)
    core = lax.axis_index("dp") % 2
    q_width, kv_width = w_query.shape[1], w_key.shape[1]
    group = q_width // kv_width
    units = w_down.shape[0] // 2
    half = hidden_in.shape[1] // 2

    columns = Columns(q_width, kv_width)
    attn_shard = jnp.concatenate([w_query, w_out.T, w_key, w_value], axis=1)
    attn_shard, hidden_in, gain_attn = barrier((attn_shard, hidden_in, gain_attn))
    attn_own = gather(attn_shard)
    residual = by_core(hidden_in, core)
    blocks_in = spread(residual)
    gains = lax.all_gather(jnp.stack([gain_attn, gain_mlp]), "dp", axis=1, tiled=True)
    gains = by_core(gains, core).astype(jnp.float32)
    cosine, sine = tables(positions)
    cotangent = by_core(cotangent, core)
    down_t = w_down.T
    shares = []
    for part in range(2):
        cut = slice(part * units, (part + 1) * units)
        shares.append(jnp.concatenate([w_gate[:, cut], w_up[:, cut], down_t[:, cut]], axis=1))
    shares, attn_own, blocks_in, cosine, sine, gains, cotangent = barrier(
        (shares, attn_own, blocks_in, cosine, sine, gains, cotangent)
    )
    mlp_own = [gather(share) for share in shares]
    cot_blocks = spread(cotangent)
    gain_one, gain_two = gains[0], gains[1]
    attn = (attn_own, cross(attn_own))

    tokens_one, query, key_pad, value_pad = project(
        me_array, blocks_in, gain_one[None, :], *attn, cosine, sine, columns
    )
    attended, log_total, *parts = attend(
        me_array, query, key_pad, value_pad, *attn, columns, size, group
    )
    parts, cot_blocks, tokens_one, attended = barrier((parts, cot_blocks, tokens_one, attended))
    arrived, _ = send_sum(parts)
    cot_other = other_half(cot_blocks)
    cot_blocks = [[block] for block in cot_blocks]
    early = (cross(tokens_one[:, half:]), cross(attended))
    arrived, cot_other, early = barrier((arrived, cot_other, early))
    out_t = [w[:, q_width : 2 * q_width] for w in attn]
    middle, normed_two = row_call(
        middle_kernel, [jnp.float32, jnp.bfloat16], [*arrived, residual, gain_two[None, :]]
    )
    tokens_two, own_share = spread_around(normed_two, mlp_own[0])
    weights = (own_share, cross(own_share))
    tokens_two, weights, out_own = barrier((tokens_two, weights, out_t[0]))
    tokens_other = other_half(sum(tokens_two, []))
    *acts, dn_part, y_part = mlp(tokens_two, cot_blocks, *weights, ())
    out_blocks = spread(out_own)
    acts, tokens_other = barrier((acts, tokens_other))
    acts_other = [cross(act) for act in acts]
    grads_one = mlp_grads(
        chips, tokens_two, cot_blocks, tokens_other, cot_other, acts, acts_other
    )
    grads_one, own_share = barrier((grads_one, mlp_own[1]))
    sums_one = scatter(grads_one)
    weights = (own_share, cross(own_share))
    *acts, y_part = mlp(tokens_two, cot_blocks, *weights, (dn_part, y_part))
    acts, dn_part = acts[:3], acts[3:]
    acts, dn_part, out_blocks = barrier((acts, dn_part, out_blocks))
    acts_other = [cross(act) for act in acts]
    arrived, acts = send_sum(dn_part, acts)
    out_other = [out_t[1]] + [cross(block) for block in out_blocks[1:]]
    grads_two = mlp_grads(
        chips, tokens_two, cot_blocks, tokens_other, cot_other, acts, acts_other
    )
    grads_two, arrived, out_other, y_part = barrier((grads_two, arrived, out_other, y_part))
    y_blocks = list(y_part.reshape((size, -1) + y_part.shape[1:]))
    y_early = [swap(y_blocks[step], step) for step in range(1, 3)]
    sums_two = scatter(grads_two)
    middle_grad, branch, gain_two_part, do_blocks = middle_back(
        arrived, middle, cotangent, gain_two[None, :], out_blocks, out_other
    )
    do_blocks = send_blocks(do_blocks)
    gain_two_other = cross(gain_two_part[half:])
    do_blocks, branch, gain_two_other, y_blocks, y_early = barrier(
        (do_blocks, branch, gain_two_other, y_blocks, y_early)
    )
    branch_blocks = spread(branch)
    qkv_grad = attend_back(
        me_array, query, log_total, key_pad, value_pad, cosine, sine, do_blocks, group
    )
    qkv_grad, sums_one = barrier((qkv_grad, sums_one))
    qkv_other = cross(qkv_grad)
    normed_part = input_grad(qkv_grad, *attn, columns, size)
    branch_blocks, normed_part = barrier((branch_blocks, normed_part))
    branch_other = other_half(branch_blocks)
    tokens_other, attended_other = early
    grads, gain_parts = attn_grads(
        chips,
        tokens_one,
        branch_blocks,
        (qkv_grad, attended),
        (tokens_other, branch_other, qkv_other, attended_other),
        attn_own,
        columns,
        gain_one[:half, None],
        (gain_two_part[:half] + gain_two_other)[:, None],
    )
    arrived, grads = send_sum(normed_part, grads)
    attn_sums = scatter(grads)
    gain_sums = add_up(line_parts(gain_parts[:, :, :2]))
    arrived, y_blocks, sums_two = barrier((arrived, y_blocks, sums_two))
    y_late = [swap(y_blocks[step], step) for step in range(3, size)]
    gain_sums = own_part(gain_sums)
    (grad_in,) = row_call(
        functools.partial(input_back_kernel, chips=chips),
        [jnp.float32],
        [*arrived, residual, middle_grad, gain_one[None, :]],
        core,
    )
    shares = [share.astype(jnp.float32) for share in (sums_one, sums_two)]
    grad_gate = jnp.concatenate([h[:, :units] for h in shares], axis=1)
    grad_up = jnp.concatenate([h[:, units : 2 * units] for h in shares], axis=1)
    grad_down = jnp.concatenate([h[:, 2 * units :].T for h in shares], axis=0)
    y_late, grad_in, gain_sums, grad_gate, grad_up, grad_down = barrier(
        (y_late, grad_in, gain_sums, grad_gate, grad_up, grad_down)
    )
    (out,) = row_call(
        functools.partial(output_kernel, chips=chips),
        [jnp.bfloat16],
        [y_blocks[0], *y_early, *y_late, middle],
        core,
    )
    out, attn_sums = barrier((out, attn_sums))
    grad_query, grad_key, grad_value, grad_out = unpack(attn_sums, q_width, kv_width)
    return (
        out,
        grad_in,
        gain_sums[:, 0],
        grad_query,
        grad_key,
        grad_value,
        grad_out,
        gain_sums[:, 1],
        grad_gate,
        grad_up,
        grad_down,
    )


def solution(mesh):
    return jax.shard_map(
        per_device,
        mesh=mesh,
        in_specs=(
            P(("dp", "tensor"), None),
            P("dp"),
            P("dp", "tensor"),
            P("dp", "tensor"),
            P("dp", "tensor"),
            P("tensor", "dp"),
            P("dp"),
            P("dp", "tensor"),
            P("dp", "tensor"),
            P("tensor", "dp"),
            P("dp"),
            P(("dp", "tensor"), None),
        ),
        out_specs=(
            P(("dp", "tensor"), None),
            P(("dp", "tensor"), None),
            P(("dp", "tensor")),
            P("dp", "tensor"),
            P("dp", "tensor"),
            P("dp", "tensor"),
            P("tensor", "dp"),
            P(("dp", "tensor")),
            P("dp", "tensor"),
            P("dp", "tensor"),
            P("tensor", "dp"),
        ),
        check_vma=False,
    )
```

```python
import functools
import math

import jax
import jax.numpy as jnp
from jax import lax
from jax.experimental import pallas as pl
from jax.experimental.pallas import tpu as pltpu
from jax.sharding import PartitionSpec as P

HEAD_DIM = 64
PAIR = 2 * HEAD_DIM
SEQ_LEN = 1024


EPS = 1e-05
ROPE_BASE = 500000.0
SCALE = 1.0 / math.sqrt(HEAD_DIM)
PARAMS = pltpu.CompilerParams(vmem_limit_bytes=58 * 2**20)
ONCE = pl.Buffered(1)

barrier = lax.optimization_barrier


def hint(flops):
    return pl.CostEstimate(flops=flops, bytes_accessed=0, transcendentals=0)


def rms_scale(values):
    return lax.rsqrt(jnp.mean(values * values, axis=-1, keepdims=True) + EPS)


def norm_back(grad, values, scale, gain):
    inner = grad * gain
    cubed = scale * scale * scale
    result = scale * inner - values * cubed * jnp.mean(inner * values, axis=-1, keepdims=True)
    return (result, jnp.sum(grad * values * scale, axis=0))


def mm(left, right):
    return jnp.dot(left, right, preferred_element_type=jnp.float32)


def mm_nt(left, right):
    return lax.dot_general(left, right, (((1,), (1,)), ((), ())), preferred_element_type=jnp.float32)


def mm_tn(left, right):
    return lax.dot_general(left, right, (((0,), (0,)), ((), ())), preferred_element_type=jnp.float32)


def lane_index(rows):
    return lax.broadcasted_iota(jnp.int32, (rows, PAIR), 1)


def turn(pair, cosine, sine):
    lower = lane_index(pair.shape[0]) % HEAD_DIM < HEAD_DIM // 2
    other = jnp.where(
        lower, pltpu.roll(pair, PAIR - HEAD_DIM // 2, 1), pltpu.roll(pair, HEAD_DIM // 2, 1)
    )
    return pair * cosine + other * sine


def project_kernel(place_ref, *refs, size, q_width, kv_width):
    x_refs = refs[:size]
    gain_ref, qo_ref, qx_ref, kvo_ref, kvx_ref, cos_ref, sin_ref = refs[size:-4]
    n_ref, q_ref, k_ref, v_ref = refs[-4:]
    rows = q_ref.shape[0]
    half = qo_ref.shape[0]

    def one(x_ref):
        x = x_ref[...].astype(jnp.float32)
        normed = (x * rms_scale(x) * gain_ref[...]).astype(jnp.bfloat16)
        n_ref[...] = normed
        cosine, sine = cos_ref[...], sin_ref[...]
        own, other = normed[:, :half], normed[:, half:]
        lin = mm(own, qo_ref[...]) + mm(other, qx_ref[...])
        for low in range(0, q_width, PAIR):
            query = turn(lin[:, low : low + PAIR], cosine, sine).astype(jnp.bfloat16)
            q_ref[:, low : low + PAIR] = query * jnp.bfloat16(SCALE)
        lin = mm(own, kvo_ref[...]) + mm(other, kvx_ref[...])
        first = lane_index(rows) < HEAD_DIM
        for ref, start, rotate in ((k_ref, 0, True), (v_ref, kv_width, False)):
            for head in range(kv_width // HEAD_DIM):
                low = start + head * HEAD_DIM
                block = lin[:, low // PAIR * PAIR : low // PAIR * PAIR + PAIR]
                if rotate:
                    block = turn(block, cosine, sine)
                moved = pltpu.roll(block, HEAD_DIM, 1)
                if low % PAIR:
                    block, moved = moved, block
                ref[head, 0] = jnp.where(first, block, 0.0).astype(jnp.bfloat16)
                ref[head, 1] = jnp.where(first, 0.0, moved).astype(jnp.bfloat16)

    for step in range(size):
        pl.when(pl.program_id(0) == step)(functools.partial(one, x_refs[step]))


class Columns:
    def __init__(self, q_width, kv_width):
        self.q_width, self.kv_width = q_width, kv_width

    def spec(self, part, rows, place=lambda *_: 0):
        width, start = {
            "q": (self.q_width, 0),
            "out": (self.q_width, self.q_width),
            "kv": (2 * self.kv_width, 2 * self.q_width),
        }[part]
        index = start // width
        mode = {"pipeline_mode": ONCE} if place() == 0 else {}
        return pl.BlockSpec((rows, width), lambda *grid: (place(*grid), index), **mode)


def project(me, blocks, gain, own, other, cosine, sine, columns):
    size = len(blocks)
    rows, features = blocks[0].shape
    total = rows * size
    q_width, kv_width = columns.q_width, columns.kv_width
    key_heads = kv_width // HEAD_DIM
    width = q_width + 2 * kv_width
    half = features // 2
    fixed = lambda p, m: (0, 0)
    placed = lambda p, m: (jnp.bitwise_xor(p, m[0]), 0)
    padded = pl.BlockSpec(
        (key_heads, 2, rows, PAIR), lambda p, m: (0, 0, jnp.bitwise_xor(p, m[0]), 0)
    )
    spec = pltpu.PrefetchScalarGridSpec(
        num_scalar_prefetch=1,
        grid=(size,),
        in_specs=[pl.BlockSpec((rows, features), fixed, pipeline_mode=ONCE)] * size
        + [
            pl.BlockSpec((1, features), fixed),
            columns.spec("q", half),
            columns.spec("q", half),
            columns.spec("kv", half),
            columns.spec("kv", half),
            pl.BlockSpec((rows, PAIR), placed),
            pl.BlockSpec((rows, PAIR), placed),
        ],
        out_specs=[
            pl.BlockSpec((rows, features), lambda p, m: (p, 0)),
            pl.BlockSpec((rows, q_width), lambda p, m: (p, 0)),
            padded,
            padded,
        ],
    )
    padded_shape = jax.ShapeDtypeStruct((key_heads, 2, total, PAIR), jnp.bfloat16)
    return pl.pallas_call(
        functools.partial(project_kernel, size=size, q_width=q_width, kv_width=kv_width),
        grid_spec=spec,
        out_shape=[
            jax.ShapeDtypeStruct((total, features), jnp.bfloat16),
            jax.ShapeDtypeStruct((total, q_width), jnp.bfloat16),
            padded_shape,
            padded_shape,
        ],
        compiler_params=PARAMS,
        cost_estimate=hint(2 * total * features * width // 16),
    )(me, *blocks, gain, own, other, own, other, cosine, sine)


def attend_kernel(
    me_ref, q_ref, k_ref, v_ref, wo_ref, wx_ref, o_ref, l_ref, *refs, size, heads, group
):
    part_refs, vt_ref = refs[:size], refs[size]
    rows = q_ref.shape[0]
    half = wo_ref.shape[0]
    mine = jnp.bitwise_xor(me_ref[0], pl.program_id(0))
    key_place = lax.broadcasted_iota(jnp.int32, (rows, rows), 0)
    query_place = lax.broadcasted_iota(jnp.int32, (rows, rows), 1)

    @pl.when(pl.program_id(0) == 0)
    def _():
        for head in range(heads // group):
            for side in range(2):
                vt_ref[head, side] = v_ref[head, side].T

    def one(span):
        keys = span * rows
        for pair in range(heads // 2):
            head = 2 * pair // group
            lanes = slice(pair * PAIR, (pair + 1) * PAIR)
            query = q_ref[:, lanes]
            acc = None
            inverse = []
            for side in range(2):
                diag = mm_nt(k_ref[head, side, keys : keys + rows, :], query)
                diag = jnp.where(key_place <= query_place, diag, -1e9)
                top = jnp.max(diag, axis=0, keepdims=True)
                if span:
                    body = mm_nt(k_ref[head, side, :keys, :], query)
                    top = jnp.maximum(top, jnp.max(body, axis=0, keepdims=True))
                diag = jnp.exp(diag - top)
                total = jnp.sum(diag, axis=0, keepdims=True)
                part = mm(vt_ref[head, side, :, keys : keys + rows], diag.astype(jnp.bfloat16))
                if span:
                    body = jnp.exp(body - top)
                    total = total + jnp.sum(body, axis=0, keepdims=True)
                    part = part + mm(vt_ref[head, side, :, :keys], body.astype(jnp.bfloat16))
                acc = part if acc is None else acc + part
                inverse.append(jnp.broadcast_to(1.0 / total, (HEAD_DIM, rows)))
                l_ref[2 * pair + side : 2 * pair + side + 1, :] = top + jnp.log(total)
            acc = acc * jnp.concatenate(inverse, axis=0)
            o_ref[:, lanes] = acc.T.astype(jnp.bfloat16)

    for span in range(size):
        pl.when(mine == span)(functools.partial(one, span))

    def project_out(ref):
        ref[:, :half] = mm_nt(o_ref[...], wo_ref[...]).astype(jnp.bfloat16)
        ref[:, half:] = mm_nt(o_ref[...], wx_ref[...]).astype(jnp.bfloat16)

    for step in range(size):
        pl.when(pl.program_id(0) == step)(functools.partial(project_out, part_refs[step]))


def attend(me, query, key_pad, value_pad, own, other, columns, size, group):
    total, width = query.shape
    features = 2 * own.shape[0]
    rows, heads = total // size, width // HEAD_DIM
    whole = pl.BlockSpec(key_pad.shape, lambda p, m: (0, 0, 0, 0), pipeline_mode=ONCE)
    spec = pltpu.PrefetchScalarGridSpec(
        num_scalar_prefetch=1,
        grid=(size,),
        in_specs=[pl.BlockSpec((rows, width), lambda p, m: (p, 0)), whole, whole]
        + [columns.spec("out", features // 2)] * 2,
        out_specs=[
            pl.BlockSpec((rows, width), lambda p, m: (p, 0)),
            pl.BlockSpec((heads, rows), lambda p, m: (0, p)),
        ]
        + [pl.BlockSpec((rows, features), lambda p, m: (0, 0))] * size,
        scratch_shapes=[pltpu.VMEM((heads // group, 2, PAIR, total), jnp.bfloat16)],
    )
    return pl.pallas_call(
        functools.partial(attend_kernel, size=size, heads=heads, group=group),
        grid_spec=spec,
        out_shape=[
            jax.ShapeDtypeStruct((total, width), jnp.bfloat16),
            jax.ShapeDtypeStruct((heads, total), jnp.float32),
        ]
        + [jax.ShapeDtypeStruct((rows, features), jnp.bfloat16)] * size,
        compiler_params=PARAMS,
        cost_estimate=hint(8 * heads * total * total * HEAD_DIM // 16),
    )(me, query, key_pad, value_pad, own, other)


def attend_back_kernel(
    me_ref, q_ref, l_ref, k_ref, v_ref, cos_ref, sin_ref, *refs, size, heads, group
):
    do_refs = refs[:size]
    out_ref, dk_ref, dv_ref, kt_ref, do_ref = refs[size:]
    rows = q_ref.shape[0]
    key_heads = heads // group
    step = pl.program_id(0)
    me = me_ref[0]
    mine = jnp.bitwise_xor(me, step)
    key_place = lax.broadcasted_iota(jnp.int32, (rows, rows), 0)
    query_place = lax.broadcasted_iota(jnp.int32, (rows, rows), 1)

    def rows_of(block):
        return pl.ds(pl.multiple_of(block * rows, rows), rows)

    @pl.when(step == 0)
    def _():
        dk_ref[...] = jnp.zeros_like(dk_ref)
        dv_ref[...] = jnp.zeros_like(dv_ref)
        for head in range(key_heads):
            for side in range(2):
                kt_ref[head, side] = k_ref[head, side].T

    def fetch(ref):
        do_ref[...] = ref[...]

    for block in range(size):
        pl.when(step == block)(functools.partial(fetch, do_refs[block]))

    def one(span):
        keys = span * rows
        parts = [(keys, keys + rows, True)] + ([(0, keys, False)] if span else [])
        cosine, sine = cos_ref[keys : keys + rows, :], sin_ref[keys : keys + rows, :]
        for pair in range(heads // 2):
            head = 2 * pair // group
            lanes = slice(pair * PAIR, (pair + 1) * PAIR)
            query, grad = q_ref[:, lanes], do_ref[:, lanes]
            acc = None
            for side in range(2):
                log_total = l_ref[2 * pair + side : 2 * pair + side + 1, :]
                inner = None
                kept = []
                for low, high, diagonal in parts:
                    probs = mm_nt(k_ref[head, side, low:high, :], query)
                    probs = jnp.exp(probs - log_total)
                    if diagonal:
                        probs = jnp.where(key_place <= query_place, probs, 0.0)
                    prob_grad = mm_nt(v_ref[head, side, low:high, :], grad)
                    dv_ref[head, side, low:high, :] += mm(probs.astype(jnp.bfloat16), grad)
                    term = jnp.sum(probs * prob_grad, axis=0, keepdims=True)
                    inner = term if inner is None else inner + term
                    kept.append((low, high, probs, prob_grad))
                for low, high, probs, prob_grad in kept:
                    score_grad = (probs * (prob_grad - inner)).astype(jnp.bfloat16)
                    dk_ref[head, side, low:high, :] += mm(score_grad, query)
                    part = mm(kt_ref[head, side, :, low:high], score_grad)
                    acc = part if acc is None else acc + part
            turned = turn(acc.T * SCALE, cosine, -sine)
            out_ref[rows_of(step), lanes] = turned.astype(jnp.bfloat16)

    for span in range(size):
        pl.when(mine == span)(functools.partial(one, span))

    @pl.when(step == size - 1)
    def _():
        first = lane_index(rows) < HEAD_DIM
        wanted = [(dk_ref, head, True) for head in range(key_heads)]
        wanted += [(dv_ref, head, False) for head in range(key_heads)]
        for span in range(size):
            place = slice(span * rows, (span + 1) * rows)
            cosine, sine = cos_ref[place, :], sin_ref[place, :]
            for block in range(len(wanted) // 2):
                halves, rotate = [], []
                for half in range(2):
                    ref, head, is_key = wanted[2 * block + half]
                    low, high = ref[head, 0, place, :], ref[head, 1, place, :]
                    if half:
                        halves.append(pltpu.roll(low, HEAD_DIM, 1) + high)
                    else:
                        halves.append(low + pltpu.roll(high, HEAD_DIM, 1))
                    rotate.append(is_key)
                value = jnp.where(first, halves[0], halves[1])
                if rotate[0] and rotate[1]:
                    value = turn(value, cosine, -sine)
                elif rotate[0]:
                    value = jnp.where(first, turn(value, cosine, -sine), value)
                start = heads * HEAD_DIM + block * PAIR
                target = rows_of(jnp.bitwise_xor(me, span))
                out_ref[target, start : start + PAIR] = value.astype(jnp.bfloat16)


def attend_back(
    me, query, log_total, key_pad, value_pad, cosine, sine, attended_grad, group
):
    total, width = query.shape
    size = len(attended_grad)
    rows, heads = total // size, width // HEAD_DIM
    key_heads = heads // group
    out_width = width + 2 * key_heads * HEAD_DIM
    whole = pl.BlockSpec(key_pad.shape, lambda p, m: (0, 0, 0, 0), pipeline_mode=ONCE)
    table = pl.BlockSpec((total, PAIR), lambda p, m: (0, 0), pipeline_mode=ONCE)
    spec = pltpu.PrefetchScalarGridSpec(
        num_scalar_prefetch=1,
        grid=(size,),
        in_specs=[
            pl.BlockSpec((rows, width), lambda p, m: (p, 0)),
            pl.BlockSpec((heads, rows), lambda p, m: (0, p)),
            whole,
            whole,
            table,
            table,
        ]
        + [pl.BlockSpec((rows, width), lambda p, m: (0, 0), pipeline_mode=ONCE)] * size,
        out_specs=pl.BlockSpec((total, out_width), lambda p, m: (0, 0)),
        scratch_shapes=[
            pltpu.VMEM(key_pad.shape, jnp.float32),
            pltpu.VMEM(key_pad.shape, jnp.float32),
            pltpu.VMEM((key_heads, 2, PAIR, total), jnp.bfloat16),
            pltpu.VMEM((rows, width), jnp.bfloat16),
        ],
    )
    return pl.pallas_call(
        functools.partial(attend_back_kernel, size=size, heads=heads, group=group),
        grid_spec=spec,
        out_shape=jax.ShapeDtypeStruct((total, out_width), jnp.bfloat16),
        compiler_params=PARAMS,
        cost_estimate=hint(20 * heads * total * total * HEAD_DIM),
    )(me, query, log_total, key_pad, value_pad, cosine, sine, *attended_grad)


def grouped(arrays, counts):
    arrays = iter(arrays)
    return [[next(arrays) for _ in range(count)] for count in counts]


def mlp_kernel(*refs, n_counts, e_counts, adds):
    size = len(n_counts)
    pieces = sum(n_counts) + sum(e_counts)
    n_refs = grouped(refs, n_counts)
    e_refs = grouped(refs[sum(n_counts) :], e_counts)
    gate_o, up_o, down_o, gate_x, up_x, down_x = refs[pieces : pieces + 6]
    y_ref, n_ref, e_ref = refs[-3:]
    dn_refs = refs[-3 - size if adds else -4 : -3]
    dg_ref, du_ref, h_ref = refs[-6 - size if adds else -7 :][:3]
    half = gate_o.shape[0]

    def fetch(step):
        for target, sources in ((n_ref, n_refs[step]), (e_ref, e_refs[step])):
            low = 0
            for source in sources:
                high = low + source.shape[0]
                target[low:high] = source[...]
                low = high

    for step in range(size):
        pl.when(pl.program_id(0) == step)(functools.partial(fetch, step))
    gate = mm(n_ref[:, :half], gate_o[...]) + mm(n_ref[:, half:], gate_x[...])
    up = mm(n_ref[:, :half], up_o[...]) + mm(n_ref[:, half:], up_x[...])
    grad = mm(e_ref[:, :half], down_o[...]) + mm(e_ref[:, half:], down_x[...])
    sigma = jax.nn.sigmoid(gate)
    silu = gate * sigma
    hidden = (silu * up).astype(jnp.bfloat16)
    gate_grad = (grad * up * sigma * (1.0 + gate * (1.0 - sigma))).astype(jnp.bfloat16)
    up_grad = (grad * silu).astype(jnp.bfloat16)
    dg_ref[...] = gate_grad
    du_ref[...] = up_grad
    h_ref[...] = hidden
    for part, gate_w, up_w, down_w in ((0, gate_o, up_o, down_o), (1, gate_x, up_x, down_x)):
        lanes = slice(part * half, (part + 1) * half)
        dn = mm_nt(gate_grad, gate_w[...]) + mm_nt(up_grad, up_w[...])
        y = mm_nt(hidden, down_w[...])
        if adds:
            dn = dn + refs[pieces + 6][:, lanes].astype(jnp.float32)
            y = y + refs[pieces + 7][:, lanes].astype(jnp.float32)
        y_ref[:, lanes] = y.astype(jnp.bfloat16)
        dn = dn.astype(jnp.bfloat16)

        def store(ref):
            ref[:, lanes] = dn

        if adds:
            for step in range(size):
                pl.when(pl.program_id(0) == step)(functools.partial(store, dn_refs[step]))
        else:
            store(dn_refs[0])


def mlp(tokens, cot, own, other, earlier):
    size = len(tokens)
    rows, features = tokens[0][0].shape
    half, units = own.shape[0], own.shape[1] // 3
    total = rows * size
    fixed = lambda p: (0, 0)
    moving = lambda p: (p, 0)
    wide = pl.BlockSpec((rows, features), moving)
    sums = jax.ShapeDtypeStruct((total, features), jnp.bfloat16)
    dn_specs, dn_shapes = [wide], [sums]
    if earlier:
        dn_specs = [pl.BlockSpec((rows, features), fixed)] * size
        dn_shapes = [jax.ShapeDtypeStruct((rows, features), jnp.bfloat16)] * size
    pieces = sum(tokens, []) + sum(cot, [])
    thirds = [
        pl.BlockSpec((half, units), lambda p, t=t: (0, t), pipeline_mode=ONCE) for t in range(3)
    ]
    return pl.pallas_call(
        functools.partial(
            mlp_kernel,
            n_counts=[len(group) for group in tokens],
            e_counts=[len(group) for group in cot],
            adds=bool(earlier),
        ),
        grid=(size,),
        in_specs=[pl.BlockSpec(piece.shape, fixed, pipeline_mode=ONCE) for piece in pieces]
        + thirds * 2
        + [wide] * len(earlier),
        out_specs=[pl.BlockSpec((rows, units), moving)] * 3 + dn_specs + [wide],
        out_shape=[jax.ShapeDtypeStruct((total, units), jnp.bfloat16)] * 3 + dn_shapes + [sums],
        scratch_shapes=[pltpu.VMEM((rows, features), jnp.bfloat16)] * 2,
        compiler_params=PARAMS,
        cost_estimate=hint(12 * total * features * units),
    )(*pieces, own, own, own, other, other, other, *earlier)


def add_refs(refs):
    total = refs[0][...].astype(jnp.float32)
    for ref in refs[1:]:
        total = total + ref[...].astype(jnp.float32)
    return total


def store_by_device(out_ref, values, core, chips):
    width = values.shape[1] // (2 * chips)
    for chip in range(chips):
        own = values[:, chip * width : (chip + 1) * width]
        other = values[:, (chips + chip) * width : (chips + chip + 1) * width]
        low = 2 * chip * width
        out_ref[:, low : low + width] = jnp.where(core == 0, own, other)
        out_ref[:, low + width : low + 2 * width] = jnp.where(core == 0, other, own)


def middle_kernel(*refs):
    x_ref, gain_ref, middle_ref, normed_ref = refs[-4:]
    values = x_ref[...].astype(jnp.float32) + add_refs(refs[:-4])
    middle_ref[...] = values
    normed_ref[...] = (values * rms_scale(values) * gain_ref[...]).astype(jnp.bfloat16)


def input_back_kernel(core_ref, *refs, chips):
    x_ref, before_ref, gain_ref, out_ref = refs[-4:]
    values = x_ref[...].astype(jnp.float32)
    inner = add_refs(refs[:-4]) * gain_ref[...]
    scale = rms_scale(values)
    mean = jnp.mean(inner * values, axis=-1, keepdims=True)
    result = before_ref[...] + scale * inner - values * (scale * scale * scale) * mean
    store_by_device(out_ref, result, core_ref[0], chips)


def output_kernel(core_ref, *refs, chips):
    middle_ref, out_ref = refs[-2:]
    values = middle_ref[...] + add_refs(refs[:-2])
    store_by_device(out_ref, values.astype(jnp.bfloat16), core_ref[0], chips)


def row_call(body, dtypes, arrays, core=None):
    rows, features = arrays[0].shape
    steps = 2
    wide = pl.BlockSpec((rows // steps, features), lambda i, *_: (i, 0))
    row = pl.BlockSpec((1, features), lambda i, *_: (0, 0))
    scalars = [] if core is None else [jnp.full((1,), core, jnp.int32)]
    return pl.pallas_call(
        body,
        grid_spec=pltpu.PrefetchScalarGridSpec(
            num_scalar_prefetch=len(scalars),
            grid=(steps,),
            in_specs=[row if array.shape[0] == 1 else wide for array in arrays],
            out_specs=[wide] * len(dtypes),
        ),
        out_shape=[jax.ShapeDtypeStruct((rows, features), dtype) for dtype in dtypes],
        compiler_params=PARAMS,
        cost_estimate=hint(0),
    )(*scalars, *arrays)


def unpack_kernel(sum_ref, q_ref, k_ref, v_ref, out_ref):
    q_width, kv_width = q_ref.shape[1], k_ref.shape[1]
    values = sum_ref[...].astype(jnp.float32)
    q_ref[...] = values[:, :q_width]
    kv = values[:, q_width : q_width + 2 * kv_width]
    k_ref[...] = kv[:, :kv_width]
    v_ref[...] = kv[:, kv_width:]
    out_ref[...] = values[:, q_width + 2 * kv_width :].T


def unpack(sums, q_width, kv_width):
    rows = sums.shape[0]
    widths = [(rows, q_width), (rows, kv_width), (rows, kv_width), (q_width, rows)]
    return pl.pallas_call(
        unpack_kernel,
        out_shape=[jax.ShapeDtypeStruct(shape, jnp.float32) for shape in widths],
        compiler_params=PARAMS,
        cost_estimate=hint(0),
    )(sums)


def middle_back_kernel(*refs, parts, size):
    n_refs, refs = refs[:parts], refs[parts:]
    x_ref, e_ref, gain_ref, refs = refs[0], refs[1], refs[2], refs[3:]
    own_refs, other_refs, refs = refs[:size], refs[size : 2 * size], refs[2 * size :]
    grad_ref, branch_ref, part_ref, do_refs = refs[0], refs[1], refs[2], refs[3:]
    half = own_refs[0].shape[0]
    grad = add_refs(n_refs)
    values = x_ref[...]
    scale = rms_scale(values)
    result, part = norm_back(grad, values, scale, gain_ref[...])

    @pl.when(pl.program_id(0) == 0)
    def _():
        part_ref[...] = jnp.zeros_like(part_ref)

    part_ref[...] += part[None, :]
    result = result + e_ref[...].astype(jnp.float32)
    grad_ref[...] = result
    branch = result.astype(jnp.bfloat16)
    branch_ref[...] = branch
    for own, other, do_ref in zip(own_refs, other_refs, do_refs):
        do = mm(branch[:, :half], own[...]) + mm(branch[:, half:], other[...])
        do_ref[...] = do.astype(jnp.bfloat16)


def middle_back(arrived, middle, cot, gain, own, other):
    parts, size = len(arrived), len(own)
    rows, features = middle.shape
    width = own[0].shape[1]
    steps = 2
    wide = pl.BlockSpec((rows // steps, features), lambda i: (i, 0))
    narrow = pl.BlockSpec((rows // steps, width), lambda i: (i, 0))
    row = pl.BlockSpec((1, features), lambda i: (0, 0))
    weight = pl.BlockSpec((features // 2, width), lambda i: (0, 0), pipeline_mode=ONCE)
    grad, branch, part, *do = pl.pallas_call(
        functools.partial(middle_back_kernel, parts=parts, size=size),
        grid=(steps,),
        in_specs=[wide] * parts + [wide, wide, row] + [weight] * (2 * size),
        out_specs=[wide, wide, row] + [narrow] * size,
        out_shape=[
            jax.ShapeDtypeStruct((rows, features), jnp.float32),
            jax.ShapeDtypeStruct((rows, features), jnp.bfloat16),
            jax.ShapeDtypeStruct((1, features), jnp.float32),
        ]
        + [jax.ShapeDtypeStruct((rows, width), jnp.bfloat16)] * size,
        compiler_params=PARAMS,
        cost_estimate=hint(2 * rows * features * width * size),
    )(*arrived, middle, cot, gain, *own, *other)
    return grad, branch, part[0], do


def column_grad(blocks, other, mine, theirs):
    total = mm_tn(other[...], theirs[...])
    low = 0
    for block in blocks:
        high = low + block.shape[0]
        total = total + mm_tn(block[...], mine[low:high, :])
        low = high
    return total


def grad_kernel(*refs, n_count, e_count):
    n_refs, refs = refs[:n_count], refs[n_count:]
    e_refs, refs = refs[:e_count], refs[e_count:]
    n_other, e_other = refs[:2]
    acts, out_ref = refs[2:-1], refs[-1]
    units = acts[0].shape[1]
    for third in range(3):
        blocks, other = (e_refs, e_other) if third == 2 else (n_refs, n_other)
        grad = column_grad(blocks, other, acts[third], acts[third + 3])
        out_ref[0, :, third * units : (third + 1) * units] = grad.astype(jnp.bfloat16)


def mlp_grads(chips, tokens, cot, tokens_other, cot_other, mine, theirs):
    tokens, cot = sum(tokens, []), sum(cot, [])
    features = tokens[0].shape[1]
    total, units = mine[0].shape
    depth = features // (2 * chips)
    long = pl.BlockSpec((total, depth), lambda b: (0, b))
    fixed = pl.BlockSpec((total, units), lambda b: (0, 0), pipeline_mode=ONCE)
    return pl.pallas_call(
        functools.partial(grad_kernel, n_count=len(tokens), e_count=len(cot)),
        grid=(chips,),
        in_specs=[pl.BlockSpec((p.shape[0], depth), lambda b: (0, b)) for p in tokens + cot]
        + [long, long]
        + [fixed] * 6,
        out_specs=pl.BlockSpec((1, depth, 3 * units), lambda b: (b, 0, 0)),
        out_shape=jax.ShapeDtypeStruct((chips, depth, 3 * units), jnp.bfloat16),
        compiler_params=PARAMS,
        cost_estimate=hint(6 * total * features * units),
    )(*tokens, *cot, tokens_other, cot_other, *mine, *theirs)


def attn_grad_kernel(*refs, size):
    e_refs = refs[2 : 2 + size]
    n_ref, n_other = refs[:2]
    e_other, d_ref, d_other, o_ref, o_other, q_ref, kv_ref, g1_ref, g2_ref = refs[2 + size : -2]
    out_ref, gain_ref = refs[-2:]
    width, out_width = d_ref.shape[1], o_ref.shape[1]
    grad = column_grad([n_ref], n_other, d_ref, d_other)
    out_ref[0, :, :width] = grad.astype(jnp.bfloat16)
    out_grad = column_grad(e_refs, e_other, o_ref, o_other)
    out_ref[0, :, width : width + out_width] = out_grad.astype(jnp.bfloat16)
    cut = q_ref.shape[1]
    first = jnp.sum(grad[:, :cut] * q_ref[...].astype(jnp.float32), axis=1, keepdims=True)
    first += jnp.sum(grad[:, cut:] * kv_ref[...].astype(jnp.float32), axis=1, keepdims=True)
    first = first / g1_ref[...]
    lane = lane_index(grad.shape[0])
    gain_ref[0] = jnp.where(lane == 0, first, g2_ref[...])


def attn_grads(
    chips, tokens, branch, mine, theirs, weights, columns, gain_one, gain_two_part
):
    size = len(branch)
    qkv_grad, attended = mine
    tokens_other, branch_other, qkv_other, attended_other = theirs
    total, features = tokens.shape
    rows = total // size
    width, out_width = qkv_grad.shape[1], attended.shape[1]
    depth = features // (2 * chips)
    column = lambda b: (0, b)
    row = lambda b: (b, 0)
    long = pl.BlockSpec((total, depth), column)
    fixed = lambda array: pl.BlockSpec(array.shape, lambda b: (0, 0), pipeline_mode=ONCE)
    place = lambda b: (b, 0, 0)
    return pl.pallas_call(
        functools.partial(attn_grad_kernel, size=size),
        grid=(chips,),
        in_specs=[long, long]
        + [pl.BlockSpec((rows, depth), column)] * size
        + [long]
        + [fixed(qkv_grad)] * 2
        + [fixed(attended)] * 2
        + [
            columns.spec("q", depth, lambda b=None: b),
            columns.spec("kv", depth, lambda b=None: b),
            pl.BlockSpec((depth, 1), row),
            pl.BlockSpec((depth, 1), row),
        ],
        out_specs=[
            pl.BlockSpec((1, depth, width + out_width), place),
            pl.BlockSpec((1, depth, PAIR), place),
        ],
        out_shape=[
            jax.ShapeDtypeStruct((chips, depth, width + out_width), jnp.bfloat16),
            jax.ShapeDtypeStruct((chips, depth, PAIR), jnp.float32),
        ],
        compiler_params=PARAMS,
        cost_estimate=hint(2 * total * features * (width + out_width)),
    )(
        tokens,
        tokens_other,
        *branch,
        branch_other,
        qkv_grad,
        qkv_other,
        attended,
        attended_other,
        weights,
        weights,
        gain_one,
        gain_two_part,
    )


def input_grad_kernel(d_ref, qo_ref, qx_ref, kvo_ref, kvx_ref, *out_refs):
    half, cut = qo_ref.shape

    def one(ref):
        query, rest = d_ref[:, :cut], d_ref[:, cut:]
        own = mm_nt(query, qo_ref[...]) + mm_nt(rest, kvo_ref[...])
        other = mm_nt(query, qx_ref[...]) + mm_nt(rest, kvx_ref[...])
        ref[:, :half] = own.astype(jnp.bfloat16)
        ref[:, half:] = other.astype(jnp.bfloat16)

    for step, ref in enumerate(out_refs):
        pl.when(pl.program_id(0) == step)(functools.partial(one, ref))


def input_grad(qkv_grad, own, other, columns, size):
    total, width = qkv_grad.shape
    features = 2 * own.shape[0]
    rows = total // size
    fixed = lambda i: (0, 0)
    weights = [columns.spec(part, own.shape[0]) for part in ("q", "q", "kv", "kv")]
    return pl.pallas_call(
        input_grad_kernel,
        grid=(size,),
        in_specs=[pl.BlockSpec((rows, width), lambda i: (i, 0))] + weights,
        out_specs=[pl.BlockSpec((rows, features), fixed)] * size,
        out_shape=[jax.ShapeDtypeStruct((rows, features), jnp.bfloat16)] * size,
        compiler_params=PARAMS,
        cost_estimate=hint(2 * total * features * width),
    )(qkv_grad, own, other, own, other)


def swap(values, step):
    size = lax.axis_size("tensor")
    return lax.ppermute(values, "tensor", [(i, i ^ step) for i in range(size)])


def spread(values):
    return [values] + [swap(values, step) for step in range(1, lax.axis_size("tensor"))]


def send_blocks(blocks):
    return [blocks[0]] + [swap(block, step + 1) for step, block in enumerate(blocks[1:])]


def spread_around(values, held):
    if lax.axis_size("tensor") != 4:
        blocks = spread(values)
        first, held = barrier((blocks[1], held))
        return [[blocks[0]], [first]] + [[block] for block in blocks[2:]], held
    half = values.shape[0] // 2
    top, bottom = values[:half], values[half:]
    x_bottom, y_top = swap(bottom, 1), swap(top, 2)
    x_bottom, y_top, top, bottom, held = barrier((x_bottom, y_top, top, bottom, held))
    far = [swap(y_top, 1), swap(x_bottom, 2)]
    x_top, y_bottom = swap(top, 1), swap(bottom, 2)
    return [[values], [x_top, x_bottom], [y_top, y_bottom], far], held


def merge_kernel(x_ref, y_ref, top_ref, bottom_ref, x_out, y_out):
    half = top_ref.shape[0]
    x_out[:half] = x_ref[:half]
    x_out[half:] = add_refs([x_ref.at[half:], bottom_ref]).astype(jnp.bfloat16)
    y_out[:half] = add_refs([y_ref.at[:half], top_ref]).astype(jnp.bfloat16)
    y_out[half:] = y_ref[half:]


def send_sum(blocks, held=()):
    if len(blocks) != 4:
        return send_blocks(blocks), held
    own, near_x, near_y, far = blocks
    half = far.shape[0] // 2
    top, bottom = swap(far[:half], 1), swap(far[half:], 2)
    near_x, near_y = pl.pallas_call(
        merge_kernel,
        out_shape=[jax.ShapeDtypeStruct(near_x.shape, near_x.dtype)] * 2,
        compiler_params=PARAMS,
        cost_estimate=hint(0),
    )(near_x, near_y, top, bottom)
    near_x, near_y, held = barrier((near_x, near_y, held))
    return [own, swap(near_x, 1), swap(near_y, 2)], held


def add_up(blocks):
    total = blocks[0].astype(jnp.float32)
    for block in blocks[1:]:
        total = total + block.astype(jnp.float32)
    return total


def cross(values):
    count = lax.axis_size("dp")
    return lax.ppermute(values, "dp", [(i, i ^ 1) for i in range(count)])


def tables(positions):
    freqs = ROPE_BASE ** (-jnp.arange(0, HEAD_DIM, 2).astype(jnp.float32) / HEAD_DIM)
    angles = positions.astype(jnp.float32)[:, None] * freqs[None, :]
    cosine, sine = jnp.cos(angles), jnp.sin(angles)
    return (
        jnp.concatenate([cosine] * 4, axis=1),
        jnp.concatenate([-sine, sine, -sine, sine], axis=1),
    )


def chip_lines():
    count = lax.axis_size("dp")
    return [list(range(core, count, 2)) for core in range(2)]


def gather(values):
    return lax.all_gather(values, "dp", axis=0, tiled=True, axis_index_groups=chip_lines())


def scatter(values):
    total = lax.psum_scatter(
        values, "dp", scatter_dimension=0, tiled=True, axis_index_groups=chip_lines()
    )
    return total[0]


def along(values, step):
    count = lax.axis_size("dp")
    return lax.ppermute(values, "dp", [(i, (i + 2 * step) % count) for i in range(count)])


def line_parts(parts):
    chips = lax.axis_size("dp") // 2
    chip = lax.axis_index("dp") // 2
    blocks = [lax.dynamic_index_in_dim(parts, chip, 0, keepdims=False)]
    for step in range(1, chips):
        sent = lax.dynamic_index_in_dim(parts, (chip + step) % chips, 0, keepdims=False)
        blocks.append(along(sent, step))
    return blocks


def own_part(values):
    size = lax.axis_size("tensor")
    me = lax.axis_index("tensor")
    blocks = values.reshape((size, -1) + values.shape[1:])
    own = lax.dynamic_index_in_dim(blocks, me, 0, keepdims=False)
    for step in range(1, size):
        sent = lax.dynamic_index_in_dim(blocks, me ^ step, 0, keepdims=False)
        own = own + swap(sent, step)
    return own


def stack_kernel(*refs):
    low = 0
    for ref in refs[:-1]:
        high = low + ref.shape[0]
        refs[-1][low:high, :] = ref[...]
        low = high


def other_half(blocks):
    features = blocks[0].shape[1]
    shape = (sum(block.shape[0] for block in blocks), features // 2)
    halves = pl.pallas_call(
        stack_kernel,
        grid=(1,),
        in_specs=[pl.BlockSpec((b.shape[0], features // 2), lambda i: (0, 1)) for b in blocks],
        out_specs=pl.BlockSpec(shape, lambda i: (0, 0)),
        out_shape=jax.ShapeDtypeStruct(shape, blocks[0].dtype),
        compiler_params=PARAMS,
        cost_estimate=hint(0),
    )(*blocks)
    return cross(halves)


def feature_blocks(values):
    width = values.shape[-1] // lax.axis_size("dp")
    return [values[..., low : low + width] for low in range(0, values.shape[-1], width)]


def by_core(values, core):
    blocks = feature_blocks(values)
    pairs = list(zip(blocks[0::2], blocks[1::2]))
    own = [jnp.where(core == 0, even, odd) for even, odd in pairs]
    other = [jnp.where(core == 0, odd, even) for even, odd in pairs]
    return jnp.concatenate(own + other, axis=-1)


def per_device(
    hidden_in,
    gain_attn,
    w_query,
    w_key,
    w_value,
    w_out,
    gain_mlp,
    w_gate,
    w_up,
    w_down,
    positions,
    cotangent,
):
    size = lax.axis_size("tensor")
    chips = lax.axis_size("dp") // 2
    me = lax.axis_index("tensor")
    me_array = jnp.full((1,), me, jnp.int32)
    core = lax.axis_index("dp") % 2
    q_width, kv_width = w_query.shape[1], w_key.shape[1]
    group = q_width // kv_width
    units = w_down.shape[0] // 2
    half = hidden_in.shape[1] // 2

    columns = Columns(q_width, kv_width)
    attn_shard = jnp.concatenate([w_query, w_out.T, w_key, w_value], axis=1)
    attn_shard, hidden_in, gain_attn = barrier((attn_shard, hidden_in, gain_attn))
    attn_own = gather(attn_shard)
    gains = lax.all_gather(jnp.stack([gain_attn, gain_mlp]), "dp", axis=1, tiled=True)
    gains, hidden_in = barrier((gains, hidden_in))
    gains = by_core(gains, core).astype(jnp.float32)
    residual = by_core(hidden_in, core)
    blocks_in = spread(residual)
    cosine, sine = tables(positions)
    cotangent = by_core(cotangent, core)
    down_t = w_down.T
    shares = []
    for part in range(2):
        cut = slice(part * units, (part + 1) * units)
        shares.append(jnp.concatenate([w_gate[:, cut], w_up[:, cut], down_t[:, cut]], axis=1))
    shares, attn_own, blocks_in, cosine, sine, gains, cotangent = barrier(
        (shares, attn_own, blocks_in, cosine, sine, gains, cotangent)
    )
    mlp_own = [gather(share) for share in shares]
    cot_blocks = spread(cotangent)
    gain_one, gain_two = gains[0], gains[1]
    attn = (attn_own, cross(attn_own))

    tokens_one, query, key_pad, value_pad = project(
        me_array, blocks_in, gain_one[None, :], *attn, cosine, sine, columns
    )
    attended, log_total, *parts = attend(
        me_array, query, key_pad, value_pad, *attn, columns, size, group
    )
    parts, cot_blocks, tokens_one, attended = barrier((parts, cot_blocks, tokens_one, attended))
    arrived, _ = send_sum(parts)
    cot_other = other_half(cot_blocks)
    cot_blocks = [[block] for block in cot_blocks]
    early = (cross(tokens_one[:, half:]), cross(attended))
    arrived, cot_other, early = barrier((arrived, cot_other, early))
    out_t = [w[:, q_width : 2 * q_width] for w in attn]
    middle, normed_two = row_call(
        middle_kernel, [jnp.float32, jnp.bfloat16], [*arrived, residual, gain_two[None, :]]
    )
    tokens_two, own_share = spread_around(normed_two, mlp_own[0])
    weights = (own_share, cross(own_share))
    tokens_two, weights, out_own = barrier((tokens_two, weights, out_t[0]))
    tokens_other = other_half(sum(tokens_two, []))
    *acts, dn_part, y_part = mlp(tokens_two, cot_blocks, *weights, ())
    out_blocks = spread(out_own)
    acts, tokens_other = barrier((acts, tokens_other))
    acts_other = [cross(act) for act in acts]
    grads_one = mlp_grads(
        chips, tokens_two, cot_blocks, tokens_other, cot_other, acts, acts_other
    )
    grads_one, own_share = barrier((grads_one, mlp_own[1]))
    sums_one = scatter(grads_one)
    weights = (own_share, cross(own_share))
    *acts, y_part = mlp(tokens_two, cot_blocks, *weights, (dn_part, y_part))
    acts, dn_part = acts[:3], acts[3:]
    acts, dn_part, out_blocks = barrier((acts, dn_part, out_blocks))
    acts_other = [cross(act) for act in acts]
    arrived, acts = send_sum(dn_part, acts)
    out_other = [out_t[1]] + [cross(block) for block in out_blocks[1:]]
    grads_two = mlp_grads(
        chips, tokens_two, cot_blocks, tokens_other, cot_other, acts, acts_other
    )
    grads_two, arrived, out_other, y_part = barrier((grads_two, arrived, out_other, y_part))
    y_blocks = list(y_part.reshape((size, -1) + y_part.shape[1:]))
    y_early = [swap(y_blocks[step], step) for step in range(1, 3)]
    sums_two = scatter(grads_two)
    middle_grad, branch, gain_two_part, do_blocks = middle_back(
        arrived, middle, cotangent, gain_two[None, :], out_blocks, out_other
    )
    do_blocks = send_blocks(do_blocks)
    gain_two_other = cross(gain_two_part[half:])
    do_blocks, branch, gain_two_other, y_blocks, y_early = barrier(
        (do_blocks, branch, gain_two_other, y_blocks, y_early)
    )
    branch_blocks = spread(branch)
    qkv_grad = attend_back(
        me_array, query, log_total, key_pad, value_pad, cosine, sine, do_blocks, group
    )
    qkv_grad, sums_one = barrier((qkv_grad, sums_one))
    qkv_other = cross(qkv_grad)
    normed_part = input_grad(qkv_grad, *attn, columns, size)
    branch_blocks, normed_part = barrier((branch_blocks, normed_part))
    branch_other = other_half(branch_blocks)
    tokens_other, attended_other = early
    grads, gain_parts = attn_grads(
        chips,
        tokens_one,
        branch_blocks,
        (qkv_grad, attended),
        (tokens_other, branch_other, qkv_other, attended_other),
        attn_own,
        columns,
        gain_one[:half, None],
        (gain_two_part[:half] + gain_two_other)[:, None],
    )
    arrived, grads = send_sum(normed_part, grads)
    attn_sums = scatter(grads)
    gain_sums = add_up(line_parts(gain_parts[:, :, :2]))
    arrived, y_blocks, sums_two, gain_sums = barrier((arrived, y_blocks, sums_two, gain_sums))
    y_late = [swap(y_blocks[step], step) for step in range(3, size)]
    gain_sums = own_part(gain_sums)
    (grad_in,) = row_call(
        functools.partial(input_back_kernel, chips=chips),
        [jnp.float32],
        [*arrived, residual, middle_grad, gain_one[None, :]],
        core,
    )
    shares = [share.astype(jnp.float32) for share in (sums_one, sums_two)]
    grad_gate = jnp.concatenate([h[:, :units] for h in shares], axis=1)
    grad_up = jnp.concatenate([h[:, units : 2 * units] for h in shares], axis=1)
    grad_down = jnp.concatenate([h[:, 2 * units :].T for h in shares], axis=0)
    y_late, grad_in, gain_sums, grad_gate, grad_up, grad_down = barrier(
        (y_late, grad_in, gain_sums, grad_gate, grad_up, grad_down)
    )
    (out,) = row_call(
        functools.partial(output_kernel, chips=chips),
        [jnp.bfloat16],
        [y_blocks[0], *y_early, *y_late, middle],
        core,
    )
    out, attn_sums = barrier((out, attn_sums))
    grad_query, grad_key, grad_value, grad_out = unpack(attn_sums, q_width, kv_width)
    return (
        out,
        grad_in,
        gain_sums[:, 0],
        grad_query,
        grad_key,
        grad_value,
        grad_out,
        gain_sums[:, 1],
        grad_gate,
        grad_up,
        grad_down,
    )


def solution(mesh):
    return jax.shard_map(
        per_device,
        mesh=mesh,
        in_specs=(
            P(("dp", "tensor"), None),
            P("dp"),
            P("dp", "tensor"),
            P("dp", "tensor"),
            P("dp", "tensor"),
            P("tensor", "dp"),
            P("dp"),
            P("dp", "tensor"),
            P("dp", "tensor"),
            P("tensor", "dp"),
            P("dp"),
            P(("dp", "tensor"), None),
        ),
        out_specs=(
            P(("dp", "tensor"), None),
            P(("dp", "tensor"), None),
            P(("dp", "tensor")),
            P("dp", "tensor"),
            P("dp", "tensor"),
            P("dp", "tensor"),
            P("tensor", "dp"),
            P(("dp", "tensor")),
            P("dp", "tensor"),
            P("dp", "tensor"),
            P("tensor", "dp"),
        ),
        check_vma=False,
    )
```

```python
import functools
import math

import jax
import jax.numpy as jnp
from jax import lax
from jax.experimental import pallas as pl
from jax.experimental.pallas import tpu as pltpu
from jax.sharding import PartitionSpec as P

HEAD_DIM = 64
PAIR = 2 * HEAD_DIM
SEQ_LEN = 1024


EPS = 1e-05
ROPE_BASE = 500000.0
SCALE = 1.0 / math.sqrt(HEAD_DIM)
PARAMS = pltpu.CompilerParams(vmem_limit_bytes=58 * 2**20)
ONCE = pl.Buffered(1)

barrier = lax.optimization_barrier


def hint(flops):
    return pl.CostEstimate(flops=flops, bytes_accessed=0, transcendentals=0)


def rms_scale(values):
    return lax.rsqrt(jnp.mean(values * values, axis=-1, keepdims=True) + EPS)


def norm_back(grad, values, scale, gain):
    inner = grad * gain
    cubed = scale * scale * scale
    result = scale * inner - values * cubed * jnp.mean(inner * values, axis=-1, keepdims=True)
    return (result, jnp.sum(grad * values * scale, axis=0))


def mm(left, right):
    return jnp.dot(left, right, preferred_element_type=jnp.float32)


def mm_nt(left, right):
    return lax.dot_general(left, right, (((1,), (1,)), ((), ())), preferred_element_type=jnp.float32)


def mm_tn(left, right):
    return lax.dot_general(left, right, (((0,), (0,)), ((), ())), preferred_element_type=jnp.float32)


def lane_index(rows):
    return lax.broadcasted_iota(jnp.int32, (rows, PAIR), 1)


def turn(pair, cosine, sine):
    lower = lane_index(pair.shape[0]) % HEAD_DIM < HEAD_DIM // 2
    other = jnp.where(
        lower, pltpu.roll(pair, PAIR - HEAD_DIM // 2, 1), pltpu.roll(pair, HEAD_DIM // 2, 1)
    )
    return pair * cosine + other * sine


def project_kernel(place_ref, *refs, size, q_width, kv_width):
    x_refs = refs[:size]
    gain_ref, qo_ref, qx_ref, kvo_ref, kvx_ref, cos_ref, sin_ref = refs[size:-4]
    n_ref, q_ref, k_ref, v_ref = refs[-4:]
    rows = q_ref.shape[0]
    half = qo_ref.shape[0]

    def one(x_ref):
        x = x_ref[...].astype(jnp.float32)
        normed = (x * rms_scale(x) * gain_ref[...]).astype(jnp.bfloat16)
        n_ref[...] = normed
        cosine, sine = cos_ref[...], sin_ref[...]
        own, other = normed[:, :half], normed[:, half:]
        lin = mm(own, qo_ref[...]) + mm(other, qx_ref[...])
        for low in range(0, q_width, PAIR):
            query = turn(lin[:, low : low + PAIR], cosine, sine).astype(jnp.bfloat16)
            q_ref[:, low : low + PAIR] = query * jnp.bfloat16(SCALE)
        lin = mm(own, kvo_ref[...]) + mm(other, kvx_ref[...])
        first = lane_index(rows) < HEAD_DIM
        for ref, start, rotate in ((k_ref, 0, True), (v_ref, kv_width, False)):
            for head in range(kv_width // HEAD_DIM):
                low = start + head * HEAD_DIM
                block = lin[:, low // PAIR * PAIR : low // PAIR * PAIR + PAIR]
                if rotate:
                    block = turn(block, cosine, sine)
                moved = pltpu.roll(block, HEAD_DIM, 1)
                if low % PAIR:
                    block, moved = moved, block
                ref[head, 0] = jnp.where(first, block, 0.0).astype(jnp.bfloat16)
                ref[head, 1] = jnp.where(first, 0.0, moved).astype(jnp.bfloat16)

    for step in range(size):
        pl.when(pl.program_id(0) == step)(functools.partial(one, x_refs[step]))


class Columns:
    def __init__(self, q_width, kv_width):
        self.q_width, self.kv_width = q_width, kv_width

    def spec(self, part, rows, place=lambda *_: 0):
        width, start = {"q": (self.q_width, 0), "kv": (2 * self.kv_width, self.q_width)}[part]
        index = start // width
        mode = {"pipeline_mode": ONCE} if place() == 0 else {}
        return pl.BlockSpec((rows, width), lambda *grid: (place(*grid), index), **mode)


def project(me, blocks, gain, own, other, cosine, sine, columns):
    size = len(blocks)
    rows, features = blocks[0].shape
    total = rows * size
    q_width, kv_width = columns.q_width, columns.kv_width
    key_heads = kv_width // HEAD_DIM
    width = q_width + 2 * kv_width
    half = features // 2
    fixed = lambda p, m: (0, 0)
    placed = lambda p, m: (jnp.bitwise_xor(p, m[0]), 0)
    padded = pl.BlockSpec(
        (key_heads, 2, rows, PAIR), lambda p, m: (0, 0, jnp.bitwise_xor(p, m[0]), 0)
    )
    spec = pltpu.PrefetchScalarGridSpec(
        num_scalar_prefetch=1,
        grid=(size,),
        in_specs=[pl.BlockSpec((rows, features), fixed, pipeline_mode=ONCE)] * size
        + [
            pl.BlockSpec((1, features), fixed),
            columns.spec("q", half),
            columns.spec("q", half),
            columns.spec("kv", half),
            columns.spec("kv", half),
            pl.BlockSpec((rows, PAIR), placed),
            pl.BlockSpec((rows, PAIR), placed),
        ],
        out_specs=[
            pl.BlockSpec((rows, features), lambda p, m: (p, 0)),
            pl.BlockSpec((rows, q_width), lambda p, m: (p, 0)),
            padded,
            padded,
        ],
    )
    padded_shape = jax.ShapeDtypeStruct((key_heads, 2, total, PAIR), jnp.bfloat16)
    return pl.pallas_call(
        functools.partial(project_kernel, size=size, q_width=q_width, kv_width=kv_width),
        grid_spec=spec,
        out_shape=[
            jax.ShapeDtypeStruct((total, features), jnp.bfloat16),
            jax.ShapeDtypeStruct((total, q_width), jnp.bfloat16),
            padded_shape,
            padded_shape,
        ],
        compiler_params=PARAMS,
        cost_estimate=hint(2 * total * features * width // 16),
    )(me, *blocks, gain, own, other, own, other, cosine, sine)


def attend_kernel(
    me_ref, q_ref, k_ref, v_ref, wo_ref, wx_ref, o_ref, l_ref, *refs, size, heads, group
):
    part_refs, vt_ref = refs[:size], refs[size]
    rows = q_ref.shape[0]
    half = wo_ref.shape[0]
    mine = jnp.bitwise_xor(me_ref[0], pl.program_id(0))
    key_place = lax.broadcasted_iota(jnp.int32, (rows, rows), 0)
    query_place = lax.broadcasted_iota(jnp.int32, (rows, rows), 1)

    @pl.when(pl.program_id(0) == 0)
    def _():
        for head in range(heads // group):
            for side in range(2):
                vt_ref[head, side] = v_ref[head, side].T

    def one(span):
        keys = span * rows
        for pair in range(heads // 2):
            head = 2 * pair // group
            lanes = slice(pair * PAIR, (pair + 1) * PAIR)
            query = q_ref[:, lanes]
            acc = None
            inverse = []
            for side in range(2):
                diag = mm_nt(k_ref[head, side, keys : keys + rows, :], query)
                diag = jnp.where(key_place <= query_place, diag, -1e9)
                top = jnp.max(diag, axis=0, keepdims=True)
                if span:
                    body = mm_nt(k_ref[head, side, :keys, :], query)
                    top = jnp.maximum(top, jnp.max(body, axis=0, keepdims=True))
                diag = jnp.exp(diag - top)
                total = jnp.sum(diag, axis=0, keepdims=True)
                part = mm(vt_ref[head, side, :, keys : keys + rows], diag.astype(jnp.bfloat16))
                if span:
                    body = jnp.exp(body - top)
                    total = total + jnp.sum(body, axis=0, keepdims=True)
                    part = part + mm(vt_ref[head, side, :, :keys], body.astype(jnp.bfloat16))
                acc = part if acc is None else acc + part
                inverse.append(jnp.broadcast_to(1.0 / total, (HEAD_DIM, rows)))
                l_ref[2 * pair + side : 2 * pair + side + 1, :] = top + jnp.log(total)
            acc = acc * jnp.concatenate(inverse, axis=0)
            o_ref[:, lanes] = acc.T.astype(jnp.bfloat16)

    for span in range(size):
        pl.when(mine == span)(functools.partial(one, span))

    def project_out(ref):
        ref[:, :half] = mm_nt(o_ref[...], wo_ref[...]).astype(jnp.bfloat16)
        ref[:, half:] = mm_nt(o_ref[...], wx_ref[...]).astype(jnp.bfloat16)

    for step in range(size):
        pl.when(pl.program_id(0) == step)(functools.partial(project_out, part_refs[step]))


def attend(me, query, key_pad, value_pad, own, other, size, group):
    total, width = query.shape
    features = 2 * own.shape[0]
    rows, heads = total // size, width // HEAD_DIM
    whole = pl.BlockSpec(key_pad.shape, lambda p, m: (0, 0, 0, 0), pipeline_mode=ONCE)
    spec = pltpu.PrefetchScalarGridSpec(
        num_scalar_prefetch=1,
        grid=(size,),
        in_specs=[pl.BlockSpec((rows, width), lambda p, m: (p, 0)), whole, whole]
        + [pl.BlockSpec(own.shape, lambda p, m: (0, 0), pipeline_mode=ONCE)] * 2,
        out_specs=[
            pl.BlockSpec((rows, width), lambda p, m: (p, 0)),
            pl.BlockSpec((heads, rows), lambda p, m: (0, p)),
        ]
        + [pl.BlockSpec((rows, features), lambda p, m: (0, 0))] * size,
        scratch_shapes=[pltpu.VMEM((heads // group, 2, PAIR, total), jnp.bfloat16)],
    )
    return pl.pallas_call(
        functools.partial(attend_kernel, size=size, heads=heads, group=group),
        grid_spec=spec,
        out_shape=[
            jax.ShapeDtypeStruct((total, width), jnp.bfloat16),
            jax.ShapeDtypeStruct((heads, total), jnp.float32),
        ]
        + [jax.ShapeDtypeStruct((rows, features), jnp.bfloat16)] * size,
        compiler_params=PARAMS,
        cost_estimate=hint(8 * heads * total * total * HEAD_DIM // 16),
    )(me, query, key_pad, value_pad, own, other)


def attend_back_kernel(
    me_ref, q_ref, l_ref, k_ref, v_ref, cos_ref, sin_ref, *refs, size, heads, group
):
    do_refs = refs[:size]
    out_ref, dk_ref, dv_ref, kt_ref, do_ref = refs[size:]
    rows = q_ref.shape[0]
    key_heads = heads // group
    step = pl.program_id(0)
    me = me_ref[0]
    mine = jnp.bitwise_xor(me, step)
    key_place = lax.broadcasted_iota(jnp.int32, (rows, rows), 0)
    query_place = lax.broadcasted_iota(jnp.int32, (rows, rows), 1)

    def rows_of(block):
        return pl.ds(pl.multiple_of(block * rows, rows), rows)

    @pl.when(step == 0)
    def _():
        dk_ref[...] = jnp.zeros_like(dk_ref)
        dv_ref[...] = jnp.zeros_like(dv_ref)
        for head in range(key_heads):
            for side in range(2):
                kt_ref[head, side] = k_ref[head, side].T

    def fetch(ref):
        do_ref[...] = ref[...]

    for block in range(size):
        pl.when(step == block)(functools.partial(fetch, do_refs[block]))

    def one(span):
        keys = span * rows
        parts = [(keys, keys + rows, True)] + ([(0, keys, False)] if span else [])
        cosine, sine = cos_ref[keys : keys + rows, :], sin_ref[keys : keys + rows, :]
        for pair in range(heads // 2):
            head = 2 * pair // group
            lanes = slice(pair * PAIR, (pair + 1) * PAIR)
            query, grad = q_ref[:, lanes], do_ref[:, lanes]
            acc = None
            for side in range(2):
                log_total = l_ref[2 * pair + side : 2 * pair + side + 1, :]
                inner = None
                kept = []
                for low, high, diagonal in parts:
                    probs = mm_nt(k_ref[head, side, low:high, :], query)
                    probs = jnp.exp(probs - log_total)
                    if diagonal:
                        probs = jnp.where(key_place <= query_place, probs, 0.0)
                    prob_grad = mm_nt(v_ref[head, side, low:high, :], grad)
                    dv_ref[head, side, low:high, :] += mm(probs.astype(jnp.bfloat16), grad)
                    term = jnp.sum(probs * prob_grad, axis=0, keepdims=True)
                    inner = term if inner is None else inner + term
                    kept.append((low, high, probs, prob_grad))
                for low, high, probs, prob_grad in kept:
                    score_grad = (probs * (prob_grad - inner)).astype(jnp.bfloat16)
                    dk_ref[head, side, low:high, :] += mm(score_grad, query)
                    part = mm(kt_ref[head, side, :, low:high], score_grad)
                    acc = part if acc is None else acc + part
            turned = turn(acc.T * SCALE, cosine, -sine)
            out_ref[rows_of(step), lanes] = turned.astype(jnp.bfloat16)

    for span in range(size):
        pl.when(mine == span)(functools.partial(one, span))

    @pl.when(step == size - 1)
    def _():
        first = lane_index(rows) < HEAD_DIM
        wanted = [(dk_ref, head, True) for head in range(key_heads)]
        wanted += [(dv_ref, head, False) for head in range(key_heads)]
        for span in range(size):
            place = slice(span * rows, (span + 1) * rows)
            cosine, sine = cos_ref[place, :], sin_ref[place, :]
            for block in range(len(wanted) // 2):
                halves, rotate = [], []
                for half in range(2):
                    ref, head, is_key = wanted[2 * block + half]
                    low, high = ref[head, 0, place, :], ref[head, 1, place, :]
                    if half:
                        halves.append(pltpu.roll(low, HEAD_DIM, 1) + high)
                    else:
                        halves.append(low + pltpu.roll(high, HEAD_DIM, 1))
                    rotate.append(is_key)
                value = jnp.where(first, halves[0], halves[1])
                if rotate[0] and rotate[1]:
                    value = turn(value, cosine, -sine)
                elif rotate[0]:
                    value = jnp.where(first, turn(value, cosine, -sine), value)
                start = heads * HEAD_DIM + block * PAIR
                target = rows_of(jnp.bitwise_xor(me, span))
                out_ref[target, start : start + PAIR] = value.astype(jnp.bfloat16)


def attend_back(
    me, query, log_total, key_pad, value_pad, cosine, sine, attended_grad, group
):
    total, width = query.shape
    size = len(attended_grad)
    rows, heads = total // size, width // HEAD_DIM
    key_heads = heads // group
    out_width = width + 2 * key_heads * HEAD_DIM
    whole = pl.BlockSpec(key_pad.shape, lambda p, m: (0, 0, 0, 0), pipeline_mode=ONCE)
    table = pl.BlockSpec((total, PAIR), lambda p, m: (0, 0), pipeline_mode=ONCE)
    spec = pltpu.PrefetchScalarGridSpec(
        num_scalar_prefetch=1,
        grid=(size,),
        in_specs=[
            pl.BlockSpec((rows, width), lambda p, m: (p, 0)),
            pl.BlockSpec((heads, rows), lambda p, m: (0, p)),
            whole,
            whole,
            table,
            table,
        ]
        + [pl.BlockSpec((rows, width), lambda p, m: (0, 0), pipeline_mode=ONCE)] * size,
        out_specs=pl.BlockSpec((total, out_width), lambda p, m: (0, 0)),
        scratch_shapes=[
            pltpu.VMEM(key_pad.shape, jnp.float32),
            pltpu.VMEM(key_pad.shape, jnp.float32),
            pltpu.VMEM((key_heads, 2, PAIR, total), jnp.bfloat16),
            pltpu.VMEM((rows, width), jnp.bfloat16),
        ],
    )
    return pl.pallas_call(
        functools.partial(attend_back_kernel, size=size, heads=heads, group=group),
        grid_spec=spec,
        out_shape=jax.ShapeDtypeStruct((total, out_width), jnp.bfloat16),
        compiler_params=PARAMS,
        cost_estimate=hint(20 * heads * total * total * HEAD_DIM),
    )(me, query, log_total, key_pad, value_pad, cosine, sine, *attended_grad)


def grouped(arrays, counts):
    arrays = iter(arrays)
    return [[next(arrays) for _ in range(count)] for count in counts]


def mlp_kernel(*refs, n_counts, e_counts, adds):
    size = len(n_counts)
    pieces = sum(n_counts) + sum(e_counts)
    n_refs = grouped(refs, n_counts)
    e_refs = grouped(refs[sum(n_counts) :], e_counts)
    gate_o, up_o, down_o, gate_x, up_x, down_x = refs[pieces : pieces + 6]
    y_ref, n_ref, e_ref = refs[-3:]
    dn_refs = refs[-3 - size if adds else -4 : -3]
    dg_ref, du_ref, h_ref = refs[-6 - size if adds else -7 :][:3]
    half = gate_o.shape[0]

    def fetch(step):
        for target, sources in ((n_ref, n_refs[step]), (e_ref, e_refs[step])):
            low = 0
            for source in sources:
                high = low + source.shape[0]
                target[low:high] = source[...]
                low = high

    for step in range(size):
        pl.when(pl.program_id(0) == step)(functools.partial(fetch, step))
    gate = mm(n_ref[:, :half], gate_o[...]) + mm(n_ref[:, half:], gate_x[...])
    up = mm(n_ref[:, :half], up_o[...]) + mm(n_ref[:, half:], up_x[...])
    grad = mm(e_ref[:, :half], down_o[...]) + mm(e_ref[:, half:], down_x[...])
    sigma = jax.nn.sigmoid(gate)
    silu = gate * sigma
    hidden = (silu * up).astype(jnp.bfloat16)
    gate_grad = (grad * up * sigma * (1.0 + gate * (1.0 - sigma))).astype(jnp.bfloat16)
    up_grad = (grad * silu).astype(jnp.bfloat16)
    dg_ref[...] = gate_grad
    du_ref[...] = up_grad
    h_ref[...] = hidden
    for part, gate_w, up_w, down_w in ((0, gate_o, up_o, down_o), (1, gate_x, up_x, down_x)):
        lanes = slice(part * half, (part + 1) * half)
        dn = mm_nt(gate_grad, gate_w[...]) + mm_nt(up_grad, up_w[...])
        y = mm_nt(hidden, down_w[...])
        if adds:
            dn = dn + refs[pieces + 6][:, lanes].astype(jnp.float32)
            y = y + refs[pieces + 7][:, lanes].astype(jnp.float32)
        y_ref[:, lanes] = y.astype(jnp.bfloat16)
        dn = dn.astype(jnp.bfloat16)

        def store(ref):
            ref[:, lanes] = dn

        if adds:
            for step in range(size):
                pl.when(pl.program_id(0) == step)(functools.partial(store, dn_refs[step]))
        else:
            store(dn_refs[0])


def mlp(tokens, cot, own, other, earlier):
    size = len(tokens)
    rows, features = tokens[0][0].shape
    half, units = own.shape[0], own.shape[1] // 3
    total = rows * size
    fixed = lambda p: (0, 0)
    moving = lambda p: (p, 0)
    wide = pl.BlockSpec((rows, features), moving)
    sums = jax.ShapeDtypeStruct((total, features), jnp.bfloat16)
    dn_specs, dn_shapes = [wide], [sums]
    if earlier:
        dn_specs = [pl.BlockSpec((rows, features), fixed)] * size
        dn_shapes = [jax.ShapeDtypeStruct((rows, features), jnp.bfloat16)] * size
    pieces = sum(tokens, []) + sum(cot, [])
    thirds = [
        pl.BlockSpec((half, units), lambda p, t=t: (0, t), pipeline_mode=ONCE) for t in range(3)
    ]
    return pl.pallas_call(
        functools.partial(
            mlp_kernel,
            n_counts=[len(group) for group in tokens],
            e_counts=[len(group) for group in cot],
            adds=bool(earlier),
        ),
        grid=(size,),
        in_specs=[pl.BlockSpec(piece.shape, fixed, pipeline_mode=ONCE) for piece in pieces]
        + thirds * 2
        + [wide] * len(earlier),
        out_specs=[pl.BlockSpec((rows, units), moving)] * 3 + dn_specs + [wide],
        out_shape=[jax.ShapeDtypeStruct((total, units), jnp.bfloat16)] * 3 + dn_shapes + [sums],
        scratch_shapes=[pltpu.VMEM((rows, features), jnp.bfloat16)] * 2,
        compiler_params=PARAMS,
        cost_estimate=hint(12 * total * features * units),
    )(*pieces, own, own, own, other, other, other, *earlier)


def add_refs(refs):
    total = refs[0][...].astype(jnp.float32)
    for ref in refs[1:]:
        total = total + ref[...].astype(jnp.float32)
    return total


def store_by_device(out_ref, values, core, chips):
    width = values.shape[1] // (2 * chips)
    for chip in range(chips):
        own = values[:, chip * width : (chip + 1) * width]
        other = values[:, (chips + chip) * width : (chips + chip + 1) * width]
        low = 2 * chip * width
        out_ref[:, low : low + width] = jnp.where(core == 0, own, other)
        out_ref[:, low + width : low + 2 * width] = jnp.where(core == 0, other, own)


def middle_kernel(*refs):
    x_ref, gain_ref, middle_ref, normed_ref = refs[-4:]
    values = x_ref[...].astype(jnp.float32) + add_refs(refs[:-4])
    middle_ref[...] = values
    normed_ref[...] = (values * rms_scale(values) * gain_ref[...]).astype(jnp.bfloat16)


def input_back_kernel(core_ref, *refs, chips):
    x_ref, before_ref, gain_ref, out_ref = refs[-4:]
    values = x_ref[...].astype(jnp.float32)
    inner = add_refs(refs[:-4]) * gain_ref[...]
    scale = rms_scale(values)
    mean = jnp.mean(inner * values, axis=-1, keepdims=True)
    result = before_ref[...] + scale * inner - values * (scale * scale * scale) * mean
    store_by_device(out_ref, result, core_ref[0], chips)


def output_kernel(core_ref, *refs, chips):
    middle_ref, out_ref = refs[-2:]
    values = middle_ref[...] + add_refs(refs[:-2])
    store_by_device(out_ref, values.astype(jnp.bfloat16), core_ref[0], chips)


def row_call(body, dtypes, arrays, core=None):
    rows, features = arrays[0].shape
    steps = 2
    wide = pl.BlockSpec((rows // steps, features), lambda i, *_: (i, 0))
    row = pl.BlockSpec((1, features), lambda i, *_: (0, 0))
    scalars = [] if core is None else [jnp.full((1,), core, jnp.int32)]
    return pl.pallas_call(
        body,
        grid_spec=pltpu.PrefetchScalarGridSpec(
            num_scalar_prefetch=len(scalars),
            grid=(steps,),
            in_specs=[row if array.shape[0] == 1 else wide for array in arrays],
            out_specs=[wide] * len(dtypes),
        ),
        out_shape=[jax.ShapeDtypeStruct((rows, features), dtype) for dtype in dtypes],
        compiler_params=PARAMS,
        cost_estimate=hint(0),
    )(*scalars, *arrays)


def unpack_kernel(sum_ref, q_ref, k_ref, v_ref, out_ref):
    q_width, kv_width = q_ref.shape[1], k_ref.shape[1]
    values = sum_ref[...].astype(jnp.float32)
    q_ref[...] = values[:, :q_width]
    kv = values[:, q_width : q_width + 2 * kv_width]
    k_ref[...] = kv[:, :kv_width]
    v_ref[...] = kv[:, kv_width:]
    out_ref[...] = values[:, q_width + 2 * kv_width :].T


def unpack(sums, q_width, kv_width):
    rows = sums.shape[0]
    widths = [(rows, q_width), (rows, kv_width), (rows, kv_width), (q_width, rows)]
    return pl.pallas_call(
        unpack_kernel,
        out_shape=[jax.ShapeDtypeStruct(shape, jnp.float32) for shape in widths],
        compiler_params=PARAMS,
        cost_estimate=hint(0),
    )(sums)


def unpack_shares_kernel(one_ref, two_ref, gate_ref, up_ref, down_ref):
    units = one_ref.shape[1] // 3
    for part, ref in enumerate((one_ref, two_ref)):
        cut = slice(part * units, (part + 1) * units)
        gate_ref[:, cut] = ref[:, :units].astype(jnp.float32)
        up_ref[:, cut] = ref[:, units : 2 * units].astype(jnp.float32)
        down_ref[cut, :] = ref[:, 2 * units :].astype(jnp.float32).T


def unpack_shares(one, two):
    rows, width = one.shape
    units = 2 * width // 3
    shapes = [(rows, units), (rows, units), (units, rows)]
    return pl.pallas_call(
        unpack_shares_kernel,
        out_shape=[jax.ShapeDtypeStruct(shape, jnp.float32) for shape in shapes],
        compiler_params=PARAMS,
        cost_estimate=hint(0),
    )(one, two)


def middle_back_kernel(*refs, parts, size):
    n_refs, refs = refs[:parts], refs[parts:]
    x_ref, e_ref, gain_ref, refs = refs[0], refs[1], refs[2], refs[3:]
    own_refs, other_refs, refs = refs[:size], refs[size : 2 * size], refs[2 * size :]
    grad_ref, branch_ref, part_ref, do_refs = refs[0], refs[1], refs[2], refs[3:]
    half = own_refs[0].shape[0]
    grad = add_refs(n_refs)
    values = x_ref[...]
    scale = rms_scale(values)
    result, part = norm_back(grad, values, scale, gain_ref[...])

    @pl.when(pl.program_id(0) == 0)
    def _():
        part_ref[...] = jnp.zeros_like(part_ref)

    part_ref[...] += part[None, :]
    result = result + e_ref[...].astype(jnp.float32)
    grad_ref[...] = result
    branch = result.astype(jnp.bfloat16)
    branch_ref[...] = branch
    for own, other, do_ref in zip(own_refs, other_refs, do_refs):
        do = mm(branch[:, :half], own[...]) + mm(branch[:, half:], other[...])
        do_ref[...] = do.astype(jnp.bfloat16)


def middle_back(arrived, middle, cot, gain, own, other):
    parts, size = len(arrived), len(own)
    rows, features = middle.shape
    width = own[0].shape[1]
    steps = 2
    wide = pl.BlockSpec((rows // steps, features), lambda i: (i, 0))
    narrow = pl.BlockSpec((rows // steps, width), lambda i: (i, 0))
    row = pl.BlockSpec((1, features), lambda i: (0, 0))
    weight = pl.BlockSpec((features // 2, width), lambda i: (0, 0), pipeline_mode=ONCE)
    grad, branch, part, *do = pl.pallas_call(
        functools.partial(middle_back_kernel, parts=parts, size=size),
        grid=(steps,),
        in_specs=[wide] * parts + [wide, wide, row] + [weight] * (2 * size),
        out_specs=[wide, wide, row] + [narrow] * size,
        out_shape=[
            jax.ShapeDtypeStruct((rows, features), jnp.float32),
            jax.ShapeDtypeStruct((rows, features), jnp.bfloat16),
            jax.ShapeDtypeStruct((1, features), jnp.float32),
        ]
        + [jax.ShapeDtypeStruct((rows, width), jnp.bfloat16)] * size,
        compiler_params=PARAMS,
        cost_estimate=hint(2 * rows * features * width * size),
    )(*arrived, middle, cot, gain, *own, *other)
    return grad, branch, part[0], do


def column_grad(blocks, other, mine, theirs):
    total = mm_tn(other[...], theirs[...])
    low = 0
    for block in blocks:
        high = low + block.shape[0]
        total = total + mm_tn(block[...], mine[low:high, :])
        low = high
    return total


def grad_kernel(*refs, n_count, e_count):
    n_refs, refs = refs[:n_count], refs[n_count:]
    e_refs, refs = refs[:e_count], refs[e_count:]
    n_other, e_other = refs[:2]
    acts, out_ref = refs[2:-1], refs[-1]
    units = acts[0].shape[1]
    for third in range(3):
        blocks, other = (e_refs, e_other) if third == 2 else (n_refs, n_other)
        grad = column_grad(blocks, other, acts[third], acts[third + 3])
        out_ref[0, :, third * units : (third + 1) * units] = grad.astype(jnp.bfloat16)


def mlp_grads(chips, tokens, cot, tokens_other, cot_other, mine, theirs):
    tokens, cot = sum(tokens, []), sum(cot, [])
    features = tokens[0].shape[1]
    total, units = mine[0].shape
    depth = features // (2 * chips)
    long = pl.BlockSpec((total, depth), lambda b: (0, b))
    fixed = pl.BlockSpec((total, units), lambda b: (0, 0), pipeline_mode=ONCE)
    return pl.pallas_call(
        functools.partial(grad_kernel, n_count=len(tokens), e_count=len(cot)),
        grid=(chips,),
        in_specs=[pl.BlockSpec((p.shape[0], depth), lambda b: (0, b)) for p in tokens + cot]
        + [long, long]
        + [fixed] * 6,
        out_specs=pl.BlockSpec((1, depth, 3 * units), lambda b: (b, 0, 0)),
        out_shape=jax.ShapeDtypeStruct((chips, depth, 3 * units), jnp.bfloat16),
        compiler_params=PARAMS,
        cost_estimate=hint(6 * total * features * units),
    )(*tokens, *cot, tokens_other, cot_other, *mine, *theirs)


def attn_grad_kernel(*refs, size):
    e_refs = refs[2 : 2 + size]
    n_ref, n_other = refs[:2]
    e_other, d_ref, d_other, o_ref, o_other, q_ref, kv_ref, g1_ref, g2_ref = refs[2 + size : -2]
    out_ref, gain_ref = refs[-2:]
    width, out_width = d_ref.shape[1], o_ref.shape[1]
    grad = column_grad([n_ref], n_other, d_ref, d_other)
    out_ref[0, :, :width] = grad.astype(jnp.bfloat16)
    out_grad = column_grad(e_refs, e_other, o_ref, o_other)
    out_ref[0, :, width : width + out_width] = out_grad.astype(jnp.bfloat16)
    cut = q_ref.shape[1]
    first = jnp.sum(grad[:, :cut] * q_ref[...].astype(jnp.float32), axis=1, keepdims=True)
    first += jnp.sum(grad[:, cut:] * kv_ref[...].astype(jnp.float32), axis=1, keepdims=True)
    first = first / g1_ref[...]
    lane = lane_index(grad.shape[0])
    gain_ref[0] = jnp.where(lane == 0, first, g2_ref[...])


def attn_grads(
    chips, tokens, branch, mine, theirs, weights, columns, gain_one, gain_two_part
):
    size = len(branch)
    qkv_grad, attended = mine
    tokens_other, branch_other, qkv_other, attended_other = theirs
    total, features = tokens.shape
    rows = total // size
    width, out_width = qkv_grad.shape[1], attended.shape[1]
    depth = features // (2 * chips)
    column = lambda b: (0, b)
    row = lambda b: (b, 0)
    long = pl.BlockSpec((total, depth), column)
    fixed = lambda array: pl.BlockSpec(array.shape, lambda b: (0, 0), pipeline_mode=ONCE)
    place = lambda b: (b, 0, 0)
    return pl.pallas_call(
        functools.partial(attn_grad_kernel, size=size),
        grid=(chips,),
        in_specs=[long, long]
        + [pl.BlockSpec((rows, depth), column)] * size
        + [long]
        + [fixed(qkv_grad)] * 2
        + [fixed(attended)] * 2
        + [
            columns.spec("q", depth, lambda b=None: b),
            columns.spec("kv", depth, lambda b=None: b),
            pl.BlockSpec((depth, 1), row),
            pl.BlockSpec((depth, 1), row),
        ],
        out_specs=[
            pl.BlockSpec((1, depth, width + out_width), place),
            pl.BlockSpec((1, depth, PAIR), place),
        ],
        out_shape=[
            jax.ShapeDtypeStruct((chips, depth, width + out_width), jnp.bfloat16),
            jax.ShapeDtypeStruct((chips, depth, PAIR), jnp.float32),
        ],
        compiler_params=PARAMS,
        cost_estimate=hint(2 * total * features * (width + out_width)),
    )(
        tokens,
        tokens_other,
        *branch,
        branch_other,
        qkv_grad,
        qkv_other,
        attended,
        attended_other,
        weights,
        weights,
        gain_one,
        gain_two_part,
    )


def input_grad_kernel(d_ref, qo_ref, qx_ref, kvo_ref, kvx_ref, *out_refs):
    half, cut = qo_ref.shape

    def one(ref):
        query, rest = d_ref[:, :cut], d_ref[:, cut:]
        own = mm_nt(query, qo_ref[...]) + mm_nt(rest, kvo_ref[...])
        other = mm_nt(query, qx_ref[...]) + mm_nt(rest, kvx_ref[...])
        ref[:, :half] = own.astype(jnp.bfloat16)
        ref[:, half:] = other.astype(jnp.bfloat16)

    for step, ref in enumerate(out_refs):
        pl.when(pl.program_id(0) == step)(functools.partial(one, ref))


def input_grad(qkv_grad, own, other, columns, size):
    total, width = qkv_grad.shape
    features = 2 * own.shape[0]
    rows = total // size
    fixed = lambda i: (0, 0)
    weights = [columns.spec(part, own.shape[0]) for part in ("q", "q", "kv", "kv")]
    return pl.pallas_call(
        input_grad_kernel,
        grid=(size,),
        in_specs=[pl.BlockSpec((rows, width), lambda i: (i, 0))] + weights,
        out_specs=[pl.BlockSpec((rows, features), fixed)] * size,
        out_shape=[jax.ShapeDtypeStruct((rows, features), jnp.bfloat16)] * size,
        compiler_params=PARAMS,
        cost_estimate=hint(2 * total * features * width),
    )(qkv_grad, own, other, own, other)


def swap(values, step):
    size = lax.axis_size("tensor")
    return lax.ppermute(values, "tensor", [(i, i ^ step) for i in range(size)])


def spread(values):
    return [values] + [swap(values, step) for step in range(1, lax.axis_size("tensor"))]


def send_blocks(blocks):
    return [blocks[0]] + [swap(block, step + 1) for step, block in enumerate(blocks[1:])]


def spread_around(values, held):
    if lax.axis_size("tensor") != 4:
        blocks = spread(values)
        first, held = barrier((blocks[1], held))
        return [[blocks[0]], [first]] + [[block] for block in blocks[2:]], held
    half = values.shape[0] // 2
    top, bottom = values[:half], values[half:]
    x_bottom, y_top = swap(bottom, 1), swap(top, 2)
    x_bottom, y_top, top, bottom, held = barrier((x_bottom, y_top, top, bottom, held))
    far = [swap(y_top, 1), swap(x_bottom, 2)]
    x_top, y_bottom = swap(top, 1), swap(bottom, 2)
    return [[values], [x_top, x_bottom], [y_top, y_bottom], far], held


def merge_kernel(x_ref, y_ref, top_ref, bottom_ref, x_out, y_out):
    half = top_ref.shape[0]
    x_out[:half] = x_ref[:half]
    x_out[half:] = add_refs([x_ref.at[half:], bottom_ref]).astype(jnp.bfloat16)
    y_out[:half] = add_refs([y_ref.at[:half], top_ref]).astype(jnp.bfloat16)
    y_out[half:] = y_ref[half:]


def send_sum(blocks, held=()):
    if len(blocks) != 4:
        return send_blocks(blocks), held
    own, near_x, near_y, far = blocks
    half = far.shape[0] // 2
    top, bottom = swap(far[:half], 1), swap(far[half:], 2)
    near_x, near_y = pl.pallas_call(
        merge_kernel,
        out_shape=[jax.ShapeDtypeStruct(near_x.shape, near_x.dtype)] * 2,
        compiler_params=PARAMS,
        cost_estimate=hint(0),
    )(near_x, near_y, top, bottom)
    near_x, near_y, held = barrier((near_x, near_y, held))
    return [own, swap(near_x, 1), swap(near_y, 2)], held


def add_up(blocks):
    total = blocks[0].astype(jnp.float32)
    for block in blocks[1:]:
        total = total + block.astype(jnp.float32)
    return total


def cross(values):
    count = lax.axis_size("dp")
    return lax.ppermute(values, "dp", [(i, i ^ 1) for i in range(count)])


def tables(positions):
    freqs = ROPE_BASE ** (-jnp.arange(0, HEAD_DIM, 2).astype(jnp.float32) / HEAD_DIM)
    angles = positions.astype(jnp.float32)[:, None] * freqs[None, :]
    cosine, sine = jnp.cos(angles), jnp.sin(angles)
    return (
        jnp.concatenate([cosine] * 4, axis=1),
        jnp.concatenate([-sine, sine, -sine, sine], axis=1),
    )


def chip_lines():
    count = lax.axis_size("dp")
    return [list(range(core, count, 2)) for core in range(2)]


def gather(values):
    return lax.all_gather(values, "dp", axis=0, tiled=True, axis_index_groups=chip_lines())


def scatter(values):
    total = lax.psum_scatter(
        values, "dp", scatter_dimension=0, tiled=True, axis_index_groups=chip_lines()
    )
    return total[0]


def along(values, step):
    count = lax.axis_size("dp")
    return lax.ppermute(values, "dp", [(i, (i + 2 * step) % count) for i in range(count)])


def line_order(blocks):
    chips = len(blocks)
    chip = lax.axis_index("dp") // 2
    placed = jnp.zeros((chips,) + blocks[0].shape, blocks[0].dtype)
    for step, block in enumerate(blocks):
        placed = lax.dynamic_update_index_in_dim(placed, block, (chip - step) % chips, 0)
    return placed.reshape((-1,) + blocks[0].shape[1:])


def line_parts(parts):
    chips = lax.axis_size("dp") // 2
    chip = lax.axis_index("dp") // 2
    blocks = [lax.dynamic_index_in_dim(parts, chip, 0, keepdims=False)]
    for step in range(1, chips):
        sent = lax.dynamic_index_in_dim(parts, (chip + step) % chips, 0, keepdims=False)
        blocks.append(along(sent, step))
    return blocks


def own_part(values):
    size = lax.axis_size("tensor")
    me = lax.axis_index("tensor")
    blocks = values.reshape((size, -1) + values.shape[1:])
    own = lax.dynamic_index_in_dim(blocks, me, 0, keepdims=False)
    for step in range(1, size):
        sent = lax.dynamic_index_in_dim(blocks, me ^ step, 0, keepdims=False)
        own = own + swap(sent, step)
    return own


def stack_kernel(*refs):
    low = 0
    for ref in refs[:-1]:
        high = low + ref.shape[0]
        refs[-1][low:high, :] = ref[...]
        low = high


def other_half(blocks):
    features = blocks[0].shape[1]
    shape = (sum(block.shape[0] for block in blocks), features // 2)
    halves = pl.pallas_call(
        stack_kernel,
        grid=(1,),
        in_specs=[pl.BlockSpec((b.shape[0], features // 2), lambda i: (0, 1)) for b in blocks],
        out_specs=pl.BlockSpec(shape, lambda i: (0, 0)),
        out_shape=jax.ShapeDtypeStruct(shape, blocks[0].dtype),
        compiler_params=PARAMS,
        cost_estimate=hint(0),
    )(*blocks)
    return cross(halves)


def feature_blocks(values):
    width = values.shape[-1] // lax.axis_size("dp")
    return [values[..., low : low + width] for low in range(0, values.shape[-1], width)]


def by_core(values, core):
    blocks = feature_blocks(values)
    pairs = list(zip(blocks[0::2], blocks[1::2]))
    own = [jnp.where(core == 0, even, odd) for even, odd in pairs]
    other = [jnp.where(core == 0, odd, even) for even, odd in pairs]
    return jnp.concatenate(own + other, axis=-1)


def per_device(
    hidden_in,
    gain_attn,
    w_query,
    w_key,
    w_value,
    w_out,
    gain_mlp,
    w_gate,
    w_up,
    w_down,
    positions,
    cotangent,
):
    size = lax.axis_size("tensor")
    chips = lax.axis_size("dp") // 2
    me = lax.axis_index("tensor")
    me_array = jnp.full((1,), me, jnp.int32)
    core = lax.axis_index("dp") % 2
    q_width, kv_width = w_query.shape[1], w_key.shape[1]
    group = q_width // kv_width
    units = w_down.shape[0] // 2
    half = hidden_in.shape[1] // 2

    columns = Columns(q_width, kv_width)
    qkv_shard = jnp.concatenate([w_query, w_key, w_value], axis=1)
    out_shard = w_out.T
    qkv_shard, out_shard, hidden_in, gain_attn = barrier(
        (qkv_shard, out_shard, hidden_in, gain_attn)
    )
    qkv_own = gather(qkv_shard)
    residual = by_core(hidden_in, core)
    early_in = [swap(residual, step) for step in range(1, 3)]
    early_out = [along(out_shard, step) for step in range(1, 3)]
    early_in, early_out, residual, out_shard = barrier(
        (early_in, early_out, residual, out_shard)
    )
    blocks_in = [residual] + early_in + [swap(residual, step) for step in range(3, size)]
    out_parts = [out_shard] + early_out + [along(out_shard, step) for step in range(3, chips)]
    gains = lax.all_gather(jnp.stack([gain_attn, gain_mlp]), "dp", axis=1, tiled=True)
    gains = by_core(gains, core).astype(jnp.float32)
    cosine, sine = tables(positions)
    cotangent = by_core(cotangent, core)
    down_t = w_down.T
    shares = []
    for part in range(2):
        cut = slice(part * units, (part + 1) * units)
        shares.append(jnp.concatenate([w_gate[:, cut], w_up[:, cut], down_t[:, cut]], axis=1))
    shares, qkv_own, out_parts, blocks_in, cosine, sine, gains, cotangent = barrier(
        (shares, qkv_own, out_parts, blocks_in, cosine, sine, gains, cotangent)
    )
    mlp_own = [gather(share) for share in shares]
    cot_blocks = spread(cotangent)
    gain_one, gain_two = gains[0], gains[1]
    qkv = (qkv_own, cross(qkv_own))
    out_own = line_order(out_parts)
    out_t = (out_own, cross(out_own))

    tokens_one, query, key_pad, value_pad = project(
        me_array, blocks_in, gain_one[None, :], *qkv, cosine, sine, columns
    )
    attended, log_total, *parts = attend(
        me_array, query, key_pad, value_pad, *out_t, size, group
    )
    parts, cot_blocks, tokens_one, attended = barrier((parts, cot_blocks, tokens_one, attended))
    arrived, _ = send_sum(parts)
    cot_other = other_half(cot_blocks)
    cot_blocks = [[block] for block in cot_blocks]
    early = (cross(tokens_one[:, half:]), cross(attended))
    arrived, cot_other, early = barrier((arrived, cot_other, early))
    middle, normed_two = row_call(
        middle_kernel, [jnp.float32, jnp.bfloat16], [*arrived, residual, gain_two[None, :]]
    )
    tokens_two, own_share = spread_around(normed_two, mlp_own[0])
    weights = (own_share, cross(own_share))
    tokens_two, weights, out_own = barrier((tokens_two, weights, out_t[0]))
    tokens_other = other_half(sum(tokens_two, []))
    *acts, dn_part, y_part = mlp(tokens_two, cot_blocks, *weights, ())
    out_blocks = spread(out_own)
    acts, tokens_other = barrier((acts, tokens_other))
    acts_other = [cross(act) for act in acts]
    grads_one = mlp_grads(
        chips, tokens_two, cot_blocks, tokens_other, cot_other, acts, acts_other
    )
    grads_one, own_share = barrier((grads_one, mlp_own[1]))
    sums_one = scatter(grads_one)
    weights = (own_share, cross(own_share))
    *acts, y_part = mlp(tokens_two, cot_blocks, *weights, (dn_part, y_part))
    acts, dn_part = acts[:3], acts[3:]
    acts, dn_part, out_blocks = barrier((acts, dn_part, out_blocks))
    acts_other = [cross(act) for act in acts]
    arrived, acts = send_sum(dn_part, acts)
    out_other = [out_t[1]] + [cross(block) for block in out_blocks[1:]]
    grads_two = mlp_grads(
        chips, tokens_two, cot_blocks, tokens_other, cot_other, acts, acts_other
    )
    grads_two, arrived, out_other, y_part = barrier((grads_two, arrived, out_other, y_part))
    y_blocks = list(y_part.reshape((size, -1) + y_part.shape[1:]))
    y_early = [swap(y_blocks[step], step) for step in range(1, 3)]
    sums_two = scatter(grads_two)
    middle_grad, branch, gain_two_part, do_blocks = middle_back(
        arrived, middle, cotangent, gain_two[None, :], out_blocks, out_other
    )
    do_blocks = send_blocks(do_blocks)
    gain_two_other = cross(gain_two_part[half:])
    do_blocks, branch, gain_two_other, y_blocks, y_early = barrier(
        (do_blocks, branch, gain_two_other, y_blocks, y_early)
    )
    branch_blocks = spread(branch)
    qkv_grad = attend_back(
        me_array, query, log_total, key_pad, value_pad, cosine, sine, do_blocks, group
    )
    qkv_grad, sums_one = barrier((qkv_grad, sums_one))
    qkv_other = cross(qkv_grad)
    normed_part = input_grad(qkv_grad, *qkv, columns, size)
    branch_blocks, normed_part = barrier((branch_blocks, normed_part))
    branch_other = other_half(branch_blocks)
    tokens_other, attended_other = early
    grads, gain_parts = attn_grads(
        chips,
        tokens_one,
        branch_blocks,
        (qkv_grad, attended),
        (tokens_other, branch_other, qkv_other, attended_other),
        qkv_own,
        columns,
        gain_one[:half, None],
        (gain_two_part[:half] + gain_two_other)[:, None],
    )
    arrived, (grads, y_blocks) = send_sum(normed_part, (grads, y_blocks))
    y_late = [swap(y_blocks[step], step) for step in range(3, size)]
    attn_sums = scatter(grads)
    gain_sums = add_up(line_parts(gain_parts[:, :, :2]))
    arrived, sums_two, gain_sums = barrier((arrived, sums_two, gain_sums))
    gain_sums = own_part(gain_sums)
    (grad_in,) = row_call(
        functools.partial(input_back_kernel, chips=chips),
        [jnp.float32],
        [*arrived, residual, middle_grad, gain_one[None, :]],
        core,
    )
    grad_gate, grad_up, grad_down = unpack_shares(sums_one, sums_two)
    y_late, grad_in, gain_sums, grad_gate, grad_up, grad_down = barrier(
        (y_late, grad_in, gain_sums, grad_gate, grad_up, grad_down)
    )
    (out,) = row_call(
        functools.partial(output_kernel, chips=chips),
        [jnp.bfloat16],
        [y_blocks[0], *y_early, *y_late, middle],
        core,
    )
    out, attn_sums = barrier((out, attn_sums))
    grad_query, grad_key, grad_value, grad_out = unpack(attn_sums, q_width, kv_width)
    return (
        out,
        grad_in,
        gain_sums[:, 0],
        grad_query,
        grad_key,
        grad_value,
        grad_out,
        gain_sums[:, 1],
        grad_gate,
        grad_up,
        grad_down,
    )


def solution(mesh):
    return jax.shard_map(
        per_device,
        mesh=mesh,
        in_specs=(
            P(("dp", "tensor"), None),
            P("dp"),
            P("dp", "tensor"),
            P("dp", "tensor"),
            P("dp", "tensor"),
            P("tensor", "dp"),
            P("dp"),
            P("dp", "tensor"),
            P("dp", "tensor"),
            P("tensor", "dp"),
            P("dp"),
            P(("dp", "tensor"), None),
        ),
        out_specs=(
            P(("dp", "tensor"), None),
            P(("dp", "tensor"), None),
            P(("dp", "tensor")),
            P("dp", "tensor"),
            P("dp", "tensor"),
            P("dp", "tensor"),
            P("tensor", "dp"),
            P(("dp", "tensor")),
            P("dp", "tensor"),
            P("dp", "tensor"),
            P("tensor", "dp"),
        ),
        check_vma=False,
    )
```

```python
import functools
import math

import jax
import jax.numpy as jnp
from jax import lax
from jax.experimental import pallas as pl
from jax.experimental.pallas import tpu as pltpu
from jax.sharding import PartitionSpec as P

HEAD_DIM = 64
PAIR = 2 * HEAD_DIM
SEQ_LEN = 1024


EPS = 1e-05
ROPE_BASE = 500000.0
SCALE = 1.0 / math.sqrt(HEAD_DIM)
PARAMS = pltpu.CompilerParams(vmem_limit_bytes=58 * 2**20)
ONCE = pl.Buffered(1)

barrier = lax.optimization_barrier


def hint(flops):
    return pl.CostEstimate(flops=flops, bytes_accessed=0, transcendentals=0)


def rms_scale(values):
    return lax.rsqrt(jnp.mean(values * values, axis=-1, keepdims=True) + EPS)


def norm_back(grad, values, scale, gain):
    inner = grad * gain
    cubed = scale * scale * scale
    result = scale * inner - values * cubed * jnp.mean(inner * values, axis=-1, keepdims=True)
    return (result, jnp.sum(grad * values * scale, axis=0))


def mm(left, right):
    return jnp.dot(left, right, preferred_element_type=jnp.float32)


def mm_nt(left, right):
    return lax.dot_general(left, right, (((1,), (1,)), ((), ())), preferred_element_type=jnp.float32)


def mm_tn(left, right):
    return lax.dot_general(left, right, (((0,), (0,)), ((), ())), preferred_element_type=jnp.float32)


def lane_index(rows):
    return lax.broadcasted_iota(jnp.int32, (rows, PAIR), 1)


def turn(pair, cosine, sine):
    lower = lane_index(pair.shape[0]) % HEAD_DIM < HEAD_DIM // 2
    other = jnp.where(
        lower, pltpu.roll(pair, PAIR - HEAD_DIM // 2, 1), pltpu.roll(pair, HEAD_DIM // 2, 1)
    )
    return pair * cosine + other * sine


def project_kernel(place_ref, *refs, size, q_width, kv_width):
    x_refs = refs[:size]
    gain_ref, qo_ref, qx_ref, kvo_ref, kvx_ref, cos_ref, sin_ref = refs[size:-4]
    n_ref, q_ref, k_ref, v_ref = refs[-4:]
    rows = q_ref.shape[0]
    half = qo_ref.shape[0]

    def one(x_ref):
        x = x_ref[...].astype(jnp.float32)
        normed = (x * rms_scale(x) * gain_ref[...]).astype(jnp.bfloat16)
        n_ref[...] = normed
        cosine, sine = cos_ref[...], sin_ref[...]
        own, other = normed[:, :half], normed[:, half:]
        lin = mm(own, qo_ref[...]) + mm(other, qx_ref[...])
        for low in range(0, q_width, PAIR):
            query = turn(lin[:, low : low + PAIR], cosine, sine).astype(jnp.bfloat16)
            q_ref[:, low : low + PAIR] = query * jnp.bfloat16(SCALE)
        lin = mm(own, kvo_ref[...]) + mm(other, kvx_ref[...])
        first = lane_index(rows) < HEAD_DIM
        for ref, start, rotate in ((k_ref, 0, True), (v_ref, kv_width, False)):
            for head in range(kv_width // HEAD_DIM):
                low = start + head * HEAD_DIM
                block = lin[:, low // PAIR * PAIR : low // PAIR * PAIR + PAIR]
                if rotate:
                    block = turn(block, cosine, sine)
                moved = pltpu.roll(block, HEAD_DIM, 1)
                if low % PAIR:
                    block, moved = moved, block
                ref[head, 0] = jnp.where(first, block, 0.0).astype(jnp.bfloat16)
                ref[head, 1] = jnp.where(first, 0.0, moved).astype(jnp.bfloat16)

    for step in range(size):
        pl.when(pl.program_id(0) == step)(functools.partial(one, x_refs[step]))


class Columns:
    def __init__(self, q_width, kv_width):
        self.q_width, self.kv_width = q_width, kv_width

    def spec(self, part, rows, place=lambda *_: 0):
        width, start = {
            "q": (self.q_width, 0),
            "out": (self.q_width, self.q_width),
            "kv": (2 * self.kv_width, 2 * self.q_width),
        }[part]
        index = start // width
        mode = {"pipeline_mode": ONCE} if place() == 0 else {}
        return pl.BlockSpec((rows, width), lambda *grid: (place(*grid), index), **mode)


def project(me, blocks, gain, own, other, cosine, sine, columns):
    size = len(blocks)
    rows, features = blocks[0].shape
    total = rows * size
    q_width, kv_width = columns.q_width, columns.kv_width
    key_heads = kv_width // HEAD_DIM
    width = q_width + 2 * kv_width
    half = features // 2
    fixed = lambda p, m: (0, 0)
    placed = lambda p, m: (jnp.bitwise_xor(p, m[0]), 0)
    padded = pl.BlockSpec(
        (key_heads, 2, rows, PAIR), lambda p, m: (0, 0, jnp.bitwise_xor(p, m[0]), 0)
    )
    spec = pltpu.PrefetchScalarGridSpec(
        num_scalar_prefetch=1,
        grid=(size,),
        in_specs=[pl.BlockSpec((rows, features), fixed, pipeline_mode=ONCE)] * size
        + [
            pl.BlockSpec((1, features), fixed),
            columns.spec("q", half),
            columns.spec("q", half),
            columns.spec("kv", half),
            columns.spec("kv", half),
            pl.BlockSpec((rows, PAIR), placed),
            pl.BlockSpec((rows, PAIR), placed),
        ],
        out_specs=[
            pl.BlockSpec((rows, features), lambda p, m: (p, 0)),
            pl.BlockSpec((rows, q_width), lambda p, m: (p, 0)),
            padded,
            padded,
        ],
    )
    padded_shape = jax.ShapeDtypeStruct((key_heads, 2, total, PAIR), jnp.bfloat16)
    return pl.pallas_call(
        functools.partial(project_kernel, size=size, q_width=q_width, kv_width=kv_width),
        grid_spec=spec,
        out_shape=[
            jax.ShapeDtypeStruct((total, features), jnp.bfloat16),
            jax.ShapeDtypeStruct((total, q_width), jnp.bfloat16),
            padded_shape,
            padded_shape,
        ],
        compiler_params=PARAMS,
        cost_estimate=hint(2 * total * features * width // 16),
    )(me, *blocks, gain, own, other, own, other, cosine, sine)


def attend_kernel(
    me_ref, q_ref, k_ref, v_ref, wo_ref, wx_ref, o_ref, l_ref, *refs, size, heads, group
):
    part_refs, vt_ref = refs[:size], refs[size]
    rows = q_ref.shape[0]
    half = wo_ref.shape[0]
    mine = jnp.bitwise_xor(me_ref[0], pl.program_id(0))
    key_place = lax.broadcasted_iota(jnp.int32, (rows, rows), 0)
    query_place = lax.broadcasted_iota(jnp.int32, (rows, rows), 1)

    @pl.when(pl.program_id(0) == 0)
    def _():
        for head in range(heads // group):
            for side in range(2):
                vt_ref[head, side] = v_ref[head, side].T

    def one(span):
        keys = span * rows
        for pair in range(heads // 2):
            head = 2 * pair // group
            lanes = slice(pair * PAIR, (pair + 1) * PAIR)
            query = q_ref[:, lanes]
            acc = None
            inverse = []
            for side in range(2):
                diag = mm_nt(k_ref[head, side, keys : keys + rows, :], query)
                diag = jnp.where(key_place <= query_place, diag, -1e9)
                top = jnp.max(diag, axis=0, keepdims=True)
                if span:
                    body = mm_nt(k_ref[head, side, :keys, :], query)
                    top = jnp.maximum(top, jnp.max(body, axis=0, keepdims=True))
                diag = jnp.exp(diag - top)
                total = jnp.sum(diag, axis=0, keepdims=True)
                part = mm(vt_ref[head, side, :, keys : keys + rows], diag.astype(jnp.bfloat16))
                if span:
                    body = jnp.exp(body - top)
                    total = total + jnp.sum(body, axis=0, keepdims=True)
                    part = part + mm(vt_ref[head, side, :, :keys], body.astype(jnp.bfloat16))
                acc = part if acc is None else acc + part
                inverse.append(jnp.broadcast_to(1.0 / total, (HEAD_DIM, rows)))
                l_ref[2 * pair + side : 2 * pair + side + 1, :] = top + jnp.log(total)
            acc = acc * jnp.concatenate(inverse, axis=0)
            o_ref[:, lanes] = acc.T.astype(jnp.bfloat16)

    for span in range(size):
        pl.when(mine == span)(functools.partial(one, span))

    def project_out(ref):
        ref[:, :half] = mm_nt(o_ref[...], wo_ref[...]).astype(jnp.bfloat16)
        ref[:, half:] = mm_nt(o_ref[...], wx_ref[...]).astype(jnp.bfloat16)

    for step in range(size):
        pl.when(pl.program_id(0) == step)(functools.partial(project_out, part_refs[step]))


def attend(me, query, key_pad, value_pad, own, other, columns, size, group):
    total, width = query.shape
    features = 2 * own.shape[0]
    rows, heads = total // size, width // HEAD_DIM
    whole = pl.BlockSpec(key_pad.shape, lambda p, m: (0, 0, 0, 0), pipeline_mode=ONCE)
    spec = pltpu.PrefetchScalarGridSpec(
        num_scalar_prefetch=1,
        grid=(size,),
        in_specs=[pl.BlockSpec((rows, width), lambda p, m: (p, 0)), whole, whole]
        + [columns.spec("out", features // 2)] * 2,
        out_specs=[
            pl.BlockSpec((rows, width), lambda p, m: (p, 0)),
            pl.BlockSpec((heads, rows), lambda p, m: (0, p)),
        ]
        + [pl.BlockSpec((rows, features), lambda p, m: (0, 0))] * size,
        scratch_shapes=[pltpu.VMEM((heads // group, 2, PAIR, total), jnp.bfloat16)],
    )
    return pl.pallas_call(
        functools.partial(attend_kernel, size=size, heads=heads, group=group),
        grid_spec=spec,
        out_shape=[
            jax.ShapeDtypeStruct((total, width), jnp.bfloat16),
            jax.ShapeDtypeStruct((heads, total), jnp.float32),
        ]
        + [jax.ShapeDtypeStruct((rows, features), jnp.bfloat16)] * size,
        compiler_params=PARAMS,
        cost_estimate=hint(8 * heads * total * total * HEAD_DIM // 16),
    )(me, query, key_pad, value_pad, own, other)


def attend_back_kernel(
    me_ref, q_ref, l_ref, k_ref, v_ref, cos_ref, sin_ref, *refs, size, heads, group
):
    do_refs = refs[:size]
    out_ref, dk_ref, dv_ref, kt_ref, do_ref = refs[size:]
    rows = q_ref.shape[0]
    key_heads = heads // group
    step = pl.program_id(0)
    me = me_ref[0]
    mine = jnp.bitwise_xor(me, step)
    key_place = lax.broadcasted_iota(jnp.int32, (rows, rows), 0)
    query_place = lax.broadcasted_iota(jnp.int32, (rows, rows), 1)

    def rows_of(block):
        return pl.ds(pl.multiple_of(block * rows, rows), rows)

    @pl.when(step == 0)
    def _():
        dk_ref[...] = jnp.zeros_like(dk_ref)
        dv_ref[...] = jnp.zeros_like(dv_ref)
        for head in range(key_heads):
            for side in range(2):
                kt_ref[head, side] = k_ref[head, side].T

    def fetch(ref):
        do_ref[...] = ref[...]

    for block in range(size):
        pl.when(step == block)(functools.partial(fetch, do_refs[block]))

    def one(span):
        keys = span * rows
        parts = [(keys, keys + rows, True)] + ([(0, keys, False)] if span else [])
        cosine, sine = cos_ref[keys : keys + rows, :], sin_ref[keys : keys + rows, :]
        for pair in range(heads // 2):
            head = 2 * pair // group
            lanes = slice(pair * PAIR, (pair + 1) * PAIR)
            query, grad = q_ref[:, lanes], do_ref[:, lanes]
            acc = None
            for side in range(2):
                log_total = l_ref[2 * pair + side : 2 * pair + side + 1, :]
                inner = None
                kept = []
                for low, high, diagonal in parts:
                    probs = mm_nt(k_ref[head, side, low:high, :], query)
                    probs = jnp.exp(probs - log_total)
                    if diagonal:
                        probs = jnp.where(key_place <= query_place, probs, 0.0)
                    prob_grad = mm_nt(v_ref[head, side, low:high, :], grad)
                    dv_ref[head, side, low:high, :] += mm(probs.astype(jnp.bfloat16), grad)
                    term = jnp.sum(probs * prob_grad, axis=0, keepdims=True)
                    inner = term if inner is None else inner + term
                    kept.append((low, high, probs, prob_grad))
                for low, high, probs, prob_grad in kept:
                    score_grad = (probs * (prob_grad - inner)).astype(jnp.bfloat16)
                    dk_ref[head, side, low:high, :] += mm(score_grad, query)
                    part = mm(kt_ref[head, side, :, low:high], score_grad)
                    acc = part if acc is None else acc + part
            turned = turn(acc.T * SCALE, cosine, -sine)
            out_ref[rows_of(step), lanes] = turned.astype(jnp.bfloat16)

    for span in range(size):
        pl.when(mine == span)(functools.partial(one, span))

    @pl.when(step == size - 1)
    def _():
        first = lane_index(rows) < HEAD_DIM
        wanted = [(dk_ref, head, True) for head in range(key_heads)]
        wanted += [(dv_ref, head, False) for head in range(key_heads)]
        for span in range(size):
            place = slice(span * rows, (span + 1) * rows)
            cosine, sine = cos_ref[place, :], sin_ref[place, :]
            for block in range(len(wanted) // 2):
                halves, rotate = [], []
                for half in range(2):
                    ref, head, is_key = wanted[2 * block + half]
                    low, high = ref[head, 0, place, :], ref[head, 1, place, :]
                    if half:
                        halves.append(pltpu.roll(low, HEAD_DIM, 1) + high)
                    else:
                        halves.append(low + pltpu.roll(high, HEAD_DIM, 1))
                    rotate.append(is_key)
                value = jnp.where(first, halves[0], halves[1])
                if rotate[0] and rotate[1]:
                    value = turn(value, cosine, -sine)
                elif rotate[0]:
                    value = jnp.where(first, turn(value, cosine, -sine), value)
                start = heads * HEAD_DIM + block * PAIR
                target = rows_of(jnp.bitwise_xor(me, span))
                out_ref[target, start : start + PAIR] = value.astype(jnp.bfloat16)


def attend_back(
    me, query, log_total, key_pad, value_pad, cosine, sine, attended_grad, group
):
    total, width = query.shape
    size = len(attended_grad)
    rows, heads = total // size, width // HEAD_DIM
    key_heads = heads // group
    out_width = width + 2 * key_heads * HEAD_DIM
    whole = pl.BlockSpec(key_pad.shape, lambda p, m: (0, 0, 0, 0), pipeline_mode=ONCE)
    table = pl.BlockSpec((total, PAIR), lambda p, m: (0, 0), pipeline_mode=ONCE)
    spec = pltpu.PrefetchScalarGridSpec(
        num_scalar_prefetch=1,
        grid=(size,),
        in_specs=[
            pl.BlockSpec((rows, width), lambda p, m: (p, 0)),
            pl.BlockSpec((heads, rows), lambda p, m: (0, p)),
            whole,
            whole,
            table,
            table,
        ]
        + [pl.BlockSpec((rows, width), lambda p, m: (0, 0), pipeline_mode=ONCE)] * size,
        out_specs=pl.BlockSpec((total, out_width), lambda p, m: (0, 0)),
        scratch_shapes=[
            pltpu.VMEM(key_pad.shape, jnp.float32),
            pltpu.VMEM(key_pad.shape, jnp.float32),
            pltpu.VMEM((key_heads, 2, PAIR, total), jnp.bfloat16),
            pltpu.VMEM((rows, width), jnp.bfloat16),
        ],
    )
    return pl.pallas_call(
        functools.partial(attend_back_kernel, size=size, heads=heads, group=group),
        grid_spec=spec,
        out_shape=jax.ShapeDtypeStruct((total, out_width), jnp.bfloat16),
        compiler_params=PARAMS,
        cost_estimate=hint(20 * heads * total * total * HEAD_DIM),
    )(me, query, log_total, key_pad, value_pad, cosine, sine, *attended_grad)


def grouped(arrays, counts):
    arrays = iter(arrays)
    return [[next(arrays) for _ in range(count)] for count in counts]


def mlp_kernel(*refs, n_counts, e_counts, adds):
    size = len(n_counts)
    pieces = sum(n_counts) + sum(e_counts)
    n_refs = grouped(refs, n_counts)
    e_refs = grouped(refs[sum(n_counts) :], e_counts)
    gate_o, up_o, down_o, gate_x, up_x, down_x = refs[pieces : pieces + 6]
    y_ref, n_ref, e_ref = refs[-3:]
    dn_refs = refs[-3 - size if adds else -4 : -3]
    dg_ref, du_ref, h_ref = refs[-6 - size if adds else -7 :][:3]
    half = gate_o.shape[0]

    def fetch(step):
        for target, sources in ((n_ref, n_refs[step]), (e_ref, e_refs[step])):
            low = 0
            for source in sources:
                high = low + source.shape[0]
                target[low:high] = source[...]
                low = high

    for step in range(size):
        pl.when(pl.program_id(0) == step)(functools.partial(fetch, step))
    gate = mm(n_ref[:, :half], gate_o[...]) + mm(n_ref[:, half:], gate_x[...])
    up = mm(n_ref[:, :half], up_o[...]) + mm(n_ref[:, half:], up_x[...])
    grad = mm(e_ref[:, :half], down_o[...]) + mm(e_ref[:, half:], down_x[...])
    sigma = jax.nn.sigmoid(gate)
    silu = gate * sigma
    hidden = (silu * up).astype(jnp.bfloat16)
    gate_grad = (grad * up * sigma * (1.0 + gate * (1.0 - sigma))).astype(jnp.bfloat16)
    up_grad = (grad * silu).astype(jnp.bfloat16)
    dg_ref[...] = gate_grad
    du_ref[...] = up_grad
    h_ref[...] = hidden
    for part, gate_w, up_w, down_w in ((0, gate_o, up_o, down_o), (1, gate_x, up_x, down_x)):
        lanes = slice(part * half, (part + 1) * half)
        dn = mm_nt(gate_grad, gate_w[...]) + mm_nt(up_grad, up_w[...])
        y = mm_nt(hidden, down_w[...])
        if adds:
            dn = dn + refs[pieces + 6][:, lanes].astype(jnp.float32)
            y = y + refs[pieces + 7][:, lanes].astype(jnp.float32)
        y_ref[:, lanes] = y.astype(jnp.bfloat16)
        dn = dn.astype(jnp.bfloat16)

        def store(ref):
            ref[:, lanes] = dn

        if adds:
            for step in range(size):
                pl.when(pl.program_id(0) == step)(functools.partial(store, dn_refs[step]))
        else:
            store(dn_refs[0])


def mlp(tokens, cot, own, other, earlier):
    size = len(tokens)
    rows, features = tokens[0][0].shape
    half, units = own.shape[0], own.shape[1] // 3
    total = rows * size
    fixed = lambda p: (0, 0)
    moving = lambda p: (p, 0)
    wide = pl.BlockSpec((rows, features), moving)
    sums = jax.ShapeDtypeStruct((total, features), jnp.bfloat16)
    dn_specs, dn_shapes = [wide], [sums]
    if earlier:
        dn_specs = [pl.BlockSpec((rows, features), fixed)] * size
        dn_shapes = [jax.ShapeDtypeStruct((rows, features), jnp.bfloat16)] * size
    pieces = sum(tokens, []) + sum(cot, [])
    thirds = [
        pl.BlockSpec((half, units), lambda p, t=t: (0, t), pipeline_mode=ONCE) for t in range(3)
    ]
    return pl.pallas_call(
        functools.partial(
            mlp_kernel,
            n_counts=[len(group) for group in tokens],
            e_counts=[len(group) for group in cot],
            adds=bool(earlier),
        ),
        grid=(size,),
        in_specs=[pl.BlockSpec(piece.shape, fixed, pipeline_mode=ONCE) for piece in pieces]
        + thirds * 2
        + [wide] * len(earlier),
        out_specs=[pl.BlockSpec((rows, units), moving)] * 3 + dn_specs + [wide],
        out_shape=[jax.ShapeDtypeStruct((total, units), jnp.bfloat16)] * 3 + dn_shapes + [sums],
        scratch_shapes=[pltpu.VMEM((rows, features), jnp.bfloat16)] * 2,
        compiler_params=PARAMS,
        cost_estimate=hint(12 * total * features * units),
    )(*pieces, own, own, own, other, other, other, *earlier)


def add_refs(refs):
    total = refs[0][...].astype(jnp.float32)
    for ref in refs[1:]:
        total = total + ref[...].astype(jnp.float32)
    return total


def store_by_device(out_ref, values, core, chips):
    width = values.shape[1] // (2 * chips)
    for chip in range(chips):
        own = values[:, chip * width : (chip + 1) * width]
        other = values[:, (chips + chip) * width : (chips + chip + 1) * width]
        low = 2 * chip * width
        out_ref[:, low : low + width] = jnp.where(core == 0, own, other)
        out_ref[:, low + width : low + 2 * width] = jnp.where(core == 0, other, own)


def middle_kernel(*refs):
    x_ref, gain_ref, middle_ref, normed_ref = refs[-4:]
    values = x_ref[...].astype(jnp.float32) + add_refs(refs[:-4])
    middle_ref[...] = values
    normed_ref[...] = (values * rms_scale(values) * gain_ref[...]).astype(jnp.bfloat16)


def input_back_kernel(core_ref, *refs, chips):
    x_ref, before_ref, gain_ref, out_ref = refs[-4:]
    values = x_ref[...].astype(jnp.float32)
    inner = add_refs(refs[:-4]) * gain_ref[...]
    scale = rms_scale(values)
    mean = jnp.mean(inner * values, axis=-1, keepdims=True)
    result = before_ref[...] + scale * inner - values * (scale * scale * scale) * mean
    store_by_device(out_ref, result, core_ref[0], chips)


def output_kernel(core_ref, *refs, chips):
    middle_ref, out_ref = refs[-2:]
    values = middle_ref[...] + add_refs(refs[:-2])
    store_by_device(out_ref, values.astype(jnp.bfloat16), core_ref[0], chips)


def row_call(body, dtypes, arrays, core=None):
    rows, features = arrays[0].shape
    steps = 2
    wide = pl.BlockSpec((rows // steps, features), lambda i, *_: (i, 0))
    row = pl.BlockSpec((1, features), lambda i, *_: (0, 0))
    scalars = [] if core is None else [jnp.full((1,), core, jnp.int32)]
    return pl.pallas_call(
        body,
        grid_spec=pltpu.PrefetchScalarGridSpec(
            num_scalar_prefetch=len(scalars),
            grid=(steps,),
            in_specs=[row if array.shape[0] == 1 else wide for array in arrays],
            out_specs=[wide] * len(dtypes),
        ),
        out_shape=[jax.ShapeDtypeStruct((rows, features), dtype) for dtype in dtypes],
        compiler_params=PARAMS,
        cost_estimate=hint(0),
    )(*scalars, *arrays)


def unpack_kernel(sum_ref, q_ref, k_ref, v_ref, out_ref):
    q_width, kv_width = q_ref.shape[1], k_ref.shape[1]
    values = sum_ref[...].astype(jnp.float32)
    q_ref[...] = values[:, :q_width]
    kv = values[:, q_width : q_width + 2 * kv_width]
    k_ref[...] = kv[:, :kv_width]
    v_ref[...] = kv[:, kv_width:]
    out_ref[...] = values[:, q_width + 2 * kv_width :].T


def unpack(sums, q_width, kv_width):
    rows = sums.shape[0]
    widths = [(rows, q_width), (rows, kv_width), (rows, kv_width), (q_width, rows)]
    return pl.pallas_call(
        unpack_kernel,
        out_shape=[jax.ShapeDtypeStruct(shape, jnp.float32) for shape in widths],
        compiler_params=PARAMS,
        cost_estimate=hint(0),
    )(sums)


def unpack_shares_kernel(one_ref, two_ref, gate_ref, up_ref, down_ref):
    units = one_ref.shape[1] // 3
    for part, ref in enumerate((one_ref, two_ref)):
        cut = slice(part * units, (part + 1) * units)
        gate_ref[:, cut] = ref[:, :units].astype(jnp.float32)
        up_ref[:, cut] = ref[:, units : 2 * units].astype(jnp.float32)
        down_ref[cut, :] = ref[:, 2 * units :].astype(jnp.float32).T


def unpack_shares(one, two):
    rows, width = one.shape
    units = 2 * width // 3
    shapes = [(rows, units), (rows, units), (units, rows)]
    return pl.pallas_call(
        unpack_shares_kernel,
        out_shape=[jax.ShapeDtypeStruct(shape, jnp.float32) for shape in shapes],
        compiler_params=PARAMS,
        cost_estimate=hint(0),
    )(one, two)


def middle_back_kernel(*refs, parts, size):
    n_refs, refs = refs[:parts], refs[parts:]
    x_ref, e_ref, gain_ref, refs = refs[0], refs[1], refs[2], refs[3:]
    own_refs, other_refs, refs = refs[:size], refs[size : 2 * size], refs[2 * size :]
    grad_ref, branch_ref, part_ref, do_refs = refs[0], refs[1], refs[2], refs[3:]
    half = own_refs[0].shape[0]
    grad = add_refs(n_refs)
    values = x_ref[...]
    scale = rms_scale(values)
    result, part = norm_back(grad, values, scale, gain_ref[...])

    @pl.when(pl.program_id(0) == 0)
    def _():
        part_ref[...] = jnp.zeros_like(part_ref)

    part_ref[...] += part[None, :]
    result = result + e_ref[...].astype(jnp.float32)
    grad_ref[...] = result
    branch = result.astype(jnp.bfloat16)
    branch_ref[...] = branch
    for own, other, do_ref in zip(own_refs, other_refs, do_refs):
        do = mm(branch[:, :half], own[...]) + mm(branch[:, half:], other[...])
        do_ref[...] = do.astype(jnp.bfloat16)


def middle_back(arrived, middle, cot, gain, own, other):
    parts, size = len(arrived), len(own)
    rows, features = middle.shape
    width = own[0].shape[1]
    steps = 2
    wide = pl.BlockSpec((rows // steps, features), lambda i: (i, 0))
    narrow = pl.BlockSpec((rows // steps, width), lambda i: (i, 0))
    row = pl.BlockSpec((1, features), lambda i: (0, 0))
    weight = pl.BlockSpec((features // 2, width), lambda i: (0, 0), pipeline_mode=ONCE)
    grad, branch, part, *do = pl.pallas_call(
        functools.partial(middle_back_kernel, parts=parts, size=size),
        grid=(steps,),
        in_specs=[wide] * parts + [wide, wide, row] + [weight] * (2 * size),
        out_specs=[wide, wide, row] + [narrow] * size,
        out_shape=[
            jax.ShapeDtypeStruct((rows, features), jnp.float32),
            jax.ShapeDtypeStruct((rows, features), jnp.bfloat16),
            jax.ShapeDtypeStruct((1, features), jnp.float32),
        ]
        + [jax.ShapeDtypeStruct((rows, width), jnp.bfloat16)] * size,
        compiler_params=PARAMS,
        cost_estimate=hint(2 * rows * features * width * size),
    )(*arrived, middle, cot, gain, *own, *other)
    return grad, branch, part[0], do


def column_grad(blocks, other, mine, theirs):
    total = mm_tn(other[...], theirs[...])
    low = 0
    for block in blocks:
        high = low + block.shape[0]
        total = total + mm_tn(block[...], mine[low:high, :])
        low = high
    return total


def grad_kernel(*refs, n_count, e_count):
    n_refs, refs = refs[:n_count], refs[n_count:]
    e_refs, refs = refs[:e_count], refs[e_count:]
    n_other, e_other = refs[:2]
    acts, out_ref = refs[2:-1], refs[-1]
    units = acts[0].shape[1]
    for third in range(3):
        blocks, other = (e_refs, e_other) if third == 2 else (n_refs, n_other)
        grad = column_grad(blocks, other, acts[third], acts[third + 3])
        out_ref[0, :, third * units : (third + 1) * units] = grad.astype(jnp.bfloat16)


def mlp_grads(chips, tokens, cot, tokens_other, cot_other, mine, theirs):
    tokens, cot = sum(tokens, []), sum(cot, [])
    features = tokens[0].shape[1]
    total, units = mine[0].shape
    depth = features // (2 * chips)
    long = pl.BlockSpec((total, depth), lambda b: (0, b))
    fixed = pl.BlockSpec((total, units), lambda b: (0, 0), pipeline_mode=ONCE)
    return pl.pallas_call(
        functools.partial(grad_kernel, n_count=len(tokens), e_count=len(cot)),
        grid=(chips,),
        in_specs=[pl.BlockSpec((p.shape[0], depth), lambda b: (0, b)) for p in tokens + cot]
        + [long, long]
        + [fixed] * 6,
        out_specs=pl.BlockSpec((1, depth, 3 * units), lambda b: (b, 0, 0)),
        out_shape=jax.ShapeDtypeStruct((chips, depth, 3 * units), jnp.bfloat16),
        compiler_params=PARAMS,
        cost_estimate=hint(6 * total * features * units),
    )(*tokens, *cot, tokens_other, cot_other, *mine, *theirs)


def attn_grad_kernel(*refs, size):
    e_refs = refs[2 : 2 + size]
    n_ref, n_other = refs[:2]
    e_other, d_ref, d_other, o_ref, o_other, q_ref, kv_ref, g1_ref, g2_ref = refs[2 + size : -2]
    out_ref, gain_ref = refs[-2:]
    width, out_width = d_ref.shape[1], o_ref.shape[1]
    grad = column_grad([n_ref], n_other, d_ref, d_other)
    out_ref[0, :, :width] = grad.astype(jnp.bfloat16)
    out_grad = column_grad(e_refs, e_other, o_ref, o_other)
    out_ref[0, :, width : width + out_width] = out_grad.astype(jnp.bfloat16)
    cut = q_ref.shape[1]
    first = jnp.sum(grad[:, :cut] * q_ref[...].astype(jnp.float32), axis=1, keepdims=True)
    first += jnp.sum(grad[:, cut:] * kv_ref[...].astype(jnp.float32), axis=1, keepdims=True)
    first = first / g1_ref[...]
    lane = lane_index(grad.shape[0])
    gain_ref[0] = jnp.where(lane == 0, first, g2_ref[...])


def attn_grads(
    chips, tokens, branch, mine, theirs, weights, columns, gain_one, gain_two_part
):
    size = len(branch)
    qkv_grad, attended = mine
    tokens_other, branch_other, qkv_other, attended_other = theirs
    total, features = tokens.shape
    rows = total // size
    width, out_width = qkv_grad.shape[1], attended.shape[1]
    depth = features // (2 * chips)
    column = lambda b: (0, b)
    row = lambda b: (b, 0)
    long = pl.BlockSpec((total, depth), column)
    fixed = lambda array: pl.BlockSpec(array.shape, lambda b: (0, 0), pipeline_mode=ONCE)
    place = lambda b: (b, 0, 0)
    return pl.pallas_call(
        functools.partial(attn_grad_kernel, size=size),
        grid=(chips,),
        in_specs=[long, long]
        + [pl.BlockSpec((rows, depth), column)] * size
        + [long]
        + [fixed(qkv_grad)] * 2
        + [fixed(attended)] * 2
        + [
            columns.spec("q", depth, lambda b=None: b),
            columns.spec("kv", depth, lambda b=None: b),
            pl.BlockSpec((depth, 1), row),
            pl.BlockSpec((depth, 1), row),
        ],
        out_specs=[
            pl.BlockSpec((1, depth, width + out_width), place),
            pl.BlockSpec((1, depth, PAIR), place),
        ],
        out_shape=[
            jax.ShapeDtypeStruct((chips, depth, width + out_width), jnp.bfloat16),
            jax.ShapeDtypeStruct((chips, depth, PAIR), jnp.float32),
        ],
        compiler_params=PARAMS,
        cost_estimate=hint(2 * total * features * (width + out_width)),
    )(
        tokens,
        tokens_other,
        *branch,
        branch_other,
        qkv_grad,
        qkv_other,
        attended,
        attended_other,
        weights,
        weights,
        gain_one,
        gain_two_part,
    )


def input_grad_kernel(d_ref, qo_ref, qx_ref, kvo_ref, kvx_ref, *out_refs):
    half, cut = qo_ref.shape

    def one(ref):
        query, rest = d_ref[:, :cut], d_ref[:, cut:]
        own = mm_nt(query, qo_ref[...]) + mm_nt(rest, kvo_ref[...])
        other = mm_nt(query, qx_ref[...]) + mm_nt(rest, kvx_ref[...])
        ref[:, :half] = own.astype(jnp.bfloat16)
        ref[:, half:] = other.astype(jnp.bfloat16)

    for step, ref in enumerate(out_refs):
        pl.when(pl.program_id(0) == step)(functools.partial(one, ref))


def input_grad(qkv_grad, own, other, columns, size):
    total, width = qkv_grad.shape
    features = 2 * own.shape[0]
    rows = total // size
    fixed = lambda i: (0, 0)
    weights = [columns.spec(part, own.shape[0]) for part in ("q", "q", "kv", "kv")]
    return pl.pallas_call(
        input_grad_kernel,
        grid=(size,),
        in_specs=[pl.BlockSpec((rows, width), lambda i: (i, 0))] + weights,
        out_specs=[pl.BlockSpec((rows, features), fixed)] * size,
        out_shape=[jax.ShapeDtypeStruct((rows, features), jnp.bfloat16)] * size,
        compiler_params=PARAMS,
        cost_estimate=hint(2 * total * features * width),
    )(qkv_grad, own, other, own, other)


def swap(values, step):
    size = lax.axis_size("tensor")
    return lax.ppermute(values, "tensor", [(i, i ^ step) for i in range(size)])


def spread(values):
    return [values] + [swap(values, step) for step in range(1, lax.axis_size("tensor"))]


def send_blocks(blocks):
    return [blocks[0]] + [swap(block, step + 1) for step, block in enumerate(blocks[1:])]


def spread_around(values, held):
    if lax.axis_size("tensor") != 4:
        blocks = spread(values)
        first, held = barrier((blocks[1], held))
        return [[blocks[0]], [first]] + [[block] for block in blocks[2:]], held
    half = values.shape[0] // 2
    top, bottom = values[:half], values[half:]
    x_bottom, y_top = swap(bottom, 1), swap(top, 2)
    x_bottom, y_top, top, bottom, held = barrier((x_bottom, y_top, top, bottom, held))
    far = [swap(y_top, 1), swap(x_bottom, 2)]
    x_top, y_bottom = swap(top, 1), swap(bottom, 2)
    return [[values], [x_top, x_bottom], [y_top, y_bottom], far], held


def merge_kernel(x_ref, y_ref, top_ref, bottom_ref, x_out, y_out):
    half = top_ref.shape[0]
    x_out[:half] = x_ref[:half]
    x_out[half:] = add_refs([x_ref.at[half:], bottom_ref]).astype(jnp.bfloat16)
    y_out[:half] = add_refs([y_ref.at[:half], top_ref]).astype(jnp.bfloat16)
    y_out[half:] = y_ref[half:]


def send_sum(blocks, held=()):
    if len(blocks) != 4:
        return send_blocks(blocks), held
    own, near_x, near_y, far = blocks
    half = far.shape[0] // 2
    top, bottom = swap(far[:half], 1), swap(far[half:], 2)
    near_x, near_y = pl.pallas_call(
        merge_kernel,
        out_shape=[jax.ShapeDtypeStruct(near_x.shape, near_x.dtype)] * 2,
        compiler_params=PARAMS,
        cost_estimate=hint(0),
    )(near_x, near_y, top, bottom)
    near_x, near_y, held = barrier((near_x, near_y, held))
    return [own, swap(near_x, 1), swap(near_y, 2)], held


def add_up(blocks):
    total = blocks[0].astype(jnp.float32)
    for block in blocks[1:]:
        total = total + block.astype(jnp.float32)
    return total


def cross(values):
    count = lax.axis_size("dp")
    return lax.ppermute(values, "dp", [(i, i ^ 1) for i in range(count)])


def tables(positions):
    freqs = ROPE_BASE ** (-jnp.arange(0, HEAD_DIM, 2).astype(jnp.float32) / HEAD_DIM)
    angles = positions.astype(jnp.float32)[:, None] * freqs[None, :]
    cosine, sine = jnp.cos(angles), jnp.sin(angles)
    return (
        jnp.concatenate([cosine] * 4, axis=1),
        jnp.concatenate([-sine, sine, -sine, sine], axis=1),
    )


def chip_lines():
    count = lax.axis_size("dp")
    return [list(range(core, count, 2)) for core in range(2)]


def gather(values):
    return lax.all_gather(values, "dp", axis=0, tiled=True, axis_index_groups=chip_lines())


def scatter(values):
    total = lax.psum_scatter(
        values, "dp", scatter_dimension=0, tiled=True, axis_index_groups=chip_lines()
    )
    return total[0]


def along(values, step):
    count = lax.axis_size("dp")
    return lax.ppermute(values, "dp", [(i, (i + 2 * step) % count) for i in range(count)])


def line_parts(parts):
    chips = lax.axis_size("dp") // 2
    chip = lax.axis_index("dp") // 2
    blocks = [lax.dynamic_index_in_dim(parts, chip, 0, keepdims=False)]
    for step in range(1, chips):
        sent = lax.dynamic_index_in_dim(parts, (chip + step) % chips, 0, keepdims=False)
        blocks.append(along(sent, step))
    return blocks


def own_part(values):
    size = lax.axis_size("tensor")
    me = lax.axis_index("tensor")
    blocks = values.reshape((size, -1) + values.shape[1:])
    own = lax.dynamic_index_in_dim(blocks, me, 0, keepdims=False)
    for step in range(1, size):
        sent = lax.dynamic_index_in_dim(blocks, me ^ step, 0, keepdims=False)
        own = own + swap(sent, step)
    return own


def stack_kernel(*refs):
    low = 0
    for ref in refs[:-1]:
        high = low + ref.shape[0]
        refs[-1][low:high, :] = ref[...]
        low = high


def other_half(blocks):
    features = blocks[0].shape[1]
    shape = (sum(block.shape[0] for block in blocks), features // 2)
    halves = pl.pallas_call(
        stack_kernel,
        grid=(1,),
        in_specs=[pl.BlockSpec((b.shape[0], features // 2), lambda i: (0, 1)) for b in blocks],
        out_specs=pl.BlockSpec(shape, lambda i: (0, 0)),
        out_shape=jax.ShapeDtypeStruct(shape, blocks[0].dtype),
        compiler_params=PARAMS,
        cost_estimate=hint(0),
    )(*blocks)
    return cross(halves)


def feature_blocks(values):
    width = values.shape[-1] // lax.axis_size("dp")
    return [values[..., low : low + width] for low in range(0, values.shape[-1], width)]


def by_core(values, core):
    blocks = feature_blocks(values)
    pairs = list(zip(blocks[0::2], blocks[1::2]))
    own = [jnp.where(core == 0, even, odd) for even, odd in pairs]
    other = [jnp.where(core == 0, odd, even) for even, odd in pairs]
    return jnp.concatenate(own + other, axis=-1)


def per_device(
    hidden_in,
    gain_attn,
    w_query,
    w_key,
    w_value,
    w_out,
    gain_mlp,
    w_gate,
    w_up,
    w_down,
    positions,
    cotangent,
):
    size = lax.axis_size("tensor")
    chips = lax.axis_size("dp") // 2
    me = lax.axis_index("tensor")
    me_array = jnp.full((1,), me, jnp.int32)
    core = lax.axis_index("dp") % 2
    q_width, kv_width = w_query.shape[1], w_key.shape[1]
    group = q_width // kv_width
    units = w_down.shape[0] // 2
    half = hidden_in.shape[1] // 2

    columns = Columns(q_width, kv_width)
    attn_shard = jnp.concatenate([w_query, w_out.T, w_key, w_value], axis=1)
    attn_shard, hidden_in, gain_attn = barrier((attn_shard, hidden_in, gain_attn))
    attn_own = gather(attn_shard)
    residual = by_core(hidden_in, core)
    blocks_in = spread(residual)
    gains = lax.all_gather(jnp.stack([gain_attn, gain_mlp]), "dp", axis=1, tiled=True)
    gains = by_core(gains, core).astype(jnp.float32)
    cosine, sine = tables(positions)
    cotangent = by_core(cotangent, core)
    down_t = w_down.T
    shares = []
    for part in range(2):
        cut = slice(part * units, (part + 1) * units)
        shares.append(jnp.concatenate([w_gate[:, cut], w_up[:, cut], down_t[:, cut]], axis=1))
    shares, attn_own, blocks_in, cosine, sine, gains, cotangent = barrier(
        (shares, attn_own, blocks_in, cosine, sine, gains, cotangent)
    )
    mlp_own = [gather(share) for share in shares]
    cot_blocks = spread(cotangent)
    gain_one, gain_two = gains[0], gains[1]
    attn = (attn_own, cross(attn_own))

    tokens_one, query, key_pad, value_pad = project(
        me_array, blocks_in, gain_one[None, :], *attn, cosine, sine, columns
    )
    attended, log_total, *parts = attend(
        me_array, query, key_pad, value_pad, *attn, columns, size, group
    )
    parts, cot_blocks, tokens_one, attended = barrier((parts, cot_blocks, tokens_one, attended))
    arrived, _ = send_sum(parts)
    cot_other = other_half(cot_blocks)
    cot_blocks = [[block] for block in cot_blocks]
    early = (cross(tokens_one[:, half:]), cross(attended))
    arrived, cot_other, early = barrier((arrived, cot_other, early))
    out_t = [w[:, q_width : 2 * q_width] for w in attn]
    middle, normed_two = row_call(
        middle_kernel, [jnp.float32, jnp.bfloat16], [*arrived, residual, gain_two[None, :]]
    )
    tokens_two, own_share = spread_around(normed_two, mlp_own[0])
    weights = (own_share, cross(own_share))
    tokens_two, weights, out_own = barrier((tokens_two, weights, out_t[0]))
    tokens_other = other_half(sum(tokens_two, []))
    *acts, dn_part, y_part = mlp(tokens_two, cot_blocks, *weights, ())
    out_blocks = spread(out_own)
    acts, tokens_other = barrier((acts, tokens_other))
    acts_other = [cross(act) for act in acts]
    grads_one = mlp_grads(
        chips, tokens_two, cot_blocks, tokens_other, cot_other, acts, acts_other
    )
    grads_one, own_share = barrier((grads_one, mlp_own[1]))
    sums_one = scatter(grads_one)
    weights = (own_share, cross(own_share))
    *acts, y_part = mlp(tokens_two, cot_blocks, *weights, (dn_part, y_part))
    acts, dn_part = acts[:3], acts[3:]
    acts, dn_part, out_blocks = barrier((acts, dn_part, out_blocks))
    acts_other = [cross(act) for act in acts]
    arrived, acts = send_sum(dn_part, acts)
    out_other = [out_t[1]] + [cross(block) for block in out_blocks[1:]]
    grads_two = mlp_grads(
        chips, tokens_two, cot_blocks, tokens_other, cot_other, acts, acts_other
    )
    grads_two, arrived, out_other, y_part = barrier((grads_two, arrived, out_other, y_part))
    y_blocks = list(y_part.reshape((size, -1) + y_part.shape[1:]))
    y_early = [swap(y_blocks[step], step) for step in range(1, 3)]
    sums_two = scatter(grads_two)
    middle_grad, branch, gain_two_part, do_blocks = middle_back(
        arrived, middle, cotangent, gain_two[None, :], out_blocks, out_other
    )
    do_blocks = send_blocks(do_blocks)
    gain_two_other = cross(gain_two_part[half:])
    do_blocks, branch, gain_two_other, y_blocks, y_early = barrier(
        (do_blocks, branch, gain_two_other, y_blocks, y_early)
    )
    branch_blocks = spread(branch)
    qkv_grad = attend_back(
        me_array, query, log_total, key_pad, value_pad, cosine, sine, do_blocks, group
    )
    qkv_grad, sums_one = barrier((qkv_grad, sums_one))
    qkv_other = cross(qkv_grad)
    normed_part = input_grad(qkv_grad, *attn, columns, size)
    branch_blocks, normed_part = barrier((branch_blocks, normed_part))
    branch_other = other_half(branch_blocks)
    tokens_other, attended_other = early
    grads, gain_parts = attn_grads(
        chips,
        tokens_one,
        branch_blocks,
        (qkv_grad, attended),
        (tokens_other, branch_other, qkv_other, attended_other),
        attn_own,
        columns,
        gain_one[:half, None],
        (gain_two_part[:half] + gain_two_other)[:, None],
    )
    arrived, (grads, sums_two) = send_sum(normed_part, (grads, sums_two))
    attn_sums = scatter(grads)
    gain_sums = add_up(line_parts(gain_parts[:, :, :2]))
    unpacked = unpack_shares(sums_one, sums_two)
    arrived, y_blocks, unpacked, gain_sums = barrier((arrived, y_blocks, unpacked, gain_sums))
    grad_gate, grad_up, grad_down = unpacked
    y_late = [swap(y_blocks[step], step) for step in range(3, size)]
    (grad_in,) = row_call(
        functools.partial(input_back_kernel, chips=chips),
        [jnp.float32],
        [*arrived, residual, middle_grad, gain_one[None, :]],
        core,
    )
    grad_in, gain_sums = barrier((grad_in, gain_sums))
    gain_sums = own_part(gain_sums)
    y_late, grad_in, gain_sums = barrier((y_late, grad_in, gain_sums))
    (out,) = row_call(
        functools.partial(output_kernel, chips=chips),
        [jnp.bfloat16],
        [y_blocks[0], *y_early, *y_late, middle],
        core,
    )
    out, attn_sums = barrier((out, attn_sums))
    grad_query, grad_key, grad_value, grad_out = unpack(attn_sums, q_width, kv_width)
    return (
        out,
        grad_in,
        gain_sums[:, 0],
        grad_query,
        grad_key,
        grad_value,
        grad_out,
        gain_sums[:, 1],
        grad_gate,
        grad_up,
        grad_down,
    )


def solution(mesh):
    return jax.shard_map(
        per_device,
        mesh=mesh,
        in_specs=(
            P(("dp", "tensor"), None),
            P("dp"),
            P("dp", "tensor"),
            P("dp", "tensor"),
            P("dp", "tensor"),
            P("tensor", "dp"),
            P("dp"),
            P("dp", "tensor"),
            P("dp", "tensor"),
            P("tensor", "dp"),
            P("dp"),
            P(("dp", "tensor"), None),
        ),
        out_specs=(
            P(("dp", "tensor"), None),
            P(("dp", "tensor"), None),
            P(("dp", "tensor")),
            P("dp", "tensor"),
            P("dp", "tensor"),
            P("dp", "tensor"),
            P("tensor", "dp"),
            P(("dp", "tensor")),
            P("dp", "tensor"),
            P("dp", "tensor"),
            P("tensor", "dp"),
        ),
        check_vma=False,
    )
```

```python
import functools
import math

import jax
import jax.numpy as jnp
from jax import lax
from jax.experimental import pallas as pl
from jax.experimental.pallas import tpu as pltpu
from jax.sharding import PartitionSpec as P

HEAD_DIM = 64
PAIR = 2 * HEAD_DIM
SEQ_LEN = 1024


EPS = 1e-05
ROPE_BASE = 500000.0
SCALE = 1.0 / math.sqrt(HEAD_DIM)
PARAMS = pltpu.CompilerParams(vmem_limit_bytes=58 * 2**20)
ONCE = pl.Buffered(1)

barrier = lax.optimization_barrier


def hint(flops):
    return pl.CostEstimate(flops=flops, bytes_accessed=0, transcendentals=0)


def rms_scale(values):
    return lax.rsqrt(jnp.mean(values * values, axis=-1, keepdims=True) + EPS)


def norm_back(grad, values, scale, gain):
    inner = grad * gain
    cubed = scale * scale * scale
    result = scale * inner - values * cubed * jnp.mean(inner * values, axis=-1, keepdims=True)
    return (result, jnp.sum(grad * values * scale, axis=0))


def mm(left, right):
    return jnp.dot(left, right, preferred_element_type=jnp.float32)


def mm_nt(left, right):
    return lax.dot_general(left, right, (((1,), (1,)), ((), ())), preferred_element_type=jnp.float32)


def mm_tn(left, right):
    return lax.dot_general(left, right, (((0,), (0,)), ((), ())), preferred_element_type=jnp.float32)


def lane_index(rows):
    return lax.broadcasted_iota(jnp.int32, (rows, PAIR), 1)


def turn(pair, cosine, sine):
    lower = lane_index(pair.shape[0]) % HEAD_DIM < HEAD_DIM // 2
    other = jnp.where(
        lower, pltpu.roll(pair, PAIR - HEAD_DIM // 2, 1), pltpu.roll(pair, HEAD_DIM // 2, 1)
    )
    return pair * cosine + other * sine


def project_kernel(place_ref, *refs, size, q_width, kv_width):
    x_refs = refs[:size]
    gain_ref, qo_ref, qx_ref, kvo_ref, kvx_ref, cos_ref, sin_ref = refs[size:-4]
    n_ref, q_ref, k_ref, v_ref = refs[-4:]
    rows = q_ref.shape[0]
    half = qo_ref.shape[0]

    def one(x_ref):
        x = x_ref[...].astype(jnp.float32)
        normed = (x * rms_scale(x) * gain_ref[...]).astype(jnp.bfloat16)
        n_ref[...] = normed
        cosine, sine = cos_ref[...], sin_ref[...]
        own, other = normed[:, :half], normed[:, half:]
        lin = mm(own, qo_ref[...]) + mm(other, qx_ref[...])
        for low in range(0, q_width, PAIR):
            query = turn(lin[:, low : low + PAIR], cosine, sine).astype(jnp.bfloat16)
            q_ref[:, low : low + PAIR] = query * jnp.bfloat16(SCALE)
        lin = mm(own, kvo_ref[...]) + mm(other, kvx_ref[...])
        first = lane_index(rows) < HEAD_DIM
        for ref, start, rotate in ((k_ref, 0, True), (v_ref, kv_width, False)):
            for head in range(kv_width // HEAD_DIM):
                low = start + head * HEAD_DIM
                block = lin[:, low // PAIR * PAIR : low // PAIR * PAIR + PAIR]
                if rotate:
                    block = turn(block, cosine, sine)
                moved = pltpu.roll(block, HEAD_DIM, 1)
                if low % PAIR:
                    block, moved = moved, block
                ref[head, 0] = jnp.where(first, block, 0.0).astype(jnp.bfloat16)
                ref[head, 1] = jnp.where(first, 0.0, moved).astype(jnp.bfloat16)

    for step in range(size):
        pl.when(pl.program_id(0) == step)(functools.partial(one, x_refs[step]))


class Columns:
    def __init__(self, q_width, kv_width):
        self.q_width, self.kv_width = q_width, kv_width

    def spec(self, part, rows, place=lambda *_: 0):
        width, start = {
            "q": (self.q_width, 0),
            "out": (self.q_width, self.q_width),
            "kv": (2 * self.kv_width, 2 * self.q_width),
        }[part]
        index = start // width
        mode = {"pipeline_mode": ONCE} if place() == 0 else {}
        return pl.BlockSpec((rows, width), lambda *grid: (place(*grid), index), **mode)


def project(me, blocks, gain, own, other, cosine, sine, columns):
    size = len(blocks)
    rows, features = blocks[0].shape
    total = rows * size
    q_width, kv_width = columns.q_width, columns.kv_width
    key_heads = kv_width // HEAD_DIM
    width = q_width + 2 * kv_width
    half = features // 2
    fixed = lambda p, m: (0, 0)
    placed = lambda p, m: (jnp.bitwise_xor(p, m[0]), 0)
    padded = pl.BlockSpec(
        (key_heads, 2, rows, PAIR), lambda p, m: (0, 0, jnp.bitwise_xor(p, m[0]), 0)
    )
    spec = pltpu.PrefetchScalarGridSpec(
        num_scalar_prefetch=1,
        grid=(size,),
        in_specs=[pl.BlockSpec((rows, features), fixed, pipeline_mode=ONCE)] * size
        + [
            pl.BlockSpec((1, features), fixed),
            columns.spec("q", half),
            columns.spec("q", half),
            columns.spec("kv", half),
            columns.spec("kv", half),
            pl.BlockSpec((rows, PAIR), placed),
            pl.BlockSpec((rows, PAIR), placed),
        ],
        out_specs=[
            pl.BlockSpec((rows, features), lambda p, m: (p, 0)),
            pl.BlockSpec((rows, q_width), lambda p, m: (p, 0)),
            padded,
            padded,
        ],
    )
    padded_shape = jax.ShapeDtypeStruct((key_heads, 2, total, PAIR), jnp.bfloat16)
    return pl.pallas_call(
        functools.partial(project_kernel, size=size, q_width=q_width, kv_width=kv_width),
        grid_spec=spec,
        out_shape=[
            jax.ShapeDtypeStruct((total, features), jnp.bfloat16),
            jax.ShapeDtypeStruct((total, q_width), jnp.bfloat16),
            padded_shape,
            padded_shape,
        ],
        compiler_params=PARAMS,
        cost_estimate=hint(2 * total * features * width // 16),
    )(me, *blocks, gain, own, other, own, other, cosine, sine)


def attend_kernel(
    me_ref, q_ref, k_ref, v_ref, wo_ref, wx_ref, o_ref, l_ref, *refs, size, heads, group
):
    part_refs, vt_ref = refs[:size], refs[size]
    rows = q_ref.shape[0]
    half = wo_ref.shape[0]
    mine = jnp.bitwise_xor(me_ref[0], pl.program_id(0))
    key_place = lax.broadcasted_iota(jnp.int32, (rows, rows), 0)
    query_place = lax.broadcasted_iota(jnp.int32, (rows, rows), 1)

    @pl.when(pl.program_id(0) == 0)
    def _():
        for head in range(heads // group):
            for side in range(2):
                vt_ref[head, side] = v_ref[head, side].T

    def one(span):
        keys = span * rows
        for pair in range(heads // 2):
            head = 2 * pair // group
            lanes = slice(pair * PAIR, (pair + 1) * PAIR)
            query = q_ref[:, lanes]
            acc = None
            inverse = []
            for side in range(2):
                diag = mm_nt(k_ref[head, side, keys : keys + rows, :], query)
                diag = jnp.where(key_place <= query_place, diag, -1e9)
                top = jnp.max(diag, axis=0, keepdims=True)
                if span:
                    body = mm_nt(k_ref[head, side, :keys, :], query)
                    top = jnp.maximum(top, jnp.max(body, axis=0, keepdims=True))
                diag = jnp.exp(diag - top)
                total = jnp.sum(diag, axis=0, keepdims=True)
                part = mm(vt_ref[head, side, :, keys : keys + rows], diag.astype(jnp.bfloat16))
                if span:
                    body = jnp.exp(body - top)
                    total = total + jnp.sum(body, axis=0, keepdims=True)
                    part = part + mm(vt_ref[head, side, :, :keys], body.astype(jnp.bfloat16))
                acc = part if acc is None else acc + part
                inverse.append(jnp.broadcast_to(1.0 / total, (HEAD_DIM, rows)))
                l_ref[2 * pair + side : 2 * pair + side + 1, :] = top + jnp.log(total)
            acc = acc * jnp.concatenate(inverse, axis=0)
            o_ref[:, lanes] = acc.T.astype(jnp.bfloat16)

    for span in range(size):
        pl.when(mine == span)(functools.partial(one, span))

    def project_out(ref):
        ref[:, :half] = mm_nt(o_ref[...], wo_ref[...]).astype(jnp.bfloat16)
        ref[:, half:] = mm_nt(o_ref[...], wx_ref[...]).astype(jnp.bfloat16)

    for step in range(size):
        pl.when(pl.program_id(0) == step)(functools.partial(project_out, part_refs[step]))


def attend(me, query, key_pad, value_pad, own, other, columns, size, group):
    total, width = query.shape
    features = 2 * own.shape[0]
    rows, heads = total // size, width // HEAD_DIM
    whole = pl.BlockSpec(key_pad.shape, lambda p, m: (0, 0, 0, 0), pipeline_mode=ONCE)
    spec = pltpu.PrefetchScalarGridSpec(
        num_scalar_prefetch=1,
        grid=(size,),
        in_specs=[pl.BlockSpec((rows, width), lambda p, m: (p, 0)), whole, whole]
        + [columns.spec("out", features // 2)] * 2,
        out_specs=[
            pl.BlockSpec((rows, width), lambda p, m: (p, 0)),
            pl.BlockSpec((heads, rows), lambda p, m: (0, p)),
        ]
        + [pl.BlockSpec((rows, features), lambda p, m: (0, 0))] * size,
        scratch_shapes=[pltpu.VMEM((heads // group, 2, PAIR, total), jnp.bfloat16)],
    )
    return pl.pallas_call(
        functools.partial(attend_kernel, size=size, heads=heads, group=group),
        grid_spec=spec,
        out_shape=[
            jax.ShapeDtypeStruct((total, width), jnp.bfloat16),
            jax.ShapeDtypeStruct((heads, total), jnp.float32),
        ]
        + [jax.ShapeDtypeStruct((rows, features), jnp.bfloat16)] * size,
        compiler_params=PARAMS,
        cost_estimate=hint(8 * heads * total * total * HEAD_DIM // 16),
    )(me, query, key_pad, value_pad, own, other)


def attend_back_kernel(
    me_ref, q_ref, l_ref, k_ref, v_ref, cos_ref, sin_ref, *refs, size, heads, group
):
    do_refs = refs[:size]
    out_ref, dk_ref, dv_ref, kt_ref, do_ref = refs[size:]
    rows = q_ref.shape[0]
    key_heads = heads // group
    step = pl.program_id(0)
    me = me_ref[0]
    mine = jnp.bitwise_xor(me, step)
    key_place = lax.broadcasted_iota(jnp.int32, (rows, rows), 0)
    query_place = lax.broadcasted_iota(jnp.int32, (rows, rows), 1)

    def rows_of(block):
        return pl.ds(pl.multiple_of(block * rows, rows), rows)

    @pl.when(step == 0)
    def _():
        dk_ref[...] = jnp.zeros_like(dk_ref)
        dv_ref[...] = jnp.zeros_like(dv_ref)
        for head in range(key_heads):
            for side in range(2):
                kt_ref[head, side] = k_ref[head, side].T

    def fetch(ref):
        do_ref[...] = ref[...]

    for block in range(size):
        pl.when(step == block)(functools.partial(fetch, do_refs[block]))

    def one(span):
        keys = span * rows
        parts = [(keys, keys + rows, True)] + ([(0, keys, False)] if span else [])
        cosine, sine = cos_ref[keys : keys + rows, :], sin_ref[keys : keys + rows, :]
        for pair in range(heads // 2):
            head = 2 * pair // group
            lanes = slice(pair * PAIR, (pair + 1) * PAIR)
            query, grad = q_ref[:, lanes], do_ref[:, lanes]
            acc = None
            for side in range(2):
                log_total = l_ref[2 * pair + side : 2 * pair + side + 1, :]
                inner = None
                kept = []
                for low, high, diagonal in parts:
                    probs = mm_nt(k_ref[head, side, low:high, :], query)
                    probs = jnp.exp(probs - log_total)
                    if diagonal:
                        probs = jnp.where(key_place <= query_place, probs, 0.0)
                    prob_grad = mm_nt(v_ref[head, side, low:high, :], grad)
                    dv_ref[head, side, low:high, :] += mm(probs.astype(jnp.bfloat16), grad)
                    term = jnp.sum(probs * prob_grad, axis=0, keepdims=True)
                    inner = term if inner is None else inner + term
                    kept.append((low, high, probs, prob_grad))
                for low, high, probs, prob_grad in kept:
                    score_grad = (probs * (prob_grad - inner)).astype(jnp.bfloat16)
                    dk_ref[head, side, low:high, :] += mm(score_grad, query)
                    part = mm(kt_ref[head, side, :, low:high], score_grad)
                    acc = part if acc is None else acc + part
            turned = turn(acc.T * SCALE, cosine, -sine)
            out_ref[rows_of(step), lanes] = turned.astype(jnp.bfloat16)

    for span in range(size):
        pl.when(mine == span)(functools.partial(one, span))

    @pl.when(step == size - 1)
    def _():
        first = lane_index(rows) < HEAD_DIM
        wanted = [(dk_ref, head, True) for head in range(key_heads)]
        wanted += [(dv_ref, head, False) for head in range(key_heads)]
        for span in range(size):
            place = slice(span * rows, (span + 1) * rows)
            cosine, sine = cos_ref[place, :], sin_ref[place, :]
            for block in range(len(wanted) // 2):
                halves, rotate = [], []
                for half in range(2):
                    ref, head, is_key = wanted[2 * block + half]
                    low, high = ref[head, 0, place, :], ref[head, 1, place, :]
                    if half:
                        halves.append(pltpu.roll(low, HEAD_DIM, 1) + high)
                    else:
                        halves.append(low + pltpu.roll(high, HEAD_DIM, 1))
                    rotate.append(is_key)
                value = jnp.where(first, halves[0], halves[1])
                if rotate[0] and rotate[1]:
                    value = turn(value, cosine, -sine)
                elif rotate[0]:
                    value = jnp.where(first, turn(value, cosine, -sine), value)
                start = heads * HEAD_DIM + block * PAIR
                target = rows_of(jnp.bitwise_xor(me, span))
                out_ref[target, start : start + PAIR] = value.astype(jnp.bfloat16)


def attend_back(
    me, query, log_total, key_pad, value_pad, cosine, sine, attended_grad, group
):
    total, width = query.shape
    size = len(attended_grad)
    rows, heads = total // size, width // HEAD_DIM
    key_heads = heads // group
    out_width = width + 2 * key_heads * HEAD_DIM
    whole = pl.BlockSpec(key_pad.shape, lambda p, m: (0, 0, 0, 0), pipeline_mode=ONCE)
    table = pl.BlockSpec((total, PAIR), lambda p, m: (0, 0), pipeline_mode=ONCE)
    spec = pltpu.PrefetchScalarGridSpec(
        num_scalar_prefetch=1,
        grid=(size,),
        in_specs=[
            pl.BlockSpec((rows, width), lambda p, m: (p, 0)),
            pl.BlockSpec((heads, rows), lambda p, m: (0, p)),
            whole,
            whole,
            table,
            table,
        ]
        + [pl.BlockSpec((rows, width), lambda p, m: (0, 0), pipeline_mode=ONCE)] * size,
        out_specs=pl.BlockSpec((total, out_width), lambda p, m: (0, 0)),
        scratch_shapes=[
            pltpu.VMEM(key_pad.shape, jnp.float32),
            pltpu.VMEM(key_pad.shape, jnp.float32),
            pltpu.VMEM((key_heads, 2, PAIR, total), jnp.bfloat16),
            pltpu.VMEM((rows, width), jnp.bfloat16),
        ],
    )
    return pl.pallas_call(
        functools.partial(attend_back_kernel, size=size, heads=heads, group=group),
        grid_spec=spec,
        out_shape=jax.ShapeDtypeStruct((total, out_width), jnp.bfloat16),
        compiler_params=PARAMS,
        cost_estimate=hint(20 * heads * total * total * HEAD_DIM),
    )(me, query, log_total, key_pad, value_pad, cosine, sine, *attended_grad)


def grouped(arrays, counts):
    arrays = iter(arrays)
    return [[next(arrays) for _ in range(count)] for count in counts]


def mlp_kernel(*refs, n_counts, e_counts, adds):
    size = len(n_counts)
    pieces = sum(n_counts) + sum(e_counts)
    n_refs = grouped(refs, n_counts)
    e_refs = grouped(refs[sum(n_counts) :], e_counts)
    gate_o, up_o, down_o, gate_x, up_x, down_x = refs[pieces : pieces + 6]
    y_ref, n_ref, e_ref = refs[-3:]
    dn_refs = refs[-3 - size if adds else -4 : -3]
    dg_ref, du_ref, h_ref = refs[-6 - size if adds else -7 :][:3]
    half = gate_o.shape[0]

    def fetch(step):
        for target, sources in ((n_ref, n_refs[step]), (e_ref, e_refs[step])):
            low = 0
            for source in sources:
                high = low + source.shape[0]
                target[low:high] = source[...]
                low = high

    for step in range(size):
        pl.when(pl.program_id(0) == step)(functools.partial(fetch, step))
    gate = mm(n_ref[:, :half], gate_o[...]) + mm(n_ref[:, half:], gate_x[...])
    up = mm(n_ref[:, :half], up_o[...]) + mm(n_ref[:, half:], up_x[...])
    grad = mm(e_ref[:, :half], down_o[...]) + mm(e_ref[:, half:], down_x[...])
    sigma = jax.nn.sigmoid(gate)
    silu = gate * sigma
    hidden = (silu * up).astype(jnp.bfloat16)
    gate_grad = (grad * up * sigma * (1.0 + gate * (1.0 - sigma))).astype(jnp.bfloat16)
    up_grad = (grad * silu).astype(jnp.bfloat16)
    dg_ref[...] = gate_grad
    du_ref[...] = up_grad
    h_ref[...] = hidden
    for part, gate_w, up_w, down_w in ((0, gate_o, up_o, down_o), (1, gate_x, up_x, down_x)):
        lanes = slice(part * half, (part + 1) * half)
        dn = mm_nt(gate_grad, gate_w[...]) + mm_nt(up_grad, up_w[...])
        y = mm_nt(hidden, down_w[...])
        if adds:
            dn = dn + refs[pieces + 6][:, lanes].astype(jnp.float32)
            y = y + refs[pieces + 7][:, lanes].astype(jnp.float32)
        y_ref[:, lanes] = y.astype(jnp.bfloat16)
        dn = dn.astype(jnp.bfloat16)

        def store(ref):
            ref[:, lanes] = dn

        if adds:
            for step in range(size):
                pl.when(pl.program_id(0) == step)(functools.partial(store, dn_refs[step]))
        else:
            store(dn_refs[0])


def mlp(tokens, cot, own, other, earlier):
    size = len(tokens)
    rows, features = tokens[0][0].shape
    half, units = own.shape[0], own.shape[1] // 3
    total = rows * size
    fixed = lambda p: (0, 0)
    moving = lambda p: (p, 0)
    wide = pl.BlockSpec((rows, features), moving)
    sums = jax.ShapeDtypeStruct((total, features), jnp.bfloat16)
    dn_specs, dn_shapes = [wide], [sums]
    if earlier:
        dn_specs = [pl.BlockSpec((rows, features), fixed)] * size
        dn_shapes = [jax.ShapeDtypeStruct((rows, features), jnp.bfloat16)] * size
    pieces = sum(tokens, []) + sum(cot, [])
    thirds = [
        pl.BlockSpec((half, units), lambda p, t=t: (0, t), pipeline_mode=ONCE) for t in range(3)
    ]
    return pl.pallas_call(
        functools.partial(
            mlp_kernel,
            n_counts=[len(group) for group in tokens],
            e_counts=[len(group) for group in cot],
            adds=bool(earlier),
        ),
        grid=(size,),
        in_specs=[pl.BlockSpec(piece.shape, fixed, pipeline_mode=ONCE) for piece in pieces]
        + thirds * 2
        + [wide] * len(earlier),
        out_specs=[pl.BlockSpec((rows, units), moving)] * 3 + dn_specs + [wide],
        out_shape=[jax.ShapeDtypeStruct((total, units), jnp.bfloat16)] * 3 + dn_shapes + [sums],
        scratch_shapes=[pltpu.VMEM((rows, features), jnp.bfloat16)] * 2,
        compiler_params=PARAMS,
        cost_estimate=hint(12 * total * features * units),
    )(*pieces, own, own, own, other, other, other, *earlier)


def add_refs(refs):
    total = refs[0][...].astype(jnp.float32)
    for ref in refs[1:]:
        total = total + ref[...].astype(jnp.float32)
    return total


def store_by_device(out_ref, values, core, chips):
    width = values.shape[1] // (2 * chips)
    for place, chip in enumerate(ring_order(chips)):
        own = values[:, place * width : (place + 1) * width]
        other = values[:, (chips + place) * width : (chips + place + 1) * width]
        low = 2 * chip * width
        out_ref[:, low : low + width] = jnp.where(core == 0, own, other)
        out_ref[:, low + width : low + 2 * width] = jnp.where(core == 0, other, own)


def middle_kernel(*refs):
    x_ref, gain_ref, middle_ref, normed_ref = refs[-4:]
    values = x_ref[...].astype(jnp.float32) + add_refs(refs[:-4])
    middle_ref[...] = values
    normed_ref[...] = (values * rms_scale(values) * gain_ref[...]).astype(jnp.bfloat16)


def input_back_kernel(core_ref, *refs, chips):
    x_ref, before_ref, gain_ref, out_ref = refs[-4:]
    values = x_ref[...].astype(jnp.float32)
    inner = add_refs(refs[:-4]) * gain_ref[...]
    scale = rms_scale(values)
    mean = jnp.mean(inner * values, axis=-1, keepdims=True)
    result = before_ref[...] + scale * inner - values * (scale * scale * scale) * mean
    store_by_device(out_ref, result, core_ref[0], chips)


def output_kernel(core_ref, *refs, chips):
    middle_ref, out_ref = refs[-2:]
    values = middle_ref[...] + add_refs(refs[:-2])
    store_by_device(out_ref, values.astype(jnp.bfloat16), core_ref[0], chips)


def row_call(body, dtypes, arrays, core=None):
    rows, features = arrays[0].shape
    steps = 2
    wide = pl.BlockSpec((rows // steps, features), lambda i, *_: (i, 0))
    row = pl.BlockSpec((1, features), lambda i, *_: (0, 0))
    scalars = [] if core is None else [jnp.full((1,), core, jnp.int32)]
    return pl.pallas_call(
        body,
        grid_spec=pltpu.PrefetchScalarGridSpec(
            num_scalar_prefetch=len(scalars),
            grid=(steps,),
            in_specs=[row if array.shape[0] == 1 else wide for array in arrays],
            out_specs=[wide] * len(dtypes),
        ),
        out_shape=[jax.ShapeDtypeStruct((rows, features), dtype) for dtype in dtypes],
        compiler_params=PARAMS,
        cost_estimate=hint(0),
    )(*scalars, *arrays)


def unpack_kernel(sum_ref, q_ref, k_ref, v_ref, out_ref):
    q_width, kv_width = q_ref.shape[1], k_ref.shape[1]
    values = sum_ref[...].astype(jnp.float32)
    q_ref[...] = values[:, :q_width]
    kv = values[:, q_width : q_width + 2 * kv_width]
    k_ref[...] = kv[:, :kv_width]
    v_ref[...] = kv[:, kv_width:]
    out_ref[...] = values[:, q_width + 2 * kv_width :].T


def unpack(sums, q_width, kv_width):
    rows = sums.shape[0]
    widths = [(rows, q_width), (rows, kv_width), (rows, kv_width), (q_width, rows)]
    return pl.pallas_call(
        unpack_kernel,
        out_shape=[jax.ShapeDtypeStruct(shape, jnp.float32) for shape in widths],
        compiler_params=PARAMS,
        cost_estimate=hint(0),
    )(sums)


def unpack_shares_kernel(one_ref, two_ref, gate_ref, up_ref, down_ref):
    units = one_ref.shape[1] // 3
    for part, ref in enumerate((one_ref, two_ref)):
        cut = slice(part * units, (part + 1) * units)
        gate_ref[:, cut] = ref[:, :units].astype(jnp.float32)
        up_ref[:, cut] = ref[:, units : 2 * units].astype(jnp.float32)
        down_ref[cut, :] = ref[:, 2 * units :].astype(jnp.float32).T


def unpack_shares(one, two):
    rows, width = one.shape
    units = 2 * width // 3
    shapes = [(rows, units), (rows, units), (units, rows)]
    return pl.pallas_call(
        unpack_shares_kernel,
        out_shape=[jax.ShapeDtypeStruct(shape, jnp.float32) for shape in shapes],
        compiler_params=PARAMS,
        cost_estimate=hint(0),
    )(one, two)


def middle_back_kernel(*refs, parts, size):
    n_refs, refs = refs[:parts], refs[parts:]
    x_ref, e_ref, gain_ref, refs = refs[0], refs[1], refs[2], refs[3:]
    own_refs, other_refs, refs = refs[:size], refs[size : 2 * size], refs[2 * size :]
    grad_ref, branch_ref, part_ref, do_refs = refs[0], refs[1], refs[2], refs[3:]
    half = own_refs[0].shape[0]
    grad = add_refs(n_refs)
    values = x_ref[...]
    scale = rms_scale(values)
    result, part = norm_back(grad, values, scale, gain_ref[...])

    @pl.when(pl.program_id(0) == 0)
    def _():
        part_ref[...] = jnp.zeros_like(part_ref)

    part_ref[...] += part[None, :]
    result = result + e_ref[...].astype(jnp.float32)
    grad_ref[...] = result
    branch = result.astype(jnp.bfloat16)
    branch_ref[...] = branch
    for own, other, do_ref in zip(own_refs, other_refs, do_refs):
        do = mm(branch[:, :half], own[...]) + mm(branch[:, half:], other[...])
        do_ref[...] = do.astype(jnp.bfloat16)


def middle_back(arrived, middle, cot, gain, own, other):
    parts, size = len(arrived), len(own)
    rows, features = middle.shape
    width = own[0].shape[1]
    steps = 2
    wide = pl.BlockSpec((rows // steps, features), lambda i: (i, 0))
    narrow = pl.BlockSpec((rows // steps, width), lambda i: (i, 0))
    row = pl.BlockSpec((1, features), lambda i: (0, 0))
    weight = pl.BlockSpec((features // 2, width), lambda i: (0, 0), pipeline_mode=ONCE)
    grad, branch, part, *do = pl.pallas_call(
        functools.partial(middle_back_kernel, parts=parts, size=size),
        grid=(steps,),
        in_specs=[wide] * parts + [wide, wide, row] + [weight] * (2 * size),
        out_specs=[wide, wide, row] + [narrow] * size,
        out_shape=[
            jax.ShapeDtypeStruct((rows, features), jnp.float32),
            jax.ShapeDtypeStruct((rows, features), jnp.bfloat16),
            jax.ShapeDtypeStruct((1, features), jnp.float32),
        ]
        + [jax.ShapeDtypeStruct((rows, width), jnp.bfloat16)] * size,
        compiler_params=PARAMS,
        cost_estimate=hint(2 * rows * features * width * size),
    )(*arrived, middle, cot, gain, *own, *other)
    return grad, branch, part[0], do


def column_grad(blocks, other, mine, theirs):
    total = mm_tn(other[...], theirs[...])
    low = 0
    for block in blocks:
        high = low + block.shape[0]
        total = total + mm_tn(block[...], mine[low:high, :])
        low = high
    return total


def grad_kernel(*refs, n_count, e_count):
    n_refs, refs = refs[:n_count], refs[n_count:]
    e_refs, refs = refs[:e_count], refs[e_count:]
    n_other, e_other = refs[:2]
    acts, out_ref = refs[2:-1], refs[-1]
    units = acts[0].shape[1]
    for third in range(3):
        blocks, other = (e_refs, e_other) if third == 2 else (n_refs, n_other)
        grad = column_grad(blocks, other, acts[third], acts[third + 3])
        out_ref[0, :, third * units : (third + 1) * units] = grad.astype(jnp.bfloat16)


def mlp_grads(chips, tokens, cot, tokens_other, cot_other, mine, theirs):
    tokens, cot = sum(tokens, []), sum(cot, [])
    features = tokens[0].shape[1]
    total, units = mine[0].shape
    depth = features // (2 * chips)
    long = pl.BlockSpec((total, depth), lambda b: (0, b))
    fixed = pl.BlockSpec((total, units), lambda b: (0, 0), pipeline_mode=ONCE)
    return pl.pallas_call(
        functools.partial(grad_kernel, n_count=len(tokens), e_count=len(cot)),
        grid=(chips,),
        in_specs=[pl.BlockSpec((p.shape[0], depth), lambda b: (0, b)) for p in tokens + cot]
        + [long, long]
        + [fixed] * 6,
        out_specs=pl.BlockSpec((1, depth, 3 * units), lambda b: (b, 0, 0)),
        out_shape=jax.ShapeDtypeStruct((chips, depth, 3 * units), jnp.bfloat16),
        compiler_params=PARAMS,
        cost_estimate=hint(6 * total * features * units),
    )(*tokens, *cot, tokens_other, cot_other, *mine, *theirs)


def attn_grad_kernel(*refs, size):
    e_refs = refs[2 : 2 + size]
    n_ref, n_other = refs[:2]
    e_other, d_ref, d_other, o_ref, o_other, q_ref, kv_ref, g1_ref, g2_ref = refs[2 + size : -2]
    out_ref, gain_ref = refs[-2:]
    width, out_width = d_ref.shape[1], o_ref.shape[1]
    grad = column_grad([n_ref], n_other, d_ref, d_other)
    out_ref[0, :, :width] = grad.astype(jnp.bfloat16)
    out_grad = column_grad(e_refs, e_other, o_ref, o_other)
    out_ref[0, :, width : width + out_width] = out_grad.astype(jnp.bfloat16)
    cut = q_ref.shape[1]
    first = jnp.sum(grad[:, :cut] * q_ref[...].astype(jnp.float32), axis=1, keepdims=True)
    first += jnp.sum(grad[:, cut:] * kv_ref[...].astype(jnp.float32), axis=1, keepdims=True)
    first = first / g1_ref[...]
    lane = lane_index(grad.shape[0])
    gain_ref[0] = jnp.where(lane == 0, first, g2_ref[...])


def attn_grads(
    chips, tokens, branch, mine, theirs, weights, columns, gain_one, gain_two_part
):
    size = len(branch)
    qkv_grad, attended = mine
    tokens_other, branch_other, qkv_other, attended_other = theirs
    total, features = tokens.shape
    rows = total // size
    width, out_width = qkv_grad.shape[1], attended.shape[1]
    depth = features // (2 * chips)
    column = lambda b: (0, b)
    row = lambda b: (b, 0)
    long = pl.BlockSpec((total, depth), column)
    fixed = lambda array: pl.BlockSpec(array.shape, lambda b: (0, 0), pipeline_mode=ONCE)
    place = lambda b: (b, 0, 0)
    return pl.pallas_call(
        functools.partial(attn_grad_kernel, size=size),
        grid=(chips,),
        in_specs=[long, long]
        + [pl.BlockSpec((rows, depth), column)] * size
        + [long]
        + [fixed(qkv_grad)] * 2
        + [fixed(attended)] * 2
        + [
            columns.spec("q", depth, lambda b=None: b),
            columns.spec("kv", depth, lambda b=None: b),
            pl.BlockSpec((depth, 1), row),
            pl.BlockSpec((depth, 1), row),
        ],
        out_specs=[
            pl.BlockSpec((1, depth, width + out_width), place),
            pl.BlockSpec((1, depth, PAIR), place),
        ],
        out_shape=[
            jax.ShapeDtypeStruct((chips, depth, width + out_width), jnp.bfloat16),
            jax.ShapeDtypeStruct((chips, depth, PAIR), jnp.float32),
        ],
        compiler_params=PARAMS,
        cost_estimate=hint(2 * total * features * (width + out_width)),
    )(
        tokens,
        tokens_other,
        *branch,
        branch_other,
        qkv_grad,
        qkv_other,
        attended,
        attended_other,
        weights,
        weights,
        gain_one,
        gain_two_part,
    )


def input_grad_kernel(d_ref, qo_ref, qx_ref, kvo_ref, kvx_ref, *out_refs):
    half, cut = qo_ref.shape

    def one(ref):
        query, rest = d_ref[:, :cut], d_ref[:, cut:]
        own = mm_nt(query, qo_ref[...]) + mm_nt(rest, kvo_ref[...])
        other = mm_nt(query, qx_ref[...]) + mm_nt(rest, kvx_ref[...])
        ref[:, :half] = own.astype(jnp.bfloat16)
        ref[:, half:] = other.astype(jnp.bfloat16)

    for step, ref in enumerate(out_refs):
        pl.when(pl.program_id(0) == step)(functools.partial(one, ref))


def input_grad(qkv_grad, own, other, columns, size):
    total, width = qkv_grad.shape
    features = 2 * own.shape[0]
    rows = total // size
    fixed = lambda i: (0, 0)
    weights = [columns.spec(part, own.shape[0]) for part in ("q", "q", "kv", "kv")]
    return pl.pallas_call(
        input_grad_kernel,
        grid=(size,),
        in_specs=[pl.BlockSpec((rows, width), lambda i: (i, 0))] + weights,
        out_specs=[pl.BlockSpec((rows, features), fixed)] * size,
        out_shape=[jax.ShapeDtypeStruct((rows, features), jnp.bfloat16)] * size,
        compiler_params=PARAMS,
        cost_estimate=hint(2 * total * features * width),
    )(qkv_grad, own, other, own, other)


def swap(values, step):
    size = lax.axis_size("tensor")
    return lax.ppermute(values, "tensor", [(i, i ^ step) for i in range(size)])


def spread(values):
    return [values] + [swap(values, step) for step in range(1, lax.axis_size("tensor"))]


def send_blocks(blocks):
    return [blocks[0]] + [swap(block, step + 1) for step, block in enumerate(blocks[1:])]


def spread_around(values, held):
    if lax.axis_size("tensor") != 4:
        blocks = spread(values)
        first, held = barrier((blocks[1], held))
        return [[blocks[0]], [first]] + [[block] for block in blocks[2:]], held
    half = values.shape[0] // 2
    top, bottom = values[:half], values[half:]
    x_bottom, y_top = swap(bottom, 1), swap(top, 2)
    x_bottom, y_top, top, bottom, held = barrier((x_bottom, y_top, top, bottom, held))
    far = [swap(y_top, 1), swap(x_bottom, 2)]
    x_top, y_bottom = swap(top, 1), swap(bottom, 2)
    return [[values], [x_top, x_bottom], [y_top, y_bottom], far], held


def merge_kernel(x_ref, y_ref, top_ref, bottom_ref, x_out, y_out):
    half = top_ref.shape[0]
    x_out[:half] = x_ref[:half]
    x_out[half:] = add_refs([x_ref.at[half:], bottom_ref]).astype(jnp.bfloat16)
    y_out[:half] = add_refs([y_ref.at[:half], top_ref]).astype(jnp.bfloat16)
    y_out[half:] = y_ref[half:]


def send_sum(blocks, held=()):
    if len(blocks) != 4:
        return send_blocks(blocks), held
    own, near_x, near_y, far = blocks
    half = far.shape[0] // 2
    top, bottom = swap(far[:half], 1), swap(far[half:], 2)
    near_x, near_y = pl.pallas_call(
        merge_kernel,
        out_shape=[jax.ShapeDtypeStruct(near_x.shape, near_x.dtype)] * 2,
        compiler_params=PARAMS,
        cost_estimate=hint(0),
    )(near_x, near_y, top, bottom)
    near_x, near_y, held = barrier((near_x, near_y, held))
    return [own, swap(near_x, 1), swap(near_y, 2)], held


def add_up(blocks):
    total = blocks[0].astype(jnp.float32)
    for block in blocks[1:]:
        total = total + block.astype(jnp.float32)
    return total


def cross(values):
    count = lax.axis_size("dp")
    return lax.ppermute(values, "dp", [(i, i ^ 1) for i in range(count)])


def tables(positions):
    freqs = ROPE_BASE ** (-jnp.arange(0, HEAD_DIM, 2).astype(jnp.float32) / HEAD_DIM)
    angles = positions.astype(jnp.float32)[:, None] * freqs[None, :]
    cosine, sine = jnp.cos(angles), jnp.sin(angles)
    return (
        jnp.concatenate([cosine] * 4, axis=1),
        jnp.concatenate([-sine, sine, -sine, sine], axis=1),
    )


def ring_order(chips):
    return list(range(0, chips, 2)) + list(range(1, chips, 2))[::-1]


def chip_lines():
    chips = lax.axis_size("dp") // 2
    return [[2 * chip + core for chip in ring_order(chips)] for core in range(2)]


def gather(values):
    return lax.all_gather(values, "dp", axis=0, tiled=True, axis_index_groups=chip_lines())


def scatter(values):
    total = lax.psum_scatter(
        values, "dp", scatter_dimension=0, tiled=True, axis_index_groups=chip_lines()
    )
    return total[0]


def along(values, step):
    count = lax.axis_size("dp")
    return lax.ppermute(values, "dp", [(i, (i + 2 * step) % count) for i in range(count)])


def line_parts(parts):
    chips = lax.axis_size("dp") // 2
    chip = lax.axis_index("dp") // 2
    order = ring_order(chips)
    places = jnp.array([order.index(c % chips) for c in range(2 * chips)], jnp.int32)
    blocks = []
    for step in range(chips):
        sent = lax.dynamic_index_in_dim(parts, places[chip + step], 0, keepdims=False)
        blocks.append(along(sent, step) if step else sent)
    return blocks


def own_part(values):
    size = lax.axis_size("tensor")
    me = lax.axis_index("tensor")
    blocks = values.reshape((size, -1) + values.shape[1:])
    own = lax.dynamic_index_in_dim(blocks, me, 0, keepdims=False)
    for step in range(1, size):
        sent = lax.dynamic_index_in_dim(blocks, me ^ step, 0, keepdims=False)
        own = own + swap(sent, step)
    return own


def stack_kernel(*refs):
    low = 0
    for ref in refs[:-1]:
        high = low + ref.shape[0]
        refs[-1][low:high, :] = ref[...]
        low = high


def other_half(blocks):
    features = blocks[0].shape[1]
    shape = (sum(block.shape[0] for block in blocks), features // 2)
    halves = pl.pallas_call(
        stack_kernel,
        grid=(1,),
        in_specs=[pl.BlockSpec((b.shape[0], features // 2), lambda i: (0, 1)) for b in blocks],
        out_specs=pl.BlockSpec(shape, lambda i: (0, 0)),
        out_shape=jax.ShapeDtypeStruct(shape, blocks[0].dtype),
        compiler_params=PARAMS,
        cost_estimate=hint(0),
    )(*blocks)
    return cross(halves)


def feature_blocks(values):
    width = values.shape[-1] // lax.axis_size("dp")
    return [values[..., low : low + width] for low in range(0, values.shape[-1], width)]


def by_core(values, core):
    blocks = feature_blocks(values)
    pairs = [(blocks[2 * chip], blocks[2 * chip + 1]) for chip in ring_order(len(blocks) // 2)]
    own = [jnp.where(core == 0, even, odd) for even, odd in pairs]
    other = [jnp.where(core == 0, odd, even) for even, odd in pairs]
    return jnp.concatenate(own + other, axis=-1)


def per_device(
    hidden_in,
    gain_attn,
    w_query,
    w_key,
    w_value,
    w_out,
    gain_mlp,
    w_gate,
    w_up,
    w_down,
    positions,
    cotangent,
):
    size = lax.axis_size("tensor")
    chips = lax.axis_size("dp") // 2
    me = lax.axis_index("tensor")
    me_array = jnp.full((1,), me, jnp.int32)
    core = lax.axis_index("dp") % 2
    q_width, kv_width = w_query.shape[1], w_key.shape[1]
    group = q_width // kv_width
    units = w_down.shape[0] // 2
    half = hidden_in.shape[1] // 2

    columns = Columns(q_width, kv_width)
    attn_shard = jnp.concatenate([w_query, w_out.T, w_key, w_value], axis=1)
    attn_shard, hidden_in, gain_attn = barrier((attn_shard, hidden_in, gain_attn))
    attn_own = gather(attn_shard)
    residual = by_core(hidden_in, core)
    blocks_in = spread(residual)
    gains = lax.all_gather(jnp.stack([gain_attn, gain_mlp]), "dp", axis=1, tiled=True)
    gains = by_core(gains, core).astype(jnp.float32)
    cosine, sine = tables(positions)
    cotangent = by_core(cotangent, core)
    down_t = w_down.T
    shares = []
    for part in range(2):
        cut = slice(part * units, (part + 1) * units)
        shares.append(jnp.concatenate([w_gate[:, cut], w_up[:, cut], down_t[:, cut]], axis=1))
    shares, attn_own, blocks_in, cosine, sine, gains, cotangent = barrier(
        (shares, attn_own, blocks_in, cosine, sine, gains, cotangent)
    )
    mlp_own = [gather(share) for share in shares]
    cot_blocks = spread(cotangent)
    gain_one, gain_two = gains[0], gains[1]
    attn = (attn_own, cross(attn_own))

    tokens_one, query, key_pad, value_pad = project(
        me_array, blocks_in, gain_one[None, :], *attn, cosine, sine, columns
    )
    attended, log_total, *parts = attend(
        me_array, query, key_pad, value_pad, *attn, columns, size, group
    )
    parts, cot_blocks, tokens_one, attended = barrier((parts, cot_blocks, tokens_one, attended))
    arrived, _ = send_sum(parts)
    cot_other = other_half(cot_blocks)
    cot_blocks = [[block] for block in cot_blocks]
    early = (cross(tokens_one[:, half:]), cross(attended))
    arrived, cot_other, early = barrier((arrived, cot_other, early))
    out_t = [w[:, q_width : 2 * q_width] for w in attn]
    middle, normed_two = row_call(
        middle_kernel, [jnp.float32, jnp.bfloat16], [*arrived, residual, gain_two[None, :]]
    )
    tokens_two, own_share = spread_around(normed_two, mlp_own[0])
    weights = (own_share, cross(own_share))
    tokens_two, weights, out_own = barrier((tokens_two, weights, out_t[0]))
    tokens_other = other_half(sum(tokens_two, []))
    *acts, dn_part, y_part = mlp(tokens_two, cot_blocks, *weights, ())
    out_blocks = spread(out_own)
    acts, tokens_other = barrier((acts, tokens_other))
    acts_other = [cross(act) for act in acts]
    grads_one = mlp_grads(
        chips, tokens_two, cot_blocks, tokens_other, cot_other, acts, acts_other
    )
    grads_one, own_share = barrier((grads_one, mlp_own[1]))
    sums_one = scatter(grads_one)
    weights = (own_share, cross(own_share))
    *acts, y_part = mlp(tokens_two, cot_blocks, *weights, (dn_part, y_part))
    acts, dn_part = acts[:3], acts[3:]
    acts, dn_part, out_blocks = barrier((acts, dn_part, out_blocks))
    acts_other = [cross(act) for act in acts]
    arrived, acts = send_sum(dn_part, acts)
    out_other = [out_t[1]] + [cross(block) for block in out_blocks[1:]]
    grads_two = mlp_grads(
        chips, tokens_two, cot_blocks, tokens_other, cot_other, acts, acts_other
    )
    grads_two, arrived, out_other, y_part = barrier((grads_two, arrived, out_other, y_part))
    y_blocks = list(y_part.reshape((size, -1) + y_part.shape[1:]))
    y_early = [swap(y_blocks[step], step) for step in range(1, 3)]
    sums_two = scatter(grads_two)
    middle_grad, branch, gain_two_part, do_blocks = middle_back(
        arrived, middle, cotangent, gain_two[None, :], out_blocks, out_other
    )
    do_blocks = send_blocks(do_blocks)
    gain_two_other = cross(gain_two_part[half:])
    do_blocks, branch, gain_two_other, y_blocks, y_early = barrier(
        (do_blocks, branch, gain_two_other, y_blocks, y_early)
    )
    branch_blocks = spread(branch)
    qkv_grad = attend_back(
        me_array, query, log_total, key_pad, value_pad, cosine, sine, do_blocks, group
    )
    qkv_grad, sums_one = barrier((qkv_grad, sums_one))
    qkv_other = cross(qkv_grad)
    normed_part = input_grad(qkv_grad, *attn, columns, size)
    branch_blocks, normed_part = barrier((branch_blocks, normed_part))
    branch_other = other_half(branch_blocks)
    tokens_other, attended_other = early
    grads, gain_parts = attn_grads(
        chips,
        tokens_one,
        branch_blocks,
        (qkv_grad, attended),
        (tokens_other, branch_other, qkv_other, attended_other),
        attn_own,
        columns,
        gain_one[:half, None],
        (gain_two_part[:half] + gain_two_other)[:, None],
    )
    arrived, (grads, sums_two) = send_sum(normed_part, (grads, sums_two))
    attn_sums = scatter(grads)
    gain_sums = add_up(line_parts(gain_parts[:, :, :2]))
    unpacked = unpack_shares(sums_one, sums_two)
    arrived, y_blocks, unpacked, gain_sums = barrier((arrived, y_blocks, unpacked, gain_sums))
    grad_gate, grad_up, grad_down = unpacked
    y_late = [swap(y_blocks[step], step) for step in range(3, size)]
    (grad_in,) = row_call(
        functools.partial(input_back_kernel, chips=chips),
        [jnp.float32],
        [*arrived, residual, middle_grad, gain_one[None, :]],
        core,
    )
    grad_in, gain_sums = barrier((grad_in, gain_sums))
    gain_sums = own_part(gain_sums)
    y_late, grad_in, gain_sums = barrier((y_late, grad_in, gain_sums))
    (out,) = row_call(
        functools.partial(output_kernel, chips=chips),
        [jnp.bfloat16],
        [y_blocks[0], *y_early, *y_late, middle],
        core,
    )
    out, attn_sums = barrier((out, attn_sums))
    grad_query, grad_key, grad_value, grad_out = unpack(attn_sums, q_width, kv_width)
    return (
        out,
        grad_in,
        gain_sums[:, 0],
        grad_query,
        grad_key,
        grad_value,
        grad_out,
        gain_sums[:, 1],
        grad_gate,
        grad_up,
        grad_down,
    )


def solution(mesh):
    return jax.shard_map(
        per_device,
        mesh=mesh,
        in_specs=(
            P(("dp", "tensor"), None),
            P("dp"),
            P("dp", "tensor"),
            P("dp", "tensor"),
            P("dp", "tensor"),
            P("tensor", "dp"),
            P("dp"),
            P("dp", "tensor"),
            P("dp", "tensor"),
            P("tensor", "dp"),
            P("dp"),
            P(("dp", "tensor"), None),
        ),
        out_specs=(
            P(("dp", "tensor"), None),
            P(("dp", "tensor"), None),
            P(("dp", "tensor")),
            P("dp", "tensor"),
            P("dp", "tensor"),
            P("dp", "tensor"),
            P("tensor", "dp"),
            P(("dp", "tensor")),
            P("dp", "tensor"),
            P("dp", "tensor"),
            P("tensor", "dp"),
        ),
        check_vma=False,
    )
```

```python
import functools
import math

import jax
import jax.numpy as jnp
from jax import lax
from jax.experimental import pallas as pl
from jax.experimental.pallas import tpu as pltpu
from jax.sharding import PartitionSpec as P

HEAD_DIM = 64
PAIR = 2 * HEAD_DIM
SEQ_LEN = 1024


EPS = 1e-05
ROPE_BASE = 500000.0
SCALE = 1.0 / math.sqrt(HEAD_DIM)
PARAMS = pltpu.CompilerParams(vmem_limit_bytes=58 * 2**20)
ONCE = pl.Buffered(1)

barrier = lax.optimization_barrier


def hint(flops):
    return pl.CostEstimate(flops=flops, bytes_accessed=0, transcendentals=0)


def rms_scale(values):
    return lax.rsqrt(jnp.mean(values * values, axis=-1, keepdims=True) + EPS)


def norm_back(grad, values, scale, gain):
    inner = grad * gain
    cubed = scale * scale * scale
    result = scale * inner - values * cubed * jnp.mean(inner * values, axis=-1, keepdims=True)
    return (result, jnp.sum(grad * values * scale, axis=0))


def mm(left, right):
    return jnp.dot(left, right, preferred_element_type=jnp.float32)


def mm_nt(left, right):
    return lax.dot_general(left, right, (((1,), (1,)), ((), ())), preferred_element_type=jnp.float32)


def mm_tn(left, right):
    return lax.dot_general(left, right, (((0,), (0,)), ((), ())), preferred_element_type=jnp.float32)


def lane_index(rows):
    return lax.broadcasted_iota(jnp.int32, (rows, PAIR), 1)


def turn(pair, cosine, sine):
    lower = lane_index(pair.shape[0]) % HEAD_DIM < HEAD_DIM // 2
    other = jnp.where(
        lower, pltpu.roll(pair, PAIR - HEAD_DIM // 2, 1), pltpu.roll(pair, HEAD_DIM // 2, 1)
    )
    return pair * cosine + other * sine


def project_kernel(place_ref, *refs, size, q_width, kv_width):
    x_refs = refs[:size]
    gain_ref, qo_ref, qx_ref, kvo_ref, kvx_ref, cos_ref, sin_ref = refs[size:-4]
    n_ref, q_ref, k_ref, v_ref = refs[-4:]
    rows = q_ref.shape[0]
    half = qo_ref.shape[0]

    def one(x_ref):
        x = x_ref[...].astype(jnp.float32)
        normed = (x * rms_scale(x) * gain_ref[...]).astype(jnp.bfloat16)
        n_ref[...] = normed
        cosine, sine = cos_ref[...], sin_ref[...]
        own, other = normed[:, :half], normed[:, half:]
        lin = mm(own, qo_ref[...]) + mm(other, qx_ref[...])
        for low in range(0, q_width, PAIR):
            query = turn(lin[:, low : low + PAIR], cosine, sine).astype(jnp.bfloat16)
            q_ref[:, low : low + PAIR] = query * jnp.bfloat16(SCALE)
        lin = mm(own, kvo_ref[...]) + mm(other, kvx_ref[...])
        first = lane_index(rows) < HEAD_DIM
        for ref, start, rotate in ((k_ref, 0, True), (v_ref, kv_width, False)):
            for head in range(kv_width // HEAD_DIM):
                low = start + head * HEAD_DIM
                block = lin[:, low // PAIR * PAIR : low // PAIR * PAIR + PAIR]
                if rotate:
                    block = turn(block, cosine, sine)
                moved = pltpu.roll(block, HEAD_DIM, 1)
                if low % PAIR:
                    block, moved = moved, block
                ref[head, 0] = jnp.where(first, block, 0.0).astype(jnp.bfloat16)
                ref[head, 1] = jnp.where(first, 0.0, moved).astype(jnp.bfloat16)

    for step in range(size):
        pl.when(pl.program_id(0) == step)(functools.partial(one, x_refs[step]))


class Columns:
    def __init__(self, q_width, kv_width):
        self.q_width, self.kv_width = q_width, kv_width

    def spec(self, part, rows, place=lambda *_: 0):
        width, start = {
            "q": (self.q_width, 0),
            "out": (self.q_width, self.q_width),
            "kv": (2 * self.kv_width, 2 * self.q_width),
        }[part]
        index = start // width
        mode = {"pipeline_mode": ONCE} if place() == 0 else {}
        return pl.BlockSpec((rows, width), lambda *grid: (place(*grid), index), **mode)


def project(me, blocks, gain, own, other, cosine, sine, columns):
    size = len(blocks)
    rows, features = blocks[0].shape
    total = rows * size
    q_width, kv_width = columns.q_width, columns.kv_width
    key_heads = kv_width // HEAD_DIM
    width = q_width + 2 * kv_width
    half = features // 2
    fixed = lambda p, m: (0, 0)
    placed = lambda p, m: (jnp.bitwise_xor(p, m[0]), 0)
    padded = pl.BlockSpec(
        (key_heads, 2, rows, PAIR), lambda p, m: (0, 0, jnp.bitwise_xor(p, m[0]), 0)
    )
    spec = pltpu.PrefetchScalarGridSpec(
        num_scalar_prefetch=1,
        grid=(size,),
        in_specs=[pl.BlockSpec((rows, features), fixed, pipeline_mode=ONCE)] * size
        + [
            pl.BlockSpec((1, features), fixed),
            columns.spec("q", half),
            columns.spec("q", half),
            columns.spec("kv", half),
            columns.spec("kv", half),
            pl.BlockSpec((rows, PAIR), placed),
            pl.BlockSpec((rows, PAIR), placed),
        ],
        out_specs=[
            pl.BlockSpec((rows, features), lambda p, m: (p, 0)),
            pl.BlockSpec((rows, q_width), lambda p, m: (p, 0)),
            padded,
            padded,
        ],
    )
    padded_shape = jax.ShapeDtypeStruct((key_heads, 2, total, PAIR), jnp.bfloat16)
    return pl.pallas_call(
        functools.partial(project_kernel, size=size, q_width=q_width, kv_width=kv_width),
        grid_spec=spec,
        out_shape=[
            jax.ShapeDtypeStruct((total, features), jnp.bfloat16),
            jax.ShapeDtypeStruct((total, q_width), jnp.bfloat16),
            padded_shape,
            padded_shape,
        ],
        compiler_params=PARAMS,
        cost_estimate=hint(2 * total * features * width // 16),
    )(me, *blocks, gain, own, other, own, other, cosine, sine)


def attend_kernel(
    me_ref, q_ref, k_ref, v_ref, wo_ref, wx_ref, o_ref, l_ref, *refs, size, heads, group
):
    part_refs, vt_ref = refs[:size], refs[size]
    rows = q_ref.shape[0]
    half = wo_ref.shape[0]
    mine = jnp.bitwise_xor(me_ref[0], pl.program_id(0))
    key_place = lax.broadcasted_iota(jnp.int32, (rows, rows), 0)
    query_place = lax.broadcasted_iota(jnp.int32, (rows, rows), 1)

    @pl.when(pl.program_id(0) == 0)
    def _():
        for head in range(heads // group):
            for side in range(2):
                vt_ref[head, side] = v_ref[head, side].T

    def one(span):
        keys = span * rows
        for pair in range(heads // 2):
            head = 2 * pair // group
            lanes = slice(pair * PAIR, (pair + 1) * PAIR)
            query = q_ref[:, lanes]
            acc = None
            inverse = []
            for side in range(2):
                diag = mm_nt(k_ref[head, side, keys : keys + rows, :], query)
                diag = jnp.where(key_place <= query_place, diag, -1e9)
                top = jnp.max(diag, axis=0, keepdims=True)
                if span:
                    body = mm_nt(k_ref[head, side, :keys, :], query)
                    top = jnp.maximum(top, jnp.max(body, axis=0, keepdims=True))
                diag = jnp.exp(diag - top)
                total = jnp.sum(diag, axis=0, keepdims=True)
                part = mm(vt_ref[head, side, :, keys : keys + rows], diag.astype(jnp.bfloat16))
                if span:
                    body = jnp.exp(body - top)
                    total = total + jnp.sum(body, axis=0, keepdims=True)
                    part = part + mm(vt_ref[head, side, :, :keys], body.astype(jnp.bfloat16))
                acc = part if acc is None else acc + part
                inverse.append(jnp.broadcast_to(1.0 / total, (HEAD_DIM, rows)))
                l_ref[2 * pair + side : 2 * pair + side + 1, :] = top + jnp.log(total)
            acc = acc * jnp.concatenate(inverse, axis=0)
            o_ref[:, lanes] = acc.T.astype(jnp.bfloat16)

    for span in range(size):
        pl.when(mine == span)(functools.partial(one, span))

    def project_out(ref):
        ref[:, :half] = mm_nt(o_ref[...], wo_ref[...]).astype(jnp.bfloat16)
        ref[:, half:] = mm_nt(o_ref[...], wx_ref[...]).astype(jnp.bfloat16)

    for step in range(size):
        pl.when(pl.program_id(0) == step)(functools.partial(project_out, part_refs[step]))


def attend(me, query, key_pad, value_pad, own, other, columns, size, group):
    total, width = query.shape
    features = 2 * own.shape[0]
    rows, heads = total // size, width // HEAD_DIM
    whole = pl.BlockSpec(key_pad.shape, lambda p, m: (0, 0, 0, 0), pipeline_mode=ONCE)
    spec = pltpu.PrefetchScalarGridSpec(
        num_scalar_prefetch=1,
        grid=(size,),
        in_specs=[pl.BlockSpec((rows, width), lambda p, m: (p, 0)), whole, whole]
        + [columns.spec("out", features // 2)] * 2,
        out_specs=[
            pl.BlockSpec((rows, width), lambda p, m: (p, 0)),
            pl.BlockSpec((heads, rows), lambda p, m: (0, p)),
        ]
        + [pl.BlockSpec((rows, features), lambda p, m: (0, 0))] * size,
        scratch_shapes=[pltpu.VMEM((heads // group, 2, PAIR, total), jnp.bfloat16)],
    )
    return pl.pallas_call(
        functools.partial(attend_kernel, size=size, heads=heads, group=group),
        grid_spec=spec,
        out_shape=[
            jax.ShapeDtypeStruct((total, width), jnp.bfloat16),
            jax.ShapeDtypeStruct((heads, total), jnp.float32),
        ]
        + [jax.ShapeDtypeStruct((rows, features), jnp.bfloat16)] * size,
        compiler_params=PARAMS,
        cost_estimate=hint(8 * heads * total * total * HEAD_DIM // 16),
    )(me, query, key_pad, value_pad, own, other)


def attend_back_kernel(
    me_ref, q_ref, l_ref, k_ref, v_ref, cos_ref, sin_ref, *refs, size, heads, group
):
    do_refs = refs[:size]
    out_ref, dk_ref, dv_ref, kt_ref, do_ref = refs[size:]
    rows = q_ref.shape[0]
    key_heads = heads // group
    step = pl.program_id(0)
    me = me_ref[0]
    mine = jnp.bitwise_xor(me, step)
    key_place = lax.broadcasted_iota(jnp.int32, (rows, rows), 0)
    query_place = lax.broadcasted_iota(jnp.int32, (rows, rows), 1)

    def rows_of(block):
        return pl.ds(pl.multiple_of(block * rows, rows), rows)

    @pl.when(step == 0)
    def _():
        dk_ref[...] = jnp.zeros_like(dk_ref)
        dv_ref[...] = jnp.zeros_like(dv_ref)
        for head in range(key_heads):
            for side in range(2):
                kt_ref[head, side] = k_ref[head, side].T

    def fetch(ref):
        do_ref[...] = ref[...]

    for block in range(size):
        pl.when(step == block)(functools.partial(fetch, do_refs[block]))

    def one(span):
        keys = span * rows
        parts = [(keys, keys + rows, True)] + ([(0, keys, False)] if span else [])
        cosine, sine = cos_ref[keys : keys + rows, :], sin_ref[keys : keys + rows, :]
        for pair in range(heads // 2):
            head = 2 * pair // group
            lanes = slice(pair * PAIR, (pair + 1) * PAIR)
            query, grad = q_ref[:, lanes], do_ref[:, lanes]
            acc = None
            for side in range(2):
                log_total = l_ref[2 * pair + side : 2 * pair + side + 1, :]
                inner = None
                kept = []
                for low, high, diagonal in parts:
                    probs = mm_nt(k_ref[head, side, low:high, :], query)
                    probs = jnp.exp(probs - log_total)
                    if diagonal:
                        probs = jnp.where(key_place <= query_place, probs, 0.0)
                    prob_grad = mm_nt(v_ref[head, side, low:high, :], grad)
                    dv_ref[head, side, low:high, :] += mm(probs.astype(jnp.bfloat16), grad)
                    term = jnp.sum(probs * prob_grad, axis=0, keepdims=True)
                    inner = term if inner is None else inner + term
                    kept.append((low, high, probs, prob_grad))
                for low, high, probs, prob_grad in kept:
                    score_grad = (probs * (prob_grad - inner)).astype(jnp.bfloat16)
                    dk_ref[head, side, low:high, :] += mm(score_grad, query)
                    part = mm(kt_ref[head, side, :, low:high], score_grad)
                    acc = part if acc is None else acc + part
            turned = turn(acc.T * SCALE, cosine, -sine)
            out_ref[rows_of(step), lanes] = turned.astype(jnp.bfloat16)

    for span in range(size):
        pl.when(mine == span)(functools.partial(one, span))

    @pl.when(step == size - 1)
    def _():
        first = lane_index(rows) < HEAD_DIM
        wanted = [(dk_ref, head, True) for head in range(key_heads)]
        wanted += [(dv_ref, head, False) for head in range(key_heads)]
        for span in range(size):
            place = slice(span * rows, (span + 1) * rows)
            cosine, sine = cos_ref[place, :], sin_ref[place, :]
            for block in range(len(wanted) // 2):
                halves, rotate = [], []
                for half in range(2):
                    ref, head, is_key = wanted[2 * block + half]
                    low, high = ref[head, 0, place, :], ref[head, 1, place, :]
                    if half:
                        halves.append(pltpu.roll(low, HEAD_DIM, 1) + high)
                    else:
                        halves.append(low + pltpu.roll(high, HEAD_DIM, 1))
                    rotate.append(is_key)
                value = jnp.where(first, halves[0], halves[1])
                if rotate[0] and rotate[1]:
                    value = turn(value, cosine, -sine)
                elif rotate[0]:
                    value = jnp.where(first, turn(value, cosine, -sine), value)
                start = heads * HEAD_DIM + block * PAIR
                target = rows_of(jnp.bitwise_xor(me, span))
                out_ref[target, start : start + PAIR] = value.astype(jnp.bfloat16)


def attend_back(
    me, query, log_total, key_pad, value_pad, cosine, sine, attended_grad, group
):
    total, width = query.shape
    size = len(attended_grad)
    rows, heads = total // size, width // HEAD_DIM
    key_heads = heads // group
    out_width = width + 2 * key_heads * HEAD_DIM
    whole = pl.BlockSpec(key_pad.shape, lambda p, m: (0, 0, 0, 0), pipeline_mode=ONCE)
    table = pl.BlockSpec((total, PAIR), lambda p, m: (0, 0), pipeline_mode=ONCE)
    spec = pltpu.PrefetchScalarGridSpec(
        num_scalar_prefetch=1,
        grid=(size,),
        in_specs=[
            pl.BlockSpec((rows, width), lambda p, m: (p, 0)),
            pl.BlockSpec((heads, rows), lambda p, m: (0, p)),
            whole,
            whole,
            table,
            table,
        ]
        + [pl.BlockSpec((rows, width), lambda p, m: (0, 0), pipeline_mode=ONCE)] * size,
        out_specs=pl.BlockSpec((total, out_width), lambda p, m: (0, 0)),
        scratch_shapes=[
            pltpu.VMEM(key_pad.shape, jnp.float32),
            pltpu.VMEM(key_pad.shape, jnp.float32),
            pltpu.VMEM((key_heads, 2, PAIR, total), jnp.bfloat16),
            pltpu.VMEM((rows, width), jnp.bfloat16),
        ],
    )
    return pl.pallas_call(
        functools.partial(attend_back_kernel, size=size, heads=heads, group=group),
        grid_spec=spec,
        out_shape=jax.ShapeDtypeStruct((total, out_width), jnp.bfloat16),
        compiler_params=PARAMS,
        cost_estimate=hint(20 * heads * total * total * HEAD_DIM),
    )(me, query, log_total, key_pad, value_pad, cosine, sine, *attended_grad)


def grouped(arrays, counts):
    arrays = iter(arrays)
    return [[next(arrays) for _ in range(count)] for count in counts]


def mlp_kernel(*refs, n_counts, e_counts, adds):
    size = len(n_counts)
    pieces = sum(n_counts) + sum(e_counts)
    n_refs = grouped(refs, n_counts)
    e_refs = grouped(refs[sum(n_counts) :], e_counts)
    gate_o, up_o, down_o, gate_x, up_x, down_x = refs[pieces : pieces + 6]
    y_ref, n_ref, e_ref = refs[-3:]
    dn_refs = refs[-3 - size if adds else -4 : -3]
    dg_ref, du_ref, h_ref = refs[-6 - size if adds else -7 :][:3]
    half = gate_o.shape[0]

    def fetch(step):
        for target, sources in ((n_ref, n_refs[step]), (e_ref, e_refs[step])):
            low = 0
            for source in sources:
                high = low + source.shape[0]
                target[low:high] = source[...]
                low = high

    for step in range(size):
        pl.when(pl.program_id(0) == step)(functools.partial(fetch, step))
    gate = mm(n_ref[:, :half], gate_o[...]) + mm(n_ref[:, half:], gate_x[...])
    up = mm(n_ref[:, :half], up_o[...]) + mm(n_ref[:, half:], up_x[...])
    grad = mm(e_ref[:, :half], down_o[...]) + mm(e_ref[:, half:], down_x[...])
    sigma = jax.nn.sigmoid(gate)
    silu = gate * sigma
    hidden = (silu * up).astype(jnp.bfloat16)
    gate_grad = (grad * up * sigma * (1.0 + gate * (1.0 - sigma))).astype(jnp.bfloat16)
    up_grad = (grad * silu).astype(jnp.bfloat16)
    dg_ref[...] = gate_grad
    du_ref[...] = up_grad
    h_ref[...] = hidden
    for part, gate_w, up_w, down_w in ((0, gate_o, up_o, down_o), (1, gate_x, up_x, down_x)):
        lanes = slice(part * half, (part + 1) * half)
        dn = mm_nt(gate_grad, gate_w[...]) + mm_nt(up_grad, up_w[...])
        y = mm_nt(hidden, down_w[...])
        if adds:
            dn = dn + refs[pieces + 6][:, lanes].astype(jnp.float32)
            y = y + refs[pieces + 7][:, lanes].astype(jnp.float32)
        y_ref[:, lanes] = y.astype(jnp.bfloat16)
        dn = dn.astype(jnp.bfloat16)

        def store(ref):
            ref[:, lanes] = dn

        if adds:
            for step in range(size):
                pl.when(pl.program_id(0) == step)(functools.partial(store, dn_refs[step]))
        else:
            store(dn_refs[0])


def mlp(tokens, cot, own, other, earlier):
    size = len(tokens)
    rows, features = tokens[0][0].shape
    half, units = own.shape[0], own.shape[1] // 3
    total = rows * size
    fixed = lambda p: (0, 0)
    moving = lambda p: (p, 0)
    wide = pl.BlockSpec((rows, features), moving)
    sums = jax.ShapeDtypeStruct((total, features), jnp.bfloat16)
    dn_specs, dn_shapes = [wide], [sums]
    if earlier:
        dn_specs = [pl.BlockSpec((rows, features), fixed)] * size
        dn_shapes = [jax.ShapeDtypeStruct((rows, features), jnp.bfloat16)] * size
    pieces = sum(tokens, []) + sum(cot, [])
    thirds = [
        pl.BlockSpec((half, units), lambda p, t=t: (0, t), pipeline_mode=ONCE) for t in range(3)
    ]
    return pl.pallas_call(
        functools.partial(
            mlp_kernel,
            n_counts=[len(group) for group in tokens],
            e_counts=[len(group) for group in cot],
            adds=bool(earlier),
        ),
        grid=(size,),
        in_specs=[pl.BlockSpec(piece.shape, fixed, pipeline_mode=ONCE) for piece in pieces]
        + thirds * 2
        + [wide] * len(earlier),
        out_specs=[pl.BlockSpec((rows, units), moving)] * 3 + dn_specs + [wide],
        out_shape=[jax.ShapeDtypeStruct((total, units), jnp.bfloat16)] * 3 + dn_shapes + [sums],
        scratch_shapes=[pltpu.VMEM((rows, features), jnp.bfloat16)] * 2,
        compiler_params=PARAMS,
        cost_estimate=hint(12 * total * features * units),
    )(*pieces, own, own, own, other, other, other, *earlier)


def add_refs(refs):
    total = refs[0][...].astype(jnp.float32)
    for ref in refs[1:]:
        total = total + ref[...].astype(jnp.float32)
    return total


def store_by_device(out_ref, values, core, chips):
    width = values.shape[1] // (2 * chips)
    for chip in range(chips):
        own = values[:, chip * width : (chip + 1) * width]
        other = values[:, (chips + chip) * width : (chips + chip + 1) * width]
        low = 2 * chip * width
        out_ref[:, low : low + width] = jnp.where(core == 0, own, other)
        out_ref[:, low + width : low + 2 * width] = jnp.where(core == 0, other, own)


def middle_kernel(*refs):
    x_ref, gain_ref, middle_ref, normed_ref = refs[-4:]
    values = x_ref[...].astype(jnp.float32) + add_refs(refs[:-4])
    middle_ref[...] = values
    normed_ref[...] = (values * rms_scale(values) * gain_ref[...]).astype(jnp.bfloat16)


def input_back_kernel(core_ref, *refs, chips):
    x_ref, before_ref, gain_ref, out_ref = refs[-4:]
    values = x_ref[...].astype(jnp.float32)
    inner = add_refs(refs[:-4]) * gain_ref[...]
    scale = rms_scale(values)
    mean = jnp.mean(inner * values, axis=-1, keepdims=True)
    result = before_ref[...] + scale * inner - values * (scale * scale * scale) * mean
    store_by_device(out_ref, result, core_ref[0], chips)


def output_kernel(core_ref, *refs, chips):
    middle_ref, out_ref = refs[-2:]
    values = middle_ref[...] + add_refs(refs[:-2])
    store_by_device(out_ref, values.astype(jnp.bfloat16), core_ref[0], chips)


def row_call(body, dtypes, arrays, core=None):
    rows, features = arrays[0].shape
    steps = 2
    wide = pl.BlockSpec((rows // steps, features), lambda i, *_: (i, 0))
    row = pl.BlockSpec((1, features), lambda i, *_: (0, 0))
    scalars = [] if core is None else [jnp.full((1,), core, jnp.int32)]
    return pl.pallas_call(
        body,
        grid_spec=pltpu.PrefetchScalarGridSpec(
            num_scalar_prefetch=len(scalars),
            grid=(steps,),
            in_specs=[row if array.shape[0] == 1 else wide for array in arrays],
            out_specs=[wide] * len(dtypes),
        ),
        out_shape=[jax.ShapeDtypeStruct((rows, features), dtype) for dtype in dtypes],
        compiler_params=PARAMS,
        cost_estimate=hint(0),
    )(*scalars, *arrays)


def unpack_kernel(sum_ref, q_ref, k_ref, v_ref, out_ref):
    q_width, kv_width = q_ref.shape[1], k_ref.shape[1]
    values = sum_ref[...].astype(jnp.float32)
    q_ref[...] = values[:, :q_width]
    kv = values[:, q_width : q_width + 2 * kv_width]
    k_ref[...] = kv[:, :kv_width]
    v_ref[...] = kv[:, kv_width:]
    out_ref[...] = values[:, q_width + 2 * kv_width :].T


def unpack(sums, q_width, kv_width):
    rows = sums.shape[0]
    widths = [(rows, q_width), (rows, kv_width), (rows, kv_width), (q_width, rows)]
    return pl.pallas_call(
        unpack_kernel,
        out_shape=[jax.ShapeDtypeStruct(shape, jnp.float32) for shape in widths],
        compiler_params=PARAMS,
        cost_estimate=hint(0),
    )(sums)


def unpack_shares_kernel(one_ref, two_ref, gate_ref, up_ref, down_ref):
    units = one_ref.shape[1] // 3
    for part, ref in enumerate((one_ref, two_ref)):
        cut = slice(part * units, (part + 1) * units)
        gate_ref[:, cut] = ref[:, :units].astype(jnp.float32)
        up_ref[:, cut] = ref[:, units : 2 * units].astype(jnp.float32)
        down_ref[cut, :] = ref[:, 2 * units :].astype(jnp.float32).T


def unpack_shares(one, two):
    rows, width = one.shape
    units = 2 * width // 3
    shapes = [(rows, units), (rows, units), (units, rows)]
    return pl.pallas_call(
        unpack_shares_kernel,
        out_shape=[jax.ShapeDtypeStruct(shape, jnp.float32) for shape in shapes],
        compiler_params=PARAMS,
        cost_estimate=hint(0),
    )(one, two)


def middle_back_kernel(*refs, parts, size):
    n_refs, refs = refs[:parts], refs[parts:]
    x_ref, e_ref, gain_ref, refs = refs[0], refs[1], refs[2], refs[3:]
    own_refs, other_refs, refs = refs[:size], refs[size : 2 * size], refs[2 * size :]
    grad_ref, branch_ref, part_ref, do_refs = refs[0], refs[1], refs[2], refs[3:]
    half = own_refs[0].shape[0]
    grad = add_refs(n_refs)
    values = x_ref[...]
    scale = rms_scale(values)
    result, part = norm_back(grad, values, scale, gain_ref[...])

    @pl.when(pl.program_id(0) == 0)
    def _():
        part_ref[...] = jnp.zeros_like(part_ref)

    part_ref[...] += part[None, :]
    result = result + e_ref[...].astype(jnp.float32)
    grad_ref[...] = result
    branch = result.astype(jnp.bfloat16)
    branch_ref[...] = branch
    for own, other, do_ref in zip(own_refs, other_refs, do_refs):
        do = mm(branch[:, :half], own[...]) + mm(branch[:, half:], other[...])
        do_ref[...] = do.astype(jnp.bfloat16)


def middle_back(arrived, middle, cot, gain, own, other):
    parts, size = len(arrived), len(own)
    rows, features = middle.shape
    width = own[0].shape[1]
    steps = 2
    wide = pl.BlockSpec((rows // steps, features), lambda i: (i, 0))
    narrow = pl.BlockSpec((rows // steps, width), lambda i: (i, 0))
    row = pl.BlockSpec((1, features), lambda i: (0, 0))
    weight = pl.BlockSpec((features // 2, width), lambda i: (0, 0), pipeline_mode=ONCE)
    grad, branch, part, *do = pl.pallas_call(
        functools.partial(middle_back_kernel, parts=parts, size=size),
        grid=(steps,),
        in_specs=[wide] * parts + [wide, wide, row] + [weight] * (2 * size),
        out_specs=[wide, wide, row] + [narrow] * size,
        out_shape=[
            jax.ShapeDtypeStruct((rows, features), jnp.float32),
            jax.ShapeDtypeStruct((rows, features), jnp.bfloat16),
            jax.ShapeDtypeStruct((1, features), jnp.float32),
        ]
        + [jax.ShapeDtypeStruct((rows, width), jnp.bfloat16)] * size,
        compiler_params=PARAMS,
        cost_estimate=hint(2 * rows * features * width * size),
    )(*arrived, middle, cot, gain, *own, *other)
    return grad, branch, part[0], do


def column_grad(blocks, other, mine, theirs):
    total = mm_tn(other[...], theirs[...])
    low = 0
    for block in blocks:
        high = low + block.shape[0]
        total = total + mm_tn(block[...], mine[low:high, :])
        low = high
    return total


def grad_kernel(*refs, n_count, e_count):
    n_refs, refs = refs[:n_count], refs[n_count:]
    e_refs, refs = refs[:e_count], refs[e_count:]
    n_other, e_other = refs[:2]
    acts, out_ref = refs[2:-1], refs[-1]
    units = acts[0].shape[1]
    for third in range(3):
        blocks, other = (e_refs, e_other) if third == 2 else (n_refs, n_other)
        grad = column_grad(blocks, other, acts[third], acts[third + 3])
        out_ref[0, :, third * units : (third + 1) * units] = grad.astype(jnp.bfloat16)


def mlp_grads(chips, tokens, cot, tokens_other, cot_other, mine, theirs):
    tokens, cot = sum(tokens, []), sum(cot, [])
    features = tokens[0].shape[1]
    total, units = mine[0].shape
    depth = features // (2 * chips)
    long = pl.BlockSpec((total, depth), lambda b: (0, b))
    fixed = pl.BlockSpec((total, units), lambda b: (0, 0), pipeline_mode=ONCE)
    return pl.pallas_call(
        functools.partial(grad_kernel, n_count=len(tokens), e_count=len(cot)),
        grid=(chips,),
        in_specs=[pl.BlockSpec((p.shape[0], depth), lambda b: (0, b)) for p in tokens + cot]
        + [long, long]
        + [fixed] * 6,
        out_specs=pl.BlockSpec((1, depth, 3 * units), lambda b: (b, 0, 0)),
        out_shape=jax.ShapeDtypeStruct((chips, depth, 3 * units), jnp.bfloat16),
        compiler_params=PARAMS,
        cost_estimate=hint(6 * total * features * units),
    )(*tokens, *cot, tokens_other, cot_other, *mine, *theirs)


def attn_grad_kernel(*refs, size):
    e_refs = refs[2 : 2 + size]
    n_ref, n_other = refs[:2]
    e_other, d_ref, d_other, o_ref, o_other, q_ref, kv_ref, g1_ref, g2_ref = refs[2 + size : -2]
    out_ref, gain_ref = refs[-2:]
    width, out_width = d_ref.shape[1], o_ref.shape[1]
    grad = column_grad([n_ref], n_other, d_ref, d_other)
    out_ref[0, :, :width] = grad.astype(jnp.bfloat16)
    out_grad = column_grad(e_refs, e_other, o_ref, o_other)
    out_ref[0, :, width : width + out_width] = out_grad.astype(jnp.bfloat16)
    cut = q_ref.shape[1]
    first = jnp.sum(grad[:, :cut] * q_ref[...].astype(jnp.float32), axis=1, keepdims=True)
    first += jnp.sum(grad[:, cut:] * kv_ref[...].astype(jnp.float32), axis=1, keepdims=True)
    first = first / g1_ref[...]
    lane = lane_index(grad.shape[0])
    gain_ref[0] = jnp.where(lane == 0, first, g2_ref[...])


def attn_grads(
    chips, tokens, branch, mine, theirs, weights, columns, gain_one, gain_two_part
):
    size = len(branch)
    qkv_grad, attended = mine
    tokens_other, branch_other, qkv_other, attended_other = theirs
    total, features = tokens.shape
    rows = total // size
    width, out_width = qkv_grad.shape[1], attended.shape[1]
    depth = features // (2 * chips)
    column = lambda b: (0, b)
    row = lambda b: (b, 0)
    long = pl.BlockSpec((total, depth), column)
    fixed = lambda array: pl.BlockSpec(array.shape, lambda b: (0, 0), pipeline_mode=ONCE)
    place = lambda b: (b, 0, 0)
    return pl.pallas_call(
        functools.partial(attn_grad_kernel, size=size),
        grid=(chips,),
        in_specs=[long, long]
        + [pl.BlockSpec((rows, depth), column)] * size
        + [long]
        + [fixed(qkv_grad)] * 2
        + [fixed(attended)] * 2
        + [
            columns.spec("q", depth, lambda b=None: b),
            columns.spec("kv", depth, lambda b=None: b),
            pl.BlockSpec((depth, 1), row),
            pl.BlockSpec((depth, 1), row),
        ],
        out_specs=[
            pl.BlockSpec((1, depth, width + out_width), place),
            pl.BlockSpec((1, depth, PAIR), place),
        ],
        out_shape=[
            jax.ShapeDtypeStruct((chips, depth, width + out_width), jnp.bfloat16),
            jax.ShapeDtypeStruct((chips, depth, PAIR), jnp.float32),
        ],
        compiler_params=PARAMS,
        cost_estimate=hint(2 * total * features * (width + out_width)),
    )(
        tokens,
        tokens_other,
        *branch,
        branch_other,
        qkv_grad,
        qkv_other,
        attended,
        attended_other,
        weights,
        weights,
        gain_one,
        gain_two_part,
    )


def input_grad_kernel(d_ref, qo_ref, qx_ref, kvo_ref, kvx_ref, *out_refs):
    half, cut = qo_ref.shape

    def one(ref):
        query, rest = d_ref[:, :cut], d_ref[:, cut:]
        own = mm_nt(query, qo_ref[...]) + mm_nt(rest, kvo_ref[...])
        other = mm_nt(query, qx_ref[...]) + mm_nt(rest, kvx_ref[...])
        ref[:, :half] = own.astype(jnp.bfloat16)
        ref[:, half:] = other.astype(jnp.bfloat16)

    for step, ref in enumerate(out_refs):
        pl.when(pl.program_id(0) == step)(functools.partial(one, ref))


def input_grad(qkv_grad, own, other, columns, size):
    total, width = qkv_grad.shape
    features = 2 * own.shape[0]
    rows = total // size
    fixed = lambda i: (0, 0)
    weights = [columns.spec(part, own.shape[0]) for part in ("q", "q", "kv", "kv")]
    return pl.pallas_call(
        input_grad_kernel,
        grid=(size,),
        in_specs=[pl.BlockSpec((rows, width), lambda i: (i, 0))] + weights,
        out_specs=[pl.BlockSpec((rows, features), fixed)] * size,
        out_shape=[jax.ShapeDtypeStruct((rows, features), jnp.bfloat16)] * size,
        compiler_params=PARAMS,
        cost_estimate=hint(2 * total * features * width),
    )(qkv_grad, own, other, own, other)


def swap(values, step):
    size = lax.axis_size("tensor")
    return lax.ppermute(values, "tensor", [(i, i ^ step) for i in range(size)])


def spread(values):
    return [values] + [swap(values, step) for step in range(1, lax.axis_size("tensor"))]


def send_blocks(blocks):
    return [blocks[0]] + [swap(block, step + 1) for step, block in enumerate(blocks[1:])]


def spread_around(values, held):
    if lax.axis_size("tensor") != 4:
        blocks = spread(values)
        first, held = barrier((blocks[1], held))
        return [[blocks[0]], [first]] + [[block] for block in blocks[2:]], held
    half = values.shape[0] // 2
    top, bottom = values[:half], values[half:]
    x_bottom, y_top = swap(bottom, 1), swap(top, 2)
    x_bottom, y_top, top, bottom, held = barrier((x_bottom, y_top, top, bottom, held))
    far = [swap(y_top, 1), swap(x_bottom, 2)]
    x_top, y_bottom = swap(top, 1), swap(bottom, 2)
    return [[values], [x_top, x_bottom], [y_top, y_bottom], far], held


def merge_kernel(x_ref, y_ref, top_ref, bottom_ref, x_out, y_out):
    half = top_ref.shape[0]
    x_out[:half] = x_ref[:half]
    x_out[half:] = add_refs([x_ref.at[half:], bottom_ref]).astype(jnp.bfloat16)
    y_out[:half] = add_refs([y_ref.at[:half], top_ref]).astype(jnp.bfloat16)
    y_out[half:] = y_ref[half:]


def send_sum(blocks, held=(), ready=()):
    if len(blocks) != 4:
        return send_blocks(blocks), held
    own, near_x, near_y, far = blocks
    half = far.shape[0] // 2
    top, bottom = swap(far[:half], 1), swap(far[half:], 2)
    if ready:
        top, bottom, _ = barrier((top, bottom, ready))
    near_x, near_y = pl.pallas_call(
        merge_kernel,
        out_shape=[jax.ShapeDtypeStruct(near_x.shape, near_x.dtype)] * 2,
        compiler_params=PARAMS,
        cost_estimate=hint(0),
    )(near_x, near_y, top, bottom)
    near_x, near_y, held = barrier((near_x, near_y, held))
    return [own, swap(near_x, 1), swap(near_y, 2)], held


def add_up(blocks):
    total = blocks[0].astype(jnp.float32)
    for block in blocks[1:]:
        total = total + block.astype(jnp.float32)
    return total


def cross(values):
    count = lax.axis_size("dp")
    return lax.ppermute(values, "dp", [(i, i ^ 1) for i in range(count)])


def tables(positions):
    freqs = ROPE_BASE ** (-jnp.arange(0, HEAD_DIM, 2).astype(jnp.float32) / HEAD_DIM)
    angles = positions.astype(jnp.float32)[:, None] * freqs[None, :]
    cosine, sine = jnp.cos(angles), jnp.sin(angles)
    return (
        jnp.concatenate([cosine] * 4, axis=1),
        jnp.concatenate([-sine, sine, -sine, sine], axis=1),
    )


def chip_lines():
    count = lax.axis_size("dp")
    return [list(range(core, count, 2)) for core in range(2)]


def gather(values):
    return lax.all_gather(values, "dp", axis=0, tiled=True, axis_index_groups=chip_lines())


def scatter(values):
    total = lax.psum_scatter(
        values, "dp", scatter_dimension=0, tiled=True, axis_index_groups=chip_lines()
    )
    return total[0]


def along(values, step):
    count = lax.axis_size("dp")
    return lax.ppermute(values, "dp", [(i, (i + 2 * step) % count) for i in range(count)])


def line_parts(parts):
    chips = lax.axis_size("dp") // 2
    chip = lax.axis_index("dp") // 2
    blocks = [lax.dynamic_index_in_dim(parts, chip, 0, keepdims=False)]
    for step in range(1, chips):
        sent = lax.dynamic_index_in_dim(parts, (chip + step) % chips, 0, keepdims=False)
        blocks.append(along(sent, step))
    return blocks


def own_part(values):
    size = lax.axis_size("tensor")
    me = lax.axis_index("tensor")
    blocks = values.reshape((size, -1) + values.shape[1:])
    own = lax.dynamic_index_in_dim(blocks, me, 0, keepdims=False)
    for step in range(1, size):
        sent = lax.dynamic_index_in_dim(blocks, me ^ step, 0, keepdims=False)
        own = own + swap(sent, step)
    return own


def stack_kernel(*refs):
    low = 0
    for ref in refs[:-1]:
        high = low + ref.shape[0]
        refs[-1][low:high, :] = ref[...]
        low = high


def other_half(blocks):
    features = blocks[0].shape[1]
    shape = (sum(block.shape[0] for block in blocks), features // 2)
    halves = pl.pallas_call(
        stack_kernel,
        grid=(1,),
        in_specs=[pl.BlockSpec((b.shape[0], features // 2), lambda i: (0, 1)) for b in blocks],
        out_specs=pl.BlockSpec(shape, lambda i: (0, 0)),
        out_shape=jax.ShapeDtypeStruct(shape, blocks[0].dtype),
        compiler_params=PARAMS,
        cost_estimate=hint(0),
    )(*blocks)
    return cross(halves)


def feature_blocks(values):
    width = values.shape[-1] // lax.axis_size("dp")
    return [values[..., low : low + width] for low in range(0, values.shape[-1], width)]


def by_core(values, core):
    blocks = feature_blocks(values)
    pairs = list(zip(blocks[0::2], blocks[1::2]))
    own = [jnp.where(core == 0, even, odd) for even, odd in pairs]
    other = [jnp.where(core == 0, odd, even) for even, odd in pairs]
    return jnp.concatenate(own + other, axis=-1)


def per_device(
    hidden_in,
    gain_attn,
    w_query,
    w_key,
    w_value,
    w_out,
    gain_mlp,
    w_gate,
    w_up,
    w_down,
    positions,
    cotangent,
):
    size = lax.axis_size("tensor")
    chips = lax.axis_size("dp") // 2
    me = lax.axis_index("tensor")
    me_array = jnp.full((1,), me, jnp.int32)
    core = lax.axis_index("dp") % 2
    q_width, kv_width = w_query.shape[1], w_key.shape[1]
    group = q_width // kv_width
    units = w_down.shape[0] // 2
    half = hidden_in.shape[1] // 2

    columns = Columns(q_width, kv_width)
    attn_shard = jnp.concatenate([w_query, w_out.T, w_key, w_value], axis=1)
    attn_shard, hidden_in, gain_attn = barrier((attn_shard, hidden_in, gain_attn))
    attn_own = gather(attn_shard)
    residual = by_core(hidden_in, core)
    blocks_in = spread(residual)
    gains = lax.all_gather(jnp.stack([gain_attn, gain_mlp]), "dp", axis=1, tiled=True)
    gains = by_core(gains, core).astype(jnp.float32)
    cosine, sine = tables(positions)
    cotangent = by_core(cotangent, core)
    down_t = w_down.T
    shares = []
    for part in range(2):
        cut = slice(part * units, (part + 1) * units)
        shares.append(jnp.concatenate([w_gate[:, cut], w_up[:, cut], down_t[:, cut]], axis=1))
    shares, attn_own, blocks_in, cosine, sine, gains, cotangent = barrier(
        (shares, attn_own, blocks_in, cosine, sine, gains, cotangent)
    )
    mlp_own = [gather(share) for share in shares]
    cot_blocks = spread(cotangent)
    gain_one, gain_two = gains[0], gains[1]
    attn = (attn_own, cross(attn_own))

    tokens_one, query, key_pad, value_pad = project(
        me_array, blocks_in, gain_one[None, :], *attn, cosine, sine, columns
    )
    attended, log_total, *parts = attend(
        me_array, query, key_pad, value_pad, *attn, columns, size, group
    )
    parts, cot_blocks, tokens_one, attended = barrier((parts, cot_blocks, tokens_one, attended))
    arrived, _ = send_sum(parts)
    cot_other = other_half(cot_blocks)
    cot_blocks = [[block] for block in cot_blocks]
    early = (cross(tokens_one[:, half:]), cross(attended))
    arrived, cot_other, early = barrier((arrived, cot_other, early))
    out_t = [w[:, q_width : 2 * q_width] for w in attn]
    middle, normed_two = row_call(
        middle_kernel, [jnp.float32, jnp.bfloat16], [*arrived, residual, gain_two[None, :]]
    )
    tokens_two, own_share = spread_around(normed_two, mlp_own[0])
    weights = (own_share, cross(own_share))
    tokens_two, weights, out_own = barrier((tokens_two, weights, out_t[0]))
    tokens_other = other_half(sum(tokens_two, []))
    *acts, dn_part, y_part = mlp(tokens_two, cot_blocks, *weights, ())
    out_blocks = spread(out_own)
    acts, tokens_other = barrier((acts, tokens_other))
    acts_other = [cross(act) for act in acts]
    grads_one = mlp_grads(
        chips, tokens_two, cot_blocks, tokens_other, cot_other, acts, acts_other
    )
    sums_one = scatter(grads_one)
    _, own_share = barrier((grads_one, mlp_own[1]))
    weights = (own_share, cross(own_share))
    *acts, y_part = mlp(tokens_two, cot_blocks, *weights, (dn_part, y_part))
    acts, dn_part = acts[:3], acts[3:]
    acts, dn_part, out_blocks = barrier((acts, dn_part, out_blocks))
    acts_other = [cross(act) for act in acts]
    arrived, acts = send_sum(dn_part, acts)
    out_other = [out_t[1]] + [cross(block) for block in out_blocks[1:]]
    grads_two = mlp_grads(
        chips, tokens_two, cot_blocks, tokens_other, cot_other, acts, acts_other
    )
    grads_two, arrived, out_other, y_part = barrier((grads_two, arrived, out_other, y_part))
    y_blocks = list(y_part.reshape((size, -1) + y_part.shape[1:]))
    y_early = [swap(y_blocks[step], step) for step in range(1, 3)]
    sums_two = scatter(grads_two)
    middle_grad, branch, gain_two_part, do_blocks = middle_back(
        arrived, middle, cotangent, gain_two[None, :], out_blocks, out_other
    )
    do_blocks = send_blocks(do_blocks)
    gain_two_other = cross(gain_two_part[half:])
    do_blocks, branch, gain_two_other, y_blocks, y_early = barrier(
        (do_blocks, branch, gain_two_other, y_blocks, y_early)
    )
    branch_blocks = spread(branch)
    qkv_grad = attend_back(
        me_array, query, log_total, key_pad, value_pad, cosine, sine, do_blocks, group
    )
    qkv_grad, sums_one = barrier((qkv_grad, sums_one))
    qkv_other = cross(qkv_grad)
    normed_part = input_grad(qkv_grad, *attn, columns, size)
    branch_blocks, normed_part = barrier((branch_blocks, normed_part))
    branch_other = other_half(branch_blocks)
    tokens_other, attended_other = early
    grads, gain_parts = attn_grads(
        chips,
        tokens_one,
        branch_blocks,
        (qkv_grad, attended),
        (tokens_other, branch_other, qkv_other, attended_other),
        attn_own,
        columns,
        gain_one[:half, None],
        (gain_two_part[:half] + gain_two_other)[:, None],
    )
    attn_sums = scatter(grads)
    arrived, _ = send_sum(normed_part, ready=(grads,))
    gain_sums = add_up(line_parts(gain_parts[:, :, :2]))
    unpacked = unpack_shares(sums_one, sums_two)
    arrived, y_blocks, unpacked, gain_sums = barrier((arrived, y_blocks, unpacked, gain_sums))
    grad_gate, grad_up, grad_down = unpacked
    y_late = [swap(y_blocks[step], step) for step in range(3, size)]
    (grad_in,) = row_call(
        functools.partial(input_back_kernel, chips=chips),
        [jnp.float32],
        [*arrived, residual, middle_grad, gain_one[None, :]],
        core,
    )
    grad_in, gain_sums = barrier((grad_in, gain_sums))
    gain_sums = own_part(gain_sums)
    y_late, grad_in, gain_sums = barrier((y_late, grad_in, gain_sums))
    (out,) = row_call(
        functools.partial(output_kernel, chips=chips),
        [jnp.bfloat16],
        [y_blocks[0], *y_early, *y_late, middle],
        core,
    )
    out, attn_sums = barrier((out, attn_sums))
    grad_query, grad_key, grad_value, grad_out = unpack(attn_sums, q_width, kv_width)
    return (
        out,
        grad_in,
        gain_sums[:, 0],
        grad_query,
        grad_key,
        grad_value,
        grad_out,
        gain_sums[:, 1],
        grad_gate,
        grad_up,
        grad_down,
    )


def solution(mesh):
    return jax.shard_map(
        per_device,
        mesh=mesh,
        in_specs=(
            P(("dp", "tensor"), None),
            P("dp"),
            P("dp", "tensor"),
            P("dp", "tensor"),
            P("dp", "tensor"),
            P("tensor", "dp"),
            P("dp"),
            P("dp", "tensor"),
            P("dp", "tensor"),
            P("tensor", "dp"),
            P("dp"),
            P(("dp", "tensor"), None),
        ),
        out_specs=(
            P(("dp", "tensor"), None),
            P(("dp", "tensor"), None),
            P(("dp", "tensor")),
            P("dp", "tensor"),
            P("dp", "tensor"),
            P("dp", "tensor"),
            P("tensor", "dp"),
            P(("dp", "tensor")),
            P("dp", "tensor"),
            P("dp", "tensor"),
            P("tensor", "dp"),
        ),
        check_vma=False,
    )
```

```python
import functools
import math

import jax
import jax.numpy as jnp
from jax import lax
from jax.experimental import pallas as pl
from jax.experimental.pallas import tpu as pltpu
from jax.sharding import PartitionSpec as P

HEAD_DIM = 64
PAIR = 2 * HEAD_DIM
SEQ_LEN = 1024


EPS = 1e-05
ROPE_BASE = 500000.0
SCALE = 1.0 / math.sqrt(HEAD_DIM)
PARAMS = pltpu.CompilerParams(vmem_limit_bytes=58 * 2**20)
ONCE = pl.Buffered(1)

barrier = lax.optimization_barrier


def hint(flops):
    return pl.CostEstimate(flops=flops, bytes_accessed=0, transcendentals=0)


def rms_scale(values):
    return lax.rsqrt(jnp.mean(values * values, axis=-1, keepdims=True) + EPS)


def norm_back(grad, values, scale, gain):
    inner = grad * gain
    cubed = scale * scale * scale
    result = scale * inner - values * cubed * jnp.mean(inner * values, axis=-1, keepdims=True)
    return (result, jnp.sum(grad * values * scale, axis=0))


def mm(left, right):
    return jnp.dot(left, right, preferred_element_type=jnp.float32)


def mm_nt(left, right):
    return lax.dot_general(left, right, (((1,), (1,)), ((), ())), preferred_element_type=jnp.float32)


def mm_tn(left, right):
    return lax.dot_general(left, right, (((0,), (0,)), ((), ())), preferred_element_type=jnp.float32)


def lane_index(rows):
    return lax.broadcasted_iota(jnp.int32, (rows, PAIR), 1)


def turn(pair, cosine, sine):
    lower = lane_index(pair.shape[0]) % HEAD_DIM < HEAD_DIM // 2
    other = jnp.where(
        lower, pltpu.roll(pair, PAIR - HEAD_DIM // 2, 1), pltpu.roll(pair, HEAD_DIM // 2, 1)
    )
    return pair * cosine + other * sine


def project_kernel(place_ref, *refs, size, q_width, kv_width):
    x_refs = refs[:size]
    gain_ref, qo_ref, qx_ref, kvo_ref, kvx_ref, cos_ref, sin_ref = refs[size:-4]
    n_ref, q_ref, k_ref, v_ref = refs[-4:]
    rows = q_ref.shape[0]
    half = qo_ref.shape[0]

    def one(x_ref):
        x = x_ref[...].astype(jnp.float32)
        normed = (x * rms_scale(x) * gain_ref[...]).astype(jnp.bfloat16)
        n_ref[...] = normed
        cosine, sine = cos_ref[...], sin_ref[...]
        own, other = normed[:, :half], normed[:, half:]
        lin = mm(own, qo_ref[...]) + mm(other, qx_ref[...])
        for low in range(0, q_width, PAIR):
            query = turn(lin[:, low : low + PAIR], cosine, sine).astype(jnp.bfloat16)
            q_ref[:, low : low + PAIR] = query * jnp.bfloat16(SCALE)
        lin = mm(own, kvo_ref[...]) + mm(other, kvx_ref[...])
        first = lane_index(rows) < HEAD_DIM
        for ref, start, rotate in ((k_ref, 0, True), (v_ref, kv_width, False)):
            for head in range(kv_width // HEAD_DIM):
                low = start + head * HEAD_DIM
                block = lin[:, low // PAIR * PAIR : low // PAIR * PAIR + PAIR]
                if rotate:
                    block = turn(block, cosine, sine)
                moved = pltpu.roll(block, HEAD_DIM, 1)
                if low % PAIR:
                    block, moved = moved, block
                ref[head, 0] = jnp.where(first, block, 0.0).astype(jnp.bfloat16)
                ref[head, 1] = jnp.where(first, 0.0, moved).astype(jnp.bfloat16)

    for step in range(size):
        pl.when(pl.program_id(0) == step)(functools.partial(one, x_refs[step]))


class Columns:
    def __init__(self, q_width, kv_width):
        self.q_width, self.kv_width = q_width, kv_width

    def spec(self, part, rows, place=lambda *_: 0):
        width, start = {"q": (self.q_width, 0), "kv": (2 * self.kv_width, self.q_width)}[part]
        index = start // width
        mode = {"pipeline_mode": ONCE} if place() == 0 else {}
        return pl.BlockSpec((rows, width), lambda *grid: (place(*grid), index), **mode)


def project(me, blocks, gain, own, other, cosine, sine, columns):
    size = len(blocks)
    rows, features = blocks[0].shape
    total = rows * size
    q_width, kv_width = columns.q_width, columns.kv_width
    key_heads = kv_width // HEAD_DIM
    width = q_width + 2 * kv_width
    half = features // 2
    fixed = lambda p, m: (0, 0)
    placed = lambda p, m: (jnp.bitwise_xor(p, m[0]), 0)
    padded = pl.BlockSpec(
        (key_heads, 2, rows, PAIR), lambda p, m: (0, 0, jnp.bitwise_xor(p, m[0]), 0)
    )
    spec = pltpu.PrefetchScalarGridSpec(
        num_scalar_prefetch=1,
        grid=(size,),
        in_specs=[pl.BlockSpec((rows, features), fixed, pipeline_mode=ONCE)] * size
        + [
            pl.BlockSpec((1, features), fixed),
            columns.spec("q", half),
            columns.spec("q", half),
            columns.spec("kv", half),
            columns.spec("kv", half),
            pl.BlockSpec((rows, PAIR), placed),
            pl.BlockSpec((rows, PAIR), placed),
        ],
        out_specs=[
            pl.BlockSpec((rows, features), lambda p, m: (p, 0)),
            pl.BlockSpec((rows, q_width), lambda p, m: (p, 0)),
            padded,
            padded,
        ],
    )
    padded_shape = jax.ShapeDtypeStruct((key_heads, 2, total, PAIR), jnp.bfloat16)
    return pl.pallas_call(
        functools.partial(project_kernel, size=size, q_width=q_width, kv_width=kv_width),
        grid_spec=spec,
        out_shape=[
            jax.ShapeDtypeStruct((total, features), jnp.bfloat16),
            jax.ShapeDtypeStruct((total, q_width), jnp.bfloat16),
            padded_shape,
            padded_shape,
        ],
        compiler_params=PARAMS,
        cost_estimate=hint(2 * total * features * width // 16),
    )(me, *blocks, gain, own, other, own, other, cosine, sine)


def attend_kernel(
    me_ref, q_ref, k_ref, v_ref, wo_ref, wx_ref, o_ref, l_ref, *refs, size, heads, group
):
    part_refs, vt_ref = refs[:size], refs[size]
    rows = q_ref.shape[0]
    half = wo_ref.shape[0]
    mine = jnp.bitwise_xor(me_ref[0], pl.program_id(0))
    key_place = lax.broadcasted_iota(jnp.int32, (rows, rows), 0)
    query_place = lax.broadcasted_iota(jnp.int32, (rows, rows), 1)

    @pl.when(pl.program_id(0) == 0)
    def _():
        for head in range(heads // group):
            for side in range(2):
                vt_ref[head, side] = v_ref[head, side].T

    def one(span):
        keys = span * rows
        for pair in range(heads // 2):
            head = 2 * pair // group
            lanes = slice(pair * PAIR, (pair + 1) * PAIR)
            query = q_ref[:, lanes]
            acc = None
            inverse = []
            for side in range(2):
                diag = mm_nt(k_ref[head, side, keys : keys + rows, :], query)
                diag = jnp.where(key_place <= query_place, diag, -1e9)
                top = jnp.max(diag, axis=0, keepdims=True)
                if span:
                    body = mm_nt(k_ref[head, side, :keys, :], query)
                    top = jnp.maximum(top, jnp.max(body, axis=0, keepdims=True))
                diag = jnp.exp(diag - top)
                total = jnp.sum(diag, axis=0, keepdims=True)
                part = mm(vt_ref[head, side, :, keys : keys + rows], diag.astype(jnp.bfloat16))
                if span:
                    body = jnp.exp(body - top)
                    total = total + jnp.sum(body, axis=0, keepdims=True)
                    part = part + mm(vt_ref[head, side, :, :keys], body.astype(jnp.bfloat16))
                acc = part if acc is None else acc + part
                inverse.append(jnp.broadcast_to(1.0 / total, (HEAD_DIM, rows)))
                l_ref[2 * pair + side : 2 * pair + side + 1, :] = top + jnp.log(total)
            acc = acc * jnp.concatenate(inverse, axis=0)
            o_ref[:, lanes] = acc.T.astype(jnp.bfloat16)

    for span in range(size):
        pl.when(mine == span)(functools.partial(one, span))

    def project_out(ref):
        ref[:, :half] = mm_nt(o_ref[...], wo_ref[...]).astype(jnp.bfloat16)
        ref[:, half:] = mm_nt(o_ref[...], wx_ref[...]).astype(jnp.bfloat16)

    for step in range(size):
        pl.when(pl.program_id(0) == step)(functools.partial(project_out, part_refs[step]))


def attend(me, query, key_pad, value_pad, own, other, size, group):
    total, width = query.shape
    features = 2 * own.shape[0]
    rows, heads = total // size, width // HEAD_DIM
    whole = pl.BlockSpec(key_pad.shape, lambda p, m: (0, 0, 0, 0), pipeline_mode=ONCE)
    spec = pltpu.PrefetchScalarGridSpec(
        num_scalar_prefetch=1,
        grid=(size,),
        in_specs=[pl.BlockSpec((rows, width), lambda p, m: (p, 0)), whole, whole]
        + [pl.BlockSpec(own.shape, lambda p, m: (0, 0), pipeline_mode=ONCE)] * 2,
        out_specs=[
            pl.BlockSpec((rows, width), lambda p, m: (p, 0)),
            pl.BlockSpec((heads, rows), lambda p, m: (0, p)),
        ]
        + [pl.BlockSpec((rows, features), lambda p, m: (0, 0))] * size,
        scratch_shapes=[pltpu.VMEM((heads // group, 2, PAIR, total), jnp.bfloat16)],
    )
    return pl.pallas_call(
        functools.partial(attend_kernel, size=size, heads=heads, group=group),
        grid_spec=spec,
        out_shape=[
            jax.ShapeDtypeStruct((total, width), jnp.bfloat16),
            jax.ShapeDtypeStruct((heads, total), jnp.float32),
        ]
        + [jax.ShapeDtypeStruct((rows, features), jnp.bfloat16)] * size,
        compiler_params=PARAMS,
        cost_estimate=hint(8 * heads * total * total * HEAD_DIM // 16),
    )(me, query, key_pad, value_pad, own, other)


def attend_back_kernel(
    me_ref, q_ref, l_ref, k_ref, v_ref, cos_ref, sin_ref, *refs, size, heads, group
):
    do_refs = refs[:size]
    out_ref, dk_ref, dv_ref, kt_ref, do_ref = refs[size:]
    rows = q_ref.shape[0]
    key_heads = heads // group
    step = pl.program_id(0)
    me = me_ref[0]
    mine = jnp.bitwise_xor(me, step)
    key_place = lax.broadcasted_iota(jnp.int32, (rows, rows), 0)
    query_place = lax.broadcasted_iota(jnp.int32, (rows, rows), 1)

    def rows_of(block):
        return pl.ds(pl.multiple_of(block * rows, rows), rows)

    @pl.when(step == 0)
    def _():
        dk_ref[...] = jnp.zeros_like(dk_ref)
        dv_ref[...] = jnp.zeros_like(dv_ref)
        for head in range(key_heads):
            for side in range(2):
                kt_ref[head, side] = k_ref[head, side].T

    def fetch(ref):
        do_ref[...] = ref[...]

    for block in range(size):
        pl.when(step == block)(functools.partial(fetch, do_refs[block]))

    def one(span):
        keys = span * rows
        parts = [(keys, keys + rows, True)] + ([(0, keys, False)] if span else [])
        cosine, sine = cos_ref[keys : keys + rows, :], sin_ref[keys : keys + rows, :]
        for pair in range(heads // 2):
            head = 2 * pair // group
            lanes = slice(pair * PAIR, (pair + 1) * PAIR)
            query, grad = q_ref[:, lanes], do_ref[:, lanes]
            acc = None
            for side in range(2):
                log_total = l_ref[2 * pair + side : 2 * pair + side + 1, :]
                inner = None
                kept = []
                for low, high, diagonal in parts:
                    probs = mm_nt(k_ref[head, side, low:high, :], query)
                    probs = jnp.exp(probs - log_total)
                    if diagonal:
                        probs = jnp.where(key_place <= query_place, probs, 0.0)
                    prob_grad = mm_nt(v_ref[head, side, low:high, :], grad)
                    dv_ref[head, side, low:high, :] += mm(probs.astype(jnp.bfloat16), grad)
                    term = jnp.sum(probs * prob_grad, axis=0, keepdims=True)
                    inner = term if inner is None else inner + term
                    kept.append((low, high, probs, prob_grad))
                for low, high, probs, prob_grad in kept:
                    score_grad = (probs * (prob_grad - inner)).astype(jnp.bfloat16)
                    dk_ref[head, side, low:high, :] += mm(score_grad, query)
                    part = mm(kt_ref[head, side, :, low:high], score_grad)
                    acc = part if acc is None else acc + part
            turned = turn(acc.T * SCALE, cosine, -sine)
            out_ref[rows_of(step), lanes] = turned.astype(jnp.bfloat16)

    for span in range(size):
        pl.when(mine == span)(functools.partial(one, span))

    @pl.when(step == size - 1)
    def _():
        first = lane_index(rows) < HEAD_DIM
        wanted = [(dk_ref, head, True) for head in range(key_heads)]
        wanted += [(dv_ref, head, False) for head in range(key_heads)]
        for span in range(size):
            place = slice(span * rows, (span + 1) * rows)
            cosine, sine = cos_ref[place, :], sin_ref[place, :]
            for block in range(len(wanted) // 2):
                halves, rotate = [], []
                for half in range(2):
                    ref, head, is_key = wanted[2 * block + half]
                    low, high = ref[head, 0, place, :], ref[head, 1, place, :]
                    if half:
                        halves.append(pltpu.roll(low, HEAD_DIM, 1) + high)
                    else:
                        halves.append(low + pltpu.roll(high, HEAD_DIM, 1))
                    rotate.append(is_key)
                value = jnp.where(first, halves[0], halves[1])
                if rotate[0] and rotate[1]:
                    value = turn(value, cosine, -sine)
                elif rotate[0]:
                    value = jnp.where(first, turn(value, cosine, -sine), value)
                start = heads * HEAD_DIM + block * PAIR
                target = rows_of(jnp.bitwise_xor(me, span))
                out_ref[target, start : start + PAIR] = value.astype(jnp.bfloat16)


def attend_back(
    me, query, log_total, key_pad, value_pad, cosine, sine, attended_grad, group
):
    total, width = query.shape
    size = len(attended_grad)
    rows, heads = total // size, width // HEAD_DIM
    key_heads = heads // group
    out_width = width + 2 * key_heads * HEAD_DIM
    whole = pl.BlockSpec(key_pad.shape, lambda p, m: (0, 0, 0, 0), pipeline_mode=ONCE)
    table = pl.BlockSpec((total, PAIR), lambda p, m: (0, 0), pipeline_mode=ONCE)
    spec = pltpu.PrefetchScalarGridSpec(
        num_scalar_prefetch=1,
        grid=(size,),
        in_specs=[
            pl.BlockSpec((rows, width), lambda p, m: (p, 0)),
            pl.BlockSpec((heads, rows), lambda p, m: (0, p)),
            whole,
            whole,
            table,
            table,
        ]
        + [pl.BlockSpec((rows, width), lambda p, m: (0, 0), pipeline_mode=ONCE)] * size,
        out_specs=pl.BlockSpec((total, out_width), lambda p, m: (0, 0)),
        scratch_shapes=[
            pltpu.VMEM(key_pad.shape, jnp.float32),
            pltpu.VMEM(key_pad.shape, jnp.float32),
            pltpu.VMEM((key_heads, 2, PAIR, total), jnp.bfloat16),
            pltpu.VMEM((rows, width), jnp.bfloat16),
        ],
    )
    return pl.pallas_call(
        functools.partial(attend_back_kernel, size=size, heads=heads, group=group),
        grid_spec=spec,
        out_shape=jax.ShapeDtypeStruct((total, out_width), jnp.bfloat16),
        compiler_params=PARAMS,
        cost_estimate=hint(20 * heads * total * total * HEAD_DIM),
    )(me, query, log_total, key_pad, value_pad, cosine, sine, *attended_grad)


def grouped(arrays, counts):
    arrays = iter(arrays)
    return [[next(arrays) for _ in range(count)] for count in counts]


def mlp_kernel(*refs, n_counts, e_counts, adds):
    size = len(n_counts)
    pieces = sum(n_counts) + sum(e_counts)
    n_refs = grouped(refs, n_counts)
    e_refs = grouped(refs[sum(n_counts) :], e_counts)
    gate_o, up_o, down_o, gate_x, up_x, down_x = refs[pieces : pieces + 6]
    y_ref, n_ref, e_ref = refs[-3:]
    dn_refs = refs[-3 - size if adds else -4 : -3]
    dg_ref, du_ref, h_ref = refs[-6 - size if adds else -7 :][:3]
    half = gate_o.shape[0]

    def fetch(step):
        for target, sources in ((n_ref, n_refs[step]), (e_ref, e_refs[step])):
            low = 0
            for source in sources:
                high = low + source.shape[0]
                target[low:high] = source[...]
                low = high

    for step in range(size):
        pl.when(pl.program_id(0) == step)(functools.partial(fetch, step))
    gate = mm(n_ref[:, :half], gate_o[...]) + mm(n_ref[:, half:], gate_x[...])
    up = mm(n_ref[:, :half], up_o[...]) + mm(n_ref[:, half:], up_x[...])
    grad = mm(e_ref[:, :half], down_o[...]) + mm(e_ref[:, half:], down_x[...])
    sigma = jax.nn.sigmoid(gate)
    silu = gate * sigma
    hidden = (silu * up).astype(jnp.bfloat16)
    gate_grad = (grad * up * sigma * (1.0 + gate * (1.0 - sigma))).astype(jnp.bfloat16)
    up_grad = (grad * silu).astype(jnp.bfloat16)
    dg_ref[...] = gate_grad
    du_ref[...] = up_grad
    h_ref[...] = hidden
    for part, gate_w, up_w, down_w in ((0, gate_o, up_o, down_o), (1, gate_x, up_x, down_x)):
        lanes = slice(part * half, (part + 1) * half)
        dn = mm_nt(gate_grad, gate_w[...]) + mm_nt(up_grad, up_w[...])
        y = mm_nt(hidden, down_w[...])
        if adds:
            dn = dn + refs[pieces + 6][:, lanes].astype(jnp.float32)
            y = y + refs[pieces + 7][:, lanes].astype(jnp.float32)
        y_ref[:, lanes] = y.astype(jnp.bfloat16)
        dn = dn.astype(jnp.bfloat16)

        def store(ref):
            ref[:, lanes] = dn

        if adds:
            for step in range(size):
                pl.when(pl.program_id(0) == step)(functools.partial(store, dn_refs[step]))
        else:
            store(dn_refs[0])


def mlp(tokens, cot, own, other, earlier):
    size = len(tokens)
    rows, features = tokens[0][0].shape
    half, units = own.shape[0], own.shape[1] // 3
    total = rows * size
    fixed = lambda p: (0, 0)
    moving = lambda p: (p, 0)
    wide = pl.BlockSpec((rows, features), moving)
    sums = jax.ShapeDtypeStruct((total, features), jnp.bfloat16)
    dn_specs, dn_shapes = [wide], [sums]
    if earlier:
        dn_specs = [pl.BlockSpec((rows, features), fixed)] * size
        dn_shapes = [jax.ShapeDtypeStruct((rows, features), jnp.bfloat16)] * size
    pieces = sum(tokens, []) + sum(cot, [])
    thirds = [
        pl.BlockSpec((half, units), lambda p, t=t: (0, t), pipeline_mode=ONCE) for t in range(3)
    ]
    return pl.pallas_call(
        functools.partial(
            mlp_kernel,
            n_counts=[len(group) for group in tokens],
            e_counts=[len(group) for group in cot],
            adds=bool(earlier),
        ),
        grid=(size,),
        in_specs=[pl.BlockSpec(piece.shape, fixed, pipeline_mode=ONCE) for piece in pieces]
        + thirds * 2
        + [wide] * len(earlier),
        out_specs=[pl.BlockSpec((rows, units), moving)] * 3 + dn_specs + [wide],
        out_shape=[jax.ShapeDtypeStruct((total, units), jnp.bfloat16)] * 3 + dn_shapes + [sums],
        scratch_shapes=[pltpu.VMEM((rows, features), jnp.bfloat16)] * 2,
        compiler_params=PARAMS,
        cost_estimate=hint(12 * total * features * units),
    )(*pieces, own, own, own, other, other, other, *earlier)


def add_refs(refs):
    total = refs[0][...].astype(jnp.float32)
    for ref in refs[1:]:
        total = total + ref[...].astype(jnp.float32)
    return total


def store_by_device(out_ref, values, core, chips):
    width = values.shape[1] // (2 * chips)
    for chip in range(chips):
        own = values[:, chip * width : (chip + 1) * width]
        other = values[:, (chips + chip) * width : (chips + chip + 1) * width]
        low = 2 * chip * width
        out_ref[:, low : low + width] = jnp.where(core == 0, own, other)
        out_ref[:, low + width : low + 2 * width] = jnp.where(core == 0, other, own)


def middle_kernel(*refs):
    x_ref, gain_ref, middle_ref, normed_ref = refs[-4:]
    values = x_ref[...].astype(jnp.float32) + add_refs(refs[:-4])
    middle_ref[...] = values
    normed_ref[...] = (values * rms_scale(values) * gain_ref[...]).astype(jnp.bfloat16)


def input_back_kernel(core_ref, *refs, chips):
    x_ref, before_ref, gain_ref, out_ref = refs[-4:]
    values = x_ref[...].astype(jnp.float32)
    inner = add_refs(refs[:-4]) * gain_ref[...]
    scale = rms_scale(values)
    mean = jnp.mean(inner * values, axis=-1, keepdims=True)
    result = before_ref[...] + scale * inner - values * (scale * scale * scale) * mean
    store_by_device(out_ref, result, core_ref[0], chips)


def output_kernel(core_ref, *refs, chips):
    middle_ref, out_ref = refs[-2:]
    values = middle_ref[...] + add_refs(refs[:-2])
    store_by_device(out_ref, values.astype(jnp.bfloat16), core_ref[0], chips)


def row_call(body, dtypes, arrays, core=None):
    rows, features = arrays[0].shape
    steps = 2
    wide = pl.BlockSpec((rows // steps, features), lambda i, *_: (i, 0))
    row = pl.BlockSpec((1, features), lambda i, *_: (0, 0))
    scalars = [] if core is None else [jnp.full((1,), core, jnp.int32)]
    return pl.pallas_call(
        body,
        grid_spec=pltpu.PrefetchScalarGridSpec(
            num_scalar_prefetch=len(scalars),
            grid=(steps,),
            in_specs=[row if array.shape[0] == 1 else wide for array in arrays],
            out_specs=[wide] * len(dtypes),
        ),
        out_shape=[jax.ShapeDtypeStruct((rows, features), dtype) for dtype in dtypes],
        compiler_params=PARAMS,
        cost_estimate=hint(0),
    )(*scalars, *arrays)


def unpack_kernel(sum_ref, q_ref, k_ref, v_ref, out_ref):
    q_width, kv_width = q_ref.shape[1], k_ref.shape[1]
    values = sum_ref[...].astype(jnp.float32)
    q_ref[...] = values[:, :q_width]
    kv = values[:, q_width : q_width + 2 * kv_width]
    k_ref[...] = kv[:, :kv_width]
    v_ref[...] = kv[:, kv_width:]
    out_ref[...] = values[:, q_width + 2 * kv_width :].T


def unpack(sums, q_width, kv_width):
    rows = sums.shape[0]
    widths = [(rows, q_width), (rows, kv_width), (rows, kv_width), (q_width, rows)]
    return pl.pallas_call(
        unpack_kernel,
        out_shape=[jax.ShapeDtypeStruct(shape, jnp.float32) for shape in widths],
        compiler_params=PARAMS,
        cost_estimate=hint(0),
    )(sums)


def unpack_shares_kernel(one_ref, two_ref, gate_ref, up_ref, down_ref):
    units = one_ref.shape[1] // 3
    for part, ref in enumerate((one_ref, two_ref)):
        cut = slice(part * units, (part + 1) * units)
        gate_ref[:, cut] = ref[:, :units].astype(jnp.float32)
        up_ref[:, cut] = ref[:, units : 2 * units].astype(jnp.float32)
        down_ref[cut, :] = ref[:, 2 * units :].astype(jnp.float32).T


def unpack_shares(one, two):
    rows, width = one.shape
    units = 2 * width // 3
    shapes = [(rows, units), (rows, units), (units, rows)]
    return pl.pallas_call(
        unpack_shares_kernel,
        out_shape=[jax.ShapeDtypeStruct(shape, jnp.float32) for shape in shapes],
        compiler_params=PARAMS,
        cost_estimate=hint(0),
    )(one, two)


def middle_back_kernel(*refs, parts, size):
    n_refs, refs = refs[:parts], refs[parts:]
    x_ref, e_ref, gain_ref, refs = refs[0], refs[1], refs[2], refs[3:]
    own_refs, other_refs, refs = refs[:size], refs[size : 2 * size], refs[2 * size :]
    grad_ref, branch_ref, part_ref, do_refs = refs[0], refs[1], refs[2], refs[3:]
    half = own_refs[0].shape[0]
    grad = add_refs(n_refs)
    values = x_ref[...]
    scale = rms_scale(values)
    result, part = norm_back(grad, values, scale, gain_ref[...])

    @pl.when(pl.program_id(0) == 0)
    def _():
        part_ref[...] = jnp.zeros_like(part_ref)

    part_ref[...] += part[None, :]
    result = result + e_ref[...].astype(jnp.float32)
    grad_ref[...] = result
    branch = result.astype(jnp.bfloat16)
    branch_ref[...] = branch
    for own, other, do_ref in zip(own_refs, other_refs, do_refs):
        do = mm(branch[:, :half], own[...]) + mm(branch[:, half:], other[...])
        do_ref[...] = do.astype(jnp.bfloat16)


def middle_back(arrived, middle, cot, gain, own, other):
    parts, size = len(arrived), len(own)
    rows, features = middle.shape
    width = own[0].shape[1]
    steps = 2
    wide = pl.BlockSpec((rows // steps, features), lambda i: (i, 0))
    narrow = pl.BlockSpec((rows // steps, width), lambda i: (i, 0))
    row = pl.BlockSpec((1, features), lambda i: (0, 0))
    weight = pl.BlockSpec((features // 2, width), lambda i: (0, 0), pipeline_mode=ONCE)
    grad, branch, part, *do = pl.pallas_call(
        functools.partial(middle_back_kernel, parts=parts, size=size),
        grid=(steps,),
        in_specs=[wide] * parts + [wide, wide, row] + [weight] * (2 * size),
        out_specs=[wide, wide, row] + [narrow] * size,
        out_shape=[
            jax.ShapeDtypeStruct((rows, features), jnp.float32),
            jax.ShapeDtypeStruct((rows, features), jnp.bfloat16),
            jax.ShapeDtypeStruct((1, features), jnp.float32),
        ]
        + [jax.ShapeDtypeStruct((rows, width), jnp.bfloat16)] * size,
        compiler_params=PARAMS,
        cost_estimate=hint(2 * rows * features * width * size),
    )(*arrived, middle, cot, gain, *own, *other)
    return grad, branch, part[0], do


def column_grad(blocks, other, mine, theirs):
    total = mm_tn(other[...], theirs[...])
    low = 0
    for block in blocks:
        high = low + block.shape[0]
        total = total + mm_tn(block[...], mine[low:high, :])
        low = high
    return total


def grad_kernel(*refs, n_count, e_count):
    n_refs, refs = refs[:n_count], refs[n_count:]
    e_refs, refs = refs[:e_count], refs[e_count:]
    n_other, e_other = refs[:2]
    acts, out_ref = refs[2:-1], refs[-1]
    units = acts[0].shape[1]
    for third in range(3):
        blocks, other = (e_refs, e_other) if third == 2 else (n_refs, n_other)
        grad = column_grad(blocks, other, acts[third], acts[third + 3])
        out_ref[0, :, third * units : (third + 1) * units] = grad.astype(jnp.bfloat16)


def mlp_grads(chips, tokens, cot, tokens_other, cot_other, mine, theirs):
    tokens, cot = sum(tokens, []), sum(cot, [])
    features = tokens[0].shape[1]
    total, units = mine[0].shape
    depth = features // (2 * chips)
    long = pl.BlockSpec((total, depth), lambda b: (0, b))
    fixed = pl.BlockSpec((total, units), lambda b: (0, 0), pipeline_mode=ONCE)
    return pl.pallas_call(
        functools.partial(grad_kernel, n_count=len(tokens), e_count=len(cot)),
        grid=(chips,),
        in_specs=[pl.BlockSpec((p.shape[0], depth), lambda b: (0, b)) for p in tokens + cot]
        + [long, long]
        + [fixed] * 6,
        out_specs=pl.BlockSpec((1, depth, 3 * units), lambda b: (b, 0, 0)),
        out_shape=jax.ShapeDtypeStruct((chips, depth, 3 * units), jnp.bfloat16),
        compiler_params=PARAMS,
        cost_estimate=hint(6 * total * features * units),
    )(*tokens, *cot, tokens_other, cot_other, *mine, *theirs)


def attn_grad_kernel(*refs, size):
    e_refs = refs[2 : 2 + size]
    n_ref, n_other = refs[:2]
    e_other, d_ref, d_other, o_ref, o_other, q_ref, kv_ref, g1_ref, g2_ref = refs[2 + size : -2]
    out_ref, gain_ref = refs[-2:]
    width, out_width = d_ref.shape[1], o_ref.shape[1]
    grad = column_grad([n_ref], n_other, d_ref, d_other)
    out_ref[0, :, :width] = grad.astype(jnp.bfloat16)
    out_grad = column_grad(e_refs, e_other, o_ref, o_other)
    out_ref[0, :, width : width + out_width] = out_grad.astype(jnp.bfloat16)
    cut = q_ref.shape[1]
    first = jnp.sum(grad[:, :cut] * q_ref[...].astype(jnp.float32), axis=1, keepdims=True)
    first += jnp.sum(grad[:, cut:] * kv_ref[...].astype(jnp.float32), axis=1, keepdims=True)
    first = first / g1_ref[...]
    lane = lane_index(grad.shape[0])
    gain_ref[0] = jnp.where(lane == 0, first, g2_ref[...])


def attn_grads(
    chips, tokens, branch, mine, theirs, weights, columns, gain_one, gain_two_part
):
    size = len(branch)
    qkv_grad, attended = mine
    tokens_other, branch_other, qkv_other, attended_other = theirs
    total, features = tokens.shape
    rows = total // size
    width, out_width = qkv_grad.shape[1], attended.shape[1]
    depth = features // (2 * chips)
    column = lambda b: (0, b)
    row = lambda b: (b, 0)
    long = pl.BlockSpec((total, depth), column)
    fixed = lambda array: pl.BlockSpec(array.shape, lambda b: (0, 0), pipeline_mode=ONCE)
    place = lambda b: (b, 0, 0)
    return pl.pallas_call(
        functools.partial(attn_grad_kernel, size=size),
        grid=(chips,),
        in_specs=[long, long]
        + [pl.BlockSpec((rows, depth), column)] * size
        + [long]
        + [fixed(qkv_grad)] * 2
        + [fixed(attended)] * 2
        + [
            columns.spec("q", depth, lambda b=None: b),
            columns.spec("kv", depth, lambda b=None: b),
            pl.BlockSpec((depth, 1), row),
            pl.BlockSpec((depth, 1), row),
        ],
        out_specs=[
            pl.BlockSpec((1, depth, width + out_width), place),
            pl.BlockSpec((1, depth, PAIR), place),
        ],
        out_shape=[
            jax.ShapeDtypeStruct((chips, depth, width + out_width), jnp.bfloat16),
            jax.ShapeDtypeStruct((chips, depth, PAIR), jnp.float32),
        ],
        compiler_params=PARAMS,
        cost_estimate=hint(2 * total * features * (width + out_width)),
    )(
        tokens,
        tokens_other,
        *branch,
        branch_other,
        qkv_grad,
        qkv_other,
        attended,
        attended_other,
        weights,
        weights,
        gain_one,
        gain_two_part,
    )


def input_grad_kernel(d_ref, qo_ref, qx_ref, kvo_ref, kvx_ref, *out_refs):
    half, cut = qo_ref.shape

    def one(ref):
        query, rest = d_ref[:, :cut], d_ref[:, cut:]
        own = mm_nt(query, qo_ref[...]) + mm_nt(rest, kvo_ref[...])
        other = mm_nt(query, qx_ref[...]) + mm_nt(rest, kvx_ref[...])
        ref[:, :half] = own.astype(jnp.bfloat16)
        ref[:, half:] = other.astype(jnp.bfloat16)

    for step, ref in enumerate(out_refs):
        pl.when(pl.program_id(0) == step)(functools.partial(one, ref))


def input_grad(qkv_grad, own, other, columns, size):
    total, width = qkv_grad.shape
    features = 2 * own.shape[0]
    rows = total // size
    fixed = lambda i: (0, 0)
    weights = [columns.spec(part, own.shape[0]) for part in ("q", "q", "kv", "kv")]
    return pl.pallas_call(
        input_grad_kernel,
        grid=(size,),
        in_specs=[pl.BlockSpec((rows, width), lambda i: (i, 0))] + weights,
        out_specs=[pl.BlockSpec((rows, features), fixed)] * size,
        out_shape=[jax.ShapeDtypeStruct((rows, features), jnp.bfloat16)] * size,
        compiler_params=PARAMS,
        cost_estimate=hint(2 * total * features * width),
    )(qkv_grad, own, other, own, other)


def swap(values, step):
    size = lax.axis_size("tensor")
    return lax.ppermute(values, "tensor", [(i, i ^ step) for i in range(size)])


def spread(values):
    return [values] + [swap(values, step) for step in range(1, lax.axis_size("tensor"))]


def send_blocks(blocks):
    return [blocks[0]] + [swap(block, step + 1) for step, block in enumerate(blocks[1:])]


def spread_around(values, held):
    if lax.axis_size("tensor") != 4:
        blocks = spread(values)
        first, held = barrier((blocks[1], held))
        return [[blocks[0]], [first]] + [[block] for block in blocks[2:]], held
    half = values.shape[0] // 2
    top, bottom = values[:half], values[half:]
    x_bottom, y_top = swap(bottom, 1), swap(top, 2)
    x_bottom, y_top, top, bottom, held = barrier((x_bottom, y_top, top, bottom, held))
    far = [swap(y_top, 1), swap(x_bottom, 2)]
    x_top, y_bottom = swap(top, 1), swap(bottom, 2)
    return [[values], [x_top, x_bottom], [y_top, y_bottom], far], held


def merge_kernel(x_ref, y_ref, top_ref, bottom_ref, x_out, y_out):
    half = top_ref.shape[0]
    x_out[:half] = x_ref[:half]
    x_out[half:] = add_refs([x_ref.at[half:], bottom_ref]).astype(jnp.bfloat16)
    y_out[:half] = add_refs([y_ref.at[:half], top_ref]).astype(jnp.bfloat16)
    y_out[half:] = y_ref[half:]


def send_sum(blocks, held=()):
    if len(blocks) != 4:
        return send_blocks(blocks), held
    own, near_x, near_y, far = blocks
    half = far.shape[0] // 2
    top, bottom = swap(far[:half], 1), swap(far[half:], 2)
    near_x, near_y = pl.pallas_call(
        merge_kernel,
        out_shape=[jax.ShapeDtypeStruct(near_x.shape, near_x.dtype)] * 2,
        compiler_params=PARAMS,
        cost_estimate=hint(0),
    )(near_x, near_y, top, bottom)
    near_x, near_y, held = barrier((near_x, near_y, held))
    return [own, swap(near_x, 1), swap(near_y, 2)], held


def add_up(blocks):
    total = blocks[0].astype(jnp.float32)
    for block in blocks[1:]:
        total = total + block.astype(jnp.float32)
    return total


def cross(values):
    count = lax.axis_size("dp")
    return lax.ppermute(values, "dp", [(i, i ^ 1) for i in range(count)])


def tables(positions):
    freqs = ROPE_BASE ** (-jnp.arange(0, HEAD_DIM, 2).astype(jnp.float32) / HEAD_DIM)
    angles = positions.astype(jnp.float32)[:, None] * freqs[None, :]
    cosine, sine = jnp.cos(angles), jnp.sin(angles)
    return (
        jnp.concatenate([cosine] * 4, axis=1),
        jnp.concatenate([-sine, sine, -sine, sine], axis=1),
    )


def chip_lines():
    count = lax.axis_size("dp")
    return [list(range(core, count, 2)) for core in range(2)]


def gather(values):
    return lax.all_gather(values, "dp", axis=0, tiled=True, axis_index_groups=chip_lines())


def scatter(values):
    total = lax.psum_scatter(
        values, "dp", scatter_dimension=0, tiled=True, axis_index_groups=chip_lines()
    )
    return total[0]


def along(values, step):
    count = lax.axis_size("dp")
    return lax.ppermute(values, "dp", [(i, (i + 2 * step) % count) for i in range(count)])


def line_order(blocks):
    chips = len(blocks)
    chip = lax.axis_index("dp") // 2
    placed = jnp.zeros((chips,) + blocks[0].shape, blocks[0].dtype)
    for step, block in enumerate(blocks):
        placed = lax.dynamic_update_index_in_dim(placed, block, (chip - step) % chips, 0)
    return placed.reshape((-1,) + blocks[0].shape[1:])


def line_parts(parts):
    chips = lax.axis_size("dp") // 2
    chip = lax.axis_index("dp") // 2
    blocks = [lax.dynamic_index_in_dim(parts, chip, 0, keepdims=False)]
    for step in range(1, chips):
        sent = lax.dynamic_index_in_dim(parts, (chip + step) % chips, 0, keepdims=False)
        blocks.append(along(sent, step))
    return blocks


def own_part(values):
    size = lax.axis_size("tensor")
    me = lax.axis_index("tensor")
    blocks = values.reshape((size, -1) + values.shape[1:])
    own = lax.dynamic_index_in_dim(blocks, me, 0, keepdims=False)
    for step in range(1, size):
        sent = lax.dynamic_index_in_dim(blocks, me ^ step, 0, keepdims=False)
        own = own + swap(sent, step)
    return own


def stack_kernel(*refs):
    low = 0
    for ref in refs[:-1]:
        high = low + ref.shape[0]
        refs[-1][low:high, :] = ref[...]
        low = high


def other_half(blocks):
    features = blocks[0].shape[1]
    shape = (sum(block.shape[0] for block in blocks), features // 2)
    halves = pl.pallas_call(
        stack_kernel,
        grid=(1,),
        in_specs=[pl.BlockSpec((b.shape[0], features // 2), lambda i: (0, 1)) for b in blocks],
        out_specs=pl.BlockSpec(shape, lambda i: (0, 0)),
        out_shape=jax.ShapeDtypeStruct(shape, blocks[0].dtype),
        compiler_params=PARAMS,
        cost_estimate=hint(0),
    )(*blocks)
    return cross(halves)


def feature_blocks(values):
    width = values.shape[-1] // lax.axis_size("dp")
    return [values[..., low : low + width] for low in range(0, values.shape[-1], width)]


def by_core(values, core):
    blocks = feature_blocks(values)
    pairs = list(zip(blocks[0::2], blocks[1::2]))
    own = [jnp.where(core == 0, even, odd) for even, odd in pairs]
    other = [jnp.where(core == 0, odd, even) for even, odd in pairs]
    return jnp.concatenate(own + other, axis=-1)


def per_device(
    hidden_in,
    gain_attn,
    w_query,
    w_key,
    w_value,
    w_out,
    gain_mlp,
    w_gate,
    w_up,
    w_down,
    positions,
    cotangent,
):
    size = lax.axis_size("tensor")
    chips = lax.axis_size("dp") // 2
    me = lax.axis_index("tensor")
    me_array = jnp.full((1,), me, jnp.int32)
    core = lax.axis_index("dp") % 2
    q_width, kv_width = w_query.shape[1], w_key.shape[1]
    group = q_width // kv_width
    units = w_down.shape[0] // 2
    half = hidden_in.shape[1] // 2

    columns = Columns(q_width, kv_width)
    qkv_shard = jnp.concatenate([w_query, w_key, w_value], axis=1)
    out_shard = w_out.T
    qkv_shard, out_shard, hidden_in, gain_attn = barrier(
        (qkv_shard, out_shard, hidden_in, gain_attn)
    )
    qkv_own = gather(qkv_shard)
    residual = by_core(hidden_in, core)
    early_in = [swap(residual, step) for step in range(1, 3)]
    out_parts = [out_shard] + [along(out_shard, step) for step in range(1, chips)]
    early_in, residual = barrier((early_in, residual))
    blocks_in = [residual] + early_in + [swap(residual, step) for step in range(3, size)]
    gains = lax.all_gather(jnp.stack([gain_attn, gain_mlp]), "dp", axis=1, tiled=True)
    gains = by_core(gains, core).astype(jnp.float32)
    cosine, sine = tables(positions)
    cotangent = by_core(cotangent, core)
    down_t = w_down.T
    shares = []
    for part in range(2):
        cut = slice(part * units, (part + 1) * units)
        shares.append(jnp.concatenate([w_gate[:, cut], w_up[:, cut], down_t[:, cut]], axis=1))
    shares, qkv_own, out_parts, blocks_in, cosine, sine, gains, cotangent = barrier(
        (shares, qkv_own, out_parts, blocks_in, cosine, sine, gains, cotangent)
    )
    mlp_own = [gather(share) for share in shares]
    cot_blocks = spread(cotangent)
    gain_one, gain_two = gains[0], gains[1]
    qkv = (qkv_own, cross(qkv_own))
    out_own = line_order(out_parts)
    out_t = (out_own, cross(out_own))

    tokens_one, query, key_pad, value_pad = project(
        me_array, blocks_in, gain_one[None, :], *qkv, cosine, sine, columns
    )
    attended, log_total, *parts = attend(
        me_array, query, key_pad, value_pad, *out_t, size, group
    )
    parts, cot_blocks, tokens_one, attended = barrier((parts, cot_blocks, tokens_one, attended))
    arrived, _ = send_sum(parts)
    cot_other = other_half(cot_blocks)
    cot_blocks = [[block] for block in cot_blocks]
    early = (cross(tokens_one[:, half:]), cross(attended))
    arrived, cot_other, early = barrier((arrived, cot_other, early))
    middle, normed_two = row_call(
        middle_kernel, [jnp.float32, jnp.bfloat16], [*arrived, residual, gain_two[None, :]]
    )
    tokens_two, own_share = spread_around(normed_two, mlp_own[0])
    weights = (own_share, cross(own_share))
    tokens_two, weights, out_own = barrier((tokens_two, weights, out_t[0]))
    tokens_other = other_half(sum(tokens_two, []))
    *acts, dn_part, y_part = mlp(tokens_two, cot_blocks, *weights, ())
    out_blocks = spread(out_own)
    acts, tokens_other = barrier((acts, tokens_other))
    acts_other = [cross(act) for act in acts]
    grads_one = mlp_grads(
        chips, tokens_two, cot_blocks, tokens_other, cot_other, acts, acts_other
    )
    grads_one, own_share = barrier((grads_one, mlp_own[1]))
    sums_one = scatter(grads_one)
    weights = (own_share, cross(own_share))
    *acts, y_part = mlp(tokens_two, cot_blocks, *weights, (dn_part, y_part))
    acts, dn_part = acts[:3], acts[3:]
    acts, dn_part, out_blocks = barrier((acts, dn_part, out_blocks))
    acts_other = [cross(act) for act in acts]
    arrived, acts = send_sum(dn_part, acts)
    out_other = [out_t[1]] + [cross(block) for block in out_blocks[1:]]
    grads_two = mlp_grads(
        chips, tokens_two, cot_blocks, tokens_other, cot_other, acts, acts_other
    )
    grads_two, arrived, out_other, y_part = barrier((grads_two, arrived, out_other, y_part))
    y_blocks = list(y_part.reshape((size, -1) + y_part.shape[1:]))
    y_early = [swap(y_blocks[step], step) for step in range(1, 3)]
    sums_two = scatter(grads_two)
    middle_grad, branch, gain_two_part, do_blocks = middle_back(
        arrived, middle, cotangent, gain_two[None, :], out_blocks, out_other
    )
    do_blocks = send_blocks(do_blocks)
    gain_two_other = cross(gain_two_part[half:])
    do_blocks, branch, gain_two_other, y_blocks, y_early = barrier(
        (do_blocks, branch, gain_two_other, y_blocks, y_early)
    )
    branch_blocks = spread(branch)
    qkv_grad = attend_back(
        me_array, query, log_total, key_pad, value_pad, cosine, sine, do_blocks, group
    )
    qkv_grad, sums_one = barrier((qkv_grad, sums_one))
    qkv_other = cross(qkv_grad)
    normed_part = input_grad(qkv_grad, *qkv, columns, size)
    branch_blocks, normed_part = barrier((branch_blocks, normed_part))
    branch_other = other_half(branch_blocks)
    tokens_other, attended_other = early
    grads, gain_parts = attn_grads(
        chips,
        tokens_one,
        branch_blocks,
        (qkv_grad, attended),
        (tokens_other, branch_other, qkv_other, attended_other),
        qkv_own,
        columns,
        gain_one[:half, None],
        (gain_two_part[:half] + gain_two_other)[:, None],
    )
    arrived, (grads, sums_two) = send_sum(normed_part, (grads, sums_two))
    attn_sums = scatter(grads)
    gain_sums = add_up(line_parts(gain_parts[:, :, :2]))
    unpacked = unpack_shares(sums_one, sums_two)
    arrived, y_blocks, unpacked, gain_sums = barrier((arrived, y_blocks, unpacked, gain_sums))
    grad_gate, grad_up, grad_down = unpacked
    y_late = [swap(y_blocks[step], step) for step in range(3, size)]
    (grad_in,) = row_call(
        functools.partial(input_back_kernel, chips=chips),
        [jnp.float32],
        [*arrived, residual, middle_grad, gain_one[None, :]],
        core,
    )
    grad_in, gain_sums = barrier((grad_in, gain_sums))
    gain_sums = own_part(gain_sums)
    y_late, grad_in, gain_sums = barrier((y_late, grad_in, gain_sums))
    (out,) = row_call(
        functools.partial(output_kernel, chips=chips),
        [jnp.bfloat16],
        [y_blocks[0], *y_early, *y_late, middle],
        core,
    )
    out, attn_sums = barrier((out, attn_sums))
    grad_query, grad_key, grad_value, grad_out = unpack(attn_sums, q_width, kv_width)
    return (
        out,
        grad_in,
        gain_sums[:, 0],
        grad_query,
        grad_key,
        grad_value,
        grad_out,
        gain_sums[:, 1],
        grad_gate,
        grad_up,
        grad_down,
    )


def solution(mesh):
    return jax.shard_map(
        per_device,
        mesh=mesh,
        in_specs=(
            P(("dp", "tensor"), None),
            P("dp"),
            P("dp", "tensor"),
            P("dp", "tensor"),
            P("dp", "tensor"),
            P("tensor", "dp"),
            P("dp"),
            P("dp", "tensor"),
            P("dp", "tensor"),
            P("tensor", "dp"),
            P("dp"),
            P(("dp", "tensor"), None),
        ),
        out_specs=(
            P(("dp", "tensor"), None),
            P(("dp", "tensor"), None),
            P(("dp", "tensor")),
            P("dp", "tensor"),
            P("dp", "tensor"),
            P("dp", "tensor"),
            P("tensor", "dp"),
            P(("dp", "tensor")),
            P("dp", "tensor"),
            P("dp", "tensor"),
            P("tensor", "dp"),
        ),
        check_vma=False,
    )
```

```python
import functools
import math

import jax
import jax.numpy as jnp
from jax import lax
from jax.experimental import pallas as pl
from jax.experimental.pallas import tpu as pltpu
from jax.sharding import PartitionSpec as P

HEAD_DIM = 64
PAIR = 2 * HEAD_DIM
SEQ_LEN = 1024


EPS = 1e-05
ROPE_BASE = 500000.0
SCALE = 1.0 / math.sqrt(HEAD_DIM)
PARAMS = pltpu.CompilerParams(vmem_limit_bytes=58 * 2**20)
ONCE = pl.Buffered(1)

barrier = lax.optimization_barrier


def hint(flops):
    return pl.CostEstimate(flops=flops, bytes_accessed=0, transcendentals=0)


def rms_scale(values):
    return lax.rsqrt(jnp.mean(values * values, axis=-1, keepdims=True) + EPS)


def norm_back(grad, values, scale, gain):
    inner = grad * gain
    cubed = scale * scale * scale
    result = scale * inner - values * cubed * jnp.mean(inner * values, axis=-1, keepdims=True)
    return (result, jnp.sum(grad * values * scale, axis=0))


def mm(left, right):
    return jnp.dot(left, right, preferred_element_type=jnp.float32)


def mm_nt(left, right):
    return lax.dot_general(left, right, (((1,), (1,)), ((), ())), preferred_element_type=jnp.float32)


def mm_tn(left, right):
    return lax.dot_general(left, right, (((0,), (0,)), ((), ())), preferred_element_type=jnp.float32)


def partner_rows(size, rows):
    return [rows] * 3 + [rows // 2] * 2 if size == 4 else [rows] * size


def store_partner(refs, step, lanes, value):
    if len(refs) == 5 and step == 3:
        half = refs[3].shape[0]
        refs[3][:, lanes] = value[:half]
        refs[4][:, lanes] = value[half:]
    else:
        refs[step][:, lanes] = value


def lane_index(rows):
    return lax.broadcasted_iota(jnp.int32, (rows, PAIR), 1)


def turn(pair, cosine, sine):
    lower = lane_index(pair.shape[0]) % HEAD_DIM < HEAD_DIM // 2
    other = jnp.where(
        lower, pltpu.roll(pair, PAIR - HEAD_DIM // 2, 1), pltpu.roll(pair, HEAD_DIM // 2, 1)
    )
    return pair * cosine + other * sine


def project_kernel(place_ref, *refs, size, q_width, kv_width):
    x_refs = refs[:size]
    gain_ref, qo_ref, qx_ref, kvo_ref, kvx_ref, cos_ref, sin_ref = refs[size:-4]
    n_ref, q_ref, k_ref, v_ref = refs[-4:]
    rows = q_ref.shape[0]
    half = qo_ref.shape[0]

    def one(x_ref):
        x = x_ref[...].astype(jnp.float32)
        normed = (x * rms_scale(x) * gain_ref[...]).astype(jnp.bfloat16)
        n_ref[...] = normed
        cosine, sine = cos_ref[...], sin_ref[...]
        own, other = normed[:, :half], normed[:, half:]
        lin = mm(own, qo_ref[...]) + mm(other, qx_ref[...])
        for low in range(0, q_width, PAIR):
            query = turn(lin[:, low : low + PAIR], cosine, sine).astype(jnp.bfloat16)
            q_ref[:, low : low + PAIR] = query * jnp.bfloat16(SCALE)
        lin = mm(own, kvo_ref[...]) + mm(other, kvx_ref[...])
        first = lane_index(rows) < HEAD_DIM
        for ref, start, rotate in ((k_ref, 0, True), (v_ref, kv_width, False)):
            for head in range(kv_width // HEAD_DIM):
                low = start + head * HEAD_DIM
                block = lin[:, low // PAIR * PAIR : low // PAIR * PAIR + PAIR]
                if rotate:
                    block = turn(block, cosine, sine)
                moved = pltpu.roll(block, HEAD_DIM, 1)
                if low % PAIR:
                    block, moved = moved, block
                ref[head, 0] = jnp.where(first, block, 0.0).astype(jnp.bfloat16)
                ref[head, 1] = jnp.where(first, 0.0, moved).astype(jnp.bfloat16)

    for step in range(size):
        pl.when(pl.program_id(0) == step)(functools.partial(one, x_refs[step]))


class Columns:
    def __init__(self, q_width, kv_width):
        self.q_width, self.kv_width = q_width, kv_width

    def spec(self, part, rows, place=lambda *_: 0):
        width, start = {
            "q": (self.q_width, 0),
            "out": (self.q_width, self.q_width),
            "kv": (2 * self.kv_width, 2 * self.q_width),
        }[part]
        index = start // width
        mode = {"pipeline_mode": ONCE} if place() == 0 else {}
        return pl.BlockSpec((rows, width), lambda *grid: (place(*grid), index), **mode)


def project(me, blocks, gain, own, other, cosine, sine, columns):
    size = len(blocks)
    rows, features = blocks[0].shape
    total = rows * size
    q_width, kv_width = columns.q_width, columns.kv_width
    key_heads = kv_width // HEAD_DIM
    width = q_width + 2 * kv_width
    half = features // 2
    fixed = lambda p, m: (0, 0)
    placed = lambda p, m: (jnp.bitwise_xor(p, m[0]), 0)
    padded = pl.BlockSpec(
        (key_heads, 2, rows, PAIR), lambda p, m: (0, 0, jnp.bitwise_xor(p, m[0]), 0)
    )
    spec = pltpu.PrefetchScalarGridSpec(
        num_scalar_prefetch=1,
        grid=(size,),
        in_specs=[pl.BlockSpec((rows, features), fixed, pipeline_mode=ONCE)] * size
        + [
            pl.BlockSpec((1, features), fixed),
            columns.spec("q", half),
            columns.spec("q", half),
            columns.spec("kv", half),
            columns.spec("kv", half),
            pl.BlockSpec((rows, PAIR), placed),
            pl.BlockSpec((rows, PAIR), placed),
        ],
        out_specs=[
            pl.BlockSpec((rows, features), lambda p, m: (p, 0)),
            pl.BlockSpec((rows, q_width), lambda p, m: (p, 0)),
            padded,
            padded,
        ],
    )
    padded_shape = jax.ShapeDtypeStruct((key_heads, 2, total, PAIR), jnp.bfloat16)
    return pl.pallas_call(
        functools.partial(project_kernel, size=size, q_width=q_width, kv_width=kv_width),
        grid_spec=spec,
        out_shape=[
            jax.ShapeDtypeStruct((total, features), jnp.bfloat16),
            jax.ShapeDtypeStruct((total, q_width), jnp.bfloat16),
            padded_shape,
            padded_shape,
        ],
        compiler_params=PARAMS,
        cost_estimate=hint(2 * total * features * width // 16),
    )(me, *blocks, gain, own, other, own, other, cosine, sine)


def attend_kernel(
    me_ref, q_ref, k_ref, v_ref, wo_ref, wx_ref, o_ref, l_ref, *refs, size, heads, group
):
    part_refs, vt_ref = refs[:-1], refs[-1]
    rows = q_ref.shape[0]
    half = wo_ref.shape[0]
    mine = jnp.bitwise_xor(me_ref[0], pl.program_id(0))
    key_place = lax.broadcasted_iota(jnp.int32, (rows, rows), 0)
    query_place = lax.broadcasted_iota(jnp.int32, (rows, rows), 1)

    @pl.when(pl.program_id(0) == 0)
    def _():
        for head in range(heads // group):
            for side in range(2):
                vt_ref[head, side] = v_ref[head, side].T

    def one(span):
        keys = span * rows
        for pair in range(heads // 2):
            head = 2 * pair // group
            lanes = slice(pair * PAIR, (pair + 1) * PAIR)
            query = q_ref[:, lanes]
            acc = None
            inverse = []
            for side in range(2):
                diag = mm_nt(k_ref[head, side, keys : keys + rows, :], query)
                diag = jnp.where(key_place <= query_place, diag, -1e9)
                top = jnp.max(diag, axis=0, keepdims=True)
                if span:
                    body = mm_nt(k_ref[head, side, :keys, :], query)
                    top = jnp.maximum(top, jnp.max(body, axis=0, keepdims=True))
                diag = jnp.exp(diag - top)
                total = jnp.sum(diag, axis=0, keepdims=True)
                part = mm(vt_ref[head, side, :, keys : keys + rows], diag.astype(jnp.bfloat16))
                if span:
                    body = jnp.exp(body - top)
                    total = total + jnp.sum(body, axis=0, keepdims=True)
                    part = part + mm(vt_ref[head, side, :, :keys], body.astype(jnp.bfloat16))
                acc = part if acc is None else acc + part
                inverse.append(jnp.broadcast_to(1.0 / total, (HEAD_DIM, rows)))
                l_ref[2 * pair + side : 2 * pair + side + 1, :] = top + jnp.log(total)
            acc = acc * jnp.concatenate(inverse, axis=0)
            o_ref[:, lanes] = acc.T.astype(jnp.bfloat16)

    for span in range(size):
        pl.when(mine == span)(functools.partial(one, span))

    def project_out(step):
        for part, w_ref in enumerate((wo_ref, wx_ref)):
            lanes = slice(part * half, (part + 1) * half)
            product = mm_nt(o_ref[...], w_ref[...]).astype(jnp.bfloat16)
            store_partner(part_refs, step, lanes, product)

    for step in range(size):
        pl.when(pl.program_id(0) == step)(functools.partial(project_out, step))


def attend(me, query, key_pad, value_pad, own, other, columns, size, group):
    total, width = query.shape
    features = 2 * own.shape[0]
    rows, heads = total // size, width // HEAD_DIM
    whole = pl.BlockSpec(key_pad.shape, lambda p, m: (0, 0, 0, 0), pipeline_mode=ONCE)
    spec = pltpu.PrefetchScalarGridSpec(
        num_scalar_prefetch=1,
        grid=(size,),
        in_specs=[pl.BlockSpec((rows, width), lambda p, m: (p, 0)), whole, whole]
        + [columns.spec("out", features // 2)] * 2,
        out_specs=[
            pl.BlockSpec((rows, width), lambda p, m: (p, 0)),
            pl.BlockSpec((heads, rows), lambda p, m: (0, p)),
        ]
        + [pl.BlockSpec((r, features), lambda p, m: (0, 0)) for r in partner_rows(size, rows)],
        scratch_shapes=[pltpu.VMEM((heads // group, 2, PAIR, total), jnp.bfloat16)],
    )
    return pl.pallas_call(
        functools.partial(attend_kernel, size=size, heads=heads, group=group),
        grid_spec=spec,
        out_shape=[
            jax.ShapeDtypeStruct((total, width), jnp.bfloat16),
            jax.ShapeDtypeStruct((heads, total), jnp.float32),
        ]
        + [jax.ShapeDtypeStruct((r, features), jnp.bfloat16) for r in partner_rows(size, rows)],
        compiler_params=PARAMS,
        cost_estimate=hint(8 * heads * total * total * HEAD_DIM // 16),
    )(me, query, key_pad, value_pad, own, other)


def attend_back_kernel(
    me_ref, q_ref, l_ref, k_ref, v_ref, cos_ref, sin_ref, *refs, size, heads, group
):
    do_refs = refs[:size]
    out_ref, dk_ref, dv_ref, kt_ref, do_ref = refs[size:]
    rows = q_ref.shape[0]
    key_heads = heads // group
    step = pl.program_id(0)
    me = me_ref[0]
    mine = jnp.bitwise_xor(me, step)
    key_place = lax.broadcasted_iota(jnp.int32, (rows, rows), 0)
    query_place = lax.broadcasted_iota(jnp.int32, (rows, rows), 1)

    def rows_of(block):
        return pl.ds(pl.multiple_of(block * rows, rows), rows)

    @pl.when(step == 0)
    def _():
        dk_ref[...] = jnp.zeros_like(dk_ref)
        dv_ref[...] = jnp.zeros_like(dv_ref)
        for head in range(key_heads):
            for side in range(2):
                kt_ref[head, side] = k_ref[head, side].T

    def fetch(ref):
        do_ref[...] = ref[...]

    for block in range(size):
        pl.when(step == block)(functools.partial(fetch, do_refs[block]))

    def one(span):
        keys = span * rows
        parts = [(keys, keys + rows, True)] + ([(0, keys, False)] if span else [])
        cosine, sine = cos_ref[keys : keys + rows, :], sin_ref[keys : keys + rows, :]
        for pair in range(heads // 2):
            head = 2 * pair // group
            lanes = slice(pair * PAIR, (pair + 1) * PAIR)
            query, grad = q_ref[:, lanes], do_ref[:, lanes]
            acc = None
            for side in range(2):
                log_total = l_ref[2 * pair + side : 2 * pair + side + 1, :]
                inner = None
                kept = []
                for low, high, diagonal in parts:
                    probs = mm_nt(k_ref[head, side, low:high, :], query)
                    probs = jnp.exp(probs - log_total)
                    if diagonal:
                        probs = jnp.where(key_place <= query_place, probs, 0.0)
                    prob_grad = mm_nt(v_ref[head, side, low:high, :], grad)
                    dv_ref[head, side, low:high, :] += mm(probs.astype(jnp.bfloat16), grad)
                    term = jnp.sum(probs * prob_grad, axis=0, keepdims=True)
                    inner = term if inner is None else inner + term
                    kept.append((low, high, probs, prob_grad))
                for low, high, probs, prob_grad in kept:
                    score_grad = (probs * (prob_grad - inner)).astype(jnp.bfloat16)
                    dk_ref[head, side, low:high, :] += mm(score_grad, query)
                    part = mm(kt_ref[head, side, :, low:high], score_grad)
                    acc = part if acc is None else acc + part
            turned = turn(acc.T * SCALE, cosine, -sine)
            out_ref[rows_of(step), lanes] = turned.astype(jnp.bfloat16)

    for span in range(size):
        pl.when(mine == span)(functools.partial(one, span))

    @pl.when(step == size - 1)
    def _():
        first = lane_index(rows) < HEAD_DIM
        wanted = [(dk_ref, head, True) for head in range(key_heads)]
        wanted += [(dv_ref, head, False) for head in range(key_heads)]
        for span in range(size):
            place = slice(span * rows, (span + 1) * rows)
            cosine, sine = cos_ref[place, :], sin_ref[place, :]
            for block in range(len(wanted) // 2):
                halves, rotate = [], []
                for half in range(2):
                    ref, head, is_key = wanted[2 * block + half]
                    low, high = ref[head, 0, place, :], ref[head, 1, place, :]
                    if half:
                        halves.append(pltpu.roll(low, HEAD_DIM, 1) + high)
                    else:
                        halves.append(low + pltpu.roll(high, HEAD_DIM, 1))
                    rotate.append(is_key)
                value = jnp.where(first, halves[0], halves[1])
                if rotate[0] and rotate[1]:
                    value = turn(value, cosine, -sine)
                elif rotate[0]:
                    value = jnp.where(first, turn(value, cosine, -sine), value)
                start = heads * HEAD_DIM + block * PAIR
                target = rows_of(jnp.bitwise_xor(me, span))
                out_ref[target, start : start + PAIR] = value.astype(jnp.bfloat16)


def attend_back(
    me, query, log_total, key_pad, value_pad, cosine, sine, attended_grad, group
):
    total, width = query.shape
    size = len(attended_grad)
    rows, heads = total // size, width // HEAD_DIM
    key_heads = heads // group
    out_width = width + 2 * key_heads * HEAD_DIM
    whole = pl.BlockSpec(key_pad.shape, lambda p, m: (0, 0, 0, 0), pipeline_mode=ONCE)
    table = pl.BlockSpec((total, PAIR), lambda p, m: (0, 0), pipeline_mode=ONCE)
    spec = pltpu.PrefetchScalarGridSpec(
        num_scalar_prefetch=1,
        grid=(size,),
        in_specs=[
            pl.BlockSpec((rows, width), lambda p, m: (p, 0)),
            pl.BlockSpec((heads, rows), lambda p, m: (0, p)),
            whole,
            whole,
            table,
            table,
        ]
        + [pl.BlockSpec((rows, width), lambda p, m: (0, 0), pipeline_mode=ONCE)] * size,
        out_specs=pl.BlockSpec((total, out_width), lambda p, m: (0, 0)),
        scratch_shapes=[
            pltpu.VMEM(key_pad.shape, jnp.float32),
            pltpu.VMEM(key_pad.shape, jnp.float32),
            pltpu.VMEM((key_heads, 2, PAIR, total), jnp.bfloat16),
            pltpu.VMEM((rows, width), jnp.bfloat16),
        ],
    )
    return pl.pallas_call(
        functools.partial(attend_back_kernel, size=size, heads=heads, group=group),
        grid_spec=spec,
        out_shape=jax.ShapeDtypeStruct((total, out_width), jnp.bfloat16),
        compiler_params=PARAMS,
        cost_estimate=hint(20 * heads * total * total * HEAD_DIM),
    )(me, query, log_total, key_pad, value_pad, cosine, sine, *attended_grad)


def grouped(arrays, counts):
    arrays = iter(arrays)
    return [[next(arrays) for _ in range(count)] for count in counts]


def mlp_kernel(*refs, n_counts, e_counts, adds):
    size = len(n_counts)
    pieces = sum(n_counts) + sum(e_counts)
    n_refs = grouped(refs, n_counts)
    e_refs = grouped(refs[sum(n_counts) :], e_counts)
    gate_o, up_o, down_o, gate_x, up_x, down_x = refs[pieces : pieces + 6]
    y_ref, n_ref, e_ref = refs[-3:]
    dn_count = len(partner_rows(size, n_ref.shape[0])) if adds else 1
    dn_refs = refs[-3 - dn_count : -3]
    dg_ref, du_ref, h_ref = refs[-6 - dn_count :][:3]
    half = gate_o.shape[0]

    def fetch(step):
        for target, sources in ((n_ref, n_refs[step]), (e_ref, e_refs[step])):
            low = 0
            for source in sources:
                high = low + source.shape[0]
                target[low:high] = source[...]
                low = high

    for step in range(size):
        pl.when(pl.program_id(0) == step)(functools.partial(fetch, step))
    gate = mm(n_ref[:, :half], gate_o[...]) + mm(n_ref[:, half:], gate_x[...])
    up = mm(n_ref[:, :half], up_o[...]) + mm(n_ref[:, half:], up_x[...])
    grad = mm(e_ref[:, :half], down_o[...]) + mm(e_ref[:, half:], down_x[...])
    sigma = jax.nn.sigmoid(gate)
    silu = gate * sigma
    hidden = (silu * up).astype(jnp.bfloat16)
    gate_grad = (grad * up * sigma * (1.0 + gate * (1.0 - sigma))).astype(jnp.bfloat16)
    up_grad = (grad * silu).astype(jnp.bfloat16)
    dg_ref[...] = gate_grad
    du_ref[...] = up_grad
    h_ref[...] = hidden
    for part, gate_w, up_w, down_w in ((0, gate_o, up_o, down_o), (1, gate_x, up_x, down_x)):
        lanes = slice(part * half, (part + 1) * half)
        dn = mm_nt(gate_grad, gate_w[...]) + mm_nt(up_grad, up_w[...])
        y = mm_nt(hidden, down_w[...])
        if adds:
            dn = dn + refs[pieces + 6][:, lanes].astype(jnp.float32)
            y = y + refs[pieces + 7][:, lanes].astype(jnp.float32)
        y_ref[:, lanes] = y.astype(jnp.bfloat16)
        dn = dn.astype(jnp.bfloat16)

        if adds:
            for step in range(size):
                pl.when(pl.program_id(0) == step)(
                    functools.partial(store_partner, dn_refs, step, lanes, dn)
                )
        else:
            dn_refs[0][:, lanes] = dn


def mlp(tokens, cot, own, other, earlier):
    size = len(tokens)
    rows, features = tokens[0][0].shape
    half, units = own.shape[0], own.shape[1] // 3
    total = rows * size
    fixed = lambda p: (0, 0)
    moving = lambda p: (p, 0)
    wide = pl.BlockSpec((rows, features), moving)
    sums = jax.ShapeDtypeStruct((total, features), jnp.bfloat16)
    dn_specs, dn_shapes = [wide], [sums]
    if earlier:
        counts = partner_rows(size, rows)
        dn_specs = [pl.BlockSpec((r, features), fixed) for r in counts]
        dn_shapes = [jax.ShapeDtypeStruct((r, features), jnp.bfloat16) for r in counts]
    pieces = sum(tokens, []) + sum(cot, [])
    thirds = [
        pl.BlockSpec((half, units), lambda p, t=t: (0, t), pipeline_mode=ONCE) for t in range(3)
    ]
    return pl.pallas_call(
        functools.partial(
            mlp_kernel,
            n_counts=[len(group) for group in tokens],
            e_counts=[len(group) for group in cot],
            adds=bool(earlier),
        ),
        grid=(size,),
        in_specs=[pl.BlockSpec(piece.shape, fixed, pipeline_mode=ONCE) for piece in pieces]
        + thirds * 2
        + [wide] * len(earlier),
        out_specs=[pl.BlockSpec((rows, units), moving)] * 3 + dn_specs + [wide],
        out_shape=[jax.ShapeDtypeStruct((total, units), jnp.bfloat16)] * 3 + dn_shapes + [sums],
        scratch_shapes=[pltpu.VMEM((rows, features), jnp.bfloat16)] * 2,
        compiler_params=PARAMS,
        cost_estimate=hint(12 * total * features * units),
    )(*pieces, own, own, own, other, other, other, *earlier)


def add_refs(refs):
    total = refs[0][...].astype(jnp.float32)
    for ref in refs[1:]:
        total = total + ref[...].astype(jnp.float32)
    return total


def store_by_device(out_ref, values, core, chips):
    width = values.shape[1] // (2 * chips)
    for chip in range(chips):
        own = values[:, chip * width : (chip + 1) * width]
        other = values[:, (chips + chip) * width : (chips + chip + 1) * width]
        low = 2 * chip * width
        out_ref[:, low : low + width] = jnp.where(core == 0, own, other)
        out_ref[:, low + width : low + 2 * width] = jnp.where(core == 0, other, own)


def middle_kernel(*refs):
    x_ref, gain_ref, middle_ref, normed_ref = refs[-4:]
    values = x_ref[...].astype(jnp.float32) + add_refs(refs[:-4])
    middle_ref[...] = values
    normed_ref[...] = (values * rms_scale(values) * gain_ref[...]).astype(jnp.bfloat16)


def input_back_kernel(core_ref, *refs, chips):
    x_ref, before_ref, gain_ref, out_ref = refs[-4:]
    values = x_ref[...].astype(jnp.float32)
    inner = add_refs(refs[:-4]) * gain_ref[...]
    scale = rms_scale(values)
    mean = jnp.mean(inner * values, axis=-1, keepdims=True)
    result = before_ref[...] + scale * inner - values * (scale * scale * scale) * mean
    store_by_device(out_ref, result, core_ref[0], chips)


def output_kernel(core_ref, *refs, chips):
    middle_ref, out_ref = refs[-2:]
    values = middle_ref[...] + add_refs(refs[:-2])
    store_by_device(out_ref, values.astype(jnp.bfloat16), core_ref[0], chips)


def row_call(body, dtypes, arrays, core=None):
    rows, features = arrays[0].shape
    steps = 2
    wide = pl.BlockSpec((rows // steps, features), lambda i, *_: (i, 0))
    row = pl.BlockSpec((1, features), lambda i, *_: (0, 0))
    scalars = [] if core is None else [jnp.full((1,), core, jnp.int32)]
    return pl.pallas_call(
        body,
        grid_spec=pltpu.PrefetchScalarGridSpec(
            num_scalar_prefetch=len(scalars),
            grid=(steps,),
            in_specs=[row if array.shape[0] == 1 else wide for array in arrays],
            out_specs=[wide] * len(dtypes),
        ),
        out_shape=[jax.ShapeDtypeStruct((rows, features), dtype) for dtype in dtypes],
        compiler_params=PARAMS,
        cost_estimate=hint(0),
    )(*scalars, *arrays)


def unpack_kernel(sum_ref, q_ref, k_ref, v_ref, out_ref):
    q_width, kv_width = q_ref.shape[1], k_ref.shape[1]
    values = sum_ref[...].astype(jnp.float32)
    q_ref[...] = values[:, :q_width]
    kv = values[:, q_width : q_width + 2 * kv_width]
    k_ref[...] = kv[:, :kv_width]
    v_ref[...] = kv[:, kv_width:]
    out_ref[...] = values[:, q_width + 2 * kv_width :].T


def unpack(sums, q_width, kv_width):
    rows = sums.shape[0]
    widths = [(rows, q_width), (rows, kv_width), (rows, kv_width), (q_width, rows)]
    return pl.pallas_call(
        unpack_kernel,
        out_shape=[jax.ShapeDtypeStruct(shape, jnp.float32) for shape in widths],
        compiler_params=PARAMS,
        cost_estimate=hint(0),
    )(sums)


def unpack_shares_kernel(one_ref, two_ref, gate_ref, up_ref, down_ref):
    units = one_ref.shape[1] // 3
    for part, ref in enumerate((one_ref, two_ref)):
        cut = slice(part * units, (part + 1) * units)
        gate_ref[:, cut] = ref[:, :units].astype(jnp.float32)
        up_ref[:, cut] = ref[:, units : 2 * units].astype(jnp.float32)
        down_ref[cut, :] = ref[:, 2 * units :].astype(jnp.float32).T


def unpack_shares(one, two):
    rows, width = one.shape
    units = 2 * width // 3
    shapes = [(rows, units), (rows, units), (units, rows)]
    return pl.pallas_call(
        unpack_shares_kernel,
        out_shape=[jax.ShapeDtypeStruct(shape, jnp.float32) for shape in shapes],
        compiler_params=PARAMS,
        cost_estimate=hint(0),
    )(one, two)


def middle_back_kernel(*refs, parts, size):
    n_refs, refs = refs[:parts], refs[parts:]
    x_ref, e_ref, gain_ref, refs = refs[0], refs[1], refs[2], refs[3:]
    own_refs, other_refs, refs = refs[:size], refs[size : 2 * size], refs[2 * size :]
    grad_ref, branch_ref, part_ref, do_refs = refs[0], refs[1], refs[2], refs[3:]
    half = own_refs[0].shape[0]
    grad = add_refs(n_refs)
    values = x_ref[...]
    scale = rms_scale(values)
    result, part = norm_back(grad, values, scale, gain_ref[...])

    @pl.when(pl.program_id(0) == 0)
    def _():
        part_ref[...] = jnp.zeros_like(part_ref)

    part_ref[...] += part[None, :]
    result = result + e_ref[...].astype(jnp.float32)
    grad_ref[...] = result
    branch = result.astype(jnp.bfloat16)
    branch_ref[...] = branch
    for own, other, do_ref in zip(own_refs, other_refs, do_refs):
        do = mm(branch[:, :half], own[...]) + mm(branch[:, half:], other[...])
        do_ref[...] = do.astype(jnp.bfloat16)


def middle_back(arrived, middle, cot, gain, own, other):
    parts, size = len(arrived), len(own)
    rows, features = middle.shape
    width = own[0].shape[1]
    steps = 2
    wide = pl.BlockSpec((rows // steps, features), lambda i: (i, 0))
    narrow = pl.BlockSpec((rows // steps, width), lambda i: (i, 0))
    row = pl.BlockSpec((1, features), lambda i: (0, 0))
    weight = pl.BlockSpec((features // 2, width), lambda i: (0, 0), pipeline_mode=ONCE)
    grad, branch, part, *do = pl.pallas_call(
        functools.partial(middle_back_kernel, parts=parts, size=size),
        grid=(steps,),
        in_specs=[wide] * parts + [wide, wide, row] + [weight] * (2 * size),
        out_specs=[wide, wide, row] + [narrow] * size,
        out_shape=[
            jax.ShapeDtypeStruct((rows, features), jnp.float32),
            jax.ShapeDtypeStruct((rows, features), jnp.bfloat16),
            jax.ShapeDtypeStruct((1, features), jnp.float32),
        ]
        + [jax.ShapeDtypeStruct((rows, width), jnp.bfloat16)] * size,
        compiler_params=PARAMS,
        cost_estimate=hint(2 * rows * features * width * size),
    )(*arrived, middle, cot, gain, *own, *other)
    return grad, branch, part[0], do


def column_grad(blocks, other, mine, theirs):
    total = mm_tn(other[...], theirs[...])
    low = 0
    for block in blocks:
        high = low + block.shape[0]
        total = total + mm_tn(block[...], mine[low:high, :])
        low = high
    return total


def grad_kernel(*refs, n_count, e_count):
    n_refs, refs = refs[:n_count], refs[n_count:]
    e_refs, refs = refs[:e_count], refs[e_count:]
    n_other, e_other = refs[:2]
    acts, out_ref = refs[2:-1], refs[-1]
    units = acts[0].shape[1]
    for third in range(3):
        blocks, other = (e_refs, e_other) if third == 2 else (n_refs, n_other)
        grad = column_grad(blocks, other, acts[third], acts[third + 3])
        out_ref[0, :, third * units : (third + 1) * units] = grad.astype(jnp.bfloat16)


def mlp_grads(chips, tokens, cot, tokens_other, cot_other, mine, theirs):
    tokens, cot = sum(tokens, []), sum(cot, [])
    features = tokens[0].shape[1]
    total, units = mine[0].shape
    depth = features // (2 * chips)
    long = pl.BlockSpec((total, depth), lambda b: (0, b))
    fixed = pl.BlockSpec((total, units), lambda b: (0, 0), pipeline_mode=ONCE)
    return pl.pallas_call(
        functools.partial(grad_kernel, n_count=len(tokens), e_count=len(cot)),
        grid=(chips,),
        in_specs=[pl.BlockSpec((p.shape[0], depth), lambda b: (0, b)) for p in tokens + cot]
        + [long, long]
        + [fixed] * 6,
        out_specs=pl.BlockSpec((1, depth, 3 * units), lambda b: (b, 0, 0)),
        out_shape=jax.ShapeDtypeStruct((chips, depth, 3 * units), jnp.bfloat16),
        compiler_params=PARAMS,
        cost_estimate=hint(6 * total * features * units),
    )(*tokens, *cot, tokens_other, cot_other, *mine, *theirs)


def attn_grad_kernel(*refs, size):
    e_refs = refs[2 : 2 + size]
    n_ref, n_other = refs[:2]
    e_other, d_ref, d_other, o_ref, o_other, q_ref, kv_ref, g1_ref, g2_ref = refs[2 + size : -2]
    out_ref, gain_ref = refs[-2:]
    width, out_width = d_ref.shape[1], o_ref.shape[1]
    grad = column_grad([n_ref], n_other, d_ref, d_other)
    out_ref[0, :, :width] = grad.astype(jnp.bfloat16)
    out_grad = column_grad(e_refs, e_other, o_ref, o_other)
    out_ref[0, :, width : width + out_width] = out_grad.astype(jnp.bfloat16)
    cut = q_ref.shape[1]
    first = jnp.sum(grad[:, :cut] * q_ref[...].astype(jnp.float32), axis=1, keepdims=True)
    first += jnp.sum(grad[:, cut:] * kv_ref[...].astype(jnp.float32), axis=1, keepdims=True)
    first = first / g1_ref[...]
    lane = lane_index(grad.shape[0])
    gain_ref[0] = jnp.where(lane == 0, first, g2_ref[...])


def attn_grads(
    chips, tokens, branch, mine, theirs, weights, columns, gain_one, gain_two_part
):
    size = len(branch)
    qkv_grad, attended = mine
    tokens_other, branch_other, qkv_other, attended_other = theirs
    total, features = tokens.shape
    rows = total // size
    width, out_width = qkv_grad.shape[1], attended.shape[1]
    depth = features // (2 * chips)
    column = lambda b: (0, b)
    row = lambda b: (b, 0)
    long = pl.BlockSpec((total, depth), column)
    fixed = lambda array: pl.BlockSpec(array.shape, lambda b: (0, 0), pipeline_mode=ONCE)
    place = lambda b: (b, 0, 0)
    return pl.pallas_call(
        functools.partial(attn_grad_kernel, size=size),
        grid=(chips,),
        in_specs=[long, long]
        + [pl.BlockSpec((rows, depth), column)] * size
        + [long]
        + [fixed(qkv_grad)] * 2
        + [fixed(attended)] * 2
        + [
            columns.spec("q", depth, lambda b=None: b),
            columns.spec("kv", depth, lambda b=None: b),
            pl.BlockSpec((depth, 1), row),
            pl.BlockSpec((depth, 1), row),
        ],
        out_specs=[
            pl.BlockSpec((1, depth, width + out_width), place),
            pl.BlockSpec((1, depth, PAIR), place),
        ],
        out_shape=[
            jax.ShapeDtypeStruct((chips, depth, width + out_width), jnp.bfloat16),
            jax.ShapeDtypeStruct((chips, depth, PAIR), jnp.float32),
        ],
        compiler_params=PARAMS,
        cost_estimate=hint(2 * total * features * (width + out_width)),
    )(
        tokens,
        tokens_other,
        *branch,
        branch_other,
        qkv_grad,
        qkv_other,
        attended,
        attended_other,
        weights,
        weights,
        gain_one,
        gain_two_part,
    )


def input_grad_kernel(d_ref, qo_ref, qx_ref, kvo_ref, kvx_ref, *out_refs, size):
    half, cut = qo_ref.shape

    def one(step):
        query, rest = d_ref[:, :cut], d_ref[:, cut:]
        for part, (q_ref, kv_ref) in enumerate(((qo_ref, kvo_ref), (qx_ref, kvx_ref))):
            lanes = slice(part * half, (part + 1) * half)
            product = mm_nt(query, q_ref[...]) + mm_nt(rest, kv_ref[...])
            store_partner(out_refs, step, lanes, product.astype(jnp.bfloat16))

    for step in range(size):
        pl.when(pl.program_id(0) == step)(functools.partial(one, step))


def input_grad(qkv_grad, own, other, columns, size):
    total, width = qkv_grad.shape
    features = 2 * own.shape[0]
    rows = total // size
    fixed = lambda i: (0, 0)
    weights = [columns.spec(part, own.shape[0]) for part in ("q", "q", "kv", "kv")]
    return pl.pallas_call(
        functools.partial(input_grad_kernel, size=size),
        grid=(size,),
        in_specs=[pl.BlockSpec((rows, width), lambda i: (i, 0))] + weights,
        out_specs=[pl.BlockSpec((r, features), fixed) for r in partner_rows(size, rows)],
        out_shape=[
            jax.ShapeDtypeStruct((r, features), jnp.bfloat16) for r in partner_rows(size, rows)
        ],
        compiler_params=PARAMS,
        cost_estimate=hint(2 * total * features * width),
    )(qkv_grad, own, other, own, other)


def swap(values, step):
    size = lax.axis_size("tensor")
    return lax.ppermute(values, "tensor", [(i, i ^ step) for i in range(size)])


def spread(values):
    return [values] + [swap(values, step) for step in range(1, lax.axis_size("tensor"))]


def send_blocks(blocks):
    return [blocks[0]] + [swap(block, step + 1) for step, block in enumerate(blocks[1:])]


def spread_around(values, held):
    if lax.axis_size("tensor") != 4:
        blocks = spread(values)
        first, held = barrier((blocks[1], held))
        return [[blocks[0]], [first]] + [[block] for block in blocks[2:]], held
    half = values.shape[0] // 2
    top, bottom = values[:half], values[half:]
    x_bottom, y_top = swap(bottom, 1), swap(top, 2)
    x_bottom, y_top, top, bottom, held = barrier((x_bottom, y_top, top, bottom, held))
    far = [swap(y_top, 1), swap(x_bottom, 2)]
    x_top, y_bottom = swap(top, 1), swap(bottom, 2)
    return [[values], [x_top, x_bottom], [y_top, y_bottom], far], held


def merge_kernel(x_ref, y_ref, top_ref, bottom_ref, x_out, y_out):
    half = top_ref.shape[0]
    x_out[:half] = x_ref[:half]
    x_out[half:] = add_refs([x_ref.at[half:], bottom_ref]).astype(jnp.bfloat16)
    y_out[:half] = add_refs([y_ref.at[:half], top_ref]).astype(jnp.bfloat16)
    y_out[half:] = y_ref[half:]


def send_sum(blocks, held=()):
    if lax.axis_size("tensor") != 4:
        return send_blocks(blocks), held
    own, near_x, near_y, top, bottom = blocks
    top, bottom = swap(top, 1), swap(bottom, 2)
    near_x, near_y = pl.pallas_call(
        merge_kernel,
        out_shape=[jax.ShapeDtypeStruct(near_x.shape, near_x.dtype)] * 2,
        compiler_params=PARAMS,
        cost_estimate=hint(0),
    )(near_x, near_y, top, bottom)
    near_x, near_y, held = barrier((near_x, near_y, held))
    return [own, swap(near_x, 1), swap(near_y, 2)], held


def add_up(blocks):
    total = blocks[0].astype(jnp.float32)
    for block in blocks[1:]:
        total = total + block.astype(jnp.float32)
    return total


def cross(values):
    count = lax.axis_size("dp")
    return lax.ppermute(values, "dp", [(i, i ^ 1) for i in range(count)])


def tables(positions):
    freqs = ROPE_BASE ** (-jnp.arange(0, HEAD_DIM, 2).astype(jnp.float32) / HEAD_DIM)
    angles = positions.astype(jnp.float32)[:, None] * freqs[None, :]
    cosine, sine = jnp.cos(angles), jnp.sin(angles)
    return (
        jnp.concatenate([cosine] * 4, axis=1),
        jnp.concatenate([-sine, sine, -sine, sine], axis=1),
    )


def chip_lines():
    count = lax.axis_size("dp")
    return [list(range(core, count, 2)) for core in range(2)]


def gather(values):
    return lax.all_gather(values, "dp", axis=0, tiled=True, axis_index_groups=chip_lines())


def scatter(values):
    total = lax.psum_scatter(
        values, "dp", scatter_dimension=0, tiled=True, axis_index_groups=chip_lines()
    )
    return total[0]


def along(values, step):
    count = lax.axis_size("dp")
    return lax.ppermute(values, "dp", [(i, (i + 2 * step) % count) for i in range(count)])


def line_parts(parts):
    chips = lax.axis_size("dp") // 2
    chip = lax.axis_index("dp") // 2
    blocks = [lax.dynamic_index_in_dim(parts, chip, 0, keepdims=False)]
    for step in range(1, chips):
        sent = lax.dynamic_index_in_dim(parts, (chip + step) % chips, 0, keepdims=False)
        blocks.append(along(sent, step))
    return blocks


def own_part(values):
    size = lax.axis_size("tensor")
    me = lax.axis_index("tensor")
    blocks = values.reshape((size, -1) + values.shape[1:])
    own = lax.dynamic_index_in_dim(blocks, me, 0, keepdims=False)
    for step in range(1, size):
        sent = lax.dynamic_index_in_dim(blocks, me ^ step, 0, keepdims=False)
        own = own + swap(sent, step)
    return own


def stack_kernel(*refs):
    low = 0
    for ref in refs[:-1]:
        high = low + ref.shape[0]
        refs[-1][low:high, :] = ref[...]
        low = high


def other_half(blocks):
    features = blocks[0].shape[1]
    shape = (sum(block.shape[0] for block in blocks), features // 2)
    halves = pl.pallas_call(
        stack_kernel,
        grid=(1,),
        in_specs=[pl.BlockSpec((b.shape[0], features // 2), lambda i: (0, 1)) for b in blocks],
        out_specs=pl.BlockSpec(shape, lambda i: (0, 0)),
        out_shape=jax.ShapeDtypeStruct(shape, blocks[0].dtype),
        compiler_params=PARAMS,
        cost_estimate=hint(0),
    )(*blocks)
    return cross(halves)


def feature_blocks(values):
    width = values.shape[-1] // lax.axis_size("dp")
    return [values[..., low : low + width] for low in range(0, values.shape[-1], width)]


def by_core(values, core):
    blocks = feature_blocks(values)
    pairs = list(zip(blocks[0::2], blocks[1::2]))
    own = [jnp.where(core == 0, even, odd) for even, odd in pairs]
    other = [jnp.where(core == 0, odd, even) for even, odd in pairs]
    return jnp.concatenate(own + other, axis=-1)


def per_device(
    hidden_in,
    gain_attn,
    w_query,
    w_key,
    w_value,
    w_out,
    gain_mlp,
    w_gate,
    w_up,
    w_down,
    positions,
    cotangent,
):
    size = lax.axis_size("tensor")
    chips = lax.axis_size("dp") // 2
    me = lax.axis_index("tensor")
    me_array = jnp.full((1,), me, jnp.int32)
    core = lax.axis_index("dp") % 2
    q_width, kv_width = w_query.shape[1], w_key.shape[1]
    group = q_width // kv_width
    units = w_down.shape[0] // 2
    half = hidden_in.shape[1] // 2

    columns = Columns(q_width, kv_width)
    attn_shard = jnp.concatenate([w_query, w_out.T, w_key, w_value], axis=1)
    attn_shard, hidden_in, gain_attn = barrier((attn_shard, hidden_in, gain_attn))
    attn_own = gather(attn_shard)
    residual = by_core(hidden_in, core)
    blocks_in = spread(residual)
    gains = lax.all_gather(jnp.stack([gain_attn, gain_mlp]), "dp", axis=1, tiled=True)
    gains = by_core(gains, core).astype(jnp.float32)
    cosine, sine = tables(positions)
    cotangent = by_core(cotangent, core)
    down_t = w_down.T
    shares = []
    for part in range(2):
        cut = slice(part * units, (part + 1) * units)
        shares.append(jnp.concatenate([w_gate[:, cut], w_up[:, cut], down_t[:, cut]], axis=1))
    shares, attn_own, blocks_in, cosine, sine, gains, cotangent = barrier(
        (shares, attn_own, blocks_in, cosine, sine, gains, cotangent)
    )
    mlp_own = [gather(share) for share in shares]
    cot_blocks = spread(cotangent)
    gain_one, gain_two = gains[0], gains[1]
    attn = (attn_own, cross(attn_own))

    tokens_one, query, key_pad, value_pad = project(
        me_array, blocks_in, gain_one[None, :], *attn, cosine, sine, columns
    )
    attended, log_total, *parts = attend(
        me_array, query, key_pad, value_pad, *attn, columns, size, group
    )
    parts, cot_blocks, tokens_one, attended = barrier((parts, cot_blocks, tokens_one, attended))
    arrived, _ = send_sum(parts)
    cot_other = other_half(cot_blocks)
    cot_blocks = [[block] for block in cot_blocks]
    early = (cross(tokens_one[:, half:]), cross(attended))
    arrived, cot_other, early = barrier((arrived, cot_other, early))
    out_t = [w[:, q_width : 2 * q_width] for w in attn]
    middle, normed_two = row_call(
        middle_kernel, [jnp.float32, jnp.bfloat16], [*arrived, residual, gain_two[None, :]]
    )
    tokens_two, own_share = spread_around(normed_two, mlp_own[0])
    weights = (own_share, cross(own_share))
    tokens_two, weights, out_own = barrier((tokens_two, weights, out_t[0]))
    tokens_other = other_half(sum(tokens_two, []))
    *acts, dn_part, y_part = mlp(tokens_two, cot_blocks, *weights, ())
    out_blocks = spread(out_own)
    acts, tokens_other = barrier((acts, tokens_other))
    acts_other = [cross(act) for act in acts]
    grads_one = mlp_grads(
        chips, tokens_two, cot_blocks, tokens_other, cot_other, acts, acts_other
    )
    grads_one, own_share = barrier((grads_one, mlp_own[1]))
    sums_one = scatter(grads_one)
    weights = (own_share, cross(own_share))
    *acts, y_part = mlp(tokens_two, cot_blocks, *weights, (dn_part, y_part))
    acts, dn_part = acts[:3], acts[3:]
    acts, dn_part, out_blocks = barrier((acts, dn_part, out_blocks))
    acts_other = [cross(act) for act in acts]
    arrived, acts = send_sum(dn_part, acts)
    out_other = [out_t[1]] + [cross(block) for block in out_blocks[1:]]
    grads_two = mlp_grads(
        chips, tokens_two, cot_blocks, tokens_other, cot_other, acts, acts_other
    )
    grads_two, arrived, out_other, y_part = barrier((grads_two, arrived, out_other, y_part))
    y_blocks = list(y_part.reshape((size, -1) + y_part.shape[1:]))
    y_early = [swap(y_blocks[step], step) for step in range(1, 3)]
    sums_two = scatter(grads_two)
    middle_grad, branch, gain_two_part, do_blocks = middle_back(
        arrived, middle, cotangent, gain_two[None, :], out_blocks, out_other
    )
    do_blocks = send_blocks(do_blocks)
    gain_two_other = cross(gain_two_part[half:])
    do_blocks, branch, gain_two_other, y_blocks, y_early = barrier(
        (do_blocks, branch, gain_two_other, y_blocks, y_early)
    )
    branch_blocks = spread(branch)
    qkv_grad = attend_back(
        me_array, query, log_total, key_pad, value_pad, cosine, sine, do_blocks, group
    )
    qkv_grad, sums_one = barrier((qkv_grad, sums_one))
    qkv_other = cross(qkv_grad)
    normed_part = input_grad(qkv_grad, *attn, columns, size)
    branch_blocks, normed_part = barrier((branch_blocks, normed_part))
    branch_other = other_half(branch_blocks)
    tokens_other, attended_other = early
    grads, gain_parts = attn_grads(
        chips,
        tokens_one,
        branch_blocks,
        (qkv_grad, attended),
        (tokens_other, branch_other, qkv_other, attended_other),
        attn_own,
        columns,
        gain_one[:half, None],
        (gain_two_part[:half] + gain_two_other)[:, None],
    )
    arrived, (grads, sums_two) = send_sum(normed_part, (grads, sums_two))
    attn_sums = scatter(grads)
    gain_sums = add_up(line_parts(gain_parts[:, :, :2]))
    unpacked = unpack_shares(sums_one, sums_two)
    arrived, y_blocks, unpacked, gain_sums = barrier((arrived, y_blocks, unpacked, gain_sums))
    grad_gate, grad_up, grad_down = unpacked
    y_late = [swap(y_blocks[step], step) for step in range(3, size)]
    (grad_in,) = row_call(
        functools.partial(input_back_kernel, chips=chips),
        [jnp.float32],
        [*arrived, residual, middle_grad, gain_one[None, :]],
        core,
    )
    grad_in, gain_sums = barrier((grad_in, gain_sums))
    gain_sums = own_part(gain_sums)
    y_late, grad_in, gain_sums = barrier((y_late, grad_in, gain_sums))
    (out,) = row_call(
        functools.partial(output_kernel, chips=chips),
        [jnp.bfloat16],
        [y_blocks[0], *y_early, *y_late, middle],
        core,
    )
    out, attn_sums = barrier((out, attn_sums))
    grad_query, grad_key, grad_value, grad_out = unpack(attn_sums, q_width, kv_width)
    return (
        out,
        grad_in,
        gain_sums[:, 0],
        grad_query,
        grad_key,
        grad_value,
        grad_out,
        gain_sums[:, 1],
        grad_gate,
        grad_up,
        grad_down,
    )


def solution(mesh):
    return jax.shard_map(
        per_device,
        mesh=mesh,
        in_specs=(
            P(("dp", "tensor"), None),
            P("dp"),
            P("dp", "tensor"),
            P("dp", "tensor"),
            P("dp", "tensor"),
            P("tensor", "dp"),
            P("dp"),
            P("dp", "tensor"),
            P("dp", "tensor"),
            P("tensor", "dp"),
            P("dp"),
            P(("dp", "tensor"), None),
        ),
        out_specs=(
            P(("dp", "tensor"), None),
            P(("dp", "tensor"), None),
            P(("dp", "tensor")),
            P("dp", "tensor"),
            P("dp", "tensor"),
            P("dp", "tensor"),
            P("tensor", "dp"),
            P(("dp", "tensor")),
            P("dp", "tensor"),
            P("dp", "tensor"),
            P("tensor", "dp"),
        ),
        check_vma=False,
    )
```

```python
import functools
import math

import jax
import jax.numpy as jnp
from jax import lax
from jax.experimental import pallas as pl
from jax.experimental.pallas import tpu as pltpu
from jax.sharding import PartitionSpec as P

HEAD_DIM = 64
PAIR = 2 * HEAD_DIM
SEQ_LEN = 1024


EPS = 1e-05
ROPE_BASE = 500000.0
SCALE = 1.0 / math.sqrt(HEAD_DIM)
PARAMS = pltpu.CompilerParams(vmem_limit_bytes=58 * 2**20)
ONCE = pl.Buffered(1)

barrier = lax.optimization_barrier


def hint(flops):
    return pl.CostEstimate(flops=flops, bytes_accessed=0, transcendentals=0)


def rms_scale(values):
    return lax.rsqrt(jnp.mean(values * values, axis=-1, keepdims=True) + EPS)


def norm_back(grad, values, scale, gain):
    inner = grad * gain
    cubed = scale * scale * scale
    result = scale * inner - values * cubed * jnp.mean(inner * values, axis=-1, keepdims=True)
    return (result, jnp.sum(grad * values * scale, axis=0))


def mm(left, right):
    return jnp.dot(left, right, preferred_element_type=jnp.float32)


def mm_nt(left, right):
    return lax.dot_general(left, right, (((1,), (1,)), ((), ())), preferred_element_type=jnp.float32)


def mm_tn(left, right):
    return lax.dot_general(left, right, (((0,), (0,)), ((), ())), preferred_element_type=jnp.float32)


def partner_rows(size, rows):
    return [rows] * 3 + [rows // 2] * 2 if size == 4 else [rows] * size


def store_partner(refs, step, lanes, value):
    if len(refs) == 5 and step == 3:
        half = refs[3].shape[0]
        refs[3][:, lanes] = value[:half]
        refs[4][:, lanes] = value[half:]
    else:
        refs[step][:, lanes] = value


def lane_index(rows):
    return lax.broadcasted_iota(jnp.int32, (rows, PAIR), 1)


def turn(pair, cosine, sine):
    lower = lane_index(pair.shape[0]) % HEAD_DIM < HEAD_DIM // 2
    other = jnp.where(
        lower, pltpu.roll(pair, PAIR - HEAD_DIM // 2, 1), pltpu.roll(pair, HEAD_DIM // 2, 1)
    )
    return pair * cosine + other * sine


def project_kernel(place_ref, *refs, size, q_width, kv_width):
    x_refs = refs[:size]
    go_ref, gx_ref, qo_ref, qx_ref, kvo_ref, kvx_ref, cos_ref, sin_ref = refs[size:-5]
    n_ref, q_ref, k_ref, v_ref, gain_ref = refs[-5:]
    rows = q_ref.shape[0]
    half = qo_ref.shape[0]

    @pl.when(pl.program_id(0) == 0)
    def _():
        gain_ref[:, :half] = go_ref[...].astype(jnp.float32).T[:1, :]
        gain_ref[:, half:] = gx_ref[...].astype(jnp.float32).T[:1, :]

    def one(x_ref):
        x = x_ref[...].astype(jnp.float32)
        normed = (x * rms_scale(x) * gain_ref[...]).astype(jnp.bfloat16)
        n_ref[...] = normed
        cosine, sine = cos_ref[...], sin_ref[...]
        own, other = normed[:, :half], normed[:, half:]
        lin = mm(own, qo_ref[...]) + mm(other, qx_ref[...])
        for low in range(0, q_width, PAIR):
            query = turn(lin[:, low : low + PAIR], cosine, sine).astype(jnp.bfloat16)
            q_ref[:, low : low + PAIR] = query * jnp.bfloat16(SCALE)
        lin = mm(own, kvo_ref[...]) + mm(other, kvx_ref[...])
        first = lane_index(rows) < HEAD_DIM
        for ref, start, rotate in ((k_ref, 0, True), (v_ref, kv_width, False)):
            for head in range(kv_width // HEAD_DIM):
                low = start + head * HEAD_DIM
                block = lin[:, low // PAIR * PAIR : low // PAIR * PAIR + PAIR]
                if rotate:
                    block = turn(block, cosine, sine)
                moved = pltpu.roll(block, HEAD_DIM, 1)
                if low % PAIR:
                    block, moved = moved, block
                ref[head, 0] = jnp.where(first, block, 0.0).astype(jnp.bfloat16)
                ref[head, 1] = jnp.where(first, 0.0, moved).astype(jnp.bfloat16)

    for step in range(size):
        pl.when(pl.program_id(0) == step)(functools.partial(one, x_refs[step]))


class Columns:
    def __init__(self, q_width, kv_width):
        self.q_width, self.kv_width = q_width, kv_width
        self.gain_start = q_width + 2 * kv_width

    def spec(self, part, rows, place=lambda *_: 0):
        width, start = {
            "q": (self.q_width, 0),
            "kv": (2 * self.kv_width, self.q_width),
            "gain": (PAIR, self.gain_start),
        }[part]
        index = start // width
        mode = {"pipeline_mode": ONCE} if place() == 0 else {}
        return pl.BlockSpec((rows, width), lambda *grid: (place(*grid), index), **mode)


def project(me, blocks, own, other, cosine, sine, columns):
    size = len(blocks)
    rows, features = blocks[0].shape
    total = rows * size
    q_width, kv_width = columns.q_width, columns.kv_width
    key_heads = kv_width // HEAD_DIM
    width = q_width + 2 * kv_width
    half = features // 2
    fixed = lambda p, m: (0, 0)
    placed = lambda p, m: (jnp.bitwise_xor(p, m[0]), 0)
    padded = pl.BlockSpec(
        (key_heads, 2, rows, PAIR), lambda p, m: (0, 0, jnp.bitwise_xor(p, m[0]), 0)
    )
    spec = pltpu.PrefetchScalarGridSpec(
        num_scalar_prefetch=1,
        grid=(size,),
        in_specs=[pl.BlockSpec((rows, features), fixed, pipeline_mode=ONCE)] * size
        + [
            columns.spec("gain", half),
            columns.spec("gain", half),
            columns.spec("q", half),
            columns.spec("q", half),
            columns.spec("kv", half),
            columns.spec("kv", half),
            pl.BlockSpec((rows, PAIR), placed),
            pl.BlockSpec((rows, PAIR), placed),
        ],
        out_specs=[
            pl.BlockSpec((rows, features), lambda p, m: (p, 0)),
            pl.BlockSpec((rows, q_width), lambda p, m: (p, 0)),
            padded,
            padded,
        ],
        scratch_shapes=[pltpu.VMEM((1, features), jnp.float32)],
    )
    padded_shape = jax.ShapeDtypeStruct((key_heads, 2, total, PAIR), jnp.bfloat16)
    return pl.pallas_call(
        functools.partial(project_kernel, size=size, q_width=q_width, kv_width=kv_width),
        grid_spec=spec,
        out_shape=[
            jax.ShapeDtypeStruct((total, features), jnp.bfloat16),
            jax.ShapeDtypeStruct((total, q_width), jnp.bfloat16),
            padded_shape,
            padded_shape,
        ],
        compiler_params=PARAMS,
        cost_estimate=hint(2 * total * features * width // 16),
    )(me, *blocks, own, other, own, other, own, other, cosine, sine)


def attend_kernel(
    me_ref, q_ref, k_ref, v_ref, wo_ref, wx_ref, o_ref, l_ref, *refs, size, heads, group
):
    part_refs, vt_ref = refs[:-1], refs[-1]
    rows = q_ref.shape[0]
    half = wo_ref.shape[0]
    mine = jnp.bitwise_xor(me_ref[0], pl.program_id(0))
    key_place = lax.broadcasted_iota(jnp.int32, (rows, rows), 0)
    query_place = lax.broadcasted_iota(jnp.int32, (rows, rows), 1)

    @pl.when(pl.program_id(0) == 0)
    def _():
        for head in range(heads // group):
            for side in range(2):
                vt_ref[head, side] = v_ref[head, side].T

    def one(span):
        keys = span * rows
        for pair in range(heads // 2):
            head = 2 * pair // group
            lanes = slice(pair * PAIR, (pair + 1) * PAIR)
            query = q_ref[:, lanes]
            acc = None
            inverse = []
            for side in range(2):
                diag = mm_nt(k_ref[head, side, keys : keys + rows, :], query)
                diag = jnp.where(key_place <= query_place, diag, -1e9)
                top = jnp.max(diag, axis=0, keepdims=True)
                if span:
                    body = mm_nt(k_ref[head, side, :keys, :], query)
                    top = jnp.maximum(top, jnp.max(body, axis=0, keepdims=True))
                diag = jnp.exp(diag - top)
                total = jnp.sum(diag, axis=0, keepdims=True)
                part = mm(vt_ref[head, side, :, keys : keys + rows], diag.astype(jnp.bfloat16))
                if span:
                    body = jnp.exp(body - top)
                    total = total + jnp.sum(body, axis=0, keepdims=True)
                    part = part + mm(vt_ref[head, side, :, :keys], body.astype(jnp.bfloat16))
                acc = part if acc is None else acc + part
                inverse.append(jnp.broadcast_to(1.0 / total, (HEAD_DIM, rows)))
                l_ref[2 * pair + side : 2 * pair + side + 1, :] = top + jnp.log(total)
            acc = acc * jnp.concatenate(inverse, axis=0)
            o_ref[:, lanes] = acc.T.astype(jnp.bfloat16)

    for span in range(size):
        pl.when(mine == span)(functools.partial(one, span))

    def project_out(step):
        for part, w_ref in enumerate((wo_ref, wx_ref)):
            lanes = slice(part * half, (part + 1) * half)
            product = mm_nt(o_ref[...], w_ref[...]).astype(jnp.bfloat16)
            store_partner(part_refs, step, lanes, product)

    for step in range(size):
        pl.when(pl.program_id(0) == step)(functools.partial(project_out, step))


def attend(me, query, key_pad, value_pad, own, other, size, group):
    total, width = query.shape
    features = 2 * own.shape[0]
    rows, heads = total // size, width // HEAD_DIM
    whole = pl.BlockSpec(key_pad.shape, lambda p, m: (0, 0, 0, 0), pipeline_mode=ONCE)
    spec = pltpu.PrefetchScalarGridSpec(
        num_scalar_prefetch=1,
        grid=(size,),
        in_specs=[pl.BlockSpec((rows, width), lambda p, m: (p, 0)), whole, whole]
        + [pl.BlockSpec(own.shape, lambda p, m: (0, 0), pipeline_mode=ONCE)] * 2,
        out_specs=[
            pl.BlockSpec((rows, width), lambda p, m: (p, 0)),
            pl.BlockSpec((heads, rows), lambda p, m: (0, p)),
        ]
        + [pl.BlockSpec((r, features), lambda p, m: (0, 0)) for r in partner_rows(size, rows)],
        scratch_shapes=[pltpu.VMEM((heads // group, 2, PAIR, total), jnp.bfloat16)],
    )
    return pl.pallas_call(
        functools.partial(attend_kernel, size=size, heads=heads, group=group),
        grid_spec=spec,
        out_shape=[
            jax.ShapeDtypeStruct((total, width), jnp.bfloat16),
            jax.ShapeDtypeStruct((heads, total), jnp.float32),
        ]
        + [jax.ShapeDtypeStruct((r, features), jnp.bfloat16) for r in partner_rows(size, rows)],
        compiler_params=PARAMS,
        cost_estimate=hint(8 * heads * total * total * HEAD_DIM // 16),
    )(me, query, key_pad, value_pad, own, other)


def attend_back_kernel(
    me_ref, q_ref, l_ref, k_ref, v_ref, cos_ref, sin_ref, *refs, size, heads, group
):
    do_refs = refs[:size]
    out_ref, dk_ref, dv_ref, kt_ref, do_ref = refs[size:]
    rows = q_ref.shape[0]
    key_heads = heads // group
    step = pl.program_id(0)
    me = me_ref[0]
    mine = jnp.bitwise_xor(me, step)
    key_place = lax.broadcasted_iota(jnp.int32, (rows, rows), 0)
    query_place = lax.broadcasted_iota(jnp.int32, (rows, rows), 1)

    def rows_of(block):
        return pl.ds(pl.multiple_of(block * rows, rows), rows)

    @pl.when(step == 0)
    def _():
        dk_ref[...] = jnp.zeros_like(dk_ref)
        dv_ref[...] = jnp.zeros_like(dv_ref)
        for head in range(key_heads):
            for side in range(2):
                kt_ref[head, side] = k_ref[head, side].T

    def fetch(ref):
        do_ref[...] = ref[...]

    for block in range(size):
        pl.when(step == block)(functools.partial(fetch, do_refs[block]))

    def one(span):
        keys = span * rows
        parts = [(keys, keys + rows, True)] + ([(0, keys, False)] if span else [])
        cosine, sine = cos_ref[keys : keys + rows, :], sin_ref[keys : keys + rows, :]
        for pair in range(heads // 2):
            head = 2 * pair // group
            lanes = slice(pair * PAIR, (pair + 1) * PAIR)
            query, grad = q_ref[:, lanes], do_ref[:, lanes]
            acc = None
            for side in range(2):
                log_total = l_ref[2 * pair + side : 2 * pair + side + 1, :]
                inner = None
                kept = []
                for low, high, diagonal in parts:
                    probs = mm_nt(k_ref[head, side, low:high, :], query)
                    probs = jnp.exp(probs - log_total)
                    if diagonal:
                        probs = jnp.where(key_place <= query_place, probs, 0.0)
                    prob_grad = mm_nt(v_ref[head, side, low:high, :], grad)
                    dv_ref[head, side, low:high, :] += mm(probs.astype(jnp.bfloat16), grad)
                    term = jnp.sum(probs * prob_grad, axis=0, keepdims=True)
                    inner = term if inner is None else inner + term
                    kept.append((low, high, probs, prob_grad))
                for low, high, probs, prob_grad in kept:
                    score_grad = (probs * (prob_grad - inner)).astype(jnp.bfloat16)
                    dk_ref[head, side, low:high, :] += mm(score_grad, query)
                    part = mm(kt_ref[head, side, :, low:high], score_grad)
                    acc = part if acc is None else acc + part
            turned = turn(acc.T * SCALE, cosine, -sine)
            out_ref[rows_of(step), lanes] = turned.astype(jnp.bfloat16)

    for span in range(size):
        pl.when(mine == span)(functools.partial(one, span))

    @pl.when(step == size - 1)
    def _():
        first = lane_index(rows) < HEAD_DIM
        wanted = [(dk_ref, head, True) for head in range(key_heads)]
        wanted += [(dv_ref, head, False) for head in range(key_heads)]
        for span in range(size):
            place = slice(span * rows, (span + 1) * rows)
            cosine, sine = cos_ref[place, :], sin_ref[place, :]
            for block in range(len(wanted) // 2):
                halves, rotate = [], []
                for half in range(2):
                    ref, head, is_key = wanted[2 * block + half]
                    low, high = ref[head, 0, place, :], ref[head, 1, place, :]
                    if half:
                        halves.append(pltpu.roll(low, HEAD_DIM, 1) + high)
                    else:
                        halves.append(low + pltpu.roll(high, HEAD_DIM, 1))
                    rotate.append(is_key)
                value = jnp.where(first, halves[0], halves[1])
                if rotate[0] and rotate[1]:
                    value = turn(value, cosine, -sine)
                elif rotate[0]:
                    value = jnp.where(first, turn(value, cosine, -sine), value)
                start = heads * HEAD_DIM + block * PAIR
                target = rows_of(jnp.bitwise_xor(me, span))
                out_ref[target, start : start + PAIR] = value.astype(jnp.bfloat16)


def attend_back(
    me, query, log_total, key_pad, value_pad, cosine, sine, attended_grad, group
):
    total, width = query.shape
    size = len(attended_grad)
    rows, heads = total // size, width // HEAD_DIM
    key_heads = heads // group
    out_width = width + 2 * key_heads * HEAD_DIM
    whole = pl.BlockSpec(key_pad.shape, lambda p, m: (0, 0, 0, 0), pipeline_mode=ONCE)
    table = pl.BlockSpec((total, PAIR), lambda p, m: (0, 0), pipeline_mode=ONCE)
    spec = pltpu.PrefetchScalarGridSpec(
        num_scalar_prefetch=1,
        grid=(size,),
        in_specs=[
            pl.BlockSpec((rows, width), lambda p, m: (p, 0)),
            pl.BlockSpec((heads, rows), lambda p, m: (0, p)),
            whole,
            whole,
            table,
            table,
        ]
        + [pl.BlockSpec((rows, width), lambda p, m: (0, 0), pipeline_mode=ONCE)] * size,
        out_specs=pl.BlockSpec((total, out_width), lambda p, m: (0, 0)),
        scratch_shapes=[
            pltpu.VMEM(key_pad.shape, jnp.float32),
            pltpu.VMEM(key_pad.shape, jnp.float32),
            pltpu.VMEM((key_heads, 2, PAIR, total), jnp.bfloat16),
            pltpu.VMEM((rows, width), jnp.bfloat16),
        ],
    )
    return pl.pallas_call(
        functools.partial(attend_back_kernel, size=size, heads=heads, group=group),
        grid_spec=spec,
        out_shape=jax.ShapeDtypeStruct((total, out_width), jnp.bfloat16),
        compiler_params=PARAMS,
        cost_estimate=hint(20 * heads * total * total * HEAD_DIM),
    )(me, query, log_total, key_pad, value_pad, cosine, sine, *attended_grad)


def grouped(arrays, counts):
    arrays = iter(arrays)
    return [[next(arrays) for _ in range(count)] for count in counts]


def mlp_kernel(*refs, n_counts, e_counts, adds):
    size = len(n_counts)
    pieces = sum(n_counts) + sum(e_counts)
    n_refs = grouped(refs, n_counts)
    e_refs = grouped(refs[sum(n_counts) :], e_counts)
    gate_o, up_o, down_o, gate_x, up_x, down_x = refs[pieces : pieces + 6]
    y_ref, n_ref, e_ref = refs[-3:]
    dn_count = len(partner_rows(size, n_ref.shape[0])) if adds else 1
    dn_refs = refs[-3 - dn_count : -3]
    dg_ref, du_ref, h_ref = refs[-6 - dn_count :][:3]
    half = gate_o.shape[0]

    def fetch(step):
        for target, sources in ((n_ref, n_refs[step]), (e_ref, e_refs[step])):
            low = 0
            for source in sources:
                high = low + source.shape[0]
                target[low:high] = source[...]
                low = high

    for step in range(size):
        pl.when(pl.program_id(0) == step)(functools.partial(fetch, step))
    gate = mm(n_ref[:, :half], gate_o[...]) + mm(n_ref[:, half:], gate_x[...])
    up = mm(n_ref[:, :half], up_o[...]) + mm(n_ref[:, half:], up_x[...])
    grad = mm(e_ref[:, :half], down_o[...]) + mm(e_ref[:, half:], down_x[...])
    sigma = jax.nn.sigmoid(gate)
    silu = gate * sigma
    hidden = (silu * up).astype(jnp.bfloat16)
    gate_grad = (grad * up * sigma * (1.0 + gate * (1.0 - sigma))).astype(jnp.bfloat16)
    up_grad = (grad * silu).astype(jnp.bfloat16)
    dg_ref[...] = gate_grad
    du_ref[...] = up_grad
    h_ref[...] = hidden
    for part, gate_w, up_w, down_w in ((0, gate_o, up_o, down_o), (1, gate_x, up_x, down_x)):
        lanes = slice(part * half, (part + 1) * half)
        dn = mm_nt(gate_grad, gate_w[...]) + mm_nt(up_grad, up_w[...])
        y = mm_nt(hidden, down_w[...])
        if adds:
            dn = dn + refs[pieces + 6][:, lanes].astype(jnp.float32)
            y = y + refs[pieces + 7][:, lanes].astype(jnp.float32)
        y_ref[:, lanes] = y.astype(jnp.bfloat16)
        dn = dn.astype(jnp.bfloat16)

        if adds:
            for step in range(size):
                pl.when(pl.program_id(0) == step)(
                    functools.partial(store_partner, dn_refs, step, lanes, dn)
                )
        else:
            dn_refs[0][:, lanes] = dn


def mlp(tokens, cot, own, other, earlier):
    size = len(tokens)
    rows, features = tokens[0][0].shape
    half, units = own.shape[0], own.shape[1] // 3
    total = rows * size
    fixed = lambda p: (0, 0)
    moving = lambda p: (p, 0)
    wide = pl.BlockSpec((rows, features), moving)
    sums = jax.ShapeDtypeStruct((total, features), jnp.bfloat16)
    dn_specs, dn_shapes = [wide], [sums]
    if earlier:
        counts = partner_rows(size, rows)
        dn_specs = [pl.BlockSpec((r, features), fixed) for r in counts]
        dn_shapes = [jax.ShapeDtypeStruct((r, features), jnp.bfloat16) for r in counts]
    pieces = sum(tokens, []) + sum(cot, [])
    thirds = [
        pl.BlockSpec((half, units), lambda p, t=t: (0, t), pipeline_mode=ONCE) for t in range(3)
    ]
    return pl.pallas_call(
        functools.partial(
            mlp_kernel,
            n_counts=[len(group) for group in tokens],
            e_counts=[len(group) for group in cot],
            adds=bool(earlier),
        ),
        grid=(size,),
        in_specs=[pl.BlockSpec(piece.shape, fixed, pipeline_mode=ONCE) for piece in pieces]
        + thirds * 2
        + [wide] * len(earlier),
        out_specs=[pl.BlockSpec((rows, units), moving)] * 3 + dn_specs + [wide],
        out_shape=[jax.ShapeDtypeStruct((total, units), jnp.bfloat16)] * 3 + dn_shapes + [sums],
        scratch_shapes=[pltpu.VMEM((rows, features), jnp.bfloat16)] * 2,
        compiler_params=PARAMS,
        cost_estimate=hint(12 * total * features * units),
    )(*pieces, own, own, own, other, other, other, *earlier)


def add_refs(refs):
    total = refs[0][...].astype(jnp.float32)
    for ref in refs[1:]:
        total = total + ref[...].astype(jnp.float32)
    return total


def store_by_device(out_ref, values, core, chips):
    width = values.shape[1] // (2 * chips)
    for chip in range(chips):
        own = values[:, chip * width : (chip + 1) * width]
        other = values[:, (chips + chip) * width : (chips + chip + 1) * width]
        low = 2 * chip * width
        out_ref[:, low : low + width] = jnp.where(core == 0, own, other)
        out_ref[:, low + width : low + 2 * width] = jnp.where(core == 0, other, own)


def middle_kernel(*refs):
    x_ref, gain_ref, middle_ref, normed_ref = refs[-4:]
    values = x_ref[...].astype(jnp.float32) + add_refs(refs[:-4])
    middle_ref[...] = values
    normed_ref[...] = (values * rms_scale(values) * gain_ref[...]).astype(jnp.bfloat16)


def input_back_kernel(core_ref, *refs, chips):
    x_ref, before_ref, gain_ref, out_ref = refs[-4:]
    values = x_ref[...].astype(jnp.float32)
    inner = add_refs(refs[:-4]) * gain_ref[...]
    scale = rms_scale(values)
    mean = jnp.mean(inner * values, axis=-1, keepdims=True)
    result = before_ref[...] + scale * inner - values * (scale * scale * scale) * mean
    store_by_device(out_ref, result, core_ref[0], chips)


def output_kernel(core_ref, *refs, chips):
    middle_ref, out_ref = refs[-2:]
    values = middle_ref[...] + add_refs(refs[:-2])
    store_by_device(out_ref, values.astype(jnp.bfloat16), core_ref[0], chips)


def row_call(body, dtypes, arrays, core=None):
    rows, features = arrays[0].shape
    steps = 2
    wide = pl.BlockSpec((rows // steps, features), lambda i, *_: (i, 0))
    row = pl.BlockSpec((1, features), lambda i, *_: (0, 0))
    scalars = [] if core is None else [jnp.full((1,), core, jnp.int32)]
    return pl.pallas_call(
        body,
        grid_spec=pltpu.PrefetchScalarGridSpec(
            num_scalar_prefetch=len(scalars),
            grid=(steps,),
            in_specs=[row if array.shape[0] == 1 else wide for array in arrays],
            out_specs=[wide] * len(dtypes),
        ),
        out_shape=[jax.ShapeDtypeStruct((rows, features), dtype) for dtype in dtypes],
        compiler_params=PARAMS,
        cost_estimate=hint(0),
    )(*scalars, *arrays)


def unpack_kernel(sum_ref, q_ref, k_ref, v_ref, out_ref):
    q_width, kv_width = q_ref.shape[1], k_ref.shape[1]
    values = sum_ref[...].astype(jnp.float32)
    q_ref[...] = values[:, :q_width]
    kv = values[:, q_width : q_width + 2 * kv_width]
    k_ref[...] = kv[:, :kv_width]
    v_ref[...] = kv[:, kv_width:]
    out_ref[...] = values[:, q_width + 2 * kv_width :].T


def unpack(sums, q_width, kv_width):
    rows = sums.shape[0]
    widths = [(rows, q_width), (rows, kv_width), (rows, kv_width), (q_width, rows)]
    return pl.pallas_call(
        unpack_kernel,
        out_shape=[jax.ShapeDtypeStruct(shape, jnp.float32) for shape in widths],
        compiler_params=PARAMS,
        cost_estimate=hint(0),
    )(sums)


def unpack_shares_kernel(one_ref, two_ref, gate_ref, up_ref, down_ref):
    units = one_ref.shape[1] // 3
    for part, ref in enumerate((one_ref, two_ref)):
        cut = slice(part * units, (part + 1) * units)
        gate_ref[:, cut] = ref[:, :units].astype(jnp.float32)
        up_ref[:, cut] = ref[:, units : 2 * units].astype(jnp.float32)
        down_ref[cut, :] = ref[:, 2 * units :].astype(jnp.float32).T


def unpack_shares(one, two):
    rows, width = one.shape
    units = 2 * width // 3
    shapes = [(rows, units), (rows, units), (units, rows)]
    return pl.pallas_call(
        unpack_shares_kernel,
        out_shape=[jax.ShapeDtypeStruct(shape, jnp.float32) for shape in shapes],
        compiler_params=PARAMS,
        cost_estimate=hint(0),
    )(one, two)


def middle_back_kernel(*refs, parts, size):
    n_refs, refs = refs[:parts], refs[parts:]
    x_ref, e_ref, gain_ref, refs = refs[0], refs[1], refs[2], refs[3:]
    own_refs, other_refs, refs = refs[:size], refs[size : 2 * size], refs[2 * size :]
    grad_ref, branch_ref, part_ref, do_refs = refs[0], refs[1], refs[2], refs[3:]
    half = own_refs[0].shape[0]
    grad = add_refs(n_refs)
    values = x_ref[...]
    scale = rms_scale(values)
    result, part = norm_back(grad, values, scale, gain_ref[...])

    @pl.when(pl.program_id(0) == 0)
    def _():
        part_ref[...] = jnp.zeros_like(part_ref)

    part_ref[...] += part[None, :]
    result = result + e_ref[...].astype(jnp.float32)
    grad_ref[...] = result
    branch = result.astype(jnp.bfloat16)
    branch_ref[...] = branch
    for own, other, do_ref in zip(own_refs, other_refs, do_refs):
        do = mm(branch[:, :half], own[...]) + mm(branch[:, half:], other[...])
        do_ref[...] = do.astype(jnp.bfloat16)


def middle_back(arrived, middle, cot, gain, own, other):
    parts, size = len(arrived), len(own)
    rows, features = middle.shape
    width = own[0].shape[1]
    steps = 2
    wide = pl.BlockSpec((rows // steps, features), lambda i: (i, 0))
    narrow = pl.BlockSpec((rows // steps, width), lambda i: (i, 0))
    row = pl.BlockSpec((1, features), lambda i: (0, 0))
    weight = pl.BlockSpec((features // 2, width), lambda i: (0, 0), pipeline_mode=ONCE)
    grad, branch, part, *do = pl.pallas_call(
        functools.partial(middle_back_kernel, parts=parts, size=size),
        grid=(steps,),
        in_specs=[wide] * parts + [wide, wide, row] + [weight] * (2 * size),
        out_specs=[wide, wide, row] + [narrow] * size,
        out_shape=[
            jax.ShapeDtypeStruct((rows, features), jnp.float32),
            jax.ShapeDtypeStruct((rows, features), jnp.bfloat16),
            jax.ShapeDtypeStruct((1, features), jnp.float32),
        ]
        + [jax.ShapeDtypeStruct((rows, width), jnp.bfloat16)] * size,
        compiler_params=PARAMS,
        cost_estimate=hint(2 * rows * features * width * size),
    )(*arrived, middle, cot, gain, *own, *other)
    return grad, branch, part[0], do


def column_grad(blocks, other, mine, theirs):
    total = mm_tn(other[...], theirs[...])
    low = 0
    for block in blocks:
        high = low + block.shape[0]
        total = total + mm_tn(block[...], mine[low:high, :])
        low = high
    return total


def grad_kernel(*refs, n_count, e_count):
    n_refs, refs = refs[:n_count], refs[n_count:]
    e_refs, refs = refs[:e_count], refs[e_count:]
    n_other, e_other = refs[:2]
    acts, out_ref = refs[2:-1], refs[-1]
    units = acts[0].shape[1]
    for third in range(3):
        blocks, other = (e_refs, e_other) if third == 2 else (n_refs, n_other)
        grad = column_grad(blocks, other, acts[third], acts[third + 3])
        out_ref[0, :, third * units : (third + 1) * units] = grad.astype(jnp.bfloat16)


def mlp_grads(chips, tokens, cot, tokens_other, cot_other, mine, theirs):
    tokens, cot = sum(tokens, []), sum(cot, [])
    features = tokens[0].shape[1]
    total, units = mine[0].shape
    depth = features // (2 * chips)
    long = pl.BlockSpec((total, depth), lambda b: (0, b))
    fixed = pl.BlockSpec((total, units), lambda b: (0, 0), pipeline_mode=ONCE)
    return pl.pallas_call(
        functools.partial(grad_kernel, n_count=len(tokens), e_count=len(cot)),
        grid=(chips,),
        in_specs=[pl.BlockSpec((p.shape[0], depth), lambda b: (0, b)) for p in tokens + cot]
        + [long, long]
        + [fixed] * 6,
        out_specs=pl.BlockSpec((1, depth, 3 * units), lambda b: (b, 0, 0)),
        out_shape=jax.ShapeDtypeStruct((chips, depth, 3 * units), jnp.bfloat16),
        compiler_params=PARAMS,
        cost_estimate=hint(6 * total * features * units),
    )(*tokens, *cot, tokens_other, cot_other, *mine, *theirs)


def attn_grad_kernel(*refs, size):
    e_refs = refs[2 : 2 + size]
    n_ref, n_other = refs[:2]
    e_other, d_ref, d_other, o_ref, o_other, q_ref, kv_ref, g1_ref, g2_ref = refs[2 + size : -2]
    out_ref, gain_ref = refs[-2:]
    width, out_width = d_ref.shape[1], o_ref.shape[1]
    grad = column_grad([n_ref], n_other, d_ref, d_other)
    out_ref[0, :, :width] = grad.astype(jnp.bfloat16)
    out_grad = column_grad(e_refs, e_other, o_ref, o_other)
    out_ref[0, :, width : width + out_width] = out_grad.astype(jnp.bfloat16)
    cut = q_ref.shape[1]
    first = jnp.sum(grad[:, :cut] * q_ref[...].astype(jnp.float32), axis=1, keepdims=True)
    first += jnp.sum(grad[:, cut:] * kv_ref[...].astype(jnp.float32), axis=1, keepdims=True)
    first = first / g1_ref[...]
    lane = lane_index(grad.shape[0])
    gain_ref[0] = jnp.where(lane == 0, first, g2_ref[...])


def attn_grads(
    chips, tokens, branch, mine, theirs, weights, columns, gain_one, gain_two_part
):
    size = len(branch)
    qkv_grad, attended = mine
    tokens_other, branch_other, qkv_other, attended_other = theirs
    total, features = tokens.shape
    rows = total // size
    width, out_width = qkv_grad.shape[1], attended.shape[1]
    depth = features // (2 * chips)
    column = lambda b: (0, b)
    row = lambda b: (b, 0)
    long = pl.BlockSpec((total, depth), column)
    fixed = lambda array: pl.BlockSpec(array.shape, lambda b: (0, 0), pipeline_mode=ONCE)
    place = lambda b: (b, 0, 0)
    return pl.pallas_call(
        functools.partial(attn_grad_kernel, size=size),
        grid=(chips,),
        in_specs=[long, long]
        + [pl.BlockSpec((rows, depth), column)] * size
        + [long]
        + [fixed(qkv_grad)] * 2
        + [fixed(attended)] * 2
        + [
            columns.spec("q", depth, lambda b=None: b),
            columns.spec("kv", depth, lambda b=None: b),
            pl.BlockSpec((depth, 1), row),
            pl.BlockSpec((depth, 1), row),
        ],
        out_specs=[
            pl.BlockSpec((1, depth, width + out_width), place),
            pl.BlockSpec((1, depth, PAIR), place),
        ],
        out_shape=[
            jax.ShapeDtypeStruct((chips, depth, width + out_width), jnp.bfloat16),
            jax.ShapeDtypeStruct((chips, depth, PAIR), jnp.float32),
        ],
        compiler_params=PARAMS,
        cost_estimate=hint(2 * total * features * (width + out_width)),
    )(
        tokens,
        tokens_other,
        *branch,
        branch_other,
        qkv_grad,
        qkv_other,
        attended,
        attended_other,
        weights,
        weights,
        gain_one,
        gain_two_part,
    )


def input_grad_kernel(d_ref, qo_ref, qx_ref, kvo_ref, kvx_ref, *out_refs, size):
    half, cut = qo_ref.shape

    def one(step):
        query, rest = d_ref[:, :cut], d_ref[:, cut:]
        for part, (q_ref, kv_ref) in enumerate(((qo_ref, kvo_ref), (qx_ref, kvx_ref))):
            lanes = slice(part * half, (part + 1) * half)
            product = mm_nt(query, q_ref[...]) + mm_nt(rest, kv_ref[...])
            store_partner(out_refs, step, lanes, product.astype(jnp.bfloat16))

    for step in range(size):
        pl.when(pl.program_id(0) == step)(functools.partial(one, step))


def input_grad(qkv_grad, own, other, columns, size):
    total, width = qkv_grad.shape
    features = 2 * own.shape[0]
    rows = total // size
    fixed = lambda i: (0, 0)
    weights = [columns.spec(part, own.shape[0]) for part in ("q", "q", "kv", "kv")]
    return pl.pallas_call(
        functools.partial(input_grad_kernel, size=size),
        grid=(size,),
        in_specs=[pl.BlockSpec((rows, width), lambda i: (i, 0))] + weights,
        out_specs=[pl.BlockSpec((r, features), fixed) for r in partner_rows(size, rows)],
        out_shape=[
            jax.ShapeDtypeStruct((r, features), jnp.bfloat16) for r in partner_rows(size, rows)
        ],
        compiler_params=PARAMS,
        cost_estimate=hint(2 * total * features * width),
    )(qkv_grad, own, other, own, other)


def swap(values, step):
    size = lax.axis_size("tensor")
    return lax.ppermute(values, "tensor", [(i, i ^ step) for i in range(size)])


def spread(values):
    return [values] + [swap(values, step) for step in range(1, lax.axis_size("tensor"))]


def send_blocks(blocks):
    return [blocks[0]] + [swap(block, step + 1) for step, block in enumerate(blocks[1:])]


def spread_around(values, held):
    if lax.axis_size("tensor") != 4:
        blocks = spread(values)
        first, held = barrier((blocks[1], held))
        return [[blocks[0]], [first]] + [[block] for block in blocks[2:]], held
    half = values.shape[0] // 2
    top, bottom = values[:half], values[half:]
    x_bottom, y_top = swap(bottom, 1), swap(top, 2)
    x_bottom, y_top, top, bottom, held = barrier((x_bottom, y_top, top, bottom, held))
    far = [swap(y_top, 1), swap(x_bottom, 2)]
    x_top, y_bottom = swap(top, 1), swap(bottom, 2)
    return [[values], [x_top, x_bottom], [y_top, y_bottom], far], held


def merge_kernel(x_ref, y_ref, top_ref, bottom_ref, x_out, y_out):
    half = top_ref.shape[0]
    x_out[:half] = x_ref[:half]
    x_out[half:] = add_refs([x_ref.at[half:], bottom_ref]).astype(jnp.bfloat16)
    y_out[:half] = add_refs([y_ref.at[:half], top_ref]).astype(jnp.bfloat16)
    y_out[half:] = y_ref[half:]


def send_sum(blocks, held=()):
    if lax.axis_size("tensor") != 4:
        return send_blocks(blocks), held
    own, near_x, near_y, top, bottom = blocks
    top, bottom = swap(top, 1), swap(bottom, 2)
    near_x, near_y = pl.pallas_call(
        merge_kernel,
        out_shape=[jax.ShapeDtypeStruct(near_x.shape, near_x.dtype)] * 2,
        compiler_params=PARAMS,
        cost_estimate=hint(0),
    )(near_x, near_y, top, bottom)
    near_x, near_y, held = barrier((near_x, near_y, held))
    return [own, swap(near_x, 1), swap(near_y, 2)], held


def add_up(blocks):
    total = blocks[0].astype(jnp.float32)
    for block in blocks[1:]:
        total = total + block.astype(jnp.float32)
    return total


def cross(values):
    count = lax.axis_size("dp")
    return lax.ppermute(values, "dp", [(i, i ^ 1) for i in range(count)])


def tables(positions):
    freqs = ROPE_BASE ** (-jnp.arange(0, HEAD_DIM, 2).astype(jnp.float32) / HEAD_DIM)
    angles = positions.astype(jnp.float32)[:, None] * freqs[None, :]
    cosine, sine = jnp.cos(angles), jnp.sin(angles)
    return (
        jnp.concatenate([cosine] * 4, axis=1),
        jnp.concatenate([-sine, sine, -sine, sine], axis=1),
    )


def chip_lines():
    count = lax.axis_size("dp")
    return [list(range(core, count, 2)) for core in range(2)]


def gather(values):
    return lax.all_gather(values, "dp", axis=0, tiled=True, axis_index_groups=chip_lines())


def scatter(values):
    total = lax.psum_scatter(
        values, "dp", scatter_dimension=0, tiled=True, axis_index_groups=chip_lines()
    )
    return total[0]


def along(values, step):
    count = lax.axis_size("dp")
    return lax.ppermute(values, "dp", [(i, (i + 2 * step) % count) for i in range(count)])


def line_order(blocks):
    chips = len(blocks)
    chip = lax.axis_index("dp") // 2
    placed = jnp.zeros((chips,) + blocks[0].shape, blocks[0].dtype)
    for step, block in enumerate(blocks):
        placed = lax.dynamic_update_index_in_dim(placed, block, (chip - step) % chips, 0)
    return placed.reshape((-1,) + blocks[0].shape[1:])


def line_parts(parts):
    chips = lax.axis_size("dp") // 2
    chip = lax.axis_index("dp") // 2
    blocks = [lax.dynamic_index_in_dim(parts, chip, 0, keepdims=False)]
    for step in range(1, chips):
        sent = lax.dynamic_index_in_dim(parts, (chip + step) % chips, 0, keepdims=False)
        blocks.append(along(sent, step))
    return blocks


def own_part(values):
    size = lax.axis_size("tensor")
    me = lax.axis_index("tensor")
    blocks = values.reshape((size, -1) + values.shape[1:])
    own = lax.dynamic_index_in_dim(blocks, me, 0, keepdims=False)
    for step in range(1, size):
        sent = lax.dynamic_index_in_dim(blocks, me ^ step, 0, keepdims=False)
        own = own + swap(sent, step)
    return own


def stack_kernel(*refs):
    low = 0
    for ref in refs[:-1]:
        high = low + ref.shape[0]
        refs[-1][low:high, :] = ref[...]
        low = high


def other_half(blocks):
    features = blocks[0].shape[1]
    shape = (sum(block.shape[0] for block in blocks), features // 2)
    halves = pl.pallas_call(
        stack_kernel,
        grid=(1,),
        in_specs=[pl.BlockSpec((b.shape[0], features // 2), lambda i: (0, 1)) for b in blocks],
        out_specs=pl.BlockSpec(shape, lambda i: (0, 0)),
        out_shape=jax.ShapeDtypeStruct(shape, blocks[0].dtype),
        compiler_params=PARAMS,
        cost_estimate=hint(0),
    )(*blocks)
    return cross(halves)


def feature_blocks(values):
    width = values.shape[-1] // lax.axis_size("dp")
    return [values[..., low : low + width] for low in range(0, values.shape[-1], width)]


def by_core(values, core):
    blocks = feature_blocks(values)
    pairs = list(zip(blocks[0::2], blocks[1::2]))
    own = [jnp.where(core == 0, even, odd) for even, odd in pairs]
    other = [jnp.where(core == 0, odd, even) for even, odd in pairs]
    return jnp.concatenate(own + other, axis=-1)


def per_device(
    hidden_in,
    gain_attn,
    w_query,
    w_key,
    w_value,
    w_out,
    gain_mlp,
    w_gate,
    w_up,
    w_down,
    positions,
    cotangent,
):
    size = lax.axis_size("tensor")
    chips = lax.axis_size("dp") // 2
    me = lax.axis_index("tensor")
    me_array = jnp.full((1,), me, jnp.int32)
    core = lax.axis_index("dp") % 2
    q_width, kv_width = w_query.shape[1], w_key.shape[1]
    group = q_width // kv_width
    units = w_down.shape[0] // 2
    half = hidden_in.shape[1] // 2

    columns = Columns(q_width, kv_width)
    gain_shard = jnp.pad(jnp.stack([gain_attn, gain_mlp], axis=1), ((0, 0), (0, PAIR - 2)))
    qkv_shard = jnp.concatenate([w_query, w_key, w_value, gain_shard], axis=1)
    out_shard = w_out.T
    qkv_shard, out_shard, hidden_in = barrier((qkv_shard, out_shard, hidden_in))
    qkv_own = gather(qkv_shard)
    residual = by_core(hidden_in, core)
    early_in = [swap(residual, step) for step in range(1, 3)]
    early_out = [along(out_shard, step) for step in range(1, 3)]
    early_in, early_out, residual, out_shard = barrier(
        (early_in, early_out, residual, out_shard)
    )
    blocks_in = [residual] + early_in + [swap(residual, step) for step in range(3, size)]
    out_parts = [out_shard] + early_out + [along(out_shard, step) for step in range(3, chips)]
    cosine, sine = tables(positions)
    cotangent = by_core(cotangent, core)
    down_t = w_down.T
    shares = []
    for part in range(2):
        cut = slice(part * units, (part + 1) * units)
        shares.append(jnp.concatenate([w_gate[:, cut], w_up[:, cut], down_t[:, cut]], axis=1))
    shares, qkv_own, out_parts, blocks_in, cosine, sine, cotangent = barrier(
        (shares, qkv_own, out_parts, blocks_in, cosine, sine, cotangent)
    )
    mlp_own = [gather(share) for share in shares]
    cot_blocks = spread(cotangent)
    qkv = (qkv_own, cross(qkv_own))
    out_own = line_order(out_parts)
    out_t = (out_own, cross(out_own))

    tokens_one, query, key_pad, value_pad = project(
        me_array, blocks_in, *qkv, cosine, sine, columns
    )
    attended, log_total, *parts = attend(
        me_array, query, key_pad, value_pad, *out_t, size, group
    )
    parts, cot_blocks, tokens_one, attended = barrier((parts, cot_blocks, tokens_one, attended))
    arrived, _ = send_sum(parts)
    cot_other = other_half(cot_blocks)
    cot_blocks = [[block] for block in cot_blocks]
    early = (cross(tokens_one[:, half:]), cross(attended))
    arrived, cot_other, early = barrier((arrived, cot_other, early))
    gain_one, gain_two = [
        jnp.concatenate([w[:, columns.gain_start + index] for w in qkv]).astype(jnp.float32)
        for index in range(2)
    ]
    middle, normed_two = row_call(
        middle_kernel, [jnp.float32, jnp.bfloat16], [*arrived, residual, gain_two[None, :]]
    )
    tokens_two, own_share = spread_around(normed_two, mlp_own[0])
    weights = (own_share, cross(own_share))
    tokens_two, weights, out_own = barrier((tokens_two, weights, out_t[0]))
    tokens_other = other_half(sum(tokens_two, []))
    *acts, dn_part, y_part = mlp(tokens_two, cot_blocks, *weights, ())
    out_blocks = spread(out_own)
    acts, tokens_other = barrier((acts, tokens_other))
    acts_other = [cross(act) for act in acts]
    grads_one = mlp_grads(
        chips, tokens_two, cot_blocks, tokens_other, cot_other, acts, acts_other
    )
    grads_one, own_share = barrier((grads_one, mlp_own[1]))
    sums_one = scatter(grads_one)
    weights = (own_share, cross(own_share))
    *acts, y_part = mlp(tokens_two, cot_blocks, *weights, (dn_part, y_part))
    acts, dn_part = acts[:3], acts[3:]
    acts, dn_part, out_blocks = barrier((acts, dn_part, out_blocks))
    acts_other = [cross(act) for act in acts]
    arrived, acts = send_sum(dn_part, acts)
    out_other = [out_t[1]] + [cross(block) for block in out_blocks[1:]]
    grads_two = mlp_grads(
        chips, tokens_two, cot_blocks, tokens_other, cot_other, acts, acts_other
    )
    grads_two, arrived, out_other, y_part = barrier((grads_two, arrived, out_other, y_part))
    y_blocks = list(y_part.reshape((size, -1) + y_part.shape[1:]))
    y_early = [swap(y_blocks[step], step) for step in range(1, 3)]
    sums_two = scatter(grads_two)
    middle_grad, branch, gain_two_part, do_blocks = middle_back(
        arrived, middle, cotangent, gain_two[None, :], out_blocks, out_other
    )
    do_blocks = send_blocks(do_blocks)
    gain_two_other = cross(gain_two_part[half:])
    do_blocks, branch, gain_two_other, y_blocks, y_early = barrier(
        (do_blocks, branch, gain_two_other, y_blocks, y_early)
    )
    branch_blocks = spread(branch)
    qkv_grad = attend_back(
        me_array, query, log_total, key_pad, value_pad, cosine, sine, do_blocks, group
    )
    qkv_grad, sums_one = barrier((qkv_grad, sums_one))
    qkv_other = cross(qkv_grad)
    normed_part = input_grad(qkv_grad, *qkv, columns, size)
    branch_blocks, normed_part = barrier((branch_blocks, normed_part))
    branch_other = other_half(branch_blocks)
    tokens_other, attended_other = early
    grads, gain_parts = attn_grads(
        chips,
        tokens_one,
        branch_blocks,
        (qkv_grad, attended),
        (tokens_other, branch_other, qkv_other, attended_other),
        qkv_own,
        columns,
        gain_one[:half, None],
        (gain_two_part[:half] + gain_two_other)[:, None],
    )
    arrived, (grads, sums_two) = send_sum(normed_part, (grads, sums_two))
    attn_sums = scatter(grads)
    gain_sums = add_up(line_parts(gain_parts[:, :, :2]))
    unpacked = unpack_shares(sums_one, sums_two)
    arrived, y_blocks, unpacked, gain_sums = barrier((arrived, y_blocks, unpacked, gain_sums))
    grad_gate, grad_up, grad_down = unpacked
    y_late = [swap(y_blocks[step], step) for step in range(3, size)]
    (grad_in,) = row_call(
        functools.partial(input_back_kernel, chips=chips),
        [jnp.float32],
        [*arrived, residual, middle_grad, gain_one[None, :]],
        core,
    )
    grad_in, gain_sums = barrier((grad_in, gain_sums))
    gain_sums = own_part(gain_sums)
    y_late, grad_in, gain_sums = barrier((y_late, grad_in, gain_sums))
    (out,) = row_call(
        functools.partial(output_kernel, chips=chips),
        [jnp.bfloat16],
        [y_blocks[0], *y_early, *y_late, middle],
        core,
    )
    out, attn_sums = barrier((out, attn_sums))
    grad_query, grad_key, grad_value, grad_out = unpack(attn_sums, q_width, kv_width)
    return (
        out,
        grad_in,
        gain_sums[:, 0],
        grad_query,
        grad_key,
        grad_value,
        grad_out,
        gain_sums[:, 1],
        grad_gate,
        grad_up,
        grad_down,
    )


def solution(mesh):
    return jax.shard_map(
        per_device,
        mesh=mesh,
        in_specs=(
            P(("dp", "tensor"), None),
            P("dp"),
            P("dp", "tensor"),
            P("dp", "tensor"),
            P("dp", "tensor"),
            P("tensor", "dp"),
            P("dp"),
            P("dp", "tensor"),
            P("dp", "tensor"),
            P("tensor", "dp"),
            P("dp"),
            P(("dp", "tensor"), None),
        ),
        out_specs=(
            P(("dp", "tensor"), None),
            P(("dp", "tensor"), None),
            P(("dp", "tensor")),
            P("dp", "tensor"),
            P("dp", "tensor"),
            P("dp", "tensor"),
            P("tensor", "dp"),
            P(("dp", "tensor")),
            P("dp", "tensor"),
            P("dp", "tensor"),
            P("tensor", "dp"),
        ),
        check_vma=False,
    )
```

```python
import functools
import math

import jax
import jax.numpy as jnp
from jax import lax
from jax.experimental import pallas as pl
from jax.experimental.pallas import tpu as pltpu
from jax.sharding import PartitionSpec as P

HEAD_DIM = 64
PAIR = 2 * HEAD_DIM
SEQ_LEN = 1024


EPS = 1e-05
ROPE_BASE = 500000.0
SCALE = 1.0 / math.sqrt(HEAD_DIM)
PARAMS = pltpu.CompilerParams(vmem_limit_bytes=58 * 2**20)
ONCE = pl.Buffered(1)

barrier = lax.optimization_barrier


def hint(flops):
    return pl.CostEstimate(flops=flops, bytes_accessed=0, transcendentals=0)


def rms_scale(values):
    return lax.rsqrt(jnp.mean(values * values, axis=-1, keepdims=True) + EPS)


def norm_back(grad, values, scale, gain):
    inner = grad * gain
    cubed = scale * scale * scale
    result = scale * inner - values * cubed * jnp.mean(inner * values, axis=-1, keepdims=True)
    return (result, jnp.sum(grad * values * scale, axis=0))


def mm(left, right):
    return jnp.dot(left, right, preferred_element_type=jnp.float32)


def mm_nt(left, right):
    return lax.dot_general(left, right, (((1,), (1,)), ((), ())), preferred_element_type=jnp.float32)


def mm_tn(left, right):
    return lax.dot_general(left, right, (((0,), (0,)), ((), ())), preferred_element_type=jnp.float32)


def partner_rows(size, rows):
    return [rows] * 3 + [rows // 2] * 2 if size == 4 else [rows] * size


def store_partner(refs, step, lanes, value):
    if len(refs) == 5 and step == 3:
        half = refs[3].shape[0]
        refs[3][:, lanes] = value[:half]
        refs[4][:, lanes] = value[half:]
    else:
        refs[step][:, lanes] = value


def lane_index(rows):
    return lax.broadcasted_iota(jnp.int32, (rows, PAIR), 1)


def turn(pair, cosine, sine):
    lower = lane_index(pair.shape[0]) % HEAD_DIM < HEAD_DIM // 2
    other = jnp.where(
        lower, pltpu.roll(pair, PAIR - HEAD_DIM // 2, 1), pltpu.roll(pair, HEAD_DIM // 2, 1)
    )
    return pair * cosine + other * sine


def project_kernel(place_ref, *refs, size, q_width, kv_width):
    x_refs = refs[:size]
    go_ref, gx_ref, qo_ref, qx_ref, kvo_ref, kvx_ref, cos_ref, sin_ref = refs[size:-5]
    n_ref, q_ref, k_ref, v_ref, gain_ref = refs[-5:]
    rows = q_ref.shape[0]
    half = qo_ref.shape[0]

    @pl.when(pl.program_id(0) == 0)
    def _():
        gain_ref[:, :half] = go_ref[...].astype(jnp.float32).T[:1, :]
        gain_ref[:, half:] = gx_ref[...].astype(jnp.float32).T[:1, :]

    def one(x_ref):
        x = x_ref[...].astype(jnp.float32)
        normed = (x * rms_scale(x) * gain_ref[...]).astype(jnp.bfloat16)
        n_ref[...] = normed
        cosine, sine = cos_ref[...], sin_ref[...]
        own, other = normed[:, :half], normed[:, half:]
        lin = mm(own, qo_ref[...]) + mm(other, qx_ref[...])
        for low in range(0, q_width, PAIR):
            query = turn(lin[:, low : low + PAIR], cosine, sine).astype(jnp.bfloat16)
            q_ref[:, low : low + PAIR] = query * jnp.bfloat16(SCALE)
        lin = mm(own, kvo_ref[...]) + mm(other, kvx_ref[...])
        first = lane_index(rows) < HEAD_DIM
        for ref, start, rotate in ((k_ref, 0, True), (v_ref, kv_width, False)):
            for head in range(kv_width // HEAD_DIM):
                low = start + head * HEAD_DIM
                block = lin[:, low // PAIR * PAIR : low // PAIR * PAIR + PAIR]
                if rotate:
                    block = turn(block, cosine, sine)
                moved = pltpu.roll(block, HEAD_DIM, 1)
                if low % PAIR:
                    block, moved = moved, block
                ref[head, 0] = jnp.where(first, block, 0.0).astype(jnp.bfloat16)
                ref[head, 1] = jnp.where(first, 0.0, moved).astype(jnp.bfloat16)

    for step in range(size):
        pl.when(pl.program_id(0) == step)(functools.partial(one, x_refs[step]))


class Columns:
    def __init__(self, q_width, kv_width):
        self.q_width, self.kv_width = q_width, kv_width
        self.gain_start = q_width + 2 * kv_width

    def spec(self, part, rows, place=lambda *_: 0):
        width, start = {
            "q": (self.q_width, 0),
            "kv": (2 * self.kv_width, self.q_width),
            "gain": (PAIR, self.gain_start),
        }[part]
        index = start // width
        mode = {"pipeline_mode": ONCE} if place() == 0 else {}
        return pl.BlockSpec((rows, width), lambda *grid: (place(*grid), index), **mode)


def project(me, blocks, own, other, cosine, sine, columns):
    size = len(blocks)
    rows, features = blocks[0].shape
    total = rows * size
    q_width, kv_width = columns.q_width, columns.kv_width
    key_heads = kv_width // HEAD_DIM
    width = q_width + 2 * kv_width
    half = features // 2
    fixed = lambda p, m: (0, 0)
    placed = lambda p, m: (jnp.bitwise_xor(p, m[0]), 0)
    padded = pl.BlockSpec(
        (key_heads, 2, rows, PAIR), lambda p, m: (0, 0, jnp.bitwise_xor(p, m[0]), 0)
    )
    spec = pltpu.PrefetchScalarGridSpec(
        num_scalar_prefetch=1,
        grid=(size,),
        in_specs=[pl.BlockSpec((rows, features), fixed, pipeline_mode=ONCE)] * size
        + [
            columns.spec("gain", half),
            columns.spec("gain", half),
            columns.spec("q", half),
            columns.spec("q", half),
            columns.spec("kv", half),
            columns.spec("kv", half),
            pl.BlockSpec((rows, PAIR), placed),
            pl.BlockSpec((rows, PAIR), placed),
        ],
        out_specs=[
            pl.BlockSpec((rows, features), lambda p, m: (p, 0)),
            pl.BlockSpec((rows, q_width), lambda p, m: (p, 0)),
            padded,
            padded,
        ],
        scratch_shapes=[pltpu.VMEM((1, features), jnp.float32)],
    )
    padded_shape = jax.ShapeDtypeStruct((key_heads, 2, total, PAIR), jnp.bfloat16)
    return pl.pallas_call(
        functools.partial(project_kernel, size=size, q_width=q_width, kv_width=kv_width),
        grid_spec=spec,
        out_shape=[
            jax.ShapeDtypeStruct((total, features), jnp.bfloat16),
            jax.ShapeDtypeStruct((total, q_width), jnp.bfloat16),
            padded_shape,
            padded_shape,
        ],
        compiler_params=PARAMS,
        cost_estimate=hint(2 * total * features * width // 16),
    )(me, *blocks, own, other, own, other, own, other, cosine, sine)


def attend_kernel(
    me_ref, q_ref, k_ref, v_ref, wo_ref, wx_ref, o_ref, l_ref, *refs, size, heads, group
):
    part_refs, vt_ref = refs[:-1], refs[-1]
    rows = q_ref.shape[0]
    half = wo_ref.shape[0]
    mine = jnp.bitwise_xor(me_ref[0], pl.program_id(0))
    key_place = lax.broadcasted_iota(jnp.int32, (rows, rows), 0)
    query_place = lax.broadcasted_iota(jnp.int32, (rows, rows), 1)

    @pl.when(pl.program_id(0) == 0)
    def _():
        for head in range(heads // group):
            for side in range(2):
                vt_ref[head, side] = v_ref[head, side].T

    def one(span):
        keys = span * rows
        for pair in range(heads // 2):
            head = 2 * pair // group
            lanes = slice(pair * PAIR, (pair + 1) * PAIR)
            query = q_ref[:, lanes]
            acc = None
            inverse = []
            for side in range(2):
                diag = mm_nt(k_ref[head, side, keys : keys + rows, :], query)
                diag = jnp.where(key_place <= query_place, diag, -1e9)
                top = jnp.max(diag, axis=0, keepdims=True)
                if span:
                    body = mm_nt(k_ref[head, side, :keys, :], query)
                    top = jnp.maximum(top, jnp.max(body, axis=0, keepdims=True))
                diag = jnp.exp(diag - top)
                total = jnp.sum(diag, axis=0, keepdims=True)
                part = mm(vt_ref[head, side, :, keys : keys + rows], diag.astype(jnp.bfloat16))
                if span:
                    body = jnp.exp(body - top)
                    total = total + jnp.sum(body, axis=0, keepdims=True)
                    part = part + mm(vt_ref[head, side, :, :keys], body.astype(jnp.bfloat16))
                acc = part if acc is None else acc + part
                inverse.append(jnp.broadcast_to(1.0 / total, (HEAD_DIM, rows)))
                l_ref[2 * pair + side : 2 * pair + side + 1, :] = top + jnp.log(total)
            acc = acc * jnp.concatenate(inverse, axis=0)
            o_ref[:, lanes] = acc.T.astype(jnp.bfloat16)

    for span in range(size):
        pl.when(mine == span)(functools.partial(one, span))

    def project_out(step):
        for part, w_ref in enumerate((wo_ref, wx_ref)):
            lanes = slice(part * half, (part + 1) * half)
            product = mm_nt(o_ref[...], w_ref[...]).astype(jnp.bfloat16)
            store_partner(part_refs, step, lanes, product)

    for step in range(size):
        pl.when(pl.program_id(0) == step)(functools.partial(project_out, step))


def attend(me, query, key_pad, value_pad, own, other, size, group):
    total, width = query.shape
    features = 2 * own.shape[0]
    rows, heads = total // size, width // HEAD_DIM
    whole = pl.BlockSpec(key_pad.shape, lambda p, m: (0, 0, 0, 0), pipeline_mode=ONCE)
    spec = pltpu.PrefetchScalarGridSpec(
        num_scalar_prefetch=1,
        grid=(size,),
        in_specs=[pl.BlockSpec((rows, width), lambda p, m: (p, 0)), whole, whole]
        + [pl.BlockSpec(own.shape, lambda p, m: (0, 0), pipeline_mode=ONCE)] * 2,
        out_specs=[
            pl.BlockSpec((rows, width), lambda p, m: (p, 0)),
            pl.BlockSpec((heads, rows), lambda p, m: (0, p)),
        ]
        + [pl.BlockSpec((r, features), lambda p, m: (0, 0)) for r in partner_rows(size, rows)],
        scratch_shapes=[pltpu.VMEM((heads // group, 2, PAIR, total), jnp.bfloat16)],
    )
    return pl.pallas_call(
        functools.partial(attend_kernel, size=size, heads=heads, group=group),
        grid_spec=spec,
        out_shape=[
            jax.ShapeDtypeStruct((total, width), jnp.bfloat16),
            jax.ShapeDtypeStruct((heads, total), jnp.float32),
        ]
        + [jax.ShapeDtypeStruct((r, features), jnp.bfloat16) for r in partner_rows(size, rows)],
        compiler_params=PARAMS,
        cost_estimate=hint(8 * heads * total * total * HEAD_DIM // 16),
    )(me, query, key_pad, value_pad, own, other)


def attend_back_kernel(
    me_ref, q_ref, l_ref, k_ref, v_ref, cos_ref, sin_ref, *refs, size, heads, group
):
    do_refs = refs[:size]
    out_ref, dk_ref, dv_ref, kt_ref, do_ref = refs[size:]
    rows = q_ref.shape[0]
    key_heads = heads // group
    step = pl.program_id(0)
    me = me_ref[0]
    mine = jnp.bitwise_xor(me, step)
    key_place = lax.broadcasted_iota(jnp.int32, (rows, rows), 0)
    query_place = lax.broadcasted_iota(jnp.int32, (rows, rows), 1)

    def rows_of(block):
        return pl.ds(pl.multiple_of(block * rows, rows), rows)

    @pl.when(step == 0)
    def _():
        dk_ref[...] = jnp.zeros_like(dk_ref)
        dv_ref[...] = jnp.zeros_like(dv_ref)
        for head in range(key_heads):
            for side in range(2):
                kt_ref[head, side] = k_ref[head, side].T

    def fetch(ref):
        do_ref[...] = ref[...]

    for block in range(size):
        pl.when(step == block)(functools.partial(fetch, do_refs[block]))

    def one(span):
        keys = span * rows
        parts = [(keys, keys + rows, True)] + ([(0, keys, False)] if span else [])
        cosine, sine = cos_ref[keys : keys + rows, :], sin_ref[keys : keys + rows, :]
        for pair in range(heads // 2):
            head = 2 * pair // group
            lanes = slice(pair * PAIR, (pair + 1) * PAIR)
            query, grad = q_ref[:, lanes], do_ref[:, lanes]
            acc = None
            for side in range(2):
                log_total = l_ref[2 * pair + side : 2 * pair + side + 1, :]
                inner = None
                kept = []
                for low, high, diagonal in parts:
                    probs = mm_nt(k_ref[head, side, low:high, :], query)
                    probs = jnp.exp(probs - log_total)
                    if diagonal:
                        probs = jnp.where(key_place <= query_place, probs, 0.0)
                    prob_grad = mm_nt(v_ref[head, side, low:high, :], grad)
                    dv_ref[head, side, low:high, :] += mm(probs.astype(jnp.bfloat16), grad)
                    term = jnp.sum(probs * prob_grad, axis=0, keepdims=True)
                    inner = term if inner is None else inner + term
                    kept.append((low, high, probs, prob_grad))
                for low, high, probs, prob_grad in kept:
                    score_grad = (probs * (prob_grad - inner)).astype(jnp.bfloat16)
                    dk_ref[head, side, low:high, :] += mm(score_grad, query)
                    part = mm(kt_ref[head, side, :, low:high], score_grad)
                    acc = part if acc is None else acc + part
            turned = turn(acc.T * SCALE, cosine, -sine)
            out_ref[rows_of(step), lanes] = turned.astype(jnp.bfloat16)

    for span in range(size):
        pl.when(mine == span)(functools.partial(one, span))

    @pl.when(step == size - 1)
    def _():
        first = lane_index(rows) < HEAD_DIM
        wanted = [(dk_ref, head, True) for head in range(key_heads)]
        wanted += [(dv_ref, head, False) for head in range(key_heads)]
        for span in range(size):
            place = slice(span * rows, (span + 1) * rows)
            cosine, sine = cos_ref[place, :], sin_ref[place, :]
            for block in range(len(wanted) // 2):
                halves, rotate = [], []
                for half in range(2):
                    ref, head, is_key = wanted[2 * block + half]
                    low, high = ref[head, 0, place, :], ref[head, 1, place, :]
                    if half:
                        halves.append(pltpu.roll(low, HEAD_DIM, 1) + high)
                    else:
                        halves.append(low + pltpu.roll(high, HEAD_DIM, 1))
                    rotate.append(is_key)
                value = jnp.where(first, halves[0], halves[1])
                if rotate[0] and rotate[1]:
                    value = turn(value, cosine, -sine)
                elif rotate[0]:
                    value = jnp.where(first, turn(value, cosine, -sine), value)
                start = heads * HEAD_DIM + block * PAIR
                target = rows_of(jnp.bitwise_xor(me, span))
                out_ref[target, start : start + PAIR] = value.astype(jnp.bfloat16)


def attend_back(
    me, query, log_total, key_pad, value_pad, cosine, sine, attended_grad, group
):
    total, width = query.shape
    size = len(attended_grad)
    rows, heads = total // size, width // HEAD_DIM
    key_heads = heads // group
    out_width = width + 2 * key_heads * HEAD_DIM
    whole = pl.BlockSpec(key_pad.shape, lambda p, m: (0, 0, 0, 0), pipeline_mode=ONCE)
    table = pl.BlockSpec((total, PAIR), lambda p, m: (0, 0), pipeline_mode=ONCE)
    spec = pltpu.PrefetchScalarGridSpec(
        num_scalar_prefetch=1,
        grid=(size,),
        in_specs=[
            pl.BlockSpec((rows, width), lambda p, m: (p, 0)),
            pl.BlockSpec((heads, rows), lambda p, m: (0, p)),
            whole,
            whole,
            table,
            table,
        ]
        + [pl.BlockSpec((rows, width), lambda p, m: (0, 0), pipeline_mode=ONCE)] * size,
        out_specs=pl.BlockSpec((total, out_width), lambda p, m: (0, 0)),
        scratch_shapes=[
            pltpu.VMEM(key_pad.shape, jnp.float32),
            pltpu.VMEM(key_pad.shape, jnp.float32),
            pltpu.VMEM((key_heads, 2, PAIR, total), jnp.bfloat16),
            pltpu.VMEM((rows, width), jnp.bfloat16),
        ],
    )
    return pl.pallas_call(
        functools.partial(attend_back_kernel, size=size, heads=heads, group=group),
        grid_spec=spec,
        out_shape=jax.ShapeDtypeStruct((total, out_width), jnp.bfloat16),
        compiler_params=PARAMS,
        cost_estimate=hint(20 * heads * total * total * HEAD_DIM),
    )(me, query, log_total, key_pad, value_pad, cosine, sine, *attended_grad)


def grouped(arrays, counts):
    arrays = iter(arrays)
    return [[next(arrays) for _ in range(count)] for count in counts]


def mlp_kernel(*refs, n_counts, e_counts, adds):
    size = len(n_counts)
    pieces = sum(n_counts) + sum(e_counts)
    n_refs = grouped(refs, n_counts)
    e_refs = grouped(refs[sum(n_counts) :], e_counts)
    gate_o, up_o, down_o, gate_x, up_x, down_x = refs[pieces : pieces + 6]
    y_ref, n_ref, e_ref = refs[-3:]
    dn_count = len(partner_rows(size, n_ref.shape[0])) if adds else 1
    dn_refs = refs[-3 - dn_count : -3]
    dg_ref, du_ref, h_ref = refs[-6 - dn_count :][:3]
    half = gate_o.shape[0]

    def fetch(step):
        for target, sources in ((n_ref, n_refs[step]), (e_ref, e_refs[step])):
            low = 0
            for source in sources:
                high = low + source.shape[0]
                target[low:high] = source[...]
                low = high

    for step in range(size):
        pl.when(pl.program_id(0) == step)(functools.partial(fetch, step))
    gate = mm(n_ref[:, :half], gate_o[...]) + mm(n_ref[:, half:], gate_x[...])
    up = mm(n_ref[:, :half], up_o[...]) + mm(n_ref[:, half:], up_x[...])
    grad = mm(e_ref[:, :half], down_o[...]) + mm(e_ref[:, half:], down_x[...])
    sigma = jax.nn.sigmoid(gate)
    silu = gate * sigma
    hidden = (silu * up).astype(jnp.bfloat16)
    gate_grad = (grad * up * sigma * (1.0 + gate * (1.0 - sigma))).astype(jnp.bfloat16)
    up_grad = (grad * silu).astype(jnp.bfloat16)
    dg_ref[...] = gate_grad
    du_ref[...] = up_grad
    h_ref[...] = hidden
    for part, gate_w, up_w, down_w in ((0, gate_o, up_o, down_o), (1, gate_x, up_x, down_x)):
        lanes = slice(part * half, (part + 1) * half)
        dn = mm_nt(gate_grad, gate_w[...]) + mm_nt(up_grad, up_w[...])
        y = mm_nt(hidden, down_w[...])
        if adds:
            dn = dn + refs[pieces + 6][:, lanes].astype(jnp.float32)
            y = y + refs[pieces + 7][:, lanes].astype(jnp.float32)
        y_ref[:, lanes] = y.astype(jnp.bfloat16)
        dn = dn.astype(jnp.bfloat16)

        if adds:
            for step in range(size):
                pl.when(pl.program_id(0) == step)(
                    functools.partial(store_partner, dn_refs, step, lanes, dn)
                )
        else:
            dn_refs[0][:, lanes] = dn


def mlp(tokens, cot, own, other, earlier):
    size = len(tokens)
    rows, features = tokens[0][0].shape
    half, units = own.shape[0], own.shape[1] // 3
    total = rows * size
    fixed = lambda p: (0, 0)
    moving = lambda p: (p, 0)
    wide = pl.BlockSpec((rows, features), moving)
    sums = jax.ShapeDtypeStruct((total, features), jnp.bfloat16)
    dn_specs, dn_shapes = [wide], [sums]
    if earlier:
        counts = partner_rows(size, rows)
        dn_specs = [pl.BlockSpec((r, features), fixed) for r in counts]
        dn_shapes = [jax.ShapeDtypeStruct((r, features), jnp.bfloat16) for r in counts]
    pieces = sum(tokens, []) + sum(cot, [])
    thirds = [
        pl.BlockSpec((half, units), lambda p, t=t: (0, t), pipeline_mode=ONCE) for t in range(3)
    ]
    return pl.pallas_call(
        functools.partial(
            mlp_kernel,
            n_counts=[len(group) for group in tokens],
            e_counts=[len(group) for group in cot],
            adds=bool(earlier),
        ),
        grid=(size,),
        in_specs=[pl.BlockSpec(piece.shape, fixed, pipeline_mode=ONCE) for piece in pieces]
        + thirds * 2
        + [wide] * len(earlier),
        out_specs=[pl.BlockSpec((rows, units), moving)] * 3 + dn_specs + [wide],
        out_shape=[jax.ShapeDtypeStruct((total, units), jnp.bfloat16)] * 3 + dn_shapes + [sums],
        scratch_shapes=[pltpu.VMEM((rows, features), jnp.bfloat16)] * 2,
        compiler_params=PARAMS,
        cost_estimate=hint(12 * total * features * units),
    )(*pieces, own, own, own, other, other, other, *earlier)


def add_refs(refs):
    total = refs[0][...].astype(jnp.float32)
    for ref in refs[1:]:
        total = total + ref[...].astype(jnp.float32)
    return total


def store_by_device(out_ref, values, core, chips):
    width = values.shape[1] // (2 * chips)
    for chip in range(chips):
        own = values[:, chip * width : (chip + 1) * width]
        other = values[:, (chips + chip) * width : (chips + chip + 1) * width]
        low = 2 * chip * width
        out_ref[:, low : low + width] = jnp.where(core == 0, own, other)
        out_ref[:, low + width : low + 2 * width] = jnp.where(core == 0, other, own)


def middle_kernel(*refs):
    x_ref, gain_ref, middle_ref, normed_ref = refs[-4:]
    values = x_ref[...].astype(jnp.float32) + add_refs(refs[:-4])
    middle_ref[...] = values
    normed_ref[...] = (values * rms_scale(values) * gain_ref[...]).astype(jnp.bfloat16)


def input_back_kernel(core_ref, *refs, chips):
    x_ref, before_ref, gain_ref, out_ref = refs[-4:]
    values = x_ref[...].astype(jnp.float32)
    inner = add_refs(refs[:-4]) * gain_ref[...]
    scale = rms_scale(values)
    mean = jnp.mean(inner * values, axis=-1, keepdims=True)
    result = before_ref[...] + scale * inner - values * (scale * scale * scale) * mean
    store_by_device(out_ref, result, core_ref[0], chips)


def output_kernel(core_ref, *refs, chips):
    middle_ref, out_ref = refs[-2:]
    values = middle_ref[...] + add_refs(refs[:-2])
    store_by_device(out_ref, values.astype(jnp.bfloat16), core_ref[0], chips)


def row_call(body, dtypes, arrays, core=None):
    rows, features = arrays[0].shape
    steps = 2
    wide = pl.BlockSpec((rows // steps, features), lambda i, *_: (i, 0))
    row = pl.BlockSpec((1, features), lambda i, *_: (0, 0))
    scalars = [] if core is None else [jnp.full((1,), core, jnp.int32)]
    return pl.pallas_call(
        body,
        grid_spec=pltpu.PrefetchScalarGridSpec(
            num_scalar_prefetch=len(scalars),
            grid=(steps,),
            in_specs=[row if array.shape[0] == 1 else wide for array in arrays],
            out_specs=[wide] * len(dtypes),
        ),
        out_shape=[jax.ShapeDtypeStruct((rows, features), dtype) for dtype in dtypes],
        compiler_params=PARAMS,
        cost_estimate=hint(0),
    )(*scalars, *arrays)


def unpack_kernel(sum_ref, q_ref, k_ref, v_ref, out_ref):
    q_width, kv_width = q_ref.shape[1], k_ref.shape[1]
    values = sum_ref[...].astype(jnp.float32)
    q_ref[...] = values[:, :q_width]
    kv = values[:, q_width : q_width + 2 * kv_width]
    k_ref[...] = kv[:, :kv_width]
    v_ref[...] = kv[:, kv_width:]
    out_ref[...] = values[:, q_width + 2 * kv_width :].T


def unpack(sums, q_width, kv_width):
    rows = sums.shape[0]
    widths = [(rows, q_width), (rows, kv_width), (rows, kv_width), (q_width, rows)]
    return pl.pallas_call(
        unpack_kernel,
        out_shape=[jax.ShapeDtypeStruct(shape, jnp.float32) for shape in widths],
        compiler_params=PARAMS,
        cost_estimate=hint(0),
    )(sums)


def unpack_shares_kernel(one_ref, two_ref, gate_ref, up_ref, down_ref):
    units = one_ref.shape[1] // 3
    for part, ref in enumerate((one_ref, two_ref)):
        cut = slice(part * units, (part + 1) * units)
        gate_ref[:, cut] = ref[:, :units].astype(jnp.float32)
        up_ref[:, cut] = ref[:, units : 2 * units].astype(jnp.float32)
        down_ref[cut, :] = ref[:, 2 * units :].astype(jnp.float32).T


def unpack_shares(one, two):
    rows, width = one.shape
    units = 2 * width // 3
    shapes = [(rows, units), (rows, units), (units, rows)]
    return pl.pallas_call(
        unpack_shares_kernel,
        out_shape=[jax.ShapeDtypeStruct(shape, jnp.float32) for shape in shapes],
        compiler_params=PARAMS,
        cost_estimate=hint(0),
    )(one, two)


def middle_back_kernel(*refs, parts, size):
    n_refs, refs = refs[:parts], refs[parts:]
    x_ref, e_ref, gain_ref, refs = refs[0], refs[1], refs[2], refs[3:]
    own_refs, other_refs, refs = refs[:size], refs[size : 2 * size], refs[2 * size :]
    grad_ref, branch_ref, part_ref, do_refs = refs[0], refs[1], refs[2], refs[3:]
    half = own_refs[0].shape[0]
    grad = add_refs(n_refs)
    values = x_ref[...]
    scale = rms_scale(values)
    result, part = norm_back(grad, values, scale, gain_ref[...])

    @pl.when(pl.program_id(0) == 0)
    def _():
        part_ref[...] = jnp.zeros_like(part_ref)

    part_ref[...] += part[None, :]
    result = result + e_ref[...].astype(jnp.float32)
    grad_ref[...] = result
    branch = result.astype(jnp.bfloat16)
    branch_ref[...] = branch
    for own, other, do_ref in zip(own_refs, other_refs, do_refs):
        do = mm(branch[:, :half], own[...]) + mm(branch[:, half:], other[...])
        do_ref[...] = do.astype(jnp.bfloat16)


def middle_back(arrived, middle, cot, gain, own, other):
    parts, size = len(arrived), len(own)
    rows, features = middle.shape
    width = own[0].shape[1]
    steps = 2
    wide = pl.BlockSpec((rows // steps, features), lambda i: (i, 0))
    narrow = pl.BlockSpec((rows // steps, width), lambda i: (i, 0))
    row = pl.BlockSpec((1, features), lambda i: (0, 0))
    weight = pl.BlockSpec((features // 2, width), lambda i: (0, 0), pipeline_mode=ONCE)
    grad, branch, part, *do = pl.pallas_call(
        functools.partial(middle_back_kernel, parts=parts, size=size),
        grid=(steps,),
        in_specs=[wide] * parts + [wide, wide, row] + [weight] * (2 * size),
        out_specs=[wide, wide, row] + [narrow] * size,
        out_shape=[
            jax.ShapeDtypeStruct((rows, features), jnp.float32),
            jax.ShapeDtypeStruct((rows, features), jnp.bfloat16),
            jax.ShapeDtypeStruct((1, features), jnp.float32),
        ]
        + [jax.ShapeDtypeStruct((rows, width), jnp.bfloat16)] * size,
        compiler_params=PARAMS,
        cost_estimate=hint(2 * rows * features * width * size),
    )(*arrived, middle, cot, gain, *own, *other)
    return grad, branch, part[0], do


def column_grad(blocks, other, mine, theirs):
    total = mm_tn(other[...], theirs[...])
    low = 0
    for block in blocks:
        high = low + block.shape[0]
        total = total + mm_tn(block[...], mine[low:high, :])
        low = high
    return total


def grad_kernel(*refs, n_count, e_count):
    n_refs, refs = refs[:n_count], refs[n_count:]
    e_refs, refs = refs[:e_count], refs[e_count:]
    n_other, e_other = refs[:2]
    acts, out_ref = refs[2:-1], refs[-1]
    units = acts[0].shape[1]
    for third in range(3):
        blocks, other = (e_refs, e_other) if third == 2 else (n_refs, n_other)
        grad = column_grad(blocks, other, acts[third], acts[third + 3])
        out_ref[0, :, third * units : (third + 1) * units] = grad.astype(jnp.bfloat16)


def mlp_grads(chips, tokens, cot, tokens_other, cot_other, mine, theirs):
    tokens, cot = sum(tokens, []), sum(cot, [])
    features = tokens[0].shape[1]
    total, units = mine[0].shape
    depth = features // (2 * chips)
    long = pl.BlockSpec((total, depth), lambda b: (0, b))
    fixed = pl.BlockSpec((total, units), lambda b: (0, 0), pipeline_mode=ONCE)
    return pl.pallas_call(
        functools.partial(grad_kernel, n_count=len(tokens), e_count=len(cot)),
        grid=(chips,),
        in_specs=[pl.BlockSpec((p.shape[0], depth), lambda b: (0, b)) for p in tokens + cot]
        + [long, long]
        + [fixed] * 6,
        out_specs=pl.BlockSpec((1, depth, 3 * units), lambda b: (b, 0, 0)),
        out_shape=jax.ShapeDtypeStruct((chips, depth, 3 * units), jnp.bfloat16),
        compiler_params=PARAMS,
        cost_estimate=hint(6 * total * features * units),
    )(*tokens, *cot, tokens_other, cot_other, *mine, *theirs)


def attn_grad_kernel(*refs, size):
    e_refs = refs[2 : 2 + size]
    n_ref, n_other = refs[:2]
    e_other, d_ref, d_other, o_ref, o_other, q_ref, kv_ref, g1_ref, g2_ref = refs[2 + size : -2]
    out_ref, gain_ref = refs[-2:]
    width, out_width = d_ref.shape[1], o_ref.shape[1]
    grad = column_grad([n_ref], n_other, d_ref, d_other)
    out_ref[0, :, :width] = grad.astype(jnp.bfloat16)
    out_grad = column_grad(e_refs, e_other, o_ref, o_other)
    out_ref[0, :, width : width + out_width] = out_grad.astype(jnp.bfloat16)
    cut = q_ref.shape[1]
    first = jnp.sum(grad[:, :cut] * q_ref[...].astype(jnp.float32), axis=1, keepdims=True)
    first += jnp.sum(grad[:, cut:] * kv_ref[...].astype(jnp.float32), axis=1, keepdims=True)
    first = first / g1_ref[...]
    lane = lane_index(grad.shape[0])
    gain_ref[0] = jnp.where(lane == 0, first, g2_ref[...])


def attn_grads(
    chips, tokens, branch, mine, theirs, weights, columns, gain_one, gain_two_part
):
    size = len(branch)
    qkv_grad, attended = mine
    tokens_other, branch_other, qkv_other, attended_other = theirs
    total, features = tokens.shape
    rows = total // size
    width, out_width = qkv_grad.shape[1], attended.shape[1]
    depth = features // (2 * chips)
    column = lambda b: (0, b)
    row = lambda b: (b, 0)
    long = pl.BlockSpec((total, depth), column)
    fixed = lambda array: pl.BlockSpec(array.shape, lambda b: (0, 0), pipeline_mode=ONCE)
    place = lambda b: (b, 0, 0)
    return pl.pallas_call(
        functools.partial(attn_grad_kernel, size=size),
        grid=(chips,),
        in_specs=[long, long]
        + [pl.BlockSpec((rows, depth), column)] * size
        + [long]
        + [fixed(qkv_grad)] * 2
        + [fixed(attended)] * 2
        + [
            columns.spec("q", depth, lambda b=None: b),
            columns.spec("kv", depth, lambda b=None: b),
            pl.BlockSpec((depth, 1), row),
            pl.BlockSpec((depth, 1), row),
        ],
        out_specs=[
            pl.BlockSpec((1, depth, width + out_width), place),
            pl.BlockSpec((1, depth, PAIR), place),
        ],
        out_shape=[
            jax.ShapeDtypeStruct((chips, depth, width + out_width), jnp.bfloat16),
            jax.ShapeDtypeStruct((chips, depth, PAIR), jnp.float32),
        ],
        compiler_params=PARAMS,
        cost_estimate=hint(2 * total * features * (width + out_width)),
    )(
        tokens,
        tokens_other,
        *branch,
        branch_other,
        qkv_grad,
        qkv_other,
        attended,
        attended_other,
        weights,
        weights,
        gain_one,
        gain_two_part,
    )


def input_grad_kernel(d_ref, qo_ref, qx_ref, kvo_ref, kvx_ref, *out_refs, size):
    half, cut = qo_ref.shape

    def one(step):
        query, rest = d_ref[:, :cut], d_ref[:, cut:]
        for part, (q_ref, kv_ref) in enumerate(((qo_ref, kvo_ref), (qx_ref, kvx_ref))):
            lanes = slice(part * half, (part + 1) * half)
            product = mm_nt(query, q_ref[...]) + mm_nt(rest, kv_ref[...])
            store_partner(out_refs, step, lanes, product.astype(jnp.bfloat16))

    for step in range(size):
        pl.when(pl.program_id(0) == step)(functools.partial(one, step))


def input_grad(qkv_grad, own, other, columns, size):
    total, width = qkv_grad.shape
    features = 2 * own.shape[0]
    rows = total // size
    fixed = lambda i: (0, 0)
    weights = [columns.spec(part, own.shape[0]) for part in ("q", "q", "kv", "kv")]
    return pl.pallas_call(
        functools.partial(input_grad_kernel, size=size),
        grid=(size,),
        in_specs=[pl.BlockSpec((rows, width), lambda i: (i, 0))] + weights,
        out_specs=[pl.BlockSpec((r, features), fixed) for r in partner_rows(size, rows)],
        out_shape=[
            jax.ShapeDtypeStruct((r, features), jnp.bfloat16) for r in partner_rows(size, rows)
        ],
        compiler_params=PARAMS,
        cost_estimate=hint(2 * total * features * width),
    )(qkv_grad, own, other, own, other)


def swap(values, step):
    size = lax.axis_size("tensor")
    return lax.ppermute(values, "tensor", [(i, i ^ step) for i in range(size)])


def spread(values):
    return [values] + [swap(values, step) for step in range(1, lax.axis_size("tensor"))]


def send_blocks(blocks):
    return [blocks[0]] + [swap(block, step + 1) for step, block in enumerate(blocks[1:])]


def spread_around(values, held):
    if lax.axis_size("tensor") != 4:
        blocks = spread(values)
        first, held = barrier((blocks[1], held))
        return [[blocks[0]], [first]] + [[block] for block in blocks[2:]], held
    half = values.shape[0] // 2
    top, bottom = values[:half], values[half:]
    x_bottom, y_top = swap(bottom, 1), swap(top, 2)
    x_bottom, y_top, top, bottom, held = barrier((x_bottom, y_top, top, bottom, held))
    far = [swap(y_top, 1), swap(x_bottom, 2)]
    x_top, y_bottom = swap(top, 1), swap(bottom, 2)
    return [[values], [x_top, x_bottom], [y_top, y_bottom], far], held


def merge_kernel(x_ref, y_ref, top_ref, bottom_ref, x_out, y_out):
    half = top_ref.shape[0]
    x_out[:half] = x_ref[:half]
    x_out[half:] = add_refs([x_ref.at[half:], bottom_ref]).astype(jnp.bfloat16)
    y_out[:half] = add_refs([y_ref.at[:half], top_ref]).astype(jnp.bfloat16)
    y_out[half:] = y_ref[half:]


def send_sum(blocks, held=()):
    if lax.axis_size("tensor") != 4:
        return send_blocks(blocks), held
    own, near_x, near_y, top, bottom = blocks
    top, bottom = swap(top, 1), swap(bottom, 2)
    near_x, near_y = pl.pallas_call(
        merge_kernel,
        out_shape=[jax.ShapeDtypeStruct(near_x.shape, near_x.dtype)] * 2,
        compiler_params=PARAMS,
        cost_estimate=hint(0),
    )(near_x, near_y, top, bottom)
    near_x, near_y, held = barrier((near_x, near_y, held))
    return [own, swap(near_x, 1), swap(near_y, 2)], held


def add_up(blocks):
    total = blocks[0].astype(jnp.float32)
    for block in blocks[1:]:
        total = total + block.astype(jnp.float32)
    return total


def cross(values):
    count = lax.axis_size("dp")
    return lax.ppermute(values, "dp", [(i, i ^ 1) for i in range(count)])


def tables(positions):
    freqs = ROPE_BASE ** (-jnp.arange(0, HEAD_DIM, 2).astype(jnp.float32) / HEAD_DIM)
    angles = positions.astype(jnp.float32)[:, None] * freqs[None, :]
    cosine, sine = jnp.cos(angles), jnp.sin(angles)
    return (
        jnp.concatenate([cosine] * 4, axis=1),
        jnp.concatenate([-sine, sine, -sine, sine], axis=1),
    )


def chip_lines():
    count = lax.axis_size("dp")
    return [list(range(core, count, 2)) for core in range(2)]


def gather(values):
    return lax.all_gather(values, "dp", axis=0, tiled=True, axis_index_groups=chip_lines())


def scatter(values):
    total = lax.psum_scatter(
        values, "dp", scatter_dimension=0, tiled=True, axis_index_groups=chip_lines()
    )
    return total[0]


def along(values, step):
    count = lax.axis_size("dp")
    return lax.ppermute(values, "dp", [(i, (i + 2 * step) % count) for i in range(count)])


def order_kernel(place_ref, *refs):
    def store(ref):
        refs[-1][0] = ref[...]

    for step, ref in enumerate(refs[:-1]):
        pl.when(pl.program_id(0) == step)(functools.partial(store, ref))


def line_order(blocks):
    chips = len(blocks)
    rows, width = blocks[0].shape
    chip = lax.axis_index("dp") // 2
    places = ((chip - jnp.arange(chips)) % chips).astype(jnp.int32)
    placed = pl.pallas_call(
        order_kernel,
        grid_spec=pltpu.PrefetchScalarGridSpec(
            num_scalar_prefetch=1,
            grid=(chips,),
            in_specs=[pl.BlockSpec((rows, width), lambda i, p: (0, 0), pipeline_mode=ONCE)] * chips,
            out_specs=pl.BlockSpec((1, rows, width), lambda i, p: (p[i], 0, 0)),
        ),
        out_shape=jax.ShapeDtypeStruct((chips, rows, width), blocks[0].dtype),
        compiler_params=PARAMS,
        cost_estimate=hint(0),
    )(places, *blocks)
    return placed.reshape(chips * rows, width)


def line_parts(parts):
    chips = lax.axis_size("dp") // 2
    chip = lax.axis_index("dp") // 2
    blocks = [lax.dynamic_index_in_dim(parts, chip, 0, keepdims=False)]
    for step in range(1, chips):
        sent = lax.dynamic_index_in_dim(parts, (chip + step) % chips, 0, keepdims=False)
        blocks.append(along(sent, step))
    return blocks


def own_part(values):
    size = lax.axis_size("tensor")
    me = lax.axis_index("tensor")
    blocks = values.reshape((size, -1) + values.shape[1:])
    own = lax.dynamic_index_in_dim(blocks, me, 0, keepdims=False)
    for step in range(1, size):
        sent = lax.dynamic_index_in_dim(blocks, me ^ step, 0, keepdims=False)
        own = own + swap(sent, step)
    return own


def stack_kernel(*refs):
    low = 0
    for ref in refs[:-1]:
        high = low + ref.shape[0]
        refs[-1][low:high, :] = ref[...]
        low = high


def other_half(blocks):
    features = blocks[0].shape[1]
    shape = (sum(block.shape[0] for block in blocks), features // 2)
    halves = pl.pallas_call(
        stack_kernel,
        grid=(1,),
        in_specs=[pl.BlockSpec((b.shape[0], features // 2), lambda i: (0, 1)) for b in blocks],
        out_specs=pl.BlockSpec(shape, lambda i: (0, 0)),
        out_shape=jax.ShapeDtypeStruct(shape, blocks[0].dtype),
        compiler_params=PARAMS,
        cost_estimate=hint(0),
    )(*blocks)
    return cross(halves)


def feature_blocks(values):
    width = values.shape[-1] // lax.axis_size("dp")
    return [values[..., low : low + width] for low in range(0, values.shape[-1], width)]


def by_core(values, core):
    blocks = feature_blocks(values)
    pairs = list(zip(blocks[0::2], blocks[1::2]))
    own = [jnp.where(core == 0, even, odd) for even, odd in pairs]
    other = [jnp.where(core == 0, odd, even) for even, odd in pairs]
    return jnp.concatenate(own + other, axis=-1)


def per_device(
    hidden_in,
    gain_attn,
    w_query,
    w_key,
    w_value,
    w_out,
    gain_mlp,
    w_gate,
    w_up,
    w_down,
    positions,
    cotangent,
):
    size = lax.axis_size("tensor")
    chips = lax.axis_size("dp") // 2
    me = lax.axis_index("tensor")
    me_array = jnp.full((1,), me, jnp.int32)
    core = lax.axis_index("dp") % 2
    q_width, kv_width = w_query.shape[1], w_key.shape[1]
    group = q_width // kv_width
    units = w_down.shape[0] // 2
    half = hidden_in.shape[1] // 2

    columns = Columns(q_width, kv_width)
    gain_shard = jnp.pad(jnp.stack([gain_attn, gain_mlp], axis=1), ((0, 0), (0, PAIR - 2)))
    qkv_shard = jnp.concatenate([w_query, w_key, w_value, gain_shard], axis=1)
    out_shard = w_out.T
    qkv_shard, out_shard, hidden_in = barrier((qkv_shard, out_shard, hidden_in))
    qkv_own = gather(qkv_shard)
    residual = by_core(hidden_in, core)
    early_in = [swap(residual, step) for step in range(1, 3)]
    early_out = [along(out_shard, step) for step in range(1, 3)]
    early_in, early_out, residual, out_shard = barrier(
        (early_in, early_out, residual, out_shard)
    )
    blocks_in = [residual] + early_in + [swap(residual, step) for step in range(3, size)]
    out_parts = [out_shard] + early_out + [along(out_shard, step) for step in range(3, chips)]
    cosine, sine = tables(positions)
    cotangent = by_core(cotangent, core)
    down_t = w_down.T
    shares = []
    for part in range(2):
        cut = slice(part * units, (part + 1) * units)
        shares.append(jnp.concatenate([w_gate[:, cut], w_up[:, cut], down_t[:, cut]], axis=1))
    shares, qkv_own, out_parts, blocks_in, cosine, sine, cotangent = barrier(
        (shares, qkv_own, out_parts, blocks_in, cosine, sine, cotangent)
    )
    mlp_own = [gather(share) for share in shares]
    cot_blocks = spread(cotangent)
    qkv = (qkv_own, cross(qkv_own))
    out_own = line_order(out_parts)
    out_t = (out_own, cross(out_own))

    tokens_one, query, key_pad, value_pad = project(
        me_array, blocks_in, *qkv, cosine, sine, columns
    )
    attended, log_total, *parts = attend(
        me_array, query, key_pad, value_pad, *out_t, size, group
    )
    parts, cot_blocks, tokens_one, attended = barrier((parts, cot_blocks, tokens_one, attended))
    arrived, _ = send_sum(parts)
    cot_other = other_half(cot_blocks)
    cot_blocks = [[block] for block in cot_blocks]
    early = (cross(tokens_one[:, half:]), cross(attended))
    arrived, cot_other, early = barrier((arrived, cot_other, early))
    gain_one, gain_two = [
        jnp.concatenate([w[:, columns.gain_start + index] for w in qkv]).astype(jnp.float32)
        for index in range(2)
    ]
    middle, normed_two = row_call(
        middle_kernel, [jnp.float32, jnp.bfloat16], [*arrived, residual, gain_two[None, :]]
    )
    tokens_two, own_share = spread_around(normed_two, mlp_own[0])
    weights = (own_share, cross(own_share))
    tokens_two, weights, out_own = barrier((tokens_two, weights, out_t[0]))
    tokens_other = other_half(sum(tokens_two, []))
    *acts, dn_part, y_part = mlp(tokens_two, cot_blocks, *weights, ())
    out_blocks = spread(out_own)
    acts, tokens_other = barrier((acts, tokens_other))
    acts_other = [cross(act) for act in acts]
    grads_one = mlp_grads(
        chips, tokens_two, cot_blocks, tokens_other, cot_other, acts, acts_other
    )
    grads_one, own_share = barrier((grads_one, mlp_own[1]))
    sums_one = scatter(grads_one)
    weights = (own_share, cross(own_share))
    *acts, y_part = mlp(tokens_two, cot_blocks, *weights, (dn_part, y_part))
    acts, dn_part = acts[:3], acts[3:]
    acts, dn_part, out_blocks = barrier((acts, dn_part, out_blocks))
    acts_other = [cross(act) for act in acts]
    arrived, acts = send_sum(dn_part, acts)
    out_other = [out_t[1]] + [cross(block) for block in out_blocks[1:]]
    grads_two = mlp_grads(
        chips, tokens_two, cot_blocks, tokens_other, cot_other, acts, acts_other
    )
    grads_two, arrived, out_other, y_part = barrier((grads_two, arrived, out_other, y_part))
    y_blocks = list(y_part.reshape((size, -1) + y_part.shape[1:]))
    y_early = [swap(y_blocks[step], step) for step in range(1, 3)]
    sums_two = scatter(grads_two)
    middle_grad, branch, gain_two_part, do_blocks = middle_back(
        arrived, middle, cotangent, gain_two[None, :], out_blocks, out_other
    )
    do_blocks = send_blocks(do_blocks)
    gain_two_other = cross(gain_two_part[half:])
    do_blocks, branch, gain_two_other, y_blocks, y_early = barrier(
        (do_blocks, branch, gain_two_other, y_blocks, y_early)
    )
    branch_blocks = spread(branch)
    qkv_grad = attend_back(
        me_array, query, log_total, key_pad, value_pad, cosine, sine, do_blocks, group
    )
    qkv_grad, sums_one = barrier((qkv_grad, sums_one))
    qkv_other = cross(qkv_grad)
    normed_part = input_grad(qkv_grad, *qkv, columns, size)
    branch_blocks, normed_part = barrier((branch_blocks, normed_part))
    branch_other = other_half(branch_blocks)
    tokens_other, attended_other = early
    grads, gain_parts = attn_grads(
        chips,
        tokens_one,
        branch_blocks,
        (qkv_grad, attended),
        (tokens_other, branch_other, qkv_other, attended_other),
        qkv_own,
        columns,
        gain_one[:half, None],
        (gain_two_part[:half] + gain_two_other)[:, None],
    )
    arrived, (grads, sums_two) = send_sum(normed_part, (grads, sums_two))
    attn_sums = scatter(grads)
    gain_sums = add_up(line_parts(gain_parts[:, :, :2]))
    unpacked = unpack_shares(sums_one, sums_two)
    arrived, y_blocks, unpacked, gain_sums = barrier((arrived, y_blocks, unpacked, gain_sums))
    grad_gate, grad_up, grad_down = unpacked
    y_late = [swap(y_blocks[step], step) for step in range(3, size)]
    (grad_in,) = row_call(
        functools.partial(input_back_kernel, chips=chips),
        [jnp.float32],
        [*arrived, residual, middle_grad, gain_one[None, :]],
        core,
    )
    grad_in, gain_sums = barrier((grad_in, gain_sums))
    gain_sums = own_part(gain_sums)
    y_late, grad_in, gain_sums = barrier((y_late, grad_in, gain_sums))
    (out,) = row_call(
        functools.partial(output_kernel, chips=chips),
        [jnp.bfloat16],
        [y_blocks[0], *y_early, *y_late, middle],
        core,
    )
    out, attn_sums = barrier((out, attn_sums))
    grad_query, grad_key, grad_value, grad_out = unpack(attn_sums, q_width, kv_width)
    return (
        out,
        grad_in,
        gain_sums[:, 0],
        grad_query,
        grad_key,
        grad_value,
        grad_out,
        gain_sums[:, 1],
        grad_gate,
        grad_up,
        grad_down,
    )


def solution(mesh):
    return jax.shard_map(
        per_device,
        mesh=mesh,
        in_specs=(
            P(("dp", "tensor"), None),
            P("dp"),
            P("dp", "tensor"),
            P("dp", "tensor"),
            P("dp", "tensor"),
            P("tensor", "dp"),
            P("dp"),
            P("dp", "tensor"),
            P("dp", "tensor"),
            P("tensor", "dp"),
            P("dp"),
            P(("dp", "tensor"), None),
        ),
        out_specs=(
            P(("dp", "tensor"), None),
            P(("dp", "tensor"), None),
            P(("dp", "tensor")),
            P("dp", "tensor"),
            P("dp", "tensor"),
            P("dp", "tensor"),
            P("tensor", "dp"),
            P(("dp", "tensor")),
            P("dp", "tensor"),
            P("dp", "tensor"),
            P("tensor", "dp"),
        ),
        check_vma=False,
    )
```
